32 devices in a mesh: dp: 2 (over core), blk: 16 (over z, y, x).
Axes of the slice: x: 2, y: 2, z: 4, core: 2. Of those that a mesh axis runs over, the one named last changes fastest.
Arguments:
- tokens: bfloat16 [4, 1024, 1024], P('dp', 'blk'), may hold values from -6 to 6
- encoder: bfloat16 [4, 1024, 1024], P('dp', 'blk'), may hold values from -6 to 6
- cotangent: bfloat16 [4, 1024, 1024], P('dp', 'blk'), may hold values from -6 to 6
- self_in: bfloat16 [1024, 3072], P('blk'), may hold values from -0.1875 to 0.1875
- self_out: bfloat16 [1024, 1024], P('blk'), may hold values from -0.75 to 0.75
- cross_q: bfloat16 [1024, 1024], P('blk'), may hold values from -0.1875 to 0.1875
- cross_kv: bfloat16 [1024, 2048], P('blk'), may hold values from -0.1875 to 0.1875
- cross_out: bfloat16 [1024, 1024], P('blk'), may hold values from -0.75 to 0.75
- ffn_in: bfloat16 [1024, 4096], P('blk'), may hold values from -0.1875 to 0.1875
- ffn_out: bfloat16 [4096, 1024], P('blk'), may hold values from -0.09375 to 0.09375
- adapt_down: bfloat16 [1024, 512], P('blk'), may hold values from -0.1875 to 0.1875
- adapt_up: bfloat16 [512, 1024], P('blk'), may hold values from -0.0625 to 0.0625
- norm_gain: float32 [3, 1024], replicated, may hold values from 0.5 to 1.5
- norm_bias: float32 [3, 1024], replicated, may hold values from -3 to 3
- tgt_lengths: int32 [4, 16], P('dp'), may hold values from 0 to 1024, as said below
- src_lengths: int32 [4, 16], P('dp'), may hold values from 0 to 1024, as said below
Outputs:
- output: bfloat16 [4, 1024, 1024], P('dp', 'blk')
- tokens_grad: float32 [4, 1024, 1024], P('dp', 'blk')
- encoder_grad: float32 [4, 1024, 1024], P('dp', 'blk')
- self_in_grad: float32 [1024, 3072], P('blk')
- self_out_grad: float32 [1024, 1024], P('blk')
- cross_q_grad: float32 [1024, 1024], P('blk')
- cross_kv_grad: float32 [1024, 2048], P('blk')
- cross_out_grad: float32 [1024, 1024], P('blk')
- adapt_down_grad: float32 [1024, 512], P('blk')
- adapt_up_grad: float32 [512, 1024], P('blk')
- gain_grad: float32 [3, 1024], replicated
- bias_grad: float32 [3, 1024], replicated
The draws below stay inside these ranges and needn't reach their ends.
Inputs may be any that keep to these rules, and one draw needn't show every extreme that they name: `tgt_lengths`: A row's target lengths sum to 1024; zeros stand only after the last nonzero slot, never in the first. Among the 2 rows of one index of dp, one row holds a single sequence of 1024; every other row packs sequences of 1 to 1024, one of them exactly 1024. `src_lengths`: A sequence's source length is 0 exactly where its target length is 0, else 1 to its target length; a row's source lengths sum to 1024 or less, the positions after that sum are padding. The row that holds a single sequence has 1024 source positions.
All inputs are finite; a program needn't handle non-finite values.
Results may differ from the reference program's by a relative error of at most 0.034.
Values may be sent and summed in bfloat16 or wider, within the bound.
No kernel may reach another device: no remote copies, remote signals or barrier semaphores. Data moves between devices by JAX's collectives and lax.ppermute only.
A program may use at most 192 MiB of HBM per device.

```python
import jax
import jax.numpy as jnp
from jax import lax

D = 1024
HEADS = 16
HEAD_DIM = 64
FF = 4096
ADAPT = 512
NSEQ = 16
SEQ_MAX = 1024
LANES = 2
ROWS = 4
ROW_LEN = 1024


def packed_row(row_key):
    exp_key = jax.random.fold_in(row_key, 21)
    off_key = jax.random.fold_in(row_key, 22)
    turn_key = jax.random.fold_in(row_key, 23)
    top_exp = SEQ_MAX.bit_length() - 1
    exps = jax.random.randint(exp_key, (NSEQ - 1,), 2, top_exp + 1, dtype=jnp.int32)
    base = jnp.left_shift(jnp.ones((NSEQ - 1,), jnp.int32), exps)
    extra = jax.random.randint(off_key, (NSEQ - 1,), 0, 2 ** top_exp, dtype=jnp.int32) % base
    heavy = jnp.minimum(base + extra, SEQ_MAX).astype(jnp.int32)
    slots_left = (NSEQ - 2 - jnp.arange(NSEQ - 1, dtype=jnp.int32)).astype(jnp.int32)

    def place(remain, slot_data):
        wanted, left_after = slot_data
        lower = jnp.maximum(remain - left_after * SEQ_MAX, 0)
        upper = jnp.minimum(remain, SEQ_MAX)
        taken = jnp.minimum(jnp.maximum(wanted, lower), upper).astype(jnp.int32)
        return ((remain - taken).astype(jnp.int32), taken)
    remain_end, taken_all = lax.scan(place, jnp.array(ROW_LEN - SEQ_MAX, jnp.int32), (heavy, slots_left))
    lengths = jnp.concatenate([jnp.full((1,), SEQ_MAX, jnp.int32), taken_all]).astype(jnp.int32)
    live = jnp.sum((lengths > 0).astype(jnp.int32))
    turn = jax.random.randint(turn_key, (), 0, NSEQ, dtype=jnp.int32) % live
    slots = jnp.arange(NSEQ, dtype=jnp.int32)
    source_slot = jnp.where(slots < live, (slots + turn) % live, slots).astype(jnp.int32)
    return jnp.take(lengths, source_slot).astype(jnp.int32)


def shared_lengths(key):
    row_keys = jax.random.split(key, ROWS)
    ragged = jax.vmap(packed_row)(row_keys)
    chosen = jax.random.randint(jax.random.fold_in(key, 11), (ROWS // LANES,), 0, LANES, dtype=jnp.int32)
    lane_of = jnp.arange(ROWS, dtype=jnp.int32) % LANES
    group_of = jnp.arange(ROWS, dtype=jnp.int32) // LANES
    spanning = lane_of == chosen[group_of]
    single = jnp.where(jnp.arange(NSEQ) == 0, ROW_LEN, 0).astype(jnp.int32)
    return jnp.where(spanning[:, None], single[None, :], ragged).astype(jnp.int32)


def draw_tgt_lengths(key, part):
    lengths = shared_lengths(key)
    return lengths


def draw_src_lengths(key, part):
    target = shared_lengths(key)
    key = jax.random.fold_in(key, 2)
    factor = jax.random.randint(key, target.shape, 8, 17, dtype=jnp.int32)
    shorter = jnp.maximum(1, target * factor // 16)
    return jnp.where(target == ROW_LEN, ROW_LEN, jnp.where(target > 0, shorter, 0)).astype(jnp.int32)


def block_scale(key, shape, shards, smallest, top_value):
    factor_of, own = 1.0, jax.random.fold_in(key, 6)
    for dim, shards_of in shards:
        draws = jnp.exp(jax.random.uniform(jax.random.fold_in(own, dim), (shards_of,), jnp.float32, smallest / len(shards), top_value / len(shards)))
        factor_of = factor_of * jnp.repeat(draws, shape[dim] // shards_of).reshape([-1 if axis == dim else 1 for axis in range(len(shape))])
    return factor_of


def noise(stream_key, shape, deviation, reach, cuts=(), held_as=jnp.bfloat16):
    values = deviation * jax.random.normal(stream_key, shape, jnp.float32)
    if cuts:
        values = values * block_scale(stream_key, shape, cuts, -0.22, 0.18)
    return jnp.clip(values, -reach, reach).astype(held_as)


def setup_inputs(seed: int = 0) -> dict:
    splits = jax.random.split(jax.random.key(seed), 17)
    tokens = noise(splits[0], (ROWS, ROW_LEN, D), 1.0, 6.0, ((0, 2), (1, 16)))
    encoder = noise(splits[1], (ROWS, ROW_LEN, D), 1.0, 6.0, ((0, 2), (1, 16)))
    cotangent = noise(splits[2], (ROWS, ROW_LEN, D), 1.0, 6.0, ((0, 2), (1, 16)))
    self_in = noise(splits[3], (D, 3 * D), D ** -0.5, 0.1875, ((0, 16),))
    self_out = noise(splits[4], (D, D), (D // 16) ** -0.5, 0.75, ((0, 16),))
    cross_q = noise(splits[5], (D, D), D ** -0.5, 0.1875, ((0, 16),))
    cross_kv = noise(splits[6], (D, 2 * D), D ** -0.5, 0.1875, ((0, 16),))
    cross_out = noise(splits[7], (D, D), (D // 16) ** -0.5, 0.75, ((0, 16),))
    ffn_in = noise(splits[8], (D, FF), D ** -0.5, 0.1875, ((0, 16),))
    ffn_out = noise(splits[9], (FF, D), FF ** -0.5, 0.09375, ((0, 16),))
    adapt_down = noise(splits[10], (D, ADAPT), D ** -0.5, 0.1875, ((0, 16),))
    adapt_up = noise(splits[11], (ADAPT, D), (16 * ADAPT) ** -0.5, 0.0625, ((0, 16),))
    norm_gain = jnp.clip(1.0 + 0.1 * jax.random.normal(splits[12], (3, D), jnp.float32), 0.5, 1.5)
    norm_bias = noise(splits[13], (3, D), 0.5, 3.0, (), jnp.float32)
    tgt_lengths = draw_tgt_lengths(jax.random.fold_in(splits[16], 71), 0)
    src_lengths = draw_src_lengths(jax.random.fold_in(splits[16], 71), 0)
    return dict(tokens=tokens, encoder=encoder, cotangent=cotangent, self_in=self_in, self_out=self_out, cross_q=cross_q, cross_kv=cross_kv, cross_out=cross_out, ffn_in=ffn_in, ffn_out=ffn_out, adapt_down=adapt_down, adapt_up=adapt_up, norm_gain=norm_gain, norm_bias=norm_bias, tgt_lengths=tgt_lengths, src_lengths=src_lengths)


@jax.custom_vjp
def low(v):
    return lax.optimization_barrier(v.astype(jnp.bfloat16)).astype(jnp.float32)

@jax.custom_vjp
def low_back(v):
    return v

def low_keep(v):
    return (low(v), None)

def low_pass(kept, grad):
    return (grad,)

def back_keep(v):
    return (v, None)

def back_low(kept, grad):
    return (low(grad),)
low.defvjp(low_keep, low_pass)
low_back.defvjp(back_keep, back_low)
HIGHEST = lax.Precision.HIGHEST
NEG = -1e+30

def matmul(left_side, right_side):
    return jnp.dot(left_side, right_side, precision=HIGHEST, preferred_element_type=jnp.float32)

def layer_norm(values, gains_row, biases_row):
    center = values - lax.optimization_barrier(jnp.mean(values, -1, keepdims=True))
    spread = lax.optimization_barrier(jnp.mean(center * center, -1, keepdims=True))
    return center * lax.rsqrt(spread + 1e-05) * gains_row + biases_row

def segment_of(lengths, total_len):
    seq_ends = jnp.cumsum(lengths).astype(jnp.int32)
    places = jnp.arange(total_len, dtype=jnp.int32)
    return lax.optimization_barrier(jnp.sum((seq_ends[None, :] <= places[:, None]).astype(jnp.int32), axis=1))

def attention(queries, key_rows, value_rows, query_seg, key_seg, causal):
    query_len = queries.shape[0]
    key_len = key_rows.shape[0]
    block_len = min(512, query_len)
    block_total = query_len // block_len
    key_heads = key_rows.reshape(key_len, HEADS, HEAD_DIM)
    value_heads = value_rows.reshape(key_len, HEADS, HEAD_DIM)
    key_pos = jnp.arange(key_len, dtype=jnp.int32)
    query_pos = jnp.arange(query_len, dtype=jnp.int32)

    def one_block(block_args):
        query_blk, seg_blk, pos_blk = block_args
        query_heads = query_blk.reshape(block_len, HEADS, HEAD_DIM)
        scores = low_back(jnp.einsum('qhd,khd->hqk', query_heads, key_heads, precision=HIGHEST) * HEAD_DIM ** (-0.5))
        allowed = seg_blk[:, None] == key_seg[None, :]
        if causal:
            allowed = allowed & (key_pos[None, :] <= pos_blk[:, None])
        masked = jnp.where(allowed[None], scores, NEG)
        row_max = lax.optimization_barrier(jnp.max(masked, -1, keepdims=True))
        exp_scores = jnp.where(allowed[None], jnp.exp(masked - row_max), 0.0)
        probs = low(exp_scores / lax.optimization_barrier(jnp.sum(exp_scores, -1, keepdims=True)))
        attended = jnp.einsum('hqk,khd->qhd', probs, value_heads, precision=HIGHEST)
        return attended.reshape(block_len, HEADS * HEAD_DIM)
    results = lax.map(jax.checkpoint(one_block), (queries.reshape(block_total, block_len, -1), query_seg.reshape(block_total, block_len), query_pos.reshape(block_total, block_len)))
    return results.reshape(query_len, HEADS * HEAD_DIM)

def decoder_layer(tokens_in, encoder_in, self_in, self_out, cross_q, cross_kv, cross_out, adapt_down, adapt_up, gains, biases, ffn_in, ffn_out, target_seg, source_seg):
    projected = low_back(low(matmul(tokens_in, self_in)))
    attended = attention(projected[:, :D], projected[:, D:2 * D], projected[:, 2 * D:], target_seg, target_seg, True)
    self_branch = low_back(matmul(low_back(low(attended)), self_out))
    hidden = layer_norm(tokens_in + self_branch, gains[0], biases[0])
    hidden_low = low(hidden)
    cross_query = low_back(low(matmul(hidden_low, cross_q)))
    cross_pair = low_back(low(matmul(encoder_in, cross_kv)))
    crossed = attention(cross_query, cross_pair[:, :D], cross_pair[:, D:], target_seg, source_seg, False)
    cross_branch = low_back(matmul(low_back(low(crossed)), cross_out))
    mixed_rows = layer_norm(hidden + cross_branch, gains[1], biases[1])
    mixed_low = low(mixed_rows)
    before = low_back(matmul(mixed_low, ffn_in))
    fed = low_back(matmul(low(jax.nn.gelu(before, approximate=False)), ffn_out))
    adapt_pre = low_back(matmul(mixed_low, adapt_down))
    adapted = low_back(matmul(low(jax.nn.silu(adapt_pre)), adapt_up))
    return layer_norm(mixed_rows + fed + 4.0 * adapted, gains[2], biases[2])

def reference(tokens, encoder, cotangent, self_in, self_out, cross_q, cross_kv, cross_out, ffn_in, ffn_out, adapt_down, adapt_up, norm_gain, norm_bias, tgt_lengths, src_lengths):
    trained = (self_in.astype(jnp.float32), self_out.astype(jnp.float32), cross_q.astype(jnp.float32), cross_kv.astype(jnp.float32), cross_out.astype(jnp.float32), adapt_down.astype(jnp.float32), adapt_up.astype(jnp.float32), norm_gain.astype(jnp.float32), norm_bias.astype(jnp.float32))
    frozen_in = ffn_in.astype(jnp.float32)
    frozen_out = ffn_out.astype(jnp.float32)

    def per_row(totals, row_data):
        tokens_row, encoder_row, cot_row, target_row, source_row = row_data
        target_seg = segment_of(target_row, ROW_LEN)
        source_seg = segment_of(source_row, ROW_LEN)

        def forward(tokens_in, encoder_in, w_self_in, w_self_out, w_cross_q, w_cross_kv, w_cross_out, w_down, w_up, gains, biases):
            return decoder_layer(tokens_in, encoder_in, w_self_in, w_self_out, w_cross_q, w_cross_kv, w_cross_out, w_down, w_up, gains, biases, frozen_in, frozen_out, target_seg, source_seg)
        result, pullback = jax.vjp(forward, tokens_row.astype(jnp.float32), encoder_row.astype(jnp.float32), trained[0], trained[1], trained[2], trained[3], trained[4], trained[5], trained[6], trained[7], trained[8])
        grads = pullback(cot_row.astype(jnp.float32))
        totals = tuple((total_grad + new_grad for total_grad, new_grad in zip(totals, grads[2:])))
        return (totals, (result.astype(jnp.bfloat16), grads[0], grads[1]))
    start_totals = tuple((jnp.zeros_like(weight) for weight in trained))
    totals, stacked = lax.scan(per_row, start_totals, (tokens, encoder, cotangent, tgt_lengths, src_lengths))
    return (stacked[0], stacked[1], stacked[2], totals[0], totals[1], totals[2], totals[3], totals[4], totals[5], totals[6], totals[7], totals[8])
```

```python
import functools
import math

import jax
import jax.numpy as jnp
from jax import lax
from jax.experimental import pallas as pl
from jax.experimental.pallas import tpu as pltpu
from jax.sharding import PartitionSpec as P

HEADS = 16
HEAD_DIM = 64


NEG = -1e30


def layer_norm(values, gains_row, biases_row):
    center = values - jnp.mean(values, -1, keepdims=True)
    spread = jnp.mean(center * center, -1, keepdims=True)
    return center * lax.rsqrt(spread + 1e-05) * gains_row + biases_row


def gelu_exact(values):
    return jax.nn.gelu(values, approximate=False)


def project(inputs, weight):
    return jnp.dot(
        inputs,
        lax.all_gather(weight, "blk", axis=0, tiled=True),
        preferred_element_type=jnp.float32,
    )


def project_back(upstream, weight):
    return lax.dot_general(
        upstream,
        lax.all_gather(weight, "blk", axis=0, tiled=True),
        (((1,), (1,)), ((), ())),
        preferred_element_type=jnp.float32,
    )


def weight_grad(inputs, upstream):
    scattered = lax.psum_scatter(
        lax.dot_general(
            inputs, upstream, (((0,), (0,)), ((), ())), preferred_element_type=jnp.float32
        ).astype(jnp.bfloat16),
        "blk",
        scatter_dimension=0,
        tiled=True,
    )
    return lax.psum(scattered, "dp").astype(jnp.float32)


def vmem_spec():
    return pl.BlockSpec(memory_space=pltpu.VMEM)


def smem_spec():
    return pl.BlockSpec(memory_space=pltpu.SMEM)


def seg_of_pos(ends_ref, pos):
    seg = jnp.zeros(pos.shape, jnp.int32)
    for slot in range(ends_ref.shape[0]):
        seg = seg + (ends_ref[slot] <= pos).astype(jnp.int32)
    return seg


def pair_dot(left, right, left_dim, right_dim):
    return lax.dot_general(
        left, right, (((left_dim,), (right_dim,)), ((), ())), preferred_element_type=jnp.float32
    )


def seg_tables(q_ends, k_ends, span):
    seg_q = seg_of_pos(q_ends, lax.broadcasted_iota(jnp.int32, (1, span), 1))
    seg_k = seg_of_pos(k_ends, lax.broadcasted_iota(jnp.int32, (span, 1), 0))
    return seg_q, seg_k


def masked_scores(keys, queries, seg_q, seg_k, first, causal):
    scores = pair_dot(keys, queries, 1, 1)
    allowed = seg_k == seg_q
    if causal:
        key_pos = lax.broadcasted_iota(jnp.int32, scores.shape, 0)
        query_pos = first + lax.broadcasted_iota(jnp.int32, scores.shape, 1)
        allowed = allowed & (key_pos <= query_pos)
    return jnp.where(allowed, scores, NEG)


def attn_forward_body(causal, width, q_ends, k_ends, q_ref, k_ref, v_ref, low_ref, full_ref, lse_ref):
    span = q_ref.shape[0]
    step = math.gcd(span, 256)
    heads = width // HEAD_DIM
    seg_q, seg_k = seg_tables(q_ends, k_ends, span)
    scaled = q_ref[...] * jnp.bfloat16(HEAD_DIM ** (-0.5))
    keys, values = k_ref[...], v_ref[...]
    for first in range(0, span, step):
        reach = first + step if causal else span
        parts = []
        for head in range(heads):
            cols = slice(head * HEAD_DIM, (head + 1) * HEAD_DIM)
            scores = masked_scores(
                keys[:reach, cols],
                scaled[first : first + step, cols],
                seg_q[:, first : first + step],
                seg_k[:reach],
                first,
                causal,
            )
            top = jnp.max(scores, axis=0, keepdims=True)
            probs = jnp.exp(scores - top)
            total = jnp.sum(probs, axis=0, keepdims=True)
            mixed = pair_dot(values[:reach, cols], probs.astype(jnp.bfloat16), 0, 0)
            parts.append(mixed / total)
            lse_ref[head : head + 1, first : first + step] = top + jnp.log(total)
        joined = jnp.concatenate(parts, axis=0).T
        full_ref[first : first + step, :] = joined
        low_ref[first : first + step, :] = joined.astype(jnp.bfloat16)


def attn_forward(q_ends, k_ends, queries, keys, values, causal):
    span, width = queries.shape
    return pl.pallas_call(
        functools.partial(attn_forward_body, causal, width),
        out_shape=(
            jax.ShapeDtypeStruct((span, width), jnp.bfloat16),
            jax.ShapeDtypeStruct((span, width), jnp.float32),
            jax.ShapeDtypeStruct((width // HEAD_DIM, span), jnp.float32),
        ),
        in_specs=[smem_spec(), smem_spec()] + [vmem_spec()] * 3,
        out_specs=(vmem_spec(),) * 3,
        compiler_params=pltpu.CompilerParams(vmem_limit_bytes=48 * 1024 * 1024),
        name="attn_forward",
    )(q_ends, k_ends, queries, keys, values)


def attn_backward_body(
    causal,
    width,
    q_ends,
    k_ends,
    q_ref,
    k_ref,
    v_ref,
    up_ref,
    full_ref,
    lse_ref,
    dq_ref,
    dk_ref,
    dv_ref,
    dk_sum,
    dv_sum,
):
    span = q_ref.shape[0]
    step = math.gcd(span, 256)
    heads = width // HEAD_DIM
    seg_q, seg_k = seg_tables(q_ends, k_ends, span)
    scaled = q_ref[...] * jnp.bfloat16(HEAD_DIM ** (-0.5))
    keys, values, upstream = k_ref[...], v_ref[...], up_ref[...]
    dk_sum[...] = jnp.zeros_like(dk_sum)
    dv_sum[...] = jnp.zeros_like(dv_sum)
    for first in range(0, span, step):
        reach = first + step if causal else span
        rows = slice(first, first + step)
        product = (upstream[rows].astype(jnp.float32) * full_ref[rows, :]).T
        parts = []
        for head in range(heads):
            cols = slice(head * HEAD_DIM, (head + 1) * HEAD_DIM)
            delta = jnp.sum(product[cols], axis=0, keepdims=True)
            scores = masked_scores(
                keys[:reach, cols], scaled[rows, cols], seg_q[:, rows], seg_k[:reach], first, causal
            )
            probs = jnp.exp(scores - lse_ref[head : head + 1, rows])
            dv_sum[head, :reach] += pair_dot(
                probs.astype(jnp.bfloat16), upstream[rows, cols], 1, 0
            )
            grad_probs = pair_dot(values[:reach, cols], upstream[rows, cols], 1, 1)
            grad_scores = (probs * (grad_probs - delta)).astype(jnp.bfloat16)
            dk_sum[head, :reach] += pair_dot(grad_scores, scaled[rows, cols], 1, 0)
            parts.append(pair_dot(keys[:reach, cols], grad_scores, 0, 0))
        joined = jnp.concatenate(parts, axis=0).T * HEAD_DIM ** (-0.5)
        dq_ref[rows, :] = joined.astype(jnp.bfloat16)
    dk_ref[...] = jnp.concatenate([dk_sum[h] for h in range(heads)], axis=1).astype(jnp.bfloat16)
    dv_ref[...] = jnp.concatenate([dv_sum[h] for h in range(heads)], axis=1).astype(jnp.bfloat16)


def attn_backward(q_ends, k_ends, queries, keys, values, upstream, full, lse, causal):
    span, width = queries.shape
    heads = width // HEAD_DIM
    return pl.pallas_call(
        functools.partial(attn_backward_body, causal, width),
        out_shape=(jax.ShapeDtypeStruct((span, width), jnp.bfloat16),) * 3,
        in_specs=[smem_spec(), smem_spec()] + [vmem_spec()] * 6,
        out_specs=(vmem_spec(),) * 3,
        scratch_shapes=[pltpu.VMEM((heads, span, HEAD_DIM), jnp.float32)] * 2,
        compiler_params=pltpu.CompilerParams(vmem_limit_bytes=48 * 1024 * 1024),
        name="attn_backward",
    )(q_ends, k_ends, queries, keys, values, upstream, full, lse)


def to_heads(flat, lanes):
    devices = lax.axis_size("blk")
    groups = devices // lanes
    width = HEADS * HEAD_DIM // groups
    span = flat.shape[0] // lanes
    kinds = flat.shape[1] // (HEADS * HEAD_DIM)
    sends = flat.reshape(lanes, span, kinds, groups, width).transpose(3, 0, 1, 2, 4)
    sends = sends.reshape(devices, span, kinds * width)
    got = lax.all_to_all(sends, "blk", 0, 0, tiled=True).reshape(devices * span, kinds * width)
    return [got[:, kind * width : (kind + 1) * width] for kind in range(kinds)]


def from_heads(pieces, lanes):
    devices = lax.axis_size("blk")
    groups = devices // lanes
    span = pieces[0].shape[0] // devices
    width = pieces[0].shape[1]
    kinds = len(pieces)
    sends = jnp.concatenate(pieces, axis=1).reshape(devices, span, kinds * width)
    got = lax.all_to_all(sends, "blk", 0, 0, tiled=True)
    got = got.reshape(groups, lanes, span, kinds, width).transpose(1, 2, 3, 0, 4)
    return got.reshape(lanes * span, kinds * groups * width)


def shards(
    tokens,
    encoder,
    cotangent,
    self_in,
    self_out,
    cross_q,
    cross_kv,
    cross_out,
    ffn_in,
    ffn_out,
    adapt_down,
    adapt_up,
    norm_gain,
    norm_bias,
    tgt_lengths,
    src_lengths,
):
    lane_count, lane_span, model_width = tokens.shape
    rows_all = lane_count * lane_span
    own_row = lax.axis_index("blk") % lane_count
    tgt_ends = jnp.cumsum(lax.dynamic_index_in_dim(tgt_lengths, own_row, 0, keepdims=False))
    src_ends = jnp.cumsum(lax.dynamic_index_in_dim(src_lengths, own_row, 0, keepdims=False))
    flat_tokens = tokens.reshape(rows_all, model_width)
    flat_encoder = encoder.reshape(rows_all, model_width)
    self_q, self_k, self_v = to_heads(
        project(flat_tokens, self_in).astype(jnp.bfloat16), lane_count
    )
    cross_k, cross_v = to_heads(project(flat_encoder, cross_kv).astype(jnp.bfloat16), lane_count)
    self_mid, self_full, self_lse = attn_forward(tgt_ends, tgt_ends, self_q, self_k, self_v, True)
    self_low = from_heads([self_mid], lane_count)
    resid_one = flat_tokens.astype(jnp.float32) + project(self_low, self_out)
    hidden, pull_one = jax.vjp(layer_norm, resid_one, norm_gain[0], norm_bias[0])
    hidden_low = hidden.astype(jnp.bfloat16)
    (cross_q_own,) = to_heads(project(hidden_low, cross_q).astype(jnp.bfloat16), lane_count)
    cross_mid, cross_full, cross_lse = attn_forward(
        tgt_ends, src_ends, cross_q_own, cross_k, cross_v, False
    )
    cross_low = from_heads([cross_mid], lane_count)
    resid_two = hidden + project(cross_low, cross_out)
    mixed_rows, pull_two = jax.vjp(layer_norm, resid_two, norm_gain[1], norm_bias[1])
    mixed_low = mixed_rows.astype(jnp.bfloat16)
    before = project(mixed_low, ffn_in)
    activated, pull_gelu = jax.vjp(gelu_exact, before)
    activated_low = activated.astype(jnp.bfloat16)
    adapt_pre = project(mixed_low, adapt_down)
    adapter_act, pull_silu = jax.vjp(jax.nn.silu, adapt_pre)
    adapter_low = adapter_act.astype(jnp.bfloat16)
    summed = mixed_rows + project(activated_low, ffn_out) + 4.0 * project(adapter_low, adapt_up)
    output, pull_three = jax.vjp(layer_norm, summed, norm_gain[2], norm_bias[2])
    upstream = cotangent.reshape(rows_all, model_width).astype(jnp.float32)
    grad_summed, gain_three, bias_three = pull_three(upstream)
    down_low = grad_summed.astype(jnp.bfloat16)
    adapt_low = (4.0 * grad_summed).astype(jnp.bfloat16)
    grad_adapt_up = weight_grad(adapter_low, adapt_low)
    grad_before = pull_gelu(project_back(down_low, ffn_out))[0].astype(jnp.bfloat16)
    grad_under = pull_silu(project_back(adapt_low, adapt_up))[0].astype(jnp.bfloat16)
    grad_adapt_down = weight_grad(mixed_low, grad_under)
    grad_mixed = (
        grad_summed + project_back(grad_before, ffn_in) + project_back(grad_under, adapt_down)
    )
    grad_resid_two, gain_two, bias_two = pull_two(grad_mixed)
    cross_branch_low = grad_resid_two.astype(jnp.bfloat16)
    grad_cross_out = weight_grad(cross_low, cross_branch_low)
    (cross_grad_out,) = to_heads(
        project_back(cross_branch_low, cross_out).astype(jnp.bfloat16), lane_count
    )
    cross_grads = attn_backward(
        tgt_ends,
        src_ends,
        cross_q_own,
        cross_k,
        cross_v,
        cross_grad_out,
        cross_full,
        cross_lse,
        False,
    )
    cq_low = from_heads(cross_grads[:1], lane_count)
    ckv_low = from_heads(cross_grads[1:], lane_count)
    grad_cross_q = weight_grad(hidden_low, cq_low)
    grad_cross_kv = weight_grad(flat_encoder, ckv_low)
    encoder_grad = project_back(ckv_low, cross_kv)
    grad_hidden = grad_resid_two + project_back(cq_low, cross_q)
    grad_resid_one, gain_one, bias_one = pull_one(grad_hidden)
    self_branch_low = grad_resid_one.astype(jnp.bfloat16)
    grad_self_out = weight_grad(self_low, self_branch_low)
    (self_grad_out,) = to_heads(
        project_back(self_branch_low, self_out).astype(jnp.bfloat16), lane_count
    )
    self_grads = attn_backward(
        tgt_ends,
        tgt_ends,
        self_q,
        self_k,
        self_v,
        self_grad_out,
        self_full,
        self_lse,
        True,
    )
    triple_low = from_heads(self_grads, lane_count)
    grad_self_in = weight_grad(flat_tokens, triple_low)
    tokens_grad = grad_resid_one + project_back(triple_low, self_in)
    gain_rows = jnp.stack([gain_one, gain_two, gain_three])
    bias_rows = jnp.stack([bias_one, bias_two, bias_three])
    gain_total, bias_total = lax.psum((gain_rows, bias_rows), ("dp", "blk"))
    return (
        output.astype(jnp.bfloat16).reshape(lane_count, lane_span, model_width),
        tokens_grad.reshape(lane_count, lane_span, model_width),
        encoder_grad.reshape(lane_count, lane_span, model_width),
        grad_self_in,
        grad_self_out,
        grad_cross_q,
        grad_cross_kv,
        grad_cross_out,
        grad_adapt_down,
        grad_adapt_up,
        gain_total,
        bias_total,
    )


def solution(mesh):
    placed = (
        P("dp", "blk", None),
        P("dp", "blk", None),
        P("dp", "blk", None),
        P("blk", None),
        P("blk", None),
        P("blk", None),
        P("blk", None),
        P("blk", None),
        P("blk", None),
        P("blk", None),
        P("blk", None),
        P("blk", None),
        P(),
        P(),
        P("dp", None),
        P("dp", None),
    )
    return jax.shard_map(
        shards,
        mesh=mesh,
        in_specs=placed,
        out_specs=(
            P("dp", "blk", None),
            P("dp", "blk", None),
            P("dp", "blk", None),
            P("blk", None),
            P("blk", None),
            P("blk", None),
            P("blk", None),
            P("blk", None),
            P("blk", None),
            P("blk", None),
            P(),
            P(),
        ),
        check_vma=False,
    )
```

```python
import functools
import math

import jax
import jax.numpy as jnp
from jax import lax
from jax.experimental import pallas as pl
from jax.experimental.pallas import tpu as pltpu
from jax.sharding import PartitionSpec as P

HEADS = 16
HEAD_DIM = 64


NEG = -1e30


def layer_norm(values, gains_row, biases_row):
    center = values - jnp.mean(values, -1, keepdims=True)
    spread = jnp.mean(center * center, -1, keepdims=True)
    return center * lax.rsqrt(spread + 1e-05) * gains_row + biases_row


def gelu_exact(values):
    return jax.nn.gelu(values, approximate=False)


def project(inputs, weight):
    return jnp.dot(
        inputs,
        lax.all_gather(weight, "blk", axis=0, tiled=True),
        preferred_element_type=jnp.float32,
    )


def project_back(upstream, weight):
    return lax.dot_general(
        upstream,
        lax.all_gather(weight, "blk", axis=0, tiled=True),
        (((1,), (1,)), ((), ())),
        preferred_element_type=jnp.float32,
    )


def swap_core(block):
    cores = lax.axis_size("dp")
    return lax.ppermute(block, "dp", [(i ^ 1, i) for i in range(cores)])


def flip(block, bit):
    chips = lax.axis_size("blk")
    return lax.ppermute(block, "blk", [(i ^ bit, i) for i in range(chips)])


def rotate_z(block, distance):
    chips = lax.axis_size("blk")
    return lax.ppermute(block, "blk", [((i + 4 * distance) % chips, i) for i in range(chips)])


def own_half(values, which):
    half = values.shape[1] // 2
    return lax.dynamic_slice_in_dim(values, which * half, half, 1)


def scatter_chips(blocks, first_y):
    own = lax.axis_index("blk")
    z, y, x = own // 4, (own // 2) % 2, own % 2
    terms = blocks.reshape(4, 2, 2, *blocks.shape[1:])

    def fold(terms, axis, place, bit):
        kept = lax.dynamic_index_in_dim(terms, place, axis, keepdims=False)
        sent = lax.dynamic_index_in_dim(terms, 1 - place, axis, keepdims=False)
        got = flip(sent, bit)
        return (kept.astype(jnp.float32) + got.astype(jnp.float32)).astype(jnp.bfloat16)

    if first_y:
        terms = fold(fold(terms, 1, y, 2), 1, x, 1)
    else:
        terms = fold(fold(terms, 2, x, 1), 1, y, 2)
    total = lax.dynamic_index_in_dim(terms, z, 0, keepdims=False).astype(jnp.float32)
    for distance in (1, 2, 3):
        sent = lax.dynamic_index_in_dim(terms, (z - distance) % 4, 0, keepdims=False)
        total = total + rotate_z(sent, distance).astype(jnp.float32)
    return total


CHUNK = 256


def weight_grads(pairs, first_y):
    if lax.axis_size("blk") != 16 or lax.axis_size("dp") != 2:
        return [weight_grad(inputs, upstream) for inputs, upstream in pairs]
    core = lax.axis_index("dp")
    packed = []
    for inputs, upstream in pairs:
        both = jnp.concatenate([inputs, swap_core(inputs)], axis=0)
        half = jnp.concatenate(
            [own_half(upstream, core), swap_core(own_half(upstream, 1 - core))], axis=0
        )
        term = lax.dot_general(
            both, half, (((0,), (0,)), ((), ())), preferred_element_type=jnp.float32
        ).astype(jnp.bfloat16)
        rows = term.shape[0] // 16
        chunks = term.shape[1] // CHUNK
        packed += [
            term[:, c * CHUNK : (c + 1) * CHUNK].reshape(16, rows, CHUNK) for c in range(chunks)
        ]
    mine = scatter_chips(jnp.concatenate(packed, axis=1), first_y).astype(jnp.bfloat16)
    other = swap_core(mine)
    low = jnp.where(core == 0, mine, other).astype(jnp.float32)
    high = jnp.where(core == 0, other, mine).astype(jnp.float32)
    found, place = [], 0
    for inputs, upstream in pairs:
        rows = inputs.shape[1] // 16
        chunks = upstream.shape[1] // 2 // CHUNK
        spots = [slice(place + c * rows, place + (c + 1) * rows) for c in range(chunks)]
        found.append(
            jnp.concatenate([low[spot] for spot in spots] + [high[spot] for spot in spots], axis=1)
        )
        place += rows * chunks
    return found


def weight_grad(inputs, upstream):
    scattered = lax.psum_scatter(
        lax.dot_general(
            inputs, upstream, (((0,), (0,)), ((), ())), preferred_element_type=jnp.float32
        ).astype(jnp.bfloat16),
        "blk",
        scatter_dimension=0,
        tiled=True,
    )
    return lax.psum(scattered, "dp").astype(jnp.float32)


def vmem_spec():
    return pl.BlockSpec(memory_space=pltpu.VMEM)


def smem_spec():
    return pl.BlockSpec(memory_space=pltpu.SMEM)


def seg_of_pos(ends_ref, pos):
    seg = jnp.zeros(pos.shape, jnp.int32)
    for slot in range(ends_ref.shape[0]):
        seg = seg + (ends_ref[slot] <= pos).astype(jnp.int32)
    return seg


def pair_dot(left, right, left_dim, right_dim):
    return lax.dot_general(
        left, right, (((left_dim,), (right_dim,)), ((), ())), preferred_element_type=jnp.float32
    )


def seg_tables(q_ends, k_ends, span):
    seg_q = seg_of_pos(q_ends, lax.broadcasted_iota(jnp.int32, (1, span), 1))
    seg_k = seg_of_pos(k_ends, lax.broadcasted_iota(jnp.int32, (span, 1), 0))
    return seg_q, seg_k


def masked_scores(keys, queries, seg_q, seg_k, first, causal):
    scores = pair_dot(keys, queries, 1, 1)
    allowed = seg_k == seg_q
    if causal:
        key_pos = lax.broadcasted_iota(jnp.int32, scores.shape, 0)
        query_pos = first + lax.broadcasted_iota(jnp.int32, scores.shape, 1)
        allowed = allowed & (key_pos <= query_pos)
    return jnp.where(allowed, scores, NEG)


def attn_forward_body(causal, width, q_ends, k_ends, q_ref, k_ref, v_ref, low_ref, full_ref, lse_ref):
    span = q_ref.shape[0]
    step = math.gcd(span, 256)
    heads = width // HEAD_DIM
    seg_q, seg_k = seg_tables(q_ends, k_ends, span)
    scaled = q_ref[...] * jnp.bfloat16(HEAD_DIM ** (-0.5))
    keys, values = k_ref[...], v_ref[...]
    for first in range(0, span, step):
        reach = first + step if causal else span
        parts = []
        for head in range(heads):
            cols = slice(head * HEAD_DIM, (head + 1) * HEAD_DIM)
            scores = masked_scores(
                keys[:reach, cols],
                scaled[first : first + step, cols],
                seg_q[:, first : first + step],
                seg_k[:reach],
                first,
                causal,
            )
            top = jnp.max(scores, axis=0, keepdims=True)
            probs = jnp.exp(scores - top)
            total = jnp.sum(probs, axis=0, keepdims=True)
            mixed = pair_dot(values[:reach, cols], probs.astype(jnp.bfloat16), 0, 0)
            parts.append(mixed / total)
            lse_ref[head : head + 1, first : first + step] = top + jnp.log(total)
        joined = jnp.concatenate(parts, axis=0).T
        full_ref[first : first + step, :] = joined
        low_ref[first : first + step, :] = joined.astype(jnp.bfloat16)


def attn_forward(q_ends, k_ends, queries, keys, values, causal):
    span, width = queries.shape
    return pl.pallas_call(
        functools.partial(attn_forward_body, causal, width),
        out_shape=(
            jax.ShapeDtypeStruct((span, width), jnp.bfloat16),
            jax.ShapeDtypeStruct((span, width), jnp.float32),
            jax.ShapeDtypeStruct((width // HEAD_DIM, span), jnp.float32),
        ),
        in_specs=[smem_spec(), smem_spec()] + [vmem_spec()] * 3,
        out_specs=(vmem_spec(),) * 3,
        compiler_params=pltpu.CompilerParams(vmem_limit_bytes=48 * 1024 * 1024),
        name="attn_forward",
    )(q_ends, k_ends, queries, keys, values)


def attn_backward_body(
    causal,
    width,
    q_ends,
    k_ends,
    q_ref,
    k_ref,
    v_ref,
    up_ref,
    full_ref,
    lse_ref,
    dq_ref,
    dk_ref,
    dv_ref,
    dk_sum,
    dv_sum,
):
    span = q_ref.shape[0]
    step = math.gcd(span, 256)
    heads = width // HEAD_DIM
    seg_q, seg_k = seg_tables(q_ends, k_ends, span)
    scaled = q_ref[...] * jnp.bfloat16(HEAD_DIM ** (-0.5))
    keys, values, upstream = k_ref[...], v_ref[...], up_ref[...]
    dk_sum[...] = jnp.zeros_like(dk_sum)
    dv_sum[...] = jnp.zeros_like(dv_sum)
    for first in range(0, span, step):
        reach = first + step if causal else span
        rows = slice(first, first + step)
        product = (upstream[rows].astype(jnp.float32) * full_ref[rows, :]).T
        parts = []
        for head in range(heads):
            cols = slice(head * HEAD_DIM, (head + 1) * HEAD_DIM)
            delta = jnp.sum(product[cols], axis=0, keepdims=True)
            scores = masked_scores(
                keys[:reach, cols], scaled[rows, cols], seg_q[:, rows], seg_k[:reach], first, causal
            )
            probs = jnp.exp(scores - lse_ref[head : head + 1, rows])
            dv_sum[head, :reach] += pair_dot(
                probs.astype(jnp.bfloat16), upstream[rows, cols], 1, 0
            )
            grad_probs = pair_dot(values[:reach, cols], upstream[rows, cols], 1, 1)
            grad_scores = (probs * (grad_probs - delta)).astype(jnp.bfloat16)
            dk_sum[head, :reach] += pair_dot(grad_scores, scaled[rows, cols], 1, 0)
            parts.append(pair_dot(keys[:reach, cols], grad_scores, 0, 0))
        joined = jnp.concatenate(parts, axis=0).T * HEAD_DIM ** (-0.5)
        dq_ref[rows, :] = joined.astype(jnp.bfloat16)
    dk_ref[...] = jnp.concatenate([dk_sum[h] for h in range(heads)], axis=1).astype(jnp.bfloat16)
    dv_ref[...] = jnp.concatenate([dv_sum[h] for h in range(heads)], axis=1).astype(jnp.bfloat16)


def attn_backward(q_ends, k_ends, queries, keys, values, upstream, full, lse, causal):
    span, width = queries.shape
    heads = width // HEAD_DIM
    return pl.pallas_call(
        functools.partial(attn_backward_body, causal, width),
        out_shape=(jax.ShapeDtypeStruct((span, width), jnp.bfloat16),) * 3,
        in_specs=[smem_spec(), smem_spec()] + [vmem_spec()] * 6,
        out_specs=(vmem_spec(),) * 3,
        scratch_shapes=[pltpu.VMEM((heads, span, HEAD_DIM), jnp.float32)] * 2,
        compiler_params=pltpu.CompilerParams(vmem_limit_bytes=48 * 1024 * 1024),
        name="attn_backward",
    )(q_ends, k_ends, queries, keys, values, upstream, full, lse)


def to_heads(flat, lanes):
    devices = lax.axis_size("blk")
    groups = devices // lanes
    width = HEADS * HEAD_DIM // groups
    span = flat.shape[0] // lanes
    kinds = flat.shape[1] // (HEADS * HEAD_DIM)
    sends = flat.reshape(lanes, span, kinds, groups, width).transpose(3, 0, 1, 2, 4)
    sends = sends.reshape(devices, span, kinds * width)
    got = lax.all_to_all(sends, "blk", 0, 0, tiled=True).reshape(devices * span, kinds * width)
    return [got[:, kind * width : (kind + 1) * width] for kind in range(kinds)]


def from_heads(pieces, lanes):
    devices = lax.axis_size("blk")
    groups = devices // lanes
    span = pieces[0].shape[0] // devices
    width = pieces[0].shape[1]
    kinds = len(pieces)
    sends = jnp.concatenate(pieces, axis=1).reshape(devices, span, kinds * width)
    got = lax.all_to_all(sends, "blk", 0, 0, tiled=True)
    got = got.reshape(groups, lanes, span, kinds, width).transpose(1, 2, 3, 0, 4)
    return got.reshape(lanes * span, kinds * groups * width)


def shards(
    tokens,
    encoder,
    cotangent,
    self_in,
    self_out,
    cross_q,
    cross_kv,
    cross_out,
    ffn_in,
    ffn_out,
    adapt_down,
    adapt_up,
    norm_gain,
    norm_bias,
    tgt_lengths,
    src_lengths,
):
    lane_count, lane_span, model_width = tokens.shape
    rows_all = lane_count * lane_span
    own_row = lax.axis_index("blk") % lane_count
    tgt_ends = jnp.cumsum(lax.dynamic_index_in_dim(tgt_lengths, own_row, 0, keepdims=False))
    src_ends = jnp.cumsum(lax.dynamic_index_in_dim(src_lengths, own_row, 0, keepdims=False))
    flat_tokens = tokens.reshape(rows_all, model_width)
    flat_encoder = encoder.reshape(rows_all, model_width)
    self_q, self_k, self_v = to_heads(
        project(flat_tokens, self_in).astype(jnp.bfloat16), lane_count
    )
    cross_k, cross_v = to_heads(project(flat_encoder, cross_kv).astype(jnp.bfloat16), lane_count)
    self_mid, self_full, self_lse = attn_forward(tgt_ends, tgt_ends, self_q, self_k, self_v, True)
    self_low = from_heads([self_mid], lane_count)
    resid_one = flat_tokens.astype(jnp.float32) + project(self_low, self_out)
    hidden, pull_one = jax.vjp(layer_norm, resid_one, norm_gain[0], norm_bias[0])
    hidden_low = hidden.astype(jnp.bfloat16)
    (cross_q_own,) = to_heads(project(hidden_low, cross_q).astype(jnp.bfloat16), lane_count)
    cross_mid, cross_full, cross_lse = attn_forward(
        tgt_ends, src_ends, cross_q_own, cross_k, cross_v, False
    )
    cross_low = from_heads([cross_mid], lane_count)
    resid_two = hidden + project(cross_low, cross_out)
    mixed_rows, pull_two = jax.vjp(layer_norm, resid_two, norm_gain[1], norm_bias[1])
    mixed_low = mixed_rows.astype(jnp.bfloat16)
    before = project(mixed_low, ffn_in)
    activated, pull_gelu = jax.vjp(gelu_exact, before)
    activated_low = activated.astype(jnp.bfloat16)
    adapt_pre = project(mixed_low, adapt_down)
    adapter_act, pull_silu = jax.vjp(jax.nn.silu, adapt_pre)
    adapter_low = adapter_act.astype(jnp.bfloat16)
    summed = mixed_rows + project(activated_low, ffn_out) + 4.0 * project(adapter_low, adapt_up)
    output, pull_three = jax.vjp(layer_norm, summed, norm_gain[2], norm_bias[2])
    upstream = cotangent.reshape(rows_all, model_width).astype(jnp.float32)
    grad_summed, gain_three, bias_three = pull_three(upstream)
    down_low = grad_summed.astype(jnp.bfloat16)
    adapt_low = (4.0 * grad_summed).astype(jnp.bfloat16)
    grad_before = pull_gelu(project_back(down_low, ffn_out))[0].astype(jnp.bfloat16)
    grad_under = pull_silu(project_back(adapt_low, adapt_up))[0].astype(jnp.bfloat16)
    grad_mixed = (
        grad_summed + project_back(grad_before, ffn_in) + project_back(grad_under, adapt_down)
    )
    grad_resid_two, gain_two, bias_two = pull_two(grad_mixed)
    cross_branch_low = grad_resid_two.astype(jnp.bfloat16)
    grad_cross_out, grad_adapt_down, grad_adapt_up = weight_grads(
        [(cross_low, cross_branch_low), (mixed_low, grad_under), (adapter_low, adapt_low)], True
    )
    (cross_grad_out,) = to_heads(
        project_back(cross_branch_low, cross_out).astype(jnp.bfloat16), lane_count
    )
    cross_grads = attn_backward(
        tgt_ends,
        src_ends,
        cross_q_own,
        cross_k,
        cross_v,
        cross_grad_out,
        cross_full,
        cross_lse,
        False,
    )
    cq_low = from_heads(cross_grads[:1], lane_count)
    ckv_low = from_heads(cross_grads[1:], lane_count)
    (grad_cross_kv,) = weight_grads([(flat_encoder, ckv_low)], False)
    encoder_grad = project_back(ckv_low, cross_kv)
    grad_hidden = grad_resid_two + project_back(cq_low, cross_q)
    grad_resid_one, gain_one, bias_one = pull_one(grad_hidden)
    self_branch_low = grad_resid_one.astype(jnp.bfloat16)
    grad_cross_q, grad_self_out = weight_grads(
        [(hidden_low, cq_low), (self_low, self_branch_low)], True
    )
    (self_grad_out,) = to_heads(
        project_back(self_branch_low, self_out).astype(jnp.bfloat16), lane_count
    )
    self_grads = attn_backward(
        tgt_ends,
        tgt_ends,
        self_q,
        self_k,
        self_v,
        self_grad_out,
        self_full,
        self_lse,
        True,
    )
    triple_low = from_heads(self_grads, lane_count)
    (grad_self_in,) = weight_grads([(flat_tokens, triple_low)], False)
    tokens_grad = grad_resid_one + project_back(triple_low, self_in)
    gain_rows = jnp.stack([gain_one, gain_two, gain_three])
    bias_rows = jnp.stack([bias_one, bias_two, bias_three])
    gain_total, bias_total = lax.psum((gain_rows, bias_rows), ("dp", "blk"))
    return (
        output.astype(jnp.bfloat16).reshape(lane_count, lane_span, model_width),
        tokens_grad.reshape(lane_count, lane_span, model_width),
        encoder_grad.reshape(lane_count, lane_span, model_width),
        grad_self_in,
        grad_self_out,
        grad_cross_q,
        grad_cross_kv,
        grad_cross_out,
        grad_adapt_down,
        grad_adapt_up,
        gain_total,
        bias_total,
    )


def solution(mesh):
    placed = (
        P("dp", "blk", None),
        P("dp", "blk", None),
        P("dp", "blk", None),
        P("blk", None),
        P("blk", None),
        P("blk", None),
        P("blk", None),
        P("blk", None),
        P("blk", None),
        P("blk", None),
        P("blk", None),
        P("blk", None),
        P(),
        P(),
        P("dp", None),
        P("dp", None),
    )
    return jax.shard_map(
        shards,
        mesh=mesh,
        in_specs=placed,
        out_specs=(
            P("dp", "blk", None),
            P("dp", "blk", None),
            P("dp", "blk", None),
            P("blk", None),
            P("blk", None),
            P("blk", None),
            P("blk", None),
            P("blk", None),
            P("blk", None),
            P("blk", None),
            P(),
            P(),
        ),
        check_vma=False,
    )
```

```python
import functools
import math

import jax
import jax.numpy as jnp
from jax import lax
from jax.experimental import pallas as pl
from jax.experimental.pallas import tpu as pltpu
from jax.sharding import PartitionSpec as P

HEADS = 16
HEAD_DIM = 64
WIDTH = HEADS * HEAD_DIM


NEG = -1e30
VMEM_BYTES = 56 * 1024 * 1024


def paired():
    return lax.axis_size("blk") == 16 and lax.axis_size("dp") == 2


def swap_core(block):
    cores = lax.axis_size("dp")
    return lax.ppermute(block, "dp", [(i ^ 1, i) for i in range(cores)])


def flip(block, bit):
    chips = lax.axis_size("blk")
    return lax.ppermute(block, "blk", [(i ^ bit, i) for i in range(chips)])


def rotate_z(block, distance):
    chips = lax.axis_size("blk")
    return lax.ppermute(block, "blk", [((i + 4 * distance) % chips, i) for i in range(chips)])


def own_half(values, which):
    half = values.shape[1] // 2
    return lax.dynamic_slice_in_dim(values, which * half, half, 1)


def scatter_chips(blocks, first_y):
    own = lax.axis_index("blk")
    z, y, x = own // 4, (own // 2) % 2, own % 2
    terms = blocks.reshape(4, 2, 2, *blocks.shape[1:])

    def fold(terms, axis, place, bit):
        kept = lax.dynamic_index_in_dim(terms, place, axis, keepdims=False)
        sent = lax.dynamic_index_in_dim(terms, 1 - place, axis, keepdims=False)
        got = flip(sent, bit)
        return (kept.astype(jnp.float32) + got.astype(jnp.float32)).astype(jnp.bfloat16)

    if first_y:
        terms = fold(fold(terms, 1, y, 2), 1, x, 1)
    else:
        terms = fold(fold(terms, 2, x, 1), 1, y, 2)
    total = lax.dynamic_index_in_dim(terms, z, 0, keepdims=False).astype(jnp.float32)
    for distance in (1, 2, 3):
        sent = lax.dynamic_index_in_dim(terms, (z - distance) % 4, 0, keepdims=False)
        total = total + rotate_z(sent, distance).astype(jnp.float32)
    return total


CHUNK = 256


def weight_grads(pairs, first_y):
    if not paired():
        return [weight_grad(inputs, upstream) for inputs, upstream in pairs]
    core = lax.axis_index("dp")
    packed = []
    for inputs, upstream in pairs:
        both = jnp.concatenate([inputs, swap_core(inputs)], axis=0)
        half = jnp.concatenate(
            [own_half(upstream, core), swap_core(own_half(upstream, 1 - core))], axis=0
        )
        term = lax.dot_general(
            both, half, (((0,), (0,)), ((), ())), preferred_element_type=jnp.float32
        ).astype(jnp.bfloat16)
        rows = term.shape[0] // 16
        chunks = term.shape[1] // CHUNK
        packed += [
            term[:, c * CHUNK : (c + 1) * CHUNK].reshape(16, rows, CHUNK) for c in range(chunks)
        ]
    mine = scatter_chips(jnp.concatenate(packed, axis=1), first_y).astype(jnp.bfloat16)
    other = swap_core(mine)
    low = jnp.where(core == 0, mine, other).astype(jnp.float32)
    high = jnp.where(core == 0, other, mine).astype(jnp.float32)
    found, place = [], 0
    for inputs, upstream in pairs:
        rows = inputs.shape[1] // 16
        chunks = upstream.shape[1] // 2 // CHUNK
        spots = [slice(place + c * rows, place + (c + 1) * rows) for c in range(chunks)]
        found.append(
            jnp.concatenate([low[spot] for spot in spots] + [high[spot] for spot in spots], axis=1)
        )
        place += rows * chunks
    return found


def weight_grad(inputs, upstream):
    scattered = lax.psum_scatter(
        lax.dot_general(
            inputs, upstream, (((0,), (0,)), ((), ())), preferred_element_type=jnp.float32
        ).astype(jnp.bfloat16),
        "blk",
        scatter_dimension=0,
        tiled=True,
    )
    return lax.psum(scattered, "dp").astype(jnp.float32)


class Source:
    def __init__(self, kind, arrays, first_flip="x"):
        self.kind, self.arrays, self.first_flip = kind, arrays, first_flip


class Part:
    def __init__(self, source, rows, width, spots):
        self.source, self.rows, self.width, self.spots = source, rows, width, spots

    def scratch(self):
        return pltpu.VMEM((4, 2, 2, 2, self.rows // 32, self.width), jnp.bfloat16)

    def start(self, refs, place, dst, sem):
        kind = self.source.kind
        z, y, x, core = [place[axis] for axis in range(4)]
        for first_row, first_col, at_col, width in self.spots:
            cols = slice(first_col, first_col + width)
            into = slice(at_col, at_col + width)
            high = self.rows // 32
            if kind == "whole":
                pltpu.make_async_copy(
                    refs[0].at[:, :, :, :, :, cols], dst.at[:, :, :, :, :, into], sem
                ).start()
            elif kind == "cores":
                for which in range(2):
                    owner = core if which == 0 else 1 - core
                    pltpu.make_async_copy(
                        refs[which].at[:, :, :, first_row : first_row + high, cols],
                        dst.at[:, :, :, owner, :, into],
                        sem,
                    ).start()
            else:
                for which in range(4):
                    owner = core if which < 2 else 1 - core
                    for near in range(2):
                        if self.source.first_flip == "x":
                            at_x = x if near == 0 else 1 - x
                            at_y = y if which % 2 == 0 else 1 - y
                        else:
                            at_y = y if near == 0 else 1 - y
                            at_x = x if which % 2 == 0 else 1 - x
                        for up in range(4):
                            at_z = lax.rem(z + up, 4)
                            pltpu.make_async_copy(
                                refs[which].at[near, up, :, cols],
                                dst.at[at_z, at_y, at_x, owner, :, into],
                                sem,
                            ).start()


def gather_flips(shard, first_flip):
    rows = shard.shape[0]
    if not paired():
        full = lax.all_gather(shard, "blk", axis=0, tiled=True)
        return Source("whole", [full.reshape(4, 2, 2, 2, full.shape[0] // 32, shard.shape[1])])
    core = lax.axis_index("dp")
    own = lax.dynamic_slice_in_dim(shard, core * (rows // 2), rows // 2, 0)
    column = jnp.stack([own] + [rotate_z(own, distance) for distance in (1, 2, 3)])
    bits = (1, 2) if first_flip == "x" else (2, 1)
    plane = jnp.stack([column, flip(column, bits[0])])
    beyond = flip(plane, bits[1])
    return Source("flips", [plane, beyond, swap_core(plane), swap_core(beyond)], first_flip)


def columns_of(source, first, width):
    return Part(source, 1024, width, [(0, first, 0, width)])


PACK = 512


def gather_packed(shards):
    if not paired():
        found = []
        for shard in shards:
            source = gather_flips(shard, "x")
            rows, columns = 32 * source.arrays[0].shape[4], shard.shape[1]
            step = min(columns, 1024)
            found.append(
                [
                    Part(source, rows, step, [(0, first, 0, step)])
                    for first in range(0, columns, step)
                ]
            )
        return found
    core = lax.axis_index("dp")
    packed, spots, place = [], [], 0
    for shard in shards:
        high = shard.shape[0] // 2
        own = lax.dynamic_slice_in_dim(shard, core * high, high, 0)
        places = []
        for first in range(0, shard.shape[1], PACK):
            packed.append(own[:, first : first + PACK])
            places.append(place)
            place += high
        spots.append((shard.shape[0] * 16, places))
    mine = lax.all_gather(jnp.concatenate(packed, axis=0), "blk", axis=0)
    mine = mine.reshape(4, 2, 2, place, PACK)
    source = Source("cores", [mine, swap_core(mine)])
    found = []
    for rows, places in spots:
        parts = []
        for first in range(0, len(places), 2):
            two = places[first : first + 2]
            parts.append(
                Part(
                    source,
                    rows,
                    PACK * len(two),
                    [(row, 0, PACK * side, PACK) for side, row in enumerate(two)],
                )
            )
        found.append(parts)
    return found


def place_now():
    own, core = lax.axis_index("blk"), lax.axis_index("dp")
    return jnp.stack([own // 4, (own // 2) % 2, own % 2, core]).astype(jnp.int32)


class Loaded:
    def __init__(self, part, dst, sem):
        self.part, self.dst, self.sem, self.here = part, dst, sem, False

    def value(self):
        if not self.here:
            pltpu.make_async_copy(self.dst, self.dst, self.sem).wait()
            self.here = True
        return self.dst[...].reshape(self.part.rows, self.part.width)


def call_with_parts(body, inputs, parts, outputs, name, scratch=()):
    sources = []
    for part in parts:
        if part.source not in sources:
            sources.append(part.source)
    arrays = [array for source in sources for array in source.arrays]

    def kernel(place, *refs):
        refs = list(refs)
        ins = [refs.pop(0) for _ in inputs]
        pieces = [[refs.pop(0) for _ in source.arrays] for source in sources]
        outs = [refs.pop(0) for _ in outputs]
        dsts = [refs.pop(0) for _ in parts]
        sems = refs.pop(0)
        loaded = []
        for index, part in enumerate(parts):
            part.start(pieces[sources.index(part.source)], place, dsts[index], sems.at[index])
            loaded.append(Loaded(part, dsts[index], sems.at[index]))
        body(ins, loaded, outs, refs)

    return pl.pallas_call(
        kernel,
        out_shape=tuple(outputs),
        in_specs=[smem_spec()]
        + [vmem_spec()] * len(inputs)
        + [pl.BlockSpec(memory_space=pl.ANY)] * len(arrays),
        out_specs=(vmem_spec(),) * len(outputs),
        scratch_shapes=[part.scratch() for part in parts]
        + [pltpu.SemaphoreType.DMA((len(parts),))]
        + list(scratch),
        compiler_params=pltpu.CompilerParams(vmem_limit_bytes=VMEM_BYTES),
        name=name,
    )(place_now(), *inputs, *arrays)


def vmem_spec():
    return pl.BlockSpec(memory_space=pltpu.VMEM)


def smem_spec():
    return pl.BlockSpec(memory_space=pltpu.SMEM)


def seg_of_pos(ends_ref, pos):
    seg = jnp.zeros(pos.shape, jnp.int32)
    for slot in range(ends_ref.shape[0]):
        seg = seg + (ends_ref[slot] <= pos).astype(jnp.int32)
    return seg


def pair_dot(left, right, left_dim, right_dim):
    return lax.dot_general(
        left, right, (((left_dim,), (right_dim,)), ((), ())), preferred_element_type=jnp.float32
    )


def seg_tables(q_ends, k_ends, span):
    seg_q = seg_of_pos(q_ends, lax.broadcasted_iota(jnp.int32, (1, span), 1))
    seg_k = seg_of_pos(k_ends, lax.broadcasted_iota(jnp.int32, (span, 1), 0))
    return seg_q, seg_k


def masked_scores(keys, queries, seg_q, seg_k, first, causal):
    scores = pair_dot(keys, queries, 1, 1)
    allowed = seg_k == seg_q
    if causal:
        key_pos = lax.broadcasted_iota(jnp.int32, scores.shape, 0)
        query_pos = first + lax.broadcasted_iota(jnp.int32, scores.shape, 1)
        allowed = allowed & (key_pos <= query_pos)
    return jnp.where(allowed, scores, NEG)


def attn_forward_body(causal, width, q_ends, k_ends, q_ref, kv_ref, low_ref, full_ref, lse_ref):
    span = q_ref.shape[0]
    step = math.gcd(span, 256)
    heads = width // HEAD_DIM
    seg_q, seg_k = seg_tables(q_ends, k_ends, span)
    key_at = kv_ref.shape[1] - 2 * width
    scaled = q_ref[:, :width] * jnp.bfloat16(HEAD_DIM ** (-0.5))
    keys = kv_ref[:, key_at : key_at + width]
    values = kv_ref[:, key_at + width : key_at + 2 * width]
    for first in range(0, span, step):
        reach = first + step if causal else span
        parts = []
        for head in range(heads):
            cols = slice(head * HEAD_DIM, (head + 1) * HEAD_DIM)
            scores = masked_scores(
                keys[:reach, cols],
                scaled[first : first + step, cols],
                seg_q[:, first : first + step],
                seg_k[:reach],
                first,
                causal,
            )
            top = jnp.max(scores, axis=0, keepdims=True)
            probs = jnp.exp(scores - top)
            total = jnp.sum(probs, axis=0, keepdims=True)
            mixed = pair_dot(values[:reach, cols], probs.astype(jnp.bfloat16), 0, 0)
            parts.append(mixed / total)
            lse_ref[head : head + 1, first : first + step] = top + jnp.log(total)
        joined = jnp.concatenate(parts, axis=0).T
        full_ref[first : first + step, :] = joined
        low_ref[first : first + step, :] = joined.astype(jnp.bfloat16)


def attn_forward(q_ends, k_ends, queries, keys_values, width, causal):
    span = queries.shape[0]
    return pl.pallas_call(
        functools.partial(attn_forward_body, causal, width),
        out_shape=(
            jax.ShapeDtypeStruct((span, width), jnp.bfloat16),
            jax.ShapeDtypeStruct((span, width), jnp.float32),
            jax.ShapeDtypeStruct((width // HEAD_DIM, span), jnp.float32),
        ),
        in_specs=[smem_spec(), smem_spec()] + [vmem_spec()] * 2,
        out_specs=(vmem_spec(),) * 3,
        compiler_params=pltpu.CompilerParams(vmem_limit_bytes=VMEM_BYTES),
        name="attn_forward",
    )(q_ends, k_ends, queries, keys_values)


def attn_backward_body(
    causal,
    width,
    q_ends,
    k_ends,
    q_ref,
    kv_ref,
    up_ref,
    full_ref,
    lse_ref,
    dq_ref,
    dkv_ref,
    dk_sum,
    dv_sum,
):
    span = q_ref.shape[0]
    step = math.gcd(span, 256)
    heads = width // HEAD_DIM
    seg_q, seg_k = seg_tables(q_ends, k_ends, span)
    key_at = kv_ref.shape[1] - 2 * width
    scaled = q_ref[:, :width] * jnp.bfloat16(HEAD_DIM ** (-0.5))
    keys = kv_ref[:, key_at : key_at + width]
    values = kv_ref[:, key_at + width : key_at + 2 * width]
    upstream = up_ref[...]
    dk_sum[...] = jnp.zeros_like(dk_sum)
    dv_sum[...] = jnp.zeros_like(dv_sum)
    for first in range(0, span, step):
        reach = first + step if causal else span
        rows = slice(first, first + step)
        product = (upstream[rows].astype(jnp.float32) * full_ref[rows, :]).T
        parts = []
        for head in range(heads):
            cols = slice(head * HEAD_DIM, (head + 1) * HEAD_DIM)
            delta = jnp.sum(product[cols], axis=0, keepdims=True)
            scores = masked_scores(
                keys[:reach, cols], scaled[rows, cols], seg_q[:, rows], seg_k[:reach], first, causal
            )
            probs = jnp.exp(scores - lse_ref[head : head + 1, rows])
            dv_sum[head, :reach] += pair_dot(
                probs.astype(jnp.bfloat16), upstream[rows, cols], 1, 0
            )
            grad_probs = pair_dot(values[:reach, cols], upstream[rows, cols], 1, 1)
            grad_scores = (probs * (grad_probs - delta)).astype(jnp.bfloat16)
            dk_sum[head, :reach] += pair_dot(grad_scores, scaled[rows, cols], 1, 0)
            parts.append(pair_dot(keys[:reach, cols], grad_scores, 0, 0))
        joined = jnp.concatenate(parts, axis=0).T * HEAD_DIM ** (-0.5)
        dq_ref[rows, :] = joined.astype(jnp.bfloat16)
    sums = [dk_sum[head] for head in range(heads)] + [dv_sum[head] for head in range(heads)]
    dkv_ref[...] = jnp.concatenate(sums, axis=1).astype(jnp.bfloat16)


def attn_backward(q_ends, k_ends, queries, keys_values, upstream, full, lse, causal):
    span, width = upstream.shape
    heads = width // HEAD_DIM
    return pl.pallas_call(
        functools.partial(attn_backward_body, causal, width),
        out_shape=(
            jax.ShapeDtypeStruct((span, width), jnp.bfloat16),
            jax.ShapeDtypeStruct((span, 2 * width), jnp.bfloat16),
        ),
        in_specs=[smem_spec(), smem_spec()] + [vmem_spec()] * 5,
        out_specs=(vmem_spec(),) * 2,
        scratch_shapes=[pltpu.VMEM((heads, span, HEAD_DIM), jnp.float32)] * 2,
        compiler_params=pltpu.CompilerParams(vmem_limit_bytes=VMEM_BYTES),
        name="attn_backward",
    )(q_ends, k_ends, queries, keys_values, upstream, full, lse)


def exchange(blocks):
    return lax.all_to_all(blocks, "blk", 0, 0, tiled=True)


def as_rows(blocks):
    return blocks.reshape(blocks.shape[0] * blocks.shape[1], blocks.shape[2])


def as_blocks(rows):
    devices = lax.axis_size("blk")
    return rows.reshape(devices, rows.shape[0] // devices, rows.shape[1])


def write_blocks(out_ref, values, lanes, kind, width):
    span = values.shape[0] // lanes
    for group in range(WIDTH // width):
        for lane in range(lanes):
            out_ref[group * lanes + lane, :, kind * width : (kind + 1) * width] = values[
                lane * span : (lane + 1) * span, group * width : (group + 1) * width
            ]


def read_blocks(got_ref, lanes, kind, width):
    groups = got_ref.shape[0] // lanes
    cols = slice(kind * width, (kind + 1) * width)
    rows = [
        jnp.concatenate([got_ref[group * lanes + lane, :, cols] for group in range(groups)], axis=1)
        for lane in range(lanes)
    ]
    return jnp.concatenate(rows, axis=0)


def dot(left, right):
    return pair_dot(left, right, 1, 0)


def dot_back(left, right):
    return pair_dot(left, right, 1, 1)


def shape(*sizes, of=jnp.float32):
    return jax.ShapeDtypeStruct(sizes, of)


def normalize(values):
    center = values - jnp.mean(values, -1, keepdims=True)
    scale = lax.rsqrt(jnp.mean(center * center, -1, keepdims=True) + 1e-05)
    return center * scale, scale


def norm_back(upstream, normed, scale, gains_row):
    grad = upstream * gains_row
    return scale * (
        grad
        - jnp.mean(grad, -1, keepdims=True)
        - normed * jnp.mean(grad * normed, -1, keepdims=True)
    )


def project_blocks(inputs, parts, lanes, width, name):
    def body(ins, loaded, outs, _):
        for kind, weight in enumerate(loaded):
            write_blocks(
                outs[0], dot(ins[0][...], weight.value()).astype(jnp.bfloat16), lanes, kind, width
            )

    devices, span = lax.axis_size("blk"), inputs.shape[0] // lanes
    (blocks,) = call_with_parts(
        body,
        [inputs],
        parts,
        [shape(devices, span, width * len(parts), of=jnp.bfloat16)],
        name,
    )
    return blocks


def after_self(got, tokens, gains, biases, out_part, query_part, lanes, width):
    def body(ins, loaded, outs, _):
        got_ref, tokens_ref, gains_ref, biases_ref = ins
        low_ref, normed_ref, scale_ref, hidden_ref, blocks_ref = outs
        attended = read_blocks(got_ref, lanes, 0, width)
        low_ref[...] = attended
        resid = tokens_ref[...].astype(jnp.float32) + dot(attended, loaded[0].value())
        normed, scale = normalize(resid)
        normed_ref[...] = normed
        scale_ref[...] = scale
        hidden = (normed * gains_ref[0:1] + biases_ref[0:1]).astype(jnp.bfloat16)
        hidden_ref[...] = hidden
        query = dot(hidden, loaded[1].value()).astype(jnp.bfloat16)
        write_blocks(blocks_ref, query, lanes, 0, width)

    rows = tokens.shape[0]
    return call_with_parts(
        body,
        [got, tokens, gains, biases],
        [out_part, query_part],
        [
            shape(rows, WIDTH, of=jnp.bfloat16),
            shape(rows, WIDTH),
            shape(rows, 1),
            shape(rows, WIDTH, of=jnp.bfloat16),
            shape(*got.shape, of=jnp.bfloat16),
        ],
        "after_self",
    )


def feed_forward(got, normed_in, cotangent, gains, biases, out_part, in_parts, down, outs, up, lanes, width):
    pieces = len(in_parts)
    step = in_parts[0].width

    def body(ins, loaded, refs, scratch):
        got_ref, normed_in_ref, cot_ref, gains_ref, biases_ref = ins
        (
            output_ref,
            low_ref,
            mixed_ref,
            adapted_ref,
            dunder_ref,
            dab_ref,
            dcb_ref,
            dresid_ref,
            blocks_ref,
            norms_ref,
        ) = refs
        (slopes,) = scratch
        w_out, w_in = loaded[0], loaded[1 : 1 + pieces]
        w_down, w_ff, w_up = loaded[1 + pieces :]
        attended = read_blocks(got_ref, lanes, 0, width)
        low_ref[...] = attended
        hidden = normed_in_ref[...] * gains_ref[0:1] + biases_ref[0:1]
        normed_one, scale_one = normalize(hidden + dot(attended, w_out.value()))
        mixed = normed_one * gains_ref[1:2] + biases_ref[1:2]
        mixed_low = mixed.astype(jnp.bfloat16)
        mixed_ref[...] = mixed_low
        summed = mixed
        under = dot(mixed_low, w_down.value())
        gate = 1.0 / (1.0 + jnp.exp(-under))
        adapted = (under * gate).astype(jnp.bfloat16)
        adapted_ref[...] = adapted
        under_slope = gate * (1.0 + under * (1.0 - gate))
        summed = summed + 4.0 * dot(adapted, w_up.value())
        for piece in range(pieces):
            before = dot(mixed_low, w_in[piece].value())
            below = 0.5 + 0.5 * lax.erf(before * (0.5**0.5))
            slopes[piece] = below + before * jnp.exp(-0.5 * before * before) * (
                (2.0 * math.pi) ** -0.5
            )
            act = (before * below).astype(jnp.bfloat16)
            summed = summed + dot(act, w_ff[piece].value())
        normed_two, scale_two = normalize(summed)
        output_ref[...] = (normed_two * gains_ref[2:3] + biases_ref[2:3]).astype(jnp.bfloat16)
        upstream = cot_ref[...].astype(jnp.float32)
        norms_ref[0:1] = jnp.sum(upstream * normed_two, axis=0, keepdims=True)
        norms_ref[1:2] = jnp.sum(upstream, axis=0, keepdims=True)
        dz = norm_back(upstream, normed_two, scale_two, gains_ref[2:3])
        dzb = dz.astype(jnp.bfloat16)
        dab = (4.0 * dz).astype(jnp.bfloat16)
        dab_ref[...] = dab
        dunder = (under_slope * dot_back(dab, w_up.value())).astype(jnp.bfloat16)
        dunder_ref[...] = dunder
        dmixed = dz + dot_back(dunder, w_down.value())
        for piece in range(pieces):
            dpre = (slopes[piece] * dot_back(dzb, w_ff[piece].value())).astype(jnp.bfloat16)
            dmixed = dmixed + dot_back(dpre, w_in[piece].value())
        norms_ref[2:3] = jnp.sum(dmixed * normed_one, axis=0, keepdims=True)
        norms_ref[3:4] = jnp.sum(dmixed, axis=0, keepdims=True)
        dresid = norm_back(dmixed, normed_one, scale_one, gains_ref[1:2])
        dresid_ref[...] = dresid
        dcb = dresid.astype(jnp.bfloat16)
        dcb_ref[...] = dcb
        write_blocks(
            blocks_ref, dot_back(dcb, w_out.value()).astype(jnp.bfloat16), lanes, 0, width
        )

    rows = normed_in.shape[0]
    low = jnp.bfloat16

    def body_rows(ins, loaded, refs, scratch):
        whole_ff = loaded[2 + pieces]

        class Rows:
            def __init__(self, piece):
                self.piece = piece

            def value(self):
                return whole_ff.value()[self.piece * step : (self.piece + 1) * step]

        loaded = loaded[: 2 + pieces] + [[Rows(piece) for piece in range(pieces)], loaded[-1]]
        body(ins, loaded, refs, scratch)

    return call_with_parts(
        body_rows,
        [got, normed_in, cotangent, gains, biases],
        [out_part] + in_parts + [down, outs, up],
        [
            shape(rows, WIDTH, of=low),
            shape(rows, WIDTH, of=low),
            shape(rows, WIDTH, of=low),
            shape(rows, down.width, of=low),
            shape(rows, down.width, of=low),
            shape(rows, WIDTH, of=low),
            shape(rows, WIDTH, of=low),
            shape(rows, WIDTH),
            shape(*got.shape, of=low),
            shape(4, WIDTH),
        ],
        "feed_forward",
        [pltpu.VMEM((pieces, rows, step), jnp.float32)],
    )


def before_self(got, dresid, normed, scale, gains, query_part, out_part, lanes, width):
    def body(ins, loaded, outs, _):
        got_ref, dresid_ref, normed_ref, scale_ref, gains_ref = ins
        dcq_ref, dr_ref, dsb_ref, blocks_ref, norms_ref = outs
        dcq = read_blocks(got_ref, lanes, 0, width)
        dcq_ref[...] = dcq
        dhidden = dresid_ref[...] + dot_back(dcq, loaded[0].value())
        normed = normed_ref[...]
        norms_ref[0:1] = jnp.sum(dhidden * normed, axis=0, keepdims=True)
        norms_ref[1:2] = jnp.sum(dhidden, axis=0, keepdims=True)
        dr = norm_back(dhidden, normed, scale_ref[...], gains_ref[0:1])
        dr_ref[...] = dr
        dsb = dr.astype(jnp.bfloat16)
        dsb_ref[...] = dsb
        grad = dot_back(dsb, loaded[1].value()).astype(jnp.bfloat16)
        write_blocks(blocks_ref, grad, lanes, 0, width)

    rows = dresid.shape[0]
    return call_with_parts(
        body,
        [got, dresid, normed, scale, gains],
        [query_part, out_part],
        [
            shape(rows, WIDTH, of=jnp.bfloat16),
            shape(rows, WIDTH),
            shape(rows, WIDTH, of=jnp.bfloat16),
            shape(*got.shape, of=jnp.bfloat16),
            shape(2, WIDTH),
        ],
        "before_self",
    )


def input_grad(got, start, parts, lanes, width, name):
    def body(ins, loaded, outs, _):
        total = None
        for kind, weight in enumerate(loaded):
            values = read_blocks(ins[0], lanes, kind, width)
            outs[0][:, kind * WIDTH : (kind + 1) * WIDTH] = values
            term = dot_back(values, weight.value())
            total = term if total is None else total + term
        outs[1][...] = total if len(ins) == 1 else total + ins[1][...]

    rows = got.shape[1] * lanes
    return call_with_parts(
        body,
        [got] if start is None else [got, start],
        parts,
        [shape(rows, WIDTH * len(parts), of=jnp.bfloat16), shape(rows, WIDTH)],
        name,
    )


def sum_everywhere(values):
    if not paired():
        return lax.psum(values, ("dp", "blk"))
    values = values + swap_core(values)
    for bit in (1, 2, 4, 8):
        values = values + flip(values, bit)
    return values


def shards(
    tokens,
    encoder,
    cotangent,
    self_in,
    self_out,
    cross_q,
    cross_kv,
    cross_out,
    ffn_in,
    ffn_out,
    adapt_down,
    adapt_up,
    norm_gain,
    norm_bias,
    tgt_lengths,
    src_lengths,
):
    lanes, span, _ = tokens.shape
    rows = lanes * span
    width = WIDTH * lanes // lax.axis_size("blk")
    own_row = lax.axis_index("blk") % lanes
    tgt_ends = jnp.cumsum(lax.dynamic_index_in_dim(tgt_lengths, own_row, 0, keepdims=False))
    src_ends = jnp.cumsum(lax.dynamic_index_in_dim(src_lengths, own_row, 0, keepdims=False))
    flat_tokens = tokens.reshape(rows, WIDTH)
    flat_encoder = encoder.reshape(rows, WIDTH)

    ff_parts, down_parts, ffo_parts, up_parts = gather_packed(
        [ffn_in, adapt_down, ffn_out, adapt_up]
    )
    source = gather_flips(self_in, "x")
    self_parts = [columns_of(source, WIDTH * kind, WIDTH) for kind in range(3)]
    source = gather_flips(jnp.concatenate([cross_kv, self_out], axis=1), "y")
    pair_parts = [columns_of(source, WIDTH * kind, WIDTH) for kind in range(2)]
    self_out_part = columns_of(source, 2 * WIDTH, WIDTH)
    source = gather_flips(jnp.concatenate([cross_q, cross_out], axis=1), "x")
    query_part, cross_out_part = [columns_of(source, WIDTH * kind, WIDTH) for kind in range(2)]

    self_qkv = as_rows(exchange(project_blocks(flat_tokens, self_parts, lanes, width, "self_in")))
    cross_kv_own = as_rows(
        exchange(project_blocks(flat_encoder, pair_parts, lanes, width, "cross_kv"))
    )
    self_mid, self_full, self_lse = attn_forward(
        tgt_ends, tgt_ends, self_qkv, self_qkv, width, True
    )
    self_low, normed, scale, hidden_low, query_blocks = after_self(
        exchange(as_blocks(self_mid)),
        flat_tokens,
        norm_gain,
        norm_bias,
        self_out_part,
        query_part,
        lanes,
        width,
    )
    cross_q_own = as_rows(exchange(query_blocks))
    cross_mid, cross_full, cross_lse = attn_forward(
        tgt_ends, src_ends, cross_q_own, cross_kv_own, width, False
    )
    (
        output,
        cross_low,
        mixed_low,
        adapter_low,
        grad_under,
        adapt_low,
        cross_branch_low,
        grad_resid_two,
        cross_blocks,
        norms_high,
    ) = feed_forward(
        exchange(as_blocks(cross_mid)),
        normed,
        cotangent.reshape(rows, WIDTH),
        norm_gain,
        norm_bias,
        cross_out_part,
        ff_parts,
        down_parts[0],
        ffo_parts[0],
        up_parts[0],
        lanes,
        width,
    )
    grad_cross_out, grad_adapt_down, grad_adapt_up = weight_grads(
        [(cross_low, cross_branch_low), (mixed_low, grad_under), (adapter_low, adapt_low)], True
    )
    cross_dq, cross_dkv = attn_backward(
        tgt_ends,
        src_ends,
        cross_q_own,
        cross_kv_own,
        as_rows(exchange(cross_blocks)),
        cross_full,
        cross_lse,
        False,
    )
    cq_low, grad_resid_one, self_branch_low, self_blocks, norms_low = before_self(
        exchange(as_blocks(cross_dq)),
        grad_resid_two,
        normed,
        scale,
        norm_gain,
        query_part,
        self_out_part,
        lanes,
        width,
    )
    ckv_low, encoder_grad = input_grad(
        exchange(as_blocks(cross_dkv)), None, pair_parts, lanes, width, "encoder_grad"
    )
    (grad_cross_kv,) = weight_grads([(flat_encoder, ckv_low)], False)
    grad_cross_q, grad_self_out = weight_grads(
        [(hidden_low, cq_low), (self_low, self_branch_low)], True
    )
    self_dq, self_dkv = attn_backward(
        tgt_ends,
        tgt_ends,
        self_qkv,
        self_qkv,
        as_rows(exchange(self_blocks)),
        self_full,
        self_lse,
        True,
    )
    triple_low, tokens_grad = input_grad(
        exchange(as_blocks(jnp.concatenate([self_dq, self_dkv], axis=1))),
        grad_resid_one,
        self_parts,
        lanes,
        width,
        "tokens_grad",
    )
    (grad_self_in,) = weight_grads([(flat_tokens, triple_low)], False)
    norms = sum_everywhere(jnp.concatenate([norms_low, norms_high], axis=0))
    return (
        output.reshape(lanes, span, WIDTH),
        tokens_grad.reshape(lanes, span, WIDTH),
        encoder_grad.reshape(lanes, span, WIDTH),
        grad_self_in,
        grad_self_out,
        grad_cross_q,
        grad_cross_kv,
        grad_cross_out,
        grad_adapt_down,
        grad_adapt_up,
        jnp.stack([norms[0], norms[4], norms[2]]),
        jnp.stack([norms[1], norms[5], norms[3]]),
    )


def solution(mesh):
    placed = (
        P("dp", "blk", None),
        P("dp", "blk", None),
        P("dp", "blk", None),
        P("blk", None),
        P("blk", None),
        P("blk", None),
        P("blk", None),
        P("blk", None),
        P("blk", None),
        P("blk", None),
        P("blk", None),
        P("blk", None),
        P(),
        P(),
        P("dp", None),
        P("dp", None),
    )
    return jax.shard_map(
        shards,
        mesh=mesh,
        in_specs=placed,
        out_specs=(
            P("dp", "blk", None),
            P("dp", "blk", None),
            P("dp", "blk", None),
            P("blk", None),
            P("blk", None),
            P("blk", None),
            P("blk", None),
            P("blk", None),
            P("blk", None),
            P("blk", None),
            P(),
            P(),
        ),
        check_vma=False,
    )
```

```python
import functools
import math

import jax
import jax.numpy as jnp
from jax import lax
from jax.experimental import pallas as pl
from jax.experimental.pallas import tpu as pltpu
from jax.sharding import PartitionSpec as P

HEADS = 16
HEAD_DIM = 64
WIDTH = HEADS * HEAD_DIM


NEG = -1e30
VMEM_BYTES = 56 * 1024 * 1024


def paired():
    return lax.axis_size("blk") == 16 and lax.axis_size("dp") == 2


def swap_core(block):
    cores = lax.axis_size("dp")
    return lax.ppermute(block, "dp", [(i ^ 1, i) for i in range(cores)])


def flip(block, bit):
    chips = lax.axis_size("blk")
    return lax.ppermute(block, "blk", [(i ^ bit, i) for i in range(chips)])


def rotate_z(block, distance):
    chips = lax.axis_size("blk")
    return lax.ppermute(block, "blk", [((i + 4 * distance) % chips, i) for i in range(chips)])


def own_half(values, which):
    half = values.shape[1] // 2
    return lax.dynamic_slice_in_dim(values, which * half, half, 1)


def scatter_chips(terms, orders):
    own = lax.axis_index("blk")
    z, y, x = own // 4, (own // 2) % 2, own % 2

    def fold(blocks, axis, place, bit):
        kept = lax.dynamic_index_in_dim(blocks, place, axis, keepdims=False)
        sent = lax.dynamic_index_in_dim(blocks, 1 - place, axis, keepdims=False)
        got = flip(sent, bit)
        return (kept.astype(jnp.float32) + got.astype(jnp.float32)).astype(jnp.bfloat16)

    terms = [blocks.reshape(4, 2, 2, *blocks.shape[1:]) for blocks in terms]
    terms = [
        fold(blocks, 1, y, 2) if first_y else fold(blocks, 2, x, 1)
        for blocks, first_y in zip(terms, orders)
    ]
    terms = [
        fold(blocks, 1, x, 1) if first_y else fold(blocks, 1, y, 2)
        for blocks, first_y in zip(terms, orders)
    ]
    totals = []
    for blocks in terms:
        total = lax.dynamic_index_in_dim(blocks, z, 0, keepdims=False).astype(jnp.float32)
        for distance in (1, 2, 3):
            sent = lax.dynamic_index_in_dim(blocks, (z - distance) % 4, 0, keepdims=False)
            total = total + rotate_z(sent, distance).astype(jnp.float32)
        totals.append(total)
    return totals


CHUNK = 256


def weight_grads(pairs, first_y):
    if not paired():
        return [weight_grad(inputs, upstream) for inputs, upstream in pairs], pairs[0][1]
    core = lax.axis_index("dp")
    packed = []
    for inputs, upstream in pairs:
        both = jnp.concatenate([inputs, swap_core(inputs)], axis=0)
        half = jnp.concatenate(
            [own_half(upstream, core), swap_core(own_half(upstream, 1 - core))], axis=0
        )
        term = lax.dot_general(
            both, half, (((0,), (0,)), ((), ())), preferred_element_type=jnp.float32
        ).astype(jnp.bfloat16)
        rows = term.shape[0] // 16
        chunks = term.shape[1] // CHUNK
        packed += [
            term[:, c * CHUNK : (c + 1) * CHUNK].reshape(16, rows, CHUNK) for c in range(chunks)
        ]
    if first_y is None:
        cut = len(packed) // 2
        terms = [jnp.concatenate(packed[:cut], axis=1), jnp.concatenate(packed[cut:], axis=1)]
        orders = [True, False]
    else:
        terms, orders = [jnp.concatenate(packed, axis=1)], [first_y]
    mine = jnp.concatenate(scatter_chips(terms, orders), axis=0).astype(jnp.bfloat16)
    other = swap_core(mine)
    low = jnp.where(core == 0, mine, other).astype(jnp.float32)
    high = jnp.where(core == 0, other, mine).astype(jnp.float32)
    found, place = [], 0
    for inputs, upstream in pairs:
        rows = inputs.shape[1] // 16
        chunks = upstream.shape[1] // 2 // CHUNK
        spots = [slice(place + c * rows, place + (c + 1) * rows) for c in range(chunks)]
        found.append(
            jnp.concatenate([low[spot] for spot in spots] + [high[spot] for spot in spots], axis=1)
        )
        place += rows * chunks
    return found, terms[0]


def weight_grad(inputs, upstream):
    scattered = lax.psum_scatter(
        lax.dot_general(
            inputs, upstream, (((0,), (0,)), ((), ())), preferred_element_type=jnp.float32
        ).astype(jnp.bfloat16),
        "blk",
        scatter_dimension=0,
        tiled=True,
    )
    return lax.psum(scattered, "dp").astype(jnp.float32)


class Source:
    def __init__(self, kind, arrays, first_flip="x"):
        self.kind, self.arrays, self.first_flip = kind, arrays, first_flip


class Part:
    def __init__(self, rows, width, spots):
        self.rows, self.width, self.spots = rows, width, spots

    def scratch(self):
        return pltpu.VMEM((4, 2, 2, 2, self.rows // 32, self.width), jnp.bfloat16)

    def start(self, refs_of, place, dst, sem):
        z, y, x, core = [place[axis] for axis in range(4)]
        high = self.rows // 32
        for source, first_row, first_col, at_col, width in self.spots:
            refs = refs_of(source)
            cols = slice(first_col, first_col + width)
            into = slice(at_col, at_col + width)
            if source.kind == "whole":
                pltpu.make_async_copy(
                    refs[0].at[:, :, :, :, :, cols], dst.at[:, :, :, :, :, into], sem
                ).start()
            elif source.kind == "cores":
                for which in range(2):
                    owner = core if which == 0 else 1 - core
                    pltpu.make_async_copy(
                        refs[which].at[:, :, :, first_row : first_row + high, cols],
                        dst.at[:, :, :, owner, :, into],
                        sem,
                    ).start()
            else:
                for which in range(4):
                    owner = core if which < 2 else 1 - core
                    for near in range(2):
                        if source.first_flip == "x":
                            at_x = x if near == 0 else 1 - x
                            at_y = y if which % 2 == 0 else 1 - y
                        else:
                            at_y = y if near == 0 else 1 - y
                            at_x = x if which % 2 == 0 else 1 - x
                        for up in range(4):
                            at_z = lax.rem(z + up, 4)
                            pltpu.make_async_copy(
                                refs[which].at[near, up, :, cols],
                                dst.at[at_z, at_y, at_x, owner, :, into],
                                sem,
                            ).start()


def after(value, *others):
    return lax.optimization_barrier((value, *others))[0]


def gather_flips(shards, first_flips, *earlier):
    if not paired():
        full = [lax.all_gather(shard, "blk", axis=0, tiled=True) for shard in shards]
        return [
            Source("whole", [array.reshape(4, 2, 2, 2, array.shape[0] // 32, array.shape[1])])
            for array in full
        ]
    core = lax.axis_index("dp")
    columns = []
    for shard in shards:
        rows = shard.shape[0]
        own = lax.dynamic_slice_in_dim(shard, core * (rows // 2), rows // 2, 0)
        if earlier:
            own = after(own, *earlier)
        columns.append(
            jnp.stack([own] + [rotate_z(own, distance) for distance in (1, 2, 3)])
        )
    sources, bits = [], {"x": (1, 2), "y": (2, 1)}
    planes = [
        jnp.stack([column, flip(column, bits[first][0])])
        for column, first in zip(columns, first_flips)
    ]
    for plane, first in zip(planes, first_flips):
        beyond = flip(plane, bits[first][1])
        sources.append(
            Source("flips", [plane, beyond, swap_core(plane), swap_core(beyond)], first)
        )
    return sources


def columns_of(*pieces):
    spots, place = [], 0
    for source, first, width in pieces:
        spots.append((source, 0, first, place, width))
        place += width
    return Part(1024, place, spots)


PACK = 512


def gather_packed(shards):
    core = lax.axis_index("dp")
    packed = []
    for shard in shards:
        high = shard.shape[0] // 2
        own = lax.dynamic_slice_in_dim(shard, core * high, high, 0)
        packed += [own[:, first : first + PACK] for first in range(0, shard.shape[1], PACK)]
    return lax.all_gather(jnp.concatenate(packed, axis=0), "blk", axis=0)


def packed_parts(shards, mine):
    if not paired():
        found = []
        for source, shard in zip(gather_flips(shards, "xxxx"), shards):
            rows, columns = 32 * source.arrays[0].shape[4], shard.shape[1]
            step = min(columns, 1024)
            found.append(
                [
                    Part(rows, step, [(source, 0, first, 0, step)])
                    for first in range(0, columns, step)
                ]
            )
        return found
    spots, place = [], 0
    for shard in shards:
        high = shard.shape[0] // 2
        places = []
        for first in range(0, shard.shape[1], PACK):
            places.append(place)
            place += high
        spots.append((shard.shape[0] * 16, places))
    mine = mine.reshape(4, 2, 2, place, PACK)
    source = Source("cores", [mine, swap_core(mine)])
    found = []
    for rows, places in spots:
        parts = []
        for first in range(0, len(places), 2):
            two = places[first : first + 2]
            parts.append(
                Part(
                    rows,
                    PACK * len(two),
                    [(source, row, 0, PACK * side, PACK) for side, row in enumerate(two)],
                )
            )
        found.append(parts)
    return found


def place_now():
    own, core = lax.axis_index("blk"), lax.axis_index("dp")
    return jnp.stack([own // 4, (own // 2) % 2, own % 2, core]).astype(jnp.int32)


class Loaded:
    def __init__(self, part, dst, sem):
        self.part, self.dst, self.sem, self.here = part, dst, sem, False

    def value(self):
        if not self.here:
            pltpu.make_async_copy(self.dst, self.dst, self.sem).wait()
            self.here = True
        return self.dst[...].reshape(self.part.rows, self.part.width)


def call_with_parts(body, inputs, parts, outputs, name, scratch=()):
    sources = []
    for part in parts:
        sources += [spot[0] for spot in part.spots if spot[0] not in sources]
    arrays = [array for source in sources for array in source.arrays]

    def kernel(place, *refs):
        refs = list(refs)
        ins = [refs.pop(0) for _ in inputs]
        pieces = [[refs.pop(0) for _ in source.arrays] for source in sources]
        outs = [refs.pop(0) for _ in outputs]
        dsts = [refs.pop(0) for _ in parts]
        sems = refs.pop(0)
        loaded = []
        for index, part in enumerate(parts):
            part.start(
                lambda source: pieces[sources.index(source)], place, dsts[index], sems.at[index]
            )
            loaded.append(Loaded(part, dsts[index], sems.at[index]))
        body(ins, loaded, outs, refs)

    return pl.pallas_call(
        kernel,
        out_shape=tuple(outputs),
        in_specs=[smem_spec()]
        + [vmem_spec()] * len(inputs)
        + [pl.BlockSpec(memory_space=pl.ANY)] * len(arrays),
        out_specs=(vmem_spec(),) * len(outputs),
        scratch_shapes=[part.scratch() for part in parts]
        + [pltpu.SemaphoreType.DMA((len(parts),))]
        + list(scratch),
        compiler_params=pltpu.CompilerParams(vmem_limit_bytes=VMEM_BYTES),
        name=name,
    )(place_now(), *inputs, *arrays)


def vmem_spec():
    return pl.BlockSpec(memory_space=pltpu.VMEM)


def smem_spec():
    return pl.BlockSpec(memory_space=pltpu.SMEM)


def seg_of_pos(ends_ref, pos):
    seg = jnp.zeros(pos.shape, jnp.int32)
    for slot in range(ends_ref.shape[0]):
        seg = seg + (ends_ref[slot] <= pos).astype(jnp.int32)
    return seg


def pair_dot(left, right, left_dim, right_dim):
    return lax.dot_general(
        left, right, (((left_dim,), (right_dim,)), ((), ())), preferred_element_type=jnp.float32
    )


def seg_tables(q_ends, k_ends, span):
    seg_q = seg_of_pos(q_ends, lax.broadcasted_iota(jnp.int32, (1, span), 1))
    seg_k = seg_of_pos(k_ends, lax.broadcasted_iota(jnp.int32, (span, 1), 0))
    return seg_q, seg_k


def masked_scores(keys, queries, seg_q, seg_k, first, causal):
    scores = pair_dot(keys, queries, 1, 1)
    allowed = seg_k == seg_q
    if causal:
        key_pos = lax.broadcasted_iota(jnp.int32, scores.shape, 0)
        query_pos = first + lax.broadcasted_iota(jnp.int32, scores.shape, 1)
        allowed = allowed & (key_pos <= query_pos)
    return jnp.where(allowed, scores, NEG)


def attn_forward_body(causal, width, q_ends, k_ends, q_ref, kv_ref, low_ref, full_ref, lse_ref):
    span = q_ref.shape[0]
    step = math.gcd(span, 256)
    heads = width // HEAD_DIM
    seg_q, seg_k = seg_tables(q_ends, k_ends, span)
    key_at = kv_ref.shape[1] - 2 * width
    scaled = q_ref[:, :width] * jnp.bfloat16(HEAD_DIM ** (-0.5))
    keys = kv_ref[:, key_at : key_at + width]
    values = kv_ref[:, key_at + width : key_at + 2 * width]
    for first in range(0, span, step):
        reach = first + step if causal else span
        parts = []
        for head in range(heads):
            cols = slice(head * HEAD_DIM, (head + 1) * HEAD_DIM)
            scores = masked_scores(
                keys[:reach, cols],
                scaled[first : first + step, cols],
                seg_q[:, first : first + step],
                seg_k[:reach],
                first,
                causal,
            )
            top = jnp.max(scores, axis=0, keepdims=True)
            probs = jnp.exp(scores - top)
            total = jnp.sum(probs, axis=0, keepdims=True)
            mixed = pair_dot(values[:reach, cols], probs.astype(jnp.bfloat16), 0, 0)
            parts.append(mixed / total)
            lse_ref[head : head + 1, first : first + step] = top + jnp.log(total)
        joined = jnp.concatenate(parts, axis=0).T
        full_ref[first : first + step, :] = joined
        low_ref[first : first + step, :] = joined.astype(jnp.bfloat16)


def attn_forward(q_ends, k_ends, queries, keys_values, width, causal):
    span = queries.shape[0]
    return pl.pallas_call(
        functools.partial(attn_forward_body, causal, width),
        out_shape=(
            jax.ShapeDtypeStruct((span, width), jnp.bfloat16),
            jax.ShapeDtypeStruct((span, width), jnp.float32),
            jax.ShapeDtypeStruct((width // HEAD_DIM, span), jnp.float32),
        ),
        in_specs=[smem_spec(), smem_spec()] + [vmem_spec()] * 2,
        out_specs=(vmem_spec(),) * 3,
        compiler_params=pltpu.CompilerParams(vmem_limit_bytes=VMEM_BYTES),
        name="attn_forward",
    )(q_ends, k_ends, queries, keys_values)


def attn_backward_body(
    causal,
    width,
    q_ends,
    k_ends,
    q_ref,
    kv_ref,
    up_ref,
    full_ref,
    lse_ref,
    dq_ref,
    dkv_ref,
    dk_sum,
    dv_sum,
):
    span = q_ref.shape[0]
    step = math.gcd(span, 256)
    heads = width // HEAD_DIM
    seg_q, seg_k = seg_tables(q_ends, k_ends, span)
    key_at = kv_ref.shape[1] - 2 * width
    scaled = q_ref[:, :width] * jnp.bfloat16(HEAD_DIM ** (-0.5))
    keys = kv_ref[:, key_at : key_at + width]
    values = kv_ref[:, key_at + width : key_at + 2 * width]
    upstream = up_ref[...]
    dk_sum[...] = jnp.zeros_like(dk_sum)
    dv_sum[...] = jnp.zeros_like(dv_sum)
    for first in range(0, span, step):
        reach = first + step if causal else span
        rows = slice(first, first + step)
        product = (upstream[rows].astype(jnp.float32) * full_ref[rows, :]).T
        parts = []
        for head in range(heads):
            cols = slice(head * HEAD_DIM, (head + 1) * HEAD_DIM)
            delta = jnp.sum(product[cols], axis=0, keepdims=True)
            scores = masked_scores(
                keys[:reach, cols], scaled[rows, cols], seg_q[:, rows], seg_k[:reach], first, causal
            )
            probs = jnp.exp(scores - lse_ref[head : head + 1, rows])
            dv_sum[head, :reach] += pair_dot(
                probs.astype(jnp.bfloat16), upstream[rows, cols], 1, 0
            )
            grad_probs = pair_dot(values[:reach, cols], upstream[rows, cols], 1, 1)
            grad_scores = (probs * (grad_probs - delta)).astype(jnp.bfloat16)
            dk_sum[head, :reach] += pair_dot(grad_scores, scaled[rows, cols], 1, 0)
            parts.append(pair_dot(keys[:reach, cols], grad_scores, 0, 0))
        joined = jnp.concatenate(parts, axis=0).T * HEAD_DIM ** (-0.5)
        dq_ref[rows, :] = joined.astype(jnp.bfloat16)
    sums = [dk_sum[head] for head in range(heads)] + [dv_sum[head] for head in range(heads)]
    dkv_ref[...] = jnp.concatenate(sums, axis=1).astype(jnp.bfloat16)


def attn_backward(q_ends, k_ends, queries, keys_values, upstream, full, lse, causal):
    span, width = upstream.shape
    heads = width // HEAD_DIM
    return pl.pallas_call(
        functools.partial(attn_backward_body, causal, width),
        out_shape=(
            jax.ShapeDtypeStruct((span, width), jnp.bfloat16),
            jax.ShapeDtypeStruct((span, 2 * width), jnp.bfloat16),
        ),
        in_specs=[smem_spec(), smem_spec()] + [vmem_spec()] * 5,
        out_specs=(vmem_spec(),) * 2,
        scratch_shapes=[pltpu.VMEM((heads, span, HEAD_DIM), jnp.float32)] * 2,
        compiler_params=pltpu.CompilerParams(vmem_limit_bytes=VMEM_BYTES),
        name="attn_backward",
    )(q_ends, k_ends, queries, keys_values, upstream, full, lse)


def exchange(blocks):
    return lax.all_to_all(blocks, "blk", 0, 0, tiled=True)


def as_rows(blocks):
    return blocks.reshape(blocks.shape[0] * blocks.shape[1], blocks.shape[2])


def as_blocks(rows):
    devices = lax.axis_size("blk")
    return rows.reshape(devices, rows.shape[0] // devices, rows.shape[1])


def write_blocks(out_ref, values, lanes, kind, width):
    span = values.shape[0] // lanes
    for group in range(WIDTH // width):
        for lane in range(lanes):
            out_ref[group * lanes + lane, :, kind * width : (kind + 1) * width] = values[
                lane * span : (lane + 1) * span, group * width : (group + 1) * width
            ]


def read_blocks(got_ref, lanes, kind, width):
    groups = got_ref.shape[0] // lanes
    cols = slice(kind * width, (kind + 1) * width)
    rows = [
        jnp.concatenate([got_ref[group * lanes + lane, :, cols] for group in range(groups)], axis=1)
        for lane in range(lanes)
    ]
    return jnp.concatenate(rows, axis=0)


def dot(left, right):
    return pair_dot(left, right, 1, 0)


def dot_back(left, right):
    return pair_dot(left, right, 1, 1)


def shape(*sizes, of=jnp.float32):
    return jax.ShapeDtypeStruct(sizes, of)


def normalize(values):
    center = values - jnp.mean(values, -1, keepdims=True)
    scale = lax.rsqrt(jnp.mean(center * center, -1, keepdims=True) + 1e-05)
    return center * scale, scale


def norm_back(upstream, normed, scale, gains_row):
    grad = upstream * gains_row
    return scale * (
        grad
        - jnp.mean(grad, -1, keepdims=True)
        - normed * jnp.mean(grad * normed, -1, keepdims=True)
    )


def project_blocks(inputs, parts, lanes, width, name):
    def body(ins, loaded, outs, _):
        for kind, weight in enumerate(loaded):
            write_blocks(
                outs[0], dot(ins[0][...], weight.value()).astype(jnp.bfloat16), lanes, kind, width
            )

    devices, span = lax.axis_size("blk"), inputs.shape[0] // lanes
    (blocks,) = call_with_parts(
        body,
        [inputs],
        parts,
        [shape(devices, span, width * len(parts), of=jnp.bfloat16)],
        name,
    )
    return blocks


def after_self(got, tokens, gains, biases, out_part, query_part, lanes, width):
    def body(ins, loaded, outs, _):
        got_ref, tokens_ref, gains_ref, biases_ref = ins
        low_ref, normed_ref, scale_ref, hidden_ref, blocks_ref = outs
        attended = read_blocks(got_ref, lanes, 0, width)
        low_ref[...] = attended
        resid = tokens_ref[...].astype(jnp.float32) + dot(attended, loaded[0].value())
        normed, scale = normalize(resid)
        normed_ref[...] = normed
        scale_ref[...] = scale
        hidden = (normed * gains_ref[0:1] + biases_ref[0:1]).astype(jnp.bfloat16)
        hidden_ref[...] = hidden
        query = dot(hidden, loaded[1].value()).astype(jnp.bfloat16)
        write_blocks(blocks_ref, query, lanes, 0, width)

    rows = tokens.shape[0]
    return call_with_parts(
        body,
        [got, tokens, gains, biases],
        [out_part, query_part],
        [
            shape(rows, WIDTH, of=jnp.bfloat16),
            shape(rows, WIDTH),
            shape(rows, 1),
            shape(rows, WIDTH, of=jnp.bfloat16),
            shape(*got.shape, of=jnp.bfloat16),
        ],
        "after_self",
    )


def feed_forward(got, normed_in, cotangent, gains, biases, out_part, in_parts, down, outs, up, lanes, width):
    pieces = len(in_parts)
    step = in_parts[0].width

    def body(ins, loaded, refs, scratch):
        got_ref, normed_in_ref, cot_ref, gains_ref, biases_ref = ins
        (
            output_ref,
            low_ref,
            mixed_ref,
            adapted_ref,
            dunder_ref,
            dab_ref,
            dcb_ref,
            dresid_ref,
            blocks_ref,
            norms_ref,
        ) = refs
        (slopes,) = scratch
        w_out, w_in = loaded[0], loaded[1 : 1 + pieces]
        w_down, w_ff, w_up = loaded[1 + pieces :]
        attended = read_blocks(got_ref, lanes, 0, width)
        low_ref[...] = attended
        hidden = normed_in_ref[...] * gains_ref[0:1] + biases_ref[0:1]
        normed_one, scale_one = normalize(hidden + dot(attended, w_out.value()))
        mixed = normed_one * gains_ref[1:2] + biases_ref[1:2]
        mixed_low = mixed.astype(jnp.bfloat16)
        mixed_ref[...] = mixed_low
        summed = mixed
        under = dot(mixed_low, w_down.value())
        gate = 1.0 / (1.0 + jnp.exp(-under))
        adapted = (under * gate).astype(jnp.bfloat16)
        adapted_ref[...] = adapted
        under_slope = gate * (1.0 + under * (1.0 - gate))
        summed = summed + 4.0 * dot(adapted, w_up.value())
        for piece in range(pieces):
            before = dot(mixed_low, w_in[piece].value())
            below = 0.5 + 0.5 * lax.erf(before * (0.5**0.5))
            slopes[piece] = below + before * jnp.exp(-0.5 * before * before) * (
                (2.0 * math.pi) ** -0.5
            )
            act = (before * below).astype(jnp.bfloat16)
            summed = summed + dot(act, w_ff[piece].value())
        normed_two, scale_two = normalize(summed)
        output_ref[...] = (normed_two * gains_ref[2:3] + biases_ref[2:3]).astype(jnp.bfloat16)
        upstream = cot_ref[...].astype(jnp.float32)
        norms_ref[0:1] = jnp.sum(upstream * normed_two, axis=0, keepdims=True)
        norms_ref[1:2] = jnp.sum(upstream, axis=0, keepdims=True)
        dz = norm_back(upstream, normed_two, scale_two, gains_ref[2:3])
        dzb = dz.astype(jnp.bfloat16)
        dab = (4.0 * dz).astype(jnp.bfloat16)
        dab_ref[...] = dab
        dunder = (under_slope * dot_back(dab, w_up.value())).astype(jnp.bfloat16)
        dunder_ref[...] = dunder
        dmixed = dz + dot_back(dunder, w_down.value())
        for piece in range(pieces):
            dpre = (slopes[piece] * dot_back(dzb, w_ff[piece].value())).astype(jnp.bfloat16)
            dmixed = dmixed + dot_back(dpre, w_in[piece].value())
        norms_ref[2:3] = jnp.sum(dmixed * normed_one, axis=0, keepdims=True)
        norms_ref[3:4] = jnp.sum(dmixed, axis=0, keepdims=True)
        dresid = norm_back(dmixed, normed_one, scale_one, gains_ref[1:2])
        dresid_ref[...] = dresid
        dcb = dresid.astype(jnp.bfloat16)
        dcb_ref[...] = dcb
        write_blocks(
            blocks_ref, dot_back(dcb, w_out.value()).astype(jnp.bfloat16), lanes, 0, width
        )

    rows = normed_in.shape[0]
    low = jnp.bfloat16

    def body_rows(ins, loaded, refs, scratch):
        whole_ff = loaded[2 + pieces]

        class Rows:
            def __init__(self, piece):
                self.piece = piece

            def value(self):
                return whole_ff.value()[self.piece * step : (self.piece + 1) * step]

        loaded = loaded[: 2 + pieces] + [[Rows(piece) for piece in range(pieces)], loaded[-1]]
        body(ins, loaded, refs, scratch)

    return call_with_parts(
        body_rows,
        [got, normed_in, cotangent, gains, biases],
        [out_part] + in_parts + [down, outs, up],
        [
            shape(rows, WIDTH, of=low),
            shape(rows, WIDTH, of=low),
            shape(rows, WIDTH, of=low),
            shape(rows, down.width, of=low),
            shape(rows, down.width, of=low),
            shape(rows, WIDTH, of=low),
            shape(rows, WIDTH, of=low),
            shape(rows, WIDTH),
            shape(*got.shape, of=low),
            shape(4, WIDTH),
        ],
        "feed_forward",
        [pltpu.VMEM((pieces, rows, step), jnp.float32)],
    )


def before_self(got, dresid, normed, scale, gains, query_part, out_part, lanes, width):
    def body(ins, loaded, outs, _):
        got_ref, dresid_ref, normed_ref, scale_ref, gains_ref = ins
        dcq_ref, dr_ref, dsb_ref, blocks_ref, norms_ref = outs
        dcq = read_blocks(got_ref, lanes, 0, width)
        dcq_ref[...] = dcq
        dhidden = dresid_ref[...] + dot_back(dcq, loaded[0].value())
        normed = normed_ref[...]
        norms_ref[0:1] = jnp.sum(dhidden * normed, axis=0, keepdims=True)
        norms_ref[1:2] = jnp.sum(dhidden, axis=0, keepdims=True)
        dr = norm_back(dhidden, normed, scale_ref[...], gains_ref[0:1])
        dr_ref[...] = dr
        dsb = dr.astype(jnp.bfloat16)
        dsb_ref[...] = dsb
        grad = dot_back(dsb, loaded[1].value()).astype(jnp.bfloat16)
        write_blocks(blocks_ref, grad, lanes, 0, width)

    rows = dresid.shape[0]
    return call_with_parts(
        body,
        [got, dresid, normed, scale, gains],
        [query_part, out_part],
        [
            shape(rows, WIDTH, of=jnp.bfloat16),
            shape(rows, WIDTH),
            shape(rows, WIDTH, of=jnp.bfloat16),
            shape(*got.shape, of=jnp.bfloat16),
            shape(2, WIDTH),
        ],
        "before_self",
    )


def input_grad(got, start, parts, lanes, width, name):
    def body(ins, loaded, outs, _):
        total = None
        for kind, weight in enumerate(loaded):
            term = dot_back(read_blocks(ins[0], lanes, kind, width), weight.value())
            total = term if total is None else total + term
        outs[0][...] = total if len(ins) == 1 else total + ins[1][...]

    rows = got.shape[1] * lanes
    return call_with_parts(
        body,
        [got] if start is None else [got, start],
        parts,
        [shape(rows, WIDTH)],
        name,
    )


def sum_everywhere(values):
    if not paired():
        return lax.psum(values, ("dp", "blk"))
    values = values + swap_core(values)
    for bit in (1, 2, 4, 8):
        values = values + flip(values, bit)
    return values


def shards(
    tokens,
    encoder,
    cotangent,
    self_in,
    self_out,
    cross_q,
    cross_kv,
    cross_out,
    ffn_in,
    ffn_out,
    adapt_down,
    adapt_up,
    norm_gain,
    norm_bias,
    tgt_lengths,
    src_lengths,
):
    lanes, span, _ = tokens.shape
    rows = lanes * span
    width = WIDTH * lanes // lax.axis_size("blk")
    own_row = lax.axis_index("blk") % lanes
    tgt_ends = jnp.cumsum(lax.dynamic_index_in_dim(tgt_lengths, own_row, 0, keepdims=False))
    src_ends = jnp.cumsum(lax.dynamic_index_in_dim(src_lengths, own_row, 0, keepdims=False))
    flat_tokens = tokens.reshape(rows, WIDTH)
    flat_encoder = encoder.reshape(rows, WIDTH)

    frozen = [ffn_in, adapt_down, ffn_out, adapt_up]
    packed = gather_packed(frozen) if paired() else None
    half = 3 * WIDTH // 2
    self_x, self_y = gather_flips([self_in[:, :half], self_in[:, half:]], "xy")
    self_parts = [
        columns_of((self_x, 0, WIDTH)),
        columns_of((self_x, WIDTH, WIDTH // 2), (self_y, 0, WIDTH // 2)),
        columns_of((self_y, WIDTH // 2, WIDTH)),
    ]
    shards_x = jnp.concatenate([cross_kv[:, :WIDTH], self_out[:, : WIDTH // 2]], axis=1)
    shards_y = jnp.concatenate([cross_kv[:, WIDTH:], self_out[:, WIDTH // 2 :]], axis=1)
    pair_x, pair_y = gather_flips([shards_x, shards_y], "xy", self_x.arrays[0])
    pair_parts = [columns_of((pair_x, 0, WIDTH)), columns_of((pair_y, 0, WIDTH))]
    self_out_part = columns_of((pair_x, WIDTH, WIDTH // 2), (pair_y, WIDTH, WIDTH // 2))
    late_x, late_y = gather_flips([cross_q, cross_out], "xy", pair_x.arrays[0])
    query_part, cross_out_part = columns_of((late_x, 0, WIDTH)), columns_of((late_y, 0, WIDTH))

    self_qkv = as_rows(exchange(project_blocks(flat_tokens, self_parts, lanes, width, "self_in")))
    cross_kv_own = as_rows(
        exchange(project_blocks(flat_encoder, pair_parts, lanes, width, "cross_kv"))
    )
    self_mid, self_full, self_lse = attn_forward(
        tgt_ends, tgt_ends, self_qkv, self_qkv, width, True
    )
    ready = after(packed, self_mid) if paired() else None
    ff_parts, down_parts, ffo_parts, up_parts = packed_parts(frozen, ready)
    self_low, normed, scale, hidden_low, query_blocks = after_self(
        exchange(as_blocks(self_mid)),
        flat_tokens,
        norm_gain,
        norm_bias,
        self_out_part,
        query_part,
        lanes,
        width,
    )
    cross_q_own = as_rows(exchange(query_blocks))
    cross_mid, cross_full, cross_lse = attn_forward(
        tgt_ends, src_ends, cross_q_own, cross_kv_own, width, False
    )
    (
        output,
        cross_low,
        mixed_low,
        adapter_low,
        grad_under,
        adapt_low,
        cross_branch_low,
        grad_resid_two,
        cross_blocks,
        norms_high,
    ) = feed_forward(
        exchange(as_blocks(cross_mid)),
        normed,
        cotangent.reshape(rows, WIDTH),
        norm_gain,
        norm_bias,
        cross_out_part,
        ff_parts,
        down_parts[0],
        ffo_parts[0],
        up_parts[0],
        lanes,
        width,
    )
    (grad_cross_out, grad_adapt_down, grad_adapt_up), _ = weight_grads(
        [(cross_low, cross_branch_low), (mixed_low, grad_under), (adapter_low, adapt_low)], True
    )
    cross_dq, cross_dkv = attn_backward(
        tgt_ends,
        src_ends,
        cross_q_own,
        cross_kv_own,
        as_rows(exchange(cross_blocks)),
        cross_full,
        cross_lse,
        False,
    )
    cq_low, grad_resid_one, self_branch_low, self_blocks, norms_low = before_self(
        exchange(as_blocks(cross_dq)),
        grad_resid_two,
        normed,
        scale,
        norm_gain,
        query_part,
        self_out_part,
        lanes,
        width,
    )
    cross_got = exchange(as_blocks(cross_dkv))
    ckv_low = cross_got.reshape(-1, lanes, span, 2, width).transpose(1, 2, 3, 0, 4)
    (grad_cross_kv,), _ = weight_grads(
        [(flat_encoder, ckv_low.reshape(rows, 2 * WIDTH))], False
    )
    (encoder_grad,) = input_grad(cross_got, None, pair_parts, lanes, width, "encoder_grad")
    (grad_cross_q, grad_self_out), _ = weight_grads(
        [(hidden_low, cq_low), (self_low, self_branch_low)], True
    )
    self_dq, self_dkv = attn_backward(
        tgt_ends,
        tgt_ends,
        self_qkv,
        self_qkv,
        as_rows(exchange(self_blocks)),
        self_full,
        self_lse,
        True,
    )
    self_got = exchange(as_blocks(jnp.concatenate([self_dq, self_dkv], axis=1)))
    triple_low = self_got.reshape(-1, lanes, span, 3, width).transpose(1, 2, 3, 0, 4)
    (grad_self_in,), sent = weight_grads(
        [(flat_tokens, triple_low.reshape(rows, 3 * WIDTH))], None
    )
    (tokens_grad,) = input_grad(
        after(self_got, sent), grad_resid_one, self_parts, lanes, width, "tokens_grad"
    )
    norms = sum_everywhere(jnp.concatenate([norms_low, norms_high], axis=0))
    return (
        output.reshape(lanes, span, WIDTH),
        tokens_grad.reshape(lanes, span, WIDTH),
        encoder_grad.reshape(lanes, span, WIDTH),
        grad_self_in,
        grad_self_out,
        grad_cross_q,
        grad_cross_kv,
        grad_cross_out,
        grad_adapt_down,
        grad_adapt_up,
        jnp.stack([norms[0], norms[4], norms[2]]),
        jnp.stack([norms[1], norms[5], norms[3]]),
    )


def solution(mesh):
    placed = (
        P("dp", "blk", None),
        P("dp", "blk", None),
        P("dp", "blk", None),
        P("blk", None),
        P("blk", None),
        P("blk", None),
        P("blk", None),
        P("blk", None),
        P("blk", None),
        P("blk", None),
        P("blk", None),
        P("blk", None),
        P(),
        P(),
        P("dp", None),
        P("dp", None),
    )
    return jax.shard_map(
        shards,
        mesh=mesh,
        in_specs=placed,
        out_specs=(
            P("dp", "blk", None),
            P("dp", "blk", None),
            P("dp", "blk", None),
            P("blk", None),
            P("blk", None),
            P("blk", None),
            P("blk", None),
            P("blk", None),
            P("blk", None),
            P("blk", None),
            P(),
            P(),
        ),
        check_vma=False,
    )
```

```python
import functools
import math

import jax
import jax.numpy as jnp
from jax import lax
from jax.experimental import pallas as pl
from jax.experimental.pallas import tpu as pltpu
from jax.sharding import PartitionSpec as P

HEADS = 16
HEAD_DIM = 64
WIDTH = HEADS * HEAD_DIM


NEG = -1e30
VMEM_BYTES = 56 * 1024 * 1024


def cost(microseconds):
    return pl.CostEstimate(
        flops=int(microseconds * 1.0e9),
        bytes_accessed=int(microseconds * 3.5e6),
        transcendentals=0,
    )


def paired():
    return lax.axis_size("blk") == 16 and lax.axis_size("dp") == 2


def swap_core(block):
    cores = lax.axis_size("dp")
    return lax.ppermute(block, "dp", [(i ^ 1, i) for i in range(cores)])


def flip(block, bit):
    chips = lax.axis_size("blk")
    return lax.ppermute(block, "blk", [(i ^ bit, i) for i in range(chips)])


def rotate_z(block, distance):
    chips = lax.axis_size("blk")
    return lax.ppermute(block, "blk", [((i + 4 * distance) % chips, i) for i in range(chips)])


def own_half(values, which):
    half = values.shape[1] // 2
    return lax.dynamic_slice_in_dim(values, which * half, half, 1)


def scatter_chips(terms, orders):
    own = lax.axis_index("blk")
    z, y, x = own // 4, (own // 2) % 2, own % 2

    def fold(blocks, axis, place, bit):
        kept = lax.dynamic_index_in_dim(blocks, place, axis, keepdims=False)
        sent = lax.dynamic_index_in_dim(blocks, 1 - place, axis, keepdims=False)
        got = flip(sent, bit)
        return (kept.astype(jnp.float32) + got.astype(jnp.float32)).astype(jnp.bfloat16)

    terms = [blocks.reshape(4, 2, 2, *blocks.shape[1:]) for blocks in terms]
    stages = [terms[0]]
    terms = [
        fold(blocks, 1, y, 2) if first_y else fold(blocks, 2, x, 1)
        for blocks, first_y in zip(terms, orders)
    ]
    stages.append(terms[0])
    terms = [
        fold(blocks, 1, x, 1) if first_y else fold(blocks, 1, y, 2)
        for blocks, first_y in zip(terms, orders)
    ]
    stages.append(terms[0])
    totals = []
    for blocks in terms:
        total = lax.dynamic_index_in_dim(blocks, z, 0, keepdims=False).astype(jnp.float32)
        for distance in (1, 2, 3):
            sent = lax.dynamic_index_in_dim(blocks, (z - distance) % 4, 0, keepdims=False)
            total = total + rotate_z(sent, distance).astype(jnp.float32)
        totals.append(total)
    return totals, stages


CHUNK = 256


def weight_grads(pairs):
    if not paired():
        return [weight_grad(inputs, upstream) for inputs, upstream in pairs], [pairs[0][1]]
    core = lax.axis_index("dp")
    packed = []
    for inputs, upstream in pairs:
        both = jnp.concatenate([inputs, swap_core(inputs)], axis=0)
        half = jnp.concatenate(
            [own_half(upstream, core), swap_core(own_half(upstream, 1 - core))], axis=0
        )
        term = lax.dot_general(
            both, half, (((0,), (0,)), ((), ())), preferred_element_type=jnp.float32
        ).astype(jnp.bfloat16)
        rows = term.shape[0] // 16
        chunks = term.shape[1] // CHUNK
        packed += [
            term[:, c * CHUNK : (c + 1) * CHUNK].reshape(16, rows, CHUNK) for c in range(chunks)
        ]
    cut = len(packed) // 2
    terms = [jnp.concatenate(packed[:cut], axis=1), jnp.concatenate(packed[cut:], axis=1)]
    totals, stages = scatter_chips(terms, [True, False])
    mine = jnp.concatenate(totals, axis=0).astype(jnp.bfloat16)
    other = swap_core(mine)
    low = jnp.where(core == 0, mine, other).astype(jnp.float32)
    high = jnp.where(core == 0, other, mine).astype(jnp.float32)
    found, place = [], 0
    for inputs, upstream in pairs:
        rows = inputs.shape[1] // 16
        chunks = upstream.shape[1] // 2 // CHUNK
        spots = [slice(place + c * rows, place + (c + 1) * rows) for c in range(chunks)]
        found.append(
            jnp.concatenate([low[spot] for spot in spots] + [high[spot] for spot in spots], axis=1)
        )
        place += rows * chunks
    return found, stages


def weight_grad(inputs, upstream):
    scattered = lax.psum_scatter(
        lax.dot_general(
            inputs, upstream, (((0,), (0,)), ((), ())), preferred_element_type=jnp.float32
        ).astype(jnp.bfloat16),
        "blk",
        scatter_dimension=0,
        tiled=True,
    )
    return lax.psum(scattered, "dp").astype(jnp.float32)


class Source:
    def __init__(self, kind, arrays, first_flip="x", column=None):
        self.kind, self.arrays, self.first_flip = kind, arrays, first_flip
        self.stages = arrays[:1] * 3 if column is None else [column] + arrays[:2]


class Part:
    def __init__(self, rows, width, spots):
        self.rows, self.width, self.spots = rows, width, spots

    def scratch(self):
        return pltpu.VMEM((4, 2, 2, 2, self.rows // 32, self.width), jnp.bfloat16)

    def start(self, refs_of, place, dst, sem):
        z, y, x, core = [place[axis] for axis in range(4)]
        high = self.rows // 32
        for source, first_row, first_col, at_col, width in self.spots:
            refs = refs_of(source)
            cols = slice(first_col, first_col + width)
            into = slice(at_col, at_col + width)
            if source.kind == "whole":
                pltpu.make_async_copy(
                    refs[0].at[:, :, :, :, :, cols], dst.at[:, :, :, :, :, into], sem
                ).start()
            elif source.kind == "cores":
                for which in range(2):
                    owner = core if which == 0 else 1 - core
                    pltpu.make_async_copy(
                        refs[which].at[:, :, :, first_row : first_row + high, cols],
                        dst.at[:, :, :, owner, :, into],
                        sem,
                    ).start()
            else:
                for which in range(4):
                    owner = core if which < 2 else 1 - core
                    for near in range(2):
                        if source.first_flip == "x":
                            at_x = x if near == 0 else 1 - x
                            at_y = y if which % 2 == 0 else 1 - y
                        else:
                            at_y = y if near == 0 else 1 - y
                            at_x = x if which % 2 == 0 else 1 - x
                        for up in range(4):
                            at_z = lax.rem(z + up, 4)
                            pltpu.make_async_copy(
                                refs[which].at[near, up, :, cols],
                                dst.at[at_z, at_y, at_x, owner, :, into],
                                sem,
                            ).start()


def after(value, *others):
    return lax.optimization_barrier((value, *others))[0]


def gather_flips(shards, first_flips):
    if not paired():
        full = [lax.all_gather(shard, "blk", axis=0, tiled=True) for shard in shards]
        return [
            Source("whole", [array.reshape(4, 2, 2, 2, array.shape[0] // 32, array.shape[1])])
            for array in full
        ]
    core = lax.axis_index("dp")
    columns = []
    for shard in shards:
        rows = shard.shape[0]
        own = lax.dynamic_slice_in_dim(shard, core * (rows // 2), rows // 2, 0)
        columns.append(
            jnp.stack([own] + [rotate_z(own, distance) for distance in (1, 2, 3)])
        )
    sources, bits = [], {"x": (1, 2), "y": (2, 1)}
    planes = [
        jnp.stack([column, flip(column, bits[first][0])])
        for column, first in zip(columns, first_flips)
    ]
    for column, plane, first in zip(columns, planes, first_flips):
        beyond = flip(plane, bits[first][1])
        sources.append(
            Source("flips", [plane, beyond, swap_core(plane), swap_core(beyond)], first, column)
        )
    return sources


def columns_of(*pieces):
    spots, place = [], 0
    for source, first, width in pieces:
        spots.append((source, 0, first, place, width))
        place += width
    return Part(1024, place, spots)


PACK = 512


def gather_packed(shards):
    core = lax.axis_index("dp")
    packed = []
    for shard in shards:
        high = shard.shape[0] // 2
        own = lax.dynamic_slice_in_dim(shard, core * high, high, 0)
        packed += [own[:, first : first + PACK] for first in range(0, shard.shape[1], PACK)]
    return lax.all_gather(jnp.concatenate(packed, axis=0), "blk", axis=0)


def packed_parts(shards, mine):
    if not paired():
        found = []
        for source, shard in zip(gather_flips(shards, "x" * len(shards)), shards):
            rows, columns = 32 * source.arrays[0].shape[4], shard.shape[1]
            step = min(columns, 1024)
            found.append(
                [
                    Part(rows, step, [(source, 0, first, 0, step)])
                    for first in range(0, columns, step)
                ]
            )
        return found
    spots, place = [], 0
    for shard in shards:
        high = shard.shape[0] // 2
        places = []
        for first in range(0, shard.shape[1], PACK):
            places.append(place)
            place += high
        spots.append((shard.shape[0] * 16, places))
    mine = mine.reshape(4, 2, 2, place, PACK)
    source = Source("cores", [mine, swap_core(mine)])
    found = []
    for rows, places in spots:
        parts = []
        for first in range(0, len(places), 2):
            two = places[first : first + 2]
            parts.append(
                Part(
                    rows,
                    PACK * len(two),
                    [(source, row, 0, PACK * side, PACK) for side, row in enumerate(two)],
                )
            )
        found.append(parts)
    return found


def place_now():
    own, core = lax.axis_index("blk"), lax.axis_index("dp")
    return jnp.stack([own // 4, (own // 2) % 2, own % 2, core]).astype(jnp.int32)


class Loaded:
    def __init__(self, part, dst, sem):
        self.part, self.dst, self.sem, self.here = part, dst, sem, False

    def value(self):
        if not self.here:
            pltpu.make_async_copy(self.dst, self.dst, self.sem).wait()
            self.here = True
        return self.dst[...].reshape(self.part.rows, self.part.width)


def call_with_parts(body, inputs, parts, outputs, name, scratch=(), takes=5):
    sources = []
    for part in parts:
        sources += [spot[0] for spot in part.spots if spot[0] not in sources]
    arrays = [array for source in sources for array in source.arrays]

    def kernel(place, *refs):
        refs = list(refs)
        ins = [refs.pop(0) for _ in inputs]
        pieces = [[refs.pop(0) for _ in source.arrays] for source in sources]
        outs = [refs.pop(0) for _ in outputs]
        dsts = [refs.pop(0) for _ in parts]
        sems = refs.pop(0)
        loaded = []
        for index, part in enumerate(parts):
            part.start(
                lambda source: pieces[sources.index(source)], place, dsts[index], sems.at[index]
            )
            loaded.append(Loaded(part, dsts[index], sems.at[index]))
        body(ins, loaded, outs, refs)

    return pl.pallas_call(
        kernel,
        out_shape=tuple(outputs),
        in_specs=[smem_spec()]
        + [vmem_spec()] * len(inputs)
        + [pl.BlockSpec(memory_space=pl.ANY)] * len(arrays),
        out_specs=(vmem_spec(),) * len(outputs),
        scratch_shapes=[part.scratch() for part in parts]
        + [pltpu.SemaphoreType.DMA((len(parts),))]
        + list(scratch),
        compiler_params=pltpu.CompilerParams(vmem_limit_bytes=VMEM_BYTES),
        cost_estimate=cost(takes),
        name=name,
    )(place_now(), *inputs, *arrays)


def vmem_spec():
    return pl.BlockSpec(memory_space=pltpu.VMEM)


def smem_spec():
    return pl.BlockSpec(memory_space=pltpu.SMEM)


def seg_of_pos(ends_ref, pos):
    seg = jnp.zeros(pos.shape, jnp.int32)
    for slot in range(ends_ref.shape[0]):
        seg = seg + (ends_ref[slot] <= pos).astype(jnp.int32)
    return seg


def pair_dot(left, right, left_dim, right_dim):
    return lax.dot_general(
        left, right, (((left_dim,), (right_dim,)), ((), ())), preferred_element_type=jnp.float32
    )


def seg_tables(q_ends, k_ends, span):
    seg_q = seg_of_pos(q_ends, lax.broadcasted_iota(jnp.int32, (1, span), 1))
    seg_k = seg_of_pos(k_ends, lax.broadcasted_iota(jnp.int32, (span, 1), 0))
    return seg_q, seg_k


def masked_scores(keys, queries, seg_q, seg_k, first, causal):
    scores = pair_dot(keys, queries, 1, 1)
    allowed = seg_k == seg_q
    if causal:
        key_pos = lax.broadcasted_iota(jnp.int32, scores.shape, 0)
        query_pos = first + lax.broadcasted_iota(jnp.int32, scores.shape, 1)
        allowed = allowed & (key_pos <= query_pos)
    return jnp.where(allowed, scores, NEG)


def attn_forward_body(causal, width, q_ends, k_ends, q_ref, kv_ref, low_ref, full_ref, lse_ref):
    span = q_ref.shape[0]
    step = math.gcd(span, 256)
    heads = width // HEAD_DIM
    seg_q, seg_k = seg_tables(q_ends, k_ends, span)
    key_at = kv_ref.shape[1] - 2 * width
    scaled = q_ref[:, :width] * jnp.bfloat16(HEAD_DIM ** (-0.5))
    keys = kv_ref[:, key_at : key_at + width]
    values = kv_ref[:, key_at + width : key_at + 2 * width]
    for first in range(0, span, step):
        reach = first + step if causal else span
        parts = []
        for head in range(heads):
            cols = slice(head * HEAD_DIM, (head + 1) * HEAD_DIM)
            scores = masked_scores(
                keys[:reach, cols],
                scaled[first : first + step, cols],
                seg_q[:, first : first + step],
                seg_k[:reach],
                first,
                causal,
            )
            top = jnp.max(scores, axis=0, keepdims=True)
            probs = jnp.exp(scores - top)
            total = jnp.sum(probs, axis=0, keepdims=True)
            mixed = pair_dot(values[:reach, cols], probs.astype(jnp.bfloat16), 0, 0)
            parts.append(mixed / total)
            lse_ref[head : head + 1, first : first + step] = top + jnp.log(total)
        joined = jnp.concatenate(parts, axis=0).T
        full_ref[first : first + step, :] = joined
        low_ref[first : first + step, :] = joined.astype(jnp.bfloat16)


def attn_forward(q_ends, k_ends, queries, keys_values, width, causal):
    span = queries.shape[0]
    return pl.pallas_call(
        functools.partial(attn_forward_body, causal, width),
        out_shape=(
            jax.ShapeDtypeStruct((span, width), jnp.bfloat16),
            jax.ShapeDtypeStruct((span, width), jnp.float32),
            jax.ShapeDtypeStruct((width // HEAD_DIM, span), jnp.float32),
        ),
        in_specs=[smem_spec(), smem_spec()] + [vmem_spec()] * 2,
        out_specs=(vmem_spec(),) * 3,
        compiler_params=pltpu.CompilerParams(vmem_limit_bytes=VMEM_BYTES),
        cost_estimate=cost(8),
        name="attn_forward",
    )(q_ends, k_ends, queries, keys_values)


def attn_backward_body(
    causal,
    width,
    q_ends,
    k_ends,
    q_ref,
    kv_ref,
    up_ref,
    full_ref,
    lse_ref,
    dq_ref,
    dkv_ref,
    dk_sum,
    dv_sum,
):
    span = q_ref.shape[0]
    step = math.gcd(span, 256)
    heads = width // HEAD_DIM
    seg_q, seg_k = seg_tables(q_ends, k_ends, span)
    key_at = kv_ref.shape[1] - 2 * width
    scaled = q_ref[:, :width] * jnp.bfloat16(HEAD_DIM ** (-0.5))
    keys = kv_ref[:, key_at : key_at + width]
    values = kv_ref[:, key_at + width : key_at + 2 * width]
    upstream = up_ref[...]
    dk_sum[...] = jnp.zeros_like(dk_sum)
    dv_sum[...] = jnp.zeros_like(dv_sum)
    for first in range(0, span, step):
        reach = first + step if causal else span
        rows = slice(first, first + step)
        product = (upstream[rows].astype(jnp.float32) * full_ref[rows, :]).T
        parts = []
        for head in range(heads):
            cols = slice(head * HEAD_DIM, (head + 1) * HEAD_DIM)
            delta = jnp.sum(product[cols], axis=0, keepdims=True)
            scores = masked_scores(
                keys[:reach, cols], scaled[rows, cols], seg_q[:, rows], seg_k[:reach], first, causal
            )
            probs = jnp.exp(scores - lse_ref[head : head + 1, rows])
            dv_sum[head, :reach] += pair_dot(
                probs.astype(jnp.bfloat16), upstream[rows, cols], 1, 0
            )
            grad_probs = pair_dot(values[:reach, cols], upstream[rows, cols], 1, 1)
            grad_scores = (probs * (grad_probs - delta)).astype(jnp.bfloat16)
            dk_sum[head, :reach] += pair_dot(grad_scores, scaled[rows, cols], 1, 0)
            parts.append(pair_dot(keys[:reach, cols], grad_scores, 0, 0))
        joined = jnp.concatenate(parts, axis=0).T * HEAD_DIM ** (-0.5)
        dq_ref[rows, :] = joined.astype(jnp.bfloat16)
    sums = [dk_sum[head] for head in range(heads)] + [dv_sum[head] for head in range(heads)]
    dkv_ref[...] = jnp.concatenate(sums, axis=1).astype(jnp.bfloat16)


def attn_backward(q_ends, k_ends, queries, keys_values, upstream, full, lse, causal):
    span, width = upstream.shape
    heads = width // HEAD_DIM
    return pl.pallas_call(
        functools.partial(attn_backward_body, causal, width),
        out_shape=(
            jax.ShapeDtypeStruct((span, width), jnp.bfloat16),
            jax.ShapeDtypeStruct((span, 2 * width), jnp.bfloat16),
        ),
        in_specs=[smem_spec(), smem_spec()] + [vmem_spec()] * 5,
        out_specs=(vmem_spec(),) * 2,
        scratch_shapes=[pltpu.VMEM((heads, span, HEAD_DIM), jnp.float32)] * 2,
        compiler_params=pltpu.CompilerParams(vmem_limit_bytes=VMEM_BYTES),
        cost_estimate=cost(8),
        name="attn_backward",
    )(q_ends, k_ends, queries, keys_values, upstream, full, lse)


def exchange(blocks):
    return lax.all_to_all(blocks, "blk", 0, 0, tiled=True)


def as_rows(blocks):
    return blocks.reshape(blocks.shape[0] * blocks.shape[1], blocks.shape[2])


def as_blocks(rows):
    devices = lax.axis_size("blk")
    return rows.reshape(devices, rows.shape[0] // devices, rows.shape[1])


def write_blocks(out_ref, values, lanes, kind, width):
    span = values.shape[0] // lanes
    for group in range(WIDTH // width):
        for lane in range(lanes):
            out_ref[group * lanes + lane, :, kind * width : (kind + 1) * width] = values[
                lane * span : (lane + 1) * span, group * width : (group + 1) * width
            ]


def read_blocks(got_ref, lanes, kind, width):
    groups = got_ref.shape[0] // lanes
    cols = slice(kind * width, (kind + 1) * width)
    rows = [
        jnp.concatenate([got_ref[group * lanes + lane, :, cols] for group in range(groups)], axis=1)
        for lane in range(lanes)
    ]
    return jnp.concatenate(rows, axis=0)


def dot(left, right):
    return pair_dot(left, right, 1, 0)


def dot_back(left, right):
    return pair_dot(left, right, 1, 1)


def shape(*sizes, of=jnp.float32):
    return jax.ShapeDtypeStruct(sizes, of)


def normalize(values):
    center = values - jnp.mean(values, -1, keepdims=True)
    scale = lax.rsqrt(jnp.mean(center * center, -1, keepdims=True) + 1e-05)
    return center * scale, scale


def norm_back(upstream, normed, scale, gains_row):
    grad = upstream * gains_row
    return scale * (
        grad
        - jnp.mean(grad, -1, keepdims=True)
        - normed * jnp.mean(grad * normed, -1, keepdims=True)
    )


def project_blocks(inputs, parts, lanes, width, name):
    def body(ins, loaded, outs, _):
        for kind, weight in enumerate(loaded):
            write_blocks(
                outs[0], dot(ins[0][...], weight.value()).astype(jnp.bfloat16), lanes, kind, width
            )

    devices, span = lax.axis_size("blk"), inputs.shape[0] // lanes
    (blocks,) = call_with_parts(
        body,
        [inputs],
        parts,
        [shape(devices, span, width * len(parts), of=jnp.bfloat16)],
        name,
    )
    return blocks


def after_self(got, tokens, gains, biases, out_part, query_part, lanes, width):
    def body(ins, loaded, outs, _):
        got_ref, tokens_ref, gains_ref, biases_ref = ins
        low_ref, normed_ref, scale_ref, hidden_ref, blocks_ref = outs
        attended = read_blocks(got_ref, lanes, 0, width)
        low_ref[...] = attended
        resid = tokens_ref[...].astype(jnp.float32) + dot(attended, loaded[0].value())
        normed, scale = normalize(resid)
        normed_ref[...] = normed
        scale_ref[...] = scale
        hidden = (normed * gains_ref[0:1] + biases_ref[0:1]).astype(jnp.bfloat16)
        hidden_ref[...] = hidden
        query = dot(hidden, loaded[1].value()).astype(jnp.bfloat16)
        write_blocks(blocks_ref, query, lanes, 0, width)

    rows = tokens.shape[0]
    return call_with_parts(
        body,
        [got, tokens, gains, biases],
        [out_part, query_part],
        [
            shape(rows, WIDTH, of=jnp.bfloat16),
            shape(rows, WIDTH),
            shape(rows, 1),
            shape(rows, WIDTH, of=jnp.bfloat16),
            shape(*got.shape, of=jnp.bfloat16),
        ],
        "after_self",
    )


def feed_forward(got, normed_in, cotangent, gains, biases, out_part, in_parts, down, outs, up, lanes, width):
    pieces = len(in_parts)
    step = in_parts[0].width

    def body(ins, loaded, refs, scratch):
        got_ref, normed_in_ref, cot_ref, gains_ref, biases_ref = ins
        (
            output_ref,
            low_ref,
            mixed_ref,
            adapted_ref,
            dunder_ref,
            dab_ref,
            dcb_ref,
            dresid_ref,
            blocks_ref,
            norms_ref,
        ) = refs
        (slopes,) = scratch
        w_out, w_in = loaded[0], loaded[1 : 1 + pieces]
        w_down, w_ff, w_up = loaded[1 + pieces :]
        attended = read_blocks(got_ref, lanes, 0, width)
        low_ref[...] = attended
        hidden = normed_in_ref[...] * gains_ref[0:1] + biases_ref[0:1]
        normed_one, scale_one = normalize(hidden + dot(attended, w_out.value()))
        mixed = normed_one * gains_ref[1:2] + biases_ref[1:2]
        mixed_low = mixed.astype(jnp.bfloat16)
        mixed_ref[...] = mixed_low
        summed = mixed
        under = dot(mixed_low, w_down.value())
        gate = 1.0 / (1.0 + jnp.exp(-under))
        adapted = (under * gate).astype(jnp.bfloat16)
        adapted_ref[...] = adapted
        under_slope = gate * (1.0 + under * (1.0 - gate))
        summed = summed + 4.0 * dot(adapted, w_up.value())
        for piece in range(pieces):
            before = dot(mixed_low, w_in[piece].value())
            below = 0.5 + 0.5 * lax.erf(before * (0.5**0.5))
            slopes[piece] = below + before * jnp.exp(-0.5 * before * before) * (
                (2.0 * math.pi) ** -0.5
            )
            act = (before * below).astype(jnp.bfloat16)
            summed = summed + dot(act, w_ff[piece].value())
        normed_two, scale_two = normalize(summed)
        output_ref[...] = (normed_two * gains_ref[2:3] + biases_ref[2:3]).astype(jnp.bfloat16)
        upstream = cot_ref[...].astype(jnp.float32)
        norms_ref[0:1] = jnp.sum(upstream * normed_two, axis=0, keepdims=True)
        norms_ref[1:2] = jnp.sum(upstream, axis=0, keepdims=True)
        dz = norm_back(upstream, normed_two, scale_two, gains_ref[2:3])
        dzb = dz.astype(jnp.bfloat16)
        dab = (4.0 * dz).astype(jnp.bfloat16)
        dab_ref[...] = dab
        dunder = (under_slope * dot_back(dab, w_up.value())).astype(jnp.bfloat16)
        dunder_ref[...] = dunder
        dmixed = dz + dot_back(dunder, w_down.value())
        for piece in range(pieces):
            dpre = (slopes[piece] * dot_back(dzb, w_ff[piece].value())).astype(jnp.bfloat16)
            dmixed = dmixed + dot_back(dpre, w_in[piece].value())
        norms_ref[2:3] = jnp.sum(dmixed * normed_one, axis=0, keepdims=True)
        norms_ref[3:4] = jnp.sum(dmixed, axis=0, keepdims=True)
        dresid = norm_back(dmixed, normed_one, scale_one, gains_ref[1:2])
        dresid_ref[...] = dresid
        dcb = dresid.astype(jnp.bfloat16)
        dcb_ref[...] = dcb
        write_blocks(
            blocks_ref, dot_back(dcb, w_out.value()).astype(jnp.bfloat16), lanes, 0, width
        )

    rows = normed_in.shape[0]
    low = jnp.bfloat16

    def body_rows(ins, loaded, refs, scratch):
        whole_ff = loaded[2 + pieces]

        class Rows:
            def __init__(self, piece):
                self.piece = piece

            def value(self):
                return whole_ff.value()[self.piece * step : (self.piece + 1) * step]

        loaded = loaded[: 2 + pieces] + [[Rows(piece) for piece in range(pieces)], loaded[-1]]
        body(ins, loaded, refs, scratch)

    return call_with_parts(
        body_rows,
        [got, normed_in, cotangent, gains, biases],
        [out_part] + in_parts + [down, outs, up],
        [
            shape(rows, WIDTH, of=low),
            shape(rows, WIDTH, of=low),
            shape(rows, WIDTH, of=low),
            shape(rows, down.width, of=low),
            shape(rows, down.width, of=low),
            shape(rows, WIDTH, of=low),
            shape(rows, WIDTH, of=low),
            shape(rows, WIDTH),
            shape(*got.shape, of=low),
            shape(4, WIDTH),
        ],
        "feed_forward",
        [pltpu.VMEM((pieces, rows, step), jnp.float32)],
        20,
    )


def before_self(got, dresid, normed, scale, gains, query_part, out_part, lanes, width):
    def body(ins, loaded, outs, _):
        got_ref, dresid_ref, normed_ref, scale_ref, gains_ref = ins
        dcq_ref, dr_ref, dsb_ref, blocks_ref, norms_ref = outs
        dcq = read_blocks(got_ref, lanes, 0, width)
        dcq_ref[...] = dcq
        dhidden = dresid_ref[...] + dot_back(dcq, loaded[0].value())
        normed = normed_ref[...]
        norms_ref[0:1] = jnp.sum(dhidden * normed, axis=0, keepdims=True)
        norms_ref[1:2] = jnp.sum(dhidden, axis=0, keepdims=True)
        dr = norm_back(dhidden, normed, scale_ref[...], gains_ref[0:1])
        dr_ref[...] = dr
        dsb = dr.astype(jnp.bfloat16)
        dsb_ref[...] = dsb
        grad = dot_back(dsb, loaded[1].value()).astype(jnp.bfloat16)
        write_blocks(blocks_ref, grad, lanes, 0, width)

    rows = dresid.shape[0]
    return call_with_parts(
        body,
        [got, dresid, normed, scale, gains],
        [query_part, out_part],
        [
            shape(rows, WIDTH, of=jnp.bfloat16),
            shape(rows, WIDTH),
            shape(rows, WIDTH, of=jnp.bfloat16),
            shape(*got.shape, of=jnp.bfloat16),
            shape(2, WIDTH),
        ],
        "before_self",
    )


def input_grad(got, start, parts, lanes, width, name):
    def body(ins, loaded, outs, _):
        total = None
        for kind, weight in enumerate(loaded):
            term = dot_back(read_blocks(ins[0], lanes, kind, width), weight.value())
            total = term if total is None else total + term
        outs[0][...] = total if len(ins) == 1 else total + ins[1][...]

    rows = got.shape[1] * lanes
    return call_with_parts(
        body,
        [got] if start is None else [got, start],
        parts,
        [shape(rows, WIDTH)],
        name,
    )


def sum_everywhere(values, stages):
    if not paired():
        return lax.psum(values, ("dp", "blk"))
    values = after(values, stages[0])
    values = values + swap_core(values)
    for step, bit in enumerate((1, 2, 4, 8)):
        if step + 1 < len(stages):
            values = after(values, stages[step + 1])
        values = values + flip(values, bit)
    return values


def shards(
    tokens,
    encoder,
    cotangent,
    self_in,
    self_out,
    cross_q,
    cross_kv,
    cross_out,
    ffn_in,
    ffn_out,
    adapt_down,
    adapt_up,
    norm_gain,
    norm_bias,
    tgt_lengths,
    src_lengths,
):
    lanes, span, _ = tokens.shape
    rows = lanes * span
    width = WIDTH * lanes // lax.axis_size("blk")
    own_row = lax.axis_index("blk") % lanes
    tgt_ends = jnp.cumsum(lax.dynamic_index_in_dim(tgt_lengths, own_row, 0, keepdims=False))
    src_ends = jnp.cumsum(lax.dynamic_index_in_dim(src_lengths, own_row, 0, keepdims=False))
    flat_tokens = tokens.reshape(rows, WIDTH)
    flat_encoder = encoder.reshape(rows, WIDTH)

    half = 3 * WIDTH // 2
    self_x, self_y = gather_flips([self_in[:, :half], self_in[:, half:]], "xy")
    self_parts = [
        columns_of((self_x, 0, WIDTH)),
        columns_of((self_x, WIDTH, WIDTH // 2), (self_y, 0, WIDTH // 2)),
        columns_of((self_y, WIDTH // 2, WIDTH)),
    ]
    shards_x = jnp.concatenate([cross_kv[:, :WIDTH], self_out], axis=1)
    shards_y = jnp.concatenate([cross_kv[:, WIDTH:], cross_q], axis=1)
    shards_x, shards_y = after((shards_x, shards_y), self_x.stages[0], self_y.stages[0])
    pair_x, pair_y = gather_flips([shards_x, shards_y], "xy")
    pair_parts = [columns_of((pair_x, 0, WIDTH)), columns_of((pair_y, 0, WIDTH))]
    self_out_part = columns_of((pair_x, WIDTH, WIDTH))
    query_part = columns_of((pair_y, WIDTH, WIDTH))
    frozen = [ffn_in, adapt_down, ffn_out, adapt_up, cross_out]
    frozen = after(frozen, self_x.stages[0], self_y.stages[0])
    packed = gather_packed(frozen) if paired() else None

    self_qkv = as_rows(
        exchange(
            project_blocks(
                after(flat_tokens, pair_x.stages[0], pair_y.stages[0]),
                self_parts,
                lanes,
                width,
                "self_in",
            )
        )
    )
    self_qkv = after(self_qkv, pair_x.stages[2], pair_y.stages[2])
    cross_kv_own = as_rows(
        exchange(project_blocks(flat_encoder, pair_parts, lanes, width, "cross_kv"))
    )
    self_mid, self_full, self_lse = attn_forward(
        tgt_ends, tgt_ends, self_qkv, self_qkv, width, True
    )
    self_low, normed, scale, hidden_low, query_blocks = after_self(
        exchange(as_blocks(self_mid)),
        flat_tokens,
        norm_gain,
        norm_bias,
        self_out_part,
        query_part,
        lanes,
        width,
    )
    ready = after(packed, query_blocks) if paired() else None
    ff_parts, down_parts, ffo_parts, up_parts, (cross_out_part,) = packed_parts(frozen, ready)
    cross_q_own = as_rows(exchange(query_blocks))
    cross_mid, cross_full, cross_lse = attn_forward(
        tgt_ends, src_ends, cross_q_own, cross_kv_own, width, False
    )
    (
        output,
        cross_low,
        mixed_low,
        adapter_low,
        grad_under,
        adapt_low,
        cross_branch_low,
        grad_resid_two,
        cross_blocks,
        norms_high,
    ) = feed_forward(
        exchange(as_blocks(cross_mid)),
        normed,
        cotangent.reshape(rows, WIDTH),
        norm_gain,
        norm_bias,
        cross_out_part,
        ff_parts,
        down_parts[0],
        ffo_parts[0],
        up_parts[0],
        lanes,
        width,
    )
    (grad_cross_out, grad_adapt_down, grad_adapt_up), _ = weight_grads(
        [(cross_low, cross_branch_low), (mixed_low, grad_under), (adapter_low, adapt_low)]
    )
    cross_dq, cross_dkv = attn_backward(
        tgt_ends,
        src_ends,
        cross_q_own,
        cross_kv_own,
        as_rows(exchange(cross_blocks)),
        cross_full,
        cross_lse,
        False,
    )
    cq_low, grad_resid_one, self_branch_low, self_blocks, norms_low = before_self(
        exchange(as_blocks(cross_dq)),
        grad_resid_two,
        normed,
        scale,
        norm_gain,
        query_part,
        self_out_part,
        lanes,
        width,
    )
    cross_got = exchange(as_blocks(cross_dkv))
    ckv_low = cross_got.reshape(-1, lanes, span, 2, width).transpose(1, 2, 3, 0, 4)
    (grad_cross_kv,), _ = weight_grads(
        [(flat_encoder, ckv_low.reshape(rows, 2 * WIDTH))]
    )
    (encoder_grad,) = input_grad(cross_got, None, pair_parts, lanes, width, "encoder_grad")
    (grad_cross_q, grad_self_out), _ = weight_grads(
        [(hidden_low, cq_low), (self_low, self_branch_low)]
    )
    self_dq, self_dkv = attn_backward(
        tgt_ends,
        tgt_ends,
        self_qkv,
        self_qkv,
        as_rows(exchange(self_blocks)),
        self_full,
        self_lse,
        True,
    )
    self_got = exchange(as_blocks(jnp.concatenate([self_dq, self_dkv], axis=1)))
    triple_low = self_got.reshape(-1, lanes, span, 3, width).transpose(1, 2, 3, 0, 4)
    (grad_self_in,), stages = weight_grads([(flat_tokens, triple_low.reshape(rows, 3 * WIDTH))])
    (tokens_grad,) = input_grad(
        after(self_got, stages[0]), grad_resid_one, self_parts, lanes, width, "tokens_grad"
    )
    norms = sum_everywhere(jnp.concatenate([norms_low, norms_high], axis=0), stages)
    return (
        output.reshape(lanes, span, WIDTH),
        tokens_grad.reshape(lanes, span, WIDTH),
        encoder_grad.reshape(lanes, span, WIDTH),
        grad_self_in,
        grad_self_out,
        grad_cross_q,
        grad_cross_kv,
        grad_cross_out,
        grad_adapt_down,
        grad_adapt_up,
        jnp.stack([norms[0], norms[4], norms[2]]),
        jnp.stack([norms[1], norms[5], norms[3]]),
    )


def solution(mesh):
    placed = (
        P("dp", "blk", None),
        P("dp", "blk", None),
        P("dp", "blk", None),
        P("blk", None),
        P("blk", None),
        P("blk", None),
        P("blk", None),
        P("blk", None),
        P("blk", None),
        P("blk", None),
        P("blk", None),
        P("blk", None),
        P(),
        P(),
        P("dp", None),
        P("dp", None),
    )
    return jax.shard_map(
        shards,
        mesh=mesh,
        in_specs=placed,
        out_specs=(
            P("dp", "blk", None),
            P("dp", "blk", None),
            P("dp", "blk", None),
            P("blk", None),
            P("blk", None),
            P("blk", None),
            P("blk", None),
            P("blk", None),
            P("blk", None),
            P("blk", None),
            P(),
            P(),
        ),
        check_vma=False,
    )
```

```python
import functools
import math

import jax
import jax.numpy as jnp
from jax import lax
from jax.experimental import pallas as pl
from jax.experimental.pallas import tpu as pltpu
from jax.sharding import PartitionSpec as P

HEADS = 16
HEAD_DIM = 64
WIDTH = HEADS * HEAD_DIM


NEG = -1e30
VMEM_BYTES = 56 * 1024 * 1024


def cost(microseconds):
    return pl.CostEstimate(
        flops=int(microseconds * 1.0e9),
        bytes_accessed=int(microseconds * 3.5e6),
        transcendentals=0,
    )


def paired():
    return lax.axis_size("blk") == 16 and lax.axis_size("dp") == 2


def swap_core(block):
    cores = lax.axis_size("dp")
    return lax.ppermute(block, "dp", [(i ^ 1, i) for i in range(cores)])


def flip(block, bit):
    chips = lax.axis_size("blk")
    return lax.ppermute(block, "blk", [(i ^ bit, i) for i in range(chips)])


def rotate_z(block, distance):
    chips = lax.axis_size("blk")
    return lax.ppermute(block, "blk", [((i + 4 * distance) % chips, i) for i in range(chips)])


def own_half(values, which):
    half = values.shape[1] // 2
    return lax.dynamic_slice_in_dim(values, which * half, half, 1)


def scatter_chips(terms, orders, hold, held_stage):
    own = lax.axis_index("blk")
    z, y, x = own // 4, (own // 2) % 2, own % 2

    def fold(blocks, axis, place, bit):
        kept = lax.dynamic_index_in_dim(blocks, place, axis, keepdims=False)
        sent = lax.dynamic_index_in_dim(blocks, 1 - place, axis, keepdims=False)
        got = flip(sent, bit)
        return (kept.astype(jnp.float32) + got.astype(jnp.float32)).astype(jnp.bfloat16)

    def held(terms, stage):
        return after(terms, hold) if hold is not None and stage == held_stage else terms

    terms = [blocks.reshape(4, 2, 2, *blocks.shape[1:]) for blocks in terms]
    stages = [terms[0]]
    terms = held(terms, 0)
    terms = [
        fold(blocks, 1, y, 2) if first_y else fold(blocks, 2, x, 1)
        for blocks, first_y in zip(terms, orders)
    ]
    stages.append(terms[0])
    terms = held(terms, 1)
    terms = [
        fold(blocks, 1, x, 1) if first_y else fold(blocks, 1, y, 2)
        for blocks, first_y in zip(terms, orders)
    ]
    stages.append(terms[0])
    terms = held(terms, 2)
    totals = []
    for blocks in terms:
        total = lax.dynamic_index_in_dim(blocks, z, 0, keepdims=False).astype(jnp.float32)
        for distance in (1, 2, 3):
            sent = lax.dynamic_index_in_dim(blocks, (z - distance) % 4, 0, keepdims=False)
            total = total + rotate_z(sent, distance).astype(jnp.float32)
        totals.append(total)
    return totals, stages


CHUNK = 256


def grad_terms(pairs):
    if not paired():
        return None
    core = lax.axis_index("dp")
    packed = []
    for inputs, upstream in pairs:
        both = jnp.concatenate([inputs, swap_core(inputs)], axis=0)
        half = jnp.concatenate(
            [own_half(upstream, core), swap_core(own_half(upstream, 1 - core))], axis=0
        )
        term = lax.dot_general(
            both, half, (((0,), (0,)), ((), ())), preferred_element_type=jnp.float32
        ).astype(jnp.bfloat16)
        rows = term.shape[0] // 16
        chunks = term.shape[1] // CHUNK
        packed += [
            term[:, c * CHUNK : (c + 1) * CHUNK].reshape(16, rows, CHUNK) for c in range(chunks)
        ]
    cut = len(packed) // 2
    return [jnp.concatenate(packed[:cut], axis=1), jnp.concatenate(packed[cut:], axis=1)]


def reduce_terms(pairs, terms, hold=None, held_stage=0):
    if not paired():
        return [weight_grad(inputs, upstream) for inputs, upstream in pairs], [pairs[0][1]]
    core = lax.axis_index("dp")
    totals, stages = scatter_chips(terms, [True, False], hold, held_stage)
    mine = jnp.concatenate(totals, axis=0).astype(jnp.bfloat16)
    other = swap_core(mine)
    low = jnp.where(core == 0, mine, other).astype(jnp.float32)
    high = jnp.where(core == 0, other, mine).astype(jnp.float32)
    found, place = [], 0
    for inputs, upstream in pairs:
        rows = inputs.shape[1] // 16
        chunks = upstream.shape[1] // 2 // CHUNK
        spots = [slice(place + c * rows, place + (c + 1) * rows) for c in range(chunks)]
        found.append(
            jnp.concatenate([low[spot] for spot in spots] + [high[spot] for spot in spots], axis=1)
        )
        place += rows * chunks
    return found, stages


def weight_grad(inputs, upstream):
    scattered = lax.psum_scatter(
        lax.dot_general(
            inputs, upstream, (((0,), (0,)), ((), ())), preferred_element_type=jnp.float32
        ).astype(jnp.bfloat16),
        "blk",
        scatter_dimension=0,
        tiled=True,
    )
    return lax.psum(scattered, "dp").astype(jnp.float32)


class Source:
    def __init__(self, kind, arrays, first_flip="x", column=None):
        self.kind, self.arrays, self.first_flip = kind, arrays, first_flip
        self.stages = arrays[:1] * 3 if column is None else [column] + arrays[:2]


class Part:
    def __init__(self, rows, width, spots):
        self.rows, self.width, self.spots = rows, width, spots

    def scratch(self):
        return pltpu.VMEM((4, 2, 2, 2, self.rows // 32, self.width), jnp.bfloat16)

    def start(self, refs_of, place, dst, sem):
        z, y, x, core = [place[axis] for axis in range(4)]
        high = self.rows // 32
        for source, first_row, first_col, at_col, width in self.spots:
            refs = refs_of(source)
            cols = slice(first_col, first_col + width)
            into = slice(at_col, at_col + width)
            if source.kind == "whole":
                pltpu.make_async_copy(
                    refs[0].at[:, :, :, :, :, cols], dst.at[:, :, :, :, :, into], sem
                ).start()
            elif source.kind == "cores":
                for which in range(2):
                    owner = core if which == 0 else 1 - core
                    pltpu.make_async_copy(
                        refs[which].at[:, :, :, first_row : first_row + high, cols],
                        dst.at[:, :, :, owner, :, into],
                        sem,
                    ).start()
            else:
                for which in range(4):
                    owner = core if which < 2 else 1 - core
                    for near in range(2):
                        if source.first_flip == "x":
                            at_x = x if near == 0 else 1 - x
                            at_y = y if which % 2 == 0 else 1 - y
                        else:
                            at_y = y if near == 0 else 1 - y
                            at_x = x if which % 2 == 0 else 1 - x
                        for up in range(4):
                            at_z = lax.rem(z + up, 4)
                            pltpu.make_async_copy(
                                refs[which].at[near, up, :, cols],
                                dst.at[at_z, at_y, at_x, owner, :, into],
                                sem,
                            ).start()


def after(value, *others):
    return lax.optimization_barrier((value, *others))[0]


def gather_flips(shards, first_flips):
    if not paired():
        full = [lax.all_gather(shard, "blk", axis=0, tiled=True) for shard in shards]
        return [
            Source("whole", [array.reshape(4, 2, 2, 2, array.shape[0] // 32, array.shape[1])])
            for array in full
        ]
    core = lax.axis_index("dp")
    columns = []
    for shard in shards:
        rows = shard.shape[0]
        own = lax.dynamic_slice_in_dim(shard, core * (rows // 2), rows // 2, 0)
        columns.append(
            jnp.stack([own] + [rotate_z(own, distance) for distance in (1, 2, 3)])
        )
    sources, bits = [], {"x": (1, 2), "y": (2, 1)}
    planes = [
        jnp.stack([column, flip(column, bits[first][0])])
        for column, first in zip(columns, first_flips)
    ]
    for column, plane, first in zip(columns, planes, first_flips):
        beyond = flip(plane, bits[first][1])
        sources.append(
            Source("flips", [plane, beyond, swap_core(plane), swap_core(beyond)], first, column)
        )
    return sources


def columns_of(*pieces):
    spots, place = [], 0
    for source, first, width in pieces:
        spots.append((source, 0, first, place, width))
        place += width
    return Part(1024, place, spots)


PACK = 512


def gather_packed(shards):
    core = lax.axis_index("dp")
    packed = []
    for shard in shards:
        high = shard.shape[0] // 2
        own = lax.dynamic_slice_in_dim(shard, core * high, high, 0)
        packed += [own[:, first : first + PACK] for first in range(0, shard.shape[1], PACK)]
    return lax.all_gather(jnp.concatenate(packed, axis=0), "blk", axis=0)


def packed_parts(shards, mine):
    if not paired():
        found = []
        for source, shard in zip(gather_flips(shards, "x" * len(shards)), shards):
            rows, columns = 32 * source.arrays[0].shape[4], shard.shape[1]
            step = min(columns, 1024)
            found.append(
                [
                    Part(rows, step, [(source, 0, first, 0, step)])
                    for first in range(0, columns, step)
                ]
            )
        return found
    spots, place = [], 0
    for shard in shards:
        high = shard.shape[0] // 2
        places = []
        for first in range(0, shard.shape[1], PACK):
            places.append(place)
            place += high
        spots.append((shard.shape[0] * 16, places))
    mine = mine.reshape(4, 2, 2, place, PACK)
    source = Source("cores", [mine, swap_core(mine)])
    found = []
    for rows, places in spots:
        parts = []
        for first in range(0, len(places), 2):
            two = places[first : first + 2]
            parts.append(
                Part(
                    rows,
                    PACK * len(two),
                    [(source, row, 0, PACK * side, PACK) for side, row in enumerate(two)],
                )
            )
        found.append(parts)
    return found


def place_now():
    own, core = lax.axis_index("blk"), lax.axis_index("dp")
    return jnp.stack([own // 4, (own // 2) % 2, own % 2, core]).astype(jnp.int32)


class Loaded:
    def __init__(self, part, dst, sem):
        self.part, self.dst, self.sem, self.here = part, dst, sem, False

    def value(self):
        if not self.here:
            pltpu.make_async_copy(self.dst, self.dst, self.sem).wait()
            self.here = True
        return self.dst[...].reshape(self.part.rows, self.part.width)


def call_with_parts(body, inputs, parts, outputs, name, scratch=(), takes=5):
    sources = []
    for part in parts:
        sources += [spot[0] for spot in part.spots if spot[0] not in sources]
    arrays = [array for source in sources for array in source.arrays]

    def kernel(place, *refs):
        refs = list(refs)
        ins = [refs.pop(0) for _ in inputs]
        pieces = [[refs.pop(0) for _ in source.arrays] for source in sources]
        outs = [refs.pop(0) for _ in outputs]
        dsts = [refs.pop(0) for _ in parts]
        sems = refs.pop(0)
        loaded = []
        for index, part in enumerate(parts):
            part.start(
                lambda source: pieces[sources.index(source)], place, dsts[index], sems.at[index]
            )
            loaded.append(Loaded(part, dsts[index], sems.at[index]))
        body(ins, loaded, outs, refs)

    return pl.pallas_call(
        kernel,
        out_shape=tuple(outputs),
        in_specs=[smem_spec()]
        + [vmem_spec()] * len(inputs)
        + [pl.BlockSpec(memory_space=pl.ANY)] * len(arrays),
        out_specs=(vmem_spec(),) * len(outputs),
        scratch_shapes=[part.scratch() for part in parts]
        + [pltpu.SemaphoreType.DMA((len(parts),))]
        + list(scratch),
        compiler_params=pltpu.CompilerParams(vmem_limit_bytes=VMEM_BYTES),
        cost_estimate=cost(takes),
        name=name,
    )(place_now(), *inputs, *arrays)


def vmem_spec():
    return pl.BlockSpec(memory_space=pltpu.VMEM)


def smem_spec():
    return pl.BlockSpec(memory_space=pltpu.SMEM)


def seg_of_pos(ends_ref, pos):
    seg = jnp.zeros(pos.shape, jnp.int32)
    for slot in range(ends_ref.shape[0]):
        seg = seg + (ends_ref[slot] <= pos).astype(jnp.int32)
    return seg


def pair_dot(left, right, left_dim, right_dim):
    return lax.dot_general(
        left, right, (((left_dim,), (right_dim,)), ((), ())), preferred_element_type=jnp.float32
    )


def seg_tables(q_ends, k_ends, span):
    seg_q = seg_of_pos(q_ends, lax.broadcasted_iota(jnp.int32, (1, span), 1))
    seg_k = seg_of_pos(k_ends, lax.broadcasted_iota(jnp.int32, (span, 1), 0))
    return seg_q, seg_k


def masked_scores(keys, queries, seg_q, seg_k, first, causal):
    scores = pair_dot(keys, queries, 1, 1)
    allowed = seg_k == seg_q
    if causal:
        key_pos = lax.broadcasted_iota(jnp.int32, scores.shape, 0)
        query_pos = first + lax.broadcasted_iota(jnp.int32, scores.shape, 1)
        allowed = allowed & (key_pos <= query_pos)
    return jnp.where(allowed, scores, NEG)


def attn_forward_body(causal, width, q_ends, k_ends, q_ref, kv_ref, low_ref, full_ref, lse_ref):
    span = q_ref.shape[0]
    step = math.gcd(span, 256)
    heads = width // HEAD_DIM
    seg_q, seg_k = seg_tables(q_ends, k_ends, span)
    key_at = kv_ref.shape[1] - 2 * width
    scaled = q_ref[:, :width] * jnp.bfloat16(HEAD_DIM ** (-0.5))
    keys = kv_ref[:, key_at : key_at + width]
    values = kv_ref[:, key_at + width : key_at + 2 * width]
    for first in range(0, span, step):
        reach = first + step if causal else span
        parts = []
        for head in range(heads):
            cols = slice(head * HEAD_DIM, (head + 1) * HEAD_DIM)
            scores = masked_scores(
                keys[:reach, cols],
                scaled[first : first + step, cols],
                seg_q[:, first : first + step],
                seg_k[:reach],
                first,
                causal,
            )
            top = jnp.max(scores, axis=0, keepdims=True)
            probs = jnp.exp(scores - top)
            total = jnp.sum(probs, axis=0, keepdims=True)
            mixed = pair_dot(values[:reach, cols], probs.astype(jnp.bfloat16), 0, 0)
            parts.append(mixed / total)
            lse_ref[head : head + 1, first : first + step] = top + jnp.log(total)
        joined = jnp.concatenate(parts, axis=0).T
        full_ref[first : first + step, :] = joined
        low_ref[first : first + step, :] = joined.astype(jnp.bfloat16)


def attn_forward(q_ends, k_ends, queries, keys_values, width, causal):
    span = queries.shape[0]
    return pl.pallas_call(
        functools.partial(attn_forward_body, causal, width),
        out_shape=(
            jax.ShapeDtypeStruct((span, width), jnp.bfloat16),
            jax.ShapeDtypeStruct((span, width), jnp.float32),
            jax.ShapeDtypeStruct((width // HEAD_DIM, span), jnp.float32),
        ),
        in_specs=[smem_spec(), smem_spec()] + [vmem_spec()] * 2,
        out_specs=(vmem_spec(),) * 3,
        compiler_params=pltpu.CompilerParams(vmem_limit_bytes=VMEM_BYTES),
        cost_estimate=cost(8),
        name="attn_forward",
    )(q_ends, k_ends, queries, keys_values)


def attn_backward_body(
    causal,
    width,
    q_ends,
    k_ends,
    q_ref,
    kv_ref,
    up_ref,
    full_ref,
    lse_ref,
    *outs,
):
    dq_ref, dkv_ref = outs[0], outs[-3]
    dk_sum, dv_sum = outs[-2:]
    span = q_ref.shape[0]
    step = math.gcd(span, 256)
    heads = width // HEAD_DIM
    seg_q, seg_k = seg_tables(q_ends, k_ends, span)
    key_at = kv_ref.shape[1] - 2 * width
    scaled = q_ref[:, :width] * jnp.bfloat16(HEAD_DIM ** (-0.5))
    keys = kv_ref[:, key_at : key_at + width]
    values = kv_ref[:, key_at + width : key_at + 2 * width]
    upstream = up_ref[...]
    dk_sum[...] = jnp.zeros_like(dk_sum)
    dv_sum[...] = jnp.zeros_like(dv_sum)
    for first in range(0, span, step):
        reach = first + step if causal else span
        rows = slice(first, first + step)
        product = (upstream[rows].astype(jnp.float32) * full_ref[rows, :]).T
        parts = []
        for head in range(heads):
            cols = slice(head * HEAD_DIM, (head + 1) * HEAD_DIM)
            delta = jnp.sum(product[cols], axis=0, keepdims=True)
            scores = masked_scores(
                keys[:reach, cols], scaled[rows, cols], seg_q[:, rows], seg_k[:reach], first, causal
            )
            probs = jnp.exp(scores - lse_ref[head : head + 1, rows])
            dv_sum[head, :reach] += pair_dot(
                probs.astype(jnp.bfloat16), upstream[rows, cols], 1, 0
            )
            grad_probs = pair_dot(values[:reach, cols], upstream[rows, cols], 1, 1)
            grad_scores = (probs * (grad_probs - delta)).astype(jnp.bfloat16)
            dk_sum[head, :reach] += pair_dot(grad_scores, scaled[rows, cols], 1, 0)
            parts.append(pair_dot(keys[:reach, cols], grad_scores, 0, 0))
        joined = jnp.concatenate(parts, axis=0).T * HEAD_DIM ** (-0.5)
        dq_ref[rows, :width] = joined.astype(jnp.bfloat16)
    sums = [dk_sum[head] for head in range(heads)] + [dv_sum[head] for head in range(heads)]
    kv_at = dkv_ref.shape[1] - 2 * width
    dkv_ref[:, kv_at:] = jnp.concatenate(sums, axis=1).astype(jnp.bfloat16)


def attn_backward(
    q_ends, k_ends, queries, keys_values, upstream, full, lse, causal, joined=False
):
    span, width = upstream.shape
    kinds = [3] if joined else [1, 2]
    heads = width // HEAD_DIM
    return pl.pallas_call(
        functools.partial(attn_backward_body, causal, width),
        out_shape=[jax.ShapeDtypeStruct((span, kind * width), jnp.bfloat16) for kind in kinds],
        in_specs=[smem_spec(), smem_spec()] + [vmem_spec()] * 5,
        out_specs=[vmem_spec()] * len(kinds),
        scratch_shapes=[pltpu.VMEM((heads, span, HEAD_DIM), jnp.float32)] * 2,
        compiler_params=pltpu.CompilerParams(vmem_limit_bytes=VMEM_BYTES),
        cost_estimate=cost(8),
        name="attn_backward",
    )(q_ends, k_ends, queries, keys_values, upstream, full, lse)


def exchange(blocks):
    return lax.all_to_all(blocks, "blk", 0, 0, tiled=True)


def as_rows(blocks):
    return blocks.reshape(blocks.shape[0] * blocks.shape[1], blocks.shape[2])


def as_blocks(rows):
    devices = lax.axis_size("blk")
    return rows.reshape(devices, rows.shape[0] // devices, rows.shape[1])


def write_blocks(out_ref, values, lanes, kind, width):
    span = values.shape[0] // lanes
    for group in range(WIDTH // width):
        for lane in range(lanes):
            out_ref[group * lanes + lane, :, kind * width : (kind + 1) * width] = values[
                lane * span : (lane + 1) * span, group * width : (group + 1) * width
            ]


def read_blocks(got_ref, lanes, kind, width):
    groups = got_ref.shape[0] // lanes
    cols = slice(kind * width, (kind + 1) * width)
    rows = [
        jnp.concatenate([got_ref[group * lanes + lane, :, cols] for group in range(groups)], axis=1)
        for lane in range(lanes)
    ]
    return jnp.concatenate(rows, axis=0)


def dot(left, right):
    return pair_dot(left, right, 1, 0)


def dot_back(left, right):
    return pair_dot(left, right, 1, 1)


def shape(*sizes, of=jnp.float32):
    return jax.ShapeDtypeStruct(sizes, of)


def normalize(values):
    center = values - jnp.mean(values, -1, keepdims=True)
    scale = lax.rsqrt(jnp.mean(center * center, -1, keepdims=True) + 1e-05)
    return center * scale, scale


def norm_back(upstream, normed, scale, gains_row):
    grad = upstream * gains_row
    return scale * (
        grad
        - jnp.mean(grad, -1, keepdims=True)
        - normed * jnp.mean(grad * normed, -1, keepdims=True)
    )


def project_blocks(inputs, parts, lanes, width, name):
    def body(ins, loaded, outs, _):
        for kind, weight in enumerate(loaded):
            write_blocks(
                outs[0], dot(ins[0][...], weight.value()).astype(jnp.bfloat16), lanes, kind, width
            )

    devices, span = lax.axis_size("blk"), inputs.shape[0] // lanes
    (blocks,) = call_with_parts(
        body,
        [inputs],
        parts,
        [shape(devices, span, width * len(parts), of=jnp.bfloat16)],
        name,
    )
    return blocks


def after_self(got, tokens, gains, biases, out_part, query_part, lanes, width):
    def body(ins, loaded, outs, _):
        got_ref, tokens_ref, gains_ref, biases_ref = ins
        low_ref, normed_ref, scale_ref, hidden_ref, blocks_ref = outs
        attended = read_blocks(got_ref, lanes, 0, width)
        low_ref[...] = attended
        resid = tokens_ref[...].astype(jnp.float32) + dot(attended, loaded[0].value())
        normed, scale = normalize(resid)
        normed_ref[...] = normed
        scale_ref[...] = scale
        hidden = (normed * gains_ref[0:1] + biases_ref[0:1]).astype(jnp.bfloat16)
        hidden_ref[...] = hidden
        query = dot(hidden, loaded[1].value()).astype(jnp.bfloat16)
        write_blocks(blocks_ref, query, lanes, 0, width)

    rows = tokens.shape[0]
    return call_with_parts(
        body,
        [got, tokens, gains, biases],
        [out_part, query_part],
        [
            shape(rows, WIDTH, of=jnp.bfloat16),
            shape(rows, WIDTH),
            shape(rows, 1),
            shape(rows, WIDTH, of=jnp.bfloat16),
            shape(*got.shape, of=jnp.bfloat16),
        ],
        "after_self",
    )


def feed_forward(got, normed_in, cotangent, gains, biases, out_part, in_parts, down, outs, up, lanes, width):
    pieces = len(in_parts)
    step = in_parts[0].width

    def body(ins, loaded, refs, scratch):
        got_ref, normed_in_ref, cot_ref, gains_ref, biases_ref = ins
        (
            output_ref,
            low_ref,
            mixed_ref,
            adapted_ref,
            dunder_ref,
            dab_ref,
            dcb_ref,
            dresid_ref,
            blocks_ref,
            norms_ref,
        ) = refs
        (slopes,) = scratch
        w_out, w_in = loaded[0], loaded[1 : 1 + pieces]
        w_down, w_ff, w_up = loaded[1 + pieces :]
        attended = read_blocks(got_ref, lanes, 0, width)
        low_ref[...] = attended
        hidden = normed_in_ref[...] * gains_ref[0:1] + biases_ref[0:1]
        normed_one, scale_one = normalize(hidden + dot(attended, w_out.value()))
        mixed = normed_one * gains_ref[1:2] + biases_ref[1:2]
        mixed_low = mixed.astype(jnp.bfloat16)
        mixed_ref[...] = mixed_low
        summed = mixed
        under = dot(mixed_low, w_down.value())
        gate = 1.0 / (1.0 + jnp.exp(-under))
        adapted = (under * gate).astype(jnp.bfloat16)
        adapted_ref[...] = adapted
        under_slope = gate * (1.0 + under * (1.0 - gate))
        summed = summed + 4.0 * dot(adapted, w_up.value())
        for piece in range(pieces):
            before = dot(mixed_low, w_in[piece].value())
            below = 0.5 + 0.5 * lax.erf(before * (0.5**0.5))
            slopes[piece] = below + before * jnp.exp(-0.5 * before * before) * (
                (2.0 * math.pi) ** -0.5
            )
            act = (before * below).astype(jnp.bfloat16)
            summed = summed + dot(act, w_ff[piece].value())
        normed_two, scale_two = normalize(summed)
        output_ref[...] = (normed_two * gains_ref[2:3] + biases_ref[2:3]).astype(jnp.bfloat16)
        upstream = cot_ref[...].astype(jnp.float32)
        norms_ref[0:1] = jnp.sum(upstream * normed_two, axis=0, keepdims=True)
        norms_ref[1:2] = jnp.sum(upstream, axis=0, keepdims=True)
        dz = norm_back(upstream, normed_two, scale_two, gains_ref[2:3])
        dzb = dz.astype(jnp.bfloat16)
        dab = (4.0 * dz).astype(jnp.bfloat16)
        dab_ref[...] = dab
        dunder = (under_slope * dot_back(dab, w_up.value())).astype(jnp.bfloat16)
        dunder_ref[...] = dunder
        dmixed = dz + dot_back(dunder, w_down.value())
        for piece in range(pieces):
            dpre = (slopes[piece] * dot_back(dzb, w_ff[piece].value())).astype(jnp.bfloat16)
            dmixed = dmixed + dot_back(dpre, w_in[piece].value())
        norms_ref[2:3] = jnp.sum(dmixed * normed_one, axis=0, keepdims=True)
        norms_ref[3:4] = jnp.sum(dmixed, axis=0, keepdims=True)
        dresid = norm_back(dmixed, normed_one, scale_one, gains_ref[1:2])
        dresid_ref[...] = dresid
        dcb = dresid.astype(jnp.bfloat16)
        dcb_ref[...] = dcb
        write_blocks(
            blocks_ref, dot_back(dcb, w_out.value()).astype(jnp.bfloat16), lanes, 0, width
        )

    rows = normed_in.shape[0]
    low = jnp.bfloat16

    def body_rows(ins, loaded, refs, scratch):
        whole_ff = loaded[2 + pieces]

        class Rows:
            def __init__(self, piece):
                self.piece = piece

            def value(self):
                return whole_ff.value()[self.piece * step : (self.piece + 1) * step]

        loaded = loaded[: 2 + pieces] + [[Rows(piece) for piece in range(pieces)], loaded[-1]]
        body(ins, loaded, refs, scratch)

    return call_with_parts(
        body_rows,
        [got, normed_in, cotangent, gains, biases],
        [out_part] + in_parts + [down, outs, up],
        [
            shape(rows, WIDTH, of=low),
            shape(rows, WIDTH, of=low),
            shape(rows, WIDTH, of=low),
            shape(rows, down.width, of=low),
            shape(rows, down.width, of=low),
            shape(rows, WIDTH, of=low),
            shape(rows, WIDTH, of=low),
            shape(rows, WIDTH),
            shape(*got.shape, of=low),
            shape(4, WIDTH),
        ],
        "feed_forward",
        [pltpu.VMEM((pieces, rows, step), jnp.float32)],
        20,
    )


def before_self(got, dresid, normed, scale, gains, query_part, out_part, lanes, width):
    def body(ins, loaded, outs, _):
        got_ref, dresid_ref, normed_ref, scale_ref, gains_ref = ins
        dcq_ref, dr_ref, dsb_ref, blocks_ref, norms_ref = outs
        dcq = read_blocks(got_ref, lanes, 0, width)
        dcq_ref[...] = dcq
        dhidden = dresid_ref[...] + dot_back(dcq, loaded[0].value())
        normed = normed_ref[...]
        norms_ref[0:1] = jnp.sum(dhidden * normed, axis=0, keepdims=True)
        norms_ref[1:2] = jnp.sum(dhidden, axis=0, keepdims=True)
        dr = norm_back(dhidden, normed, scale_ref[...], gains_ref[0:1])
        dr_ref[...] = dr
        dsb = dr.astype(jnp.bfloat16)
        dsb_ref[...] = dsb
        grad = dot_back(dsb, loaded[1].value()).astype(jnp.bfloat16)
        write_blocks(blocks_ref, grad, lanes, 0, width)

    rows = dresid.shape[0]
    return call_with_parts(
        body,
        [got, dresid, normed, scale, gains],
        [query_part, out_part],
        [
            shape(rows, WIDTH, of=jnp.bfloat16),
            shape(rows, WIDTH),
            shape(rows, WIDTH, of=jnp.bfloat16),
            shape(*got.shape, of=jnp.bfloat16),
            shape(2, WIDTH),
        ],
        "before_self",
    )


def input_grad(got, start, parts, lanes, width, name):
    def body(ins, loaded, outs, _):
        total = None
        for kind, weight in enumerate(loaded):
            term = dot_back(read_blocks(ins[0], lanes, kind, width), weight.value())
            total = term if total is None else total + term
        outs[0][...] = total if len(ins) == 1 else total + ins[1][...]

    rows = got.shape[1] * lanes
    return call_with_parts(
        body,
        [got] if start is None else [got, start],
        parts,
        [shape(rows, WIDTH)],
        name,
    )


def sum_everywhere(values, stages):
    if not paired():
        return lax.psum(values, ("dp", "blk"))
    values = after(values, stages[0])
    values = values + swap_core(values)
    for step, bit in enumerate((1, 2, 4, 8)):
        if step + 1 < len(stages):
            values = after(values, stages[step + 1])
        values = values + flip(values, bit)
    return values


def shards(
    tokens,
    encoder,
    cotangent,
    self_in,
    self_out,
    cross_q,
    cross_kv,
    cross_out,
    ffn_in,
    ffn_out,
    adapt_down,
    adapt_up,
    norm_gain,
    norm_bias,
    tgt_lengths,
    src_lengths,
):
    lanes, span, _ = tokens.shape
    rows = lanes * span
    width = WIDTH * lanes // lax.axis_size("blk")
    own_row = lax.axis_index("blk") % lanes
    tgt_ends = jnp.cumsum(lax.dynamic_index_in_dim(tgt_lengths, own_row, 0, keepdims=False))
    src_ends = jnp.cumsum(lax.dynamic_index_in_dim(src_lengths, own_row, 0, keepdims=False))
    flat_tokens = tokens.reshape(rows, WIDTH)
    flat_encoder = encoder.reshape(rows, WIDTH)

    half = 3 * WIDTH // 2
    self_x, self_y = gather_flips([self_in[:, :half], self_in[:, half:]], "xy")
    self_parts = [
        columns_of((self_x, 0, WIDTH)),
        columns_of((self_x, WIDTH, WIDTH // 2), (self_y, 0, WIDTH // 2)),
        columns_of((self_y, WIDTH // 2, WIDTH)),
    ]
    shards_x = jnp.concatenate([cross_kv[:, :WIDTH], self_out], axis=1)
    shards_y = jnp.concatenate([cross_kv[:, WIDTH:], cross_q], axis=1)
    shards_x, shards_y = after((shards_x, shards_y), self_x.stages[1], self_y.stages[1])
    pair_x, pair_y = gather_flips([shards_x, shards_y], "xy")
    pair_parts = [columns_of((pair_x, 0, WIDTH)), columns_of((pair_y, 0, WIDTH))]
    self_out_part = columns_of((pair_x, WIDTH, WIDTH))
    query_part = columns_of((pair_y, WIDTH, WIDTH))
    frozen = [ffn_in, adapt_down, ffn_out, adapt_up, cross_out]
    frozen = after(frozen, self_x.stages[0], self_y.stages[0])
    packed = gather_packed(frozen) if paired() else None

    self_qkv = as_rows(
        exchange(
            project_blocks(
                after(flat_tokens, pair_x.stages[0], pair_y.stages[0]),
                self_parts,
                lanes,
                width,
                "self_in",
            )
        )
    )
    cross_blocks = project_blocks(flat_encoder, pair_parts, lanes, width, "cross_kv")
    cross_kv_own = as_rows(exchange(cross_blocks))
    self_qkv = after(self_qkv, cross_blocks)
    self_mid, self_full, self_lse = attn_forward(
        tgt_ends, tgt_ends, self_qkv, self_qkv, width, True
    )
    self_low, normed, scale, hidden_low, query_blocks = after_self(
        after(exchange(as_blocks(self_mid)), cross_kv_own),
        flat_tokens,
        norm_gain,
        norm_bias,
        self_out_part,
        query_part,
        lanes,
        width,
    )
    cross_q_own = as_rows(exchange(query_blocks))
    ready = after(packed, cross_q_own) if paired() else None
    ff_parts, down_parts, ffo_parts, up_parts, (cross_out_part,) = packed_parts(frozen, ready)
    cross_mid, cross_full, cross_lse = attn_forward(
        tgt_ends, src_ends, cross_q_own, cross_kv_own, width, False
    )
    (
        output,
        cross_low,
        mixed_low,
        adapter_low,
        grad_under,
        adapt_low,
        cross_branch_low,
        grad_resid_two,
        cross_blocks,
        norms_high,
    ) = feed_forward(
        exchange(as_blocks(cross_mid)),
        normed,
        cotangent.reshape(rows, WIDTH),
        norm_gain,
        norm_bias,
        cross_out_part,
        ff_parts,
        down_parts[0],
        ffo_parts[0],
        up_parts[0],
        lanes,
        width,
    )
    high_pairs = [(cross_low, cross_branch_low), (mixed_low, grad_under), (adapter_low, adapt_low)]
    (grad_cross_out, grad_adapt_down, grad_adapt_up), _ = reduce_terms(
        high_pairs, grad_terms(high_pairs)
    )
    cross_dq, cross_dkv = attn_backward(
        tgt_ends,
        src_ends,
        cross_q_own,
        cross_kv_own,
        as_rows(exchange(cross_blocks)),
        cross_full,
        cross_lse,
        False,
    )
    cq_low, grad_resid_one, self_branch_low, self_blocks, norms_low = before_self(
        exchange(as_blocks(cross_dq)),
        grad_resid_two,
        normed,
        scale,
        norm_gain,
        query_part,
        self_out_part,
        lanes,
        width,
    )
    cross_got = exchange(as_blocks(cross_dkv))
    ckv_low = cross_got.reshape(-1, lanes, span, 2, width).transpose(1, 2, 3, 0, 4)
    kv_pairs = [(flat_encoder, ckv_low.reshape(rows, 2 * WIDTH))]
    kv_terms = grad_terms(kv_pairs)
    (encoder_grad,) = input_grad(cross_got, None, pair_parts, lanes, width, "encoder_grad")
    mid_pairs = [(hidden_low, cq_low), (self_low, self_branch_low)]
    mid_terms = grad_terms(mid_pairs)
    (self_grads,) = attn_backward(
        tgt_ends,
        tgt_ends,
        self_qkv,
        self_qkv,
        as_rows(exchange(self_blocks)),
        self_full,
        self_lse,
        True,
        joined=True,
    )
    self_got = exchange(as_blocks(self_grads))
    triple_low = self_got.reshape(-1, lanes, span, 3, width).transpose(1, 2, 3, 0, 4)
    low_pairs = [(flat_tokens, triple_low.reshape(rows, 3 * WIDTH))]
    low_terms = grad_terms(low_pairs)
    (grad_self_in,), stages = reduce_terms(low_pairs, low_terms)
    (grad_cross_kv,), _ = reduce_terms(kv_pairs, kv_terms, stages[0], 1)
    (grad_cross_q, grad_self_out), _ = reduce_terms(mid_pairs, mid_terms, stages[0], 2)
    (tokens_grad,) = input_grad(
        after(self_got, stages[0]), grad_resid_one, self_parts, lanes, width, "tokens_grad"
    )
    norms = sum_everywhere(jnp.concatenate([norms_low, norms_high], axis=0), stages)
    return (
        output.reshape(lanes, span, WIDTH),
        tokens_grad.reshape(lanes, span, WIDTH),
        encoder_grad.reshape(lanes, span, WIDTH),
        grad_self_in,
        grad_self_out,
        grad_cross_q,
        grad_cross_kv,
        grad_cross_out,
        grad_adapt_down,
        grad_adapt_up,
        jnp.stack([norms[0], norms[4], norms[2]]),
        jnp.stack([norms[1], norms[5], norms[3]]),
    )


def solution(mesh):
    placed = (
        P("dp", "blk", None),
        P("dp", "blk", None),
        P("dp", "blk", None),
        P("blk", None),
        P("blk", None),
        P("blk", None),
        P("blk", None),
        P("blk", None),
        P("blk", None),
        P("blk", None),
        P("blk", None),
        P("blk", None),
        P(),
        P(),
        P("dp", None),
        P("dp", None),
    )
    return jax.shard_map(
        shards,
        mesh=mesh,
        in_specs=placed,
        out_specs=(
            P("dp", "blk", None),
            P("dp", "blk", None),
            P("dp", "blk", None),
            P("blk", None),
            P("blk", None),
            P("blk", None),
            P("blk", None),
            P("blk", None),
            P("blk", None),
            P("blk", None),
            P(),
            P(),
        ),
        check_vma=False,
    )
```

```python
import functools
import math

import jax
import jax.numpy as jnp
from jax import lax
from jax.experimental import pallas as pl
from jax.experimental.pallas import tpu as pltpu
from jax.sharding import PartitionSpec as P

HEADS = 16
HEAD_DIM = 64
WIDTH = HEADS * HEAD_DIM


NEG = -1e30
VMEM_BYTES = 56 * 1024 * 1024


def cost(microseconds):
    return pl.CostEstimate(
        flops=int(microseconds * 1.0e9),
        bytes_accessed=int(microseconds * 3.5e6),
        transcendentals=0,
    )


def paired():
    return lax.axis_size("blk") == 16 and lax.axis_size("dp") == 2


def swap_core(block):
    cores = lax.axis_size("dp")
    return lax.ppermute(block, "dp", [(i ^ 1, i) for i in range(cores)])


def flip(block, bit):
    chips = lax.axis_size("blk")
    return lax.ppermute(block, "blk", [(i ^ bit, i) for i in range(chips)])


def rotate_z(block, distance):
    chips = lax.axis_size("blk")
    return lax.ppermute(block, "blk", [((i + 4 * distance) % chips, i) for i in range(chips)])


def own_half(values, which):
    half = values.shape[1] // 2
    return lax.dynamic_slice_in_dim(values, which * half, half, 1)


def scatter_chips(terms, orders, hold, held_stage):
    own = lax.axis_index("blk")
    z, y, x = own // 4, (own // 2) % 2, own % 2

    def fold(blocks, axis, place, bit):
        kept = lax.dynamic_index_in_dim(blocks, place, axis, keepdims=False)
        sent = lax.dynamic_index_in_dim(blocks, 1 - place, axis, keepdims=False)
        got = flip(sent, bit)
        return (kept.astype(jnp.float32) + got.astype(jnp.float32)).astype(jnp.bfloat16)

    def held(terms, stage):
        return after(terms, hold) if hold is not None and stage == held_stage else terms

    terms = [blocks.reshape(4, 2, 2, *blocks.shape[1:]) for blocks in terms]
    stages = [terms[0]]
    terms = held(terms, 0)
    terms = [
        fold(blocks, 1, y, 2) if first_y else fold(blocks, 2, x, 1)
        for blocks, first_y in zip(terms, orders)
    ]
    stages.append(terms[0])
    terms = held(terms, 1)
    terms = [
        fold(blocks, 1, x, 1) if first_y else fold(blocks, 1, y, 2)
        for blocks, first_y in zip(terms, orders)
    ]
    stages.append(terms[0])
    terms = held(terms, 2)
    totals = []
    for blocks in terms:
        total = lax.dynamic_index_in_dim(blocks, z, 0, keepdims=False).astype(jnp.float32)
        for distance in (1, 2, 3):
            sent = lax.dynamic_index_in_dim(blocks, (z - distance) % 4, 0, keepdims=False)
            total = total + rotate_z(sent, distance).astype(jnp.float32)
        totals.append(total)
    return totals, stages


CHUNK = 256


def grad_terms(pairs):
    if not paired():
        return None
    core = lax.axis_index("dp")
    packed = []
    for inputs, upstream in pairs:
        both = jnp.concatenate([inputs, swap_core(inputs)], axis=0)
        half = jnp.concatenate(
            [own_half(upstream, core), swap_core(own_half(upstream, 1 - core))], axis=0
        )
        term = lax.dot_general(
            both, half, (((0,), (0,)), ((), ())), preferred_element_type=jnp.float32
        ).astype(jnp.bfloat16)
        rows = term.shape[0] // 16
        chunks = term.shape[1] // CHUNK
        packed += [
            term[:, c * CHUNK : (c + 1) * CHUNK].reshape(16, rows, CHUNK) for c in range(chunks)
        ]
    return jnp.concatenate(packed, axis=1)


def split_terms(terms):
    return None if terms is None else jnp.split(terms, 2, axis=1)


def reduce_terms(groups, terms, orders, hold=None, held_stage=0):
    if not paired():
        found = [[weight_grad(inputs, upstream) for inputs, upstream in pairs] for pairs in groups]
        return found, [groups[0][0][1]] * 4
    core = lax.axis_index("dp")
    totals, stages = scatter_chips(terms, orders, hold, held_stage)
    mine = jnp.concatenate(totals, axis=0).astype(jnp.bfloat16)
    stages.append(mine)
    other = swap_core(mine)
    low = jnp.where(core == 0, mine, other).astype(jnp.float32)
    high = jnp.where(core == 0, other, mine).astype(jnp.float32)
    found, place = [], 0
    for pairs in groups:
        found.append([])
        for inputs, upstream in pairs:
            rows = inputs.shape[1] // 16
            chunks = upstream.shape[1] // 2 // CHUNK
            spots = [slice(place + c * rows, place + (c + 1) * rows) for c in range(chunks)]
            found[-1].append(
                jnp.concatenate(
                    [low[spot] for spot in spots] + [high[spot] for spot in spots], axis=1
                )
            )
            place += rows * chunks
    return found, stages


def weight_grad(inputs, upstream):
    scattered = lax.psum_scatter(
        lax.dot_general(
            inputs, upstream, (((0,), (0,)), ((), ())), preferred_element_type=jnp.float32
        ).astype(jnp.bfloat16),
        "blk",
        scatter_dimension=0,
        tiled=True,
    )
    return lax.psum(scattered, "dp").astype(jnp.float32)


class Source:
    def __init__(self, kind, arrays, first_flip="x", column=None):
        self.kind, self.arrays, self.first_flip = kind, arrays, first_flip
        self.stages = arrays[:1] * 3 if column is None else [column] + arrays[:2]


class Part:
    def __init__(self, rows, width, spots):
        self.rows, self.width, self.spots = rows, width, spots

    def scratch(self):
        return pltpu.VMEM((4, 2, 2, 2, self.rows // 32, self.width), jnp.bfloat16)

    def start(self, refs_of, place, dst, sem):
        z, y, x, core = [place[axis] for axis in range(4)]
        high = self.rows // 32
        for source, first_row, first_col, at_col, width in self.spots:
            refs = refs_of(source)
            cols = slice(first_col, first_col + width)
            into = slice(at_col, at_col + width)
            if source.kind == "whole":
                pltpu.make_async_copy(
                    refs[0].at[:, :, :, :, :, cols], dst.at[:, :, :, :, :, into], sem
                ).start()
            elif source.kind == "cores":
                for which in range(2):
                    owner = core if which == 0 else 1 - core
                    pltpu.make_async_copy(
                        refs[which].at[:, :, :, first_row : first_row + high, cols],
                        dst.at[:, :, :, owner, :, into],
                        sem,
                    ).start()
            else:
                for which in range(4):
                    owner = core if which < 2 else 1 - core
                    for near in range(2):
                        if source.first_flip == "x":
                            at_x = x if near == 0 else 1 - x
                            at_y = y if which % 2 == 0 else 1 - y
                        else:
                            at_y = y if near == 0 else 1 - y
                            at_x = x if which % 2 == 0 else 1 - x
                        for up in range(4):
                            at_z = lax.rem(z + up, 4)
                            pltpu.make_async_copy(
                                refs[which].at[near, up, :, cols],
                                dst.at[at_z, at_y, at_x, owner, :, into],
                                sem,
                            ).start()


def after(value, *others):
    return lax.optimization_barrier((value, *others))[0]


def gather_flips(shards, first_flips, hold=None):
    if not paired():
        full = [lax.all_gather(shard, "blk", axis=0, tiled=True) for shard in shards]
        return [
            Source("whole", [array.reshape(4, 2, 2, 2, array.shape[0] // 32, array.shape[1])])
            for array in full
        ]
    core = lax.axis_index("dp")
    columns = []
    for shard in shards:
        rows = shard.shape[0]
        own = lax.dynamic_slice_in_dim(shard, core * (rows // 2), rows // 2, 0)
        columns.append(
            jnp.stack([own] + [rotate_z(own, distance) for distance in (1, 2, 3)])
        )
    sources, bits = [], {"x": (1, 2), "y": (2, 1)}
    if hold is not None:
        columns = after(columns, hold)
    planes = [
        jnp.stack([column, flip(column, bits[first][0])])
        for column, first in zip(columns, first_flips)
    ]
    for column, plane, first in zip(columns, planes, first_flips):
        beyond = flip(plane, bits[first][1])
        sources.append(
            Source("flips", [plane, beyond, swap_core(plane), swap_core(beyond)], first, column)
        )
    return sources


def columns_of(*pieces):
    spots, place = [], 0
    for source, first, width in pieces:
        spots.append((source, 0, first, place, width))
        place += width
    return Part(1024, place, spots)


PACK = 512


def gather_packed(shards):
    core = lax.axis_index("dp")
    packed = []
    for shard in shards:
        high = shard.shape[0] // 2
        own = lax.dynamic_slice_in_dim(shard, core * high, high, 0)
        packed += [own[:, first : first + PACK] for first in range(0, shard.shape[1], PACK)]
    return lax.all_gather(jnp.concatenate(packed, axis=0), "blk", axis=0)


def packed_parts(shards, mine):
    if not paired():
        found = []
        for source, shard in zip(gather_flips(shards, "x" * len(shards)), shards):
            rows, columns = 32 * source.arrays[0].shape[4], shard.shape[1]
            step = min(columns, 1024)
            found.append(
                [
                    Part(rows, step, [(source, 0, first, 0, step)])
                    for first in range(0, columns, step)
                ]
            )
        return found
    spots, place = [], 0
    for shard in shards:
        high = shard.shape[0] // 2
        places = []
        for first in range(0, shard.shape[1], PACK):
            places.append(place)
            place += high
        spots.append((shard.shape[0] * 16, places))
    mine = mine.reshape(4, 2, 2, place, PACK)
    source = Source("cores", [mine, swap_core(mine)])
    found = []
    for rows, places in spots:
        parts = []
        for first in range(0, len(places), 2):
            two = places[first : first + 2]
            parts.append(
                Part(
                    rows,
                    PACK * len(two),
                    [(source, row, 0, PACK * side, PACK) for side, row in enumerate(two)],
                )
            )
        found.append(parts)
    return found


def place_now():
    own, core = lax.axis_index("blk"), lax.axis_index("dp")
    return jnp.stack([own // 4, (own // 2) % 2, own % 2, core]).astype(jnp.int32)


class Loaded:
    def __init__(self, part, dst, sem):
        self.part, self.dst, self.sem, self.here = part, dst, sem, False

    def value(self):
        if not self.here:
            pltpu.make_async_copy(self.dst, self.dst, self.sem).wait()
            self.here = True
        return self.dst[...].reshape(self.part.rows, self.part.width)


def call_with_parts(body, inputs, parts, outputs, name, scratch=(), takes=5):
    sources = []
    for part in parts:
        sources += [spot[0] for spot in part.spots if spot[0] not in sources]
    arrays = [array for source in sources for array in source.arrays]

    def kernel(place, *refs):
        refs = list(refs)
        ins = [refs.pop(0) for _ in inputs]
        pieces = [[refs.pop(0) for _ in source.arrays] for source in sources]
        outs = [refs.pop(0) for _ in outputs]
        dsts = [refs.pop(0) for _ in parts]
        sems = refs.pop(0)
        loaded = []
        for index, part in enumerate(parts):
            part.start(
                lambda source: pieces[sources.index(source)], place, dsts[index], sems.at[index]
            )
            loaded.append(Loaded(part, dsts[index], sems.at[index]))
        body(ins, loaded, outs, refs)

    return pl.pallas_call(
        kernel,
        out_shape=tuple(outputs),
        in_specs=[smem_spec()]
        + [vmem_spec()] * len(inputs)
        + [pl.BlockSpec(memory_space=pl.ANY)] * len(arrays),
        out_specs=(vmem_spec(),) * len(outputs),
        scratch_shapes=[part.scratch() for part in parts]
        + [pltpu.SemaphoreType.DMA((len(parts),))]
        + list(scratch),
        compiler_params=pltpu.CompilerParams(vmem_limit_bytes=VMEM_BYTES),
        cost_estimate=cost(takes),
        name=name,
    )(place_now(), *inputs, *arrays)


def vmem_spec():
    return pl.BlockSpec(memory_space=pltpu.VMEM)


def smem_spec():
    return pl.BlockSpec(memory_space=pltpu.SMEM)


def seg_of_pos(ends_ref, pos):
    seg = jnp.zeros(pos.shape, jnp.int32)
    for slot in range(ends_ref.shape[0]):
        seg = seg + (ends_ref[slot] <= pos).astype(jnp.int32)
    return seg


def pair_dot(left, right, left_dim, right_dim):
    return lax.dot_general(
        left, right, (((left_dim,), (right_dim,)), ((), ())), preferred_element_type=jnp.float32
    )


def seg_tables(q_ends, k_ends, span):
    seg_q = seg_of_pos(q_ends, lax.broadcasted_iota(jnp.int32, (1, span), 1))
    seg_k = seg_of_pos(k_ends, lax.broadcasted_iota(jnp.int32, (span, 1), 0))
    return seg_q, seg_k


def masked_scores(keys, queries, seg_q, seg_k, first, causal):
    scores = pair_dot(keys, queries, 1, 1)
    allowed = seg_k == seg_q
    if causal:
        key_pos = lax.broadcasted_iota(jnp.int32, scores.shape, 0)
        query_pos = first + lax.broadcasted_iota(jnp.int32, scores.shape, 1)
        allowed = allowed & (key_pos <= query_pos)
    return jnp.where(allowed, scores, NEG)


def attn_forward_body(causal, width, q_ends, k_ends, q_ref, kv_ref, low_ref, full_ref, lse_ref):
    span = q_ref.shape[0]
    step = math.gcd(span, 256)
    heads = width // HEAD_DIM
    seg_q, seg_k = seg_tables(q_ends, k_ends, span)
    key_at = kv_ref.shape[1] - 2 * width
    scaled = q_ref[:, :width] * jnp.bfloat16(HEAD_DIM ** (-0.5))
    keys = kv_ref[:, key_at : key_at + width]
    values = kv_ref[:, key_at + width : key_at + 2 * width]
    for first in range(0, span, step):
        reach = first + step if causal else span
        parts = []
        for head in range(heads):
            cols = slice(head * HEAD_DIM, (head + 1) * HEAD_DIM)
            scores = masked_scores(
                keys[:reach, cols],
                scaled[first : first + step, cols],
                seg_q[:, first : first + step],
                seg_k[:reach],
                first,
                causal,
            )
            top = jnp.max(scores, axis=0, keepdims=True)
            probs = jnp.exp(scores - top)
            total = jnp.sum(probs, axis=0, keepdims=True)
            mixed = pair_dot(values[:reach, cols], probs.astype(jnp.bfloat16), 0, 0)
            parts.append(mixed / total)
            lse_ref[head : head + 1, first : first + step] = top + jnp.log(total)
        joined = jnp.concatenate(parts, axis=0).T
        full_ref[first : first + step, :] = joined
        low_ref[first : first + step, :] = joined.astype(jnp.bfloat16)


def attn_forward(q_ends, k_ends, queries, keys_values, width, causal):
    span = queries.shape[0]
    return pl.pallas_call(
        functools.partial(attn_forward_body, causal, width),
        out_shape=(
            jax.ShapeDtypeStruct((span, width), jnp.bfloat16),
            jax.ShapeDtypeStruct((span, width), jnp.float32),
            jax.ShapeDtypeStruct((width // HEAD_DIM, span), jnp.float32),
        ),
        in_specs=[smem_spec(), smem_spec()] + [vmem_spec()] * 2,
        out_specs=(vmem_spec(),) * 3,
        compiler_params=pltpu.CompilerParams(vmem_limit_bytes=VMEM_BYTES),
        cost_estimate=cost(8),
        name="attn_forward",
    )(q_ends, k_ends, queries, keys_values)


def attn_backward_body(
    causal,
    width,
    q_ends,
    k_ends,
    q_ref,
    kv_ref,
    up_ref,
    full_ref,
    lse_ref,
    *outs,
):
    dq_ref, dkv_ref = outs[0], outs[-3]
    dk_sum, dv_sum = outs[-2:]
    span = q_ref.shape[0]
    step = math.gcd(span, 256)
    heads = width // HEAD_DIM
    seg_q, seg_k = seg_tables(q_ends, k_ends, span)
    key_at = kv_ref.shape[1] - 2 * width
    scaled = q_ref[:, :width] * jnp.bfloat16(HEAD_DIM ** (-0.5))
    keys = kv_ref[:, key_at : key_at + width]
    values = kv_ref[:, key_at + width : key_at + 2 * width]
    upstream = up_ref[...]
    dk_sum[...] = jnp.zeros_like(dk_sum)
    dv_sum[...] = jnp.zeros_like(dv_sum)
    for first in range(0, span, step):
        reach = first + step if causal else span
        rows = slice(first, first + step)
        product = (upstream[rows].astype(jnp.float32) * full_ref[rows, :]).T
        parts = []
        for head in range(heads):
            cols = slice(head * HEAD_DIM, (head + 1) * HEAD_DIM)
            delta = jnp.sum(product[cols], axis=0, keepdims=True)
            scores = masked_scores(
                keys[:reach, cols], scaled[rows, cols], seg_q[:, rows], seg_k[:reach], first, causal
            )
            probs = jnp.exp(scores - lse_ref[head : head + 1, rows])
            dv_sum[head, :reach] += pair_dot(
                probs.astype(jnp.bfloat16), upstream[rows, cols], 1, 0
            )
            grad_probs = pair_dot(values[:reach, cols], upstream[rows, cols], 1, 1)
            grad_scores = (probs * (grad_probs - delta)).astype(jnp.bfloat16)
            dk_sum[head, :reach] += pair_dot(grad_scores, scaled[rows, cols], 1, 0)
            parts.append(pair_dot(keys[:reach, cols], grad_scores, 0, 0))
        joined = jnp.concatenate(parts, axis=0).T * HEAD_DIM ** (-0.5)
        dq_ref[rows, :width] = joined.astype(jnp.bfloat16)
    sums = [dk_sum[head] for head in range(heads)] + [dv_sum[head] for head in range(heads)]
    kv_at = dkv_ref.shape[1] - 2 * width
    dkv_ref[:, kv_at:] = jnp.concatenate(sums, axis=1).astype(jnp.bfloat16)


def attn_backward(
    q_ends, k_ends, queries, keys_values, upstream, full, lse, causal, joined=False
):
    span, width = upstream.shape
    kinds = [3] if joined else [1, 2]
    heads = width // HEAD_DIM
    return pl.pallas_call(
        functools.partial(attn_backward_body, causal, width),
        out_shape=[jax.ShapeDtypeStruct((span, kind * width), jnp.bfloat16) for kind in kinds],
        in_specs=[smem_spec(), smem_spec()] + [vmem_spec()] * 5,
        out_specs=[vmem_spec()] * len(kinds),
        scratch_shapes=[pltpu.VMEM((heads, span, HEAD_DIM), jnp.float32)] * 2,
        compiler_params=pltpu.CompilerParams(vmem_limit_bytes=VMEM_BYTES),
        cost_estimate=cost(8),
        name="attn_backward",
    )(q_ends, k_ends, queries, keys_values, upstream, full, lse)


def exchange(blocks):
    return lax.all_to_all(blocks, "blk", 0, 0, tiled=True)


def as_rows(blocks):
    return blocks.reshape(blocks.shape[0] * blocks.shape[1], blocks.shape[2])


def as_blocks(rows):
    devices = lax.axis_size("blk")
    return rows.reshape(devices, rows.shape[0] // devices, rows.shape[1])


def write_blocks(out_ref, values, lanes, kind, width):
    span = values.shape[0] // lanes
    for group in range(WIDTH // width):
        for lane in range(lanes):
            out_ref[group * lanes + lane, :, kind * width : (kind + 1) * width] = values[
                lane * span : (lane + 1) * span, group * width : (group + 1) * width
            ]


def read_blocks(got_ref, lanes, kind, width):
    groups = got_ref.shape[0] // lanes
    cols = slice(kind * width, (kind + 1) * width)
    rows = [
        jnp.concatenate([got_ref[group * lanes + lane, :, cols] for group in range(groups)], axis=1)
        for lane in range(lanes)
    ]
    return jnp.concatenate(rows, axis=0)


def dot(left, right):
    return pair_dot(left, right, 1, 0)


def dot_back(left, right):
    return pair_dot(left, right, 1, 1)


def shape(*sizes, of=jnp.float32):
    return jax.ShapeDtypeStruct(sizes, of)


def normalize(values):
    center = values - jnp.mean(values, -1, keepdims=True)
    scale = lax.rsqrt(jnp.mean(center * center, -1, keepdims=True) + 1e-05)
    return center * scale, scale


def norm_back(upstream, normed, scale, gains_row):
    grad = upstream * gains_row
    return scale * (
        grad
        - jnp.mean(grad, -1, keepdims=True)
        - normed * jnp.mean(grad * normed, -1, keepdims=True)
    )


def project_blocks(inputs, parts, lanes, width, name):
    def body(ins, loaded, outs, _):
        for kind, weight in enumerate(loaded):
            write_blocks(
                outs[0], dot(ins[0][...], weight.value()).astype(jnp.bfloat16), lanes, kind, width
            )

    devices, span = lax.axis_size("blk"), inputs.shape[0] // lanes
    (blocks,) = call_with_parts(
        body,
        [inputs],
        parts,
        [shape(devices, span, width * len(parts), of=jnp.bfloat16)],
        name,
    )
    return blocks


def after_self(got, pair_blocks, tokens, gains, biases, out_part, query_part, lanes, width):
    def body(ins, loaded, outs, _):
        got_ref, pair_ref, tokens_ref, gains_ref, biases_ref = ins
        low_ref, normed_ref, scale_ref, hidden_ref, blocks_ref = outs
        attended = read_blocks(got_ref, lanes, 0, width)
        low_ref[...] = attended
        resid = tokens_ref[...].astype(jnp.float32) + dot(attended, loaded[0].value())
        normed, scale = normalize(resid)
        normed_ref[...] = normed
        scale_ref[...] = scale
        hidden = (normed * gains_ref[0:1] + biases_ref[0:1]).astype(jnp.bfloat16)
        hidden_ref[...] = hidden
        query = dot(hidden, loaded[1].value()).astype(jnp.bfloat16)
        write_blocks(blocks_ref, query, lanes, 0, width)
        blocks_ref[:, :, width:] = pair_ref[...]

    rows = tokens.shape[0]
    return call_with_parts(
        body,
        [got, pair_blocks, tokens, gains, biases],
        [out_part, query_part],
        [
            shape(rows, WIDTH, of=jnp.bfloat16),
            shape(rows, WIDTH),
            shape(rows, 1),
            shape(rows, WIDTH, of=jnp.bfloat16),
            shape(*got.shape[:2], 3 * width, of=jnp.bfloat16),
        ],
        "after_self",
    )


def feed_forward(got, normed_in, cotangent, gains, biases, out_part, in_parts, down, outs, up, lanes, width):
    pieces = len(in_parts)
    step = in_parts[0].width

    def body(ins, loaded, refs, scratch):
        got_ref, normed_in_ref, cot_ref, gains_ref, biases_ref = ins
        (
            output_ref,
            low_ref,
            mixed_ref,
            adapted_ref,
            dunder_ref,
            dab_ref,
            dcb_ref,
            dresid_ref,
            blocks_ref,
            norms_ref,
        ) = refs
        (slopes,) = scratch
        w_out, w_in = loaded[0], loaded[1 : 1 + pieces]
        w_down, w_ff, w_up = loaded[1 + pieces :]
        attended = read_blocks(got_ref, lanes, 0, width)
        low_ref[...] = attended
        hidden = normed_in_ref[...] * gains_ref[0:1] + biases_ref[0:1]
        normed_one, scale_one = normalize(hidden + dot(attended, w_out.value()))
        mixed = normed_one * gains_ref[1:2] + biases_ref[1:2]
        mixed_low = mixed.astype(jnp.bfloat16)
        mixed_ref[...] = mixed_low
        summed = mixed
        under = dot(mixed_low, w_down.value())
        gate = 1.0 / (1.0 + jnp.exp(-under))
        adapted = (under * gate).astype(jnp.bfloat16)
        adapted_ref[...] = adapted
        under_slope = gate * (1.0 + under * (1.0 - gate))
        summed = summed + 4.0 * dot(adapted, w_up.value())
        for piece in range(pieces):
            before = dot(mixed_low, w_in[piece].value())
            below = 0.5 + 0.5 * lax.erf(before * (0.5**0.5))
            slopes[piece] = below + before * jnp.exp(-0.5 * before * before) * (
                (2.0 * math.pi) ** -0.5
            )
            act = (before * below).astype(jnp.bfloat16)
            summed = summed + dot(act, w_ff[piece].value())
        normed_two, scale_two = normalize(summed)
        output_ref[...] = (normed_two * gains_ref[2:3] + biases_ref[2:3]).astype(jnp.bfloat16)
        upstream = cot_ref[...].astype(jnp.float32)
        norms_ref[0:1] = jnp.sum(upstream * normed_two, axis=0, keepdims=True)
        norms_ref[1:2] = jnp.sum(upstream, axis=0, keepdims=True)
        dz = norm_back(upstream, normed_two, scale_two, gains_ref[2:3])
        dzb = dz.astype(jnp.bfloat16)
        dab = (4.0 * dz).astype(jnp.bfloat16)
        dab_ref[...] = dab
        dunder = (under_slope * dot_back(dab, w_up.value())).astype(jnp.bfloat16)
        dunder_ref[...] = dunder
        dmixed = dz + dot_back(dunder, w_down.value())
        for piece in range(pieces):
            dpre = (slopes[piece] * dot_back(dzb, w_ff[piece].value())).astype(jnp.bfloat16)
            dmixed = dmixed + dot_back(dpre, w_in[piece].value())
        norms_ref[2:3] = jnp.sum(dmixed * normed_one, axis=0, keepdims=True)
        norms_ref[3:4] = jnp.sum(dmixed, axis=0, keepdims=True)
        dresid = norm_back(dmixed, normed_one, scale_one, gains_ref[1:2])
        dresid_ref[...] = dresid
        dcb = dresid.astype(jnp.bfloat16)
        dcb_ref[...] = dcb
        write_blocks(
            blocks_ref, dot_back(dcb, w_out.value()).astype(jnp.bfloat16), lanes, 0, width
        )

    rows = normed_in.shape[0]
    low = jnp.bfloat16

    def body_rows(ins, loaded, refs, scratch):
        whole_ff = loaded[2 + pieces]

        class Rows:
            def __init__(self, piece):
                self.piece = piece

            def value(self):
                return whole_ff.value()[self.piece * step : (self.piece + 1) * step]

        loaded = loaded[: 2 + pieces] + [[Rows(piece) for piece in range(pieces)], loaded[-1]]
        body(ins, loaded, refs, scratch)

    return call_with_parts(
        body_rows,
        [got, normed_in, cotangent, gains, biases],
        [out_part] + in_parts + [down, outs, up],
        [
            shape(rows, WIDTH, of=low),
            shape(rows, WIDTH, of=low),
            shape(rows, WIDTH, of=low),
            shape(rows, down.width, of=low),
            shape(rows, down.width, of=low),
            shape(rows, WIDTH, of=low),
            shape(rows, WIDTH, of=low),
            shape(rows, WIDTH),
            shape(*got.shape, of=low),
            shape(4, WIDTH),
        ],
        "feed_forward",
        [pltpu.VMEM((pieces, rows, step), jnp.float32)],
        20,
    )


def before_self(got, dresid, normed, scale, gains, query_part, out_part, lanes, width):
    def body(ins, loaded, outs, _):
        got_ref, dresid_ref, normed_ref, scale_ref, gains_ref = ins
        dcq_ref, dr_ref, dsb_ref, blocks_ref, norms_ref = outs
        dcq = read_blocks(got_ref, lanes, 0, width)
        dcq_ref[...] = dcq
        dhidden = dresid_ref[...] + dot_back(dcq, loaded[0].value())
        normed = normed_ref[...]
        norms_ref[0:1] = jnp.sum(dhidden * normed, axis=0, keepdims=True)
        norms_ref[1:2] = jnp.sum(dhidden, axis=0, keepdims=True)
        dr = norm_back(dhidden, normed, scale_ref[...], gains_ref[0:1])
        dr_ref[...] = dr
        dsb = dr.astype(jnp.bfloat16)
        dsb_ref[...] = dsb
        grad = dot_back(dsb, loaded[1].value()).astype(jnp.bfloat16)
        write_blocks(blocks_ref, grad, lanes, 0, width)

    rows = dresid.shape[0]
    return call_with_parts(
        body,
        [got, dresid, normed, scale, gains],
        [query_part, out_part],
        [
            shape(rows, WIDTH, of=jnp.bfloat16),
            shape(rows, WIDTH),
            shape(rows, WIDTH, of=jnp.bfloat16),
            shape(*got.shape, of=jnp.bfloat16),
            shape(2, WIDTH),
        ],
        "before_self",
    )


def input_grad(got, start, parts, lanes, width, name):
    def body(ins, loaded, outs, _):
        total = None
        for kind, weight in enumerate(loaded):
            term = dot_back(read_blocks(ins[0], lanes, kind, width), weight.value())
            total = term if total is None else total + term
        outs[0][...] = total if len(ins) == 1 else total + ins[1][...]

    rows = got.shape[1] * lanes
    return call_with_parts(
        body,
        [got] if start is None else [got, start],
        parts,
        [shape(rows, WIDTH)],
        name,
    )


def sum_everywhere(values, stages):
    if not paired():
        return lax.psum(values, ("dp", "blk"))
    values = after(values, stages[0])
    values = values + swap_core(values)
    for step, bit in enumerate((1, 2, 4, 8)):
        if step + 1 < len(stages):
            values = after(values, stages[step + 1])
        values = values + flip(values, bit)
    return values


def shards(
    tokens,
    encoder,
    cotangent,
    self_in,
    self_out,
    cross_q,
    cross_kv,
    cross_out,
    ffn_in,
    ffn_out,
    adapt_down,
    adapt_up,
    norm_gain,
    norm_bias,
    tgt_lengths,
    src_lengths,
):
    lanes, span, _ = tokens.shape
    rows = lanes * span
    width = WIDTH * lanes // lax.axis_size("blk")
    own_row = lax.axis_index("blk") % lanes
    tgt_ends = jnp.cumsum(lax.dynamic_index_in_dim(tgt_lengths, own_row, 0, keepdims=False))
    src_ends = jnp.cumsum(lax.dynamic_index_in_dim(src_lengths, own_row, 0, keepdims=False))
    flat_tokens = tokens.reshape(rows, WIDTH)
    flat_encoder = encoder.reshape(rows, WIDTH)

    half = 3 * WIDTH // 2
    self_x, self_y = gather_flips([self_in[:, :half], self_in[:, half:]], "xy")
    self_parts = [
        columns_of((self_x, 0, WIDTH)),
        columns_of((self_x, WIDTH, WIDTH // 2), (self_y, 0, WIDTH // 2)),
        columns_of((self_y, WIDTH // 2, WIDTH)),
    ]
    shards_x = jnp.concatenate([cross_kv[:, :WIDTH], self_out], axis=1)
    shards_y = jnp.concatenate([cross_kv[:, WIDTH:], cross_q], axis=1)
    shards_x, shards_y = after((shards_x, shards_y), self_x.stages[1], self_y.stages[1])
    pair_x, pair_y = gather_flips([shards_x, shards_y], "xy", self_x.stages[2])
    pair_parts = [columns_of((pair_x, 0, WIDTH)), columns_of((pair_y, 0, WIDTH))]
    self_out_part = columns_of((pair_x, WIDTH, WIDTH))
    query_part = columns_of((pair_y, WIDTH, WIDTH))
    frozen = [ffn_in, adapt_down, ffn_out, adapt_up, cross_out]
    frozen = after(frozen, self_x.stages[1])
    packed = gather_packed(frozen) if paired() else None

    self_blocks = project_blocks(flat_tokens, self_parts, lanes, width, "self_in")
    self_blocks = after(self_blocks, pair_x.stages[0], pair_y.stages[0])
    self_qkv = as_rows(exchange(self_blocks))
    self_qkv = after(self_qkv, pair_x.stages[2], pair_y.stages[2])
    pair_blocks = project_blocks(flat_encoder, pair_parts, lanes, width, "cross_kv")
    self_mid, self_full, self_lse = attn_forward(
        tgt_ends, tgt_ends, self_qkv, self_qkv, width, True
    )
    self_low, normed, scale, hidden_low, cross_blocks = after_self(
        exchange(as_blocks(self_mid)),
        pair_blocks,
        flat_tokens,
        norm_gain,
        norm_bias,
        self_out_part,
        query_part,
        lanes,
        width,
    )
    cross_qkv = as_rows(exchange(cross_blocks))
    ready = after(packed, cross_qkv) if paired() else None
    ff_parts, down_parts, ffo_parts, up_parts, (cross_out_part,) = packed_parts(frozen, ready)
    cross_mid, cross_full, cross_lse = attn_forward(
        tgt_ends, src_ends, cross_qkv, cross_qkv, width, False
    )
    (
        output,
        cross_low,
        mixed_low,
        adapter_low,
        grad_under,
        adapt_low,
        cross_branch_low,
        grad_resid_two,
        cross_grad_blocks,
        norms_high,
    ) = feed_forward(
        exchange(as_blocks(cross_mid)),
        normed,
        cotangent.reshape(rows, WIDTH),
        norm_gain,
        norm_bias,
        cross_out_part,
        ff_parts,
        down_parts[0],
        ffo_parts[0],
        up_parts[0],
        lanes,
        width,
    )
    high_pairs = [(cross_low, cross_branch_low), (mixed_low, grad_under), (adapter_low, adapt_low)]
    high_terms = grad_terms(high_pairs)
    (high_grads,), high_stages = reduce_terms([high_pairs], [high_terms], [True])
    grad_cross_out, grad_adapt_down, grad_adapt_up = high_grads
    cross_dq, cross_dkv = attn_backward(
        tgt_ends,
        src_ends,
        cross_qkv,
        cross_qkv,
        as_rows(after(exchange(cross_grad_blocks), high_stages[0])),
        cross_full,
        cross_lse,
        False,
    )
    cq_low, grad_resid_one, self_branch_low, self_grad_blocks, norms_low = before_self(
        after(exchange(as_blocks(cross_dq)), high_stages[1]),
        grad_resid_two,
        normed,
        scale,
        norm_gain,
        query_part,
        self_out_part,
        lanes,
        width,
    )
    cross_got = exchange(as_blocks(cross_dkv))
    ckv_low = cross_got.reshape(-1, lanes, span, 2, width).transpose(1, 2, 3, 0, 4)
    kv_pairs = [(flat_encoder, ckv_low.reshape(rows, 2 * WIDTH))]
    kv_terms = grad_terms(kv_pairs)
    (encoder_grad,) = input_grad(cross_got, None, pair_parts, lanes, width, "encoder_grad")
    mid_pairs = [(hidden_low, cq_low), (self_low, self_branch_low)]
    mid_terms = grad_terms(mid_pairs)
    (self_grads,) = attn_backward(
        tgt_ends,
        tgt_ends,
        self_qkv,
        self_qkv,
        as_rows(after(exchange(self_grad_blocks), high_stages[2])),
        self_full,
        self_lse,
        True,
        joined=True,
    )
    self_got = exchange(as_blocks(after(self_grads, high_stages[3])))
    triple_low = self_got.reshape(-1, lanes, span, 3, width).transpose(1, 2, 3, 0, 4)
    low_pairs = [(flat_tokens, triple_low.reshape(rows, 3 * WIDTH))]
    low_terms = grad_terms(low_pairs)
    half_terms = split_terms(low_terms)
    (halves,), stages = reduce_terms([low_pairs], half_terms, [True, False])
    (grad_self_in,) = halves
    ((grad_cross_kv,), (grad_cross_q, grad_self_out)), _ = reduce_terms(
        [kv_pairs, mid_pairs], [kv_terms, mid_terms], [False, True], stages[0], 1
    )
    (tokens_grad,) = input_grad(
        after(self_got, stages[0]), grad_resid_one, self_parts, lanes, width, "tokens_grad"
    )
    norms = sum_everywhere(jnp.concatenate([norms_low, norms_high], axis=0), stages)
    return (
        output.reshape(lanes, span, WIDTH),
        tokens_grad.reshape(lanes, span, WIDTH),
        encoder_grad.reshape(lanes, span, WIDTH),
        grad_self_in,
        grad_self_out,
        grad_cross_q,
        grad_cross_kv,
        grad_cross_out,
        grad_adapt_down,
        grad_adapt_up,
        jnp.stack([norms[0], norms[4], norms[2]]),
        jnp.stack([norms[1], norms[5], norms[3]]),
    )


def solution(mesh):
    placed = (
        P("dp", "blk", None),
        P("dp", "blk", None),
        P("dp", "blk", None),
        P("blk", None),
        P("blk", None),
        P("blk", None),
        P("blk", None),
        P("blk", None),
        P("blk", None),
        P("blk", None),
        P("blk", None),
        P("blk", None),
        P(),
        P(),
        P("dp", None),
        P("dp", None),
    )
    return jax.shard_map(
        shards,
        mesh=mesh,
        in_specs=placed,
        out_specs=(
            P("dp", "blk", None),
            P("dp", "blk", None),
            P("dp", "blk", None),
            P("blk", None),
            P("blk", None),
            P("blk", None),
            P("blk", None),
            P("blk", None),
            P("blk", None),
            P("blk", None),
            P(),
            P(),
        ),
        check_vma=False,
    )
```

```python
import functools
import math

import jax
import jax.numpy as jnp
from jax import lax
from jax.experimental import pallas as pl
from jax.experimental.pallas import tpu as pltpu
from jax.sharding import PartitionSpec as P

HEADS = 16
HEAD_DIM = 64
WIDTH = HEADS * HEAD_DIM


NEG = -1e30
VMEM_BYTES = 56 * 1024 * 1024


def cost(microseconds):
    return pl.CostEstimate(
        flops=int(microseconds * 0.4e9),
        bytes_accessed=int(microseconds * 1.2e6),
        transcendentals=0,
    )


def paired():
    return lax.axis_size("blk") == 16 and lax.axis_size("dp") == 2


def swap_core(block):
    cores = lax.axis_size("dp")
    return lax.ppermute(block, "dp", [(i ^ 1, i) for i in range(cores)])


def flip(block, bit):
    chips = lax.axis_size("blk")
    return lax.ppermute(block, "blk", [(i ^ bit, i) for i in range(chips)])


def rotate_z(block, distance):
    chips = lax.axis_size("blk")
    return lax.ppermute(block, "blk", [((i + 4 * distance) % chips, i) for i in range(chips)])


def own_half(values, which):
    half = values.shape[1] // 2
    return lax.dynamic_slice_in_dim(values, which * half, half, 1)


def scatter_chips(terms, orders, hold, held_stage):
    own = lax.axis_index("blk")
    z, y, x = own // 4, (own // 2) % 2, own % 2

    def fold(blocks, axis, place, bit):
        kept = lax.dynamic_index_in_dim(blocks, place, axis, keepdims=False)
        sent = lax.dynamic_index_in_dim(blocks, 1 - place, axis, keepdims=False)
        got = flip(sent, bit)
        return (kept.astype(jnp.float32) + got.astype(jnp.float32)).astype(jnp.bfloat16)

    def held(terms, stage):
        return after(terms, hold) if hold is not None and stage == held_stage else terms

    terms = [blocks.reshape(4, 2, 2, *blocks.shape[1:]) for blocks in terms]
    stages = [terms[0]]
    terms = held(terms, 0)
    terms = [
        fold(blocks, 1, y, 2) if first_y else fold(blocks, 2, x, 1)
        for blocks, first_y in zip(terms, orders)
    ]
    stages.append(terms[0])
    terms = held(terms, 1)
    terms = [
        fold(blocks, 1, x, 1) if first_y else fold(blocks, 1, y, 2)
        for blocks, first_y in zip(terms, orders)
    ]
    stages.append(terms[0])
    terms = held(terms, 2)
    totals = []
    for blocks in terms:
        total = lax.dynamic_index_in_dim(blocks, z, 0, keepdims=False).astype(jnp.float32)
        for distance in (1, 2, 3):
            sent = lax.dynamic_index_in_dim(blocks, (z - distance) % 4, 0, keepdims=False)
            total = total + rotate_z(sent, distance).astype(jnp.float32)
        totals.append(total)
    return totals, stages


CHUNK = 256


def grad_terms(pairs):
    if not paired():
        return None
    core = lax.axis_index("dp")
    packed = []
    for inputs, upstream in pairs:
        both = jnp.concatenate([inputs, swap_core(inputs)], axis=0)
        half = jnp.concatenate(
            [own_half(upstream, core), swap_core(own_half(upstream, 1 - core))], axis=0
        )
        term = lax.dot_general(
            both, half, (((0,), (0,)), ((), ())), preferred_element_type=jnp.float32
        ).astype(jnp.bfloat16)
        rows = term.shape[0] // 16
        chunks = term.shape[1] // CHUNK
        packed += [
            term[:, c * CHUNK : (c + 1) * CHUNK].reshape(16, rows, CHUNK) for c in range(chunks)
        ]
    return jnp.concatenate(packed, axis=1)


def reduce_terms(groups, terms, orders, hold=None, held_stage=0):
    if not paired():
        found = [[weight_grad(inputs, upstream) for inputs, upstream in pairs] for pairs in groups]
        return found, [groups[0][0][1]] * 4
    core = lax.axis_index("dp")
    totals, stages = scatter_chips(terms, orders, hold, held_stage)
    mine = jnp.concatenate(totals, axis=0).astype(jnp.bfloat16)
    stages.append(mine)
    other = swap_core(mine)
    low = jnp.where(core == 0, mine, other).astype(jnp.float32)
    high = jnp.where(core == 0, other, mine).astype(jnp.float32)
    found, place = [], 0
    for pairs in groups:
        found.append([])
        for inputs, upstream in pairs:
            rows = inputs.shape[1] // 16
            chunks = upstream.shape[1] // 2 // CHUNK
            spots = [slice(place + c * rows, place + (c + 1) * rows) for c in range(chunks)]
            found[-1].append(
                jnp.concatenate(
                    [low[spot] for spot in spots] + [high[spot] for spot in spots], axis=1
                )
            )
            place += rows * chunks
    return found, stages


def weight_grad(inputs, upstream):
    scattered = lax.psum_scatter(
        lax.dot_general(
            inputs, upstream, (((0,), (0,)), ((), ())), preferred_element_type=jnp.float32
        ).astype(jnp.bfloat16),
        "blk",
        scatter_dimension=0,
        tiled=True,
    )
    return lax.psum(scattered, "dp").astype(jnp.float32)


class Source:
    def __init__(self, kind, arrays, first_flip="x", column=None):
        self.kind, self.arrays, self.first_flip = kind, arrays, first_flip
        self.stages = arrays[:1] * 3 if column is None else [column] + arrays[:2]


class Part:
    def __init__(self, rows, width, spots):
        self.rows, self.width, self.spots = rows, width, spots

    def scratch(self):
        return pltpu.VMEM((4, 2, 2, 2, self.rows // 32, self.width), jnp.bfloat16)

    def start(self, refs_of, place, dst, sem):
        z, y, x, core = [place[axis] for axis in range(4)]
        high = self.rows // 32
        for source, first_row, first_col, at_col, width in self.spots:
            refs = refs_of(source)
            cols = slice(first_col, first_col + width)
            into = slice(at_col, at_col + width)
            if source.kind == "whole":
                pltpu.make_async_copy(
                    refs[0].at[:, :, :, :, :, cols], dst.at[:, :, :, :, :, into], sem
                ).start()
            elif source.kind == "cores":
                for which in range(2):
                    owner = core if which == 0 else 1 - core
                    pltpu.make_async_copy(
                        refs[which].at[:, :, :, first_row : first_row + high, cols],
                        dst.at[:, :, :, owner, :, into],
                        sem,
                    ).start()
            else:
                for which in range(4):
                    owner = core if which < 2 else 1 - core
                    for near in range(2):
                        if source.first_flip == "x":
                            at_x = x if near == 0 else 1 - x
                            at_y = y if which % 2 == 0 else 1 - y
                        else:
                            at_y = y if near == 0 else 1 - y
                            at_x = x if which % 2 == 0 else 1 - x
                        for up in range(4):
                            at_z = lax.rem(z + up, 4)
                            pltpu.make_async_copy(
                                refs[which].at[near, up, :, cols],
                                dst.at[at_z, at_y, at_x, owner, :, into],
                                sem,
                            ).start()


def after(value, *others):
    return lax.optimization_barrier((value, *others))[0]


def gather_flips(shards, first_flips, hold=None):
    if not paired():
        full = [lax.all_gather(shard, "blk", axis=0, tiled=True) for shard in shards]
        return [
            Source("whole", [array.reshape(4, 2, 2, 2, array.shape[0] // 32, array.shape[1])])
            for array in full
        ]
    core = lax.axis_index("dp")
    columns = []
    for shard in shards:
        rows = shard.shape[0]
        own = lax.dynamic_slice_in_dim(shard, core * (rows // 2), rows // 2, 0)
        columns.append(
            jnp.stack([own] + [rotate_z(own, distance) for distance in (1, 2, 3)])
        )
    sources, bits = [], {"x": (1, 2), "y": (2, 1)}
    if hold is not None:
        columns = after(columns, hold)
    planes = [
        jnp.stack([column, flip(column, bits[first][0])])
        for column, first in zip(columns, first_flips)
    ]
    for column, plane, first in zip(columns, planes, first_flips):
        beyond = flip(plane, bits[first][1])
        sources.append(
            Source("flips", [plane, beyond, swap_core(plane), swap_core(beyond)], first, column)
        )
    return sources


class RowPart:
    def __init__(self, source, span):
        self.source, self.span = source, span
        self.rows, self.width = 16 * span, WIDTH
        self.spots = [(source,)]

    def scratch(self):
        return pltpu.VMEM((4, 2, 2, self.span, WIDTH), jnp.bfloat16)

    def start(self, refs_of, place, dst, sem):
        z, y, x = [place[axis] for axis in range(3)]
        refs = refs_of(self.source)
        for beyond in range(2):
            for up in range(4):
                for near in range(2):
                    pltpu.make_async_copy(
                        refs[beyond].at[up, near],
                        dst.at[
                            lax.rem(z + up, 4),
                            y if beyond == 0 else 1 - y,
                            x if near == 0 else 1 - x,
                        ],
                        sem,
                    ).start()


def gather_row(block):
    x = lax.axis_index("blk") % 2
    own = lax.dynamic_index_in_dim(block, x, 0, keepdims=False)
    other = lax.dynamic_index_in_dim(block, 1 - x, 0, keepdims=False)
    pair = jnp.stack([own, flip(other, 1)])
    column = jnp.stack([pair] + [rotate_z(pair, distance) for distance in (1, 2, 3)])
    source = Source("row", [column, flip(column, 2)], "x", pair)
    source.stages = [pair, column]
    return RowPart(source, block.shape[1])


def head_columns(shard, kinds):
    core = lax.axis_index("dp")
    own = lax.dynamic_slice_in_dim(shard, core * 32, 32, 0)
    blocks = own.reshape(32, kinds, 8, 128).transpose(2, 0, 1, 3).reshape(8, 1, 32, kinds * 128)
    blocks = jnp.broadcast_to(blocks, (8, 2, 32, kinds * 128)).reshape(16, 32, kinds * 128)
    mine = exchange(blocks).reshape(4, 2, 2, 32, kinds * 128)
    source = Source("cores", [mine, swap_core(mine)])
    return Part(1024, kinds * 128, [(source, 0, 0, 0, kinds * 128)])


def project_row(row_part, head_part, name):
    def body(ins, loaded, outs, _):
        weight = loaded[1].value()
        inputs = loaded[0].value()
        for first in range(0, row_part.rows, 256):
            rows = slice(first, first + 256)
            outs[0][rows, :] = dot(inputs[rows], weight).astype(jnp.bfloat16)

    (found,) = call_with_parts(
        body,
        [],
        [row_part, head_part],
        [shape(row_part.rows, head_part.width, of=jnp.bfloat16)],
        name,
    )
    return found


def row_grad(row_part, upstream, name):
    columns = upstream.shape[1]

    def body(ins, loaded, outs, _):
        core = ins[1][0]
        inputs = loaded[0].value()
        grads = []
        for first in range(0, columns, 128):
            grads.append(pair_dot(ins[0][:, first : first + 128], inputs, 0, 0).T)
        grad = jnp.concatenate(grads, axis=1).astype(jnp.bfloat16).reshape(16, 2, 32, columns)
        outs[0][core] = grad[:, 0]
        outs[0][1 - core] = grad[:, 1]

    (terms,) = call_with_parts(
        body,
        [upstream],
        [row_part],
        [shape(2, 16, 32, columns, of=jnp.bfloat16)],
        name,
        scalars=[lax.axis_index("dp").reshape(1).astype(jnp.int32)],
    )
    got = swap_core(terms[1])
    return (terms[0].astype(jnp.float32) + got.astype(jnp.float32)).astype(jnp.bfloat16)


def finish_row_grad(got, kinds):
    total = jnp.sum(got.reshape(8, 2, 32, kinds, 128).astype(jnp.float32), axis=1)
    mine = total.astype(jnp.bfloat16).transpose(1, 2, 0, 3).reshape(32, kinds * WIDTH)
    other = swap_core(mine)
    core = lax.axis_index("dp")
    low = jnp.where(core == 0, mine, other)
    high = jnp.where(core == 0, other, mine)
    return jnp.concatenate([low, high], axis=0).astype(jnp.float32)


def columns_of(*pieces):
    spots, place = [], 0
    for source, first, width in pieces:
        spots.append((source, 0, first, place, width))
        place += width
    return Part(1024, place, spots)


PACK = 512


def gather_packed(shards):
    core = lax.axis_index("dp")
    packed = []
    for shard in shards:
        high = shard.shape[0] // 2
        own = lax.dynamic_slice_in_dim(shard, core * high, high, 0)
        packed += [own[:, first : first + PACK] for first in range(0, shard.shape[1], PACK)]
    return lax.all_gather(jnp.concatenate(packed, axis=0), "blk", axis=0)


def packed_parts(shards, mine):
    if not paired():
        found = []
        for source, shard in zip(gather_flips(shards, "x" * len(shards)), shards):
            rows, columns = 32 * source.arrays[0].shape[4], shard.shape[1]
            step = min(columns, 1024)
            found.append(
                [
                    Part(rows, step, [(source, 0, first, 0, step)])
                    for first in range(0, columns, step)
                ]
            )
        return found
    spots, place = [], 0
    for shard in shards:
        high = shard.shape[0] // 2
        places = []
        for first in range(0, shard.shape[1], PACK):
            places.append(place)
            place += high
        spots.append((shard.shape[0] * 16, places))
    mine = mine.reshape(4, 2, 2, place, PACK)
    source = Source("cores", [mine, swap_core(mine)])
    found = []
    for rows, places in spots:
        parts = []
        for first in range(0, len(places), 2):
            two = places[first : first + 2]
            parts.append(
                Part(
                    rows,
                    PACK * len(two),
                    [(source, row, 0, PACK * side, PACK) for side, row in enumerate(two)],
                )
            )
        found.append(parts)
    return found


def place_now():
    own, core = lax.axis_index("blk"), lax.axis_index("dp")
    return jnp.stack([own // 4, (own // 2) % 2, own % 2, core]).astype(jnp.int32)


class Loaded:
    def __init__(self, part, dst, sem):
        self.part, self.dst, self.sem, self.here = part, dst, sem, False

    def value(self):
        if not self.here:
            pltpu.make_async_copy(self.dst, self.dst, self.sem).wait()
            self.here = True
        return self.dst[...].reshape(self.part.rows, self.part.width)


def call_with_parts(body, inputs, parts, outputs, name, scratch=(), takes=5, scalars=()):
    sources = []
    for part in parts:
        sources += [spot[0] for spot in part.spots if spot[0] not in sources]
    arrays = [array for source in sources for array in source.arrays]

    def kernel(place, *refs):
        refs = list(refs)
        ins = [refs.pop(0) for _ in (*inputs, *scalars)]
        pieces = [[refs.pop(0) for _ in source.arrays] for source in sources]
        outs = [refs.pop(0) for _ in outputs]
        dsts = [refs.pop(0) for _ in parts]
        sems = refs.pop(0)
        loaded = []
        for index, part in enumerate(parts):
            part.start(
                lambda source: pieces[sources.index(source)], place, dsts[index], sems.at[index]
            )
            loaded.append(Loaded(part, dsts[index], sems.at[index]))
        body(ins, loaded, outs, refs)

    return pl.pallas_call(
        kernel,
        out_shape=tuple(outputs),
        in_specs=[smem_spec()]
        + [vmem_spec()] * len(inputs)
        + [smem_spec()] * len(scalars)
        + [pl.BlockSpec(memory_space=pl.ANY)] * len(arrays),
        out_specs=(vmem_spec(),) * len(outputs),
        scratch_shapes=[part.scratch() for part in parts]
        + [pltpu.SemaphoreType.DMA((len(parts),))]
        + list(scratch),
        compiler_params=pltpu.CompilerParams(vmem_limit_bytes=VMEM_BYTES),
        cost_estimate=cost(takes),
        name=name,
    )(place_now(), *inputs, *scalars, *arrays)


def vmem_spec():
    return pl.BlockSpec(memory_space=pltpu.VMEM)


def smem_spec():
    return pl.BlockSpec(memory_space=pltpu.SMEM)


def seg_of_pos(ends_ref, pos):
    seg = jnp.zeros(pos.shape, jnp.int32)
    for slot in range(ends_ref.shape[0]):
        seg = seg + (ends_ref[slot] <= pos).astype(jnp.int32)
    return seg


def pair_dot(left, right, left_dim, right_dim):
    return lax.dot_general(
        left, right, (((left_dim,), (right_dim,)), ((), ())), preferred_element_type=jnp.float32
    )


def seg_tables(q_ends, k_ends, span):
    seg_q = seg_of_pos(q_ends, lax.broadcasted_iota(jnp.int32, (1, span), 1))
    seg_k = seg_of_pos(k_ends, lax.broadcasted_iota(jnp.int32, (span, 1), 0))
    return seg_q, seg_k


def masked_scores(keys, queries, seg_q, seg_k, first, causal):
    scores = pair_dot(keys, queries, 1, 1)
    allowed = seg_k == seg_q
    if causal:
        key_pos = lax.broadcasted_iota(jnp.int32, scores.shape, 0)
        query_pos = first + lax.broadcasted_iota(jnp.int32, scores.shape, 1)
        allowed = allowed & (key_pos <= query_pos)
    return jnp.where(allowed, scores, NEG)


def attn_forward_body(causal, width, q_ends, k_ends, q_ref, kv_ref, low_ref, full_ref, lse_ref):
    span = q_ref.shape[0]
    step = math.gcd(span, 256)
    heads = width // HEAD_DIM
    seg_q, seg_k = seg_tables(q_ends, k_ends, span)
    key_at = kv_ref.shape[1] - 2 * width
    scaled = q_ref[:, :width] * jnp.bfloat16(HEAD_DIM ** (-0.5))
    keys = kv_ref[:, key_at : key_at + width]
    values = kv_ref[:, key_at + width : key_at + 2 * width]
    for first in range(0, span, step):
        reach = first + step if causal else span
        parts = []
        for head in range(heads):
            cols = slice(head * HEAD_DIM, (head + 1) * HEAD_DIM)
            scores = masked_scores(
                keys[:reach, cols],
                scaled[first : first + step, cols],
                seg_q[:, first : first + step],
                seg_k[:reach],
                first,
                causal,
            )
            top = jnp.max(scores, axis=0, keepdims=True)
            probs = jnp.exp(scores - top)
            total = jnp.sum(probs, axis=0, keepdims=True)
            mixed = pair_dot(values[:reach, cols], probs.astype(jnp.bfloat16), 0, 0)
            parts.append(mixed / total)
            lse_ref[head : head + 1, first : first + step] = top + jnp.log(total)
        joined = jnp.concatenate(parts, axis=0).T
        full_ref[first : first + step, :] = joined
        low_ref[first : first + step, :] = joined.astype(jnp.bfloat16)


def attn_forward(q_ends, k_ends, queries, keys_values, width, causal):
    span = queries.shape[0]
    return pl.pallas_call(
        functools.partial(attn_forward_body, causal, width),
        out_shape=(
            jax.ShapeDtypeStruct((span, width), jnp.bfloat16),
            jax.ShapeDtypeStruct((span, width), jnp.float32),
            jax.ShapeDtypeStruct((width // HEAD_DIM, span), jnp.float32),
        ),
        in_specs=[smem_spec(), smem_spec()] + [vmem_spec()] * 2,
        out_specs=(vmem_spec(),) * 3,
        compiler_params=pltpu.CompilerParams(vmem_limit_bytes=VMEM_BYTES),
        cost_estimate=cost(8),
        name="attn_forward",
    )(q_ends, k_ends, queries, keys_values)


def attn_backward_body(
    causal,
    width,
    q_ends,
    k_ends,
    q_ref,
    kv_ref,
    up_ref,
    full_ref,
    lse_ref,
    *outs,
):
    dq_ref, dkv_ref = outs[0], outs[-3]
    dk_sum, dv_sum = outs[-2:]
    span = q_ref.shape[0]
    step = math.gcd(span, 256)
    heads = width // HEAD_DIM
    seg_q, seg_k = seg_tables(q_ends, k_ends, span)
    key_at = kv_ref.shape[1] - 2 * width
    scaled = q_ref[:, :width] * jnp.bfloat16(HEAD_DIM ** (-0.5))
    keys = kv_ref[:, key_at : key_at + width]
    values = kv_ref[:, key_at + width : key_at + 2 * width]
    upstream = up_ref[...]
    dk_sum[...] = jnp.zeros_like(dk_sum)
    dv_sum[...] = jnp.zeros_like(dv_sum)
    for first in range(0, span, step):
        reach = first + step if causal else span
        rows = slice(first, first + step)
        product = (upstream[rows].astype(jnp.float32) * full_ref[rows, :]).T
        parts = []
        for head in range(heads):
            cols = slice(head * HEAD_DIM, (head + 1) * HEAD_DIM)
            delta = jnp.sum(product[cols], axis=0, keepdims=True)
            scores = masked_scores(
                keys[:reach, cols], scaled[rows, cols], seg_q[:, rows], seg_k[:reach], first, causal
            )
            probs = jnp.exp(scores - lse_ref[head : head + 1, rows])
            dv_sum[head, :reach] += pair_dot(
                probs.astype(jnp.bfloat16), upstream[rows, cols], 1, 0
            )
            grad_probs = pair_dot(values[:reach, cols], upstream[rows, cols], 1, 1)
            grad_scores = (probs * (grad_probs - delta)).astype(jnp.bfloat16)
            dk_sum[head, :reach] += pair_dot(grad_scores, scaled[rows, cols], 1, 0)
            parts.append(pair_dot(keys[:reach, cols], grad_scores, 0, 0))
        joined = jnp.concatenate(parts, axis=0).T * HEAD_DIM ** (-0.5)
        dq_ref[rows, :width] = joined.astype(jnp.bfloat16)
    sums = [dk_sum[head] for head in range(heads)] + [dv_sum[head] for head in range(heads)]
    kv_at = dkv_ref.shape[1] - 2 * width
    dkv_ref[:, kv_at:] = jnp.concatenate(sums, axis=1).astype(jnp.bfloat16)


def attn_backward(
    q_ends, k_ends, queries, keys_values, upstream, full, lse, causal, joined=False
):
    span, width = upstream.shape
    kinds = [3] if joined else [1, 2]
    heads = width // HEAD_DIM
    return pl.pallas_call(
        functools.partial(attn_backward_body, causal, width),
        out_shape=[jax.ShapeDtypeStruct((span, kind * width), jnp.bfloat16) for kind in kinds],
        in_specs=[smem_spec(), smem_spec()] + [vmem_spec()] * 5,
        out_specs=[vmem_spec()] * len(kinds),
        scratch_shapes=[pltpu.VMEM((heads, span, HEAD_DIM), jnp.float32)] * 2,
        compiler_params=pltpu.CompilerParams(vmem_limit_bytes=VMEM_BYTES),
        cost_estimate=cost(8),
        name="attn_backward",
    )(q_ends, k_ends, queries, keys_values, upstream, full, lse)


def exchange(blocks):
    return lax.all_to_all(blocks, "blk", 0, 0, tiled=True)


def as_rows(blocks):
    return blocks.reshape(blocks.shape[0] * blocks.shape[1], blocks.shape[2])


def as_blocks(rows):
    devices = lax.axis_size("blk")
    return rows.reshape(devices, rows.shape[0] // devices, rows.shape[1])


def write_blocks(out_ref, values, lanes, kind, width):
    span = values.shape[0] // lanes
    for group in range(WIDTH // width):
        for lane in range(lanes):
            out_ref[group * lanes + lane, :, kind * width : (kind + 1) * width] = values[
                lane * span : (lane + 1) * span, group * width : (group + 1) * width
            ]


def read_blocks(got_ref, lanes, kind, width):
    groups = got_ref.shape[0] // lanes
    cols = slice(kind * width, (kind + 1) * width)
    rows = [
        jnp.concatenate([got_ref[group * lanes + lane, :, cols] for group in range(groups)], axis=1)
        for lane in range(lanes)
    ]
    return jnp.concatenate(rows, axis=0)


def dot(left, right):
    return pair_dot(left, right, 1, 0)


def dot_back(left, right):
    return pair_dot(left, right, 1, 1)


def shape(*sizes, of=jnp.float32):
    return jax.ShapeDtypeStruct(sizes, of)


def normalize(values):
    center = values - jnp.mean(values, -1, keepdims=True)
    scale = lax.rsqrt(jnp.mean(center * center, -1, keepdims=True) + 1e-05)
    return center * scale, scale


def norm_back(upstream, normed, scale, gains_row):
    grad = upstream * gains_row
    return scale * (
        grad
        - jnp.mean(grad, -1, keepdims=True)
        - normed * jnp.mean(grad * normed, -1, keepdims=True)
    )


def project_blocks(inputs, parts, lanes, width, name):
    def body(ins, loaded, outs, _):
        for kind, weight in enumerate(loaded):
            write_blocks(
                outs[0], dot(ins[0][...], weight.value()).astype(jnp.bfloat16), lanes, kind, width
            )

    devices, span = lax.axis_size("blk"), inputs.shape[0] // lanes
    (blocks,) = call_with_parts(
        body,
        [inputs],
        parts,
        [shape(devices, span, width * len(parts), of=jnp.bfloat16)],
        name,
    )
    return blocks


def after_self(got, tokens, gains, biases, out_part, query_part, lanes, width):
    def body(ins, loaded, outs, _):
        got_ref, tokens_ref, gains_ref, biases_ref = ins
        low_ref, normed_ref, scale_ref, hidden_ref, blocks_ref = outs
        attended = read_blocks(got_ref, lanes, 0, width)
        low_ref[...] = attended
        resid = tokens_ref[...].astype(jnp.float32) + dot(attended, loaded[0].value())
        normed, scale = normalize(resid)
        normed_ref[...] = normed
        scale_ref[...] = scale
        hidden = (normed * gains_ref[0:1] + biases_ref[0:1]).astype(jnp.bfloat16)
        hidden_ref[...] = hidden
        query = dot(hidden, loaded[1].value()).astype(jnp.bfloat16)
        write_blocks(blocks_ref, query, lanes, 0, width)

    rows = tokens.shape[0]
    return call_with_parts(
        body,
        [got, tokens, gains, biases],
        [out_part, query_part],
        [
            shape(rows, WIDTH, of=jnp.bfloat16),
            shape(rows, WIDTH),
            shape(rows, 1),
            shape(rows, WIDTH, of=jnp.bfloat16),
            shape(*got.shape, of=jnp.bfloat16),
        ],
        "after_self",
    )


def feed_forward(got, normed_in, cotangent, gains, biases, out_part, in_parts, down, outs, up, lanes, width):
    pieces = len(in_parts)
    step = in_parts[0].width

    def body(ins, loaded, refs, scratch):
        got_ref, normed_in_ref, cot_ref, gains_ref, biases_ref = ins
        (
            output_ref,
            low_ref,
            mixed_ref,
            adapted_ref,
            dunder_ref,
            dab_ref,
            dcb_ref,
            dresid_ref,
            blocks_ref,
            norms_ref,
        ) = refs
        (slopes,) = scratch
        w_out, w_in = loaded[0], loaded[1 : 1 + pieces]
        w_down, w_ff, w_up = loaded[1 + pieces :]
        attended = read_blocks(got_ref, lanes, 0, width)
        low_ref[...] = attended
        hidden = normed_in_ref[...] * gains_ref[0:1] + biases_ref[0:1]
        normed_one, scale_one = normalize(hidden + dot(attended, w_out.value()))
        mixed = normed_one * gains_ref[1:2] + biases_ref[1:2]
        mixed_low = mixed.astype(jnp.bfloat16)
        mixed_ref[...] = mixed_low
        summed = mixed
        under = dot(mixed_low, w_down.value())
        gate = 1.0 / (1.0 + jnp.exp(-under))
        adapted = (under * gate).astype(jnp.bfloat16)
        adapted_ref[...] = adapted
        under_slope = gate * (1.0 + under * (1.0 - gate))
        summed = summed + 4.0 * dot(adapted, w_up.value())
        for piece in range(pieces):
            before = dot(mixed_low, w_in[piece].value())
            below = 0.5 + 0.5 * lax.erf(before * (0.5**0.5))
            slopes[piece] = below + before * jnp.exp(-0.5 * before * before) * (
                (2.0 * math.pi) ** -0.5
            )
            act = (before * below).astype(jnp.bfloat16)
            summed = summed + dot(act, w_ff[piece].value())
        normed_two, scale_two = normalize(summed)
        output_ref[...] = (normed_two * gains_ref[2:3] + biases_ref[2:3]).astype(jnp.bfloat16)
        upstream = cot_ref[...].astype(jnp.float32)
        norms_ref[0:1] = jnp.sum(upstream * normed_two, axis=0, keepdims=True)
        norms_ref[1:2] = jnp.sum(upstream, axis=0, keepdims=True)
        dz = norm_back(upstream, normed_two, scale_two, gains_ref[2:3])
        dzb = dz.astype(jnp.bfloat16)
        dab = (4.0 * dz).astype(jnp.bfloat16)
        dab_ref[...] = dab
        dunder = (under_slope * dot_back(dab, w_up.value())).astype(jnp.bfloat16)
        dunder_ref[...] = dunder
        dmixed = dz + dot_back(dunder, w_down.value())
        for piece in range(pieces):
            dpre = (slopes[piece] * dot_back(dzb, w_ff[piece].value())).astype(jnp.bfloat16)
            dmixed = dmixed + dot_back(dpre, w_in[piece].value())
        norms_ref[2:3] = jnp.sum(dmixed * normed_one, axis=0, keepdims=True)
        norms_ref[3:4] = jnp.sum(dmixed, axis=0, keepdims=True)
        dresid = norm_back(dmixed, normed_one, scale_one, gains_ref[1:2])
        dresid_ref[...] = dresid
        dcb = dresid.astype(jnp.bfloat16)
        dcb_ref[...] = dcb
        write_blocks(
            blocks_ref, dot_back(dcb, w_out.value()).astype(jnp.bfloat16), lanes, 0, width
        )

    rows = normed_in.shape[0]
    low = jnp.bfloat16

    def body_rows(ins, loaded, refs, scratch):
        whole_ff = loaded[2 + pieces]

        class Rows:
            def __init__(self, piece):
                self.piece = piece

            def value(self):
                return whole_ff.value()[self.piece * step : (self.piece + 1) * step]

        loaded = loaded[: 2 + pieces] + [[Rows(piece) for piece in range(pieces)], loaded[-1]]
        body(ins, loaded, refs, scratch)

    return call_with_parts(
        body_rows,
        [got, normed_in, cotangent, gains, biases],
        [out_part] + in_parts + [down, outs, up],
        [
            shape(rows, WIDTH, of=low),
            shape(rows, WIDTH, of=low),
            shape(rows, WIDTH, of=low),
            shape(rows, down.width, of=low),
            shape(rows, down.width, of=low),
            shape(rows, WIDTH, of=low),
            shape(rows, WIDTH, of=low),
            shape(rows, WIDTH),
            shape(*got.shape, of=low),
            shape(4, WIDTH),
        ],
        "feed_forward",
        [pltpu.VMEM((pieces, rows, step), jnp.float32)],
        20,
    )


def before_self(got, dresid, normed, scale, gains, query_part, out_part, lanes, width):
    def body(ins, loaded, outs, _):
        got_ref, dresid_ref, normed_ref, scale_ref, gains_ref = ins
        dcq_ref, dr_ref, dsb_ref, blocks_ref, norms_ref = outs
        dcq = read_blocks(got_ref, lanes, 0, width)
        dcq_ref[...] = dcq
        dhidden = dresid_ref[...] + dot_back(dcq, loaded[0].value())
        normed = normed_ref[...]
        norms_ref[0:1] = jnp.sum(dhidden * normed, axis=0, keepdims=True)
        norms_ref[1:2] = jnp.sum(dhidden, axis=0, keepdims=True)
        dr = norm_back(dhidden, normed, scale_ref[...], gains_ref[0:1])
        dr_ref[...] = dr
        dsb = dr.astype(jnp.bfloat16)
        dsb_ref[...] = dsb
        grad = dot_back(dsb, loaded[1].value()).astype(jnp.bfloat16)
        write_blocks(blocks_ref, grad, lanes, 0, width)

    rows = dresid.shape[0]
    return call_with_parts(
        body,
        [got, dresid, normed, scale, gains],
        [query_part, out_part],
        [
            shape(rows, WIDTH, of=jnp.bfloat16),
            shape(rows, WIDTH),
            shape(rows, WIDTH, of=jnp.bfloat16),
            shape(*got.shape, of=jnp.bfloat16),
            shape(2, WIDTH),
        ],
        "before_self",
    )


def input_grad(got, start, parts, lanes, span, width, name):
    def body(ins, loaded, outs, _):
        total = None
        for kind, weight in enumerate(loaded):
            values = read_blocks(ins[0].at[:, :span], lanes, kind, width)
            term = dot_back(values, weight.value())
            total = term if total is None else total + term
        outs[0][...] = total if len(ins) == 1 else total + ins[1][...]

    rows = span * lanes
    return call_with_parts(
        body,
        [got] if start is None else [got, start],
        parts,
        [shape(rows, WIDTH)],
        name,
    )


def sum_everywhere(values, stages):
    if not paired():
        return lax.psum(values, ("dp", "blk"))
    values = after(values, stages[0])
    values = values + swap_core(values)
    for step, bit in enumerate((1, 2, 4, 8)):
        if step + 1 < len(stages):
            values = after(values, stages[step + 1])
        values = values + flip(values, bit)
    return values


def shards(
    tokens,
    encoder,
    cotangent,
    self_in,
    self_out,
    cross_q,
    cross_kv,
    cross_out,
    ffn_in,
    ffn_out,
    adapt_down,
    adapt_up,
    norm_gain,
    norm_bias,
    tgt_lengths,
    src_lengths,
):
    lanes, span, _ = tokens.shape
    rows = lanes * span
    width = WIDTH * lanes // lax.axis_size("blk")
    own_row = lax.axis_index("blk") % lanes
    tgt_ends = jnp.cumsum(lax.dynamic_index_in_dim(tgt_lengths, own_row, 0, keepdims=False))
    src_ends = jnp.cumsum(lax.dynamic_index_in_dim(src_lengths, own_row, 0, keepdims=False))
    flat_tokens = tokens.reshape(rows, WIDTH)
    flat_encoder = encoder.reshape(rows, WIDTH)
    frozen = [ffn_in, adapt_down, ffn_out, adapt_up, cross_out]
    inward = [self_in, cross_kv]

    if paired():
        self_heads = head_columns(self_in, 3)
        token_row = gather_row(tokens)
        packed = gather_packed(after(frozen, token_row.source.stages[0]))
        out_shard, query_shard, pair_shard, encoder_block = after(
            (self_out, cross_q, cross_kv, encoder), token_row.source.stages[1]
        )
        out_source, query_source = gather_flips([out_shard, query_shard], "xy")
        pair_heads = head_columns(pair_shard, 2)
        encoder_row = gather_row(
            after(encoder_block, out_source.stages[0], query_source.stages[0])
        )
        self_qkv = project_row(token_row, self_heads, "self_in")
        pair_own = project_row(encoder_row, pair_heads, "cross_kv")
    else:
        (self_source, pair_source, out_source, query_source) = gather_flips(
            [self_in, cross_kv, self_out, cross_q], "xyxy"
        )
        self_parts = [columns_of((self_source, WIDTH * kind, WIDTH)) for kind in range(3)]
        pair_parts = [columns_of((pair_source, WIDTH * kind, WIDTH)) for kind in range(2)]
        self_qkv = as_rows(
            exchange(project_blocks(flat_tokens, self_parts, lanes, width, "self_in"))
        )
        pair_own = as_rows(
            exchange(project_blocks(flat_encoder, pair_parts, lanes, width, "cross_kv"))
        )
    self_out_part = columns_of((out_source, 0, WIDTH))
    query_part = columns_of((query_source, 0, WIDTH))

    self_mid, self_full, self_lse = attn_forward(
        tgt_ends, tgt_ends, self_qkv, self_qkv, width, True
    )
    self_low, normed, scale, hidden_low, query_blocks = after_self(
        exchange(as_blocks(self_mid)),
        flat_tokens,
        norm_gain,
        norm_bias,
        self_out_part,
        query_part,
        lanes,
        width,
    )
    ready = after(packed, query_blocks) if paired() else None
    ff_parts, down_parts, ffo_parts, up_parts, (cross_out_part,) = packed_parts(frozen, ready)
    cross_own = as_rows(exchange(query_blocks))
    cross_mid, cross_full, cross_lse = attn_forward(
        tgt_ends, src_ends, cross_own, pair_own, width, False
    )
    (
        output,
        cross_low,
        mixed_low,
        adapter_low,
        grad_under,
        adapt_low,
        cross_branch_low,
        grad_resid_two,
        cross_grad_blocks,
        norms_high,
    ) = feed_forward(
        exchange(as_blocks(cross_mid)),
        normed,
        cotangent.reshape(rows, WIDTH),
        norm_gain,
        norm_bias,
        cross_out_part,
        ff_parts,
        down_parts[0],
        ffo_parts[0],
        up_parts[0],
        lanes,
        width,
    )
    if paired():
        inward_packed = gather_packed(after(inward, cross_mid))
    high_pairs = [(cross_low, cross_branch_low), (mixed_low, grad_under), (adapter_low, adapt_low)]
    high_terms = grad_terms(high_pairs)
    (high_grads,), high_stages = reduce_terms([high_pairs], [high_terms], [True])
    grad_cross_out, grad_adapt_down, grad_adapt_up = high_grads
    cross_dq, cross_dkv = attn_backward(
        tgt_ends,
        src_ends,
        cross_own,
        pair_own,
        as_rows(after(exchange(cross_grad_blocks), high_stages[0])),
        cross_full,
        cross_lse,
        False,
    )
    cq_low, grad_resid_one, self_branch_low, self_grad_blocks, norms_low = before_self(
        after(exchange(as_blocks(cross_dq)), high_stages[1]),
        grad_resid_two,
        normed,
        scale,
        norm_gain,
        query_part,
        self_out_part,
        lanes,
        width,
    )
    mid_pairs = [(hidden_low, cq_low), (self_low, self_branch_low)]
    (mid_grads,), mid_stages = reduce_terms([mid_pairs], [grad_terms(mid_pairs)], [False])
    grad_cross_q, grad_self_out = mid_grads
    (self_grads,) = attn_backward(
        tgt_ends,
        tgt_ends,
        self_qkv,
        self_qkv,
        as_rows(after(exchange(self_grad_blocks), high_stages[2])),
        self_full,
        self_lse,
        True,
        joined=True,
    )
    pair_got = as_blocks(cross_dkv)
    self_got = as_blocks(self_grads)
    if paired():
        self_parts, pair_parts = packed_parts(inward, after(inward_packed, self_grad_blocks))
        pair_got = exchange(
            jnp.concatenate([pair_got, row_grad(encoder_row, cross_dkv, "cross_kv_grad")], axis=1)
        )
        self_got = exchange(
            jnp.concatenate([self_got, row_grad(token_row, self_grads, "self_in_grad")], axis=1)
        )
        grad_cross_kv = finish_row_grad(pair_got[:, span:], 2)
        grad_self_in = finish_row_grad(self_got[:, span:], 3)
    else:
        pair_got, self_got = exchange(pair_got), exchange(self_got)
        pair_low = pair_got.reshape(-1, lanes, span, 2, width).transpose(1, 2, 3, 0, 4)
        self_back = self_got.reshape(-1, lanes, span, 3, width).transpose(1, 2, 3, 0, 4)
        grad_cross_kv = weight_grad(flat_encoder, pair_low.reshape(rows, 2 * WIDTH))
        grad_self_in = weight_grad(flat_tokens, self_back.reshape(rows, 3 * WIDTH))
    (encoder_grad,) = input_grad(pair_got, None, pair_parts, lanes, span, width, "encoder_grad")
    (tokens_grad,) = input_grad(
        self_got, grad_resid_one, self_parts, lanes, span, width, "tokens_grad"
    )
    norms = sum_everywhere(jnp.concatenate([norms_low, norms_high], axis=0), mid_stages)
    return (
        output.reshape(lanes, span, WIDTH),
        tokens_grad.reshape(lanes, span, WIDTH),
        encoder_grad.reshape(lanes, span, WIDTH),
        grad_self_in,
        grad_self_out,
        grad_cross_q,
        grad_cross_kv,
        grad_cross_out,
        grad_adapt_down,
        grad_adapt_up,
        jnp.stack([norms[0], norms[4], norms[2]]),
        jnp.stack([norms[1], norms[5], norms[3]]),
    )


def solution(mesh):
    placed = (
        P("dp", "blk", None),
        P("dp", "blk", None),
        P("dp", "blk", None),
        P("blk", None),
        P("blk", None),
        P("blk", None),
        P("blk", None),
        P("blk", None),
        P("blk", None),
        P("blk", None),
        P("blk", None),
        P("blk", None),
        P(),
        P(),
        P("dp", None),
        P("dp", None),
    )
    return jax.shard_map(
        shards,
        mesh=mesh,
        in_specs=placed,
        out_specs=(
            P("dp", "blk", None),
            P("dp", "blk", None),
            P("dp", "blk", None),
            P("blk", None),
            P("blk", None),
            P("blk", None),
            P("blk", None),
            P("blk", None),
            P("blk", None),
            P("blk", None),
            P(),
            P(),
        ),
        check_vma=False,
    )
```

```python
import functools
import math

import jax
import jax.numpy as jnp
from jax import lax
from jax.experimental import pallas as pl
from jax.experimental.pallas import tpu as pltpu
from jax.sharding import PartitionSpec as P

HEADS = 16
HEAD_DIM = 64
WIDTH = HEADS * HEAD_DIM


NEG = -1e30
VMEM_BYTES = 56 * 1024 * 1024


def cost(microseconds):
    return pl.CostEstimate(
        flops=int(microseconds * 0.4e9),
        bytes_accessed=int(microseconds * 1.2e6),
        transcendentals=0,
    )


def paired():
    return lax.axis_size("blk") == 16 and lax.axis_size("dp") == 2


def swap_core(block):
    cores = lax.axis_size("dp")
    return lax.ppermute(block, "dp", [(i ^ 1, i) for i in range(cores)])


def flip(block, bit):
    chips = lax.axis_size("blk")
    return lax.ppermute(block, "blk", [(i ^ bit, i) for i in range(chips)])


FLIPS = (8, 4, 2, 1)


def with_flip(block, bit):
    return jnp.stack([block, flip(block, bit)])


def own_half(values, which):
    half = values.shape[1] // 2
    return lax.dynamic_slice_in_dim(values, which * half, half, 1)


def scatter_chips(terms, orders, hold, held_stage):
    own = lax.axis_index("blk")

    def fold(blocks, left, bit):
        axis, place = left.index(bit), (own // bit) % 2
        kept = lax.dynamic_index_in_dim(blocks, place, axis, keepdims=False)
        sent = lax.dynamic_index_in_dim(blocks, 1 - place, axis, keepdims=False)
        got = flip(sent, bit)
        return (kept.astype(jnp.float32) + got.astype(jnp.float32)).astype(jnp.bfloat16)

    terms = [blocks.reshape(2, 2, 2, 2, *blocks.shape[1:]) for blocks in terms]
    stages = [terms[0]]
    for stage in range(4):
        if hold is not None and stage == held_stage:
            terms = after(terms, hold)
        terms = [
            fold(blocks, [bit for bit in FLIPS if bit not in order[:stage]], order[stage])
            for blocks, order in zip(terms, orders)
        ]
        stages.append(terms[0])
    return terms, stages


CHUNK = 256


def grad_terms(pairs):
    if not paired():
        return None
    core = lax.axis_index("dp")
    packed = []
    for inputs, upstream in pairs:
        both = jnp.concatenate([inputs, swap_core(inputs)], axis=0)
        half = jnp.concatenate(
            [own_half(upstream, core), swap_core(own_half(upstream, 1 - core))], axis=0
        )
        term = lax.dot_general(
            both, half, (((0,), (0,)), ((), ())), preferred_element_type=jnp.float32
        ).astype(jnp.bfloat16)
        rows = term.shape[0] // 16
        chunks = term.shape[1] // CHUNK
        packed += [
            term[:, c * CHUNK : (c + 1) * CHUNK].reshape(16, rows, CHUNK) for c in range(chunks)
        ]
    return jnp.concatenate(packed, axis=1)


def reduce_terms(groups, terms, orders, hold=None, held_stage=0):
    if not paired():
        found = [[weight_grad(inputs, upstream) for inputs, upstream in pairs] for pairs in groups]
        return found, [groups[0][0][1]] * 5
    core = lax.axis_index("dp")
    totals, stages = scatter_chips(terms, orders, hold, held_stage)
    mine = jnp.concatenate(totals, axis=0)
    other = swap_core(mine)
    low = jnp.where(core == 0, mine, other).astype(jnp.float32)
    high = jnp.where(core == 0, other, mine).astype(jnp.float32)
    found, place = [], 0
    for pairs in groups:
        found.append([])
        for inputs, upstream in pairs:
            rows = inputs.shape[1] // 16
            chunks = upstream.shape[1] // 2 // CHUNK
            spots = [slice(place + c * rows, place + (c + 1) * rows) for c in range(chunks)]
            found[-1].append(
                jnp.concatenate(
                    [low[spot] for spot in spots] + [high[spot] for spot in spots], axis=1
                )
            )
            place += rows * chunks
    return found, stages


def weight_grad(inputs, upstream):
    scattered = lax.psum_scatter(
        lax.dot_general(
            inputs, upstream, (((0,), (0,)), ((), ())), preferred_element_type=jnp.float32
        ).astype(jnp.bfloat16),
        "blk",
        scatter_dimension=0,
        tiled=True,
    )
    return lax.psum(scattered, "dp").astype(jnp.float32)


class Source:
    def __init__(self, kind, arrays, first_flip="x", column=None):
        self.kind, self.arrays, self.first_flip = kind, arrays, first_flip
        self.stages = arrays[:1] * 3 if column is None else [column] + arrays[:2]


class Part:
    def __init__(self, rows, width, spots):
        self.rows, self.width, self.spots = rows, width, spots

    def scratch(self):
        return pltpu.VMEM((2, 2, 2, 2, 2, self.rows // 32, self.width), jnp.bfloat16)

    def start(self, refs_of, place, dst, sem):
        z1, z0, y, x, core = [place[axis] for axis in range(5)]
        high = self.rows // 32
        for source, first_row, first_col, at_col, width in self.spots:
            refs = refs_of(source)
            cols = slice(first_col, first_col + width)
            into = slice(at_col, at_col + width)
            if source.kind == "whole":
                pltpu.make_async_copy(
                    refs[0].at[:, :, :, :, :, :, cols], dst.at[:, :, :, :, :, :, into], sem
                ).start()
            elif source.kind == "cores":
                for which in range(2):
                    owner = core if which == 0 else 1 - core
                    pltpu.make_async_copy(
                        refs[which].at[:, :, :, :, first_row : first_row + high, cols],
                        dst.at[:, :, :, :, owner, :, into],
                        sem,
                    ).start()
            else:
                for which in range(4):
                    owner = core if which < 2 else 1 - core
                    for near, at_y, at_x in flipped(source.first_flip, which % 2, y, x):
                        for up, at_z1, at_z0 in four(z1, z0):
                            pltpu.make_async_copy(
                                refs[which].at[near, up[0], up[1], :, cols],
                                dst.at[at_z1, at_z0, at_y, at_x, owner, :, into],
                                sem,
                            ).start()


def four(z1, z0):
    return [
        ((low, high), z1 if high == 0 else 1 - z1, z0 if low == 0 else 1 - z0)
        for low in range(2)
        for high in range(2)
    ]


def flipped(first_flip, beyond, y, x):
    found = []
    for near in range(2):
        a, b = (near, beyond) if first_flip == "x" else (beyond, near)
        found.append((near, y if b == 0 else 1 - y, x if a == 0 else 1 - x))
    return found


def after(value, *others):
    return lax.optimization_barrier((value, *others))[0]


def gather_flips(shards, first_flips, hold=None):
    if not paired():
        full = [lax.all_gather(shard, "blk", axis=0, tiled=True) for shard in shards]
        return [
            Source("whole", [array.reshape(2, 2, 2, 2, 2, array.shape[0] // 32, array.shape[1])])
            for array in full
        ]
    core = lax.axis_index("dp")
    columns = []
    for shard in shards:
        rows = shard.shape[0]
        own = lax.dynamic_slice_in_dim(shard, core * (rows // 2), rows // 2, 0)
        columns.append(with_flip(with_flip(own, 8), 4))
    sources, bits = [], {"x": (1, 2), "y": (2, 1)}
    if hold is not None:
        columns = after(columns, hold)
    planes = [
        with_flip(column, bits[first][0]) for column, first in zip(columns, first_flips)
    ]
    for column, plane, first in zip(columns, planes, first_flips):
        beyond = flip(plane, bits[first][1])
        sources.append(
            Source("flips", [plane, beyond, swap_core(plane), swap_core(beyond)], first, column)
        )
    return sources


class RowPart:
    def __init__(self, sources, span):
        self.span = span
        self.rows, self.width = 16 * span, WIDTH
        self.spots = [(source,) for source in sources]

    def scratch(self):
        return pltpu.VMEM((2, 2, 2, 2, self.span, WIDTH), jnp.bfloat16)

    def start(self, refs_of, place, dst, sem):
        z1, z0, y, x = [place[axis] for axis in range(4)]
        half = WIDTH // 2
        for side, (source,) in enumerate(self.spots):
            refs = refs_of(source)
            for beyond in range(2):
                for near, at_y, at_x in flipped(source.first_flip, beyond, y, x):
                    for up, at_z1, at_z0 in four(z1, z0):
                        pltpu.make_async_copy(
                            refs[beyond].at[near, up[0], up[1]],
                            dst.at[at_z1, at_z0, at_y, at_x, :, side * half : (side + 1) * half],
                            sem,
                        ).start()


def gather_row(block, hold=None):
    row = lax.axis_index("blk") // 8
    own = lax.dynamic_index_in_dim(block, row, 0, keepdims=False)
    other = lax.dynamic_index_in_dim(block, 1 - row, 0, keepdims=False)
    pair = jnp.stack([own, flip(other, 8)])
    column = with_flip(pair, 4)
    stages, sources = [pair, column], []
    if hold is not None:
        column = after(column, hold)
    half = WIDTH // 2
    planes = [with_flip(column[..., :half], 1), with_flip(column[..., half:], 2)]
    for plane, first, bit in zip(planes, "xy", (2, 1)):
        sources.append(Source("row", [plane, flip(plane, bit)], first))
    stages += [planes, [source.arrays[1] for source in sources]]
    return RowPart(sources, block.shape[1]), stages


def head_columns(shards, kinds):
    core = lax.axis_index("dp")
    blocks, widths = [], [128 * kind for kind in kinds]
    for shard, kind in zip(shards, kinds):
        own = lax.dynamic_slice_in_dim(shard, core * 32, 32, 0)
        own = own.reshape(32, kind, 8, 128).transpose(2, 0, 1, 3)
        blocks.append(own.reshape(8, 32, kind * 128))
    blocks = jnp.concatenate(blocks, axis=2)
    mine = exchange(jnp.concatenate([blocks, blocks], axis=0))
    mine = mine.reshape(2, 2, 2, 2, 32, sum(widths))
    source = Source("cores", [mine, swap_core(mine)])
    parts, place = [], 0
    for width in widths:
        parts.append(Part(1024, width, [(source, 0, place, 0, width)]))
        place += width
    return parts


def project_row(row_part, head_part, name):
    def body(ins, loaded, outs, _):
        weight = loaded[1].value()
        inputs = loaded[0].value()
        for first in range(0, row_part.rows, 256):
            rows = slice(first, first + 256)
            outs[0][rows, :] = dot(inputs[rows], weight).astype(jnp.bfloat16)

    (found,) = call_with_parts(
        body,
        [],
        [row_part, head_part],
        [shape(row_part.rows, head_part.width, of=jnp.bfloat16)],
        name,
    )
    return found


def row_grad(row_part, upstream, name):
    columns = upstream.shape[1]

    def body(ins, loaded, outs, _):
        core = ins[1][0]
        inputs = loaded[0].value()
        grads = []
        for first in range(0, columns, 128):
            grads.append(pair_dot(ins[0][:, first : first + 128], inputs, 0, 0).T)
        grad = jnp.concatenate(grads, axis=1).astype(jnp.bfloat16).reshape(16, 2, 32, columns)
        outs[0][core] = grad[:, 0]
        outs[0][1 - core] = grad[:, 1]

    (terms,) = call_with_parts(
        body,
        [upstream],
        [row_part],
        [shape(2, 16, 32, columns, of=jnp.bfloat16)],
        name,
        scalars=[lax.axis_index("dp").reshape(1).astype(jnp.int32)],
    )
    got = swap_core(terms[1])
    return (terms[0].astype(jnp.float32) + got.astype(jnp.float32)).astype(jnp.bfloat16)


def finish_row_grad(got, kinds):
    total = jnp.sum(got.reshape(2, 8, 32, kinds, 128).astype(jnp.float32), axis=0)
    mine = total.astype(jnp.bfloat16).transpose(1, 2, 0, 3).reshape(32, kinds * WIDTH)
    other = swap_core(mine)
    core = lax.axis_index("dp")
    low = jnp.where(core == 0, mine, other)
    high = jnp.where(core == 0, other, mine)
    return jnp.concatenate([low, high], axis=0).astype(jnp.float32)


def columns_of(*pieces):
    spots, place = [], 0
    for source, first, width in pieces:
        spots.append((source, 0, first, place, width))
        place += width
    return Part(1024, place, spots)


PACK = 512


def gather_packed(shards):
    core = lax.axis_index("dp")
    packed = []
    for shard in shards:
        high = shard.shape[0] // 2
        own = lax.dynamic_slice_in_dim(shard, core * high, high, 0)
        packed += [own[:, first : first + PACK] for first in range(0, shard.shape[1], PACK)]
    return lax.all_gather(jnp.concatenate(packed, axis=0), "blk", axis=0)


def packed_parts(shards, mine):
    if not paired():
        found = []
        for source, shard in zip(gather_flips(shards, "x" * len(shards)), shards):
            rows, columns = 32 * source.arrays[0].shape[5], shard.shape[1]
            step = min(columns, 1024)
            found.append(
                [
                    Part(rows, step, [(source, 0, first, 0, step)])
                    for first in range(0, columns, step)
                ]
            )
        return found
    spots, place = [], 0
    for shard in shards:
        high = shard.shape[0] // 2
        places = []
        for first in range(0, shard.shape[1], PACK):
            places.append(place)
            place += high
        spots.append((shard.shape[0] * 16, places))
    mine = mine.reshape(2, 2, 2, 2, place, PACK)
    source = Source("cores", [mine, swap_core(mine)])
    found = []
    for rows, places in spots:
        parts = []
        for first in range(0, len(places), 2):
            two = places[first : first + 2]
            parts.append(
                Part(
                    rows,
                    PACK * len(two),
                    [(source, row, 0, PACK * side, PACK) for side, row in enumerate(two)],
                )
            )
        found.append(parts)
    return found


def place_now():
    own, core = lax.axis_index("blk"), lax.axis_index("dp")
    bits = [(own // bit) % 2 for bit in FLIPS]
    return jnp.stack(bits + [core]).astype(jnp.int32)


class Loaded:
    def __init__(self, part, dst, sem):
        self.part, self.dst, self.sem, self.here = part, dst, sem, False

    def value(self):
        if not self.here:
            pltpu.make_async_copy(self.dst, self.dst, self.sem).wait()
            self.here = True
        return self.dst[...].reshape(self.part.rows, self.part.width)


def call_with_parts(body, inputs, parts, outputs, name, scratch=(), takes=5, scalars=()):
    sources = []
    for part in parts:
        sources += [spot[0] for spot in part.spots if spot[0] not in sources]
    arrays = [array for source in sources for array in source.arrays]

    def kernel(place, *refs):
        refs = list(refs)
        ins = [refs.pop(0) for _ in (*inputs, *scalars)]
        pieces = [[refs.pop(0) for _ in source.arrays] for source in sources]
        outs = [refs.pop(0) for _ in outputs]
        dsts = [refs.pop(0) for _ in parts]
        sems = refs.pop(0)
        loaded = []
        for index, part in enumerate(parts):
            part.start(
                lambda source: pieces[sources.index(source)], place, dsts[index], sems.at[index]
            )
            loaded.append(Loaded(part, dsts[index], sems.at[index]))
        body(ins, loaded, outs, refs)

    return pl.pallas_call(
        kernel,
        out_shape=tuple(outputs),
        in_specs=[smem_spec()]
        + [vmem_spec()] * len(inputs)
        + [smem_spec()] * len(scalars)
        + [pl.BlockSpec(memory_space=pl.ANY)] * len(arrays),
        out_specs=(vmem_spec(),) * len(outputs),
        scratch_shapes=[part.scratch() for part in parts]
        + [pltpu.SemaphoreType.DMA((len(parts),))]
        + list(scratch),
        compiler_params=pltpu.CompilerParams(vmem_limit_bytes=VMEM_BYTES),
        cost_estimate=cost(takes),
        name=name,
    )(place_now(), *inputs, *scalars, *arrays)


def vmem_spec():
    return pl.BlockSpec(memory_space=pltpu.VMEM)


def smem_spec():
    return pl.BlockSpec(memory_space=pltpu.SMEM)


def seg_of_pos(ends_ref, pos):
    seg = jnp.zeros(pos.shape, jnp.int32)
    for slot in range(ends_ref.shape[0]):
        seg = seg + (ends_ref[slot] <= pos).astype(jnp.int32)
    return seg


def pair_dot(left, right, left_dim, right_dim):
    return lax.dot_general(
        left, right, (((left_dim,), (right_dim,)), ((), ())), preferred_element_type=jnp.float32
    )


def seg_tables(q_ends, k_ends, span):
    seg_q = seg_of_pos(q_ends, lax.broadcasted_iota(jnp.int32, (1, span), 1))
    seg_k = seg_of_pos(k_ends, lax.broadcasted_iota(jnp.int32, (span, 1), 0))
    return seg_q, seg_k


def masked_scores(keys, queries, seg_q, seg_k, first, causal):
    scores = pair_dot(keys, queries, 1, 1)
    allowed = seg_k == seg_q
    if causal:
        key_pos = lax.broadcasted_iota(jnp.int32, scores.shape, 0)
        query_pos = first + lax.broadcasted_iota(jnp.int32, scores.shape, 1)
        allowed = allowed & (key_pos <= query_pos)
    return jnp.where(allowed, scores, NEG)


def attn_forward_body(causal, width, q_ends, k_ends, q_ref, kv_ref, low_ref, full_ref, lse_ref):
    span = q_ref.shape[0]
    step = math.gcd(span, 256)
    heads = width // HEAD_DIM
    seg_q, seg_k = seg_tables(q_ends, k_ends, span)
    key_at = kv_ref.shape[1] - 2 * width
    scaled = q_ref[:, :width] * jnp.bfloat16(HEAD_DIM ** (-0.5))
    keys = kv_ref[:, key_at : key_at + width]
    values = kv_ref[:, key_at + width : key_at + 2 * width]
    for first in range(0, span, step):
        reach = first + step if causal else span
        parts = []
        for head in range(heads):
            cols = slice(head * HEAD_DIM, (head + 1) * HEAD_DIM)
            scores = masked_scores(
                keys[:reach, cols],
                scaled[first : first + step, cols],
                seg_q[:, first : first + step],
                seg_k[:reach],
                first,
                causal,
            )
            top = jnp.max(scores, axis=0, keepdims=True)
            probs = jnp.exp(scores - top)
            total = jnp.sum(probs, axis=0, keepdims=True)
            mixed = pair_dot(values[:reach, cols], probs.astype(jnp.bfloat16), 0, 0)
            parts.append(mixed / total)
            lse_ref[head : head + 1, first : first + step] = top + jnp.log(total)
        joined = jnp.concatenate(parts, axis=0).T
        full_ref[first : first + step, :] = joined
        low_ref[first : first + step, :] = joined.astype(jnp.bfloat16)


def attn_forward(q_ends, k_ends, queries, keys_values, width, causal):
    span = queries.shape[0]
    return pl.pallas_call(
        functools.partial(attn_forward_body, causal, width),
        out_shape=(
            jax.ShapeDtypeStruct((span, width), jnp.bfloat16),
            jax.ShapeDtypeStruct((span, width), jnp.float32),
            jax.ShapeDtypeStruct((width // HEAD_DIM, span), jnp.float32),
        ),
        in_specs=[smem_spec(), smem_spec()] + [vmem_spec()] * 2,
        out_specs=(vmem_spec(),) * 3,
        compiler_params=pltpu.CompilerParams(vmem_limit_bytes=VMEM_BYTES),
        cost_estimate=cost(8),
        name="attn_forward",
    )(q_ends, k_ends, queries, keys_values)


def attn_backward_body(
    causal,
    width,
    q_ends,
    k_ends,
    q_ref,
    kv_ref,
    up_ref,
    full_ref,
    lse_ref,
    *outs,
):
    dq_ref, dkv_ref = outs[0], outs[-3]
    dk_sum, dv_sum = outs[-2:]
    span = q_ref.shape[0]
    step = math.gcd(span, 256)
    heads = width // HEAD_DIM
    seg_q, seg_k = seg_tables(q_ends, k_ends, span)
    key_at = kv_ref.shape[1] - 2 * width
    scaled = q_ref[:, :width] * jnp.bfloat16(HEAD_DIM ** (-0.5))
    keys = kv_ref[:, key_at : key_at + width]
    values = kv_ref[:, key_at + width : key_at + 2 * width]
    upstream = up_ref[...]
    dk_sum[...] = jnp.zeros_like(dk_sum)
    dv_sum[...] = jnp.zeros_like(dv_sum)
    for first in range(0, span, step):
        reach = first + step if causal else span
        rows = slice(first, first + step)
        product = (upstream[rows].astype(jnp.float32) * full_ref[rows, :]).T
        parts = []
        for head in range(heads):
            cols = slice(head * HEAD_DIM, (head + 1) * HEAD_DIM)
            delta = jnp.sum(product[cols], axis=0, keepdims=True)
            scores = masked_scores(
                keys[:reach, cols], scaled[rows, cols], seg_q[:, rows], seg_k[:reach], first, causal
            )
            probs = jnp.exp(scores - lse_ref[head : head + 1, rows])
            dv_sum[head, :reach] += pair_dot(
                probs.astype(jnp.bfloat16), upstream[rows, cols], 1, 0
            )
            grad_probs = pair_dot(values[:reach, cols], upstream[rows, cols], 1, 1)
            grad_scores = (probs * (grad_probs - delta)).astype(jnp.bfloat16)
            dk_sum[head, :reach] += pair_dot(grad_scores, scaled[rows, cols], 1, 0)
            parts.append(pair_dot(keys[:reach, cols], grad_scores, 0, 0))
        joined = jnp.concatenate(parts, axis=0).T * HEAD_DIM ** (-0.5)
        dq_ref[rows, :width] = joined.astype(jnp.bfloat16)
    sums = [dk_sum[head] for head in range(heads)] + [dv_sum[head] for head in range(heads)]
    kv_at = dkv_ref.shape[1] - 2 * width
    dkv_ref[:, kv_at:] = jnp.concatenate(sums, axis=1).astype(jnp.bfloat16)


def attn_backward(
    q_ends, k_ends, queries, keys_values, upstream, full, lse, causal, joined=False
):
    span, width = upstream.shape
    kinds = [3] if joined else [1, 2]
    heads = width // HEAD_DIM
    return pl.pallas_call(
        functools.partial(attn_backward_body, causal, width),
        out_shape=[jax.ShapeDtypeStruct((span, kind * width), jnp.bfloat16) for kind in kinds],
        in_specs=[smem_spec(), smem_spec()] + [vmem_spec()] * 5,
        out_specs=[vmem_spec()] * len(kinds),
        scratch_shapes=[pltpu.VMEM((heads, span, HEAD_DIM), jnp.float32)] * 2,
        compiler_params=pltpu.CompilerParams(vmem_limit_bytes=VMEM_BYTES),
        cost_estimate=cost(8),
        name="attn_backward",
    )(q_ends, k_ends, queries, keys_values, upstream, full, lse)


def exchange(blocks):
    return lax.all_to_all(blocks, "blk", 0, 0, tiled=True)


def as_rows(blocks):
    return blocks.reshape(blocks.shape[0] * blocks.shape[1], blocks.shape[2])


def as_blocks(rows):
    devices = lax.axis_size("blk")
    return rows.reshape(devices, rows.shape[0] // devices, rows.shape[1])


def write_blocks(out_ref, values, lanes, kind, width):
    span = values.shape[0] // lanes
    for group in range(WIDTH // width):
        for lane in range(lanes):
            out_ref[lane * (WIDTH // width) + group, :, kind * width : (kind + 1) * width] = values[
                lane * span : (lane + 1) * span, group * width : (group + 1) * width
            ]


def read_blocks(got_ref, lanes, kind, width):
    groups = got_ref.shape[0] // lanes
    cols = slice(kind * width, (kind + 1) * width)
    rows = [
        jnp.concatenate([got_ref[lane * groups + group, :, cols] for group in range(groups)], axis=1)
        for lane in range(lanes)
    ]
    return jnp.concatenate(rows, axis=0)


def dot(left, right):
    return pair_dot(left, right, 1, 0)


def dot_back(left, right):
    return pair_dot(left, right, 1, 1)


def shape(*sizes, of=jnp.float32):
    return jax.ShapeDtypeStruct(sizes, of)


def normalize(values):
    center = values - jnp.mean(values, -1, keepdims=True)
    scale = lax.rsqrt(jnp.mean(center * center, -1, keepdims=True) + 1e-05)
    return center * scale, scale


def norm_back(upstream, normed, scale, gains_row):
    grad = upstream * gains_row
    return scale * (
        grad
        - jnp.mean(grad, -1, keepdims=True)
        - normed * jnp.mean(grad * normed, -1, keepdims=True)
    )


def project_blocks(inputs, parts, lanes, width, name):
    def body(ins, loaded, outs, _):
        for kind, weight in enumerate(loaded):
            write_blocks(
                outs[0], dot(ins[0][...], weight.value()).astype(jnp.bfloat16), lanes, kind, width
            )

    devices, span = lax.axis_size("blk"), inputs.shape[0] // lanes
    (blocks,) = call_with_parts(
        body,
        [inputs],
        parts,
        [shape(devices, span, width * len(parts), of=jnp.bfloat16)],
        name,
    )
    return blocks


def after_self(got, tokens, gains, biases, out_part, query_part, lanes, width):
    def body(ins, loaded, outs, _):
        got_ref, tokens_ref, gains_ref, biases_ref = ins
        low_ref, normed_ref, scale_ref, hidden_ref, blocks_ref = outs
        attended = read_blocks(got_ref, lanes, 0, width)
        low_ref[...] = attended
        resid = tokens_ref[...].astype(jnp.float32) + dot(attended, loaded[0].value())
        normed, scale = normalize(resid)
        normed_ref[...] = normed
        scale_ref[...] = scale
        hidden = (normed * gains_ref[0:1] + biases_ref[0:1]).astype(jnp.bfloat16)
        hidden_ref[...] = hidden
        query = dot(hidden, loaded[1].value()).astype(jnp.bfloat16)
        write_blocks(blocks_ref, query, lanes, 0, width)

    rows = tokens.shape[0]
    return call_with_parts(
        body,
        [got, tokens, gains, biases],
        [out_part, query_part],
        [
            shape(rows, WIDTH, of=jnp.bfloat16),
            shape(rows, WIDTH),
            shape(rows, 1),
            shape(rows, WIDTH, of=jnp.bfloat16),
            shape(*got.shape, of=jnp.bfloat16),
        ],
        "after_self",
    )


def feed_forward(got, normed_in, cotangent, gains, biases, out_part, in_parts, down, outs, up, lanes, width):
    pieces = len(in_parts)
    step = in_parts[0].width

    def body(ins, loaded, refs, scratch):
        got_ref, normed_in_ref, cot_ref, gains_ref, biases_ref = ins
        (
            output_ref,
            low_ref,
            mixed_ref,
            adapted_ref,
            dunder_ref,
            dab_ref,
            dcb_ref,
            dresid_ref,
            blocks_ref,
            norms_ref,
        ) = refs
        (slopes,) = scratch
        w_out, w_in = loaded[0], loaded[1 : 1 + pieces]
        w_down, w_ff, w_up = loaded[1 + pieces :]
        attended = read_blocks(got_ref, lanes, 0, width)
        low_ref[...] = attended
        hidden = normed_in_ref[...] * gains_ref[0:1] + biases_ref[0:1]
        normed_one, scale_one = normalize(hidden + dot(attended, w_out.value()))
        mixed = normed_one * gains_ref[1:2] + biases_ref[1:2]
        mixed_low = mixed.astype(jnp.bfloat16)
        mixed_ref[...] = mixed_low
        summed = mixed
        under = dot(mixed_low, w_down.value())
        gate = 1.0 / (1.0 + jnp.exp(-under))
        adapted = (under * gate).astype(jnp.bfloat16)
        adapted_ref[...] = adapted
        under_slope = gate * (1.0 + under * (1.0 - gate))
        summed = summed + 4.0 * dot(adapted, w_up.value())
        for piece in range(pieces):
            before = dot(mixed_low, w_in[piece].value())
            below = 0.5 + 0.5 * lax.erf(before * (0.5**0.5))
            slopes[piece] = below + before * jnp.exp(-0.5 * before * before) * (
                (2.0 * math.pi) ** -0.5
            )
            act = (before * below).astype(jnp.bfloat16)
            summed = summed + dot(act, w_ff[piece].value())
        normed_two, scale_two = normalize(summed)
        output_ref[...] = (normed_two * gains_ref[2:3] + biases_ref[2:3]).astype(jnp.bfloat16)
        upstream = cot_ref[...].astype(jnp.float32)
        norms_ref[0:1] = jnp.sum(upstream * normed_two, axis=0, keepdims=True)
        norms_ref[1:2] = jnp.sum(upstream, axis=0, keepdims=True)
        dz = norm_back(upstream, normed_two, scale_two, gains_ref[2:3])
        dzb = dz.astype(jnp.bfloat16)
        dab = (4.0 * dz).astype(jnp.bfloat16)
        dab_ref[...] = dab
        dunder = (under_slope * dot_back(dab, w_up.value())).astype(jnp.bfloat16)
        dunder_ref[...] = dunder
        dmixed = dz + dot_back(dunder, w_down.value())
        for piece in range(pieces):
            dpre = (slopes[piece] * dot_back(dzb, w_ff[piece].value())).astype(jnp.bfloat16)
            dmixed = dmixed + dot_back(dpre, w_in[piece].value())
        norms_ref[2:3] = jnp.sum(dmixed * normed_one, axis=0, keepdims=True)
        norms_ref[3:4] = jnp.sum(dmixed, axis=0, keepdims=True)
        dresid = norm_back(dmixed, normed_one, scale_one, gains_ref[1:2])
        dresid_ref[...] = dresid
        dcb = dresid.astype(jnp.bfloat16)
        dcb_ref[...] = dcb
        write_blocks(
            blocks_ref, dot_back(dcb, w_out.value()).astype(jnp.bfloat16), lanes, 0, width
        )

    rows = normed_in.shape[0]
    low = jnp.bfloat16

    def body_rows(ins, loaded, refs, scratch):
        whole_ff = loaded[2 + pieces]

        class Rows:
            def __init__(self, piece):
                self.piece = piece

            def value(self):
                return whole_ff.value()[self.piece * step : (self.piece + 1) * step]

        loaded = loaded[: 2 + pieces] + [[Rows(piece) for piece in range(pieces)], loaded[-1]]
        body(ins, loaded, refs, scratch)

    return call_with_parts(
        body_rows,
        [got, normed_in, cotangent, gains, biases],
        [out_part] + in_parts + [down, outs, up],
        [
            shape(rows, WIDTH, of=low),
            shape(rows, WIDTH, of=low),
            shape(rows, WIDTH, of=low),
            shape(rows, down.width, of=low),
            shape(rows, down.width, of=low),
            shape(rows, WIDTH, of=low),
            shape(rows, WIDTH, of=low),
            shape(rows, WIDTH),
            shape(*got.shape, of=low),
            shape(4, WIDTH),
        ],
        "feed_forward",
        [pltpu.VMEM((pieces, rows, step), jnp.float32)],
        20,
    )


def before_self(got, dresid, normed, scale, gains, query_part, out_part, lanes, width):
    def body(ins, loaded, outs, _):
        got_ref, dresid_ref, normed_ref, scale_ref, gains_ref = ins
        dcq_ref, dr_ref, dsb_ref, blocks_ref, norms_ref = outs
        dcq = read_blocks(got_ref, lanes, 0, width)
        dcq_ref[...] = dcq
        dhidden = dresid_ref[...] + dot_back(dcq, loaded[0].value())
        normed = normed_ref[...]
        norms_ref[0:1] = jnp.sum(dhidden * normed, axis=0, keepdims=True)
        norms_ref[1:2] = jnp.sum(dhidden, axis=0, keepdims=True)
        dr = norm_back(dhidden, normed, scale_ref[...], gains_ref[0:1])
        dr_ref[...] = dr
        dsb = dr.astype(jnp.bfloat16)
        dsb_ref[...] = dsb
        grad = dot_back(dsb, loaded[1].value()).astype(jnp.bfloat16)
        write_blocks(blocks_ref, grad, lanes, 0, width)

    rows = dresid.shape[0]
    return call_with_parts(
        body,
        [got, dresid, normed, scale, gains],
        [query_part, out_part],
        [
            shape(rows, WIDTH, of=jnp.bfloat16),
            shape(rows, WIDTH),
            shape(rows, WIDTH, of=jnp.bfloat16),
            shape(*got.shape, of=jnp.bfloat16),
            shape(2, WIDTH),
        ],
        "before_self",
    )


def input_grad(got, start, parts, lanes, span, width, name):
    stacked = got.shape[2] == width

    def body(ins, loaded, outs, _):
        total = None
        for kind, weight in enumerate(loaded):
            if stacked:
                values = read_blocks(
                    ins[0].at[:, kind * span : (kind + 1) * span], lanes, 0, width
                )
            else:
                values = read_blocks(ins[0], lanes, kind, width)
            term = dot_back(values, weight.value())
            total = term if total is None else total + term
        outs[0][...] = total if len(ins) == 1 else total + ins[1][...]

    rows = span * lanes
    return call_with_parts(
        body,
        [got] if start is None else [got, start],
        parts,
        [shape(rows, WIDTH)],
        name,
    )


def sum_everywhere(values, stages):
    if not paired():
        return lax.psum(values, ("dp", "blk"))
    values = after(values, stages[0])
    values = values + swap_core(values)
    for step, bit in enumerate((1, 2, 4, 8)):
        if step + 1 < len(stages):
            values = after(values, stages[step + 1])
        values = values + flip(values, bit)
    return values


def shards(
    tokens,
    encoder,
    cotangent,
    self_in,
    self_out,
    cross_q,
    cross_kv,
    cross_out,
    ffn_in,
    ffn_out,
    adapt_down,
    adapt_up,
    norm_gain,
    norm_bias,
    tgt_lengths,
    src_lengths,
):
    lanes, span, _ = tokens.shape
    rows = lanes * span
    width = WIDTH * lanes // lax.axis_size("blk")
    own_row = lax.axis_index("blk") // (lax.axis_size("blk") // lanes)
    tgt_ends = jnp.cumsum(lax.dynamic_index_in_dim(tgt_lengths, own_row, 0, keepdims=False))
    src_ends = jnp.cumsum(lax.dynamic_index_in_dim(src_lengths, own_row, 0, keepdims=False))
    flat_tokens = tokens.reshape(rows, WIDTH)
    flat_encoder = encoder.reshape(rows, WIDTH)
    frozen = [ffn_in, adapt_down, ffn_out, adapt_up, cross_out]
    inward = [self_in, cross_kv]

    if paired():
        token_row, stages = gather_row(tokens)
        self_heads, pair_heads = head_columns(inward, [3, 2])
        packed = gather_packed(after(frozen, stages[1]))
        out_shard, query_shard, encoder_block = after((self_out, cross_q, encoder), stages[1])
        out_source, query_source = gather_flips([out_shard, query_shard], "xy", stages[3])
        encoder_row, encoder_stages = gather_row(encoder_block, out_source.arrays[1])
        self_qkv = project_row(token_row, self_heads, "self_in")
        self_qkv = after(
            self_qkv, encoder_stages[1], out_source.stages[0], query_source.stages[0]
        )
        pair_own = project_row(encoder_row, pair_heads, "cross_kv")
    else:
        (self_source, pair_source, out_source, query_source) = gather_flips(
            [self_in, cross_kv, self_out, cross_q], "xyxy"
        )
        self_parts = [columns_of((self_source, WIDTH * kind, WIDTH)) for kind in range(3)]
        pair_parts = [columns_of((pair_source, WIDTH * kind, WIDTH)) for kind in range(2)]
        self_qkv = as_rows(
            exchange(project_blocks(flat_tokens, self_parts, lanes, width, "self_in"))
        )
        pair_own = as_rows(
            exchange(project_blocks(flat_encoder, pair_parts, lanes, width, "cross_kv"))
        )
    self_out_part = columns_of((out_source, 0, WIDTH))
    query_part = columns_of((query_source, 0, WIDTH))

    self_mid, self_full, self_lse = attn_forward(
        tgt_ends, tgt_ends, self_qkv, self_qkv, width, True
    )
    self_low, normed, scale, hidden_low, query_blocks = after_self(
        exchange(as_blocks(after(self_mid, out_source.stages[1], query_source.stages[1]))),
        flat_tokens,
        norm_gain,
        norm_bias,
        self_out_part,
        query_part,
        lanes,
        width,
    )
    cross_own = as_rows(exchange(query_blocks))
    ready = after(packed, cross_own) if paired() else None
    ff_parts, down_parts, ffo_parts, up_parts, (cross_out_part,) = packed_parts(frozen, ready)
    cross_mid, cross_full, cross_lse = attn_forward(
        tgt_ends, src_ends, cross_own, pair_own, width, False
    )
    (
        output,
        cross_low,
        mixed_low,
        adapter_low,
        grad_under,
        adapt_low,
        cross_branch_low,
        grad_resid_two,
        cross_grad_blocks,
        norms_high,
    ) = feed_forward(
        exchange(as_blocks(cross_mid)),
        normed,
        cotangent.reshape(rows, WIDTH),
        norm_gain,
        norm_bias,
        cross_out_part,
        ff_parts,
        down_parts[0],
        ffo_parts[0],
        up_parts[0],
        lanes,
        width,
    )
    if paired():
        inward_packed = gather_packed(after(inward, cross_mid))
    high_pairs = [(cross_low, cross_branch_low), (mixed_low, grad_under), (adapter_low, adapt_low)]
    high_terms = grad_terms(high_pairs)
    (high_grads,), high_stages = reduce_terms([high_pairs], [high_terms], [(2, 1, 4, 8)])
    grad_cross_out, grad_adapt_down, grad_adapt_up = high_grads
    cross_dq, cross_dkv = attn_backward(
        tgt_ends,
        src_ends,
        cross_own,
        pair_own,
        as_rows(after(exchange(cross_grad_blocks), high_stages[0])),
        cross_full,
        cross_lse,
        False,
    )
    cq_low, grad_resid_one, self_branch_low, self_grad_blocks, norms_low = before_self(
        after(exchange(as_blocks(cross_dq)), high_stages[1]),
        grad_resid_two,
        normed,
        scale,
        norm_gain,
        query_part,
        self_out_part,
        lanes,
        width,
    )
    mid_pairs = [(hidden_low, cq_low), (self_low, self_branch_low)]
    (mid_grads,), mid_stages = reduce_terms([mid_pairs], [grad_terms(mid_pairs)], [(1, 2, 4, 8)])
    grad_cross_q, grad_self_out = mid_grads
    (self_grads,) = attn_backward(
        tgt_ends,
        tgt_ends,
        self_qkv,
        self_qkv,
        as_rows(after(exchange(self_grad_blocks), high_stages[2])),
        self_full,
        self_lse,
        True,
        joined=True,
    )
    pair_got = exchange(as_blocks(cross_dkv))
    self_got = as_blocks(self_grads)
    if paired():
        self_parts, pair_parts = packed_parts(inward, after(inward_packed, self_grad_blocks))
        sent = [self_got, row_grad(token_row, self_grads, "self_in_grad")]
        sent.append(row_grad(encoder_row, cross_dkv, "cross_kv_grad"))
        sent = [
            array[:, :, kind * width : (kind + 1) * width]
            for array in sent
            for kind in range(array.shape[2] // width)
        ]
        self_got = exchange(jnp.concatenate(sent, axis=1))
        ends = [3 * span + 32 * kind for kind in range(6)]
        chunks = [self_got[:, first : first + 32] for first in ends[:5]]
        grad_self_in = finish_row_grad(jnp.concatenate(chunks[:3], axis=2), 3)
        grad_cross_kv = finish_row_grad(jnp.concatenate(chunks[3:], axis=2), 2)
    else:
        self_got = exchange(self_got)
        pair_low = pair_got.reshape(lanes, -1, span, 2, width).transpose(0, 2, 3, 1, 4)
        self_back = self_got.reshape(lanes, -1, span, 3, width).transpose(0, 2, 3, 1, 4)
        grad_cross_kv = weight_grad(flat_encoder, pair_low.reshape(rows, 2 * WIDTH))
        grad_self_in = weight_grad(flat_tokens, self_back.reshape(rows, 3 * WIDTH))
    (encoder_grad,) = input_grad(pair_got, None, pair_parts, lanes, span, width, "encoder_grad")
    (tokens_grad,) = input_grad(
        after(self_got, encoder_grad),
        grad_resid_one,
        self_parts,
        lanes,
        span,
        width,
        "tokens_grad",
    )
    norms = sum_everywhere(jnp.concatenate([norms_low, norms_high], axis=0), mid_stages)
    return (
        output.reshape(lanes, span, WIDTH),
        tokens_grad.reshape(lanes, span, WIDTH),
        encoder_grad.reshape(lanes, span, WIDTH),
        grad_self_in,
        grad_self_out,
        grad_cross_q,
        grad_cross_kv,
        grad_cross_out,
        grad_adapt_down,
        grad_adapt_up,
        jnp.stack([norms[0], norms[4], norms[2]]),
        jnp.stack([norms[1], norms[5], norms[3]]),
    )


def solution(mesh):
    placed = (
        P("dp", "blk", None),
        P("dp", "blk", None),
        P("dp", "blk", None),
        P("blk", None),
        P("blk", None),
        P("blk", None),
        P("blk", None),
        P("blk", None),
        P("blk", None),
        P("blk", None),
        P("blk", None),
        P("blk", None),
        P(),
        P(),
        P("dp", None),
        P("dp", None),
    )
    return jax.shard_map(
        shards,
        mesh=mesh,
        in_specs=placed,
        out_specs=(
            P("dp", "blk", None),
            P("dp", "blk", None),
            P("dp", "blk", None),
            P("blk", None),
            P("blk", None),
            P("blk", None),
            P("blk", None),
            P("blk", None),
            P("blk", None),
            P("blk", None),
            P(),
            P(),
        ),
        check_vma=False,
    )
```

```python
import functools
import math

import jax
import jax.numpy as jnp
from jax import lax
from jax.experimental import pallas as pl
from jax.experimental.pallas import tpu as pltpu
from jax.sharding import PartitionSpec as P

HEADS = 16
HEAD_DIM = 64
WIDTH = HEADS * HEAD_DIM


NEG = -1e30
VMEM_BYTES = 56 * 1024 * 1024


def cost(microseconds):
    return pl.CostEstimate(
        flops=int(microseconds * 0.4e9),
        bytes_accessed=int(microseconds * 1.2e6),
        transcendentals=0,
    )


def paired():
    return lax.axis_size("blk") == 16 and lax.axis_size("dp") == 2


def swap_core(block):
    cores = lax.axis_size("dp")
    return lax.ppermute(block, "dp", [(i ^ 1, i) for i in range(cores)])


def flip(block, bit):
    chips = lax.axis_size("blk")
    return lax.ppermute(block, "blk", [(i ^ bit, i) for i in range(chips)])


FLIPS = (8, 4, 2, 1)


def with_flip(block, bit):
    return jnp.stack([block, flip(block, bit)])


def own_half(values, which):
    half = values.shape[1] // 2
    return lax.dynamic_slice_in_dim(values, which * half, half, 1)


def scatter_chips(terms, orders, hold, held_stage):
    own = lax.axis_index("blk")

    def fold(blocks, left, bit):
        axis, place = left.index(bit), (own // bit) % 2
        kept = lax.dynamic_index_in_dim(blocks, place, axis, keepdims=False)
        sent = lax.dynamic_index_in_dim(blocks, 1 - place, axis, keepdims=False)
        got = flip(sent, bit)
        return (kept.astype(jnp.float32) + got.astype(jnp.float32)).astype(jnp.bfloat16)

    terms = [blocks.reshape(2, 2, 2, 2, *blocks.shape[1:]) for blocks in terms]
    stages = [terms[0]]
    for stage in range(4):
        if hold is not None and stage == held_stage:
            terms = after(terms, hold)
        terms = [
            fold(blocks, [bit for bit in FLIPS if bit not in order[:stage]], order[stage])
            for blocks, order in zip(terms, orders)
        ]
        stages.append(terms[0])
    return terms, stages


CHUNK = 256


def grad_terms(pairs):
    if not paired():
        return None
    core = lax.axis_index("dp")
    packed = []
    for inputs, upstream in pairs:
        both = jnp.concatenate([inputs, swap_core(inputs)], axis=0)
        half = jnp.concatenate(
            [own_half(upstream, core), swap_core(own_half(upstream, 1 - core))], axis=0
        )
        term = lax.dot_general(
            both, half, (((0,), (0,)), ((), ())), preferred_element_type=jnp.float32
        ).astype(jnp.bfloat16)
        rows = term.shape[0] // 16
        chunks = term.shape[1] // CHUNK
        packed += [
            term[:, c * CHUNK : (c + 1) * CHUNK].reshape(16, rows, CHUNK) for c in range(chunks)
        ]
    return jnp.concatenate(packed, axis=1)


def reduce_terms(groups, terms, orders, hold=None, held_stage=0):
    if not paired():
        found = [[weight_grad(inputs, upstream) for inputs, upstream in pairs] for pairs in groups]
        return found, [groups[0][0][1]] * 5
    core = lax.axis_index("dp")
    totals, stages = scatter_chips(terms, orders, hold, held_stage)
    mine = jnp.concatenate(totals, axis=0)
    other = swap_core(mine)
    low = jnp.where(core == 0, mine, other).astype(jnp.float32)
    high = jnp.where(core == 0, other, mine).astype(jnp.float32)
    found, place = [], 0
    for pairs in groups:
        found.append([])
        for inputs, upstream in pairs:
            rows = inputs.shape[1] // 16
            chunks = upstream.shape[1] // 2 // CHUNK
            spots = [slice(place + c * rows, place + (c + 1) * rows) for c in range(chunks)]
            found[-1].append(
                jnp.concatenate(
                    [low[spot] for spot in spots] + [high[spot] for spot in spots], axis=1
                )
            )
            place += rows * chunks
    return found, stages


def weight_grad(inputs, upstream):
    scattered = lax.psum_scatter(
        lax.dot_general(
            inputs, upstream, (((0,), (0,)), ((), ())), preferred_element_type=jnp.float32
        ).astype(jnp.bfloat16),
        "blk",
        scatter_dimension=0,
        tiled=True,
    )
    return lax.psum(scattered, "dp").astype(jnp.float32)


class Source:
    def __init__(self, kind, arrays, first_flip="x", column=None):
        self.kind, self.arrays, self.first_flip = kind, arrays, first_flip
        self.stages = arrays[:1] * 3 if column is None else [column] + arrays[:2]


class Part:
    def __init__(self, rows, width, spots):
        self.rows, self.width, self.spots = rows, width, spots

    def scratch(self):
        return pltpu.VMEM((2, 2, 2, 2, 2, self.rows // 32, self.width), jnp.bfloat16)

    def start(self, refs_of, place, dst, sem):
        z1, z0, y, x, core = [place[axis] for axis in range(5)]
        high = self.rows // 32
        for source, first_row, first_col, at_col, width in self.spots:
            refs = refs_of(source)
            cols = slice(first_col, first_col + width)
            into = slice(at_col, at_col + width)
            if source.kind == "whole":
                pltpu.make_async_copy(
                    refs[0].at[:, :, :, :, :, :, cols], dst.at[:, :, :, :, :, :, into], sem
                ).start()
            elif source.kind == "cores":
                for which in range(2):
                    owner = core if which == 0 else 1 - core
                    pltpu.make_async_copy(
                        refs[which].at[:, :, :, :, first_row : first_row + high, cols],
                        dst.at[:, :, :, :, owner, :, into],
                        sem,
                    ).start()
            else:
                for which in range(4):
                    owner = core if which < 2 else 1 - core
                    for near, at_y, at_x in flipped(source.first_flip, which % 2, y, x):
                        for up, at_z1, at_z0 in four(z1, z0):
                            pltpu.make_async_copy(
                                refs[which].at[near, up[0], up[1], :, cols],
                                dst.at[at_z1, at_z0, at_y, at_x, owner, :, into],
                                sem,
                            ).start()


def four(z1, z0):
    return [
        ((low, high), z1 if high == 0 else 1 - z1, z0 if low == 0 else 1 - z0)
        for low in range(2)
        for high in range(2)
    ]


def flipped(first_flip, beyond, y, x):
    found = []
    for near in range(2):
        a, b = (near, beyond) if first_flip == "x" else (beyond, near)
        found.append((near, y if b == 0 else 1 - y, x if a == 0 else 1 - x))
    return found


def after(value, *others):
    return lax.optimization_barrier((value, *others))[0]


def gather_flips(shards, first_flips, hold=None):
    if not paired():
        full = [lax.all_gather(shard, "blk", axis=0, tiled=True) for shard in shards]
        return [
            Source("whole", [array.reshape(2, 2, 2, 2, 2, array.shape[0] // 32, array.shape[1])])
            for array in full
        ]
    core = lax.axis_index("dp")
    columns = []
    for shard in shards:
        rows = shard.shape[0]
        own = lax.dynamic_slice_in_dim(shard, core * (rows // 2), rows // 2, 0)
        columns.append(with_flip(with_flip(own, 8), 4))
    sources, bits = [], {"x": (1, 2), "y": (2, 1)}
    if hold is not None:
        columns = after(columns, hold)
    planes = [
        with_flip(column, bits[first][0]) for column, first in zip(columns, first_flips)
    ]
    for column, plane, first in zip(columns, planes, first_flips):
        beyond = flip(plane, bits[first][1])
        sources.append(
            Source("flips", [plane, beyond, swap_core(plane), swap_core(beyond)], first, column)
        )
    return sources


class RowPart:
    def __init__(self, sources, span):
        self.span = span
        self.rows, self.width = 16 * span, WIDTH
        self.spots = [(source,) for source in sources]

    def scratch(self):
        return pltpu.VMEM((2, 2, 2, 2, self.span, WIDTH), jnp.bfloat16)

    def start(self, refs_of, place, dst, sem):
        z1, z0, y, x = [place[axis] for axis in range(4)]
        half = WIDTH // 2
        for side, (source,) in enumerate(self.spots):
            refs = refs_of(source)
            for beyond in range(2):
                for near, at_y, at_x in flipped(source.first_flip, beyond, y, x):
                    for up, at_z1, at_z0 in four(z1, z0):
                        pltpu.make_async_copy(
                            refs[beyond].at[near, up[0], up[1]],
                            dst.at[at_z1, at_z0, at_y, at_x, :, side * half : (side + 1) * half],
                            sem,
                        ).start()


def gather_row(block, hold=None):
    row = lax.axis_index("blk") // 8
    own = lax.dynamic_index_in_dim(block, row, 0, keepdims=False)
    other = lax.dynamic_index_in_dim(block, 1 - row, 0, keepdims=False)
    pair = jnp.stack([own, flip(other, 8)])
    column = with_flip(pair, 4)
    stages, sources = [pair, column], []
    if hold is not None:
        column = after(column, hold)
    half = WIDTH // 2
    planes = [with_flip(column[..., :half], 1), with_flip(column[..., half:], 2)]
    for plane, first, bit in zip(planes, "xy", (2, 1)):
        sources.append(Source("row", [plane, flip(plane, bit)], first))
    stages += [planes, [source.arrays[1] for source in sources]]
    return RowPart(sources, block.shape[1]), stages


def head_columns(shards, kinds):
    core = lax.axis_index("dp")
    blocks, widths = [], [128 * kind for kind in kinds]
    for shard, kind in zip(shards, kinds):
        own = lax.dynamic_slice_in_dim(shard, core * 32, 32, 0)
        own = own.reshape(32, kind, 8, 128).transpose(2, 0, 1, 3)
        blocks.append(own.reshape(8, 32, kind * 128))
    blocks = jnp.concatenate(blocks, axis=2)
    mine = exchange(jnp.concatenate([blocks, blocks], axis=0))
    mine = mine.reshape(2, 2, 2, 2, 32, sum(widths))
    source = Source("cores", [mine, swap_core(mine)])
    parts, place = [], 0
    for width in widths:
        parts.append(Part(1024, width, [(source, 0, place, 0, width)]))
        place += width
    return parts


def project_row(row_part, head_part, name):
    def body(ins, loaded, outs, _):
        weight = loaded[1].value()
        inputs = loaded[0].value()
        for first in range(0, row_part.rows, 256):
            rows = slice(first, first + 256)
            outs[0][rows, :] = dot(inputs[rows], weight).astype(jnp.bfloat16)

    (found,) = call_with_parts(
        body,
        [],
        [row_part, head_part],
        [shape(row_part.rows, head_part.width, of=jnp.bfloat16)],
        name,
    )
    return found


def row_grad(row_part, upstream, name):
    columns = upstream.shape[1]

    def body(ins, loaded, outs, _):
        core = ins[1][0]
        inputs = loaded[0].value()
        grads = []
        for first in range(0, columns, 128):
            grads.append(pair_dot(ins[0][:, first : first + 128], inputs, 0, 0).T)
        grad = jnp.concatenate(grads, axis=1).astype(jnp.bfloat16).reshape(16, 2, 32, columns)
        outs[0][core] = grad[:, 0]
        outs[0][1 - core] = grad[:, 1]

    (terms,) = call_with_parts(
        body,
        [upstream],
        [row_part],
        [shape(2, 16, 32, columns, of=jnp.bfloat16)],
        name,
        scalars=[lax.axis_index("dp").reshape(1).astype(jnp.int32)],
    )
    got = swap_core(terms[1])
    return (terms[0].astype(jnp.float32) + got.astype(jnp.float32)).astype(jnp.bfloat16)


def finish_row_grad(got, kinds):
    total = jnp.sum(got.reshape(2, 8, 32, kinds, 128).astype(jnp.float32), axis=0)
    mine = total.astype(jnp.bfloat16).transpose(1, 2, 0, 3).reshape(32, kinds * WIDTH)
    other = swap_core(mine)
    core = lax.axis_index("dp")
    low = jnp.where(core == 0, mine, other)
    high = jnp.where(core == 0, other, mine)
    return jnp.concatenate([low, high], axis=0).astype(jnp.float32)


def columns_of(*pieces):
    spots, place = [], 0
    for source, first, width in pieces:
        spots.append((source, 0, first, place, width))
        place += width
    return Part(1024, place, spots)


PACK = 512


def pack_halves(shards):
    places = [
        (index, shard.shape[0] // 2, first)
        for index, shard in enumerate(shards)
        for first in range(0, shard.shape[1], PACK)
    ]

    def body(core, *refs):
        out_ref, place = refs[-1], 0
        for index, high, first in places:
            start = pl.multiple_of(core[0] * high, 16)
            out_ref[place : place + high, :] = refs[index][pl.ds(start, high), first : first + PACK]
            place += high

    return pl.pallas_call(
        body,
        out_shape=shape(sum(high for _, high, _ in places), PACK, of=jnp.bfloat16),
        in_specs=[smem_spec()] + [vmem_spec()] * len(shards),
        out_specs=vmem_spec(),
        compiler_params=pltpu.CompilerParams(vmem_limit_bytes=VMEM_BYTES),
        cost_estimate=cost(2),
        name="pack_halves",
    )(lax.axis_index("dp").reshape(1).astype(jnp.int32), *shards)


def gather_packed(packed):
    return lax.all_gather(packed, "blk", axis=0)


def packed_parts(shards, mine):
    if not paired():
        found = []
        for source, shard in zip(gather_flips(shards, "x" * len(shards)), shards):
            rows, columns = 32 * source.arrays[0].shape[5], shard.shape[1]
            step = min(columns, 1024)
            found.append(
                [
                    Part(rows, step, [(source, 0, first, 0, step)])
                    for first in range(0, columns, step)
                ]
            )
        return found
    spots, place = [], 0
    for shard in shards:
        high = shard.shape[0] // 2
        places = []
        for first in range(0, shard.shape[1], PACK):
            places.append(place)
            place += high
        spots.append((shard.shape[0] * 16, places))
    mine = mine.reshape(2, 2, 2, 2, place, PACK)
    source = Source("cores", [mine, swap_core(mine)])
    found = []
    for rows, places in spots:
        parts = []
        for first in range(0, len(places), 2):
            two = places[first : first + 2]
            parts.append(
                Part(
                    rows,
                    PACK * len(two),
                    [(source, row, 0, PACK * side, PACK) for side, row in enumerate(two)],
                )
            )
        found.append(parts)
    return found


def place_now():
    own, core = lax.axis_index("blk"), lax.axis_index("dp")
    bits = [(own // bit) % 2 for bit in FLIPS]
    return jnp.stack(bits + [core]).astype(jnp.int32)


class Loaded:
    def __init__(self, part, dst, sem):
        self.part, self.dst, self.sem, self.here = part, dst, sem, False

    def value(self):
        if not self.here:
            pltpu.make_async_copy(self.dst, self.dst, self.sem).wait()
            self.here = True
        return self.dst[...].reshape(self.part.rows, self.part.width)


def call_with_parts(body, inputs, parts, outputs, name, scratch=(), takes=5, scalars=()):
    sources = []
    for part in parts:
        sources += [spot[0] for spot in part.spots if spot[0] not in sources]
    arrays = [array for source in sources for array in source.arrays]

    def kernel(place, *refs):
        refs = list(refs)
        ins = [refs.pop(0) for _ in (*inputs, *scalars)]
        pieces = [[refs.pop(0) for _ in source.arrays] for source in sources]
        outs = [refs.pop(0) for _ in outputs]
        dsts = [refs.pop(0) for _ in parts]
        sems = refs.pop(0)
        loaded = []
        for index, part in enumerate(parts):
            part.start(
                lambda source: pieces[sources.index(source)], place, dsts[index], sems.at[index]
            )
            loaded.append(Loaded(part, dsts[index], sems.at[index]))
        body(ins, loaded, outs, refs)

    return pl.pallas_call(
        kernel,
        out_shape=tuple(outputs),
        in_specs=[smem_spec()]
        + [vmem_spec()] * len(inputs)
        + [smem_spec()] * len(scalars)
        + [pl.BlockSpec(memory_space=pl.ANY)] * len(arrays),
        out_specs=(vmem_spec(),) * len(outputs),
        scratch_shapes=[part.scratch() for part in parts]
        + [pltpu.SemaphoreType.DMA((len(parts),))]
        + list(scratch),
        compiler_params=pltpu.CompilerParams(vmem_limit_bytes=VMEM_BYTES),
        cost_estimate=cost(takes),
        name=name,
    )(place_now(), *inputs, *scalars, *arrays)


def vmem_spec():
    return pl.BlockSpec(memory_space=pltpu.VMEM)


def smem_spec():
    return pl.BlockSpec(memory_space=pltpu.SMEM)


def seg_of_pos(ends_ref, pos):
    seg = jnp.zeros(pos.shape, jnp.int32)
    for slot in range(ends_ref.shape[0]):
        seg = seg + (ends_ref[slot] <= pos).astype(jnp.int32)
    return seg


def pair_dot(left, right, left_dim, right_dim):
    return lax.dot_general(
        left, right, (((left_dim,), (right_dim,)), ((), ())), preferred_element_type=jnp.float32
    )


def seg_tables(q_ends, k_ends, span):
    seg_q = seg_of_pos(q_ends, lax.broadcasted_iota(jnp.int32, (1, span), 1))
    seg_k = seg_of_pos(k_ends, lax.broadcasted_iota(jnp.int32, (span, 1), 0))
    return seg_q, seg_k


def masked_scores(keys, queries, seg_q, seg_k, first, causal):
    scores = pair_dot(keys, queries, 1, 1)
    allowed = seg_k == seg_q
    if causal:
        key_pos = lax.broadcasted_iota(jnp.int32, scores.shape, 0)
        query_pos = first + lax.broadcasted_iota(jnp.int32, scores.shape, 1)
        allowed = allowed & (key_pos <= query_pos)
    return jnp.where(allowed, scores, NEG)


def attn_forward_body(causal, width, q_ends, k_ends, q_ref, kv_ref, low_ref, full_ref, lse_ref):
    span = q_ref.shape[0]
    step = math.gcd(span, 256)
    heads = width // HEAD_DIM
    seg_q, seg_k = seg_tables(q_ends, k_ends, span)
    key_at = kv_ref.shape[1] - 2 * width
    scaled = q_ref[:, :width] * jnp.bfloat16(HEAD_DIM ** (-0.5))
    keys = kv_ref[:, key_at : key_at + width]
    values = kv_ref[:, key_at + width : key_at + 2 * width]
    for first in range(0, span, step):
        reach = first + step if causal else span
        parts = []
        for head in range(heads):
            cols = slice(head * HEAD_DIM, (head + 1) * HEAD_DIM)
            scores = masked_scores(
                keys[:reach, cols],
                scaled[first : first + step, cols],
                seg_q[:, first : first + step],
                seg_k[:reach],
                first,
                causal,
            )
            top = jnp.max(scores, axis=0, keepdims=True)
            probs = jnp.exp(scores - top)
            total = jnp.sum(probs, axis=0, keepdims=True)
            mixed = pair_dot(values[:reach, cols], probs.astype(jnp.bfloat16), 0, 0)
            parts.append(mixed / total)
            lse_ref[head : head + 1, first : first + step] = top + jnp.log(total)
        joined = jnp.concatenate(parts, axis=0).T
        full_ref[first : first + step, :] = joined
        low_ref[first : first + step, :] = joined.astype(jnp.bfloat16)


def attn_forward(q_ends, k_ends, queries, keys_values, width, causal):
    span = queries.shape[0]
    return pl.pallas_call(
        functools.partial(attn_forward_body, causal, width),
        out_shape=(
            jax.ShapeDtypeStruct((span, width), jnp.bfloat16),
            jax.ShapeDtypeStruct((span, width), jnp.float32),
            jax.ShapeDtypeStruct((width // HEAD_DIM, span), jnp.float32),
        ),
        in_specs=[smem_spec(), smem_spec()] + [vmem_spec()] * 2,
        out_specs=(vmem_spec(),) * 3,
        compiler_params=pltpu.CompilerParams(vmem_limit_bytes=VMEM_BYTES),
        cost_estimate=cost(8),
        name="attn_forward",
    )(q_ends, k_ends, queries, keys_values)


def attn_backward_body(
    causal,
    width,
    q_ends,
    k_ends,
    q_ref,
    kv_ref,
    up_ref,
    full_ref,
    lse_ref,
    *outs,
):
    dq_ref, dkv_ref = outs[0], outs[-3]
    dk_sum, dv_sum = outs[-2:]
    span = q_ref.shape[0]
    step = math.gcd(span, 256)
    heads = width // HEAD_DIM
    seg_q, seg_k = seg_tables(q_ends, k_ends, span)
    key_at = kv_ref.shape[1] - 2 * width
    scaled = q_ref[:, :width] * jnp.bfloat16(HEAD_DIM ** (-0.5))
    keys = kv_ref[:, key_at : key_at + width]
    values = kv_ref[:, key_at + width : key_at + 2 * width]
    upstream = up_ref[...]
    dk_sum[...] = jnp.zeros_like(dk_sum)
    dv_sum[...] = jnp.zeros_like(dv_sum)
    for first in range(0, span, step):
        reach = first + step if causal else span
        rows = slice(first, first + step)
        product = (upstream[rows].astype(jnp.float32) * full_ref[rows, :]).T
        parts = []
        for head in range(heads):
            cols = slice(head * HEAD_DIM, (head + 1) * HEAD_DIM)
            delta = jnp.sum(product[cols], axis=0, keepdims=True)
            scores = masked_scores(
                keys[:reach, cols], scaled[rows, cols], seg_q[:, rows], seg_k[:reach], first, causal
            )
            probs = jnp.exp(scores - lse_ref[head : head + 1, rows])
            dv_sum[head, :reach] += pair_dot(
                probs.astype(jnp.bfloat16), upstream[rows, cols], 1, 0
            )
            grad_probs = pair_dot(values[:reach, cols], upstream[rows, cols], 1, 1)
            grad_scores = (probs * (grad_probs - delta)).astype(jnp.bfloat16)
            dk_sum[head, :reach] += pair_dot(grad_scores, scaled[rows, cols], 1, 0)
            parts.append(pair_dot(keys[:reach, cols], grad_scores, 0, 0))
        joined = jnp.concatenate(parts, axis=0).T * HEAD_DIM ** (-0.5)
        dq_ref[rows, :width] = joined.astype(jnp.bfloat16)
    sums = [dk_sum[head] for head in range(heads)] + [dv_sum[head] for head in range(heads)]
    kv_at = dkv_ref.shape[1] - 2 * width
    dkv_ref[:, kv_at:] = jnp.concatenate(sums, axis=1).astype(jnp.bfloat16)


def attn_backward(
    q_ends, k_ends, queries, keys_values, upstream, full, lse, causal, joined=False
):
    span, width = upstream.shape
    kinds = [3] if joined else [1, 2]
    heads = width // HEAD_DIM
    return pl.pallas_call(
        functools.partial(attn_backward_body, causal, width),
        out_shape=[jax.ShapeDtypeStruct((span, kind * width), jnp.bfloat16) for kind in kinds],
        in_specs=[smem_spec(), smem_spec()] + [vmem_spec()] * 5,
        out_specs=[vmem_spec()] * len(kinds),
        scratch_shapes=[pltpu.VMEM((heads, span, HEAD_DIM), jnp.float32)] * 2,
        compiler_params=pltpu.CompilerParams(vmem_limit_bytes=VMEM_BYTES),
        cost_estimate=cost(8),
        name="attn_backward",
    )(q_ends, k_ends, queries, keys_values, upstream, full, lse)


def exchange(blocks):
    return lax.all_to_all(blocks, "blk", 0, 0, tiled=True)


def as_rows(blocks):
    return blocks.reshape(blocks.shape[0] * blocks.shape[1], blocks.shape[2])


def as_blocks(rows):
    devices = lax.axis_size("blk")
    return rows.reshape(devices, rows.shape[0] // devices, rows.shape[1])


def write_blocks(out_ref, values, lanes, kind, width):
    span = values.shape[0] // lanes
    for group in range(WIDTH // width):
        for lane in range(lanes):
            out_ref[lane * (WIDTH // width) + group, :, kind * width : (kind + 1) * width] = values[
                lane * span : (lane + 1) * span, group * width : (group + 1) * width
            ]


def read_blocks(got_ref, lanes, kind, width):
    groups = got_ref.shape[0] // lanes
    cols = slice(kind * width, (kind + 1) * width)
    rows = [
        jnp.concatenate([got_ref[lane * groups + group, :, cols] for group in range(groups)], axis=1)
        for lane in range(lanes)
    ]
    return jnp.concatenate(rows, axis=0)


def dot(left, right):
    return pair_dot(left, right, 1, 0)


def dot_back(left, right):
    return pair_dot(left, right, 1, 1)


def shape(*sizes, of=jnp.float32):
    return jax.ShapeDtypeStruct(sizes, of)


def normalize(values):
    center = values - jnp.mean(values, -1, keepdims=True)
    scale = lax.rsqrt(jnp.mean(center * center, -1, keepdims=True) + 1e-05)
    return center * scale, scale


def norm_back(upstream, normed, scale, gains_row):
    grad = upstream * gains_row
    return scale * (
        grad
        - jnp.mean(grad, -1, keepdims=True)
        - normed * jnp.mean(grad * normed, -1, keepdims=True)
    )


def project_blocks(inputs, parts, lanes, width, name):
    def body(ins, loaded, outs, _):
        for kind, weight in enumerate(loaded):
            write_blocks(
                outs[0], dot(ins[0][...], weight.value()).astype(jnp.bfloat16), lanes, kind, width
            )

    devices, span = lax.axis_size("blk"), inputs.shape[0] // lanes
    (blocks,) = call_with_parts(
        body,
        [inputs],
        parts,
        [shape(devices, span, width * len(parts), of=jnp.bfloat16)],
        name,
    )
    return blocks


def after_self(got, tokens, gains, biases, out_part, query_part, lanes, width):
    def body(ins, loaded, outs, _):
        got_ref, tokens_ref, gains_ref, biases_ref = ins
        low_ref, normed_ref, scale_ref, hidden_ref, blocks_ref = outs
        attended = read_blocks(got_ref, lanes, 0, width)
        low_ref[...] = attended
        resid = tokens_ref[...].astype(jnp.float32) + dot(attended, loaded[0].value())
        normed, scale = normalize(resid)
        normed_ref[...] = normed
        scale_ref[...] = scale
        hidden = (normed * gains_ref[0:1] + biases_ref[0:1]).astype(jnp.bfloat16)
        hidden_ref[...] = hidden
        query = dot(hidden, loaded[1].value()).astype(jnp.bfloat16)
        write_blocks(blocks_ref, query, lanes, 0, width)

    rows = tokens.shape[0]
    return call_with_parts(
        body,
        [got, tokens, gains, biases],
        [out_part, query_part],
        [
            shape(rows, WIDTH, of=jnp.bfloat16),
            shape(rows, WIDTH),
            shape(rows, 1),
            shape(rows, WIDTH, of=jnp.bfloat16),
            shape(*got.shape, of=jnp.bfloat16),
        ],
        "after_self",
    )


def feed_forward(got, normed_in, cotangent, gains, biases, out_part, in_parts, down, outs, up, lanes, width):
    pieces = len(in_parts)
    step = in_parts[0].width

    def body(ins, loaded, refs, scratch):
        got_ref, normed_in_ref, cot_ref, gains_ref, biases_ref = ins
        (
            output_ref,
            low_ref,
            mixed_ref,
            adapted_ref,
            dunder_ref,
            dab_ref,
            dcb_ref,
            dresid_ref,
            blocks_ref,
            norms_ref,
        ) = refs
        (slopes,) = scratch
        w_out, w_in = loaded[0], loaded[1 : 1 + pieces]
        w_down, w_ff, w_up = loaded[1 + pieces :]
        attended = read_blocks(got_ref, lanes, 0, width)
        low_ref[...] = attended
        hidden = normed_in_ref[...] * gains_ref[0:1] + biases_ref[0:1]
        normed_one, scale_one = normalize(hidden + dot(attended, w_out.value()))
        mixed = normed_one * gains_ref[1:2] + biases_ref[1:2]
        mixed_low = mixed.astype(jnp.bfloat16)
        mixed_ref[...] = mixed_low
        summed = mixed
        under = dot(mixed_low, w_down.value())
        gate = 1.0 / (1.0 + jnp.exp(-under))
        adapted = (under * gate).astype(jnp.bfloat16)
        adapted_ref[...] = adapted
        under_slope = gate * (1.0 + under * (1.0 - gate))
        summed = summed + 4.0 * dot(adapted, w_up.value())
        for piece in range(pieces):
            before = dot(mixed_low, w_in[piece].value())
            below = 0.5 + 0.5 * lax.erf(before * (0.5**0.5))
            slopes[piece] = below + before * jnp.exp(-0.5 * before * before) * (
                (2.0 * math.pi) ** -0.5
            )
            act = (before * below).astype(jnp.bfloat16)
            summed = summed + dot(act, w_ff[piece].value())
        normed_two, scale_two = normalize(summed)
        output_ref[...] = (normed_two * gains_ref[2:3] + biases_ref[2:3]).astype(jnp.bfloat16)
        upstream = cot_ref[...].astype(jnp.float32)
        norms_ref[0:1] = jnp.sum(upstream * normed_two, axis=0, keepdims=True)
        norms_ref[1:2] = jnp.sum(upstream, axis=0, keepdims=True)
        dz = norm_back(upstream, normed_two, scale_two, gains_ref[2:3])
        dzb = dz.astype(jnp.bfloat16)
        dab = (4.0 * dz).astype(jnp.bfloat16)
        dab_ref[...] = dab
        dunder = (under_slope * dot_back(dab, w_up.value())).astype(jnp.bfloat16)
        dunder_ref[...] = dunder
        dmixed = dz + dot_back(dunder, w_down.value())
        for piece in range(pieces):
            dpre = (slopes[piece] * dot_back(dzb, w_ff[piece].value())).astype(jnp.bfloat16)
            dmixed = dmixed + dot_back(dpre, w_in[piece].value())
        norms_ref[2:3] = jnp.sum(dmixed * normed_one, axis=0, keepdims=True)
        norms_ref[3:4] = jnp.sum(dmixed, axis=0, keepdims=True)
        dresid = norm_back(dmixed, normed_one, scale_one, gains_ref[1:2])
        dresid_ref[...] = dresid
        dcb = dresid.astype(jnp.bfloat16)
        dcb_ref[...] = dcb
        write_blocks(
            blocks_ref, dot_back(dcb, w_out.value()).astype(jnp.bfloat16), lanes, 0, width
        )

    rows = normed_in.shape[0]
    low = jnp.bfloat16

    def body_rows(ins, loaded, refs, scratch):
        whole_ff = loaded[2 + pieces]

        class Rows:
            def __init__(self, piece):
                self.piece = piece

            def value(self):
                return whole_ff.value()[self.piece * step : (self.piece + 1) * step]

        loaded = loaded[: 2 + pieces] + [[Rows(piece) for piece in range(pieces)], loaded[-1]]
        body(ins, loaded, refs, scratch)

    return call_with_parts(
        body_rows,
        [got, normed_in, cotangent, gains, biases],
        [out_part] + in_parts + [down, outs, up],
        [
            shape(rows, WIDTH, of=low),
            shape(rows, WIDTH, of=low),
            shape(rows, WIDTH, of=low),
            shape(rows, down.width, of=low),
            shape(rows, down.width, of=low),
            shape(rows, WIDTH, of=low),
            shape(rows, WIDTH, of=low),
            shape(rows, WIDTH),
            shape(*got.shape, of=low),
            shape(4, WIDTH),
        ],
        "feed_forward",
        [pltpu.VMEM((pieces, rows, step), jnp.float32)],
        20,
    )


def before_self(got, dresid, normed, scale, gains, query_part, out_part, lanes, width):
    def body(ins, loaded, outs, _):
        got_ref, dresid_ref, normed_ref, scale_ref, gains_ref = ins
        dcq_ref, dr_ref, dsb_ref, blocks_ref, norms_ref = outs
        dcq = read_blocks(got_ref, lanes, 0, width)
        dcq_ref[...] = dcq
        dhidden = dresid_ref[...] + dot_back(dcq, loaded[0].value())
        normed = normed_ref[...]
        norms_ref[0:1] = jnp.sum(dhidden * normed, axis=0, keepdims=True)
        norms_ref[1:2] = jnp.sum(dhidden, axis=0, keepdims=True)
        dr = norm_back(dhidden, normed, scale_ref[...], gains_ref[0:1])
        dr_ref[...] = dr
        dsb = dr.astype(jnp.bfloat16)
        dsb_ref[...] = dsb
        grad = dot_back(dsb, loaded[1].value()).astype(jnp.bfloat16)
        write_blocks(blocks_ref, grad, lanes, 0, width)

    rows = dresid.shape[0]
    return call_with_parts(
        body,
        [got, dresid, normed, scale, gains],
        [query_part, out_part],
        [
            shape(rows, WIDTH, of=jnp.bfloat16),
            shape(rows, WIDTH),
            shape(rows, WIDTH, of=jnp.bfloat16),
            shape(*got.shape, of=jnp.bfloat16),
            shape(2, WIDTH),
        ],
        "before_self",
    )


def input_grad(got, start, parts, lanes, span, width, name):
    def body(ins, loaded, outs, _):
        total = None
        for kind, weight in enumerate(loaded):
            values = read_blocks(ins[0], lanes, kind, width)
            term = dot_back(values, weight.value())
            total = term if total is None else total + term
        outs[0][...] = total if len(ins) == 1 else total + ins[1][...]

    rows = span * lanes
    return call_with_parts(
        body,
        [got] if start is None else [got, start],
        parts,
        [shape(rows, WIDTH)],
        name,
    )


def sum_everywhere(values, stages):
    if not paired():
        return lax.psum(values, ("dp", "blk"))
    values = after(values, stages[0])
    values = values + swap_core(values)
    for step, bit in enumerate((1, 2, 4, 8)):
        if step + 1 < len(stages):
            values = after(values, stages[step + 1])
        values = values + flip(values, bit)
    return values


def shards(
    tokens,
    encoder,
    cotangent,
    self_in,
    self_out,
    cross_q,
    cross_kv,
    cross_out,
    ffn_in,
    ffn_out,
    adapt_down,
    adapt_up,
    norm_gain,
    norm_bias,
    tgt_lengths,
    src_lengths,
):
    lanes, span, _ = tokens.shape
    rows = lanes * span
    width = WIDTH * lanes // lax.axis_size("blk")
    own_row = lax.axis_index("blk") // (lax.axis_size("blk") // lanes)
    tgt_ends = jnp.cumsum(lax.dynamic_index_in_dim(tgt_lengths, own_row, 0, keepdims=False))
    src_ends = jnp.cumsum(lax.dynamic_index_in_dim(src_lengths, own_row, 0, keepdims=False))
    flat_tokens = tokens.reshape(rows, WIDTH)
    flat_encoder = encoder.reshape(rows, WIDTH)
    frozen = [ffn_in, adapt_down, ffn_out, adapt_up, cross_out]
    inward = [self_in, cross_kv]

    if paired():
        packed = gather_packed(pack_halves(frozen))
        inward_packed = pack_halves(inward)
        token_row, stages = gather_row(tokens)
        self_heads, pair_heads = head_columns(inward, [3, 2])
        out_shard, query_shard = after((self_out, cross_q), stages[1])
        out_source, query_source = gather_flips([out_shard, query_shard], "xy", stages[3])
        self_qkv = project_row(token_row, self_heads, "self_in")
        encoder_row, encoder_stages = gather_row(after(encoder, self_qkv), out_source.arrays[1])
        self_qkv = after(self_qkv, out_source.stages[0], query_source.stages[0])
        pair_own = project_row(encoder_row, pair_heads, "cross_kv")
    else:
        (self_source, pair_source, out_source, query_source) = gather_flips(
            [self_in, cross_kv, self_out, cross_q], "xyxy"
        )
        self_parts = [columns_of((self_source, WIDTH * kind, WIDTH)) for kind in range(3)]
        pair_parts = [columns_of((pair_source, WIDTH * kind, WIDTH)) for kind in range(2)]
        self_qkv = as_rows(
            exchange(project_blocks(flat_tokens, self_parts, lanes, width, "self_in"))
        )
        pair_own = as_rows(
            exchange(project_blocks(flat_encoder, pair_parts, lanes, width, "cross_kv"))
        )
    self_out_part = columns_of((out_source, 0, WIDTH))
    query_part = columns_of((query_source, 0, WIDTH))

    self_mid, self_full, self_lse = attn_forward(
        tgt_ends, tgt_ends, self_qkv, self_qkv, width, True
    )
    self_sent = after(self_mid, out_source.stages[1], query_source.stages[1])
    if paired():
        self_sent = after(self_sent, encoder_stages[0])
    self_back = exchange(as_blocks(self_sent))
    if paired():
        self_back = after(self_back, encoder_stages[1])
    self_low, normed, scale, hidden_low, query_blocks = after_self(
        self_back,
        flat_tokens,
        norm_gain,
        norm_bias,
        self_out_part,
        query_part,
        lanes,
        width,
    )
    cross_own = as_rows(exchange(query_blocks))
    cross_mid, cross_full, cross_lse = attn_forward(
        tgt_ends, src_ends, cross_own, pair_own, width, False
    )
    cross_back = exchange(as_blocks(cross_mid))
    ready = after(packed, cross_mid) if paired() else None
    ff_parts, down_parts, ffo_parts, up_parts, (cross_out_part,) = packed_parts(frozen, ready)
    if paired():
        inward_packed = gather_packed(after(inward_packed, cross_back))
    (
        output,
        cross_low,
        mixed_low,
        adapter_low,
        grad_under,
        adapt_low,
        cross_branch_low,
        grad_resid_two,
        cross_grad_blocks,
        norms_high,
    ) = feed_forward(
        cross_back,
        normed,
        cotangent.reshape(rows, WIDTH),
        norm_gain,
        norm_bias,
        cross_out_part,
        ff_parts,
        down_parts[0],
        ffo_parts[0],
        up_parts[0],
        lanes,
        width,
    )
    high_groups = [
        [(cross_low, cross_branch_low)],
        [(mixed_low, grad_under), (adapter_low, adapt_low)],
    ]
    (high_grads, adapt_grads), high_stages = reduce_terms(
        high_groups, [grad_terms(pairs) for pairs in high_groups], [(2, 1, 4, 8), (1, 2, 4, 8)]
    )
    (grad_cross_out,), (grad_adapt_down, grad_adapt_up) = high_grads, adapt_grads
    cross_dq, cross_dkv = attn_backward(
        tgt_ends,
        src_ends,
        cross_own,
        pair_own,
        as_rows(after(exchange(cross_grad_blocks), high_stages[0])),
        cross_full,
        cross_lse,
        False,
    )
    cq_low, grad_resid_one, self_branch_low, self_grad_blocks, norms_low = before_self(
        after(exchange(as_blocks(cross_dq)), high_stages[1]),
        grad_resid_two,
        normed,
        scale,
        norm_gain,
        query_part,
        self_out_part,
        lanes,
        width,
    )
    mid_groups = [[(hidden_low, cq_low)], [(self_low, self_branch_low)]]
    ((grad_cross_q,), (grad_self_out,)), mid_stages = reduce_terms(
        mid_groups, [grad_terms(pairs) for pairs in mid_groups], [(2, 1, 4, 8), (1, 2, 4, 8)]
    )
    (self_grads,) = attn_backward(
        tgt_ends,
        tgt_ends,
        self_qkv,
        self_qkv,
        as_rows(after(exchange(self_grad_blocks), high_stages[2])),
        self_full,
        self_lse,
        True,
        joined=True,
    )
    pair_got = exchange(as_blocks(cross_dkv))
    self_got = as_blocks(self_grads)
    if paired():
        self_parts, pair_parts = packed_parts(inward, after(inward_packed, self_grad_blocks))
        self_got = exchange(after(self_got, pair_got, mid_stages[1]))
        dkv_late = after(cross_dkv, self_grad_blocks)
        sent = [
            row_grad(token_row, self_grads, "self_in_grad"),
            row_grad(encoder_row, dkv_late, "cross_kv_grad"),
        ]
        grads_got = exchange(after(jnp.concatenate(sent, axis=2), self_got, mid_stages[2]))
        grad_self_in = finish_row_grad(grads_got[:, :, : 3 * width], 3)
        grad_cross_kv = finish_row_grad(grads_got[:, :, 3 * width :], 2)
    else:
        self_got = exchange(self_got)
        pair_low = pair_got.reshape(lanes, -1, span, 2, width).transpose(0, 2, 3, 1, 4)
        self_back = self_got.reshape(lanes, -1, span, 3, width).transpose(0, 2, 3, 1, 4)
        grad_cross_kv = weight_grad(flat_encoder, pair_low.reshape(rows, 2 * WIDTH))
        grad_self_in = weight_grad(flat_tokens, self_back.reshape(rows, 3 * WIDTH))
    (encoder_grad,) = input_grad(pair_got, None, pair_parts, lanes, span, width, "encoder_grad")
    (tokens_grad,) = input_grad(
        after(self_got, encoder_grad),
        grad_resid_one,
        self_parts,
        lanes,
        span,
        width,
        "tokens_grad",
    )
    norms = sum_everywhere(jnp.concatenate([norms_low, norms_high], axis=0), mid_stages)
    return (
        output.reshape(lanes, span, WIDTH),
        tokens_grad.reshape(lanes, span, WIDTH),
        encoder_grad.reshape(lanes, span, WIDTH),
        grad_self_in,
        grad_self_out,
        grad_cross_q,
        grad_cross_kv,
        grad_cross_out,
        grad_adapt_down,
        grad_adapt_up,
        jnp.stack([norms[0], norms[4], norms[2]]),
        jnp.stack([norms[1], norms[5], norms[3]]),
    )


def solution(mesh):
    placed = (
        P("dp", "blk", None),
        P("dp", "blk", None),
        P("dp", "blk", None),
        P("blk", None),
        P("blk", None),
        P("blk", None),
        P("blk", None),
        P("blk", None),
        P("blk", None),
        P("blk", None),
        P("blk", None),
        P("blk", None),
        P(),
        P(),
        P("dp", None),
        P("dp", None),
    )
    return jax.shard_map(
        shards,
        mesh=mesh,
        in_specs=placed,
        out_specs=(
            P("dp", "blk", None),
            P("dp", "blk", None),
            P("dp", "blk", None),
            P("blk", None),
            P("blk", None),
            P("blk", None),
            P("blk", None),
            P("blk", None),
            P("blk", None),
            P("blk", None),
            P(),
            P(),
        ),
        check_vma=False,
    )
```

```python
import functools
import math

import jax
import jax.numpy as jnp
from jax import lax
from jax.experimental import pallas as pl
from jax.experimental.pallas import tpu as pltpu
from jax.sharding import PartitionSpec as P

HEADS = 16
HEAD_DIM = 64
WIDTH = HEADS * HEAD_DIM


NEG = -1e30
VMEM_BYTES = 56 * 1024 * 1024


def cost(microseconds):
    return pl.CostEstimate(
        flops=int(microseconds * 0.4e9),
        bytes_accessed=int(microseconds * 1.2e6),
        transcendentals=0,
    )


def paired():
    return lax.axis_size("blk") == 16 and lax.axis_size("dp") == 2


def swap_core(block):
    cores = lax.axis_size("dp")
    return lax.ppermute(block, "dp", [(i ^ 1, i) for i in range(cores)])


def flip(block, bit):
    chips = lax.axis_size("blk")
    return lax.ppermute(block, "blk", [(i ^ bit, i) for i in range(chips)])


FLIPS = (8, 4, 2, 1)


def with_flip(block, bit):
    return jnp.stack([block, flip(block, bit)])


def own_half(values, which):
    half = values.shape[1] // 2
    return lax.dynamic_slice_in_dim(values, which * half, half, 1)


def scatter_chips(terms, orders, first, last):
    if not paired():
        return terms, [terms] * 5
    own = lax.axis_index("blk")

    def fold(blocks, left, bit):
        axis, place = left.index(bit), (own // bit) % 2
        kept = lax.dynamic_index_in_dim(blocks, place, axis, keepdims=False)
        sent = lax.dynamic_index_in_dim(blocks, 1 - place, axis, keepdims=False)
        got = flip(sent, bit)
        return (kept.astype(jnp.float32) + got.astype(jnp.float32)).astype(jnp.bfloat16)

    if first == 0:
        terms = [blocks.reshape(2, 2, 2, 2, *blocks.shape[1:]) for blocks in terms]
    stages = [terms[0]]
    for stage in range(first, last):
        terms = [
            fold(blocks, [bit for bit in FLIPS if bit not in order[:stage]], order[stage])
            for blocks, order in zip(terms, orders)
        ]
        stages.append(terms[0])
    return terms, stages


CHUNK = 256


def grad_terms(pairs):
    if not paired():
        return pairs[0][1]
    core = lax.axis_index("dp")
    packed = []
    for inputs, upstream in pairs:
        both = jnp.concatenate([inputs, swap_core(inputs)], axis=0)
        half = jnp.concatenate(
            [own_half(upstream, core), swap_core(own_half(upstream, 1 - core))], axis=0
        )
        term = lax.dot_general(
            both, half, (((0,), (0,)), ((), ())), preferred_element_type=jnp.float32
        ).astype(jnp.bfloat16)
        rows = term.shape[0] // 16
        chunks = term.shape[1] // CHUNK
        packed += [
            term[:, c * CHUNK : (c + 1) * CHUNK].reshape(16, rows, CHUNK) for c in range(chunks)
        ]
    return jnp.concatenate(packed, axis=1)


def finish_terms(groups, terms):
    if not paired():
        return [[weight_grad(inputs, upstream) for inputs, upstream in pairs] for pairs in groups]
    core = lax.axis_index("dp")
    mine = jnp.concatenate(terms, axis=0)
    other = swap_core(mine)
    low = jnp.where(core == 0, mine, other).astype(jnp.float32)
    high = jnp.where(core == 0, other, mine).astype(jnp.float32)
    found, place = [], 0
    for pairs in groups:
        found.append([])
        for inputs, upstream in pairs:
            rows = inputs.shape[1] // 16
            chunks = upstream.shape[1] // 2 // CHUNK
            spots = [slice(place + c * rows, place + (c + 1) * rows) for c in range(chunks)]
            found[-1].append(
                jnp.concatenate(
                    [low[spot] for spot in spots] + [high[spot] for spot in spots], axis=1
                )
            )
            place += rows * chunks
    return found


def weight_grad(inputs, upstream):
    scattered = lax.psum_scatter(
        lax.dot_general(
            inputs, upstream, (((0,), (0,)), ((), ())), preferred_element_type=jnp.float32
        ).astype(jnp.bfloat16),
        "blk",
        scatter_dimension=0,
        tiled=True,
    )
    return lax.psum(scattered, "dp").astype(jnp.float32)


class Source:
    def __init__(self, kind, arrays, first_flip="x", column=None):
        self.kind, self.arrays, self.first_flip = kind, arrays, first_flip
        self.stages = arrays[:1] * 3 if column is None else [column] + arrays[:2]


class Part:
    def __init__(self, rows, width, spots):
        self.rows, self.width, self.spots = rows, width, spots

    def scratch(self):
        return pltpu.VMEM((2, 2, 2, 2, 2, self.rows // 32, self.width), jnp.bfloat16)

    def start(self, refs_of, place, dst, sem):
        z1, z0, y, x, core = [place[axis] for axis in range(5)]
        high = self.rows // 32
        for source, first_row, first_col, at_col, width in self.spots:
            refs = refs_of(source)
            cols = slice(first_col, first_col + width)
            into = slice(at_col, at_col + width)
            if source.kind == "whole":
                pltpu.make_async_copy(
                    refs[0].at[:, :, :, :, :, :, cols], dst.at[:, :, :, :, :, :, into], sem
                ).start()
            elif source.kind == "cores":
                for which in range(2):
                    owner = core if which == 0 else 1 - core
                    pltpu.make_async_copy(
                        refs[which].at[:, :, :, :, first_row : first_row + high, cols],
                        dst.at[:, :, :, :, owner, :, into],
                        sem,
                    ).start()
            else:
                for which in range(4):
                    owner = core if which < 2 else 1 - core
                    for near, at_y, at_x in flipped(source.first_flip, which % 2, y, x):
                        for up, at_z1, at_z0 in four(z1, z0):
                            pltpu.make_async_copy(
                                refs[which].at[near, up[0], up[1], :, cols],
                                dst.at[at_z1, at_z0, at_y, at_x, owner, :, into],
                                sem,
                            ).start()


def four(z1, z0):
    return [
        ((low, high), z1 if high == 0 else 1 - z1, z0 if low == 0 else 1 - z0)
        for low in range(2)
        for high in range(2)
    ]


def flipped(first_flip, beyond, y, x):
    found = []
    for near in range(2):
        a, b = (near, beyond) if first_flip == "x" else (beyond, near)
        found.append((near, y if b == 0 else 1 - y, x if a == 0 else 1 - x))
    return found


def after(value, *others):
    return lax.optimization_barrier((value, *others))[0]


def gather_flips(shards, first_flips, hold=None):
    if not paired():
        full = [lax.all_gather(shard, "blk", axis=0, tiled=True) for shard in shards]
        return [
            Source("whole", [array.reshape(2, 2, 2, 2, 2, array.shape[0] // 32, array.shape[1])])
            for array in full
        ]
    core = lax.axis_index("dp")
    columns = []
    for shard in shards:
        rows = shard.shape[0]
        own = lax.dynamic_slice_in_dim(shard, core * (rows // 2), rows // 2, 0)
        columns.append(with_flip(with_flip(own, 8), 4))
    sources, bits = [], {"x": (1, 2), "y": (2, 1)}
    if hold is not None:
        columns = after(columns, hold)
    planes = [
        with_flip(column, bits[first][0]) for column, first in zip(columns, first_flips)
    ]
    for column, plane, first in zip(columns, planes, first_flips):
        beyond = flip(plane, bits[first][1])
        sources.append(
            Source("flips", [plane, beyond, swap_core(plane), swap_core(beyond)], first, column)
        )
    return sources


class RowPart:
    def __init__(self, sources, span):
        self.span = span
        self.rows, self.width = 16 * span, WIDTH
        self.spots = [(source,) for source in sources]

    def scratch(self):
        return pltpu.VMEM((2, 2, 2, 2, self.span, WIDTH), jnp.bfloat16)

    def start(self, refs_of, place, dst, sem):
        z1, z0, y, x = [place[axis] for axis in range(4)]
        half = WIDTH // 2
        for side, (source,) in enumerate(self.spots):
            refs = refs_of(source)
            for beyond in range(2):
                for near, at_y, at_x in flipped(source.first_flip, beyond, y, x):
                    for up, at_z1, at_z0 in four(z1, z0):
                        pltpu.make_async_copy(
                            refs[beyond].at[near, up[0], up[1]],
                            dst.at[at_z1, at_z0, at_y, at_x, :, side * half : (side + 1) * half],
                            sem,
                        ).start()


def gather_row(block, hold_near=None, hold=None):
    row = lax.axis_index("blk") // 8
    own = lax.dynamic_index_in_dim(block, row, 0, keepdims=False)
    other = lax.dynamic_index_in_dim(block, 1 - row, 0, keepdims=False)
    pair = jnp.stack([own, flip(other, 8)])
    if hold_near is not None:
        pair = after(pair, hold_near)
    column = with_flip(pair, 4)
    stages, sources = [pair, column], []
    if hold is not None:
        column = after(column, hold)
    half = WIDTH // 2
    planes = [with_flip(column[..., :half], 1), with_flip(column[..., half:], 2)]
    for plane, first, bit in zip(planes, "xy", (2, 1)):
        sources.append(Source("row", [plane, flip(plane, bit)], first))
    stages += [planes, [source.arrays[1] for source in sources]]
    return RowPart(sources, block.shape[1]), stages


def head_columns(shards, kinds):
    core = lax.axis_index("dp")
    blocks, widths = [], [128 * kind for kind in kinds]
    for shard, kind in zip(shards, kinds):
        own = lax.dynamic_slice_in_dim(shard, core * 32, 32, 0)
        own = own.reshape(32, kind, 8, 128).transpose(2, 0, 1, 3)
        blocks.append(own.reshape(8, 32, kind * 128))
    blocks = jnp.concatenate(blocks, axis=2)
    mine = exchange(jnp.concatenate([blocks, blocks], axis=0))
    mine = mine.reshape(2, 2, 2, 2, 32, sum(widths))
    source = Source("cores", [mine, swap_core(mine)])
    parts, place = [], 0
    for width in widths:
        parts.append(Part(1024, width, [(source, 0, place, 0, width)]))
        place += width
    return parts


def project_row(row_part, head_part, name):
    def body(ins, loaded, outs, _):
        weight = loaded[1].value()
        inputs = loaded[0].value()
        for first in range(0, row_part.rows, 256):
            rows = slice(first, first + 256)
            outs[0][rows, :] = dot(inputs[rows], weight).astype(jnp.bfloat16)

    (found,) = call_with_parts(
        body,
        [],
        [row_part, head_part],
        [shape(row_part.rows, head_part.width, of=jnp.bfloat16)],
        name,
    )
    return found


def row_grad(row_part, upstream, name):
    columns = upstream.shape[1]

    def body(ins, loaded, outs, _):
        core = ins[1][0]
        inputs = loaded[0].value()
        grads = []
        for first in range(0, columns, 128):
            grads.append(pair_dot(ins[0][:, first : first + 128], inputs, 0, 0).T)
        grad = jnp.concatenate(grads, axis=1).astype(jnp.bfloat16).reshape(16, 2, 32, columns)
        outs[0][core] = grad[:, 0]
        outs[0][1 - core] = grad[:, 1]

    (terms,) = call_with_parts(
        body,
        [upstream],
        [row_part],
        [shape(2, 16, 32, columns, of=jnp.bfloat16)],
        name,
        scalars=[lax.axis_index("dp").reshape(1).astype(jnp.int32)],
    )
    got = swap_core(terms[1])
    return (terms[0].astype(jnp.float32) + got.astype(jnp.float32)).astype(jnp.bfloat16)


def finish_row_grad(got, kinds):
    total = jnp.sum(got.reshape(2, 8, 32, kinds, 128).astype(jnp.float32), axis=0)
    mine = total.astype(jnp.bfloat16).transpose(1, 2, 0, 3).reshape(32, kinds * WIDTH)
    other = swap_core(mine)
    core = lax.axis_index("dp")
    low = jnp.where(core == 0, mine, other)
    high = jnp.where(core == 0, other, mine)
    return jnp.concatenate([low, high], axis=0).astype(jnp.float32)


def columns_of(*pieces):
    spots, place = [], 0
    for source, first, width in pieces:
        spots.append((source, 0, first, place, width))
        place += width
    return Part(1024, place, spots)


PACK = 512


def pack_halves(shards):
    places = [
        (index, shard.shape[0] // 2, first)
        for index, shard in enumerate(shards)
        for first in range(0, shard.shape[1], PACK)
    ]

    def body(core, *refs):
        out_ref, place = refs[-1], 0
        for index, high, first in places:
            start = pl.multiple_of(core[0] * high, 16)
            out_ref[place : place + high, :] = refs[index][pl.ds(start, high), first : first + PACK]
            place += high

    return pl.pallas_call(
        body,
        out_shape=shape(sum(high for _, high, _ in places), PACK, of=jnp.bfloat16),
        in_specs=[smem_spec()] + [vmem_spec()] * len(shards),
        out_specs=vmem_spec(),
        compiler_params=pltpu.CompilerParams(vmem_limit_bytes=VMEM_BYTES),
        cost_estimate=cost(2),
        name="pack_halves",
    )(lax.axis_index("dp").reshape(1).astype(jnp.int32), *shards)


def gather_packed(packed):
    return lax.all_gather(packed, "blk", axis=0)


def packed_parts(shards, mine):
    if not paired():
        found = []
        for source, shard in zip(gather_flips(shards, "x" * len(shards)), shards):
            rows, columns = 32 * source.arrays[0].shape[5], shard.shape[1]
            step = min(columns, 1024)
            found.append(
                [
                    Part(rows, step, [(source, 0, first, 0, step)])
                    for first in range(0, columns, step)
                ]
            )
        return found
    spots, place = [], 0
    for shard in shards:
        high = shard.shape[0] // 2
        places = []
        for first in range(0, shard.shape[1], PACK):
            places.append(place)
            place += high
        spots.append((shard.shape[0] * 16, places))
    mine = mine.reshape(2, 2, 2, 2, place, PACK)
    source = Source("cores", [mine, swap_core(mine)])
    found = []
    for rows, places in spots:
        parts = []
        for first in range(0, len(places), 2):
            two = places[first : first + 2]
            parts.append(
                Part(
                    rows,
                    PACK * len(two),
                    [(source, row, 0, PACK * side, PACK) for side, row in enumerate(two)],
                )
            )
        found.append(parts)
    return found


def place_now():
    own, core = lax.axis_index("blk"), lax.axis_index("dp")
    bits = [(own // bit) % 2 for bit in FLIPS]
    return jnp.stack(bits + [core]).astype(jnp.int32)


class Loaded:
    def __init__(self, part, dst, sem):
        self.part, self.dst, self.sem, self.here = part, dst, sem, False

    def value(self):
        if not self.here:
            pltpu.make_async_copy(self.dst, self.dst, self.sem).wait()
            self.here = True
        return self.dst[...].reshape(self.part.rows, self.part.width)


def call_with_parts(body, inputs, parts, outputs, name, scratch=(), takes=5, scalars=()):
    sources = []
    for part in parts:
        sources += [spot[0] for spot in part.spots if spot[0] not in sources]
    arrays = [array for source in sources for array in source.arrays]

    def kernel(place, *refs):
        refs = list(refs)
        ins = [refs.pop(0) for _ in (*inputs, *scalars)]
        pieces = [[refs.pop(0) for _ in source.arrays] for source in sources]
        outs = [refs.pop(0) for _ in outputs]
        dsts = [refs.pop(0) for _ in parts]
        sems = refs.pop(0)
        loaded = []
        for index, part in enumerate(parts):
            part.start(
                lambda source: pieces[sources.index(source)], place, dsts[index], sems.at[index]
            )
            loaded.append(Loaded(part, dsts[index], sems.at[index]))
        body(ins, loaded, outs, refs)

    return pl.pallas_call(
        kernel,
        out_shape=tuple(outputs),
        in_specs=[smem_spec()]
        + [vmem_spec()] * len(inputs)
        + [smem_spec()] * len(scalars)
        + [pl.BlockSpec(memory_space=pl.ANY)] * len(arrays),
        out_specs=(vmem_spec(),) * len(outputs),
        scratch_shapes=[part.scratch() for part in parts]
        + [pltpu.SemaphoreType.DMA((len(parts),))]
        + list(scratch),
        compiler_params=pltpu.CompilerParams(vmem_limit_bytes=VMEM_BYTES),
        cost_estimate=cost(takes),
        name=name,
    )(place_now(), *inputs, *scalars, *arrays)


def vmem_spec():
    return pl.BlockSpec(memory_space=pltpu.VMEM)


def smem_spec():
    return pl.BlockSpec(memory_space=pltpu.SMEM)


def seg_of_pos(ends_ref, pos):
    seg = jnp.zeros(pos.shape, jnp.int32)
    for slot in range(ends_ref.shape[0]):
        seg = seg + (ends_ref[slot] <= pos).astype(jnp.int32)
    return seg


def pair_dot(left, right, left_dim, right_dim):
    return lax.dot_general(
        left, right, (((left_dim,), (right_dim,)), ((), ())), preferred_element_type=jnp.float32
    )


def seg_tables(q_ends, k_ends, span):
    seg_q = seg_of_pos(q_ends, lax.broadcasted_iota(jnp.int32, (1, span), 1))
    seg_k = seg_of_pos(k_ends, lax.broadcasted_iota(jnp.int32, (span, 1), 0))
    return seg_q, seg_k


def masked_scores(keys, queries, seg_q, seg_k, first, causal):
    scores = pair_dot(keys, queries, 1, 1)
    allowed = seg_k == seg_q
    if causal:
        key_pos = lax.broadcasted_iota(jnp.int32, scores.shape, 0)
        query_pos = first + lax.broadcasted_iota(jnp.int32, scores.shape, 1)
        allowed = allowed & (key_pos <= query_pos)
    return jnp.where(allowed, scores, NEG)


def attn_forward_body(causal, width, q_ends, k_ends, q_ref, kv_ref, low_ref, full_ref, lse_ref):
    span = q_ref.shape[0]
    step = math.gcd(span, 256)
    heads = width // HEAD_DIM
    seg_q, seg_k = seg_tables(q_ends, k_ends, span)
    key_at = kv_ref.shape[1] - 2 * width
    scaled = q_ref[:, :width] * jnp.bfloat16(HEAD_DIM ** (-0.5))
    keys = kv_ref[:, key_at : key_at + width]
    values = kv_ref[:, key_at + width : key_at + 2 * width]
    for first in range(0, span, step):
        reach = first + step if causal else span
        parts = []
        for head in range(heads):
            cols = slice(head * HEAD_DIM, (head + 1) * HEAD_DIM)
            scores = masked_scores(
                keys[:reach, cols],
                scaled[first : first + step, cols],
                seg_q[:, first : first + step],
                seg_k[:reach],
                first,
                causal,
            )
            top = jnp.max(scores, axis=0, keepdims=True)
            probs = jnp.exp(scores - top)
            total = jnp.sum(probs, axis=0, keepdims=True)
            mixed = pair_dot(values[:reach, cols], probs.astype(jnp.bfloat16), 0, 0)
            parts.append(mixed / total)
            lse_ref[head : head + 1, first : first + step] = top + jnp.log(total)
        joined = jnp.concatenate(parts, axis=0).T
        full_ref[first : first + step, :] = joined
        low_ref[first : first + step, :] = joined.astype(jnp.bfloat16)


def attn_forward(q_ends, k_ends, queries, keys_values, width, causal):
    span = queries.shape[0]
    return pl.pallas_call(
        functools.partial(attn_forward_body, causal, width),
        out_shape=(
            jax.ShapeDtypeStruct((span, width), jnp.bfloat16),
            jax.ShapeDtypeStruct((span, width), jnp.float32),
            jax.ShapeDtypeStruct((width // HEAD_DIM, span), jnp.float32),
        ),
        in_specs=[smem_spec(), smem_spec()] + [vmem_spec()] * 2,
        out_specs=(vmem_spec(),) * 3,
        compiler_params=pltpu.CompilerParams(vmem_limit_bytes=VMEM_BYTES),
        cost_estimate=cost(8),
        name="attn_forward",
    )(q_ends, k_ends, queries, keys_values)


def attn_backward_body(
    causal,
    width,
    q_ends,
    k_ends,
    q_ref,
    kv_ref,
    up_ref,
    full_ref,
    lse_ref,
    *outs,
):
    dq_ref, dkv_ref = outs[0], outs[-3]
    dk_sum, dv_sum = outs[-2:]
    span = q_ref.shape[0]
    step = math.gcd(span, 256)
    heads = width // HEAD_DIM
    seg_q, seg_k = seg_tables(q_ends, k_ends, span)
    key_at = kv_ref.shape[1] - 2 * width
    scaled = q_ref[:, :width] * jnp.bfloat16(HEAD_DIM ** (-0.5))
    keys = kv_ref[:, key_at : key_at + width]
    values = kv_ref[:, key_at + width : key_at + 2 * width]
    upstream = up_ref[...]
    dk_sum[...] = jnp.zeros_like(dk_sum)
    dv_sum[...] = jnp.zeros_like(dv_sum)
    for first in range(0, span, step):
        reach = first + step if causal else span
        rows = slice(first, first + step)
        product = (upstream[rows].astype(jnp.float32) * full_ref[rows, :]).T
        parts = []
        for head in range(heads):
            cols = slice(head * HEAD_DIM, (head + 1) * HEAD_DIM)
            delta = jnp.sum(product[cols], axis=0, keepdims=True)
            scores = masked_scores(
                keys[:reach, cols], scaled[rows, cols], seg_q[:, rows], seg_k[:reach], first, causal
            )
            probs = jnp.exp(scores - lse_ref[head : head + 1, rows])
            dv_sum[head, :reach] += pair_dot(
                probs.astype(jnp.bfloat16), upstream[rows, cols], 1, 0
            )
            grad_probs = pair_dot(values[:reach, cols], upstream[rows, cols], 1, 1)
            grad_scores = (probs * (grad_probs - delta)).astype(jnp.bfloat16)
            dk_sum[head, :reach] += pair_dot(grad_scores, scaled[rows, cols], 1, 0)
            parts.append(pair_dot(keys[:reach, cols], grad_scores, 0, 0))
        joined = jnp.concatenate(parts, axis=0).T * HEAD_DIM ** (-0.5)
        dq_ref[rows, :width] = joined.astype(jnp.bfloat16)
    sums = [dk_sum[head] for head in range(heads)] + [dv_sum[head] for head in range(heads)]
    kv_at = dkv_ref.shape[1] - 2 * width
    dkv_ref[:, kv_at:] = jnp.concatenate(sums, axis=1).astype(jnp.bfloat16)


def attn_backward(
    q_ends, k_ends, queries, keys_values, upstream, full, lse, causal, joined=False
):
    span, width = upstream.shape
    kinds = [3] if joined else [1, 2]
    heads = width // HEAD_DIM
    return pl.pallas_call(
        functools.partial(attn_backward_body, causal, width),
        out_shape=[jax.ShapeDtypeStruct((span, kind * width), jnp.bfloat16) for kind in kinds],
        in_specs=[smem_spec(), smem_spec()] + [vmem_spec()] * 5,
        out_specs=[vmem_spec()] * len(kinds),
        scratch_shapes=[pltpu.VMEM((heads, span, HEAD_DIM), jnp.float32)] * 2,
        compiler_params=pltpu.CompilerParams(vmem_limit_bytes=VMEM_BYTES),
        cost_estimate=cost(8),
        name="attn_backward",
    )(q_ends, k_ends, queries, keys_values, upstream, full, lse)


def exchange(blocks):
    return lax.all_to_all(blocks, "blk", 0, 0, tiled=True)


def as_rows(blocks):
    return blocks.reshape(blocks.shape[0] * blocks.shape[1], blocks.shape[2])


def as_blocks(rows):
    devices = lax.axis_size("blk")
    return rows.reshape(devices, rows.shape[0] // devices, rows.shape[1])


def write_blocks(out_ref, values, lanes, kind, width):
    span = values.shape[0] // lanes
    for group in range(WIDTH // width):
        for lane in range(lanes):
            out_ref[lane * (WIDTH // width) + group, :, kind * width : (kind + 1) * width] = values[
                lane * span : (lane + 1) * span, group * width : (group + 1) * width
            ]


def read_blocks(got_ref, lanes, kind, width):
    groups = got_ref.shape[0] // lanes
    cols = slice(kind * width, (kind + 1) * width)
    rows = [
        jnp.concatenate([got_ref[lane * groups + group, :, cols] for group in range(groups)], axis=1)
        for lane in range(lanes)
    ]
    return jnp.concatenate(rows, axis=0)


def dot(left, right):
    return pair_dot(left, right, 1, 0)


def dot_back(left, right):
    return pair_dot(left, right, 1, 1)


def shape(*sizes, of=jnp.float32):
    return jax.ShapeDtypeStruct(sizes, of)


def normalize(values):
    center = values - jnp.mean(values, -1, keepdims=True)
    scale = lax.rsqrt(jnp.mean(center * center, -1, keepdims=True) + 1e-05)
    return center * scale, scale


def norm_back(upstream, normed, scale, gains_row):
    grad = upstream * gains_row
    return scale * (
        grad
        - jnp.mean(grad, -1, keepdims=True)
        - normed * jnp.mean(grad * normed, -1, keepdims=True)
    )


def project_blocks(inputs, parts, lanes, width, name):
    def body(ins, loaded, outs, _):
        for kind, weight in enumerate(loaded):
            write_blocks(
                outs[0], dot(ins[0][...], weight.value()).astype(jnp.bfloat16), lanes, kind, width
            )

    devices, span = lax.axis_size("blk"), inputs.shape[0] // lanes
    (blocks,) = call_with_parts(
        body,
        [inputs],
        parts,
        [shape(devices, span, width * len(parts), of=jnp.bfloat16)],
        name,
    )
    return blocks


def after_self(got, tokens, gains, biases, out_part, query_part, lanes, width):
    def body(ins, loaded, outs, _):
        got_ref, tokens_ref, gains_ref, biases_ref = ins
        low_ref, normed_ref, scale_ref, hidden_ref, blocks_ref = outs
        attended = read_blocks(got_ref, lanes, 0, width)
        low_ref[...] = attended
        resid = tokens_ref[...].astype(jnp.float32) + dot(attended, loaded[0].value())
        normed, scale = normalize(resid)
        normed_ref[...] = normed
        scale_ref[...] = scale
        hidden = (normed * gains_ref[0:1] + biases_ref[0:1]).astype(jnp.bfloat16)
        hidden_ref[...] = hidden
        query = dot(hidden, loaded[1].value()).astype(jnp.bfloat16)
        write_blocks(blocks_ref, query, lanes, 0, width)

    rows = tokens.shape[0]
    return call_with_parts(
        body,
        [got, tokens, gains, biases],
        [out_part, query_part],
        [
            shape(rows, WIDTH, of=jnp.bfloat16),
            shape(rows, WIDTH),
            shape(rows, 1),
            shape(rows, WIDTH, of=jnp.bfloat16),
            shape(*got.shape, of=jnp.bfloat16),
        ],
        "after_self",
    )


def feed_forward(got, normed_in, cotangent, gains, biases, out_part, in_parts, down, outs, up, lanes, width):
    pieces = len(in_parts)
    step = in_parts[0].width

    def body(ins, loaded, refs, scratch):
        got_ref, normed_in_ref, cot_ref, gains_ref, biases_ref = ins
        (
            output_ref,
            low_ref,
            mixed_ref,
            adapted_ref,
            dunder_ref,
            dab_ref,
            dcb_ref,
            dresid_ref,
            blocks_ref,
            norms_ref,
        ) = refs
        (slopes,) = scratch
        w_out, w_in = loaded[0], loaded[1 : 1 + pieces]
        w_down, w_ff, w_up = loaded[1 + pieces :]
        attended = read_blocks(got_ref, lanes, 0, width)
        low_ref[...] = attended
        hidden = normed_in_ref[...] * gains_ref[0:1] + biases_ref[0:1]
        normed_one, scale_one = normalize(hidden + dot(attended, w_out.value()))
        mixed = normed_one * gains_ref[1:2] + biases_ref[1:2]
        mixed_low = mixed.astype(jnp.bfloat16)
        mixed_ref[...] = mixed_low
        summed = mixed
        under = dot(mixed_low, w_down.value())
        gate = 1.0 / (1.0 + jnp.exp(-under))
        adapted = (under * gate).astype(jnp.bfloat16)
        adapted_ref[...] = adapted
        under_slope = gate * (1.0 + under * (1.0 - gate))
        summed = summed + 4.0 * dot(adapted, w_up.value())
        for piece in range(pieces):
            before = dot(mixed_low, w_in[piece].value())
            below = 0.5 + 0.5 * lax.erf(before * (0.5**0.5))
            slopes[piece] = below + before * jnp.exp(-0.5 * before * before) * (
                (2.0 * math.pi) ** -0.5
            )
            act = (before * below).astype(jnp.bfloat16)
            summed = summed + dot(act, w_ff[piece].value())
        normed_two, scale_two = normalize(summed)
        output_ref[...] = (normed_two * gains_ref[2:3] + biases_ref[2:3]).astype(jnp.bfloat16)
        upstream = cot_ref[...].astype(jnp.float32)
        norms_ref[0:1] = jnp.sum(upstream * normed_two, axis=0, keepdims=True)
        norms_ref[1:2] = jnp.sum(upstream, axis=0, keepdims=True)
        dz = norm_back(upstream, normed_two, scale_two, gains_ref[2:3])
        dzb = dz.astype(jnp.bfloat16)
        dab = (4.0 * dz).astype(jnp.bfloat16)
        dab_ref[...] = dab
        dunder = (under_slope * dot_back(dab, w_up.value())).astype(jnp.bfloat16)
        dunder_ref[...] = dunder
        dmixed = dz + dot_back(dunder, w_down.value())
        for piece in range(pieces):
            dpre = (slopes[piece] * dot_back(dzb, w_ff[piece].value())).astype(jnp.bfloat16)
            dmixed = dmixed + dot_back(dpre, w_in[piece].value())
        norms_ref[2:3] = jnp.sum(dmixed * normed_one, axis=0, keepdims=True)
        norms_ref[3:4] = jnp.sum(dmixed, axis=0, keepdims=True)
        dresid = norm_back(dmixed, normed_one, scale_one, gains_ref[1:2])
        dresid_ref[...] = dresid
        dcb = dresid.astype(jnp.bfloat16)
        dcb_ref[...] = dcb
        write_blocks(
            blocks_ref, dot_back(dcb, w_out.value()).astype(jnp.bfloat16), lanes, 0, width
        )

    rows = normed_in.shape[0]
    low = jnp.bfloat16

    def body_rows(ins, loaded, refs, scratch):
        whole_ff = loaded[2 + pieces]

        class Rows:
            def __init__(self, piece):
                self.piece = piece

            def value(self):
                return whole_ff.value()[self.piece * step : (self.piece + 1) * step]

        loaded = loaded[: 2 + pieces] + [[Rows(piece) for piece in range(pieces)], loaded[-1]]
        body(ins, loaded, refs, scratch)

    return call_with_parts(
        body_rows,
        [got, normed_in, cotangent, gains, biases],
        [out_part] + in_parts + [down, outs, up],
        [
            shape(rows, WIDTH, of=low),
            shape(rows, WIDTH, of=low),
            shape(rows, WIDTH, of=low),
            shape(rows, down.width, of=low),
            shape(rows, down.width, of=low),
            shape(rows, WIDTH, of=low),
            shape(rows, WIDTH, of=low),
            shape(rows, WIDTH),
            shape(*got.shape, of=low),
            shape(4, WIDTH),
        ],
        "feed_forward",
        [pltpu.VMEM((pieces, rows, step), jnp.float32)],
        20,
    )


def before_self(got, dresid, normed, scale, gains, query_part, out_part, lanes, width):
    def body(ins, loaded, outs, _):
        got_ref, dresid_ref, normed_ref, scale_ref, gains_ref = ins
        dcq_ref, dr_ref, dsb_ref, blocks_ref, norms_ref = outs
        dcq = read_blocks(got_ref, lanes, 0, width)
        dcq_ref[...] = dcq
        dhidden = dresid_ref[...] + dot_back(dcq, loaded[0].value())
        normed = normed_ref[...]
        norms_ref[0:1] = jnp.sum(dhidden * normed, axis=0, keepdims=True)
        norms_ref[1:2] = jnp.sum(dhidden, axis=0, keepdims=True)
        dr = norm_back(dhidden, normed, scale_ref[...], gains_ref[0:1])
        dr_ref[...] = dr
        dsb = dr.astype(jnp.bfloat16)
        dsb_ref[...] = dsb
        grad = dot_back(dsb, loaded[1].value()).astype(jnp.bfloat16)
        write_blocks(blocks_ref, grad, lanes, 0, width)

    rows = dresid.shape[0]
    return call_with_parts(
        body,
        [got, dresid, normed, scale, gains],
        [query_part, out_part],
        [
            shape(rows, WIDTH, of=jnp.bfloat16),
            shape(rows, WIDTH),
            shape(rows, WIDTH, of=jnp.bfloat16),
            shape(*got.shape, of=jnp.bfloat16),
            shape(2, WIDTH),
        ],
        "before_self",
    )


def input_grad(got, start, parts, lanes, span, width, name):
    def body(ins, loaded, outs, _):
        total = None
        for kind, weight in enumerate(loaded):
            values = read_blocks(ins[0], lanes, kind, width)
            term = dot_back(values, weight.value())
            total = term if total is None else total + term
        outs[0][...] = total if len(ins) == 1 else total + ins[1][...]

    rows = span * lanes
    return call_with_parts(
        body,
        [got] if start is None else [got, start],
        parts,
        [shape(rows, WIDTH)],
        name,
    )


def sum_everywhere(values, stages):
    if not paired():
        return lax.psum(values, ("dp", "blk"))
    values = after(values, stages[0])
    values = values + swap_core(values)
    for step, bit in enumerate((1, 2, 4, 8)):
        if step + 1 < len(stages):
            values = after(values, stages[step + 1])
        values = values + flip(values, bit)
    return values


def shards(
    tokens,
    encoder,
    cotangent,
    self_in,
    self_out,
    cross_q,
    cross_kv,
    cross_out,
    ffn_in,
    ffn_out,
    adapt_down,
    adapt_up,
    norm_gain,
    norm_bias,
    tgt_lengths,
    src_lengths,
):
    lanes, span, _ = tokens.shape
    rows = lanes * span
    width = WIDTH * lanes // lax.axis_size("blk")
    own_row = lax.axis_index("blk") // (lax.axis_size("blk") // lanes)
    tgt_ends = jnp.cumsum(lax.dynamic_index_in_dim(tgt_lengths, own_row, 0, keepdims=False))
    src_ends = jnp.cumsum(lax.dynamic_index_in_dim(src_lengths, own_row, 0, keepdims=False))
    flat_tokens = tokens.reshape(rows, WIDTH)
    flat_encoder = encoder.reshape(rows, WIDTH)
    frozen = [ffn_in, adapt_down, ffn_out, adapt_up, cross_out]
    inward = [self_in, cross_kv]

    if paired():
        packed = gather_packed(pack_halves(frozen))
        inward_packed = pack_halves(inward)
        token_row, stages = gather_row(tokens)
        self_heads, pair_heads = head_columns(inward, [3, 2])
        out_shard, query_shard = after((self_out, cross_q), stages[1])
        encoder_block = after(encoder, stages[1])
        self_qkv = project_row(token_row, self_heads, "self_in")
        out_source, query_source = gather_flips([out_shard, query_shard], "xy", self_qkv)
        encoder_row, encoder_stages = gather_row(
            encoder_block, self_qkv, (out_source.arrays[1], query_source.arrays[1])
        )
        self_qkv = after(self_qkv, out_source.stages[0], query_source.stages[0])
        pair_own = project_row(encoder_row, pair_heads, "cross_kv")
    else:
        (self_source, pair_source, out_source, query_source) = gather_flips(
            [self_in, cross_kv, self_out, cross_q], "xyxy"
        )
        self_parts = [columns_of((self_source, WIDTH * kind, WIDTH)) for kind in range(3)]
        pair_parts = [columns_of((pair_source, WIDTH * kind, WIDTH)) for kind in range(2)]
        self_qkv = as_rows(
            exchange(project_blocks(flat_tokens, self_parts, lanes, width, "self_in"))
        )
        pair_own = as_rows(
            exchange(project_blocks(flat_encoder, pair_parts, lanes, width, "cross_kv"))
        )
    self_out_part = columns_of((out_source, 0, WIDTH))
    query_part = columns_of((query_source, 0, WIDTH))

    self_mid, self_full, self_lse = attn_forward(
        tgt_ends, tgt_ends, self_qkv, self_qkv, width, True
    )
    self_sent = after(self_mid, out_source.stages[1], query_source.stages[1])
    if paired():
        self_sent = after(self_sent, encoder_stages[0])
    self_back = exchange(as_blocks(self_sent))
    if paired():
        self_back = after(self_back, encoder_stages[1])
    self_low, normed, scale, hidden_low, query_blocks = after_self(
        self_back,
        flat_tokens,
        norm_gain,
        norm_bias,
        self_out_part,
        query_part,
        lanes,
        width,
    )
    cross_own = as_rows(exchange(query_blocks))
    cross_mid, cross_full, cross_lse = attn_forward(
        tgt_ends, src_ends, cross_own, pair_own, width, False
    )
    cross_back = exchange(as_blocks(cross_mid))
    ready = after(packed, cross_mid) if paired() else None
    ff_parts, down_parts, ffo_parts, up_parts, (cross_out_part,) = packed_parts(frozen, ready)
    if paired():
        inward_packed = gather_packed(after(inward_packed, cross_back))
    (
        output,
        cross_low,
        mixed_low,
        adapter_low,
        grad_under,
        adapt_low,
        cross_branch_low,
        grad_resid_two,
        cross_grad_blocks,
        norms_high,
    ) = feed_forward(
        cross_back,
        normed,
        cotangent.reshape(rows, WIDTH),
        norm_gain,
        norm_bias,
        cross_out_part,
        ff_parts,
        down_parts[0],
        ffo_parts[0],
        up_parts[0],
        lanes,
        width,
    )
    high_groups = [
        [(cross_low, cross_branch_low)],
        [(mixed_low, grad_under), (adapter_low, adapt_low)],
    ]
    high_terms = [grad_terms(pairs) for pairs in high_groups]
    high_orders = [(2, 1, 4, 8), (1, 2, 4, 8)]
    high_terms, high_stages = scatter_chips(high_terms, high_orders, 0, 2)
    cross_dq, cross_dkv = attn_backward(
        tgt_ends,
        src_ends,
        cross_own,
        pair_own,
        as_rows(after(exchange(cross_grad_blocks), high_stages[0])),
        cross_full,
        cross_lse,
        False,
    )
    cq_low, grad_resid_one, self_branch_low, self_grad_blocks, norms_low = before_self(
        after(exchange(as_blocks(cross_dq)), high_stages[1]),
        grad_resid_two,
        normed,
        scale,
        norm_gain,
        query_part,
        self_out_part,
        lanes,
        width,
    )
    mid_groups = [[(hidden_low, cq_low)], [(self_low, self_branch_low)]]
    mid_terms, mid_stages = scatter_chips(
        [grad_terms(pairs) for pairs in mid_groups], [(2, 1, 4, 8), (1, 2, 4, 8)], 0, 4
    )
    (grad_cross_q,), (grad_self_out,) = finish_terms(mid_groups, mid_terms)
    (self_grads,) = attn_backward(
        tgt_ends,
        tgt_ends,
        self_qkv,
        self_qkv,
        as_rows(after(exchange(self_grad_blocks), high_stages[2])),
        self_full,
        self_lse,
        True,
        joined=True,
    )
    pair_got = exchange(as_blocks(cross_dkv))
    self_got = as_blocks(self_grads)
    high_terms, _ = scatter_chips(after(high_terms, self_grads), high_orders, 2, 4)
    (high_grads, adapt_grads) = finish_terms(high_groups, high_terms)
    (grad_cross_out,), (grad_adapt_down, grad_adapt_up) = high_grads, adapt_grads
    if paired():
        self_parts, pair_parts = packed_parts(inward, after(inward_packed, self_grads))
        self_got = exchange(after(self_got, pair_got, mid_stages[1]))
        (encoder_grad,) = input_grad(
            pair_got, None, pair_parts, lanes, span, width, "encoder_grad"
        )
        dkv_late = after(cross_dkv, self_grad_blocks)
        sent = [
            row_grad(token_row, self_grads, "self_in_grad"),
            row_grad(encoder_row, dkv_late, "cross_kv_grad"),
        ]
        sent = after(jnp.concatenate(sent, axis=2), self_got, encoder_grad, mid_stages[2])
        grads_got = exchange(sent)
    else:
        self_got = exchange(self_got)
        (encoder_grad,) = input_grad(
            pair_got, None, pair_parts, lanes, span, width, "encoder_grad"
        )
    (tokens_grad,) = input_grad(
        self_got, grad_resid_one, self_parts, lanes, span, width, "tokens_grad"
    )
    if paired():
        grads_got = after(grads_got, tokens_grad)
        grad_self_in = finish_row_grad(grads_got[:, :, : 3 * width], 3)
        grad_cross_kv = finish_row_grad(grads_got[:, :, 3 * width :], 2)
    else:
        pair_low = pair_got.reshape(lanes, -1, span, 2, width).transpose(0, 2, 3, 1, 4)
        self_low_grads = self_got.reshape(lanes, -1, span, 3, width).transpose(0, 2, 3, 1, 4)
        grad_cross_kv = weight_grad(flat_encoder, pair_low.reshape(rows, 2 * WIDTH))
        grad_self_in = weight_grad(flat_tokens, self_low_grads.reshape(rows, 3 * WIDTH))
    norms = sum_everywhere(jnp.concatenate([norms_low, norms_high], axis=0), mid_stages)
    return (
        output.reshape(lanes, span, WIDTH),
        tokens_grad.reshape(lanes, span, WIDTH),
        encoder_grad.reshape(lanes, span, WIDTH),
        grad_self_in,
        grad_self_out,
        grad_cross_q,
        grad_cross_kv,
        grad_cross_out,
        grad_adapt_down,
        grad_adapt_up,
        jnp.stack([norms[0], norms[4], norms[2]]),
        jnp.stack([norms[1], norms[5], norms[3]]),
    )


def solution(mesh):
    placed = (
        P("dp", "blk", None),
        P("dp", "blk", None),
        P("dp", "blk", None),
        P("blk", None),
        P("blk", None),
        P("blk", None),
        P("blk", None),
        P("blk", None),
        P("blk", None),
        P("blk", None),
        P("blk", None),
        P("blk", None),
        P(),
        P(),
        P("dp", None),
        P("dp", None),
    )
    return jax.shard_map(
        shards,
        mesh=mesh,
        in_specs=placed,
        out_specs=(
            P("dp", "blk", None),
            P("dp", "blk", None),
            P("dp", "blk", None),
            P("blk", None),
            P("blk", None),
            P("blk", None),
            P("blk", None),
            P("blk", None),
            P("blk", None),
            P("blk", None),
            P(),
            P(),
        ),
        check_vma=False,
    )
```

```python
import functools
import math

import jax
import jax.numpy as jnp
from jax import lax
from jax.experimental import pallas as pl
from jax.experimental.pallas import tpu as pltpu
from jax.sharding import PartitionSpec as P

HEADS = 16
HEAD_DIM = 64
WIDTH = HEADS * HEAD_DIM


NEG = -1e30
VMEM_BYTES = 56 * 1024 * 1024


def cost(microseconds):
    return pl.CostEstimate(
        flops=int(microseconds * 0.4e9),
        bytes_accessed=int(microseconds * 1.2e6),
        transcendentals=0,
    )


def paired():
    return lax.axis_size("blk") == 16 and lax.axis_size("dp") == 2


def swap_core(block):
    cores = lax.axis_size("dp")
    return lax.ppermute(block, "dp", [(i ^ 1, i) for i in range(cores)])


def flip(block, bit):
    chips = lax.axis_size("blk")
    return lax.ppermute(block, "blk", [(i ^ bit, i) for i in range(chips)])


FLIPS = (8, 4, 2, 1)


def with_flip(block, bit):
    return jnp.stack([block, flip(block, bit)])


def own_half(values, which):
    half = values.shape[1] // 2
    return lax.dynamic_slice_in_dim(values, which * half, half, 1)


def scatter_chips(terms, orders, first, last):
    if not paired():
        return terms, [terms] * 5
    own = lax.axis_index("blk")

    def fold(blocks, left, bit):
        axis, place = left.index(bit), (own // bit) % 2
        kept = lax.dynamic_index_in_dim(blocks, place, axis, keepdims=False)
        sent = lax.dynamic_index_in_dim(blocks, 1 - place, axis, keepdims=False)
        got = flip(sent, bit)
        return (kept.astype(jnp.float32) + got.astype(jnp.float32)).astype(jnp.bfloat16)

    if first == 0:
        terms = [blocks.reshape(2, 2, 2, 2, *blocks.shape[1:]) for blocks in terms]
    stages = [terms[0]]
    for stage in range(first, last):
        terms = [
            fold(blocks, [bit for bit in FLIPS if bit not in order[:stage]], order[stage])
            for blocks, order in zip(terms, orders)
        ]
        stages.append(terms[0])
    return terms, stages


CHUNK = 256


def grad_terms(pairs):
    if not paired():
        return pairs[0][1]
    core = lax.axis_index("dp")
    packed = []
    for inputs, upstream in pairs:
        both = jnp.concatenate([inputs, swap_core(inputs)], axis=0)
        half = jnp.concatenate(
            [own_half(upstream, core), swap_core(own_half(upstream, 1 - core))], axis=0
        )
        term = lax.dot_general(
            both, half, (((0,), (0,)), ((), ())), preferred_element_type=jnp.float32
        ).astype(jnp.bfloat16)
        rows = term.shape[0] // 16
        chunks = term.shape[1] // CHUNK
        packed += [
            term[:, c * CHUNK : (c + 1) * CHUNK].reshape(16, rows, CHUNK) for c in range(chunks)
        ]
    return jnp.concatenate(packed, axis=1)


def finish_terms(groups, terms):
    if not paired():
        return [[weight_grad(inputs, upstream) for inputs, upstream in pairs] for pairs in groups]
    core = lax.axis_index("dp")
    mine = jnp.concatenate(terms, axis=0)
    other = swap_core(mine)
    low = jnp.where(core == 0, mine, other).astype(jnp.float32)
    high = jnp.where(core == 0, other, mine).astype(jnp.float32)
    found, place = [], 0
    for pairs in groups:
        found.append([])
        for inputs, upstream in pairs:
            rows = inputs.shape[1] // 16
            chunks = upstream.shape[1] // 2 // CHUNK
            spots = [slice(place + c * rows, place + (c + 1) * rows) for c in range(chunks)]
            found[-1].append(
                jnp.concatenate(
                    [low[spot] for spot in spots] + [high[spot] for spot in spots], axis=1
                )
            )
            place += rows * chunks
    return found


def weight_grad(inputs, upstream):
    scattered = lax.psum_scatter(
        lax.dot_general(
            inputs, upstream, (((0,), (0,)), ((), ())), preferred_element_type=jnp.float32
        ).astype(jnp.bfloat16),
        "blk",
        scatter_dimension=0,
        tiled=True,
    )
    return lax.psum(scattered, "dp").astype(jnp.float32)


class Source:
    def __init__(self, kind, arrays, first_flip="x", column=None):
        self.kind, self.arrays, self.first_flip = kind, arrays, first_flip
        self.stages = arrays[:1] * 3 if column is None else [column] + arrays[:2]


class Part:
    def __init__(self, rows, width, spots):
        self.rows, self.width, self.spots = rows, width, spots

    def scratch(self):
        return pltpu.VMEM((2, 2, 2, 2, 2, self.rows // 32, self.width), jnp.bfloat16)

    def start(self, refs_of, place, dst, sem):
        z1, z0, y, x, core = [place[axis] for axis in range(5)]
        high = self.rows // 32
        for source, first_row, first_col, at_col, width in self.spots:
            refs = refs_of(source)
            cols = slice(first_col, first_col + width)
            into = slice(at_col, at_col + width)
            if source.kind == "whole":
                pltpu.make_async_copy(
                    refs[0].at[:, :, :, :, :, :, cols], dst.at[:, :, :, :, :, :, into], sem
                ).start()
            elif source.kind == "cores":
                for which in range(2):
                    owner = core if which == 0 else 1 - core
                    pltpu.make_async_copy(
                        refs[which].at[:, :, :, :, first_row : first_row + high, cols],
                        dst.at[:, :, :, :, owner, :, into],
                        sem,
                    ).start()
            else:
                for which in range(4):
                    owner = core if which < 2 else 1 - core
                    for near, at_y, at_x in flipped(source.first_flip, which % 2, y, x):
                        for up, at_z1, at_z0 in four(z1, z0):
                            pltpu.make_async_copy(
                                refs[which].at[near, up[0], up[1], :, cols],
                                dst.at[at_z1, at_z0, at_y, at_x, owner, :, into],
                                sem,
                            ).start()


def four(z1, z0):
    return [
        ((low, high), z1 if high == 0 else 1 - z1, z0 if low == 0 else 1 - z0)
        for low in range(2)
        for high in range(2)
    ]


def flipped(first_flip, beyond, y, x):
    found = []
    for near in range(2):
        a, b = (near, beyond) if first_flip == "x" else (beyond, near)
        found.append((near, y if b == 0 else 1 - y, x if a == 0 else 1 - x))
    return found


def after(value, *others):
    return lax.optimization_barrier((value, *others))[0]


def gather_flips(shards, first_flips, hold=None):
    if not paired():
        full = [lax.all_gather(shard, "blk", axis=0, tiled=True) for shard in shards]
        return [
            Source("whole", [array.reshape(2, 2, 2, 2, 2, array.shape[0] // 32, array.shape[1])])
            for array in full
        ]
    core = lax.axis_index("dp")
    columns = []
    for shard in shards:
        rows = shard.shape[0]
        own = lax.dynamic_slice_in_dim(shard, core * (rows // 2), rows // 2, 0)
        columns.append(with_flip(with_flip(own, 8), 4))
    sources, bits = [], {"x": (1, 2), "y": (2, 1)}
    if hold is not None:
        columns = after(columns, hold)
    planes = [
        with_flip(column, bits[first][0]) for column, first in zip(columns, first_flips)
    ]
    for column, plane, first in zip(columns, planes, first_flips):
        beyond = flip(plane, bits[first][1])
        sources.append(
            Source("flips", [plane, beyond, swap_core(plane), swap_core(beyond)], first, column)
        )
    return sources


class RowPart:
    def __init__(self, sources, span):
        self.span = span
        self.rows, self.width = 16 * span, WIDTH
        self.spots = [(source,) for source in sources]

    def scratch(self):
        return pltpu.VMEM((2, 2, 2, 2, self.span, WIDTH), jnp.bfloat16)

    def start(self, refs_of, place, dst, sem):
        z1, z0, y, x = [place[axis] for axis in range(4)]
        half = WIDTH // 2
        for side, (source,) in enumerate(self.spots):
            refs = refs_of(source)
            for beyond in range(2):
                for near, at_y, at_x in flipped(source.first_flip, beyond, y, x):
                    for up, at_z1, at_z0 in four(z1, z0):
                        pltpu.make_async_copy(
                            refs[beyond].at[near, up[0], up[1]],
                            dst.at[at_z1, at_z0, at_y, at_x, :, side * half : (side + 1) * half],
                            sem,
                        ).start()


def gather_row(block, hold_near=None, hold=None):
    row = lax.axis_index("blk") // 8
    own = lax.dynamic_index_in_dim(block, row, 0, keepdims=False)
    other = lax.dynamic_index_in_dim(block, 1 - row, 0, keepdims=False)
    pair = jnp.stack([own, flip(other, 8)])
    if hold_near is not None:
        pair = after(pair, hold_near)
    column = with_flip(pair, 4)
    stages, sources = [pair, column], []
    if hold is not None:
        column = after(column, hold)
    half = WIDTH // 2
    planes = [with_flip(column[..., :half], 1), with_flip(column[..., half:], 2)]
    for plane, first, bit in zip(planes, "xy", (2, 1)):
        sources.append(Source("row", [plane, flip(plane, bit)], first))
    stages += [planes, [source.arrays[1] for source in sources]]
    return RowPart(sources, block.shape[1]), stages


def head_columns(shards, kinds):
    core = lax.axis_index("dp")
    blocks, widths = [], [128 * kind for kind in kinds]
    for shard, kind in zip(shards, kinds):
        own = lax.dynamic_slice_in_dim(shard, core * 32, 32, 0)
        own = own.reshape(32, kind, 8, 128).transpose(2, 0, 1, 3)
        blocks.append(own.reshape(8, 32, kind * 128))
    blocks = jnp.concatenate(blocks, axis=2)
    mine = exchange(jnp.concatenate([blocks, blocks], axis=0))
    mine = mine.reshape(2, 2, 2, 2, 32, sum(widths))
    source = Source("cores", [mine, swap_core(mine)])
    parts, place = [], 0
    for width in widths:
        parts.append(Part(1024, width, [(source, 0, place, 0, width)]))
        place += width
    return parts


def project_row(row_part, head_part, name):
    def body(ins, loaded, outs, _):
        weight = loaded[1].value()
        inputs = loaded[0].value()
        for first in range(0, row_part.rows, 256):
            rows = slice(first, first + 256)
            outs[0][rows, :] = dot(inputs[rows], weight).astype(jnp.bfloat16)

    (found,) = call_with_parts(
        body,
        [],
        [row_part, head_part],
        [shape(row_part.rows, head_part.width, of=jnp.bfloat16)],
        name,
    )
    return found


def row_grad(row_part, upstream, name):
    columns = upstream.shape[1]

    def body(ins, loaded, outs, _):
        core = ins[1][0]
        inputs = loaded[0].value()
        grads = []
        for first in range(0, columns, 128):
            grads.append(pair_dot(ins[0][:, first : first + 128], inputs, 0, 0).T)
        grad = jnp.concatenate(grads, axis=1).astype(jnp.bfloat16).reshape(16, 2, 32, columns)
        outs[0][core] = grad[:, 0]
        outs[0][1 - core] = grad[:, 1]

    (terms,) = call_with_parts(
        body,
        [upstream],
        [row_part],
        [shape(2, 16, 32, columns, of=jnp.bfloat16)],
        name,
        scalars=[lax.axis_index("dp").reshape(1).astype(jnp.int32)],
    )
    got = swap_core(terms[1])
    return (terms[0].astype(jnp.float32) + got.astype(jnp.float32)).astype(jnp.bfloat16)


def row_back(upstream, head_part, name):
    def body(ins, loaded, outs, _):
        weight = loaded[0].value()
        for first in range(0, ins[0].shape[0], 256):
            rows = slice(first, first + 256)
            outs[0][rows, :] = dot_back(ins[0][rows, :], weight).astype(jnp.bfloat16)

    (terms,) = call_with_parts(
        body, [upstream], [head_part], [shape(upstream.shape[0], WIDTH, of=jnp.bfloat16)], name
    )
    return terms


def reduce_row(terms):
    blocks = terms.reshape(16, terms.shape[0] // 16, WIDTH)
    half = WIDTH // 2
    halves, stages = scatter_chips(
        [blocks[..., :half], blocks[..., half:]], [(1, 2, 4, 8), (2, 1, 4, 8)], 0, 3
    )
    both = jnp.concatenate(halves, axis=2)
    row = lax.axis_index("blk") // 8
    kept = lax.dynamic_index_in_dim(both, row, 0, keepdims=False)
    got = flip(lax.dynamic_index_in_dim(both, 1 - row, 0, keepdims=False), 8)
    found = jnp.stack([jnp.where(row == 0, kept, got), jnp.where(row == 0, got, kept)])
    return found.astype(jnp.float32), stages


def finish_row_grad(got, kinds):
    total = jnp.sum(got.reshape(2, 8, 32, kinds, 128).astype(jnp.float32), axis=0)
    mine = total.astype(jnp.bfloat16).transpose(1, 2, 0, 3).reshape(32, kinds * WIDTH)
    other = swap_core(mine)
    core = lax.axis_index("dp")
    low = jnp.where(core == 0, mine, other)
    high = jnp.where(core == 0, other, mine)
    return jnp.concatenate([low, high], axis=0).astype(jnp.float32)


def columns_of(*pieces):
    spots, place = [], 0
    for source, first, width in pieces:
        spots.append((source, 0, first, place, width))
        place += width
    return Part(1024, place, spots)


PACK = 512


def pack_halves(shards):
    places = [
        (index, shard.shape[0] // 2, first)
        for index, shard in enumerate(shards)
        for first in range(0, shard.shape[1], PACK)
    ]

    def body(core, *refs):
        out_ref, place = refs[-1], 0
        for index, high, first in places:
            start = pl.multiple_of(core[0] * high, 16)
            out_ref[place : place + high, :] = refs[index][pl.ds(start, high), first : first + PACK]
            place += high

    return pl.pallas_call(
        body,
        out_shape=shape(sum(high for _, high, _ in places), PACK, of=jnp.bfloat16),
        in_specs=[smem_spec()] + [vmem_spec()] * len(shards),
        out_specs=vmem_spec(),
        compiler_params=pltpu.CompilerParams(vmem_limit_bytes=VMEM_BYTES),
        cost_estimate=cost(2),
        name="pack_halves",
    )(lax.axis_index("dp").reshape(1).astype(jnp.int32), *shards)


def gather_packed(packed):
    return lax.all_gather(packed, "blk", axis=0)


def packed_parts(shards, mine):
    if not paired():
        found = []
        for source, shard in zip(gather_flips(shards, "x" * len(shards)), shards):
            rows, columns = 32 * source.arrays[0].shape[5], shard.shape[1]
            step = min(columns, 1024)
            found.append(
                [
                    Part(rows, step, [(source, 0, first, 0, step)])
                    for first in range(0, columns, step)
                ]
            )
        return found
    spots, place = [], 0
    for shard in shards:
        high = shard.shape[0] // 2
        places = []
        for first in range(0, shard.shape[1], PACK):
            places.append(place)
            place += high
        spots.append((shard.shape[0] * 16, places))
    mine = mine.reshape(2, 2, 2, 2, place, PACK)
    source = Source("cores", [mine, swap_core(mine)])
    found = []
    for rows, places in spots:
        parts = []
        for first in range(0, len(places), 2):
            two = places[first : first + 2]
            parts.append(
                Part(
                    rows,
                    PACK * len(two),
                    [(source, row, 0, PACK * side, PACK) for side, row in enumerate(two)],
                )
            )
        found.append(parts)
    return found


def place_now():
    own, core = lax.axis_index("blk"), lax.axis_index("dp")
    bits = [(own // bit) % 2 for bit in FLIPS]
    return jnp.stack(bits + [core]).astype(jnp.int32)


class Loaded:
    def __init__(self, part, dst, sem):
        self.part, self.dst, self.sem, self.here = part, dst, sem, False

    def value(self):
        if not self.here:
            pltpu.make_async_copy(self.dst, self.dst, self.sem).wait()
            self.here = True
        return self.dst[...].reshape(self.part.rows, self.part.width)


def call_with_parts(body, inputs, parts, outputs, name, scratch=(), takes=5, scalars=()):
    sources = []
    for part in parts:
        sources += [spot[0] for spot in part.spots if spot[0] not in sources]
    arrays = [array for source in sources for array in source.arrays]

    def kernel(place, *refs):
        refs = list(refs)
        ins = [refs.pop(0) for _ in (*inputs, *scalars)]
        pieces = [[refs.pop(0) for _ in source.arrays] for source in sources]
        outs = [refs.pop(0) for _ in outputs]
        dsts = [refs.pop(0) for _ in parts]
        sems = refs.pop(0)
        loaded = []
        for index, part in enumerate(parts):
            part.start(
                lambda source: pieces[sources.index(source)], place, dsts[index], sems.at[index]
            )
            loaded.append(Loaded(part, dsts[index], sems.at[index]))
        body(ins, loaded, outs, refs)

    return pl.pallas_call(
        kernel,
        out_shape=tuple(outputs),
        in_specs=[smem_spec()]
        + [vmem_spec()] * len(inputs)
        + [smem_spec()] * len(scalars)
        + [pl.BlockSpec(memory_space=pl.ANY)] * len(arrays),
        out_specs=(vmem_spec(),) * len(outputs),
        scratch_shapes=[part.scratch() for part in parts]
        + [pltpu.SemaphoreType.DMA((len(parts),))]
        + list(scratch),
        compiler_params=pltpu.CompilerParams(vmem_limit_bytes=VMEM_BYTES),
        cost_estimate=cost(takes),
        name=name,
    )(place_now(), *inputs, *scalars, *arrays)


def vmem_spec():
    return pl.BlockSpec(memory_space=pltpu.VMEM)


def smem_spec():
    return pl.BlockSpec(memory_space=pltpu.SMEM)


def seg_of_pos(ends_ref, pos):
    seg = jnp.zeros(pos.shape, jnp.int32)
    for slot in range(ends_ref.shape[0]):
        seg = seg + (ends_ref[slot] <= pos).astype(jnp.int32)
    return seg


def pair_dot(left, right, left_dim, right_dim):
    return lax.dot_general(
        left, right, (((left_dim,), (right_dim,)), ((), ())), preferred_element_type=jnp.float32
    )


def seg_tables(q_ends, k_ends, span):
    seg_q = seg_of_pos(q_ends, lax.broadcasted_iota(jnp.int32, (1, span), 1))
    seg_k = seg_of_pos(k_ends, lax.broadcasted_iota(jnp.int32, (span, 1), 0))
    return seg_q, seg_k


def masked_scores(keys, queries, seg_q, seg_k, first, causal):
    scores = pair_dot(keys, queries, 1, 1)
    allowed = seg_k == seg_q
    if causal:
        key_pos = lax.broadcasted_iota(jnp.int32, scores.shape, 0)
        query_pos = first + lax.broadcasted_iota(jnp.int32, scores.shape, 1)
        allowed = allowed & (key_pos <= query_pos)
    return jnp.where(allowed, scores, NEG)


def attn_forward_body(causal, width, q_ends, k_ends, q_ref, kv_ref, low_ref, full_ref, lse_ref):
    span = q_ref.shape[0]
    step = math.gcd(span, 256)
    heads = width // HEAD_DIM
    seg_q, seg_k = seg_tables(q_ends, k_ends, span)
    key_at = kv_ref.shape[1] - 2 * width
    scaled = q_ref[:, :width] * jnp.bfloat16(HEAD_DIM ** (-0.5))
    keys = kv_ref[:, key_at : key_at + width]
    values = kv_ref[:, key_at + width : key_at + 2 * width]
    for first in range(0, span, step):
        reach = first + step if causal else span
        parts = []
        for head in range(heads):
            cols = slice(head * HEAD_DIM, (head + 1) * HEAD_DIM)
            scores = masked_scores(
                keys[:reach, cols],
                scaled[first : first + step, cols],
                seg_q[:, first : first + step],
                seg_k[:reach],
                first,
                causal,
            )
            top = jnp.max(scores, axis=0, keepdims=True)
            probs = jnp.exp(scores - top)
            total = jnp.sum(probs, axis=0, keepdims=True)
            mixed = pair_dot(values[:reach, cols], probs.astype(jnp.bfloat16), 0, 0)
            parts.append(mixed / total)
            lse_ref[head : head + 1, first : first + step] = top + jnp.log(total)
        joined = jnp.concatenate(parts, axis=0).T
        full_ref[first : first + step, :] = joined
        low_ref[first : first + step, :] = joined.astype(jnp.bfloat16)


def attn_forward(q_ends, k_ends, queries, keys_values, width, causal):
    span = queries.shape[0]
    return pl.pallas_call(
        functools.partial(attn_forward_body, causal, width),
        out_shape=(
            jax.ShapeDtypeStruct((span, width), jnp.bfloat16),
            jax.ShapeDtypeStruct((span, width), jnp.float32),
            jax.ShapeDtypeStruct((width // HEAD_DIM, span), jnp.float32),
        ),
        in_specs=[smem_spec(), smem_spec()] + [vmem_spec()] * 2,
        out_specs=(vmem_spec(),) * 3,
        compiler_params=pltpu.CompilerParams(vmem_limit_bytes=VMEM_BYTES),
        cost_estimate=cost(8),
        name="attn_forward",
    )(q_ends, k_ends, queries, keys_values)


def attn_backward_body(
    causal,
    width,
    q_ends,
    k_ends,
    q_ref,
    kv_ref,
    up_ref,
    full_ref,
    lse_ref,
    *outs,
):
    dq_ref, dkv_ref = outs[0], outs[-3]
    dk_sum, dv_sum = outs[-2:]
    span = q_ref.shape[0]
    step = math.gcd(span, 256)
    heads = width // HEAD_DIM
    seg_q, seg_k = seg_tables(q_ends, k_ends, span)
    key_at = kv_ref.shape[1] - 2 * width
    scaled = q_ref[:, :width] * jnp.bfloat16(HEAD_DIM ** (-0.5))
    keys = kv_ref[:, key_at : key_at + width]
    values = kv_ref[:, key_at + width : key_at + 2 * width]
    upstream = up_ref[...]
    dk_sum[...] = jnp.zeros_like(dk_sum)
    dv_sum[...] = jnp.zeros_like(dv_sum)
    for first in range(0, span, step):
        reach = first + step if causal else span
        rows = slice(first, first + step)
        product = (upstream[rows].astype(jnp.float32) * full_ref[rows, :]).T
        parts = []
        for head in range(heads):
            cols = slice(head * HEAD_DIM, (head + 1) * HEAD_DIM)
            delta = jnp.sum(product[cols], axis=0, keepdims=True)
            scores = masked_scores(
                keys[:reach, cols], scaled[rows, cols], seg_q[:, rows], seg_k[:reach], first, causal
            )
            probs = jnp.exp(scores - lse_ref[head : head + 1, rows])
            dv_sum[head, :reach] += pair_dot(
                probs.astype(jnp.bfloat16), upstream[rows, cols], 1, 0
            )
            grad_probs = pair_dot(values[:reach, cols], upstream[rows, cols], 1, 1)
            grad_scores = (probs * (grad_probs - delta)).astype(jnp.bfloat16)
            dk_sum[head, :reach] += pair_dot(grad_scores, scaled[rows, cols], 1, 0)
            parts.append(pair_dot(keys[:reach, cols], grad_scores, 0, 0))
        joined = jnp.concatenate(parts, axis=0).T * HEAD_DIM ** (-0.5)
        dq_ref[rows, :width] = joined.astype(jnp.bfloat16)
    sums = [dk_sum[head] for head in range(heads)] + [dv_sum[head] for head in range(heads)]
    kv_at = dkv_ref.shape[1] - 2 * width
    dkv_ref[:, kv_at:] = jnp.concatenate(sums, axis=1).astype(jnp.bfloat16)


def attn_backward(
    q_ends, k_ends, queries, keys_values, upstream, full, lse, causal, joined=False
):
    span, width = upstream.shape
    kinds = [3] if joined else [1, 2]
    heads = width // HEAD_DIM
    return pl.pallas_call(
        functools.partial(attn_backward_body, causal, width),
        out_shape=[jax.ShapeDtypeStruct((span, kind * width), jnp.bfloat16) for kind in kinds],
        in_specs=[smem_spec(), smem_spec()] + [vmem_spec()] * 5,
        out_specs=[vmem_spec()] * len(kinds),
        scratch_shapes=[pltpu.VMEM((heads, span, HEAD_DIM), jnp.float32)] * 2,
        compiler_params=pltpu.CompilerParams(vmem_limit_bytes=VMEM_BYTES),
        cost_estimate=cost(8),
        name="attn_backward",
    )(q_ends, k_ends, queries, keys_values, upstream, full, lse)


def exchange(blocks):
    return lax.all_to_all(blocks, "blk", 0, 0, tiled=True)


def as_rows(blocks):
    return blocks.reshape(blocks.shape[0] * blocks.shape[1], blocks.shape[2])


def as_blocks(rows):
    devices = lax.axis_size("blk")
    return rows.reshape(devices, rows.shape[0] // devices, rows.shape[1])


def write_blocks(out_ref, values, lanes, kind, width):
    span = values.shape[0] // lanes
    for group in range(WIDTH // width):
        for lane in range(lanes):
            out_ref[lane * (WIDTH // width) + group, :, kind * width : (kind + 1) * width] = values[
                lane * span : (lane + 1) * span, group * width : (group + 1) * width
            ]


def read_blocks(got_ref, lanes, kind, width):
    groups = got_ref.shape[0] // lanes
    cols = slice(kind * width, (kind + 1) * width)
    rows = [
        jnp.concatenate([got_ref[lane * groups + group, :, cols] for group in range(groups)], axis=1)
        for lane in range(lanes)
    ]
    return jnp.concatenate(rows, axis=0)


def dot(left, right):
    return pair_dot(left, right, 1, 0)


def dot_back(left, right):
    return pair_dot(left, right, 1, 1)


def shape(*sizes, of=jnp.float32):
    return jax.ShapeDtypeStruct(sizes, of)


def normalize(values):
    center = values - jnp.mean(values, -1, keepdims=True)
    scale = lax.rsqrt(jnp.mean(center * center, -1, keepdims=True) + 1e-05)
    return center * scale, scale


def norm_back(upstream, normed, scale, gains_row):
    grad = upstream * gains_row
    return scale * (
        grad
        - jnp.mean(grad, -1, keepdims=True)
        - normed * jnp.mean(grad * normed, -1, keepdims=True)
    )


def project_blocks(inputs, parts, lanes, width, name):
    def body(ins, loaded, outs, _):
        for kind, weight in enumerate(loaded):
            write_blocks(
                outs[0], dot(ins[0][...], weight.value()).astype(jnp.bfloat16), lanes, kind, width
            )

    devices, span = lax.axis_size("blk"), inputs.shape[0] // lanes
    (blocks,) = call_with_parts(
        body,
        [inputs],
        parts,
        [shape(devices, span, width * len(parts), of=jnp.bfloat16)],
        name,
    )
    return blocks


def after_self(got, tokens, gains, biases, out_part, query_part, lanes, width):
    def body(ins, loaded, outs, _):
        got_ref, tokens_ref, gains_ref, biases_ref = ins
        low_ref, normed_ref, scale_ref, hidden_ref, blocks_ref = outs
        attended = read_blocks(got_ref, lanes, 0, width)
        low_ref[...] = attended
        resid = tokens_ref[...].astype(jnp.float32) + dot(attended, loaded[0].value())
        normed, scale = normalize(resid)
        normed_ref[...] = normed
        scale_ref[...] = scale
        hidden = (normed * gains_ref[0:1] + biases_ref[0:1]).astype(jnp.bfloat16)
        hidden_ref[...] = hidden
        query = dot(hidden, loaded[1].value()).astype(jnp.bfloat16)
        write_blocks(blocks_ref, query, lanes, 0, width)

    rows = tokens.shape[0]
    return call_with_parts(
        body,
        [got, tokens, gains, biases],
        [out_part, query_part],
        [
            shape(rows, WIDTH, of=jnp.bfloat16),
            shape(rows, WIDTH),
            shape(rows, 1),
            shape(rows, WIDTH, of=jnp.bfloat16),
            shape(*got.shape, of=jnp.bfloat16),
        ],
        "after_self",
    )


def feed_forward(got, normed_in, cotangent, gains, biases, out_part, in_parts, down, outs, up, lanes, width):
    pieces = len(in_parts)
    step = in_parts[0].width

    def body(ins, loaded, refs, scratch):
        got_ref, normed_in_ref, cot_ref, gains_ref, biases_ref = ins
        (
            output_ref,
            low_ref,
            mixed_ref,
            adapted_ref,
            dunder_ref,
            dab_ref,
            dcb_ref,
            dresid_ref,
            blocks_ref,
            norms_ref,
        ) = refs
        (slopes,) = scratch
        w_out, w_in = loaded[0], loaded[1 : 1 + pieces]
        w_down, w_ff, w_up = loaded[1 + pieces :]
        attended = read_blocks(got_ref, lanes, 0, width)
        low_ref[...] = attended
        hidden = normed_in_ref[...] * gains_ref[0:1] + biases_ref[0:1]
        normed_one, scale_one = normalize(hidden + dot(attended, w_out.value()))
        mixed = normed_one * gains_ref[1:2] + biases_ref[1:2]
        mixed_low = mixed.astype(jnp.bfloat16)
        mixed_ref[...] = mixed_low
        summed = mixed
        under = dot(mixed_low, w_down.value())
        gate = 1.0 / (1.0 + jnp.exp(-under))
        adapted = (under * gate).astype(jnp.bfloat16)
        adapted_ref[...] = adapted
        under_slope = gate * (1.0 + under * (1.0 - gate))
        summed = summed + 4.0 * dot(adapted, w_up.value())
        for piece in range(pieces):
            before = dot(mixed_low, w_in[piece].value())
            below = 0.5 + 0.5 * lax.erf(before * (0.5**0.5))
            slopes[piece] = below + before * jnp.exp(-0.5 * before * before) * (
                (2.0 * math.pi) ** -0.5
            )
            act = (before * below).astype(jnp.bfloat16)
            summed = summed + dot(act, w_ff[piece].value())
        normed_two, scale_two = normalize(summed)
        output_ref[...] = (normed_two * gains_ref[2:3] + biases_ref[2:3]).astype(jnp.bfloat16)
        upstream = cot_ref[...].astype(jnp.float32)
        norms_ref[0:1] = jnp.sum(upstream * normed_two, axis=0, keepdims=True)
        norms_ref[1:2] = jnp.sum(upstream, axis=0, keepdims=True)
        dz = norm_back(upstream, normed_two, scale_two, gains_ref[2:3])
        dzb = dz.astype(jnp.bfloat16)
        dab = (4.0 * dz).astype(jnp.bfloat16)
        dab_ref[...] = dab
        dunder = (under_slope * dot_back(dab, w_up.value())).astype(jnp.bfloat16)
        dunder_ref[...] = dunder
        dmixed = dz + dot_back(dunder, w_down.value())
        for piece in range(pieces):
            dpre = (slopes[piece] * dot_back(dzb, w_ff[piece].value())).astype(jnp.bfloat16)
            dmixed = dmixed + dot_back(dpre, w_in[piece].value())
        norms_ref[2:3] = jnp.sum(dmixed * normed_one, axis=0, keepdims=True)
        norms_ref[3:4] = jnp.sum(dmixed, axis=0, keepdims=True)
        dresid = norm_back(dmixed, normed_one, scale_one, gains_ref[1:2])
        dresid_ref[...] = dresid
        dcb = dresid.astype(jnp.bfloat16)
        dcb_ref[...] = dcb
        write_blocks(
            blocks_ref, dot_back(dcb, w_out.value()).astype(jnp.bfloat16), lanes, 0, width
        )

    rows = normed_in.shape[0]
    low = jnp.bfloat16

    def body_rows(ins, loaded, refs, scratch):
        whole_ff = loaded[2 + pieces]

        class Rows:
            def __init__(self, piece):
                self.piece = piece

            def value(self):
                return whole_ff.value()[self.piece * step : (self.piece + 1) * step]

        loaded = loaded[: 2 + pieces] + [[Rows(piece) for piece in range(pieces)], loaded[-1]]
        body(ins, loaded, refs, scratch)

    return call_with_parts(
        body_rows,
        [got, normed_in, cotangent, gains, biases],
        [out_part] + in_parts + [down, outs, up],
        [
            shape(rows, WIDTH, of=low),
            shape(rows, WIDTH, of=low),
            shape(rows, WIDTH, of=low),
            shape(rows, down.width, of=low),
            shape(rows, down.width, of=low),
            shape(rows, WIDTH, of=low),
            shape(rows, WIDTH, of=low),
            shape(rows, WIDTH),
            shape(*got.shape, of=low),
            shape(4, WIDTH),
        ],
        "feed_forward",
        [pltpu.VMEM((pieces, rows, step), jnp.float32)],
        20,
    )


def before_self(got, dresid, normed, scale, gains, query_part, out_part, lanes, width):
    def body(ins, loaded, outs, _):
        got_ref, dresid_ref, normed_ref, scale_ref, gains_ref = ins
        dcq_ref, dr_ref, dsb_ref, blocks_ref, norms_ref = outs
        dcq = read_blocks(got_ref, lanes, 0, width)
        dcq_ref[...] = dcq
        dhidden = dresid_ref[...] + dot_back(dcq, loaded[0].value())
        normed = normed_ref[...]
        norms_ref[0:1] = jnp.sum(dhidden * normed, axis=0, keepdims=True)
        norms_ref[1:2] = jnp.sum(dhidden, axis=0, keepdims=True)
        dr = norm_back(dhidden, normed, scale_ref[...], gains_ref[0:1])
        dr_ref[...] = dr
        dsb = dr.astype(jnp.bfloat16)
        dsb_ref[...] = dsb
        grad = dot_back(dsb, loaded[1].value()).astype(jnp.bfloat16)
        write_blocks(blocks_ref, grad, lanes, 0, width)

    rows = dresid.shape[0]
    return call_with_parts(
        body,
        [got, dresid, normed, scale, gains],
        [query_part, out_part],
        [
            shape(rows, WIDTH, of=jnp.bfloat16),
            shape(rows, WIDTH),
            shape(rows, WIDTH, of=jnp.bfloat16),
            shape(*got.shape, of=jnp.bfloat16),
            shape(2, WIDTH),
        ],
        "before_self",
    )


def input_grad(got, start, parts, lanes, span, width, name):
    def body(ins, loaded, outs, _):
        total = None
        for kind, weight in enumerate(loaded):
            values = read_blocks(ins[0], lanes, kind, width)
            term = dot_back(values, weight.value())
            total = term if total is None else total + term
        outs[0][...] = total if len(ins) == 1 else total + ins[1][...]

    rows = span * lanes
    return call_with_parts(
        body,
        [got] if start is None else [got, start],
        parts,
        [shape(rows, WIDTH)],
        name,
    )


def sum_everywhere(values, stages):
    if not paired():
        return lax.psum(values, ("dp", "blk"))
    values = after(values, stages[0])
    values = values + swap_core(values)
    for step, bit in enumerate((1, 2, 4, 8)):
        if step + 1 < len(stages):
            values = after(values, stages[step + 1])
        values = values + flip(values, bit)
    return values


def shards(
    tokens,
    encoder,
    cotangent,
    self_in,
    self_out,
    cross_q,
    cross_kv,
    cross_out,
    ffn_in,
    ffn_out,
    adapt_down,
    adapt_up,
    norm_gain,
    norm_bias,
    tgt_lengths,
    src_lengths,
):
    lanes, span, _ = tokens.shape
    rows = lanes * span
    width = WIDTH * lanes // lax.axis_size("blk")
    own_row = lax.axis_index("blk") // (lax.axis_size("blk") // lanes)
    tgt_ends = jnp.cumsum(lax.dynamic_index_in_dim(tgt_lengths, own_row, 0, keepdims=False))
    src_ends = jnp.cumsum(lax.dynamic_index_in_dim(src_lengths, own_row, 0, keepdims=False))
    flat_tokens = tokens.reshape(rows, WIDTH)
    flat_encoder = encoder.reshape(rows, WIDTH)
    frozen = [ffn_in, adapt_down, ffn_out, adapt_up, cross_out]
    inward = [self_in, cross_kv]

    if paired():
        packed = gather_packed(pack_halves(frozen))
        token_row, stages = gather_row(tokens)
        self_heads, pair_heads = head_columns(after(inward, stages[1]), [3, 2])
        out_shard, query_shard = after((self_out, cross_q), stages[1])
        encoder_block = after(encoder, stages[1])
        self_qkv = project_row(token_row, self_heads, "self_in")
        out_source, query_source = gather_flips([out_shard, query_shard], "xy", self_qkv)
        encoder_row, encoder_stages = gather_row(
            encoder_block, self_qkv, (out_source.arrays[1], query_source.arrays[1])
        )
        self_qkv = after(self_qkv, out_source.stages[0], query_source.stages[0])
        pair_own = project_row(encoder_row, pair_heads, "cross_kv")
    else:
        (self_source, pair_source, out_source, query_source) = gather_flips(
            [self_in, cross_kv, self_out, cross_q], "xyxy"
        )
        self_parts = [columns_of((self_source, WIDTH * kind, WIDTH)) for kind in range(3)]
        pair_parts = [columns_of((pair_source, WIDTH * kind, WIDTH)) for kind in range(2)]
        self_qkv = as_rows(
            exchange(project_blocks(flat_tokens, self_parts, lanes, width, "self_in"))
        )
        pair_own = as_rows(
            exchange(project_blocks(flat_encoder, pair_parts, lanes, width, "cross_kv"))
        )
    self_out_part = columns_of((out_source, 0, WIDTH))
    query_part = columns_of((query_source, 0, WIDTH))

    self_mid, self_full, self_lse = attn_forward(
        tgt_ends, tgt_ends, self_qkv, self_qkv, width, True
    )
    self_sent = after(self_mid, out_source.stages[1], query_source.stages[1])
    if paired():
        self_sent = after(self_sent, encoder_stages[0])
    self_back = exchange(as_blocks(self_sent))
    if paired():
        self_back = after(self_back, encoder_stages[1])
    self_low, normed, scale, hidden_low, query_blocks = after_self(
        self_back,
        flat_tokens,
        norm_gain,
        norm_bias,
        self_out_part,
        query_part,
        lanes,
        width,
    )
    cross_own = as_rows(exchange(query_blocks))
    cross_mid, cross_full, cross_lse = attn_forward(
        tgt_ends, src_ends, cross_own, pair_own, width, False
    )
    cross_back = exchange(as_blocks(cross_mid))
    ready = after(packed, cross_mid) if paired() else None
    ff_parts, down_parts, ffo_parts, up_parts, (cross_out_part,) = packed_parts(frozen, ready)
    (
        output,
        cross_low,
        mixed_low,
        adapter_low,
        grad_under,
        adapt_low,
        cross_branch_low,
        grad_resid_two,
        cross_grad_blocks,
        norms_high,
    ) = feed_forward(
        cross_back,
        normed,
        cotangent.reshape(rows, WIDTH),
        norm_gain,
        norm_bias,
        cross_out_part,
        ff_parts,
        down_parts[0],
        ffo_parts[0],
        up_parts[0],
        lanes,
        width,
    )
    high_groups = [
        [(cross_low, cross_branch_low)],
        [(mixed_low, grad_under), (adapter_low, adapt_low)],
    ]
    high_terms = [grad_terms(pairs) for pairs in high_groups]
    high_orders = [(2, 1, 4, 8), (1, 2, 4, 8)]
    high_terms, high_stages = scatter_chips(high_terms, high_orders, 0, 2)
    cross_dq, cross_dkv = attn_backward(
        tgt_ends,
        src_ends,
        cross_own,
        pair_own,
        as_rows(after(exchange(cross_grad_blocks), high_stages[0])),
        cross_full,
        cross_lse,
        False,
    )
    cq_low, grad_resid_one, self_branch_low, self_grad_blocks, norms_low = before_self(
        after(exchange(as_blocks(cross_dq)), high_stages[1]),
        grad_resid_two,
        normed,
        scale,
        norm_gain,
        query_part,
        self_out_part,
        lanes,
        width,
    )
    mid_groups = [[(hidden_low, cq_low)], [(self_low, self_branch_low)]]
    mid_terms, mid_stages = scatter_chips(
        [grad_terms(pairs) for pairs in mid_groups], [(2, 1, 4, 8), (1, 2, 4, 8)], 0, 4
    )
    (grad_cross_q,), (grad_self_out,) = finish_terms(mid_groups, mid_terms)
    self_upstream = after(exchange(self_grad_blocks), high_stages[2])
    if paired():
        dkv_late = after(cross_dkv, self_grad_blocks)
        pair_terms = row_back(dkv_late, pair_heads, "encoder_grad")
        encoder_grad, encoder_stages = reduce_row(pair_terms)
        encoder_grad = encoder_grad.reshape(rows, WIDTH)
        self_upstream = after(self_upstream, pair_terms)
    (self_grads,) = attn_backward(
        tgt_ends,
        tgt_ends,
        self_qkv,
        self_qkv,
        as_rows(self_upstream),
        self_full,
        self_lse,
        True,
        joined=True,
    )
    high_terms, _ = scatter_chips(after(high_terms, self_grads), high_orders, 2, 4)
    (high_grads, adapt_grads) = finish_terms(high_groups, high_terms)
    (grad_cross_out,), (grad_adapt_down, grad_adapt_up) = high_grads, adapt_grads
    if paired():
        self_terms = row_back(self_grads, self_heads, "tokens_grad")
        self_back_sum, _ = reduce_row(self_terms)
        tokens_grad = grad_resid_one + self_back_sum.reshape(rows, WIDTH)
        sent = [
            row_grad(token_row, after(self_grads, self_terms), "self_in_grad"),
            row_grad(encoder_row, dkv_late, "cross_kv_grad"),
        ]
        grads_got = exchange(
            after(jnp.concatenate(sent, axis=2), encoder_stages[1], mid_stages[1])
        )
        grad_self_in = finish_row_grad(grads_got[:, :, : 3 * width], 3)
        grad_cross_kv = finish_row_grad(grads_got[:, :, 3 * width :], 2)
    else:
        pair_got = exchange(as_blocks(cross_dkv))
        self_got = exchange(as_blocks(self_grads))
        (encoder_grad,) = input_grad(
            pair_got, None, pair_parts, lanes, span, width, "encoder_grad"
        )
        (tokens_grad,) = input_grad(
            self_got, grad_resid_one, self_parts, lanes, span, width, "tokens_grad"
        )
        pair_low = pair_got.reshape(lanes, -1, span, 2, width).transpose(0, 2, 3, 1, 4)
        self_low_grads = self_got.reshape(lanes, -1, span, 3, width).transpose(0, 2, 3, 1, 4)
        grad_cross_kv = weight_grad(flat_encoder, pair_low.reshape(rows, 2 * WIDTH))
        grad_self_in = weight_grad(flat_tokens, self_low_grads.reshape(rows, 3 * WIDTH))
    norms = sum_everywhere(jnp.concatenate([norms_low, norms_high], axis=0), mid_stages)
    return (
        output.reshape(lanes, span, WIDTH),
        tokens_grad.reshape(lanes, span, WIDTH),
        encoder_grad.reshape(lanes, span, WIDTH),
        grad_self_in,
        grad_self_out,
        grad_cross_q,
        grad_cross_kv,
        grad_cross_out,
        grad_adapt_down,
        grad_adapt_up,
        jnp.stack([norms[0], norms[4], norms[2]]),
        jnp.stack([norms[1], norms[5], norms[3]]),
    )


def solution(mesh):
    placed = (
        P("dp", "blk", None),
        P("dp", "blk", None),
        P("dp", "blk", None),
        P("blk", None),
        P("blk", None),
        P("blk", None),
        P("blk", None),
        P("blk", None),
        P("blk", None),
        P("blk", None),
        P("blk", None),
        P("blk", None),
        P(),
        P(),
        P("dp", None),
        P("dp", None),
    )
    return jax.shard_map(
        shards,
        mesh=mesh,
        in_specs=placed,
        out_specs=(
            P("dp", "blk", None),
            P("dp", "blk", None),
            P("dp", "blk", None),
            P("blk", None),
            P("blk", None),
            P("blk", None),
            P("blk", None),
            P("blk", None),
            P("blk", None),
            P("blk", None),
            P(),
            P(),
        ),
        check_vma=False,
    )
```

```python
import functools
import math

import jax
import jax.numpy as jnp
from jax import lax
from jax.experimental import pallas as pl
from jax.experimental.pallas import tpu as pltpu
from jax.sharding import PartitionSpec as P

HEADS = 16
HEAD_DIM = 64
WIDTH = HEADS * HEAD_DIM


NEG = -1e30
VMEM_BYTES = 56 * 1024 * 1024


def cost(microseconds):
    return pl.CostEstimate(
        flops=int(microseconds * 0.4e9),
        bytes_accessed=int(microseconds * 1.2e6),
        transcendentals=0,
    )


def paired():
    return lax.axis_size("blk") == 16 and lax.axis_size("dp") == 2


def swap_core(block):
    cores = lax.axis_size("dp")
    return lax.ppermute(block, "dp", [(i ^ 1, i) for i in range(cores)])


def flip(block, bit):
    chips = lax.axis_size("blk")
    return lax.ppermute(block, "blk", [(i ^ bit, i) for i in range(chips)])


FLIPS = (8, 4, 2, 1)


def with_flip(block, bit):
    return jnp.stack([block, flip(block, bit)])


def own_half(values, which):
    half = values.shape[1] // 2
    return lax.dynamic_slice_in_dim(values, which * half, half, 1)


def scatter_chips(terms, orders, first, last, holds=None):
    if not paired():
        return terms, [terms] * 5
    own = lax.axis_index("blk")

    def fold(blocks, left, bit):
        axis, place = left.index(bit), (own // bit) % 2
        kept = lax.dynamic_index_in_dim(blocks, place, axis, keepdims=False)
        sent = lax.dynamic_index_in_dim(blocks, 1 - place, axis, keepdims=False)
        got = flip(sent, bit)
        return (kept.astype(jnp.float32) + got.astype(jnp.float32)).astype(jnp.bfloat16)

    if first == 0:
        terms = [blocks.reshape(2, 2, 2, 2, *blocks.shape[1:]) for blocks in terms]
    stages = [terms[0]]
    for stage in range(first, last):
        if holds and stage in holds:
            terms = after(terms, holds[stage])
        terms = [
            fold(blocks, [bit for bit in FLIPS if bit not in order[:stage]], order[stage])
            for blocks, order in zip(terms, orders)
        ]
        stages.append(terms[0])
    return terms, stages


CHUNK = 256


def grad_terms(pairs):
    if not paired():
        return pairs[0][1]
    core = lax.axis_index("dp")
    packed = []
    for inputs, upstream in pairs:
        both = jnp.concatenate([inputs, swap_core(inputs)], axis=0)
        half = jnp.concatenate(
            [own_half(upstream, core), swap_core(own_half(upstream, 1 - core))], axis=0
        )
        term = lax.dot_general(
            both, half, (((0,), (0,)), ((), ())), preferred_element_type=jnp.float32
        ).astype(jnp.bfloat16)
        rows = term.shape[0] // 16
        chunks = term.shape[1] // CHUNK
        packed += [
            term[:, c * CHUNK : (c + 1) * CHUNK].reshape(16, rows, CHUNK) for c in range(chunks)
        ]
    return jnp.concatenate(packed, axis=1)


def finish_terms(groups, terms):
    if not paired():
        return [[weight_grad(inputs, upstream) for inputs, upstream in pairs] for pairs in groups]
    core = lax.axis_index("dp")
    mine = jnp.concatenate(terms, axis=0)
    other = swap_core(mine)
    low = jnp.where(core == 0, mine, other).astype(jnp.float32)
    high = jnp.where(core == 0, other, mine).astype(jnp.float32)
    found, place = [], 0
    for pairs in groups:
        found.append([])
        for inputs, upstream in pairs:
            rows = inputs.shape[1] // 16
            chunks = upstream.shape[1] // 2 // CHUNK
            spots = [slice(place + c * rows, place + (c + 1) * rows) for c in range(chunks)]
            found[-1].append(
                jnp.concatenate(
                    [low[spot] for spot in spots] + [high[spot] for spot in spots], axis=1
                )
            )
            place += rows * chunks
    return found


def weight_grad(inputs, upstream):
    scattered = lax.psum_scatter(
        lax.dot_general(
            inputs, upstream, (((0,), (0,)), ((), ())), preferred_element_type=jnp.float32
        ).astype(jnp.bfloat16),
        "blk",
        scatter_dimension=0,
        tiled=True,
    )
    return lax.psum(scattered, "dp").astype(jnp.float32)


class Source:
    def __init__(self, kind, arrays, first_flip="x", column=None):
        self.kind, self.arrays, self.first_flip = kind, arrays, first_flip
        self.stages = arrays[:1] * 3 if column is None else [column] + arrays[:2]


class Part:
    def __init__(self, rows, width, spots):
        self.rows, self.width, self.spots = rows, width, spots

    def scratch(self):
        return pltpu.VMEM((2, 2, 2, 2, 2, self.rows // 32, self.width), jnp.bfloat16)

    def start(self, refs_of, place, dst, sem):
        z1, z0, y, x, core = [place[axis] for axis in range(5)]
        high = self.rows // 32
        for source, first_row, first_col, at_col, width in self.spots:
            refs = refs_of(source)
            cols = slice(first_col, first_col + width)
            into = slice(at_col, at_col + width)
            if source.kind == "whole":
                pltpu.make_async_copy(
                    refs[0].at[:, :, :, :, :, :, cols], dst.at[:, :, :, :, :, :, into], sem
                ).start()
            elif source.kind == "cores":
                for which in range(2):
                    owner = core if which == 0 else 1 - core
                    pltpu.make_async_copy(
                        refs[which].at[:, :, :, :, first_row : first_row + high, cols],
                        dst.at[:, :, :, :, owner, :, into],
                        sem,
                    ).start()
            else:
                for which in range(4):
                    owner = core if which < 2 else 1 - core
                    for near, at_y, at_x in flipped(source.first_flip, which % 2, y, x):
                        for up, at_z1, at_z0 in four(z1, z0):
                            pltpu.make_async_copy(
                                refs[which].at[near, up[0], up[1], :, cols],
                                dst.at[at_z1, at_z0, at_y, at_x, owner, :, into],
                                sem,
                            ).start()


def four(z1, z0):
    return [
        ((low, high), z1 if high == 0 else 1 - z1, z0 if low == 0 else 1 - z0)
        for low in range(2)
        for high in range(2)
    ]


def flipped(first_flip, beyond, y, x):
    found = []
    for near in range(2):
        a, b = (near, beyond) if first_flip == "x" else (beyond, near)
        found.append((near, y if b == 0 else 1 - y, x if a == 0 else 1 - x))
    return found


def after(value, *others):
    return lax.optimization_barrier((value, *others))[0]


def gather_flips(shards, first_flips, hold=None):
    if not paired():
        full = [lax.all_gather(shard, "blk", axis=0, tiled=True) for shard in shards]
        return [
            Source("whole", [array.reshape(2, 2, 2, 2, 2, array.shape[0] // 32, array.shape[1])])
            for array in full
        ]
    core = lax.axis_index("dp")
    columns = []
    for shard in shards:
        rows = shard.shape[0]
        own = lax.dynamic_slice_in_dim(shard, core * (rows // 2), rows // 2, 0)
        columns.append(with_flip(with_flip(own, 8), 4))
    sources, bits = [], {"x": (1, 2), "y": (2, 1)}
    if hold is not None:
        columns = after(columns, hold)
    planes = [
        with_flip(column, bits[first][0]) for column, first in zip(columns, first_flips)
    ]
    for column, plane, first in zip(columns, planes, first_flips):
        beyond = flip(plane, bits[first][1])
        sources.append(
            Source("flips", [plane, beyond, swap_core(plane), swap_core(beyond)], first, column)
        )
    return sources


class RowPart:
    def __init__(self, sources, span):
        self.span = span
        self.rows, self.width = 16 * span, WIDTH
        self.spots = [(source,) for source in sources]

    def scratch(self):
        return pltpu.VMEM((2, 2, 2, 2, self.span, WIDTH), jnp.bfloat16)

    def start(self, refs_of, place, dst, sem):
        z1, z0, y, x = [place[axis] for axis in range(4)]
        half = WIDTH // 2
        for side, (source,) in enumerate(self.spots):
            refs = refs_of(source)
            for beyond in range(2):
                for near, at_y, at_x in flipped(source.first_flip, beyond, y, x):
                    for up, at_z1, at_z0 in four(z1, z0):
                        pltpu.make_async_copy(
                            refs[beyond].at[near, up[0], up[1]],
                            dst.at[at_z1, at_z0, at_y, at_x, :, side * half : (side + 1) * half],
                            sem,
                        ).start()


def gather_row(block, hold_near=None, hold=None):
    row = lax.axis_index("blk") // 8
    own = lax.dynamic_index_in_dim(block, row, 0, keepdims=False)
    other = lax.dynamic_index_in_dim(block, 1 - row, 0, keepdims=False)
    pair = jnp.stack([own, flip(other, 8)])
    if hold_near is not None:
        pair = after(pair, hold_near)
    column = with_flip(pair, 4)
    stages, sources = [pair, column], []
    if hold is not None:
        column = after(column, hold)
    half = WIDTH // 2
    planes = [with_flip(column[..., :half], 1), with_flip(column[..., half:], 2)]
    for plane, first, bit in zip(planes, "xy", (2, 1)):
        sources.append(Source("row", [plane, flip(plane, bit)], first))
    stages += [planes, [source.arrays[1] for source in sources]]
    return RowPart(sources, block.shape[1]), stages


def head_columns(shards, kinds):
    core = lax.axis_index("dp")
    blocks, widths = [], [128 * kind for kind in kinds]
    for shard, kind in zip(shards, kinds):
        own = lax.dynamic_slice_in_dim(shard, core * 32, 32, 0)
        own = own.reshape(32, kind, 8, 128).transpose(2, 0, 1, 3)
        blocks.append(own.reshape(8, 32, kind * 128))
    blocks = jnp.concatenate(blocks, axis=2)
    mine = exchange(jnp.concatenate([blocks, blocks], axis=0))
    mine = mine.reshape(2, 2, 2, 2, 32, sum(widths))
    source = Source("cores", [mine, swap_core(mine)])
    parts, place = [], 0
    for width in widths:
        parts.append(Part(1024, width, [(source, 0, place, 0, width)]))
        place += width
    return parts


def project_row(row_part, head_part, name):
    def body(ins, loaded, outs, _):
        weight = loaded[1].value()
        inputs = loaded[0].value()
        for first in range(0, row_part.rows, 256):
            rows = slice(first, first + 256)
            outs[0][rows, :] = dot(inputs[rows], weight).astype(jnp.bfloat16)

    (found,) = call_with_parts(
        body,
        [],
        [row_part, head_part],
        [shape(row_part.rows, head_part.width, of=jnp.bfloat16)],
        name,
    )
    return found


def row_grad(row_part, upstream, name):
    columns = upstream.shape[1]

    def body(ins, loaded, outs, _):
        core = ins[1][0]
        inputs = loaded[0].value()
        grads = []
        for first in range(0, columns, 128):
            grads.append(pair_dot(ins[0][:, first : first + 128], inputs, 0, 0).T)
        grad = jnp.concatenate(grads, axis=1).astype(jnp.bfloat16).reshape(16, 2, 32, columns)
        outs[0][core] = grad[:, 0]
        outs[0][1 - core] = grad[:, 1]

    (terms,) = call_with_parts(
        body,
        [upstream],
        [row_part],
        [shape(2, 16, 32, columns, of=jnp.bfloat16)],
        name,
        scalars=[lax.axis_index("dp").reshape(1).astype(jnp.int32)],
    )
    got = swap_core(terms[1])
    return (terms[0].astype(jnp.float32) + got.astype(jnp.float32)).astype(jnp.bfloat16)


def row_back(upstream, head_part, name):
    def body(ins, loaded, outs, _):
        weight = loaded[0].value()
        for first in range(0, ins[0].shape[0], 256):
            rows = slice(first, first + 256)
            outs[0][rows, :] = dot_back(ins[0][rows, :], weight).astype(jnp.bfloat16)

    (terms,) = call_with_parts(
        body, [upstream], [head_part], [shape(upstream.shape[0], WIDTH, of=jnp.bfloat16)], name
    )
    return terms


def reduce_row(terms, holds=None):
    blocks = terms.reshape(16, terms.shape[0] // 16, WIDTH)
    half = WIDTH // 2
    halves, stages = scatter_chips(
        [blocks[..., :half], blocks[..., half:]], [(1, 2, 4, 8), (2, 1, 4, 8)], 0, 3, holds
    )
    both = jnp.concatenate(halves, axis=2)
    row = lax.axis_index("blk") // 8
    kept = lax.dynamic_index_in_dim(both, row, 0, keepdims=False)
    got = flip(lax.dynamic_index_in_dim(both, 1 - row, 0, keepdims=False), 8)
    found = jnp.stack([jnp.where(row == 0, kept, got), jnp.where(row == 0, got, kept)])
    return found.astype(jnp.float32), stages


def finish_row_grad(got, kinds):
    total = jnp.sum(got.reshape(2, 8, 32, kinds, 128).astype(jnp.float32), axis=0)
    mine = total.astype(jnp.bfloat16).transpose(1, 2, 0, 3).reshape(32, kinds * WIDTH)
    other = swap_core(mine)
    core = lax.axis_index("dp")
    low = jnp.where(core == 0, mine, other)
    high = jnp.where(core == 0, other, mine)
    return jnp.concatenate([low, high], axis=0).astype(jnp.float32)


def columns_of(*pieces):
    spots, place = [], 0
    for source, first, width in pieces:
        spots.append((source, 0, first, place, width))
        place += width
    return Part(1024, place, spots)


PACK = 512


def pack_halves(shards):
    places = [
        (index, shard.shape[0] // 2, first)
        for index, shard in enumerate(shards)
        for first in range(0, shard.shape[1], PACK)
    ]

    def body(core, *refs):
        out_ref, place = refs[-1], 0
        for index, high, first in places:
            start = pl.multiple_of(core[0] * high, 16)
            out_ref[place : place + high, :] = refs[index][pl.ds(start, high), first : first + PACK]
            place += high

    return pl.pallas_call(
        body,
        out_shape=shape(sum(high for _, high, _ in places), PACK, of=jnp.bfloat16),
        in_specs=[smem_spec()] + [vmem_spec()] * len(shards),
        out_specs=vmem_spec(),
        compiler_params=pltpu.CompilerParams(vmem_limit_bytes=VMEM_BYTES),
        cost_estimate=cost(2),
        name="pack_halves",
    )(lax.axis_index("dp").reshape(1).astype(jnp.int32), *shards)


def gather_packed(packed):
    return lax.all_gather(packed, "blk", axis=0)


def packed_parts(shards, mine):
    if not paired():
        found = []
        for source, shard in zip(gather_flips(shards, "x" * len(shards)), shards):
            rows, columns = 32 * source.arrays[0].shape[5], shard.shape[1]
            step = min(columns, 1024)
            found.append(
                [
                    Part(rows, step, [(source, 0, first, 0, step)])
                    for first in range(0, columns, step)
                ]
            )
        return found
    spots, place = [], 0
    for shard in shards:
        high = shard.shape[0] // 2
        places = []
        for first in range(0, shard.shape[1], PACK):
            places.append(place)
            place += high
        spots.append((shard.shape[0] * 16, places))
    mine = mine.reshape(2, 2, 2, 2, place, PACK)
    source = Source("cores", [mine, swap_core(mine)])
    found = []
    for rows, places in spots:
        parts = []
        for first in range(0, len(places), 2):
            two = places[first : first + 2]
            parts.append(
                Part(
                    rows,
                    PACK * len(two),
                    [(source, row, 0, PACK * side, PACK) for side, row in enumerate(two)],
                )
            )
        found.append(parts)
    return found


def place_now():
    own, core = lax.axis_index("blk"), lax.axis_index("dp")
    bits = [(own // bit) % 2 for bit in FLIPS]
    return jnp.stack(bits + [core]).astype(jnp.int32)


class Loaded:
    def __init__(self, part, dst, sem):
        self.part, self.dst, self.sem, self.here = part, dst, sem, False

    def value(self):
        if not self.here:
            pltpu.make_async_copy(self.dst, self.dst, self.sem).wait()
            self.here = True
        return self.dst[...].reshape(self.part.rows, self.part.width)


def call_with_parts(body, inputs, parts, outputs, name, scratch=(), takes=5, scalars=()):
    sources = []
    for part in parts:
        sources += [spot[0] for spot in part.spots if spot[0] not in sources]
    arrays = [array for source in sources for array in source.arrays]

    def kernel(place, *refs):
        refs = list(refs)
        ins = [refs.pop(0) for _ in (*inputs, *scalars)]
        pieces = [[refs.pop(0) for _ in source.arrays] for source in sources]
        outs = [refs.pop(0) for _ in outputs]
        dsts = [refs.pop(0) for _ in parts]
        sems = refs.pop(0)
        loaded = []
        for index, part in enumerate(parts):
            part.start(
                lambda source: pieces[sources.index(source)], place, dsts[index], sems.at[index]
            )
            loaded.append(Loaded(part, dsts[index], sems.at[index]))
        body(ins, loaded, outs, refs)

    return pl.pallas_call(
        kernel,
        out_shape=tuple(outputs),
        in_specs=[smem_spec()]
        + [vmem_spec()] * len(inputs)
        + [smem_spec()] * len(scalars)
        + [pl.BlockSpec(memory_space=pl.ANY)] * len(arrays),
        out_specs=(vmem_spec(),) * len(outputs),
        scratch_shapes=[part.scratch() for part in parts]
        + [pltpu.SemaphoreType.DMA((len(parts),))]
        + list(scratch),
        compiler_params=pltpu.CompilerParams(vmem_limit_bytes=VMEM_BYTES),
        cost_estimate=cost(takes),
        name=name,
    )(place_now(), *inputs, *scalars, *arrays)


def vmem_spec():
    return pl.BlockSpec(memory_space=pltpu.VMEM)


def smem_spec():
    return pl.BlockSpec(memory_space=pltpu.SMEM)


def seg_of_pos(ends_ref, pos):
    seg = jnp.zeros(pos.shape, jnp.int32)
    for slot in range(ends_ref.shape[0]):
        seg = seg + (ends_ref[slot] <= pos).astype(jnp.int32)
    return seg


def pair_dot(left, right, left_dim, right_dim):
    return lax.dot_general(
        left, right, (((left_dim,), (right_dim,)), ((), ())), preferred_element_type=jnp.float32
    )


def seg_tables(q_ends, k_ends, span):
    seg_q = seg_of_pos(q_ends, lax.broadcasted_iota(jnp.int32, (1, span), 1))
    seg_k = seg_of_pos(k_ends, lax.broadcasted_iota(jnp.int32, (span, 1), 0))
    return seg_q, seg_k


def masked_scores(keys, queries, seg_q, seg_k, first, causal):
    scores = pair_dot(keys, queries, 1, 1)
    allowed = seg_k == seg_q
    if causal:
        key_pos = lax.broadcasted_iota(jnp.int32, scores.shape, 0)
        query_pos = first + lax.broadcasted_iota(jnp.int32, scores.shape, 1)
        allowed = allowed & (key_pos <= query_pos)
    return jnp.where(allowed, scores, NEG)


def attn_forward_body(causal, width, q_ends, k_ends, q_ref, kv_ref, low_ref, full_ref, lse_ref):
    span = q_ref.shape[0]
    step = math.gcd(span, 256)
    heads = width // HEAD_DIM
    seg_q, seg_k = seg_tables(q_ends, k_ends, span)
    key_at = kv_ref.shape[1] - 2 * width
    scaled = q_ref[:, :width] * jnp.bfloat16(HEAD_DIM ** (-0.5))
    keys = kv_ref[:, key_at : key_at + width]
    values = kv_ref[:, key_at + width : key_at + 2 * width]
    for first in range(0, span, step):
        reach = first + step if causal else span
        parts = []
        for head in range(heads):
            cols = slice(head * HEAD_DIM, (head + 1) * HEAD_DIM)
            scores = masked_scores(
                keys[:reach, cols],
                scaled[first : first + step, cols],
                seg_q[:, first : first + step],
                seg_k[:reach],
                first,
                causal,
            )
            top = jnp.max(scores, axis=0, keepdims=True)
            probs = jnp.exp(scores - top)
            total = jnp.sum(probs, axis=0, keepdims=True)
            mixed = pair_dot(values[:reach, cols], probs.astype(jnp.bfloat16), 0, 0)
            parts.append(mixed / total)
            lse_ref[head : head + 1, first : first + step] = top + jnp.log(total)
        joined = jnp.concatenate(parts, axis=0).T
        full_ref[first : first + step, :] = joined
        low_ref[first : first + step, :] = joined.astype(jnp.bfloat16)


def attn_forward(q_ends, k_ends, queries, keys_values, width, causal):
    span = queries.shape[0]
    return pl.pallas_call(
        functools.partial(attn_forward_body, causal, width),
        out_shape=(
            jax.ShapeDtypeStruct((span, width), jnp.bfloat16),
            jax.ShapeDtypeStruct((span, width), jnp.float32),
            jax.ShapeDtypeStruct((width // HEAD_DIM, span), jnp.float32),
        ),
        in_specs=[smem_spec(), smem_spec()] + [vmem_spec()] * 2,
        out_specs=(vmem_spec(),) * 3,
        compiler_params=pltpu.CompilerParams(vmem_limit_bytes=VMEM_BYTES),
        cost_estimate=cost(8),
        name="attn_forward",
    )(q_ends, k_ends, queries, keys_values)


def attn_backward_body(
    causal,
    width,
    q_ends,
    k_ends,
    q_ref,
    kv_ref,
    up_ref,
    full_ref,
    lse_ref,
    *outs,
):
    dq_ref, dkv_ref = outs[0], outs[-3]
    dk_sum, dv_sum = outs[-2:]
    span = q_ref.shape[0]
    step = math.gcd(span, 256)
    heads = width // HEAD_DIM
    seg_q, seg_k = seg_tables(q_ends, k_ends, span)
    key_at = kv_ref.shape[1] - 2 * width
    scaled = q_ref[:, :width] * jnp.bfloat16(HEAD_DIM ** (-0.5))
    keys = kv_ref[:, key_at : key_at + width]
    values = kv_ref[:, key_at + width : key_at + 2 * width]
    upstream = up_ref[...]
    dk_sum[...] = jnp.zeros_like(dk_sum)
    dv_sum[...] = jnp.zeros_like(dv_sum)
    for first in range(0, span, step):
        reach = first + step if causal else span
        rows = slice(first, first + step)
        product = (upstream[rows].astype(jnp.float32) * full_ref[rows, :]).T
        parts = []
        for head in range(heads):
            cols = slice(head * HEAD_DIM, (head + 1) * HEAD_DIM)
            delta = jnp.sum(product[cols], axis=0, keepdims=True)
            scores = masked_scores(
                keys[:reach, cols], scaled[rows, cols], seg_q[:, rows], seg_k[:reach], first, causal
            )
            probs = jnp.exp(scores - lse_ref[head : head + 1, rows])
            dv_sum[head, :reach] += pair_dot(
                probs.astype(jnp.bfloat16), upstream[rows, cols], 1, 0
            )
            grad_probs = pair_dot(values[:reach, cols], upstream[rows, cols], 1, 1)
            grad_scores = (probs * (grad_probs - delta)).astype(jnp.bfloat16)
            dk_sum[head, :reach] += pair_dot(grad_scores, scaled[rows, cols], 1, 0)
            parts.append(pair_dot(keys[:reach, cols], grad_scores, 0, 0))
        joined = jnp.concatenate(parts, axis=0).T * HEAD_DIM ** (-0.5)
        dq_ref[rows, :width] = joined.astype(jnp.bfloat16)
    sums = [dk_sum[head] for head in range(heads)] + [dv_sum[head] for head in range(heads)]
    kv_at = dkv_ref.shape[1] - 2 * width
    dkv_ref[:, kv_at:] = jnp.concatenate(sums, axis=1).astype(jnp.bfloat16)


def attn_backward(
    q_ends, k_ends, queries, keys_values, upstream, full, lse, causal, joined=False
):
    span, width = upstream.shape
    kinds = [3] if joined else [1, 2]
    heads = width // HEAD_DIM
    return pl.pallas_call(
        functools.partial(attn_backward_body, causal, width),
        out_shape=[jax.ShapeDtypeStruct((span, kind * width), jnp.bfloat16) for kind in kinds],
        in_specs=[smem_spec(), smem_spec()] + [vmem_spec()] * 5,
        out_specs=[vmem_spec()] * len(kinds),
        scratch_shapes=[pltpu.VMEM((heads, span, HEAD_DIM), jnp.float32)] * 2,
        compiler_params=pltpu.CompilerParams(vmem_limit_bytes=VMEM_BYTES),
        cost_estimate=cost(8),
        name="attn_backward",
    )(q_ends, k_ends, queries, keys_values, upstream, full, lse)


def exchange(blocks):
    return lax.all_to_all(blocks, "blk", 0, 0, tiled=True)


def as_rows(blocks):
    return blocks.reshape(blocks.shape[0] * blocks.shape[1], blocks.shape[2])


def as_blocks(rows):
    devices = lax.axis_size("blk")
    return rows.reshape(devices, rows.shape[0] // devices, rows.shape[1])


def write_blocks(out_ref, values, lanes, kind, width):
    span = values.shape[0] // lanes
    for group in range(WIDTH // width):
        for lane in range(lanes):
            out_ref[lane * (WIDTH // width) + group, :, kind * width : (kind + 1) * width] = values[
                lane * span : (lane + 1) * span, group * width : (group + 1) * width
            ]


def read_blocks(got_ref, lanes, kind, width):
    groups = got_ref.shape[0] // lanes
    cols = slice(kind * width, (kind + 1) * width)
    rows = [
        jnp.concatenate([got_ref[lane * groups + group, :, cols] for group in range(groups)], axis=1)
        for lane in range(lanes)
    ]
    return jnp.concatenate(rows, axis=0)


def dot(left, right):
    return pair_dot(left, right, 1, 0)


def dot_back(left, right):
    return pair_dot(left, right, 1, 1)


def shape(*sizes, of=jnp.float32):
    return jax.ShapeDtypeStruct(sizes, of)


def normalize(values):
    center = values - jnp.mean(values, -1, keepdims=True)
    scale = lax.rsqrt(jnp.mean(center * center, -1, keepdims=True) + 1e-05)
    return center * scale, scale


def norm_back(upstream, normed, scale, gains_row):
    grad = upstream * gains_row
    return scale * (
        grad
        - jnp.mean(grad, -1, keepdims=True)
        - normed * jnp.mean(grad * normed, -1, keepdims=True)
    )


def project_blocks(inputs, parts, lanes, width, name):
    def body(ins, loaded, outs, _):
        for kind, weight in enumerate(loaded):
            write_blocks(
                outs[0], dot(ins[0][...], weight.value()).astype(jnp.bfloat16), lanes, kind, width
            )

    devices, span = lax.axis_size("blk"), inputs.shape[0] // lanes
    (blocks,) = call_with_parts(
        body,
        [inputs],
        parts,
        [shape(devices, span, width * len(parts), of=jnp.bfloat16)],
        name,
    )
    return blocks


def after_self(got, tokens, gains, biases, out_part, query_part, lanes, width):
    def body(ins, loaded, outs, _):
        got_ref, tokens_ref, gains_ref, biases_ref = ins
        low_ref, normed_ref, scale_ref, hidden_ref, blocks_ref = outs
        attended = read_blocks(got_ref, lanes, 0, width)
        low_ref[...] = attended
        resid = tokens_ref[...].astype(jnp.float32) + dot(attended, loaded[0].value())
        normed, scale = normalize(resid)
        normed_ref[...] = normed
        scale_ref[...] = scale
        hidden = (normed * gains_ref[0:1] + biases_ref[0:1]).astype(jnp.bfloat16)
        hidden_ref[...] = hidden
        query = dot(hidden, loaded[1].value()).astype(jnp.bfloat16)
        write_blocks(blocks_ref, query, lanes, 0, width)

    rows = tokens.shape[0]
    return call_with_parts(
        body,
        [got, tokens, gains, biases],
        [out_part, query_part],
        [
            shape(rows, WIDTH, of=jnp.bfloat16),
            shape(rows, WIDTH),
            shape(rows, 1),
            shape(rows, WIDTH, of=jnp.bfloat16),
            shape(*got.shape, of=jnp.bfloat16),
        ],
        "after_self",
    )


def feed_forward(got, normed_in, cotangent, gains, biases, out_part, in_parts, down, outs, up, lanes, width):
    pieces = len(in_parts)
    step = in_parts[0].width

    def body(ins, loaded, refs, scratch):
        got_ref, normed_in_ref, cot_ref, gains_ref, biases_ref = ins
        (
            output_ref,
            low_ref,
            mixed_ref,
            adapted_ref,
            dunder_ref,
            dab_ref,
            dcb_ref,
            dresid_ref,
            blocks_ref,
            norms_ref,
        ) = refs
        (slopes,) = scratch
        w_out, w_in = loaded[0], loaded[1 : 1 + pieces]
        w_down, w_ff, w_up = loaded[1 + pieces :]
        attended = read_blocks(got_ref, lanes, 0, width)
        low_ref[...] = attended
        hidden = normed_in_ref[...] * gains_ref[0:1] + biases_ref[0:1]
        normed_one, scale_one = normalize(hidden + dot(attended, w_out.value()))
        mixed = normed_one * gains_ref[1:2] + biases_ref[1:2]
        mixed_low = mixed.astype(jnp.bfloat16)
        mixed_ref[...] = mixed_low
        summed = mixed
        under = dot(mixed_low, w_down.value())
        gate = 1.0 / (1.0 + jnp.exp(-under))
        adapted = (under * gate).astype(jnp.bfloat16)
        adapted_ref[...] = adapted
        under_slope = gate * (1.0 + under * (1.0 - gate))
        summed = summed + 4.0 * dot(adapted, w_up.value())
        for piece in range(pieces):
            before = dot(mixed_low, w_in[piece].value())
            below = 0.5 + 0.5 * lax.erf(before * (0.5**0.5))
            slopes[piece] = below + before * jnp.exp(-0.5 * before * before) * (
                (2.0 * math.pi) ** -0.5
            )
            act = (before * below).astype(jnp.bfloat16)
            summed = summed + dot(act, w_ff[piece].value())
        normed_two, scale_two = normalize(summed)
        output_ref[...] = (normed_two * gains_ref[2:3] + biases_ref[2:3]).astype(jnp.bfloat16)
        upstream = cot_ref[...].astype(jnp.float32)
        norms_ref[0:1] = jnp.sum(upstream * normed_two, axis=0, keepdims=True)
        norms_ref[1:2] = jnp.sum(upstream, axis=0, keepdims=True)
        dz = norm_back(upstream, normed_two, scale_two, gains_ref[2:3])
        dzb = dz.astype(jnp.bfloat16)
        dab = (4.0 * dz).astype(jnp.bfloat16)
        dab_ref[...] = dab
        dunder = (under_slope * dot_back(dab, w_up.value())).astype(jnp.bfloat16)
        dunder_ref[...] = dunder
        dmixed = dz + dot_back(dunder, w_down.value())
        for piece in range(pieces):
            dpre = (slopes[piece] * dot_back(dzb, w_ff[piece].value())).astype(jnp.bfloat16)
            dmixed = dmixed + dot_back(dpre, w_in[piece].value())
        norms_ref[2:3] = jnp.sum(dmixed * normed_one, axis=0, keepdims=True)
        norms_ref[3:4] = jnp.sum(dmixed, axis=0, keepdims=True)
        dresid = norm_back(dmixed, normed_one, scale_one, gains_ref[1:2])
        dresid_ref[...] = dresid
        dcb = dresid.astype(jnp.bfloat16)
        dcb_ref[...] = dcb
        write_blocks(
            blocks_ref, dot_back(dcb, w_out.value()).astype(jnp.bfloat16), lanes, 0, width
        )

    rows = normed_in.shape[0]
    low = jnp.bfloat16

    def body_rows(ins, loaded, refs, scratch):
        whole_ff = loaded[2 + pieces]

        class Rows:
            def __init__(self, piece):
                self.piece = piece

            def value(self):
                return whole_ff.value()[self.piece * step : (self.piece + 1) * step]

        loaded = loaded[: 2 + pieces] + [[Rows(piece) for piece in range(pieces)], loaded[-1]]
        body(ins, loaded, refs, scratch)

    return call_with_parts(
        body_rows,
        [got, normed_in, cotangent, gains, biases],
        [out_part] + in_parts + [down, outs, up],
        [
            shape(rows, WIDTH, of=low),
            shape(rows, WIDTH, of=low),
            shape(rows, WIDTH, of=low),
            shape(rows, down.width, of=low),
            shape(rows, down.width, of=low),
            shape(rows, WIDTH, of=low),
            shape(rows, WIDTH, of=low),
            shape(rows, WIDTH),
            shape(*got.shape, of=low),
            shape(4, WIDTH),
        ],
        "feed_forward",
        [pltpu.VMEM((pieces, rows, step), jnp.float32)],
        20,
    )


def before_self(got, dresid, normed, scale, gains, query_part, out_part, lanes, width):
    def body(ins, loaded, outs, _):
        got_ref, dresid_ref, normed_ref, scale_ref, gains_ref = ins
        dcq_ref, dr_ref, dsb_ref, blocks_ref, norms_ref = outs
        dcq = read_blocks(got_ref, lanes, 0, width)
        dcq_ref[...] = dcq
        dhidden = dresid_ref[...] + dot_back(dcq, loaded[0].value())
        normed = normed_ref[...]
        norms_ref[0:1] = jnp.sum(dhidden * normed, axis=0, keepdims=True)
        norms_ref[1:2] = jnp.sum(dhidden, axis=0, keepdims=True)
        dr = norm_back(dhidden, normed, scale_ref[...], gains_ref[0:1])
        dr_ref[...] = dr
        dsb = dr.astype(jnp.bfloat16)
        dsb_ref[...] = dsb
        grad = dot_back(dsb, loaded[1].value()).astype(jnp.bfloat16)
        write_blocks(blocks_ref, grad, lanes, 0, width)

    rows = dresid.shape[0]
    return call_with_parts(
        body,
        [got, dresid, normed, scale, gains],
        [query_part, out_part],
        [
            shape(rows, WIDTH, of=jnp.bfloat16),
            shape(rows, WIDTH),
            shape(rows, WIDTH, of=jnp.bfloat16),
            shape(*got.shape, of=jnp.bfloat16),
            shape(2, WIDTH),
        ],
        "before_self",
    )


def input_grad(got, start, parts, lanes, span, width, name):
    def body(ins, loaded, outs, _):
        total = None
        for kind, weight in enumerate(loaded):
            values = read_blocks(ins[0], lanes, kind, width)
            term = dot_back(values, weight.value())
            total = term if total is None else total + term
        outs[0][...] = total if len(ins) == 1 else total + ins[1][...]

    rows = span * lanes
    return call_with_parts(
        body,
        [got] if start is None else [got, start],
        parts,
        [shape(rows, WIDTH)],
        name,
    )


def shards(
    tokens,
    encoder,
    cotangent,
    self_in,
    self_out,
    cross_q,
    cross_kv,
    cross_out,
    ffn_in,
    ffn_out,
    adapt_down,
    adapt_up,
    norm_gain,
    norm_bias,
    tgt_lengths,
    src_lengths,
):
    lanes, span, _ = tokens.shape
    rows = lanes * span
    width = WIDTH * lanes // lax.axis_size("blk")
    own_row = lax.axis_index("blk") // (lax.axis_size("blk") // lanes)
    tgt_ends = jnp.cumsum(lax.dynamic_index_in_dim(tgt_lengths, own_row, 0, keepdims=False))
    src_ends = jnp.cumsum(lax.dynamic_index_in_dim(src_lengths, own_row, 0, keepdims=False))
    flat_tokens = tokens.reshape(rows, WIDTH)
    flat_encoder = encoder.reshape(rows, WIDTH)
    frozen = [ffn_in, adapt_down, ffn_out, adapt_up, cross_out]
    inward = [self_in, cross_kv]

    if paired():
        packed = gather_packed(pack_halves(frozen))
        token_row, stages = gather_row(tokens)
        self_heads, pair_heads = head_columns(after(inward, stages[1]), [3, 2])
        out_shard, query_shard = after((self_out, cross_q), stages[1])
        encoder_block = after(encoder, stages[1])
        self_qkv = project_row(token_row, self_heads, "self_in")
        out_source, query_source = gather_flips([out_shard, query_shard], "xy", self_qkv)
        encoder_row, encoder_stages = gather_row(
            encoder_block, self_qkv, (out_source.arrays[1], query_source.arrays[1])
        )
        self_qkv = after(self_qkv, out_source.stages[0], query_source.stages[0])
        pair_own = project_row(encoder_row, pair_heads, "cross_kv")
    else:
        (self_source, pair_source, out_source, query_source) = gather_flips(
            [self_in, cross_kv, self_out, cross_q], "xyxy"
        )
        self_parts = [columns_of((self_source, WIDTH * kind, WIDTH)) for kind in range(3)]
        pair_parts = [columns_of((pair_source, WIDTH * kind, WIDTH)) for kind in range(2)]
        self_qkv = as_rows(
            exchange(project_blocks(flat_tokens, self_parts, lanes, width, "self_in"))
        )
        pair_own = as_rows(
            exchange(project_blocks(flat_encoder, pair_parts, lanes, width, "cross_kv"))
        )
    self_out_part = columns_of((out_source, 0, WIDTH))
    query_part = columns_of((query_source, 0, WIDTH))

    self_mid, self_full, self_lse = attn_forward(
        tgt_ends, tgt_ends, self_qkv, self_qkv, width, True
    )
    self_sent = after(self_mid, out_source.stages[1], query_source.stages[1])
    if paired():
        self_sent = after(self_sent, encoder_stages[0])
    self_back = exchange(as_blocks(self_sent))
    if paired():
        self_back = after(self_back, encoder_stages[1])
    self_low, normed, scale, hidden_low, query_blocks = after_self(
        self_back,
        flat_tokens,
        norm_gain,
        norm_bias,
        self_out_part,
        query_part,
        lanes,
        width,
    )
    cross_own = as_rows(exchange(query_blocks))
    cross_mid, cross_full, cross_lse = attn_forward(
        tgt_ends, src_ends, cross_own, pair_own, width, False
    )
    cross_back = exchange(as_blocks(cross_mid))
    ready = after(packed, cross_mid) if paired() else None
    ff_parts, down_parts, ffo_parts, up_parts, (cross_out_part,) = packed_parts(frozen, ready)
    (
        output,
        cross_low,
        mixed_low,
        adapter_low,
        grad_under,
        adapt_low,
        cross_branch_low,
        grad_resid_two,
        cross_grad_blocks,
        norms_high,
    ) = feed_forward(
        cross_back,
        normed,
        cotangent.reshape(rows, WIDTH),
        norm_gain,
        norm_bias,
        cross_out_part,
        ff_parts,
        down_parts[0],
        ffo_parts[0],
        up_parts[0],
        lanes,
        width,
    )
    high_groups = [
        [(cross_low, cross_branch_low)],
        [(mixed_low, grad_under), (adapter_low, adapt_low)],
    ]
    high_terms = [grad_terms(pairs) for pairs in high_groups]
    high_orders = [(2, 1, 4, 8), (1, 2, 4, 8)]
    high_terms, high_stages = scatter_chips(high_terms, high_orders, 0, 2)
    cross_dq, cross_dkv = attn_backward(
        tgt_ends,
        src_ends,
        cross_own,
        pair_own,
        as_rows(after(exchange(cross_grad_blocks), high_stages[0])),
        cross_full,
        cross_lse,
        False,
    )
    cross_dq_got = after(exchange(as_blocks(cross_dq)), high_stages[1])
    if paired():
        dkv_late = after(cross_dkv, high_stages[1])
        pair_terms = row_back(dkv_late, pair_heads, "encoder_grad")
        kv_sent = row_grad(encoder_row, dkv_late, "cross_kv_grad")
        cross_dq_got = after(cross_dq_got, pair_terms, kv_sent)
    cq_low, grad_resid_one, self_branch_low, self_grad_blocks, norms_low = before_self(
        cross_dq_got,
        grad_resid_two,
        normed,
        scale,
        norm_gain,
        query_part,
        self_out_part,
        lanes,
        width,
    )
    norms = jnp.concatenate([norms_low, norms_high], axis=0)
    mid_groups = [[(hidden_low, cq_low)], [(self_low, self_branch_low)]]
    mid_terms = [grad_terms(pairs) for pairs in mid_groups]
    mid_orders = [(2, 1, 4, 8), (1, 2, 4, 8)]
    high_terms, high_near = scatter_chips(
        after(high_terms, self_grad_blocks), high_orders, 2, 3
    )
    self_upstream = after(exchange(self_grad_blocks), high_stages[2])
    (self_grads,) = attn_backward(
        tgt_ends,
        tgt_ends,
        self_qkv,
        self_qkv,
        as_rows(self_upstream),
        self_full,
        self_lse,
        True,
        joined=True,
    )
    if paired():
        self_terms = row_back(self_grads, self_heads, "tokens_grad")
        self_sent = row_grad(token_row, after(self_grads, self_terms), "self_in_grad")
        self_back_sum, stages = reduce_row(self_terms, {1: self_sent})
        tokens_grad = grad_resid_one + self_back_sum.reshape(rows, WIDTH)
        encoder_grad, _ = reduce_row(pair_terms, {2: self_terms})
        encoder_grad = encoder_grad.reshape(rows, WIDTH)
        mid_terms, _ = scatter_chips(
            mid_terms, mid_orders, 0, 4, {1: self_terms, 2: stages[1], 3: stages[2]}
        )
        high_terms, _ = scatter_chips(after(high_terms, stages[1]), high_orders, 3, 4)
        chunks = [
            array[:, :, first : first + width]
            for array in (self_sent, kv_sent)
            for first in range(0, array.shape[2], width)
        ]
        partials = norms.astype(jnp.bfloat16).reshape(1, 48, width)
        chunks.append(jnp.broadcast_to(partials, (16, 48, width)))
        got = exchange(jnp.concatenate(chunks, axis=1))
        chunks = [got[:, first : first + 32] for first in range(0, 160, 32)]
        grad_self_in = finish_row_grad(jnp.concatenate(chunks[:3], axis=2), 3)
        grad_cross_kv = finish_row_grad(jnp.concatenate(chunks[3:], axis=2), 2)
        norms = jnp.sum(got[:, 160:].astype(jnp.float32), axis=0).reshape(6, WIDTH)
        norms = norms + swap_core(norms)
    else:
        pair_got = exchange(as_blocks(cross_dkv))
        self_got = exchange(as_blocks(self_grads))
        (encoder_grad,) = input_grad(
            pair_got, None, pair_parts, lanes, span, width, "encoder_grad"
        )
        (tokens_grad,) = input_grad(
            self_got, grad_resid_one, self_parts, lanes, span, width, "tokens_grad"
        )
        pair_low = pair_got.reshape(lanes, -1, span, 2, width).transpose(0, 2, 3, 1, 4)
        self_low_grads = self_got.reshape(lanes, -1, span, 3, width).transpose(0, 2, 3, 1, 4)
        grad_cross_kv = weight_grad(flat_encoder, pair_low.reshape(rows, 2 * WIDTH))
        grad_self_in = weight_grad(flat_tokens, self_low_grads.reshape(rows, 3 * WIDTH))
        norms = lax.psum(norms, ("dp", "blk"))
    (grad_cross_q,), (grad_self_out,) = finish_terms(mid_groups, mid_terms)
    (grad_cross_out,), (grad_adapt_down, grad_adapt_up) = finish_terms(high_groups, high_terms)
    return (
        output.reshape(lanes, span, WIDTH),
        tokens_grad.reshape(lanes, span, WIDTH),
        encoder_grad.reshape(lanes, span, WIDTH),
        grad_self_in,
        grad_self_out,
        grad_cross_q,
        grad_cross_kv,
        grad_cross_out,
        grad_adapt_down,
        grad_adapt_up,
        jnp.stack([norms[0], norms[4], norms[2]]),
        jnp.stack([norms[1], norms[5], norms[3]]),
    )


def solution(mesh):
    placed = (
        P("dp", "blk", None),
        P("dp", "blk", None),
        P("dp", "blk", None),
        P("blk", None),
        P("blk", None),
        P("blk", None),
        P("blk", None),
        P("blk", None),
        P("blk", None),
        P("blk", None),
        P("blk", None),
        P("blk", None),
        P(),
        P(),
        P("dp", None),
        P("dp", None),
    )
    return jax.shard_map(
        shards,
        mesh=mesh,
        in_specs=placed,
        out_specs=(
            P("dp", "blk", None),
            P("dp", "blk", None),
            P("dp", "blk", None),
            P("blk", None),
            P("blk", None),
            P("blk", None),
            P("blk", None),
            P("blk", None),
            P("blk", None),
            P("blk", None),
            P(),
            P(),
        ),
        check_vma=False,
    )
```

```python
import functools
import math

import jax
import jax.numpy as jnp
from jax import lax
from jax.experimental import pallas as pl
from jax.experimental.pallas import tpu as pltpu
from jax.sharding import PartitionSpec as P

HEADS = 16
HEAD_DIM = 64
WIDTH = HEADS * HEAD_DIM


NEG = -1e30
VMEM_BYTES = 56 * 1024 * 1024


def cost(microseconds):
    return pl.CostEstimate(
        flops=int(microseconds * 0.4e9),
        bytes_accessed=int(microseconds * 1.2e6),
        transcendentals=0,
    )


def paired():
    return lax.axis_size("blk") == 16 and lax.axis_size("dp") == 2


def swap_core(block):
    cores = lax.axis_size("dp")
    return lax.ppermute(block, "dp", [(i ^ 1, i) for i in range(cores)])


def flip(block, bit):
    chips = lax.axis_size("blk")
    return lax.ppermute(block, "blk", [(i ^ bit, i) for i in range(chips)])


FLIPS = (8, 4, 2, 1)


def with_flip(block, bit):
    return jnp.stack([block, flip(block, bit)])


def own_half(values, which):
    half = values.shape[1] // 2
    return lax.dynamic_slice_in_dim(values, which * half, half, 1)


def scatter_chips(terms, orders, first, last, holds=None):
    if not paired():
        return terms, [terms] * 5
    own = lax.axis_index("blk")

    def fold(blocks, left, bit):
        axis, place = left.index(bit), (own // bit) % 2
        kept = lax.dynamic_index_in_dim(blocks, place, axis, keepdims=False)
        sent = lax.dynamic_index_in_dim(blocks, 1 - place, axis, keepdims=False)
        got = flip(sent, bit)
        return (kept.astype(jnp.float32) + got.astype(jnp.float32)).astype(jnp.bfloat16)

    if first == 0:
        terms = [blocks.reshape(2, 2, 2, 2, *blocks.shape[1:]) for blocks in terms]
    stages = [terms[0]]
    for stage in range(first, last):
        if holds and stage in holds:
            terms = after(terms, holds[stage])
        terms = [
            fold(blocks, [bit for bit in FLIPS if bit not in order[:stage]], order[stage])
            for blocks, order in zip(terms, orders)
        ]
        stages.append(terms[0])
    return terms, stages


CHUNK = 256


def grad_terms(pairs):
    if not paired():
        return pairs[0][1]
    core = lax.axis_index("dp")
    packed = []
    for inputs, upstream in pairs:
        both = jnp.concatenate([inputs, swap_core(inputs)], axis=0)
        half = jnp.concatenate(
            [own_half(upstream, core), swap_core(own_half(upstream, 1 - core))], axis=0
        )
        term = lax.dot_general(
            both, half, (((0,), (0,)), ((), ())), preferred_element_type=jnp.float32
        ).astype(jnp.bfloat16)
        rows = term.shape[0] // 16
        chunks = term.shape[1] // CHUNK
        packed += [
            term[:, c * CHUNK : (c + 1) * CHUNK].reshape(16, rows, CHUNK) for c in range(chunks)
        ]
    return jnp.concatenate(packed, axis=1)


def finish_terms(groups, terms):
    if not paired():
        return [[weight_grad(inputs, upstream) for inputs, upstream in pairs] for pairs in groups]
    core = lax.axis_index("dp")
    mine = jnp.concatenate(terms, axis=0)
    other = swap_core(mine)
    low = jnp.where(core == 0, mine, other).astype(jnp.float32)
    high = jnp.where(core == 0, other, mine).astype(jnp.float32)
    found, place = [], 0
    for pairs in groups:
        found.append([])
        for inputs, upstream in pairs:
            rows = inputs.shape[1] // 16
            chunks = upstream.shape[1] // 2 // CHUNK
            spots = [slice(place + c * rows, place + (c + 1) * rows) for c in range(chunks)]
            found[-1].append(
                jnp.concatenate(
                    [low[spot] for spot in spots] + [high[spot] for spot in spots], axis=1
                )
            )
            place += rows * chunks
    return found


def weight_grad(inputs, upstream):
    scattered = lax.psum_scatter(
        lax.dot_general(
            inputs, upstream, (((0,), (0,)), ((), ())), preferred_element_type=jnp.float32
        ).astype(jnp.bfloat16),
        "blk",
        scatter_dimension=0,
        tiled=True,
    )
    return lax.psum(scattered, "dp").astype(jnp.float32)


class Source:
    def __init__(self, kind, arrays, first_flip="x", column=None):
        self.kind, self.arrays, self.first_flip = kind, arrays, first_flip
        self.stages = arrays[:1] * 3 if column is None else [column] + arrays[:2]


class Part:
    def __init__(self, rows, width, spots):
        self.rows, self.width, self.spots = rows, width, spots

    def scratch(self):
        return pltpu.VMEM((2, 2, 2, 2, 2, self.rows // 32, self.width), jnp.bfloat16)

    def start(self, refs_of, place, dst, sem):
        z1, z0, y, x, core = [place[axis] for axis in range(5)]
        high = self.rows // 32
        for source, first_row, first_col, at_col, width in self.spots:
            refs = refs_of(source)
            cols = slice(first_col, first_col + width)
            into = slice(at_col, at_col + width)
            if source.kind == "whole":
                pltpu.make_async_copy(
                    refs[0].at[:, :, :, :, :, :, cols], dst.at[:, :, :, :, :, :, into], sem
                ).start()
            elif source.kind == "cores":
                for which in range(2):
                    owner = core if which == 0 else 1 - core
                    pltpu.make_async_copy(
                        refs[which].at[:, :, :, :, first_row : first_row + high, cols],
                        dst.at[:, :, :, :, owner, :, into],
                        sem,
                    ).start()
            else:
                for which in range(4):
                    owner = core if which < 2 else 1 - core
                    for near, at_y, at_x in flipped(source.first_flip, which % 2, y, x):
                        for up, at_z1, at_z0 in four(z1, z0):
                            pltpu.make_async_copy(
                                refs[which].at[near, up[0], up[1], :, cols],
                                dst.at[at_z1, at_z0, at_y, at_x, owner, :, into],
                                sem,
                            ).start()


def four(z1, z0):
    return [
        ((low, high), z1 if high == 0 else 1 - z1, z0 if low == 0 else 1 - z0)
        for low in range(2)
        for high in range(2)
    ]


def flipped(first_flip, beyond, y, x):
    found = []
    for near in range(2):
        a, b = (near, beyond) if first_flip == "x" else (beyond, near)
        found.append((near, y if b == 0 else 1 - y, x if a == 0 else 1 - x))
    return found


def after(value, *others):
    return lax.optimization_barrier((value, *others))[0]


def gather_flips(shards, first_flips, hold=None):
    if not paired():
        full = [lax.all_gather(shard, "blk", axis=0, tiled=True) for shard in shards]
        return [
            Source("whole", [array.reshape(2, 2, 2, 2, 2, array.shape[0] // 32, array.shape[1])])
            for array in full
        ]
    core = lax.axis_index("dp")
    columns = []
    for shard in shards:
        rows = shard.shape[0]
        own = lax.dynamic_slice_in_dim(shard, core * (rows // 2), rows // 2, 0)
        columns.append(with_flip(with_flip(own, 8), 4))
    sources, bits = [], {"x": (1, 2), "y": (2, 1)}
    if hold is not None:
        columns = after(columns, hold)
    planes = [
        with_flip(column, bits[first][0]) for column, first in zip(columns, first_flips)
    ]
    for column, plane, first in zip(columns, planes, first_flips):
        beyond = flip(plane, bits[first][1])
        sources.append(
            Source("flips", [plane, beyond, swap_core(plane), swap_core(beyond)], first, column)
        )
    return sources


class RowPart:
    def __init__(self, sources, span):
        self.span = span
        self.rows, self.width = 16 * span, WIDTH
        self.spots = [(source,) for source in sources]

    def scratch(self):
        return pltpu.VMEM((2, 2, 2, 2, self.span, WIDTH), jnp.bfloat16)

    def start(self, refs_of, place, dst, sem):
        z1, z0, y, x = [place[axis] for axis in range(4)]
        half = WIDTH // 2
        for side, (source,) in enumerate(self.spots):
            refs = refs_of(source)
            for beyond in range(2):
                for near, at_y, at_x in flipped(source.first_flip, beyond, y, x):
                    for up, at_z1, at_z0 in four(z1, z0):
                        pltpu.make_async_copy(
                            refs[beyond].at[near, up[0], up[1]],
                            dst.at[at_z1, at_z0, at_y, at_x, :, side * half : (side + 1) * half],
                            sem,
                        ).start()


def gather_row(block, hold_near=None, hold=None):
    row = lax.axis_index("blk") // 8
    own = lax.dynamic_index_in_dim(block, row, 0, keepdims=False)
    other = lax.dynamic_index_in_dim(block, 1 - row, 0, keepdims=False)
    pair = jnp.stack([own, flip(other, 8)])
    if hold_near is not None:
        pair = after(pair, hold_near)
    column = with_flip(pair, 4)
    stages, sources = [pair, column], []
    if hold is not None:
        column = after(column, hold)
    half = WIDTH // 2
    planes = [with_flip(column[..., :half], 1), with_flip(column[..., half:], 2)]
    for plane, first, bit in zip(planes, "xy", (2, 1)):
        sources.append(Source("row", [plane, flip(plane, bit)], first))
    stages += [planes, [source.arrays[1] for source in sources]]
    return RowPart(sources, block.shape[1]), stages


def head_columns(shards, kinds):
    core = lax.axis_index("dp")
    blocks, widths = [], [128 * kind for kind in kinds]
    for shard, kind in zip(shards, kinds):
        own = lax.dynamic_slice_in_dim(shard, core * 32, 32, 0)
        own = own.reshape(32, kind, 8, 128).transpose(2, 0, 1, 3)
        blocks.append(own.reshape(8, 32, kind * 128))
    blocks = jnp.concatenate(blocks, axis=2)
    mine = exchange(jnp.concatenate([blocks, blocks], axis=0))
    mine = mine.reshape(2, 2, 2, 2, 32, sum(widths))
    source = Source("cores", [mine, swap_core(mine)])
    parts, place = [], 0
    for width in widths:
        parts.append(Part(1024, width, [(source, 0, place, 0, width)]))
        place += width
    return parts


def project_row(row_part, head_part, name):
    def body(ins, loaded, outs, _):
        weight = loaded[1].value()
        inputs = loaded[0].value()
        for first in range(0, row_part.rows, 256):
            rows = slice(first, first + 256)
            outs[0][rows, :] = dot(inputs[rows], weight).astype(jnp.bfloat16)

    (found,) = call_with_parts(
        body,
        [],
        [row_part, head_part],
        [shape(row_part.rows, head_part.width, of=jnp.bfloat16)],
        name,
    )
    return found


def row_grad(row_part, upstream, name):
    columns = upstream.shape[1]

    def body(ins, loaded, outs, _):
        core = ins[1][0]
        inputs = loaded[0].value()
        grads = []
        for first in range(0, columns, 128):
            grads.append(pair_dot(ins[0][:, first : first + 128], inputs, 0, 0).T)
        grad = jnp.concatenate(grads, axis=1).astype(jnp.bfloat16).reshape(16, 2, 32, columns)
        outs[0][core] = grad[:, 0]
        outs[0][1 - core] = grad[:, 1]

    (terms,) = call_with_parts(
        body,
        [upstream],
        [row_part],
        [shape(2, 16, 32, columns, of=jnp.bfloat16)],
        name,
        scalars=[lax.axis_index("dp").reshape(1).astype(jnp.int32)],
    )
    got = swap_core(terms[1])
    return (terms[0].astype(jnp.float32) + got.astype(jnp.float32)).astype(jnp.bfloat16)


def row_back(upstream, head_part, name):
    def body(ins, loaded, outs, _):
        weight = loaded[0].value()
        for first in range(0, ins[0].shape[0], 256):
            rows = slice(first, first + 256)
            outs[0][rows, :] = dot_back(ins[0][rows, :], weight).astype(jnp.bfloat16)

    (terms,) = call_with_parts(
        body, [upstream], [head_part], [shape(upstream.shape[0], WIDTH, of=jnp.bfloat16)], name
    )
    return terms


def reduce_row(terms, holds=None):
    blocks = terms.reshape(16, terms.shape[0] // 16, WIDTH)
    half = WIDTH // 2
    halves, stages = scatter_chips(
        [blocks[..., :half], blocks[..., half:]], [(1, 2, 4, 8), (2, 1, 4, 8)], 0, 3, holds
    )
    both = jnp.concatenate(halves, axis=2)
    row = lax.axis_index("blk") // 8
    kept = lax.dynamic_index_in_dim(both, row, 0, keepdims=False)
    got = flip(lax.dynamic_index_in_dim(both, 1 - row, 0, keepdims=False), 8)
    found = jnp.stack([jnp.where(row == 0, kept, got), jnp.where(row == 0, got, kept)])
    return found.astype(jnp.float32), stages


def finish_row_grad(got, kinds):
    total = jnp.sum(got.reshape(2, 8, 32, kinds, 128).astype(jnp.float32), axis=0)
    mine = total.astype(jnp.bfloat16).transpose(1, 2, 0, 3).reshape(32, kinds * WIDTH)
    other = swap_core(mine)
    core = lax.axis_index("dp")
    low = jnp.where(core == 0, mine, other)
    high = jnp.where(core == 0, other, mine)
    return jnp.concatenate([low, high], axis=0).astype(jnp.float32)


def columns_of(*pieces):
    spots, place = [], 0
    for source, first, width in pieces:
        spots.append((source, 0, first, place, width))
        place += width
    return Part(1024, place, spots)


PACK = 512


def pack_halves(shards):
    places = [
        (index, shard.shape[0] // 2, first)
        for index, shard in enumerate(shards)
        for first in range(0, shard.shape[1], PACK)
    ]

    def body(core, *refs):
        out_ref, place = refs[-1], 0
        for index, high, first in places:
            start = pl.multiple_of(core[0] * high, 16)
            out_ref[place : place + high, :] = refs[index][pl.ds(start, high), first : first + PACK]
            place += high

    return pl.pallas_call(
        body,
        out_shape=shape(sum(high for _, high, _ in places), PACK, of=jnp.bfloat16),
        in_specs=[smem_spec()] + [vmem_spec()] * len(shards),
        out_specs=vmem_spec(),
        compiler_params=pltpu.CompilerParams(vmem_limit_bytes=VMEM_BYTES),
        cost_estimate=cost(2),
        name="pack_halves",
    )(lax.axis_index("dp").reshape(1).astype(jnp.int32), *shards)


def gather_packed(packed):
    return lax.all_gather(packed, "blk", axis=0)


def packed_parts(shards, mine):
    if not paired():
        found = []
        for source, shard in zip(gather_flips(shards, "x" * len(shards)), shards):
            rows, columns = 32 * source.arrays[0].shape[5], shard.shape[1]
            step = min(columns, 1024)
            found.append(
                [
                    Part(rows, step, [(source, 0, first, 0, step)])
                    for first in range(0, columns, step)
                ]
            )
        return found
    spots, place = [], 0
    for shard in shards:
        high = shard.shape[0] // 2
        places = []
        for first in range(0, shard.shape[1], PACK):
            places.append(place)
            place += high
        spots.append((shard.shape[0] * 16, places))
    mine = mine.reshape(2, 2, 2, 2, place, PACK)
    source = Source("cores", [mine, swap_core(mine)])
    found = []
    for rows, places in spots:
        parts = []
        for first in range(0, len(places), 2):
            two = places[first : first + 2]
            parts.append(
                Part(
                    rows,
                    PACK * len(two),
                    [(source, row, 0, PACK * side, PACK) for side, row in enumerate(two)],
                )
            )
        found.append(parts)
    return found


def place_now():
    own, core = lax.axis_index("blk"), lax.axis_index("dp")
    bits = [(own // bit) % 2 for bit in FLIPS]
    return jnp.stack(bits + [core]).astype(jnp.int32)


class Loaded:
    def __init__(self, part, dst, sem):
        self.part, self.dst, self.sem, self.here = part, dst, sem, False

    def value(self):
        if not self.here:
            pltpu.make_async_copy(self.dst, self.dst, self.sem).wait()
            self.here = True
        return self.dst[...].reshape(self.part.rows, self.part.width)


def call_with_parts(body, inputs, parts, outputs, name, scratch=(), takes=5, scalars=()):
    sources = []
    for part in parts:
        sources += [spot[0] for spot in part.spots if spot[0] not in sources]
    arrays = [array for source in sources for array in source.arrays]

    def kernel(place, *refs):
        refs = list(refs)
        ins = [refs.pop(0) for _ in (*inputs, *scalars)]
        pieces = [[refs.pop(0) for _ in source.arrays] for source in sources]
        outs = [refs.pop(0) for _ in outputs]
        dsts = [refs.pop(0) for _ in parts]
        sems = refs.pop(0)
        loaded = []
        for index, part in enumerate(parts):
            part.start(
                lambda source: pieces[sources.index(source)], place, dsts[index], sems.at[index]
            )
            loaded.append(Loaded(part, dsts[index], sems.at[index]))
        body(ins, loaded, outs, refs)

    return pl.pallas_call(
        kernel,
        out_shape=tuple(outputs),
        in_specs=[smem_spec()]
        + [vmem_spec()] * len(inputs)
        + [smem_spec()] * len(scalars)
        + [pl.BlockSpec(memory_space=pl.ANY)] * len(arrays),
        out_specs=(vmem_spec(),) * len(outputs),
        scratch_shapes=[part.scratch() for part in parts]
        + [pltpu.SemaphoreType.DMA((len(parts),))]
        + list(scratch),
        compiler_params=pltpu.CompilerParams(vmem_limit_bytes=VMEM_BYTES),
        cost_estimate=cost(takes),
        name=name,
    )(place_now(), *inputs, *scalars, *arrays)


def vmem_spec():
    return pl.BlockSpec(memory_space=pltpu.VMEM)


def smem_spec():
    return pl.BlockSpec(memory_space=pltpu.SMEM)


def seg_of_pos(ends_ref, pos):
    seg = jnp.zeros(pos.shape, jnp.int32)
    for slot in range(ends_ref.shape[0]):
        seg = seg + (ends_ref[slot] <= pos).astype(jnp.int32)
    return seg


def pair_dot(left, right, left_dim, right_dim):
    return lax.dot_general(
        left, right, (((left_dim,), (right_dim,)), ((), ())), preferred_element_type=jnp.float32
    )


def seg_tables(q_ends, k_ends, span):
    seg_q = seg_of_pos(q_ends, lax.broadcasted_iota(jnp.int32, (1, span), 1))
    seg_k = seg_of_pos(k_ends, lax.broadcasted_iota(jnp.int32, (span, 1), 0))
    return seg_q, seg_k


def masked_scores(keys, queries, seg_q, seg_k, first, causal):
    scores = pair_dot(keys, queries, 1, 1)
    allowed = seg_k == seg_q
    if causal:
        key_pos = lax.broadcasted_iota(jnp.int32, scores.shape, 0)
        query_pos = first + lax.broadcasted_iota(jnp.int32, scores.shape, 1)
        allowed = allowed & (key_pos <= query_pos)
    return jnp.where(allowed, scores, NEG)


def attn_forward_body(causal, width, q_ends, k_ends, q_ref, kv_ref, low_ref, full_ref, lse_ref):
    span = q_ref.shape[0]
    step = math.gcd(span, 256)
    heads = width // HEAD_DIM
    seg_q, seg_k = seg_tables(q_ends, k_ends, span)
    key_at = kv_ref.shape[1] - 2 * width
    scaled = q_ref[:, :width] * jnp.bfloat16(HEAD_DIM ** (-0.5))
    keys = kv_ref[:, key_at : key_at + width]
    values = kv_ref[:, key_at + width : key_at + 2 * width]
    for first in range(0, span, step):
        reach = first + step if causal else span
        parts = []
        for head in range(heads):
            cols = slice(head * HEAD_DIM, (head + 1) * HEAD_DIM)
            scores = masked_scores(
                keys[:reach, cols],
                scaled[first : first + step, cols],
                seg_q[:, first : first + step],
                seg_k[:reach],
                first,
                causal,
            )
            top = jnp.max(scores, axis=0, keepdims=True)
            probs = jnp.exp(scores - top)
            total = jnp.sum(probs, axis=0, keepdims=True)
            mixed = pair_dot(values[:reach, cols], probs.astype(jnp.bfloat16), 0, 0)
            parts.append(mixed / total)
            lse_ref[head : head + 1, first : first + step] = top + jnp.log(total)
        joined = jnp.concatenate(parts, axis=0).T
        full_ref[first : first + step, :] = joined
        low_ref[first : first + step, :] = joined.astype(jnp.bfloat16)


def attn_forward(q_ends, k_ends, queries, keys_values, width, causal):
    span = queries.shape[0]
    return pl.pallas_call(
        functools.partial(attn_forward_body, causal, width),
        out_shape=(
            jax.ShapeDtypeStruct((span, width), jnp.bfloat16),
            jax.ShapeDtypeStruct((span, width), jnp.float32),
            jax.ShapeDtypeStruct((width // HEAD_DIM, span), jnp.float32),
        ),
        in_specs=[smem_spec(), smem_spec()] + [vmem_spec()] * 2,
        out_specs=(vmem_spec(),) * 3,
        compiler_params=pltpu.CompilerParams(vmem_limit_bytes=VMEM_BYTES),
        cost_estimate=cost(8),
        name="attn_forward",
    )(q_ends, k_ends, queries, keys_values)


def attn_backward_body(
    causal,
    width,
    q_ends,
    k_ends,
    q_ref,
    kv_ref,
    up_ref,
    full_ref,
    lse_ref,
    *outs,
):
    dq_ref, dkv_ref = outs[0], outs[-3]
    dk_sum, dv_sum = outs[-2:]
    span = q_ref.shape[0]
    step = math.gcd(span, 256)
    heads = width // HEAD_DIM
    seg_q, seg_k = seg_tables(q_ends, k_ends, span)
    key_at = kv_ref.shape[1] - 2 * width
    scaled = q_ref[:, :width] * jnp.bfloat16(HEAD_DIM ** (-0.5))
    keys = kv_ref[:, key_at : key_at + width]
    values = kv_ref[:, key_at + width : key_at + 2 * width]
    upstream = up_ref[...]
    dk_sum[...] = jnp.zeros_like(dk_sum)
    dv_sum[...] = jnp.zeros_like(dv_sum)
    for first in range(0, span, step):
        reach = first + step if causal else span
        rows = slice(first, first + step)
        product = (upstream[rows].astype(jnp.float32) * full_ref[rows, :]).T
        parts = []
        for head in range(heads):
            cols = slice(head * HEAD_DIM, (head + 1) * HEAD_DIM)
            delta = jnp.sum(product[cols], axis=0, keepdims=True)
            scores = masked_scores(
                keys[:reach, cols], scaled[rows, cols], seg_q[:, rows], seg_k[:reach], first, causal
            )
            probs = jnp.exp(scores - lse_ref[head : head + 1, rows])
            dv_sum[head, :reach] += pair_dot(
                probs.astype(jnp.bfloat16), upstream[rows, cols], 1, 0
            )
            grad_probs = pair_dot(values[:reach, cols], upstream[rows, cols], 1, 1)
            grad_scores = (probs * (grad_probs - delta)).astype(jnp.bfloat16)
            dk_sum[head, :reach] += pair_dot(grad_scores, scaled[rows, cols], 1, 0)
            parts.append(pair_dot(keys[:reach, cols], grad_scores, 0, 0))
        joined = jnp.concatenate(parts, axis=0).T * HEAD_DIM ** (-0.5)
        dq_ref[rows, :width] = joined.astype(jnp.bfloat16)
    sums = [dk_sum[head] for head in range(heads)] + [dv_sum[head] for head in range(heads)]
    kv_at = dkv_ref.shape[1] - 2 * width
    dkv_ref[:, kv_at:] = jnp.concatenate(sums, axis=1).astype(jnp.bfloat16)


def attn_backward(
    q_ends, k_ends, queries, keys_values, upstream, full, lse, causal, joined=False
):
    span, width = upstream.shape
    kinds = [3] if joined else [1, 2]
    heads = width // HEAD_DIM
    return pl.pallas_call(
        functools.partial(attn_backward_body, causal, width),
        out_shape=[jax.ShapeDtypeStruct((span, kind * width), jnp.bfloat16) for kind in kinds],
        in_specs=[smem_spec(), smem_spec()] + [vmem_spec()] * 5,
        out_specs=[vmem_spec()] * len(kinds),
        scratch_shapes=[pltpu.VMEM((heads, span, HEAD_DIM), jnp.float32)] * 2,
        compiler_params=pltpu.CompilerParams(vmem_limit_bytes=VMEM_BYTES),
        cost_estimate=cost(8),
        name="attn_backward",
    )(q_ends, k_ends, queries, keys_values, upstream, full, lse)


def exchange(blocks):
    return lax.all_to_all(blocks, "blk", 0, 0, tiled=True)


def as_rows(blocks):
    return blocks.reshape(blocks.shape[0] * blocks.shape[1], blocks.shape[2])


def as_blocks(rows):
    devices = lax.axis_size("blk")
    return rows.reshape(devices, rows.shape[0] // devices, rows.shape[1])


def write_blocks(out_ref, values, lanes, kind, width):
    span = values.shape[0] // lanes
    for group in range(WIDTH // width):
        for lane in range(lanes):
            out_ref[lane * (WIDTH // width) + group, :, kind * width : (kind + 1) * width] = values[
                lane * span : (lane + 1) * span, group * width : (group + 1) * width
            ]


def read_blocks(got_ref, lanes, kind, width):
    groups = got_ref.shape[0] // lanes
    cols = slice(kind * width, (kind + 1) * width)
    rows = [
        jnp.concatenate([got_ref[lane * groups + group, :, cols] for group in range(groups)], axis=1)
        for lane in range(lanes)
    ]
    return jnp.concatenate(rows, axis=0)


def dot(left, right):
    return pair_dot(left, right, 1, 0)


def dot_back(left, right):
    return pair_dot(left, right, 1, 1)


def shape(*sizes, of=jnp.float32):
    return jax.ShapeDtypeStruct(sizes, of)


def normalize(values):
    center = values - jnp.mean(values, -1, keepdims=True)
    scale = lax.rsqrt(jnp.mean(center * center, -1, keepdims=True) + 1e-05)
    return center * scale, scale


def norm_back(upstream, normed, scale, gains_row):
    grad = upstream * gains_row
    return scale * (
        grad
        - jnp.mean(grad, -1, keepdims=True)
        - normed * jnp.mean(grad * normed, -1, keepdims=True)
    )


def project_blocks(inputs, parts, lanes, width, name):
    def body(ins, loaded, outs, _):
        for kind, weight in enumerate(loaded):
            write_blocks(
                outs[0], dot(ins[0][...], weight.value()).astype(jnp.bfloat16), lanes, kind, width
            )

    devices, span = lax.axis_size("blk"), inputs.shape[0] // lanes
    (blocks,) = call_with_parts(
        body,
        [inputs],
        parts,
        [shape(devices, span, width * len(parts), of=jnp.bfloat16)],
        name,
    )
    return blocks


def after_self(got, tokens, gains, biases, out_part, query_part, lanes, width):
    def body(ins, loaded, outs, _):
        got_ref, tokens_ref, gains_ref, biases_ref = ins
        low_ref, normed_ref, scale_ref, hidden_ref, blocks_ref = outs
        attended = read_blocks(got_ref, lanes, 0, width)
        low_ref[...] = attended
        resid = tokens_ref[...].astype(jnp.float32) + dot(attended, loaded[0].value())
        normed, scale = normalize(resid)
        normed_ref[...] = normed
        scale_ref[...] = scale
        hidden = (normed * gains_ref[0:1] + biases_ref[0:1]).astype(jnp.bfloat16)
        hidden_ref[...] = hidden
        query = dot(hidden, loaded[1].value()).astype(jnp.bfloat16)
        write_blocks(blocks_ref, query, lanes, 0, width)

    rows = tokens.shape[0]
    return call_with_parts(
        body,
        [got, tokens, gains, biases],
        [out_part, query_part],
        [
            shape(rows, WIDTH, of=jnp.bfloat16),
            shape(rows, WIDTH),
            shape(rows, 1),
            shape(rows, WIDTH, of=jnp.bfloat16),
            shape(*got.shape, of=jnp.bfloat16),
        ],
        "after_self",
    )


def feed_forward(got, normed_in, cotangent, gains, biases, out_part, in_parts, down, outs, up, lanes, width):
    pieces = len(in_parts)
    step = in_parts[0].width

    def body(ins, loaded, refs, scratch):
        got_ref, normed_in_ref, cot_ref, gains_ref, biases_ref = ins
        (
            output_ref,
            low_ref,
            mixed_ref,
            adapted_ref,
            dunder_ref,
            dab_ref,
            dcb_ref,
            dresid_ref,
            blocks_ref,
            norms_ref,
        ) = refs
        (slopes,) = scratch
        w_out, w_in = loaded[0], loaded[1 : 1 + pieces]
        w_down, w_ff, w_up = loaded[1 + pieces :]
        attended = read_blocks(got_ref, lanes, 0, width)
        low_ref[...] = attended
        hidden = normed_in_ref[...] * gains_ref[0:1] + biases_ref[0:1]
        normed_one, scale_one = normalize(hidden + dot(attended, w_out.value()))
        mixed = normed_one * gains_ref[1:2] + biases_ref[1:2]
        mixed_low = mixed.astype(jnp.bfloat16)
        mixed_ref[...] = mixed_low
        summed = mixed
        under = dot(mixed_low, w_down.value())
        gate = 1.0 / (1.0 + jnp.exp(-under))
        adapted = (under * gate).astype(jnp.bfloat16)
        adapted_ref[...] = adapted
        under_slope = gate * (1.0 + under * (1.0 - gate))
        summed = summed + 4.0 * dot(adapted, w_up.value())
        for piece in range(pieces):
            before = dot(mixed_low, w_in[piece].value())
            below = 0.5 + 0.5 * lax.erf(before * (0.5**0.5))
            slopes[piece] = below + before * jnp.exp(-0.5 * before * before) * (
                (2.0 * math.pi) ** -0.5
            )
            act = (before * below).astype(jnp.bfloat16)
            summed = summed + dot(act, w_ff[piece].value())
        normed_two, scale_two = normalize(summed)
        output_ref[...] = (normed_two * gains_ref[2:3] + biases_ref[2:3]).astype(jnp.bfloat16)
        upstream = cot_ref[...].astype(jnp.float32)
        norms_ref[0:1] = jnp.sum(upstream * normed_two, axis=0, keepdims=True)
        norms_ref[1:2] = jnp.sum(upstream, axis=0, keepdims=True)
        dz = norm_back(upstream, normed_two, scale_two, gains_ref[2:3])
        dzb = dz.astype(jnp.bfloat16)
        dab = (4.0 * dz).astype(jnp.bfloat16)
        dab_ref[...] = dab
        dunder = (under_slope * dot_back(dab, w_up.value())).astype(jnp.bfloat16)
        dunder_ref[...] = dunder
        dmixed = dz + dot_back(dunder, w_down.value())
        for piece in range(pieces):
            dpre = (slopes[piece] * dot_back(dzb, w_ff[piece].value())).astype(jnp.bfloat16)
            dmixed = dmixed + dot_back(dpre, w_in[piece].value())
        norms_ref[2:3] = jnp.sum(dmixed * normed_one, axis=0, keepdims=True)
        norms_ref[3:4] = jnp.sum(dmixed, axis=0, keepdims=True)
        dresid = norm_back(dmixed, normed_one, scale_one, gains_ref[1:2])
        dresid_ref[...] = dresid
        dcb = dresid.astype(jnp.bfloat16)
        dcb_ref[...] = dcb
        write_blocks(
            blocks_ref, dot_back(dcb, w_out.value()).astype(jnp.bfloat16), lanes, 0, width
        )

    rows = normed_in.shape[0]
    low = jnp.bfloat16

    def body_rows(ins, loaded, refs, scratch):
        whole_ff = loaded[2 + pieces]

        class Rows:
            def __init__(self, piece):
                self.piece = piece

            def value(self):
                return whole_ff.value()[self.piece * step : (self.piece + 1) * step]

        loaded = loaded[: 2 + pieces] + [[Rows(piece) for piece in range(pieces)], loaded[-1]]
        body(ins, loaded, refs, scratch)

    return call_with_parts(
        body_rows,
        [got, normed_in, cotangent, gains, biases],
        [out_part] + in_parts + [down, outs, up],
        [
            shape(rows, WIDTH, of=low),
            shape(rows, WIDTH, of=low),
            shape(rows, WIDTH, of=low),
            shape(rows, down.width, of=low),
            shape(rows, down.width, of=low),
            shape(rows, WIDTH, of=low),
            shape(rows, WIDTH, of=low),
            shape(rows, WIDTH),
            shape(*got.shape, of=low),
            shape(4, WIDTH),
        ],
        "feed_forward",
        [pltpu.VMEM((pieces, rows, step), jnp.float32)],
        20,
    )


def before_self(got, dresid, normed, scale, gains, query_part, out_part, lanes, width):
    def body(ins, loaded, outs, _):
        got_ref, dresid_ref, normed_ref, scale_ref, gains_ref = ins
        dcq_ref, dr_ref, dsb_ref, blocks_ref, norms_ref = outs
        dcq = read_blocks(got_ref, lanes, 0, width)
        dcq_ref[...] = dcq
        dhidden = dresid_ref[...] + dot_back(dcq, loaded[0].value())
        normed = normed_ref[...]
        norms_ref[0:1] = jnp.sum(dhidden * normed, axis=0, keepdims=True)
        norms_ref[1:2] = jnp.sum(dhidden, axis=0, keepdims=True)
        dr = norm_back(dhidden, normed, scale_ref[...], gains_ref[0:1])
        dr_ref[...] = dr
        dsb = dr.astype(jnp.bfloat16)
        dsb_ref[...] = dsb
        grad = dot_back(dsb, loaded[1].value()).astype(jnp.bfloat16)
        write_blocks(blocks_ref, grad, lanes, 0, width)

    rows = dresid.shape[0]
    return call_with_parts(
        body,
        [got, dresid, normed, scale, gains],
        [query_part, out_part],
        [
            shape(rows, WIDTH, of=jnp.bfloat16),
            shape(rows, WIDTH),
            shape(rows, WIDTH, of=jnp.bfloat16),
            shape(*got.shape, of=jnp.bfloat16),
            shape(2, WIDTH),
        ],
        "before_self",
    )


def input_grad(got, start, parts, lanes, span, width, name):
    def body(ins, loaded, outs, _):
        total = None
        for kind, weight in enumerate(loaded):
            values = read_blocks(ins[0], lanes, kind, width)
            term = dot_back(values, weight.value())
            total = term if total is None else total + term
        outs[0][...] = total if len(ins) == 1 else total + ins[1][...]

    rows = span * lanes
    return call_with_parts(
        body,
        [got] if start is None else [got, start],
        parts,
        [shape(rows, WIDTH)],
        name,
    )


def shards(
    tokens,
    encoder,
    cotangent,
    self_in,
    self_out,
    cross_q,
    cross_kv,
    cross_out,
    ffn_in,
    ffn_out,
    adapt_down,
    adapt_up,
    norm_gain,
    norm_bias,
    tgt_lengths,
    src_lengths,
):
    lanes, span, _ = tokens.shape
    rows = lanes * span
    width = WIDTH * lanes // lax.axis_size("blk")
    own_row = lax.axis_index("blk") // (lax.axis_size("blk") // lanes)
    tgt_ends = jnp.cumsum(lax.dynamic_index_in_dim(tgt_lengths, own_row, 0, keepdims=False))
    src_ends = jnp.cumsum(lax.dynamic_index_in_dim(src_lengths, own_row, 0, keepdims=False))
    flat_tokens = tokens.reshape(rows, WIDTH)
    flat_encoder = encoder.reshape(rows, WIDTH)
    frozen = [ffn_in, adapt_down, ffn_out, adapt_up, cross_out]

    if paired():
        packed = gather_packed(pack_halves(frozen))
        self_packed = pack_halves([self_in])
        token_row, stages = gather_row(tokens)
        self_heads, pair_heads = head_columns([self_in, cross_kv], [3, 2])
        out_shard, query_shard = after((self_out, cross_q), stages[1])
        encoder_block = after(encoder, stages[1])
        self_qkv = project_row(token_row, self_heads, "self_in")
        out_source, query_source = gather_flips([out_shard, query_shard], "xy", self_qkv)
        encoder_row, encoder_stages = gather_row(
            encoder_block, self_qkv, (out_source.arrays[1], query_source.arrays[1])
        )
        self_qkv = after(self_qkv, out_source.stages[0], query_source.stages[0])
        pair_own = project_row(encoder_row, pair_heads, "cross_kv")
    else:
        (self_source, pair_source, out_source, query_source) = gather_flips(
            [self_in, cross_kv, self_out, cross_q], "xyxy"
        )
        self_parts = [columns_of((self_source, WIDTH * kind, WIDTH)) for kind in range(3)]
        pair_parts = [columns_of((pair_source, WIDTH * kind, WIDTH)) for kind in range(2)]
        self_qkv = as_rows(
            exchange(project_blocks(flat_tokens, self_parts, lanes, width, "self_in"))
        )
        pair_own = as_rows(
            exchange(project_blocks(flat_encoder, pair_parts, lanes, width, "cross_kv"))
        )
    self_out_part = columns_of((out_source, 0, WIDTH))
    query_part = columns_of((query_source, 0, WIDTH))

    self_mid, self_full, self_lse = attn_forward(
        tgt_ends, tgt_ends, self_qkv, self_qkv, width, True
    )
    self_sent = after(self_mid, out_source.stages[1], query_source.stages[1])
    if paired():
        self_sent = after(self_sent, encoder_stages[0])
    self_back = exchange(as_blocks(self_sent))
    if paired():
        self_back = after(self_back, encoder_stages[1])
    self_low, normed, scale, hidden_low, query_blocks = after_self(
        self_back,
        flat_tokens,
        norm_gain,
        norm_bias,
        self_out_part,
        query_part,
        lanes,
        width,
    )
    cross_own = as_rows(exchange(query_blocks))
    cross_mid, cross_full, cross_lse = attn_forward(
        tgt_ends, src_ends, cross_own, pair_own, width, False
    )
    cross_back = exchange(as_blocks(cross_mid))
    ready = after(packed, cross_mid) if paired() else None
    ff_parts, down_parts, ffo_parts, up_parts, (cross_out_part,) = packed_parts(frozen, ready)
    if paired():
        self_packed = gather_packed(after(self_packed, cross_back))
    (
        output,
        cross_low,
        mixed_low,
        adapter_low,
        grad_under,
        adapt_low,
        cross_branch_low,
        grad_resid_two,
        cross_grad_blocks,
        norms_high,
    ) = feed_forward(
        cross_back,
        normed,
        cotangent.reshape(rows, WIDTH),
        norm_gain,
        norm_bias,
        cross_out_part,
        ff_parts,
        down_parts[0],
        ffo_parts[0],
        up_parts[0],
        lanes,
        width,
    )
    high_groups = [
        [(cross_low, cross_branch_low)],
        [(mixed_low, grad_under), (adapter_low, adapt_low)],
    ]
    high_terms = [grad_terms(pairs) for pairs in high_groups]
    high_orders = [(2, 1, 4, 8), (1, 2, 4, 8)]
    high_terms, high_stages = scatter_chips(high_terms, high_orders, 0, 2)
    cross_dq, cross_dkv = attn_backward(
        tgt_ends,
        src_ends,
        cross_own,
        pair_own,
        as_rows(after(exchange(cross_grad_blocks), high_stages[0])),
        cross_full,
        cross_lse,
        False,
    )
    cross_dq_got = after(exchange(as_blocks(cross_dq)), high_stages[1])
    if paired():
        dkv_late = after(cross_dkv, high_stages[1])
        pair_terms = row_back(dkv_late, pair_heads, "encoder_grad")
        kv_sent = row_grad(encoder_row, dkv_late, "cross_kv_grad")
        cross_dq_got = after(cross_dq_got, pair_terms, kv_sent)
    cq_low, grad_resid_one, self_branch_low, self_grad_blocks, norms_low = before_self(
        cross_dq_got,
        grad_resid_two,
        normed,
        scale,
        norm_gain,
        query_part,
        self_out_part,
        lanes,
        width,
    )
    norms = jnp.concatenate([norms_low, norms_high], axis=0)
    self_upstream = after(exchange(self_grad_blocks), high_stages[2])
    (self_grads,) = attn_backward(
        tgt_ends,
        tgt_ends,
        self_qkv,
        self_qkv,
        as_rows(self_upstream),
        self_full,
        self_lse,
        True,
        joined=True,
    )
    mid_groups = after(
        [[(hidden_low, cq_low)], [(self_low, self_branch_low)]], self_grads
    )
    mid_terms = [grad_terms(pairs) for pairs in mid_groups]
    mid_orders = [(2, 1, 4, 8), (1, 2, 4, 8)]
    if paired():
        (self_parts,) = packed_parts([self_in], after(self_packed, self_grads))
        self_got = exchange(as_blocks(self_grads))
        self_sent = row_grad(token_row, self_grads, "self_in_grad")
        encoder_grad, _ = reduce_row(pair_terms, {1: self_grads})
        encoder_grad = encoder_grad.reshape(rows, WIDTH)
        mid_terms, mid_stages = scatter_chips(mid_terms, mid_orders, 0, 4)
        high_terms, _ = scatter_chips(after(high_terms, self_grads), high_orders, 2, 4)
        chunks = [
            array[:, :, first : first + width]
            for array in (self_sent, kv_sent)
            for first in range(0, array.shape[2], width)
        ]
        partials = norms.astype(jnp.bfloat16).reshape(1, 48, width)
        chunks.append(jnp.broadcast_to(partials, (16, 48, width)))
        sent = after(jnp.concatenate(chunks, axis=1), self_got, mid_stages[1])
        got = exchange(sent)
        (tokens_grad,) = input_grad(
            self_got, grad_resid_one, self_parts, lanes, span, width, "tokens_grad"
        )
        got = after(got, tokens_grad)
        chunks = [got[:, first : first + 32] for first in range(0, 160, 32)]
        grad_self_in = finish_row_grad(jnp.concatenate(chunks[:3], axis=2), 3)
        grad_cross_kv = finish_row_grad(jnp.concatenate(chunks[3:], axis=2), 2)
        norms = jnp.sum(got[:, 160:].astype(jnp.float32), axis=0).reshape(6, WIDTH)
        norms = norms + swap_core(norms)
    else:
        pair_got = exchange(as_blocks(cross_dkv))
        self_got = exchange(as_blocks(self_grads))
        (encoder_grad,) = input_grad(
            pair_got, None, pair_parts, lanes, span, width, "encoder_grad"
        )
        (tokens_grad,) = input_grad(
            self_got, grad_resid_one, self_parts, lanes, span, width, "tokens_grad"
        )
        pair_low = pair_got.reshape(lanes, -1, span, 2, width).transpose(0, 2, 3, 1, 4)
        self_low_grads = self_got.reshape(lanes, -1, span, 3, width).transpose(0, 2, 3, 1, 4)
        grad_cross_kv = weight_grad(flat_encoder, pair_low.reshape(rows, 2 * WIDTH))
        grad_self_in = weight_grad(flat_tokens, self_low_grads.reshape(rows, 3 * WIDTH))
        norms = lax.psum(norms, ("dp", "blk"))
    (grad_cross_q,), (grad_self_out,) = finish_terms(mid_groups, mid_terms)
    (grad_cross_out,), (grad_adapt_down, grad_adapt_up) = finish_terms(high_groups, high_terms)
    return (
        output.reshape(lanes, span, WIDTH),
        tokens_grad.reshape(lanes, span, WIDTH),
        encoder_grad.reshape(lanes, span, WIDTH),
        grad_self_in,
        grad_self_out,
        grad_cross_q,
        grad_cross_kv,
        grad_cross_out,
        grad_adapt_down,
        grad_adapt_up,
        jnp.stack([norms[0], norms[4], norms[2]]),
        jnp.stack([norms[1], norms[5], norms[3]]),
    )


def solution(mesh):
    placed = (
        P("dp", "blk", None),
        P("dp", "blk", None),
        P("dp", "blk", None),
        P("blk", None),
        P("blk", None),
        P("blk", None),
        P("blk", None),
        P("blk", None),
        P("blk", None),
        P("blk", None),
        P("blk", None),
        P("blk", None),
        P(),
        P(),
        P("dp", None),
        P("dp", None),
    )
    return jax.shard_map(
        shards,
        mesh=mesh,
        in_specs=placed,
        out_specs=(
            P("dp", "blk", None),
            P("dp", "blk", None),
            P("dp", "blk", None),
            P("blk", None),
            P("blk", None),
            P("blk", None),
            P("blk", None),
            P("blk", None),
            P("blk", None),
            P("blk", None),
            P(),
            P(),
        ),
        check_vma=False,
    )
```

```python
import functools
import math

import jax
import jax.numpy as jnp
from jax import lax
from jax.experimental import pallas as pl
from jax.experimental.pallas import tpu as pltpu
from jax.sharding import PartitionSpec as P

HEADS = 16
HEAD_DIM = 64
WIDTH = HEADS * HEAD_DIM


NEG = -1e30
VMEM_BYTES = 56 * 1024 * 1024


def cost(microseconds):
    return pl.CostEstimate(
        flops=int(microseconds * 0.4e9),
        bytes_accessed=int(microseconds * 1.2e6),
        transcendentals=0,
    )


def paired():
    return lax.axis_size("blk") == 16 and lax.axis_size("dp") == 2


def swap_core(block):
    cores = lax.axis_size("dp")
    return lax.ppermute(block, "dp", [(i ^ 1, i) for i in range(cores)])


def flip(block, bit):
    chips = lax.axis_size("blk")
    return lax.ppermute(block, "blk", [(i ^ bit, i) for i in range(chips)])


FLIPS = (8, 4, 2, 1)


def with_flip(block, bit):
    return jnp.stack([block, flip(block, bit)])


def own_half(values, which):
    half = values.shape[1] // 2
    return lax.dynamic_slice_in_dim(values, which * half, half, 1)


def scatter_chips(terms, orders, first, last, holds=None):
    if not paired():
        return terms, [terms] * 5
    own = lax.axis_index("blk")

    def fold(blocks, left, bit):
        axis, place = left.index(bit), (own // bit) % 2
        kept = lax.dynamic_index_in_dim(blocks, place, axis, keepdims=False)
        sent = lax.dynamic_index_in_dim(blocks, 1 - place, axis, keepdims=False)
        got = flip(sent, bit)
        return (kept.astype(jnp.float32) + got.astype(jnp.float32)).astype(jnp.bfloat16)

    if first == 0:
        terms = [blocks.reshape(2, 2, 2, 2, *blocks.shape[1:]) for blocks in terms]
    stages = [terms[0]]
    for stage in range(first, last):
        if holds and stage in holds:
            terms = after(terms, holds[stage])
        terms = [
            fold(blocks, [bit for bit in FLIPS if bit not in order[:stage]], order[stage])
            for blocks, order in zip(terms, orders)
        ]
        stages.append(terms[0])
    return terms, stages


CHUNK = 256


def grad_terms(pairs):
    if not paired():
        return pairs[0][1]
    core = lax.axis_index("dp")
    packed = []
    for inputs, upstream in pairs:
        both = jnp.concatenate([inputs, swap_core(inputs)], axis=0)
        half = jnp.concatenate(
            [own_half(upstream, core), swap_core(own_half(upstream, 1 - core))], axis=0
        )
        term = lax.dot_general(
            both, half, (((0,), (0,)), ((), ())), preferred_element_type=jnp.float32
        ).astype(jnp.bfloat16)
        rows = term.shape[0] // 16
        chunks = term.shape[1] // CHUNK
        packed += [
            term[:, c * CHUNK : (c + 1) * CHUNK].reshape(16, rows, CHUNK) for c in range(chunks)
        ]
    return jnp.concatenate(packed, axis=1)


def finish_terms(groups, terms):
    if not paired():
        return [[weight_grad(inputs, upstream) for inputs, upstream in pairs] for pairs in groups]
    core = lax.axis_index("dp")
    mine = jnp.concatenate(terms, axis=0)
    other = swap_core(mine)
    low = jnp.where(core == 0, mine, other).astype(jnp.float32)
    high = jnp.where(core == 0, other, mine).astype(jnp.float32)
    found, place = [], 0
    for pairs in groups:
        found.append([])
        for inputs, upstream in pairs:
            rows = inputs.shape[1] // 16
            chunks = upstream.shape[1] // 2 // CHUNK
            spots = [slice(place + c * rows, place + (c + 1) * rows) for c in range(chunks)]
            found[-1].append(
                jnp.concatenate(
                    [low[spot] for spot in spots] + [high[spot] for spot in spots], axis=1
                )
            )
            place += rows * chunks
    return found


def weight_grad(inputs, upstream):
    scattered = lax.psum_scatter(
        lax.dot_general(
            inputs, upstream, (((0,), (0,)), ((), ())), preferred_element_type=jnp.float32
        ).astype(jnp.bfloat16),
        "blk",
        scatter_dimension=0,
        tiled=True,
    )
    return lax.psum(scattered, "dp").astype(jnp.float32)


class Source:
    def __init__(self, kind, arrays, first_flip="x", column=None):
        self.kind, self.arrays, self.first_flip = kind, arrays, first_flip
        self.stages = arrays[:1] * 3 if column is None else [column] + arrays[:2]


class Part:
    def __init__(self, rows, width, spots):
        self.rows, self.width, self.spots = rows, width, spots

    def scratch(self):
        return pltpu.VMEM((2, 2, 2, 2, 2, self.rows // 32, self.width), jnp.bfloat16)

    def start(self, refs_of, place, dst, sem):
        z1, z0, y, x, core = [place[axis] for axis in range(5)]
        high = self.rows // 32
        for source, first_row, first_col, at_col, width in self.spots:
            refs = refs_of(source)
            cols = slice(first_col, first_col + width)
            into = slice(at_col, at_col + width)
            if source.kind == "whole":
                pltpu.make_async_copy(
                    refs[0].at[:, :, :, :, :, :, cols], dst.at[:, :, :, :, :, :, into], sem
                ).start()
            elif source.kind == "cores":
                for which in range(2):
                    owner = core if which == 0 else 1 - core
                    pltpu.make_async_copy(
                        refs[which].at[:, :, :, :, first_row : first_row + high, cols],
                        dst.at[:, :, :, :, owner, :, into],
                        sem,
                    ).start()
            else:
                for which in range(4):
                    owner = core if which < 2 else 1 - core
                    for near, at_y, at_x in flipped(source.first_flip, which % 2, y, x):
                        for up, at_z1, at_z0 in four(z1, z0):
                            pltpu.make_async_copy(
                                refs[which].at[near, up[0], up[1], :, cols],
                                dst.at[at_z1, at_z0, at_y, at_x, owner, :, into],
                                sem,
                            ).start()


def four(z1, z0):
    return [
        ((low, high), z1 if high == 0 else 1 - z1, z0 if low == 0 else 1 - z0)
        for low in range(2)
        for high in range(2)
    ]


def flipped(first_flip, beyond, y, x):
    found = []
    for near in range(2):
        a, b = (near, beyond) if first_flip == "x" else (beyond, near)
        found.append((near, y if b == 0 else 1 - y, x if a == 0 else 1 - x))
    return found


def after(value, *others):
    return lax.optimization_barrier((value, *others))[0]


def gather_flips(shards, first_flips, hold=None):
    if not paired():
        full = [lax.all_gather(shard, "blk", axis=0, tiled=True) for shard in shards]
        return [
            Source("whole", [array.reshape(2, 2, 2, 2, 2, array.shape[0] // 32, array.shape[1])])
            for array in full
        ]
    core = lax.axis_index("dp")
    columns = []
    for shard in shards:
        rows = shard.shape[0]
        own = lax.dynamic_slice_in_dim(shard, core * (rows // 2), rows // 2, 0)
        columns.append(with_flip(with_flip(own, 8), 4))
    sources, bits = [], {"x": (1, 2), "y": (2, 1)}
    if hold is not None:
        columns = after(columns, hold)
    planes = [
        with_flip(column, bits[first][0]) for column, first in zip(columns, first_flips)
    ]
    for column, plane, first in zip(columns, planes, first_flips):
        beyond = flip(plane, bits[first][1])
        sources.append(
            Source("flips", [plane, beyond, swap_core(plane), swap_core(beyond)], first, column)
        )
    return sources


class RowPart:
    def __init__(self, sources, span):
        self.span = span
        self.rows, self.width = 16 * span, WIDTH
        self.spots = [(source,) for source in sources]

    def scratch(self):
        return pltpu.VMEM((2, 2, 2, 2, self.span, WIDTH), jnp.bfloat16)

    def start(self, refs_of, place, dst, sem):
        z1, z0, y, x = [place[axis] for axis in range(4)]
        half = WIDTH // 2
        for side, (source,) in enumerate(self.spots):
            refs = refs_of(source)
            for beyond in range(2):
                for near, at_y, at_x in flipped(source.first_flip, beyond, y, x):
                    for up, at_z1, at_z0 in four(z1, z0):
                        pltpu.make_async_copy(
                            refs[beyond].at[near, up[0], up[1]],
                            dst.at[at_z1, at_z0, at_y, at_x, :, side * half : (side + 1) * half],
                            sem,
                        ).start()


def gather_row(block, hold_near=None, hold=None):
    row = lax.axis_index("blk") // 8
    own = lax.dynamic_index_in_dim(block, row, 0, keepdims=False)
    other = lax.dynamic_index_in_dim(block, 1 - row, 0, keepdims=False)
    pair = jnp.stack([own, flip(other, 8)])
    if hold_near is not None:
        pair = after(pair, hold_near)
    column = with_flip(pair, 4)
    stages, sources = [pair, column], []
    if hold is not None:
        column = after(column, hold)
    half = WIDTH // 2
    planes = [with_flip(column[..., :half], 1), with_flip(column[..., half:], 2)]
    for plane, first, bit in zip(planes, "xy", (2, 1)):
        sources.append(Source("row", [plane, flip(plane, bit)], first))
    stages += [planes, [source.arrays[1] for source in sources]]
    return RowPart(sources, block.shape[1]), stages


def head_columns(shards, kinds):
    core = lax.axis_index("dp")
    blocks, widths = [], [128 * kind for kind in kinds]
    for shard, kind in zip(shards, kinds):
        own = lax.dynamic_slice_in_dim(shard, core * 32, 32, 0)
        own = own.reshape(32, kind, 8, 128).transpose(2, 0, 1, 3)
        blocks.append(own.reshape(8, 32, kind * 128))
    blocks = jnp.concatenate(blocks, axis=2)
    mine = exchange(jnp.concatenate([blocks, blocks], axis=0))
    mine = mine.reshape(2, 2, 2, 2, 32, sum(widths))
    source = Source("cores", [mine, swap_core(mine)])
    parts, place = [], 0
    for width in widths:
        parts.append(Part(1024, width, [(source, 0, place, 0, width)]))
        place += width
    return parts


def project_row(row_part, head_part, name):
    def body(ins, loaded, outs, _):
        weight = loaded[1].value()
        inputs = loaded[0].value()
        for first in range(0, row_part.rows, 256):
            rows = slice(first, first + 256)
            outs[0][rows, :] = dot(inputs[rows], weight).astype(jnp.bfloat16)

    (found,) = call_with_parts(
        body,
        [],
        [row_part, head_part],
        [shape(row_part.rows, head_part.width, of=jnp.bfloat16)],
        name,
    )
    return found


def row_grad(row_part, upstream, name):
    columns = upstream.shape[1]

    def body(ins, loaded, outs, _):
        core = ins[1][0]
        inputs = loaded[0].value()
        grads = []
        for first in range(0, columns, 128):
            grads.append(pair_dot(ins[0][:, first : first + 128], inputs, 0, 0).T)
        grad = jnp.concatenate(grads, axis=1).astype(jnp.bfloat16).reshape(16, 2, 32, columns)
        outs[0][core] = grad[:, 0]
        outs[0][1 - core] = grad[:, 1]

    (terms,) = call_with_parts(
        body,
        [upstream],
        [row_part],
        [shape(2, 16, 32, columns, of=jnp.bfloat16)],
        name,
        scalars=[lax.axis_index("dp").reshape(1).astype(jnp.int32)],
    )
    got = swap_core(terms[1])
    return (terms[0].astype(jnp.float32) + got.astype(jnp.float32)).astype(jnp.bfloat16)


def row_back(upstream, head_part, name):
    def body(ins, loaded, outs, _):
        weight = loaded[0].value()
        for first in range(0, ins[0].shape[0], 256):
            rows = slice(first, first + 256)
            outs[0][rows, :] = dot_back(ins[0][rows, :], weight).astype(jnp.bfloat16)

    (terms,) = call_with_parts(
        body, [upstream], [head_part], [shape(upstream.shape[0], WIDTH, of=jnp.bfloat16)], name
    )
    return terms


def reduce_row(terms, holds=None):
    blocks = terms.reshape(16, terms.shape[0] // 16, WIDTH)
    (both,), stages = scatter_chips([blocks], [(1, 2, 4, 8)], 0, 3, holds)
    row = lax.axis_index("blk") // 8
    kept = lax.dynamic_index_in_dim(both, row, 0, keepdims=False)
    got = flip(lax.dynamic_index_in_dim(both, 1 - row, 0, keepdims=False), 8)
    found = jnp.stack([jnp.where(row == 0, kept, got), jnp.where(row == 0, got, kept)])
    return found.astype(jnp.float32), stages


def finish_row_grad(got, kinds):
    total = jnp.sum(got.reshape(2, 8, 32, kinds, 128).astype(jnp.float32), axis=0)
    mine = total.astype(jnp.bfloat16).transpose(1, 2, 0, 3).reshape(32, kinds * WIDTH)
    other = swap_core(mine)
    core = lax.axis_index("dp")
    low = jnp.where(core == 0, mine, other)
    high = jnp.where(core == 0, other, mine)
    return jnp.concatenate([low, high], axis=0).astype(jnp.float32)


def columns_of(*pieces):
    spots, place = [], 0
    for source, first, width in pieces:
        spots.append((source, 0, first, place, width))
        place += width
    return Part(1024, place, spots)


PACK = 512


def pack_halves(shards):
    places = [
        (index, shard.shape[0] // 2, first)
        for index, shard in enumerate(shards)
        for first in range(0, shard.shape[1], PACK)
    ]

    def body(core, *refs):
        out_ref, place = refs[-1], 0
        for index, high, first in places:
            start = pl.multiple_of(core[0] * high, 16)
            out_ref[place : place + high, :] = refs[index][pl.ds(start, high), first : first + PACK]
            place += high

    return pl.pallas_call(
        body,
        out_shape=shape(sum(high for _, high, _ in places), PACK, of=jnp.bfloat16),
        in_specs=[smem_spec()] + [vmem_spec()] * len(shards),
        out_specs=vmem_spec(),
        compiler_params=pltpu.CompilerParams(vmem_limit_bytes=VMEM_BYTES),
        cost_estimate=cost(2),
        name="pack_halves",
    )(lax.axis_index("dp").reshape(1).astype(jnp.int32), *shards)


def gather_packed(packed):
    return lax.all_gather(packed, "blk", axis=0)


def packed_parts(shards, mine):
    if not paired():
        found = []
        for source, shard in zip(gather_flips(shards, "x" * len(shards)), shards):
            rows, columns = 32 * source.arrays[0].shape[5], shard.shape[1]
            step = min(columns, 1024)
            found.append(
                [
                    Part(rows, step, [(source, 0, first, 0, step)])
                    for first in range(0, columns, step)
                ]
            )
        return found
    spots, place = [], 0
    for shard in shards:
        high = shard.shape[0] // 2
        places = []
        for first in range(0, shard.shape[1], PACK):
            places.append(place)
            place += high
        spots.append((shard.shape[0] * 16, places))
    mine = mine.reshape(2, 2, 2, 2, place, PACK)
    source = Source("cores", [mine, swap_core(mine)])
    found = []
    for rows, places in spots:
        parts = []
        for first in range(0, len(places), 2):
            two = places[first : first + 2]
            parts.append(
                Part(
                    rows,
                    PACK * len(two),
                    [(source, row, 0, PACK * side, PACK) for side, row in enumerate(two)],
                )
            )
        found.append(parts)
    return found


def place_now():
    own, core = lax.axis_index("blk"), lax.axis_index("dp")
    bits = [(own // bit) % 2 for bit in FLIPS]
    return jnp.stack(bits + [core]).astype(jnp.int32)


class Loaded:
    def __init__(self, part, dst, sem):
        self.part, self.dst, self.sem, self.here = part, dst, sem, False

    def value(self):
        if not self.here:
            pltpu.make_async_copy(self.dst, self.dst, self.sem).wait()
            self.here = True
        return self.dst[...].reshape(self.part.rows, self.part.width)


def call_with_parts(body, inputs, parts, outputs, name, scratch=(), takes=5, scalars=()):
    sources = []
    for part in parts:
        sources += [spot[0] for spot in part.spots if spot[0] not in sources]
    arrays = [array for source in sources for array in source.arrays]

    def kernel(place, *refs):
        refs = list(refs)
        ins = [refs.pop(0) for _ in (*inputs, *scalars)]
        pieces = [[refs.pop(0) for _ in source.arrays] for source in sources]
        outs = [refs.pop(0) for _ in outputs]
        dsts = [refs.pop(0) for _ in parts]
        sems = refs.pop(0)
        loaded = []
        for index, part in enumerate(parts):
            part.start(
                lambda source: pieces[sources.index(source)], place, dsts[index], sems.at[index]
            )
            loaded.append(Loaded(part, dsts[index], sems.at[index]))
        body(ins, loaded, outs, refs)

    return pl.pallas_call(
        kernel,
        out_shape=tuple(outputs),
        in_specs=[smem_spec()]
        + [vmem_spec()] * len(inputs)
        + [smem_spec()] * len(scalars)
        + [pl.BlockSpec(memory_space=pl.ANY)] * len(arrays),
        out_specs=(vmem_spec(),) * len(outputs),
        scratch_shapes=[part.scratch() for part in parts]
        + [pltpu.SemaphoreType.DMA((len(parts),))]
        + list(scratch),
        compiler_params=pltpu.CompilerParams(vmem_limit_bytes=VMEM_BYTES),
        cost_estimate=cost(takes),
        name=name,
    )(place_now(), *inputs, *scalars, *arrays)


def vmem_spec():
    return pl.BlockSpec(memory_space=pltpu.VMEM)


def smem_spec():
    return pl.BlockSpec(memory_space=pltpu.SMEM)


def seg_of_pos(ends_ref, pos):
    seg = jnp.zeros(pos.shape, jnp.int32)
    for slot in range(ends_ref.shape[0]):
        seg = seg + (ends_ref[slot] <= pos).astype(jnp.int32)
    return seg


def pair_dot(left, right, left_dim, right_dim):
    return lax.dot_general(
        left, right, (((left_dim,), (right_dim,)), ((), ())), preferred_element_type=jnp.float32
    )


def seg_tables(q_ends, k_ends, span):
    seg_q = seg_of_pos(q_ends, lax.broadcasted_iota(jnp.int32, (1, span), 1))
    seg_k = seg_of_pos(k_ends, lax.broadcasted_iota(jnp.int32, (span, 1), 0))
    return seg_q, seg_k


def masked_scores(keys, queries, seg_q, seg_k, first, causal):
    scores = pair_dot(keys, queries, 1, 1)
    allowed = seg_k == seg_q
    if causal:
        key_pos = lax.broadcasted_iota(jnp.int32, scores.shape, 0)
        query_pos = first + lax.broadcasted_iota(jnp.int32, scores.shape, 1)
        allowed = allowed & (key_pos <= query_pos)
    return jnp.where(allowed, scores, NEG)


def attn_forward_body(causal, width, q_ends, k_ends, q_ref, kv_ref, low_ref, full_ref, lse_ref):
    span = q_ref.shape[0]
    step = math.gcd(span, 256)
    heads = width // HEAD_DIM
    seg_q, seg_k = seg_tables(q_ends, k_ends, span)
    key_at = kv_ref.shape[1] - 2 * width
    scaled = q_ref[:, :width] * jnp.bfloat16(HEAD_DIM ** (-0.5))
    keys = kv_ref[:, key_at : key_at + width]
    values = kv_ref[:, key_at + width : key_at + 2 * width]
    for first in range(0, span, step):
        reach = first + step if causal else span
        parts = []
        for head in range(heads):
            cols = slice(head * HEAD_DIM, (head + 1) * HEAD_DIM)
            scores = masked_scores(
                keys[:reach, cols],
                scaled[first : first + step, cols],
                seg_q[:, first : first + step],
                seg_k[:reach],
                first,
                causal,
            )
            top = jnp.max(scores, axis=0, keepdims=True)
            probs = jnp.exp(scores - top)
            total = jnp.sum(probs, axis=0, keepdims=True)
            mixed = pair_dot(values[:reach, cols], probs.astype(jnp.bfloat16), 0, 0)
            parts.append(mixed / total)
            lse_ref[head : head + 1, first : first + step] = top + jnp.log(total)
        joined = jnp.concatenate(parts, axis=0).T
        full_ref[first : first + step, :] = joined
        low_ref[first : first + step, :] = joined.astype(jnp.bfloat16)


def attn_forward(q_ends, k_ends, queries, keys_values, width, causal):
    span = queries.shape[0]
    return pl.pallas_call(
        functools.partial(attn_forward_body, causal, width),
        out_shape=(
            jax.ShapeDtypeStruct((span, width), jnp.bfloat16),
            jax.ShapeDtypeStruct((span, width), jnp.float32),
            jax.ShapeDtypeStruct((width // HEAD_DIM, span), jnp.float32),
        ),
        in_specs=[smem_spec(), smem_spec()] + [vmem_spec()] * 2,
        out_specs=(vmem_spec(),) * 3,
        compiler_params=pltpu.CompilerParams(vmem_limit_bytes=VMEM_BYTES),
        cost_estimate=cost(8),
        name="attn_forward",
    )(q_ends, k_ends, queries, keys_values)


def attn_backward_body(
    causal,
    width,
    q_ends,
    k_ends,
    q_ref,
    kv_ref,
    up_ref,
    full_ref,
    lse_ref,
    *outs,
):
    dq_ref, dkv_ref = outs[0], outs[-3]
    dk_sum, dv_sum = outs[-2:]
    span = q_ref.shape[0]
    step = math.gcd(span, 256)
    heads = width // HEAD_DIM
    seg_q, seg_k = seg_tables(q_ends, k_ends, span)
    key_at = kv_ref.shape[1] - 2 * width
    scaled = q_ref[:, :width] * jnp.bfloat16(HEAD_DIM ** (-0.5))
    keys = kv_ref[:, key_at : key_at + width]
    values = kv_ref[:, key_at + width : key_at + 2 * width]
    upstream = up_ref[...]
    dk_sum[...] = jnp.zeros_like(dk_sum)
    dv_sum[...] = jnp.zeros_like(dv_sum)
    for first in range(0, span, step):
        reach = first + step if causal else span
        rows = slice(first, first + step)
        product = (upstream[rows].astype(jnp.float32) * full_ref[rows, :]).T
        parts = []
        for head in range(heads):
            cols = slice(head * HEAD_DIM, (head + 1) * HEAD_DIM)
            delta = jnp.sum(product[cols], axis=0, keepdims=True)
            scores = masked_scores(
                keys[:reach, cols], scaled[rows, cols], seg_q[:, rows], seg_k[:reach], first, causal
            )
            probs = jnp.exp(scores - lse_ref[head : head + 1, rows])
            dv_sum[head, :reach] += pair_dot(
                probs.astype(jnp.bfloat16), upstream[rows, cols], 1, 0
            )
            grad_probs = pair_dot(values[:reach, cols], upstream[rows, cols], 1, 1)
            grad_scores = (probs * (grad_probs - delta)).astype(jnp.bfloat16)
            dk_sum[head, :reach] += pair_dot(grad_scores, scaled[rows, cols], 1, 0)
            parts.append(pair_dot(keys[:reach, cols], grad_scores, 0, 0))
        joined = jnp.concatenate(parts, axis=0).T * HEAD_DIM ** (-0.5)
        dq_ref[rows, :width] = joined.astype(jnp.bfloat16)
    sums = [dk_sum[head] for head in range(heads)] + [dv_sum[head] for head in range(heads)]
    kv_at = dkv_ref.shape[1] - 2 * width
    dkv_ref[:, kv_at:] = jnp.concatenate(sums, axis=1).astype(jnp.bfloat16)


def attn_backward(
    q_ends, k_ends, queries, keys_values, upstream, full, lse, causal, joined=False
):
    span, width = upstream.shape
    kinds = [3] if joined else [1, 2]
    heads = width // HEAD_DIM
    return pl.pallas_call(
        functools.partial(attn_backward_body, causal, width),
        out_shape=[jax.ShapeDtypeStruct((span, kind * width), jnp.bfloat16) for kind in kinds],
        in_specs=[smem_spec(), smem_spec()] + [vmem_spec()] * 5,
        out_specs=[vmem_spec()] * len(kinds),
        scratch_shapes=[pltpu.VMEM((heads, span, HEAD_DIM), jnp.float32)] * 2,
        compiler_params=pltpu.CompilerParams(vmem_limit_bytes=VMEM_BYTES),
        cost_estimate=cost(8),
        name="attn_backward",
    )(q_ends, k_ends, queries, keys_values, upstream, full, lse)


def exchange(blocks):
    return lax.all_to_all(blocks, "blk", 0, 0, tiled=True)


def as_rows(blocks):
    return blocks.reshape(blocks.shape[0] * blocks.shape[1], blocks.shape[2])


def as_blocks(rows):
    devices = lax.axis_size("blk")
    return rows.reshape(devices, rows.shape[0] // devices, rows.shape[1])


def write_blocks(out_ref, values, lanes, kind, width):
    span = values.shape[0] // lanes
    for group in range(WIDTH // width):
        for lane in range(lanes):
            out_ref[lane * (WIDTH // width) + group, :, kind * width : (kind + 1) * width] = values[
                lane * span : (lane + 1) * span, group * width : (group + 1) * width
            ]


def read_blocks(got_ref, lanes, kind, width):
    groups = got_ref.shape[0] // lanes
    cols = slice(kind * width, (kind + 1) * width)
    rows = [
        jnp.concatenate([got_ref[lane * groups + group, :, cols] for group in range(groups)], axis=1)
        for lane in range(lanes)
    ]
    return jnp.concatenate(rows, axis=0)


def dot(left, right):
    return pair_dot(left, right, 1, 0)


def dot_back(left, right):
    return pair_dot(left, right, 1, 1)


def shape(*sizes, of=jnp.float32):
    return jax.ShapeDtypeStruct(sizes, of)


def normalize(values):
    center = values - jnp.mean(values, -1, keepdims=True)
    scale = lax.rsqrt(jnp.mean(center * center, -1, keepdims=True) + 1e-05)
    return center * scale, scale


def norm_back(upstream, normed, scale, gains_row):
    grad = upstream * gains_row
    return scale * (
        grad
        - jnp.mean(grad, -1, keepdims=True)
        - normed * jnp.mean(grad * normed, -1, keepdims=True)
    )


def project_blocks(inputs, parts, lanes, width, name):
    def body(ins, loaded, outs, _):
        for kind, weight in enumerate(loaded):
            write_blocks(
                outs[0], dot(ins[0][...], weight.value()).astype(jnp.bfloat16), lanes, kind, width
            )

    devices, span = lax.axis_size("blk"), inputs.shape[0] // lanes
    (blocks,) = call_with_parts(
        body,
        [inputs],
        parts,
        [shape(devices, span, width * len(parts), of=jnp.bfloat16)],
        name,
    )
    return blocks


def after_self(got, tokens, gains, biases, out_part, query_part, lanes, width):
    def body(ins, loaded, outs, _):
        got_ref, tokens_ref, gains_ref, biases_ref = ins
        low_ref, normed_ref, scale_ref, hidden_ref, blocks_ref = outs
        attended = read_blocks(got_ref, lanes, 0, width)
        low_ref[...] = attended
        resid = tokens_ref[...].astype(jnp.float32) + dot(attended, loaded[0].value())
        normed, scale = normalize(resid)
        normed_ref[...] = normed
        scale_ref[...] = scale
        hidden = (normed * gains_ref[0:1] + biases_ref[0:1]).astype(jnp.bfloat16)
        hidden_ref[...] = hidden
        query = dot(hidden, loaded[1].value()).astype(jnp.bfloat16)
        write_blocks(blocks_ref, query, lanes, 0, width)

    rows = tokens.shape[0]
    return call_with_parts(
        body,
        [got, tokens, gains, biases],
        [out_part, query_part],
        [
            shape(rows, WIDTH, of=jnp.bfloat16),
            shape(rows, WIDTH),
            shape(rows, 1),
            shape(rows, WIDTH, of=jnp.bfloat16),
            shape(*got.shape, of=jnp.bfloat16),
        ],
        "after_self",
    )


def feed_forward(got, normed_in, cotangent, gains, biases, out_part, in_parts, down, outs, up, lanes, width):
    pieces = len(in_parts)
    step = in_parts[0].width

    def body(ins, loaded, refs, scratch):
        got_ref, normed_in_ref, cot_ref, gains_ref, biases_ref = ins
        (
            output_ref,
            low_ref,
            mixed_ref,
            adapted_ref,
            dunder_ref,
            dab_ref,
            dcb_ref,
            dresid_ref,
            blocks_ref,
            norms_ref,
        ) = refs
        (slopes,) = scratch
        w_out, w_in = loaded[0], loaded[1 : 1 + pieces]
        w_down, w_ff, w_up = loaded[1 + pieces :]
        attended = read_blocks(got_ref, lanes, 0, width)
        low_ref[...] = attended
        hidden = normed_in_ref[...] * gains_ref[0:1] + biases_ref[0:1]
        normed_one, scale_one = normalize(hidden + dot(attended, w_out.value()))
        mixed = normed_one * gains_ref[1:2] + biases_ref[1:2]
        mixed_low = mixed.astype(jnp.bfloat16)
        mixed_ref[...] = mixed_low
        summed = mixed
        under = dot(mixed_low, w_down.value())
        gate = 1.0 / (1.0 + jnp.exp(-under))
        adapted = (under * gate).astype(jnp.bfloat16)
        adapted_ref[...] = adapted
        under_slope = gate * (1.0 + under * (1.0 - gate))
        summed = summed + 4.0 * dot(adapted, w_up.value())
        for piece in range(pieces):
            before = dot(mixed_low, w_in[piece].value())
            below = 0.5 + 0.5 * lax.erf(before * (0.5**0.5))
            slopes[piece] = below + before * jnp.exp(-0.5 * before * before) * (
                (2.0 * math.pi) ** -0.5
            )
            act = (before * below).astype(jnp.bfloat16)
            summed = summed + dot(act, w_ff[piece].value())
        normed_two, scale_two = normalize(summed)
        output_ref[...] = (normed_two * gains_ref[2:3] + biases_ref[2:3]).astype(jnp.bfloat16)
        upstream = cot_ref[...].astype(jnp.float32)
        norms_ref[0:1] = jnp.sum(upstream * normed_two, axis=0, keepdims=True)
        norms_ref[1:2] = jnp.sum(upstream, axis=0, keepdims=True)
        dz = norm_back(upstream, normed_two, scale_two, gains_ref[2:3])
        dzb = dz.astype(jnp.bfloat16)
        dab = (4.0 * dz).astype(jnp.bfloat16)
        dab_ref[...] = dab
        dunder = (under_slope * dot_back(dab, w_up.value())).astype(jnp.bfloat16)
        dunder_ref[...] = dunder
        dmixed = dz + dot_back(dunder, w_down.value())
        for piece in range(pieces):
            dpre = (slopes[piece] * dot_back(dzb, w_ff[piece].value())).astype(jnp.bfloat16)
            dmixed = dmixed + dot_back(dpre, w_in[piece].value())
        norms_ref[2:3] = jnp.sum(dmixed * normed_one, axis=0, keepdims=True)
        norms_ref[3:4] = jnp.sum(dmixed, axis=0, keepdims=True)
        dresid = norm_back(dmixed, normed_one, scale_one, gains_ref[1:2])
        dresid_ref[...] = dresid
        dcb = dresid.astype(jnp.bfloat16)
        dcb_ref[...] = dcb
        write_blocks(
            blocks_ref, dot_back(dcb, w_out.value()).astype(jnp.bfloat16), lanes, 0, width
        )

    rows = normed_in.shape[0]
    low = jnp.bfloat16

    def body_rows(ins, loaded, refs, scratch):
        whole_ff = loaded[2 + pieces]

        class Rows:
            def __init__(self, piece):
                self.piece = piece

            def value(self):
                return whole_ff.value()[self.piece * step : (self.piece + 1) * step]

        loaded = loaded[: 2 + pieces] + [[Rows(piece) for piece in range(pieces)], loaded[-1]]
        body(ins, loaded, refs, scratch)

    return call_with_parts(
        body_rows,
        [got, normed_in, cotangent, gains, biases],
        [out_part] + in_parts + [down, outs, up],
        [
            shape(rows, WIDTH, of=low),
            shape(rows, WIDTH, of=low),
            shape(rows, WIDTH, of=low),
            shape(rows, down.width, of=low),
            shape(rows, down.width, of=low),
            shape(rows, WIDTH, of=low),
            shape(rows, WIDTH, of=low),
            shape(rows, WIDTH),
            shape(*got.shape, of=low),
            shape(4, WIDTH),
        ],
        "feed_forward",
        [pltpu.VMEM((pieces, rows, step), jnp.float32)],
        20,
    )


def before_self(got, dresid, normed, scale, gains, query_part, out_part, lanes, width):
    def body(ins, loaded, outs, _):
        got_ref, dresid_ref, normed_ref, scale_ref, gains_ref = ins
        dcq_ref, dr_ref, dsb_ref, blocks_ref, norms_ref = outs
        dcq = read_blocks(got_ref, lanes, 0, width)
        dcq_ref[...] = dcq
        dhidden = dresid_ref[...] + dot_back(dcq, loaded[0].value())
        normed = normed_ref[...]
        norms_ref[0:1] = jnp.sum(dhidden * normed, axis=0, keepdims=True)
        norms_ref[1:2] = jnp.sum(dhidden, axis=0, keepdims=True)
        dr = norm_back(dhidden, normed, scale_ref[...], gains_ref[0:1])
        dr_ref[...] = dr
        dsb = dr.astype(jnp.bfloat16)
        dsb_ref[...] = dsb
        grad = dot_back(dsb, loaded[1].value()).astype(jnp.bfloat16)
        write_blocks(blocks_ref, grad, lanes, 0, width)

    rows = dresid.shape[0]
    return call_with_parts(
        body,
        [got, dresid, normed, scale, gains],
        [query_part, out_part],
        [
            shape(rows, WIDTH, of=jnp.bfloat16),
            shape(rows, WIDTH),
            shape(rows, WIDTH, of=jnp.bfloat16),
            shape(*got.shape, of=jnp.bfloat16),
            shape(2, WIDTH),
        ],
        "before_self",
    )


def input_grad(got, start, parts, lanes, span, width, name):
    def body(ins, loaded, outs, _):
        total = None
        for kind, weight in enumerate(loaded):
            values = read_blocks(ins[0], lanes, kind, width)
            term = dot_back(values, weight.value())
            total = term if total is None else total + term
        outs[0][...] = total if len(ins) == 1 else total + ins[1][...]

    rows = span * lanes
    return call_with_parts(
        body,
        [got] if start is None else [got, start],
        parts,
        [shape(rows, WIDTH)],
        name,
    )


def shards(
    tokens,
    encoder,
    cotangent,
    self_in,
    self_out,
    cross_q,
    cross_kv,
    cross_out,
    ffn_in,
    ffn_out,
    adapt_down,
    adapt_up,
    norm_gain,
    norm_bias,
    tgt_lengths,
    src_lengths,
):
    lanes, span, _ = tokens.shape
    rows = lanes * span
    width = WIDTH * lanes // lax.axis_size("blk")
    own_row = lax.axis_index("blk") // (lax.axis_size("blk") // lanes)
    tgt_ends = jnp.cumsum(lax.dynamic_index_in_dim(tgt_lengths, own_row, 0, keepdims=False))
    src_ends = jnp.cumsum(lax.dynamic_index_in_dim(src_lengths, own_row, 0, keepdims=False))
    flat_tokens = tokens.reshape(rows, WIDTH)
    flat_encoder = encoder.reshape(rows, WIDTH)
    frozen = [ffn_in, adapt_down, ffn_out, adapt_up, cross_out]

    if paired():
        packed = gather_packed(pack_halves(frozen))
        self_packed = pack_halves([self_in])
        token_row, stages = gather_row(tokens)
        self_heads, pair_heads = head_columns([self_in, cross_kv], [3, 2])
        out_shard, query_shard = after((self_out, cross_q), stages[1])
        encoder_block = after(encoder, stages[1])
        self_qkv = project_row(token_row, self_heads, "self_in")
        out_source, query_source = gather_flips([out_shard, query_shard], "xy", self_qkv)
        encoder_row, encoder_stages = gather_row(
            encoder_block, self_qkv, (out_source.arrays[1], query_source.arrays[1])
        )
        self_qkv = after(self_qkv, out_source.stages[0], query_source.stages[0])
        pair_own = project_row(encoder_row, pair_heads, "cross_kv")
    else:
        (self_source, pair_source, out_source, query_source) = gather_flips(
            [self_in, cross_kv, self_out, cross_q], "xyxy"
        )
        self_parts = [columns_of((self_source, WIDTH * kind, WIDTH)) for kind in range(3)]
        pair_parts = [columns_of((pair_source, WIDTH * kind, WIDTH)) for kind in range(2)]
        self_qkv = as_rows(
            exchange(project_blocks(flat_tokens, self_parts, lanes, width, "self_in"))
        )
        pair_own = as_rows(
            exchange(project_blocks(flat_encoder, pair_parts, lanes, width, "cross_kv"))
        )
    self_out_part = columns_of((out_source, 0, WIDTH))
    query_part = columns_of((query_source, 0, WIDTH))

    self_mid, self_full, self_lse = attn_forward(
        tgt_ends, tgt_ends, self_qkv, self_qkv, width, True
    )
    self_sent = after(self_mid, out_source.stages[1], query_source.stages[1])
    if paired():
        self_sent = after(self_sent, encoder_stages[0])
    self_back = exchange(as_blocks(self_sent))
    if paired():
        self_back = after(self_back, encoder_stages[1])
    self_low, normed, scale, hidden_low, query_blocks = after_self(
        self_back,
        flat_tokens,
        norm_gain,
        norm_bias,
        self_out_part,
        query_part,
        lanes,
        width,
    )
    cross_own = as_rows(exchange(query_blocks))
    cross_mid, cross_full, cross_lse = attn_forward(
        tgt_ends, src_ends, cross_own, pair_own, width, False
    )
    cross_back = exchange(as_blocks(cross_mid))
    ready = after(packed, cross_mid) if paired() else None
    ff_parts, down_parts, ffo_parts, up_parts, (cross_out_part,) = packed_parts(frozen, ready)
    if paired():
        self_packed = gather_packed(after(self_packed, cross_back))
    (
        output,
        cross_low,
        mixed_low,
        adapter_low,
        grad_under,
        adapt_low,
        cross_branch_low,
        grad_resid_two,
        cross_grad_blocks,
        norms_high,
    ) = feed_forward(
        cross_back,
        normed,
        cotangent.reshape(rows, WIDTH),
        norm_gain,
        norm_bias,
        cross_out_part,
        ff_parts,
        down_parts[0],
        ffo_parts[0],
        up_parts[0],
        lanes,
        width,
    )
    high_groups = [
        [(cross_low, cross_branch_low)],
        [(mixed_low, grad_under), (adapter_low, adapt_low)],
    ]
    high_terms = [grad_terms(pairs) for pairs in high_groups]
    high_orders = [(2, 1, 4, 8), (1, 2, 4, 8)]
    high_terms, high_stages = scatter_chips(high_terms, high_orders, 0, 2)
    cross_dq, cross_dkv = attn_backward(
        tgt_ends,
        src_ends,
        cross_own,
        pair_own,
        as_rows(after(exchange(cross_grad_blocks), high_stages[0])),
        cross_full,
        cross_lse,
        False,
    )
    cross_dq_got = after(exchange(as_blocks(cross_dq)), high_stages[1])
    if paired():
        dkv_late = after(cross_dkv, high_stages[1])
        pair_terms = row_back(dkv_late, pair_heads, "encoder_grad")
        kv_sent = row_grad(encoder_row, dkv_late, "cross_kv_grad")
        cross_dq_got = after(cross_dq_got, pair_terms, kv_sent)
    cq_low, grad_resid_one, self_branch_low, self_grad_blocks, norms_low = before_self(
        cross_dq_got,
        grad_resid_two,
        normed,
        scale,
        norm_gain,
        query_part,
        self_out_part,
        lanes,
        width,
    )
    norms = jnp.concatenate([norms_low, norms_high], axis=0)
    if paired():
        high_terms = [jnp.concatenate(after(high_terms, self_grad_blocks), axis=2)]
        high_terms, _ = scatter_chips(high_terms, [(2, 1, 4, 8)], 2, 3)
    self_upstream = after(exchange(self_grad_blocks), high_stages[2])
    (self_grads,) = attn_backward(
        tgt_ends,
        tgt_ends,
        self_qkv,
        self_qkv,
        as_rows(self_upstream),
        self_full,
        self_lse,
        True,
        joined=True,
    )
    mid_pairs = after([(hidden_low, cq_low), (self_low, self_branch_low)], self_grads)
    mid_terms = [grad_terms(mid_pairs)]
    if paired():
        (self_parts,) = packed_parts([self_in], after(self_packed, self_grads))
        self_got = exchange(as_blocks(self_grads))
        self_sent = row_grad(token_row, self_grads, "self_in_grad")
        encoder_grad, _ = reduce_row(pair_terms, {1: self_grads, 2: self_got})
        encoder_grad = encoder_grad.reshape(rows, WIDTH)
        mid_terms, mid_stages = scatter_chips(mid_terms, [(2, 1, 4, 8)], 0, 4, {1: self_got})
        high_terms, _ = scatter_chips(after(high_terms, self_grads), [(2, 1, 4, 8)], 3, 4)
        chunks = [
            array[:, :, first : first + width]
            for array in (self_sent, kv_sent)
            for first in range(0, array.shape[2], width)
        ]
        partials = norms.astype(jnp.bfloat16).reshape(1, 48, width)
        chunks.append(jnp.broadcast_to(partials, (16, 48, width)))
        sent = after(jnp.concatenate(chunks, axis=1), self_got)
        got = exchange(sent)
        (tokens_grad,) = input_grad(
            self_got, grad_resid_one, self_parts, lanes, span, width, "tokens_grad"
        )
        got = after(got, tokens_grad)
        chunks = [got[:, first : first + 32] for first in range(0, 160, 32)]
        grad_self_in = finish_row_grad(jnp.concatenate(chunks[:3], axis=2), 3)
        grad_cross_kv = finish_row_grad(jnp.concatenate(chunks[3:], axis=2), 2)
        norms = jnp.sum(got[:, 160:].astype(jnp.float32), axis=0).reshape(6, WIDTH)
        norms = norms + swap_core(norms)
    else:
        pair_got = exchange(as_blocks(cross_dkv))
        self_got = exchange(as_blocks(self_grads))
        (encoder_grad,) = input_grad(
            pair_got, None, pair_parts, lanes, span, width, "encoder_grad"
        )
        (tokens_grad,) = input_grad(
            self_got, grad_resid_one, self_parts, lanes, span, width, "tokens_grad"
        )
        pair_low = pair_got.reshape(lanes, -1, span, 2, width).transpose(0, 2, 3, 1, 4)
        self_low_grads = self_got.reshape(lanes, -1, span, 3, width).transpose(0, 2, 3, 1, 4)
        grad_cross_kv = weight_grad(flat_encoder, pair_low.reshape(rows, 2 * WIDTH))
        grad_self_in = weight_grad(flat_tokens, self_low_grads.reshape(rows, 3 * WIDTH))
        norms = lax.psum(norms, ("dp", "blk"))
    ((grad_cross_q, grad_self_out),) = finish_terms([mid_pairs], mid_terms)
    (grad_cross_out,), (grad_adapt_down, grad_adapt_up) = finish_terms(high_groups, high_terms)
    return (
        output.reshape(lanes, span, WIDTH),
        tokens_grad.reshape(lanes, span, WIDTH),
        encoder_grad.reshape(lanes, span, WIDTH),
        grad_self_in,
        grad_self_out,
        grad_cross_q,
        grad_cross_kv,
        grad_cross_out,
        grad_adapt_down,
        grad_adapt_up,
        jnp.stack([norms[0], norms[4], norms[2]]),
        jnp.stack([norms[1], norms[5], norms[3]]),
    )


def solution(mesh):
    placed = (
        P("dp", "blk", None),
        P("dp", "blk", None),
        P("dp", "blk", None),
        P("blk", None),
        P("blk", None),
        P("blk", None),
        P("blk", None),
        P("blk", None),
        P("blk", None),
        P("blk", None),
        P("blk", None),
        P("blk", None),
        P(),
        P(),
        P("dp", None),
        P("dp", None),
    )
    return jax.shard_map(
        shards,
        mesh=mesh,
        in_specs=placed,
        out_specs=(
            P("dp", "blk", None),
            P("dp", "blk", None),
            P("dp", "blk", None),
            P("blk", None),
            P("blk", None),
            P("blk", None),
            P("blk", None),
            P("blk", None),
            P("blk", None),
            P("blk", None),
            P(),
            P(),
        ),
        check_vma=False,
    )
```

```python
import functools
import math

import jax
import jax.numpy as jnp
from jax import lax
from jax.experimental import pallas as pl
from jax.experimental.pallas import tpu as pltpu
from jax.sharding import PartitionSpec as P

HEADS = 16
HEAD_DIM = 64
WIDTH = HEADS * HEAD_DIM


NEG = -1e30
VMEM_BYTES = 56 * 1024 * 1024


def cost(microseconds):
    return pl.CostEstimate(
        flops=int(microseconds * 0.4e9),
        bytes_accessed=int(microseconds * 1.2e6),
        transcendentals=0,
    )


def paired():
    return lax.axis_size("blk") == 16 and lax.axis_size("dp") == 2


def swap_core(block):
    cores = lax.axis_size("dp")
    return lax.ppermute(block, "dp", [(i ^ 1, i) for i in range(cores)])


def flip(block, bit):
    chips = lax.axis_size("blk")
    return lax.ppermute(block, "blk", [(i ^ bit, i) for i in range(chips)])


FLIPS = (8, 4, 2, 1)


def with_flip(block, bit):
    return jnp.stack([block, flip(block, bit)])


def own_half(values, which):
    half = values.shape[1] // 2
    return lax.dynamic_slice_in_dim(values, which * half, half, 1)


def scatter_chips(terms, orders, first, last, holds=None):
    if not paired():
        return terms, [terms] * 5
    own = lax.axis_index("blk")

    def fold(blocks, left, bit):
        axis, place = left.index(bit), (own // bit) % 2
        kept = lax.dynamic_index_in_dim(blocks, place, axis, keepdims=False)
        sent = lax.dynamic_index_in_dim(blocks, 1 - place, axis, keepdims=False)
        got = flip(sent, bit)
        return (kept.astype(jnp.float32) + got.astype(jnp.float32)).astype(jnp.bfloat16)

    if first == 0:
        terms = [blocks.reshape(2, 2, 2, 2, *blocks.shape[1:]) for blocks in terms]
    stages = [terms[0]]
    for stage in range(first, last):
        if holds and stage in holds:
            terms = after(terms, holds[stage])
        terms = [
            fold(blocks, [bit for bit in FLIPS if bit not in order[:stage]], order[stage])
            for blocks, order in zip(terms, orders)
        ]
        stages.append(terms[0])
    return terms, stages


CHUNK = 256


def grad_terms(pairs):
    if not paired():
        return pairs[0][1]
    core = lax.axis_index("dp")
    packed = []
    for inputs, upstream in pairs:
        both = jnp.concatenate([inputs, swap_core(inputs)], axis=0)
        half = jnp.concatenate(
            [own_half(upstream, core), swap_core(own_half(upstream, 1 - core))], axis=0
        )
        term = lax.dot_general(
            both, half, (((0,), (0,)), ((), ())), preferred_element_type=jnp.float32
        ).astype(jnp.bfloat16)
        rows = term.shape[0] // 16
        chunks = term.shape[1] // CHUNK
        packed += [
            term[:, c * CHUNK : (c + 1) * CHUNK].reshape(16, rows, CHUNK) for c in range(chunks)
        ]
    return jnp.concatenate(packed, axis=1)


def finish_terms(groups, terms):
    if not paired():
        return [[weight_grad(inputs, upstream) for inputs, upstream in pairs] for pairs in groups]
    core = lax.axis_index("dp")
    mine = jnp.concatenate(terms, axis=0)
    other = swap_core(mine)
    low = jnp.where(core == 0, mine, other).astype(jnp.float32)
    high = jnp.where(core == 0, other, mine).astype(jnp.float32)
    found, place = [], 0
    for pairs in groups:
        found.append([])
        for inputs, upstream in pairs:
            rows = inputs.shape[1] // 16
            chunks = upstream.shape[1] // 2 // CHUNK
            spots = [slice(place + c * rows, place + (c + 1) * rows) for c in range(chunks)]
            found[-1].append(
                jnp.concatenate(
                    [low[spot] for spot in spots] + [high[spot] for spot in spots], axis=1
                )
            )
            place += rows * chunks
    return found


def weight_grad(inputs, upstream):
    scattered = lax.psum_scatter(
        lax.dot_general(
            inputs, upstream, (((0,), (0,)), ((), ())), preferred_element_type=jnp.float32
        ).astype(jnp.bfloat16),
        "blk",
        scatter_dimension=0,
        tiled=True,
    )
    return lax.psum(scattered, "dp").astype(jnp.float32)


class Source:
    def __init__(self, kind, arrays, first_flip="x", column=None):
        self.kind, self.arrays, self.first_flip = kind, arrays, first_flip
        self.stages = arrays[:1] * 3 if column is None else [column] + arrays[:2]


class Part:
    def __init__(self, rows, width, spots):
        self.rows, self.width, self.spots = rows, width, spots

    def scratch(self):
        return pltpu.VMEM((2, 2, 2, 2, 2, self.rows // 32, self.width), jnp.bfloat16)

    def start(self, refs_of, place, dst, sem):
        z1, z0, y, x, core = [place[axis] for axis in range(5)]
        high = self.rows // 32
        for source, first_row, first_col, at_col, width in self.spots:
            refs = refs_of(source)
            cols = slice(first_col, first_col + width)
            into = slice(at_col, at_col + width)
            if source.kind == "whole":
                pltpu.make_async_copy(
                    refs[0].at[:, :, :, :, :, :, cols], dst.at[:, :, :, :, :, :, into], sem
                ).start()
            elif source.kind == "cores":
                for which in range(2):
                    owner = core if which == 0 else 1 - core
                    pltpu.make_async_copy(
                        refs[which].at[:, :, :, :, first_row : first_row + high, cols],
                        dst.at[:, :, :, :, owner, :, into],
                        sem,
                    ).start()
            else:
                for which in range(4):
                    owner = core if which < 2 else 1 - core
                    for near, at_y, at_x in flipped(source.first_flip, which % 2, y, x):
                        for up, at_z1, at_z0 in four(z1, z0):
                            pltpu.make_async_copy(
                                refs[which].at[near, up[0], up[1], :, cols],
                                dst.at[at_z1, at_z0, at_y, at_x, owner, :, into],
                                sem,
                            ).start()


def four(z1, z0):
    return [
        ((low, high), z1 if high == 0 else 1 - z1, z0 if low == 0 else 1 - z0)
        for low in range(2)
        for high in range(2)
    ]


def flipped(first_flip, beyond, y, x):
    found = []
    for near in range(2):
        a, b = (near, beyond) if first_flip == "x" else (beyond, near)
        found.append((near, y if b == 0 else 1 - y, x if a == 0 else 1 - x))
    return found


def after(value, *others):
    return lax.optimization_barrier((value, *others))[0]


def gather_flips(shards, first_flips, hold=None):
    if not paired():
        full = [lax.all_gather(shard, "blk", axis=0, tiled=True) for shard in shards]
        return [
            Source("whole", [array.reshape(2, 2, 2, 2, 2, array.shape[0] // 32, array.shape[1])])
            for array in full
        ]
    core = lax.axis_index("dp")
    columns = []
    for shard in shards:
        rows = shard.shape[0]
        own = lax.dynamic_slice_in_dim(shard, core * (rows // 2), rows // 2, 0)
        columns.append(with_flip(with_flip(own, 8), 4))
    sources, bits = [], {"x": (1, 2), "y": (2, 1)}
    if hold is not None:
        columns = after(columns, hold)
    planes = [
        with_flip(column, bits[first][0]) for column, first in zip(columns, first_flips)
    ]
    for column, plane, first in zip(columns, planes, first_flips):
        beyond = flip(plane, bits[first][1])
        sources.append(
            Source("flips", [plane, beyond, swap_core(plane), swap_core(beyond)], first, column)
        )
    return sources


class RowPart:
    def __init__(self, sources, span):
        self.span = span
        self.rows, self.width = 16 * span, WIDTH
        self.spots = [(source,) for source in sources]

    def scratch(self):
        return pltpu.VMEM((2, 2, 2, 2, self.span, WIDTH), jnp.bfloat16)

    def start(self, refs_of, place, dst, sem):
        z1, z0, y, x = [place[axis] for axis in range(4)]
        half = WIDTH // 2
        for side, (source,) in enumerate(self.spots):
            refs = refs_of(source)
            for beyond in range(2):
                for near, at_y, at_x in flipped(source.first_flip, beyond, y, x):
                    for up, at_z1, at_z0 in four(z1, z0):
                        pltpu.make_async_copy(
                            refs[beyond].at[near, up[0], up[1]],
                            dst.at[at_z1, at_z0, at_y, at_x, :, side * half : (side + 1) * half],
                            sem,
                        ).start()


def gather_row(block, hold_near=None, hold=None):
    row = lax.axis_index("blk") // 8
    own = lax.dynamic_index_in_dim(block, row, 0, keepdims=False)
    other = lax.dynamic_index_in_dim(block, 1 - row, 0, keepdims=False)
    pair = jnp.stack([own, flip(other, 8)])
    if hold_near is not None:
        pair = after(pair, hold_near)
    column = with_flip(pair, 4)
    stages, sources = [pair, column], []
    if hold is not None:
        column = after(column, hold)
    half = WIDTH // 2
    planes = [with_flip(column[..., :half], 1), with_flip(column[..., half:], 2)]
    for plane, first, bit in zip(planes, "xy", (2, 1)):
        sources.append(Source("row", [plane, flip(plane, bit)], first))
    stages += [planes, [source.arrays[1] for source in sources]]
    return RowPart(sources, block.shape[1]), stages


def head_columns(shards, kinds):
    core = lax.axis_index("dp")
    blocks, widths = [], [128 * kind for kind in kinds]
    for shard, kind in zip(shards, kinds):
        own = lax.dynamic_slice_in_dim(shard, core * 32, 32, 0)
        own = own.reshape(32, kind, 8, 128).transpose(2, 0, 1, 3)
        blocks.append(own.reshape(8, 32, kind * 128))
    blocks = jnp.concatenate(blocks, axis=2)
    mine = exchange(jnp.concatenate([blocks, blocks], axis=0))
    mine = mine.reshape(2, 2, 2, 2, 32, sum(widths))
    source = Source("cores", [mine, swap_core(mine)])
    parts, place = [], 0
    for width in widths:
        parts.append(Part(1024, width, [(source, 0, place, 0, width)]))
        place += width
    return parts


def project_row(row_part, head_part, name):
    def body(ins, loaded, outs, _):
        weight = loaded[1].value()
        inputs = loaded[0].value()
        for first in range(0, row_part.rows, 256):
            rows = slice(first, first + 256)
            outs[0][rows, :] = dot(inputs[rows], weight).astype(jnp.bfloat16)

    (found,) = call_with_parts(
        body,
        [],
        [row_part, head_part],
        [shape(row_part.rows, head_part.width, of=jnp.bfloat16)],
        name,
    )
    return found


def row_grad(row_part, upstream, name):
    columns = upstream.shape[1]

    def body(ins, loaded, outs, _):
        core = ins[1][0]
        inputs = loaded[0].value()
        grads = []
        for first in range(0, columns, 128):
            grads.append(pair_dot(ins[0][:, first : first + 128], inputs, 0, 0).T)
        grad = jnp.concatenate(grads, axis=1).astype(jnp.bfloat16).reshape(16, 2, 32, columns)
        outs[0][core] = grad[:, 0]
        outs[0][1 - core] = grad[:, 1]

    (terms,) = call_with_parts(
        body,
        [upstream],
        [row_part],
        [shape(2, 16, 32, columns, of=jnp.bfloat16)],
        name,
        scalars=[lax.axis_index("dp").reshape(1).astype(jnp.int32)],
    )
    got = swap_core(terms[1])
    return (terms[0].astype(jnp.float32) + got.astype(jnp.float32)).astype(jnp.bfloat16)


def row_back(upstream, head_part, name):
    def body(ins, loaded, outs, _):
        weight = loaded[0].value()
        for first in range(0, ins[0].shape[0], 256):
            rows = slice(first, first + 256)
            outs[0][rows, :] = dot_back(ins[0][rows, :], weight).astype(jnp.bfloat16)

    (terms,) = call_with_parts(
        body, [upstream], [head_part], [shape(upstream.shape[0], WIDTH, of=jnp.bfloat16)], name
    )
    return terms


def reduce_row(terms, holds=None):
    blocks = terms.reshape(16, terms.shape[0] // 16, WIDTH)
    (both,), stages = scatter_chips([blocks], [(1, 2, 4, 8)], 0, 3, holds)
    row = lax.axis_index("blk") // 8
    kept = lax.dynamic_index_in_dim(both, row, 0, keepdims=False)
    got = flip(lax.dynamic_index_in_dim(both, 1 - row, 0, keepdims=False), 8)
    found = jnp.stack([jnp.where(row == 0, kept, got), jnp.where(row == 0, got, kept)])
    return found.astype(jnp.float32), stages


def finish_row_grad(got, kinds):
    total = jnp.sum(got.reshape(2, 8, 32, kinds, 128).astype(jnp.float32), axis=0)
    mine = total.astype(jnp.bfloat16).transpose(1, 2, 0, 3).reshape(32, kinds * WIDTH)
    other = swap_core(mine)
    core = lax.axis_index("dp")
    low = jnp.where(core == 0, mine, other)
    high = jnp.where(core == 0, other, mine)
    return jnp.concatenate([low, high], axis=0).astype(jnp.float32)


def columns_of(*pieces):
    spots, place = [], 0
    for source, first, width in pieces:
        spots.append((source, 0, first, place, width))
        place += width
    return Part(1024, place, spots)


PACK = 512


def pack_halves(shards):
    places = [
        (index, shard.shape[0] // 2, first)
        for index, shard in enumerate(shards)
        for first in range(0, shard.shape[1], PACK)
    ]

    def body(core, *refs):
        out_ref, place = refs[-1], 0
        for index, high, first in places:
            start = pl.multiple_of(core[0] * high, 16)
            out_ref[place : place + high, :] = refs[index][pl.ds(start, high), first : first + PACK]
            place += high

    return pl.pallas_call(
        body,
        out_shape=shape(sum(high for _, high, _ in places), PACK, of=jnp.bfloat16),
        in_specs=[smem_spec()] + [vmem_spec()] * len(shards),
        out_specs=vmem_spec(),
        compiler_params=pltpu.CompilerParams(vmem_limit_bytes=VMEM_BYTES),
        cost_estimate=cost(2),
        name="pack_halves",
    )(lax.axis_index("dp").reshape(1).astype(jnp.int32), *shards)


def gather_packed(packed):
    return lax.all_gather(packed, "blk", axis=0)


def packed_parts(shards, mine):
    if not paired():
        found = []
        for source, shard in zip(gather_flips(shards, "x" * len(shards)), shards):
            rows, columns = 32 * source.arrays[0].shape[5], shard.shape[1]
            step = min(columns, 1024)
            found.append(
                [
                    Part(rows, step, [(source, 0, first, 0, step)])
                    for first in range(0, columns, step)
                ]
            )
        return found
    spots, place = [], 0
    for shard in shards:
        high = shard.shape[0] // 2
        places = []
        for first in range(0, shard.shape[1], PACK):
            places.append(place)
            place += high
        spots.append((shard.shape[0] * 16, places))
    mine = mine.reshape(2, 2, 2, 2, place, PACK)
    source = Source("cores", [mine, swap_core(mine)])
    found = []
    for rows, places in spots:
        parts = []
        for first in range(0, len(places), 2):
            two = places[first : first + 2]
            parts.append(
                Part(
                    rows,
                    PACK * len(two),
                    [(source, row, 0, PACK * side, PACK) for side, row in enumerate(two)],
                )
            )
        found.append(parts)
    return found


def place_now():
    own, core = lax.axis_index("blk"), lax.axis_index("dp")
    bits = [(own // bit) % 2 for bit in FLIPS]
    return jnp.stack(bits + [core]).astype(jnp.int32)


class Loaded:
    def __init__(self, part, dst, sem):
        self.part, self.dst, self.sem, self.here = part, dst, sem, False

    def value(self):
        if not self.here:
            pltpu.make_async_copy(self.dst, self.dst, self.sem).wait()
            self.here = True
        return self.dst[...].reshape(self.part.rows, self.part.width)


def call_with_parts(body, inputs, parts, outputs, name, scratch=(), takes=5, scalars=()):
    sources = []
    for part in parts:
        sources += [spot[0] for spot in part.spots if spot[0] not in sources]
    arrays = [array for source in sources for array in source.arrays]

    def kernel(place, *refs):
        refs = list(refs)
        ins = [refs.pop(0) for _ in (*inputs, *scalars)]
        pieces = [[refs.pop(0) for _ in source.arrays] for source in sources]
        outs = [refs.pop(0) for _ in outputs]
        dsts = [refs.pop(0) for _ in parts]
        sems = refs.pop(0)
        loaded = []
        for index, part in enumerate(parts):
            part.start(
                lambda source: pieces[sources.index(source)], place, dsts[index], sems.at[index]
            )
            loaded.append(Loaded(part, dsts[index], sems.at[index]))
        body(ins, loaded, outs, refs)

    return pl.pallas_call(
        kernel,
        out_shape=tuple(outputs),
        in_specs=[smem_spec()]
        + [vmem_spec()] * len(inputs)
        + [smem_spec()] * len(scalars)
        + [pl.BlockSpec(memory_space=pl.ANY)] * len(arrays),
        out_specs=(vmem_spec(),) * len(outputs),
        scratch_shapes=[part.scratch() for part in parts]
        + [pltpu.SemaphoreType.DMA((len(parts),))]
        + list(scratch),
        compiler_params=pltpu.CompilerParams(vmem_limit_bytes=VMEM_BYTES),
        cost_estimate=cost(takes),
        name=name,
    )(place_now(), *inputs, *scalars, *arrays)


def vmem_spec():
    return pl.BlockSpec(memory_space=pltpu.VMEM)


def smem_spec():
    return pl.BlockSpec(memory_space=pltpu.SMEM)


def seg_of_pos(ends_ref, pos):
    seg = jnp.zeros(pos.shape, jnp.int32)
    for slot in range(ends_ref.shape[0]):
        seg = seg + (ends_ref[slot] <= pos).astype(jnp.int32)
    return seg


def pair_dot(left, right, left_dim, right_dim):
    return lax.dot_general(
        left, right, (((left_dim,), (right_dim,)), ((), ())), preferred_element_type=jnp.float32
    )


def seg_tables(q_ends, k_ends, span):
    seg_q = seg_of_pos(q_ends, lax.broadcasted_iota(jnp.int32, (1, span), 1))
    seg_k = seg_of_pos(k_ends, lax.broadcasted_iota(jnp.int32, (span, 1), 0))
    return seg_q, seg_k


def masked_scores(keys, queries, seg_q, seg_k, first, causal):
    scores = pair_dot(keys, queries, 1, 1)
    allowed = seg_k == seg_q
    if causal:
        key_pos = lax.broadcasted_iota(jnp.int32, scores.shape, 0)
        query_pos = first + lax.broadcasted_iota(jnp.int32, scores.shape, 1)
        allowed = allowed & (key_pos <= query_pos)
    return jnp.where(allowed, scores, NEG)


def attn_forward_body(causal, width, q_ends, k_ends, q_ref, kv_ref, low_ref, full_ref, lse_ref):
    span = q_ref.shape[0]
    step = math.gcd(span, 256)
    heads = width // HEAD_DIM
    seg_q, seg_k = seg_tables(q_ends, k_ends, span)
    key_at = kv_ref.shape[1] - 2 * width
    scaled = q_ref[:, :width] * jnp.bfloat16(HEAD_DIM ** (-0.5))
    keys = kv_ref[:, key_at : key_at + width]
    values = kv_ref[:, key_at + width : key_at + 2 * width]
    for first in range(0, span, step):
        reach = first + step if causal else span
        parts = []
        for head in range(heads):
            cols = slice(head * HEAD_DIM, (head + 1) * HEAD_DIM)
            scores = masked_scores(
                keys[:reach, cols],
                scaled[first : first + step, cols],
                seg_q[:, first : first + step],
                seg_k[:reach],
                first,
                causal,
            )
            top = jnp.max(scores, axis=0, keepdims=True)
            probs = jnp.exp(scores - top)
            total = jnp.sum(probs, axis=0, keepdims=True)
            mixed = pair_dot(values[:reach, cols], probs.astype(jnp.bfloat16), 0, 0)
            parts.append(mixed / total)
            lse_ref[head : head + 1, first : first + step] = top + jnp.log(total)
        joined = jnp.concatenate(parts, axis=0).T
        full_ref[first : first + step, :] = joined
        low_ref[first : first + step, :] = joined.astype(jnp.bfloat16)


def attn_forward(q_ends, k_ends, queries, keys_values, width, causal):
    span = queries.shape[0]
    return pl.pallas_call(
        functools.partial(attn_forward_body, causal, width),
        out_shape=(
            jax.ShapeDtypeStruct((span, width), jnp.bfloat16),
            jax.ShapeDtypeStruct((span, width), jnp.float32),
            jax.ShapeDtypeStruct((width // HEAD_DIM, span), jnp.float32),
        ),
        in_specs=[smem_spec(), smem_spec()] + [vmem_spec()] * 2,
        out_specs=(vmem_spec(),) * 3,
        compiler_params=pltpu.CompilerParams(vmem_limit_bytes=VMEM_BYTES),
        cost_estimate=cost(8),
        name="attn_forward",
    )(q_ends, k_ends, queries, keys_values)


def attn_backward_body(
    causal,
    width,
    q_ends,
    k_ends,
    q_ref,
    kv_ref,
    up_ref,
    full_ref,
    lse_ref,
    *outs,
):
    dq_ref, dkv_ref = outs[0], outs[-3]
    dk_sum, dv_sum = outs[-2:]
    span = q_ref.shape[0]
    step = math.gcd(span, 256)
    heads = width // HEAD_DIM
    seg_q, seg_k = seg_tables(q_ends, k_ends, span)
    key_at = kv_ref.shape[1] - 2 * width
    scaled = q_ref[:, :width] * jnp.bfloat16(HEAD_DIM ** (-0.5))
    keys = kv_ref[:, key_at : key_at + width]
    values = kv_ref[:, key_at + width : key_at + 2 * width]
    upstream = up_ref[...]
    dk_sum[...] = jnp.zeros_like(dk_sum)
    dv_sum[...] = jnp.zeros_like(dv_sum)
    for first in range(0, span, step):
        reach = first + step if causal else span
        rows = slice(first, first + step)
        product = (upstream[rows].astype(jnp.float32) * full_ref[rows, :]).T
        parts = []
        for head in range(heads):
            cols = slice(head * HEAD_DIM, (head + 1) * HEAD_DIM)
            delta = jnp.sum(product[cols], axis=0, keepdims=True)
            scores = masked_scores(
                keys[:reach, cols], scaled[rows, cols], seg_q[:, rows], seg_k[:reach], first, causal
            )
            probs = jnp.exp(scores - lse_ref[head : head + 1, rows])
            dv_sum[head, :reach] += pair_dot(
                probs.astype(jnp.bfloat16), upstream[rows, cols], 1, 0
            )
            grad_probs = pair_dot(values[:reach, cols], upstream[rows, cols], 1, 1)
            grad_scores = (probs * (grad_probs - delta)).astype(jnp.bfloat16)
            dk_sum[head, :reach] += pair_dot(grad_scores, scaled[rows, cols], 1, 0)
            parts.append(pair_dot(keys[:reach, cols], grad_scores, 0, 0))
        joined = jnp.concatenate(parts, axis=0).T * HEAD_DIM ** (-0.5)
        dq_ref[rows, :width] = joined.astype(jnp.bfloat16)
    sums = [dk_sum[head] for head in range(heads)] + [dv_sum[head] for head in range(heads)]
    kv_at = dkv_ref.shape[1] - 2 * width
    dkv_ref[:, kv_at:] = jnp.concatenate(sums, axis=1).astype(jnp.bfloat16)


def attn_backward(
    q_ends, k_ends, queries, keys_values, upstream, full, lse, causal, joined=False
):
    span, width = upstream.shape
    kinds = [3] if joined else [1, 2]
    heads = width // HEAD_DIM
    return pl.pallas_call(
        functools.partial(attn_backward_body, causal, width),
        out_shape=[jax.ShapeDtypeStruct((span, kind * width), jnp.bfloat16) for kind in kinds],
        in_specs=[smem_spec(), smem_spec()] + [vmem_spec()] * 5,
        out_specs=[vmem_spec()] * len(kinds),
        scratch_shapes=[pltpu.VMEM((heads, span, HEAD_DIM), jnp.float32)] * 2,
        compiler_params=pltpu.CompilerParams(vmem_limit_bytes=VMEM_BYTES),
        cost_estimate=cost(8),
        name="attn_backward",
    )(q_ends, k_ends, queries, keys_values, upstream, full, lse)


def exchange(blocks):
    return lax.all_to_all(blocks, "blk", 0, 0, tiled=True)


def as_rows(blocks):
    return blocks.reshape(blocks.shape[0] * blocks.shape[1], blocks.shape[2])


def as_blocks(rows):
    devices = lax.axis_size("blk")
    return rows.reshape(devices, rows.shape[0] // devices, rows.shape[1])


def write_blocks(out_ref, values, lanes, kind, width):
    span = values.shape[0] // lanes
    for group in range(WIDTH // width):
        for lane in range(lanes):
            out_ref[lane * (WIDTH // width) + group, :, kind * width : (kind + 1) * width] = values[
                lane * span : (lane + 1) * span, group * width : (group + 1) * width
            ]


def read_blocks(got_ref, lanes, kind, width):
    groups = got_ref.shape[0] // lanes
    cols = slice(kind * width, (kind + 1) * width)
    rows = [
        jnp.concatenate([got_ref[lane * groups + group, :, cols] for group in range(groups)], axis=1)
        for lane in range(lanes)
    ]
    return jnp.concatenate(rows, axis=0)


def dot(left, right):
    return pair_dot(left, right, 1, 0)


def dot_back(left, right):
    return pair_dot(left, right, 1, 1)


def shape(*sizes, of=jnp.float32):
    return jax.ShapeDtypeStruct(sizes, of)


def normalize(values):
    center = values - jnp.mean(values, -1, keepdims=True)
    scale = lax.rsqrt(jnp.mean(center * center, -1, keepdims=True) + 1e-05)
    return center * scale, scale


def norm_back(upstream, normed, scale, gains_row):
    grad = upstream * gains_row
    return scale * (
        grad
        - jnp.mean(grad, -1, keepdims=True)
        - normed * jnp.mean(grad * normed, -1, keepdims=True)
    )


def project_blocks(inputs, parts, lanes, width, name):
    def body(ins, loaded, outs, _):
        for kind, weight in enumerate(loaded):
            write_blocks(
                outs[0], dot(ins[0][...], weight.value()).astype(jnp.bfloat16), lanes, kind, width
            )

    devices, span = lax.axis_size("blk"), inputs.shape[0] // lanes
    (blocks,) = call_with_parts(
        body,
        [inputs],
        parts,
        [shape(devices, span, width * len(parts), of=jnp.bfloat16)],
        name,
    )
    return blocks


def after_self(got, tokens, gains, biases, out_part, query_part, lanes, width):
    def body(ins, loaded, outs, _):
        got_ref, tokens_ref, gains_ref, biases_ref = ins
        low_ref, normed_ref, scale_ref, hidden_ref, blocks_ref = outs
        attended = read_blocks(got_ref, lanes, 0, width)
        low_ref[...] = attended
        resid = tokens_ref[...].astype(jnp.float32) + dot(attended, loaded[0].value())
        normed, scale = normalize(resid)
        normed_ref[...] = normed
        scale_ref[...] = scale
        hidden = (normed * gains_ref[0:1] + biases_ref[0:1]).astype(jnp.bfloat16)
        hidden_ref[...] = hidden
        query = dot(hidden, loaded[1].value()).astype(jnp.bfloat16)
        write_blocks(blocks_ref, query, lanes, 0, width)

    rows = tokens.shape[0]
    return call_with_parts(
        body,
        [got, tokens, gains, biases],
        [out_part, query_part],
        [
            shape(rows, WIDTH, of=jnp.bfloat16),
            shape(rows, WIDTH),
            shape(rows, 1),
            shape(rows, WIDTH, of=jnp.bfloat16),
            shape(*got.shape, of=jnp.bfloat16),
        ],
        "after_self",
    )


def feed_forward(got, normed_in, cotangent, gains, biases, out_part, in_parts, down, outs, up, lanes, width):
    pieces = len(in_parts)
    step = in_parts[0].width

    def body(ins, loaded, refs, scratch):
        got_ref, normed_in_ref, cot_ref, gains_ref, biases_ref = ins
        (
            output_ref,
            low_ref,
            mixed_ref,
            adapted_ref,
            dunder_ref,
            dab_ref,
            dcb_ref,
            dresid_ref,
            blocks_ref,
            norms_ref,
        ) = refs
        (slopes,) = scratch
        w_out, w_in = loaded[0], loaded[1 : 1 + pieces]
        w_down, w_ff, w_up = loaded[1 + pieces :]
        attended = read_blocks(got_ref, lanes, 0, width)
        low_ref[...] = attended
        hidden = normed_in_ref[...] * gains_ref[0:1] + biases_ref[0:1]
        normed_one, scale_one = normalize(hidden + dot(attended, w_out.value()))
        mixed = normed_one * gains_ref[1:2] + biases_ref[1:2]
        mixed_low = mixed.astype(jnp.bfloat16)
        mixed_ref[...] = mixed_low
        summed = mixed
        under = dot(mixed_low, w_down.value())
        gate = 1.0 / (1.0 + jnp.exp(-under))
        adapted = (under * gate).astype(jnp.bfloat16)
        adapted_ref[...] = adapted
        under_slope = gate * (1.0 + under * (1.0 - gate))
        summed = summed + 4.0 * dot(adapted, w_up.value())
        for piece in range(pieces):
            before = dot(mixed_low, w_in[piece].value())
            below = 0.5 + 0.5 * lax.erf(before * (0.5**0.5))
            slopes[piece] = below + before * jnp.exp(-0.5 * before * before) * (
                (2.0 * math.pi) ** -0.5
            )
            act = (before * below).astype(jnp.bfloat16)
            summed = summed + dot(act, w_ff[piece].value())
        normed_two, scale_two = normalize(summed)
        output_ref[...] = (normed_two * gains_ref[2:3] + biases_ref[2:3]).astype(jnp.bfloat16)
        upstream = cot_ref[...].astype(jnp.float32)
        norms_ref[0:1] = jnp.sum(upstream * normed_two, axis=0, keepdims=True)
        norms_ref[1:2] = jnp.sum(upstream, axis=0, keepdims=True)
        dz = norm_back(upstream, normed_two, scale_two, gains_ref[2:3])
        dzb = dz.astype(jnp.bfloat16)
        dab = (4.0 * dz).astype(jnp.bfloat16)
        dab_ref[...] = dab
        dunder = (under_slope * dot_back(dab, w_up.value())).astype(jnp.bfloat16)
        dunder_ref[...] = dunder
        dmixed = dz + dot_back(dunder, w_down.value())
        for piece in range(pieces):
            dpre = (slopes[piece] * dot_back(dzb, w_ff[piece].value())).astype(jnp.bfloat16)
            dmixed = dmixed + dot_back(dpre, w_in[piece].value())
        norms_ref[2:3] = jnp.sum(dmixed * normed_one, axis=0, keepdims=True)
        norms_ref[3:4] = jnp.sum(dmixed, axis=0, keepdims=True)
        dresid = norm_back(dmixed, normed_one, scale_one, gains_ref[1:2])
        dresid_ref[...] = dresid
        dcb = dresid.astype(jnp.bfloat16)
        dcb_ref[...] = dcb
        write_blocks(
            blocks_ref, dot_back(dcb, w_out.value()).astype(jnp.bfloat16), lanes, 0, width
        )

    rows = normed_in.shape[0]
    low = jnp.bfloat16

    def body_rows(ins, loaded, refs, scratch):
        whole_ff = loaded[2 + pieces]

        class Rows:
            def __init__(self, piece):
                self.piece = piece

            def value(self):
                return whole_ff.value()[self.piece * step : (self.piece + 1) * step]

        loaded = loaded[: 2 + pieces] + [[Rows(piece) for piece in range(pieces)], loaded[-1]]
        body(ins, loaded, refs, scratch)

    return call_with_parts(
        body_rows,
        [got, normed_in, cotangent, gains, biases],
        [out_part] + in_parts + [down, outs, up],
        [
            shape(rows, WIDTH, of=low),
            shape(rows, WIDTH, of=low),
            shape(rows, WIDTH, of=low),
            shape(rows, down.width, of=low),
            shape(rows, down.width, of=low),
            shape(rows, WIDTH, of=low),
            shape(rows, WIDTH, of=low),
            shape(rows, WIDTH),
            shape(*got.shape, of=low),
            shape(4, WIDTH),
        ],
        "feed_forward",
        [pltpu.VMEM((pieces, rows, step), jnp.float32)],
        20,
    )


def before_self(got, dresid, normed, scale, gains, query_part, out_part, lanes, width):
    def body(ins, loaded, outs, _):
        got_ref, dresid_ref, normed_ref, scale_ref, gains_ref = ins
        dcq_ref, dr_ref, dsb_ref, blocks_ref, norms_ref = outs
        dcq = read_blocks(got_ref, lanes, 0, width)
        dcq_ref[...] = dcq
        dhidden = dresid_ref[...] + dot_back(dcq, loaded[0].value())
        normed = normed_ref[...]
        norms_ref[0:1] = jnp.sum(dhidden * normed, axis=0, keepdims=True)
        norms_ref[1:2] = jnp.sum(dhidden, axis=0, keepdims=True)
        dr = norm_back(dhidden, normed, scale_ref[...], gains_ref[0:1])
        dr_ref[...] = dr
        dsb = dr.astype(jnp.bfloat16)
        dsb_ref[...] = dsb
        grad = dot_back(dsb, loaded[1].value()).astype(jnp.bfloat16)
        write_blocks(blocks_ref, grad, lanes, 0, width)

    rows = dresid.shape[0]
    return call_with_parts(
        body,
        [got, dresid, normed, scale, gains],
        [query_part, out_part],
        [
            shape(rows, WIDTH, of=jnp.bfloat16),
            shape(rows, WIDTH),
            shape(rows, WIDTH, of=jnp.bfloat16),
            shape(*got.shape, of=jnp.bfloat16),
            shape(2, WIDTH),
        ],
        "before_self",
    )


def input_grad(got, start, parts, lanes, span, width, name):
    stacked = got.shape[2] == width

    def body(ins, loaded, outs, _):
        total = None
        for kind, weight in enumerate(loaded):
            if stacked:
                values = read_blocks(
                    ins[0].at[:, kind * span : (kind + 1) * span], lanes, 0, width
                )
            else:
                values = read_blocks(ins[0], lanes, kind, width)
            term = dot_back(values, weight.value())
            total = term if total is None else total + term
        outs[0][...] = total if len(ins) == 1 else total + ins[1][...]

    rows = span * lanes
    return call_with_parts(
        body,
        [got] if start is None else [got, start],
        parts,
        [shape(rows, WIDTH)],
        name,
    )


def shards(
    tokens,
    encoder,
    cotangent,
    self_in,
    self_out,
    cross_q,
    cross_kv,
    cross_out,
    ffn_in,
    ffn_out,
    adapt_down,
    adapt_up,
    norm_gain,
    norm_bias,
    tgt_lengths,
    src_lengths,
):
    lanes, span, _ = tokens.shape
    rows = lanes * span
    width = WIDTH * lanes // lax.axis_size("blk")
    own_row = lax.axis_index("blk") // (lax.axis_size("blk") // lanes)
    tgt_ends = jnp.cumsum(lax.dynamic_index_in_dim(tgt_lengths, own_row, 0, keepdims=False))
    src_ends = jnp.cumsum(lax.dynamic_index_in_dim(src_lengths, own_row, 0, keepdims=False))
    flat_tokens = tokens.reshape(rows, WIDTH)
    flat_encoder = encoder.reshape(rows, WIDTH)
    frozen = [ffn_in, adapt_down, ffn_out, adapt_up, cross_out]

    if paired():
        packed = gather_packed(pack_halves(frozen))
        self_packed = pack_halves([self_in])
        token_row, stages = gather_row(tokens)
        self_heads, pair_heads = head_columns([self_in, cross_kv], [3, 2])
        out_shard, query_shard = after((self_out, cross_q), stages[1])
        encoder_block = after(encoder, stages[1])
        self_qkv = project_row(token_row, self_heads, "self_in")
        out_source, query_source = gather_flips([out_shard, query_shard], "xy", self_qkv)
        encoder_row, encoder_stages = gather_row(
            encoder_block, self_qkv, (out_source.arrays[1], query_source.arrays[1])
        )
        self_qkv = after(self_qkv, out_source.stages[0], query_source.stages[0])
        pair_own = project_row(encoder_row, pair_heads, "cross_kv")
    else:
        (self_source, pair_source, out_source, query_source) = gather_flips(
            [self_in, cross_kv, self_out, cross_q], "xyxy"
        )
        self_parts = [columns_of((self_source, WIDTH * kind, WIDTH)) for kind in range(3)]
        pair_parts = [columns_of((pair_source, WIDTH * kind, WIDTH)) for kind in range(2)]
        self_qkv = as_rows(
            exchange(project_blocks(flat_tokens, self_parts, lanes, width, "self_in"))
        )
        pair_own = as_rows(
            exchange(project_blocks(flat_encoder, pair_parts, lanes, width, "cross_kv"))
        )
    self_out_part = columns_of((out_source, 0, WIDTH))
    query_part = columns_of((query_source, 0, WIDTH))

    self_mid, self_full, self_lse = attn_forward(
        tgt_ends, tgt_ends, self_qkv, self_qkv, width, True
    )
    self_sent = after(self_mid, out_source.stages[1], query_source.stages[1])
    if paired():
        self_sent = after(self_sent, encoder_stages[0])
    self_back = exchange(as_blocks(self_sent))
    if paired():
        self_back = after(self_back, encoder_stages[1])
    self_low, normed, scale, hidden_low, query_blocks = after_self(
        self_back,
        flat_tokens,
        norm_gain,
        norm_bias,
        self_out_part,
        query_part,
        lanes,
        width,
    )
    cross_own = as_rows(exchange(query_blocks))
    cross_mid, cross_full, cross_lse = attn_forward(
        tgt_ends, src_ends, cross_own, pair_own, width, False
    )
    cross_back = exchange(as_blocks(cross_mid))
    ready = after(packed, cross_mid) if paired() else None
    ff_parts, down_parts, ffo_parts, up_parts, (cross_out_part,) = packed_parts(frozen, ready)
    if paired():
        self_packed = gather_packed(after(self_packed, cross_back))
    (
        output,
        cross_low,
        mixed_low,
        adapter_low,
        grad_under,
        adapt_low,
        cross_branch_low,
        grad_resid_two,
        cross_grad_blocks,
        norms_high,
    ) = feed_forward(
        cross_back,
        normed,
        cotangent.reshape(rows, WIDTH),
        norm_gain,
        norm_bias,
        cross_out_part,
        ff_parts,
        down_parts[0],
        ffo_parts[0],
        up_parts[0],
        lanes,
        width,
    )
    high_groups = [
        [(cross_low, cross_branch_low)],
        [(mixed_low, grad_under), (adapter_low, adapt_low)],
    ]
    high_terms = [grad_terms(pairs) for pairs in high_groups]
    high_orders = [(2, 1, 4, 8), (1, 2, 4, 8)]
    high_terms, high_stages = scatter_chips(high_terms, high_orders, 0, 2)
    cross_dq, cross_dkv = attn_backward(
        tgt_ends,
        src_ends,
        cross_own,
        pair_own,
        as_rows(after(exchange(cross_grad_blocks), high_stages[0])),
        cross_full,
        cross_lse,
        False,
    )
    cross_dq_got = after(exchange(as_blocks(cross_dq)), high_stages[1])
    if paired():
        dkv_late = after(cross_dkv, high_stages[1])
        pair_terms = row_back(dkv_late, pair_heads, "encoder_grad")
        kv_sent = row_grad(encoder_row, dkv_late, "cross_kv_grad")
        cross_dq_got = after(cross_dq_got, pair_terms, kv_sent)
    cq_low, grad_resid_one, self_branch_low, self_grad_blocks, norms_low = before_self(
        cross_dq_got,
        grad_resid_two,
        normed,
        scale,
        norm_gain,
        query_part,
        self_out_part,
        lanes,
        width,
    )
    norms = jnp.concatenate([norms_low, norms_high], axis=0)
    if paired():
        high_terms = [jnp.concatenate(after(high_terms, self_grad_blocks), axis=2)]
        high_terms, _ = scatter_chips(high_terms, [(2, 1, 4, 8)], 2, 3)
    self_upstream = after(exchange(self_grad_blocks), high_stages[2])
    (self_grads,) = attn_backward(
        tgt_ends,
        tgt_ends,
        self_qkv,
        self_qkv,
        as_rows(self_upstream),
        self_full,
        self_lse,
        True,
        joined=True,
    )
    mid_pairs = after([(hidden_low, cq_low), (self_low, self_branch_low)], self_grads)
    mid_terms = [grad_terms([pair]) for pair in mid_pairs]
    if paired():
        mid_terms, _ = scatter_chips(mid_terms, [(2, 1, 4, 8), (1, 2, 4, 8)], 0, 2)
        mid_terms = [jnp.concatenate(mid_terms, axis=2)]
        mid_terms, _ = scatter_chips(mid_terms, [(2, 1, 4, 8)], 2, 4)
    if paired():
        (self_parts,) = packed_parts([self_in], after(self_packed, self_grads))
        self_sent = row_grad(token_row, self_grads, "self_in_grad")
        encoder_grad, _ = reduce_row(pair_terms, {1: self_grads})
        encoder_grad = encoder_grad.reshape(rows, WIDTH)
        high_terms, _ = scatter_chips(after(high_terms, self_grads), [(2, 1, 4, 8)], 3, 4)
        chunks = [
            array[:, :, first : first + width]
            for array in (as_blocks(self_grads), self_sent, kv_sent)
            for first in range(0, array.shape[2], width)
        ]
        partials = norms.astype(jnp.bfloat16).reshape(1, 48, width)
        chunks.append(jnp.broadcast_to(partials, (16, 48, width)))
        got = exchange(jnp.concatenate(chunks, axis=1))
        (tokens_grad,) = input_grad(
            got, grad_resid_one, self_parts, lanes, span, width, "tokens_grad"
        )
        got = got[:, 3 * span :]
        chunks = [got[:, first : first + 32] for first in range(0, 160, 32)]
        grad_self_in = finish_row_grad(jnp.concatenate(chunks[:3], axis=2), 3)
        grad_cross_kv = finish_row_grad(jnp.concatenate(chunks[3:], axis=2), 2)
        norms = jnp.sum(got[:, 160:].astype(jnp.float32), axis=0).reshape(6, WIDTH)
        norms = norms + swap_core(norms)
    else:
        pair_got = exchange(as_blocks(cross_dkv))
        self_got = exchange(as_blocks(self_grads))
        (encoder_grad,) = input_grad(
            pair_got, None, pair_parts, lanes, span, width, "encoder_grad"
        )
        (tokens_grad,) = input_grad(
            self_got, grad_resid_one, self_parts, lanes, span, width, "tokens_grad"
        )
        pair_low = pair_got.reshape(lanes, -1, span, 2, width).transpose(0, 2, 3, 1, 4)
        self_low_grads = self_got.reshape(lanes, -1, span, 3, width).transpose(0, 2, 3, 1, 4)
        grad_cross_kv = weight_grad(flat_encoder, pair_low.reshape(rows, 2 * WIDTH))
        grad_self_in = weight_grad(flat_tokens, self_low_grads.reshape(rows, 3 * WIDTH))
        norms = lax.psum(norms, ("dp", "blk"))
    ((grad_cross_q, grad_self_out),) = finish_terms([mid_pairs], mid_terms)
    (grad_cross_out,), (grad_adapt_down, grad_adapt_up) = finish_terms(high_groups, high_terms)
    return (
        output.reshape(lanes, span, WIDTH),
        tokens_grad.reshape(lanes, span, WIDTH),
        encoder_grad.reshape(lanes, span, WIDTH),
        grad_self_in,
        grad_self_out,
        grad_cross_q,
        grad_cross_kv,
        grad_cross_out,
        grad_adapt_down,
        grad_adapt_up,
        jnp.stack([norms[0], norms[4], norms[2]]),
        jnp.stack([norms[1], norms[5], norms[3]]),
    )


def solution(mesh):
    placed = (
        P("dp", "blk", None),
        P("dp", "blk", None),
        P("dp", "blk", None),
        P("blk", None),
        P("blk", None),
        P("blk", None),
        P("blk", None),
        P("blk", None),
        P("blk", None),
        P("blk", None),
        P("blk", None),
        P("blk", None),
        P(),
        P(),
        P("dp", None),
        P("dp", None),
    )
    return jax.shard_map(
        shards,
        mesh=mesh,
        in_specs=placed,
        out_specs=(
            P("dp", "blk", None),
            P("dp", "blk", None),
            P("dp", "blk", None),
            P("blk", None),
            P("blk", None),
            P("blk", None),
            P("blk", None),
            P("blk", None),
            P("blk", None),
            P("blk", None),
            P(),
            P(),
        ),
        check_vma=False,
    )
```

```python
import functools
import math

import jax
import jax.numpy as jnp
from jax import lax
from jax.experimental import pallas as pl
from jax.experimental.pallas import tpu as pltpu
from jax.sharding import PartitionSpec as P

HEADS = 16
HEAD_DIM = 64
WIDTH = HEADS * HEAD_DIM


NEG = -1e30
VMEM_BYTES = 56 * 1024 * 1024


def cost(microseconds):
    return pl.CostEstimate(
        flops=int(microseconds * 0.4e9),
        bytes_accessed=int(microseconds * 1.2e6),
        transcendentals=0,
    )


def paired():
    return lax.axis_size("blk") == 16 and lax.axis_size("dp") == 2


def swap_core(block):
    cores = lax.axis_size("dp")
    return lax.ppermute(block, "dp", [(i ^ 1, i) for i in range(cores)])


def flip(block, bit):
    chips = lax.axis_size("blk")
    return lax.ppermute(block, "blk", [(i ^ bit, i) for i in range(chips)])


FLIPS = (8, 4, 2, 1)


def with_flip(block, bit):
    return jnp.stack([block, flip(block, bit)])


def own_half(values, which):
    half = values.shape[1] // 2
    return lax.dynamic_slice_in_dim(values, which * half, half, 1)


def scatter_chips(terms, orders, first, last, holds=None):
    if not paired():
        return terms, [terms] * 5
    own = lax.axis_index("blk")

    def fold(blocks, left, bit):
        axis, place = left.index(bit), (own // bit) % 2
        kept = lax.dynamic_index_in_dim(blocks, place, axis, keepdims=False)
        sent = lax.dynamic_index_in_dim(blocks, 1 - place, axis, keepdims=False)
        got = flip(sent, bit)
        return (kept.astype(jnp.float32) + got.astype(jnp.float32)).astype(jnp.bfloat16)

    if first == 0:
        terms = [blocks.reshape(2, 2, 2, 2, *blocks.shape[1:]) for blocks in terms]
    stages = [terms[0]]
    for stage in range(first, last):
        if holds and stage in holds:
            terms = after(terms, holds[stage])
        terms = [
            fold(blocks, [bit for bit in FLIPS if bit not in order[:stage]], order[stage])
            for blocks, order in zip(terms, orders)
        ]
        stages.append(terms[0])
    return terms, stages


CHUNK = 256


def grad_terms(pairs):
    if not paired():
        return pairs[0][1]
    core = lax.axis_index("dp")
    packed = []
    for inputs, upstream in pairs:
        both = jnp.concatenate([inputs, swap_core(inputs)], axis=0)
        half = jnp.concatenate(
            [own_half(upstream, core), swap_core(own_half(upstream, 1 - core))], axis=0
        )
        term = lax.dot_general(
            both, half, (((0,), (0,)), ((), ())), preferred_element_type=jnp.float32
        ).astype(jnp.bfloat16)
        rows = term.shape[0] // 16
        chunks = term.shape[1] // CHUNK
        packed += [
            term[:, c * CHUNK : (c + 1) * CHUNK].reshape(16, rows, CHUNK) for c in range(chunks)
        ]
    return jnp.concatenate(packed, axis=1)


def finish_terms(groups, terms):
    if not paired():
        return [[weight_grad(inputs, upstream) for inputs, upstream in pairs] for pairs in groups]
    core = lax.axis_index("dp")
    mine = jnp.concatenate(terms, axis=0)
    other = swap_core(mine)
    low = jnp.where(core == 0, mine, other).astype(jnp.float32)
    high = jnp.where(core == 0, other, mine).astype(jnp.float32)
    found, place = [], 0
    for pairs in groups:
        found.append([])
        for inputs, upstream in pairs:
            rows = inputs.shape[1] // 16
            chunks = upstream.shape[1] // 2 // CHUNK
            spots = [slice(place + c * rows, place + (c + 1) * rows) for c in range(chunks)]
            found[-1].append(
                jnp.concatenate(
                    [low[spot] for spot in spots] + [high[spot] for spot in spots], axis=1
                )
            )
            place += rows * chunks
    return found


def weight_grad(inputs, upstream):
    scattered = lax.psum_scatter(
        lax.dot_general(
            inputs, upstream, (((0,), (0,)), ((), ())), preferred_element_type=jnp.float32
        ).astype(jnp.bfloat16),
        "blk",
        scatter_dimension=0,
        tiled=True,
    )
    return lax.psum(scattered, "dp").astype(jnp.float32)


class Source:
    def __init__(self, kind, arrays, first_flip="x", column=None):
        self.kind, self.arrays, self.first_flip = kind, arrays, first_flip
        self.stages = arrays[:1] * 3 if column is None else [column] + arrays[:2]


class Part:
    def __init__(self, rows, width, spots):
        self.rows, self.width, self.spots = rows, width, spots

    def scratch(self):
        return pltpu.VMEM((2, 2, 2, 2, 2, self.rows // 32, self.width), jnp.bfloat16)

    def start(self, refs_of, place, dst, sem):
        z1, z0, y, x, core = [place[axis] for axis in range(5)]
        high = self.rows // 32
        for source, first_row, first_col, at_col, width in self.spots:
            refs = refs_of(source)
            cols = slice(first_col, first_col + width)
            into = slice(at_col, at_col + width)
            if source.kind == "whole":
                pltpu.make_async_copy(
                    refs[0].at[:, :, :, :, :, :, cols], dst.at[:, :, :, :, :, :, into], sem
                ).start()
            elif source.kind == "cores":
                for which in range(2):
                    owner = core if which == 0 else 1 - core
                    pltpu.make_async_copy(
                        refs[which].at[:, :, :, :, first_row : first_row + high, cols],
                        dst.at[:, :, :, :, owner, :, into],
                        sem,
                    ).start()
            else:
                for which in range(4):
                    owner = core if which < 2 else 1 - core
                    for near, at_y, at_x in flipped(source.first_flip, which % 2, y, x):
                        for up, at_z1, at_z0 in four(z1, z0):
                            pltpu.make_async_copy(
                                refs[which].at[near, up[0], up[1], :, cols],
                                dst.at[at_z1, at_z0, at_y, at_x, owner, :, into],
                                sem,
                            ).start()


def four(z1, z0):
    return [
        ((low, high), z1 if high == 0 else 1 - z1, z0 if low == 0 else 1 - z0)
        for low in range(2)
        for high in range(2)
    ]


def flipped(first_flip, beyond, y, x):
    found = []
    for near in range(2):
        a, b = (near, beyond) if first_flip == "x" else (beyond, near)
        found.append((near, y if b == 0 else 1 - y, x if a == 0 else 1 - x))
    return found


def after(value, *others):
    return lax.optimization_barrier((value, *others))[0]


def gather_flips(shards, first_flips, hold=None):
    if not paired():
        full = [lax.all_gather(shard, "blk", axis=0, tiled=True) for shard in shards]
        return [
            Source("whole", [array.reshape(2, 2, 2, 2, 2, array.shape[0] // 32, array.shape[1])])
            for array in full
        ]
    core = lax.axis_index("dp")
    columns = []
    for shard in shards:
        rows = shard.shape[0]
        own = lax.dynamic_slice_in_dim(shard, core * (rows // 2), rows // 2, 0)
        columns.append(with_flip(with_flip(own, 8), 4))
    sources, bits = [], {"x": (1, 2), "y": (2, 1)}
    if hold is not None:
        columns = after(columns, hold)
    planes = [
        with_flip(column, bits[first][0]) for column, first in zip(columns, first_flips)
    ]
    for column, plane, first in zip(columns, planes, first_flips):
        beyond = flip(plane, bits[first][1])
        sources.append(
            Source("flips", [plane, beyond, swap_core(plane), swap_core(beyond)], first, column)
        )
    return sources


class RowPart:
    def __init__(self, sources, span):
        self.span = span
        self.rows, self.width = 16 * span, WIDTH
        self.spots = [(source,) for source in sources]

    def scratch(self):
        return pltpu.VMEM((2, 2, 2, 2, self.span, WIDTH), jnp.bfloat16)

    def start(self, refs_of, place, dst, sem):
        z1, z0, y, x = [place[axis] for axis in range(4)]
        half = WIDTH // 2
        for side, (source,) in enumerate(self.spots):
            refs = refs_of(source)
            for beyond in range(2):
                for near, at_y, at_x in flipped(source.first_flip, beyond, y, x):
                    for up, at_z1, at_z0 in four(z1, z0):
                        pltpu.make_async_copy(
                            refs[beyond].at[near, up[0], up[1]],
                            dst.at[at_z1, at_z0, at_y, at_x, :, side * half : (side + 1) * half],
                            sem,
                        ).start()


def gather_row(block, hold_near=None, hold=None):
    row = lax.axis_index("blk") // 8
    own = lax.dynamic_index_in_dim(block, row, 0, keepdims=False)
    other = lax.dynamic_index_in_dim(block, 1 - row, 0, keepdims=False)
    pair = jnp.stack([own, flip(other, 8)])
    if hold_near is not None:
        pair = after(pair, hold_near)
    column = with_flip(pair, 4)
    stages, sources = [pair, column], []
    if hold is not None:
        column = after(column, hold)
    half = WIDTH // 2
    planes = [with_flip(column[..., :half], 1), with_flip(column[..., half:], 2)]
    for plane, first, bit in zip(planes, "xy", (2, 1)):
        sources.append(Source("row", [plane, flip(plane, bit)], first))
    stages += [planes, [source.arrays[1] for source in sources]]
    return RowPart(sources, block.shape[1]), stages


def head_columns(shards, kinds):
    core = lax.axis_index("dp")
    blocks, widths = [], [128 * kind for kind in kinds]
    for shard, kind in zip(shards, kinds):
        own = lax.dynamic_slice_in_dim(shard, core * 32, 32, 0)
        own = own.reshape(32, kind, 8, 128).transpose(2, 0, 1, 3)
        blocks.append(own.reshape(8, 32, kind * 128))
    blocks = jnp.concatenate(blocks, axis=2)
    mine = exchange(jnp.concatenate([blocks, blocks], axis=0))
    mine = mine.reshape(2, 2, 2, 2, 32, sum(widths))
    source = Source("cores", [mine, swap_core(mine)])
    parts, place = [], 0
    for width in widths:
        parts.append(Part(1024, width, [(source, 0, place, 0, width)]))
        place += width
    return parts


def project_row(row_part, head_part, name):
    def body(ins, loaded, outs, _):
        weight = loaded[1].value()
        inputs = loaded[0].value()
        for first in range(0, row_part.rows, 256):
            rows = slice(first, first + 256)
            outs[0][rows, :] = dot(inputs[rows], weight).astype(jnp.bfloat16)

    (found,) = call_with_parts(
        body,
        [],
        [row_part, head_part],
        [shape(row_part.rows, head_part.width, of=jnp.bfloat16)],
        name,
    )
    return found


def row_grad(row_part, upstream, name):
    columns = upstream.shape[1]

    def body(ins, loaded, outs, _):
        core = ins[1][0]
        inputs = loaded[0].value()
        grads = []
        for first in range(0, columns, 128):
            grads.append(pair_dot(ins[0][:, first : first + 128], inputs, 0, 0).T)
        grad = jnp.concatenate(grads, axis=1).astype(jnp.bfloat16).reshape(16, 2, 32, columns)
        outs[0][core] = grad[:, 0]
        outs[0][1 - core] = grad[:, 1]

    (terms,) = call_with_parts(
        body,
        [upstream],
        [row_part],
        [shape(2, 16, 32, columns, of=jnp.bfloat16)],
        name,
        scalars=[lax.axis_index("dp").reshape(1).astype(jnp.int32)],
    )
    got = swap_core(terms[1])
    return (terms[0].astype(jnp.float32) + got.astype(jnp.float32)).astype(jnp.bfloat16)


def row_back(upstream, head_part, name):
    def body(ins, loaded, outs, _):
        weight = loaded[0].value()
        for first in range(0, ins[0].shape[0], 256):
            rows = slice(first, first + 256)
            outs[0][rows, :] = dot_back(ins[0][rows, :], weight).astype(jnp.bfloat16)

    (terms,) = call_with_parts(
        body, [upstream], [head_part], [shape(upstream.shape[0], WIDTH, of=jnp.bfloat16)], name
    )
    return terms


def reduce_row(terms, holds=None):
    blocks = terms.reshape(16, terms.shape[0] // 16, WIDTH)
    (both,), stages = scatter_chips([blocks], [(1, 2, 4, 8)], 0, 3, holds)
    row = lax.axis_index("blk") // 8
    kept = lax.dynamic_index_in_dim(both, row, 0, keepdims=False)
    got = flip(lax.dynamic_index_in_dim(both, 1 - row, 0, keepdims=False), 8)
    found = jnp.stack([jnp.where(row == 0, kept, got), jnp.where(row == 0, got, kept)])
    return found.astype(jnp.float32), stages


def finish_row_grad(got, kinds):
    total = jnp.sum(got.reshape(2, 8, 32, kinds, 128).astype(jnp.float32), axis=0)
    mine = total.astype(jnp.bfloat16).transpose(1, 2, 0, 3).reshape(32, kinds * WIDTH)
    other = swap_core(mine)
    core = lax.axis_index("dp")
    low = jnp.where(core == 0, mine, other)
    high = jnp.where(core == 0, other, mine)
    return jnp.concatenate([low, high], axis=0).astype(jnp.float32)


def columns_of(*pieces):
    spots, place = [], 0
    for source, first, width in pieces:
        spots.append((source, 0, first, place, width))
        place += width
    return Part(1024, place, spots)


PACK = 512


def pack_halves(shards):
    places = [
        (index, shard.shape[0] // 2, first)
        for index, shard in enumerate(shards)
        for first in range(0, shard.shape[1], PACK)
    ]

    def body(core, *refs):
        out_ref, place = refs[-1], 0
        for index, high, first in places:
            start = pl.multiple_of(core[0] * high, 16)
            out_ref[place : place + high, :] = refs[index][pl.ds(start, high), first : first + PACK]
            place += high

    return pl.pallas_call(
        body,
        out_shape=shape(sum(high for _, high, _ in places), PACK, of=jnp.bfloat16),
        in_specs=[smem_spec()] + [vmem_spec()] * len(shards),
        out_specs=vmem_spec(),
        compiler_params=pltpu.CompilerParams(vmem_limit_bytes=VMEM_BYTES),
        cost_estimate=cost(2),
        name="pack_halves",
    )(lax.axis_index("dp").reshape(1).astype(jnp.int32), *shards)


def gather_packed(packed):
    return lax.all_gather(packed, "blk", axis=0)


def packed_parts(shards, mine):
    if not paired():
        found = []
        for source, shard in zip(gather_flips(shards, "x" * len(shards)), shards):
            rows, columns = 32 * source.arrays[0].shape[5], shard.shape[1]
            step = min(columns, 1024)
            found.append(
                [
                    Part(rows, step, [(source, 0, first, 0, step)])
                    for first in range(0, columns, step)
                ]
            )
        return found
    spots, place = [], 0
    for shard in shards:
        high = shard.shape[0] // 2
        places = []
        for first in range(0, shard.shape[1], PACK):
            places.append(place)
            place += high
        spots.append((shard.shape[0] * 16, places))
    mine = mine.reshape(2, 2, 2, 2, place, PACK)
    source = Source("cores", [mine, swap_core(mine)])
    found = []
    for rows, places in spots:
        parts = []
        for first in range(0, len(places), 2):
            two = places[first : first + 2]
            parts.append(
                Part(
                    rows,
                    PACK * len(two),
                    [(source, row, 0, PACK * side, PACK) for side, row in enumerate(two)],
                )
            )
        found.append(parts)
    return found


def place_now():
    own, core = lax.axis_index("blk"), lax.axis_index("dp")
    bits = [(own // bit) % 2 for bit in FLIPS]
    return jnp.stack(bits + [core]).astype(jnp.int32)


class Loaded:
    def __init__(self, part, dst, sem):
        self.part, self.dst, self.sem, self.here = part, dst, sem, False

    def value(self):
        if not self.here:
            pltpu.make_async_copy(self.dst, self.dst, self.sem).wait()
            self.here = True
        return self.dst[...].reshape(self.part.rows, self.part.width)


def call_with_parts(body, inputs, parts, outputs, name, scratch=(), takes=5, scalars=()):
    sources = []
    for part in parts:
        sources += [spot[0] for spot in part.spots if spot[0] not in sources]
    arrays = [array for source in sources for array in source.arrays]

    def kernel(place, *refs):
        refs = list(refs)
        ins = [refs.pop(0) for _ in (*inputs, *scalars)]
        pieces = [[refs.pop(0) for _ in source.arrays] for source in sources]
        outs = [refs.pop(0) for _ in outputs]
        dsts = [refs.pop(0) for _ in parts]
        sems = refs.pop(0)
        loaded = []
        for index, part in enumerate(parts):
            part.start(
                lambda source: pieces[sources.index(source)], place, dsts[index], sems.at[index]
            )
            loaded.append(Loaded(part, dsts[index], sems.at[index]))
        body(ins, loaded, outs, refs)

    return pl.pallas_call(
        kernel,
        out_shape=tuple(outputs),
        in_specs=[smem_spec()]
        + [vmem_spec()] * len(inputs)
        + [smem_spec()] * len(scalars)
        + [pl.BlockSpec(memory_space=pl.ANY)] * len(arrays),
        out_specs=(vmem_spec(),) * len(outputs),
        scratch_shapes=[part.scratch() for part in parts]
        + [pltpu.SemaphoreType.DMA((len(parts),))]
        + list(scratch),
        compiler_params=pltpu.CompilerParams(vmem_limit_bytes=VMEM_BYTES),
        cost_estimate=cost(takes),
        name=name,
    )(place_now(), *inputs, *scalars, *arrays)


def vmem_spec():
    return pl.BlockSpec(memory_space=pltpu.VMEM)


def smem_spec():
    return pl.BlockSpec(memory_space=pltpu.SMEM)


def seg_of_pos(ends_ref, pos):
    seg = jnp.zeros(pos.shape, jnp.int32)
    for slot in range(ends_ref.shape[0]):
        seg = seg + (ends_ref[slot] <= pos).astype(jnp.int32)
    return seg


def pair_dot(left, right, left_dim, right_dim):
    return lax.dot_general(
        left, right, (((left_dim,), (right_dim,)), ((), ())), preferred_element_type=jnp.float32
    )


def seg_tables(q_ends, k_ends, span):
    seg_q = seg_of_pos(q_ends, lax.broadcasted_iota(jnp.int32, (1, span), 1))
    seg_k = seg_of_pos(k_ends, lax.broadcasted_iota(jnp.int32, (span, 1), 0))
    return seg_q, seg_k


def masked_scores(keys, queries, seg_q, seg_k, first, causal):
    scores = pair_dot(keys, queries, 1, 1)
    allowed = seg_k == seg_q
    if causal:
        key_pos = lax.broadcasted_iota(jnp.int32, scores.shape, 0)
        query_pos = first + lax.broadcasted_iota(jnp.int32, scores.shape, 1)
        allowed = allowed & (key_pos <= query_pos)
    return jnp.where(allowed, scores, NEG)


def attn_forward_body(causal, width, q_ends, k_ends, q_ref, kv_ref, low_ref, full_ref, lse_ref):
    span = q_ref.shape[0]
    step = math.gcd(span, 256)
    heads = width // HEAD_DIM
    seg_q, seg_k = seg_tables(q_ends, k_ends, span)
    key_at = kv_ref.shape[1] - 2 * width
    scaled = q_ref[:, :width] * jnp.bfloat16(HEAD_DIM ** (-0.5))
    keys = kv_ref[:, key_at : key_at + width]
    values = kv_ref[:, key_at + width : key_at + 2 * width]
    for first in range(0, span, step):
        reach = first + step if causal else span
        parts = []
        for head in range(heads):
            cols = slice(head * HEAD_DIM, (head + 1) * HEAD_DIM)
            scores = masked_scores(
                keys[:reach, cols],
                scaled[first : first + step, cols],
                seg_q[:, first : first + step],
                seg_k[:reach],
                first,
                causal,
            )
            top = jnp.max(scores, axis=0, keepdims=True)
            probs = jnp.exp(scores - top)
            total = jnp.sum(probs, axis=0, keepdims=True)
            mixed = pair_dot(values[:reach, cols], probs.astype(jnp.bfloat16), 0, 0)
            parts.append(mixed / total)
            lse_ref[head : head + 1, first : first + step] = top + jnp.log(total)
        joined = jnp.concatenate(parts, axis=0).T
        full_ref[first : first + step, :] = joined
        low_ref[first : first + step, :] = joined.astype(jnp.bfloat16)


def attn_forward(q_ends, k_ends, queries, keys_values, width, causal):
    span = queries.shape[0]
    return pl.pallas_call(
        functools.partial(attn_forward_body, causal, width),
        out_shape=(
            jax.ShapeDtypeStruct((span, width), jnp.bfloat16),
            jax.ShapeDtypeStruct((span, width), jnp.float32),
            jax.ShapeDtypeStruct((width // HEAD_DIM, span), jnp.float32),
        ),
        in_specs=[smem_spec(), smem_spec()] + [vmem_spec()] * 2,
        out_specs=(vmem_spec(),) * 3,
        compiler_params=pltpu.CompilerParams(vmem_limit_bytes=VMEM_BYTES),
        cost_estimate=cost(8),
        name="attn_forward",
    )(q_ends, k_ends, queries, keys_values)


def attn_backward_body(
    causal,
    width,
    q_ends,
    k_ends,
    q_ref,
    kv_ref,
    up_ref,
    full_ref,
    lse_ref,
    *outs,
):
    dq_ref, dkv_ref = outs[0], outs[-3]
    dk_sum, dv_sum = outs[-2:]
    span = q_ref.shape[0]
    step = math.gcd(span, 256)
    heads = width // HEAD_DIM
    seg_q, seg_k = seg_tables(q_ends, k_ends, span)
    key_at = kv_ref.shape[1] - 2 * width
    scaled = q_ref[:, :width] * jnp.bfloat16(HEAD_DIM ** (-0.5))
    keys = kv_ref[:, key_at : key_at + width]
    values = kv_ref[:, key_at + width : key_at + 2 * width]
    upstream = up_ref[...]
    dk_sum[...] = jnp.zeros_like(dk_sum)
    dv_sum[...] = jnp.zeros_like(dv_sum)
    for first in range(0, span, step):
        reach = first + step if causal else span
        rows = slice(first, first + step)
        product = (upstream[rows].astype(jnp.float32) * full_ref[rows, :]).T
        parts = []
        for head in range(heads):
            cols = slice(head * HEAD_DIM, (head + 1) * HEAD_DIM)
            delta = jnp.sum(product[cols], axis=0, keepdims=True)
            scores = masked_scores(
                keys[:reach, cols], scaled[rows, cols], seg_q[:, rows], seg_k[:reach], first, causal
            )
            probs = jnp.exp(scores - lse_ref[head : head + 1, rows])
            dv_sum[head, :reach] += pair_dot(
                probs.astype(jnp.bfloat16), upstream[rows, cols], 1, 0
            )
            grad_probs = pair_dot(values[:reach, cols], upstream[rows, cols], 1, 1)
            grad_scores = (probs * (grad_probs - delta)).astype(jnp.bfloat16)
            dk_sum[head, :reach] += pair_dot(grad_scores, scaled[rows, cols], 1, 0)
            parts.append(pair_dot(keys[:reach, cols], grad_scores, 0, 0))
        joined = jnp.concatenate(parts, axis=0).T * HEAD_DIM ** (-0.5)
        dq_ref[rows, :width] = joined.astype(jnp.bfloat16)
    sums = [dk_sum[head] for head in range(heads)] + [dv_sum[head] for head in range(heads)]
    kv_at = dkv_ref.shape[1] - 2 * width
    dkv_ref[:, kv_at:] = jnp.concatenate(sums, axis=1).astype(jnp.bfloat16)


def attn_backward(
    q_ends, k_ends, queries, keys_values, upstream, full, lse, causal, joined=False
):
    span, width = upstream.shape
    kinds = [3] if joined else [1, 2]
    heads = width // HEAD_DIM
    return pl.pallas_call(
        functools.partial(attn_backward_body, causal, width),
        out_shape=[jax.ShapeDtypeStruct((span, kind * width), jnp.bfloat16) for kind in kinds],
        in_specs=[smem_spec(), smem_spec()] + [vmem_spec()] * 5,
        out_specs=[vmem_spec()] * len(kinds),
        scratch_shapes=[pltpu.VMEM((heads, span, HEAD_DIM), jnp.float32)] * 2,
        compiler_params=pltpu.CompilerParams(vmem_limit_bytes=VMEM_BYTES),
        cost_estimate=cost(8),
        name="attn_backward",
    )(q_ends, k_ends, queries, keys_values, upstream, full, lse)


def exchange(blocks):
    return lax.all_to_all(blocks, "blk", 0, 0, tiled=True)


def as_rows(blocks):
    return blocks.reshape(blocks.shape[0] * blocks.shape[1], blocks.shape[2])


def as_blocks(rows):
    devices = lax.axis_size("blk")
    return rows.reshape(devices, rows.shape[0] // devices, rows.shape[1])


def write_blocks(out_ref, values, lanes, kind, width):
    span = values.shape[0] // lanes
    for group in range(WIDTH // width):
        for lane in range(lanes):
            out_ref[lane * (WIDTH // width) + group, :, kind * width : (kind + 1) * width] = values[
                lane * span : (lane + 1) * span, group * width : (group + 1) * width
            ]


def read_blocks(got_ref, lanes, kind, width):
    groups = got_ref.shape[0] // lanes
    cols = slice(kind * width, (kind + 1) * width)
    rows = [
        jnp.concatenate([got_ref[lane * groups + group, :, cols] for group in range(groups)], axis=1)
        for lane in range(lanes)
    ]
    return jnp.concatenate(rows, axis=0)


def dot(left, right):
    return pair_dot(left, right, 1, 0)


def dot_back(left, right):
    return pair_dot(left, right, 1, 1)


def shape(*sizes, of=jnp.float32):
    return jax.ShapeDtypeStruct(sizes, of)


def normalize(values):
    center = values - jnp.mean(values, -1, keepdims=True)
    scale = lax.rsqrt(jnp.mean(center * center, -1, keepdims=True) + 1e-05)
    return center * scale, scale


def norm_back(upstream, normed, scale, gains_row):
    grad = upstream * gains_row
    return scale * (
        grad
        - jnp.mean(grad, -1, keepdims=True)
        - normed * jnp.mean(grad * normed, -1, keepdims=True)
    )


def project_blocks(inputs, parts, lanes, width, name):
    def body(ins, loaded, outs, _):
        for kind, weight in enumerate(loaded):
            write_blocks(
                outs[0], dot(ins[0][...], weight.value()).astype(jnp.bfloat16), lanes, kind, width
            )

    devices, span = lax.axis_size("blk"), inputs.shape[0] // lanes
    (blocks,) = call_with_parts(
        body,
        [inputs],
        parts,
        [shape(devices, span, width * len(parts), of=jnp.bfloat16)],
        name,
    )
    return blocks


def after_self(got, tokens, gains, biases, out_part, query_part, lanes, width):
    def body(ins, loaded, outs, _):
        got_ref, tokens_ref, gains_ref, biases_ref = ins
        low_ref, normed_ref, scale_ref, hidden_ref, blocks_ref = outs
        attended = read_blocks(got_ref, lanes, 0, width)
        low_ref[...] = attended
        resid = tokens_ref[...].astype(jnp.float32) + dot(attended, loaded[0].value())
        normed, scale = normalize(resid)
        normed_ref[...] = normed
        scale_ref[...] = scale
        hidden = (normed * gains_ref[0:1] + biases_ref[0:1]).astype(jnp.bfloat16)
        hidden_ref[...] = hidden
        query = dot(hidden, loaded[1].value()).astype(jnp.bfloat16)
        write_blocks(blocks_ref, query, lanes, 0, width)

    rows = tokens.shape[0]
    return call_with_parts(
        body,
        [got, tokens, gains, biases],
        [out_part, query_part],
        [
            shape(rows, WIDTH, of=jnp.bfloat16),
            shape(rows, WIDTH),
            shape(rows, 1),
            shape(rows, WIDTH, of=jnp.bfloat16),
            shape(*got.shape, of=jnp.bfloat16),
        ],
        "after_self",
    )


def feed_forward(got, normed_in, cotangent, gains, biases, out_part, in_parts, down, outs, up, lanes, width):
    pieces = len(in_parts)
    step = in_parts[0].width

    def body(ins, loaded, refs, scratch):
        got_ref, normed_in_ref, cot_ref, gains_ref, biases_ref = ins
        (
            output_ref,
            low_ref,
            mixed_ref,
            adapted_ref,
            dunder_ref,
            dab_ref,
            dcb_ref,
            dresid_ref,
            blocks_ref,
            norms_ref,
        ) = refs
        slopes, acts = scratch
        w_out, w_down, w_in = loaded[0], loaded[1], loaded[2 : 2 + pieces]
        w_ff, w_up = loaded[2 + pieces :]
        attended = read_blocks(got_ref, lanes, 0, width)
        low_ref[...] = attended
        hidden = normed_in_ref[...] * gains_ref[0:1] + biases_ref[0:1]
        normed_one, scale_one = normalize(hidden + dot(attended, w_out.value()))
        mixed = normed_one * gains_ref[1:2] + biases_ref[1:2]
        mixed_low = mixed.astype(jnp.bfloat16)
        mixed_ref[...] = mixed_low
        summed = mixed
        under = dot(mixed_low, w_down.value())
        gate = 1.0 / (1.0 + jnp.exp(-under))
        adapted = (under * gate).astype(jnp.bfloat16)
        adapted_ref[...] = adapted
        under_slope = gate * (1.0 + under * (1.0 - gate))
        for piece in range(pieces):
            before = dot(mixed_low, w_in[piece].value())
            below = 0.5 + 0.5 * lax.erf(before * (0.5**0.5))
            slopes[piece] = below + before * jnp.exp(-0.5 * before * before) * (
                (2.0 * math.pi) ** -0.5
            )
            acts[piece] = (before * below).astype(jnp.bfloat16)
        for piece in range(pieces):
            summed = summed + dot(acts[piece], w_ff[piece].value())
        summed = summed + 4.0 * dot(adapted, w_up.value())
        normed_two, scale_two = normalize(summed)
        output_ref[...] = (normed_two * gains_ref[2:3] + biases_ref[2:3]).astype(jnp.bfloat16)
        upstream = cot_ref[...].astype(jnp.float32)
        norms_ref[0:1] = jnp.sum(upstream * normed_two, axis=0, keepdims=True)
        norms_ref[1:2] = jnp.sum(upstream, axis=0, keepdims=True)
        dz = norm_back(upstream, normed_two, scale_two, gains_ref[2:3])
        dzb = dz.astype(jnp.bfloat16)
        dab = (4.0 * dz).astype(jnp.bfloat16)
        dab_ref[...] = dab
        dunder = (under_slope * dot_back(dab, w_up.value())).astype(jnp.bfloat16)
        dunder_ref[...] = dunder
        dmixed = dz + dot_back(dunder, w_down.value())
        for piece in range(pieces):
            dpre = (slopes[piece] * dot_back(dzb, w_ff[piece].value())).astype(jnp.bfloat16)
            dmixed = dmixed + dot_back(dpre, w_in[piece].value())
        norms_ref[2:3] = jnp.sum(dmixed * normed_one, axis=0, keepdims=True)
        norms_ref[3:4] = jnp.sum(dmixed, axis=0, keepdims=True)
        dresid = norm_back(dmixed, normed_one, scale_one, gains_ref[1:2])
        dresid_ref[...] = dresid
        dcb = dresid.astype(jnp.bfloat16)
        dcb_ref[...] = dcb
        write_blocks(
            blocks_ref, dot_back(dcb, w_out.value()).astype(jnp.bfloat16), lanes, 0, width
        )

    rows = normed_in.shape[0]
    low = jnp.bfloat16

    def body_rows(ins, loaded, refs, scratch):
        whole_ff = loaded[2 + pieces]

        class Rows:
            def __init__(self, piece):
                self.piece = piece

            def value(self):
                return whole_ff.value()[self.piece * step : (self.piece + 1) * step]

        loaded = loaded[: 2 + pieces] + [[Rows(piece) for piece in range(pieces)], loaded[-1]]
        body(ins, loaded, refs, scratch)

    return call_with_parts(
        body_rows,
        [got, normed_in, cotangent, gains, biases],
        [out_part, down] + in_parts + [outs, up],
        [
            shape(rows, WIDTH, of=low),
            shape(rows, WIDTH, of=low),
            shape(rows, WIDTH, of=low),
            shape(rows, down.width, of=low),
            shape(rows, down.width, of=low),
            shape(rows, WIDTH, of=low),
            shape(rows, WIDTH, of=low),
            shape(rows, WIDTH),
            shape(*got.shape, of=low),
            shape(4, WIDTH),
        ],
        "feed_forward",
        [
            pltpu.VMEM((pieces, rows, step), jnp.float32),
            pltpu.VMEM((pieces, rows, step), jnp.bfloat16),
        ],
        20,
    )


def before_self(got, dresid, normed, scale, gains, query_part, out_part, lanes, width):
    def body(ins, loaded, outs, _):
        got_ref, dresid_ref, normed_ref, scale_ref, gains_ref = ins
        dcq_ref, dr_ref, dsb_ref, blocks_ref, norms_ref = outs
        dcq = read_blocks(got_ref, lanes, 0, width)
        dcq_ref[...] = dcq
        dhidden = dresid_ref[...] + dot_back(dcq, loaded[0].value())
        normed = normed_ref[...]
        norms_ref[0:1] = jnp.sum(dhidden * normed, axis=0, keepdims=True)
        norms_ref[1:2] = jnp.sum(dhidden, axis=0, keepdims=True)
        dr = norm_back(dhidden, normed, scale_ref[...], gains_ref[0:1])
        dr_ref[...] = dr
        dsb = dr.astype(jnp.bfloat16)
        dsb_ref[...] = dsb
        grad = dot_back(dsb, loaded[1].value()).astype(jnp.bfloat16)
        write_blocks(blocks_ref, grad, lanes, 0, width)

    rows = dresid.shape[0]
    return call_with_parts(
        body,
        [got, dresid, normed, scale, gains],
        [query_part, out_part],
        [
            shape(rows, WIDTH, of=jnp.bfloat16),
            shape(rows, WIDTH),
            shape(rows, WIDTH, of=jnp.bfloat16),
            shape(*got.shape, of=jnp.bfloat16),
            shape(2, WIDTH),
        ],
        "before_self",
    )


def input_grad(got, start, parts, lanes, span, width, name):
    def body(ins, loaded, outs, _):
        total = None
        for kind, weight in enumerate(loaded):
            values = read_blocks(ins[0], lanes, kind, width)
            term = dot_back(values, weight.value())
            total = term if total is None else total + term
        outs[0][...] = total if len(ins) == 1 else total + ins[1][...]

    rows = span * lanes
    return call_with_parts(
        body,
        [got] if start is None else [got, start],
        parts,
        [shape(rows, WIDTH)],
        name,
    )


def shards(
    tokens,
    encoder,
    cotangent,
    self_in,
    self_out,
    cross_q,
    cross_kv,
    cross_out,
    ffn_in,
    ffn_out,
    adapt_down,
    adapt_up,
    norm_gain,
    norm_bias,
    tgt_lengths,
    src_lengths,
):
    lanes, span, _ = tokens.shape
    rows = lanes * span
    width = WIDTH * lanes // lax.axis_size("blk")
    own_row = lax.axis_index("blk") // (lax.axis_size("blk") // lanes)
    tgt_ends = jnp.cumsum(lax.dynamic_index_in_dim(tgt_lengths, own_row, 0, keepdims=False))
    src_ends = jnp.cumsum(lax.dynamic_index_in_dim(src_lengths, own_row, 0, keepdims=False))
    flat_tokens = tokens.reshape(rows, WIDTH)
    flat_encoder = encoder.reshape(rows, WIDTH)
    frozen = [ffn_in, adapt_down, ffn_out, adapt_up, cross_out]

    if paired():
        packed = gather_packed(pack_halves(frozen))
        self_packed = pack_halves([self_in])
        token_row, stages = gather_row(tokens)
        self_heads, pair_heads = head_columns([self_in, cross_kv], [3, 2])
        out_shard, query_shard = after((self_out, cross_q), stages[1])
        encoder_block = after(encoder, stages[1])
        self_qkv = project_row(token_row, self_heads, "self_in")
        out_source, query_source = gather_flips([out_shard, query_shard], "xy", self_qkv)
        encoder_row, encoder_stages = gather_row(
            encoder_block, self_qkv, (out_source.arrays[1], query_source.arrays[1])
        )
        self_qkv = after(self_qkv, out_source.stages[0], query_source.stages[0])
        pair_own = project_row(encoder_row, pair_heads, "cross_kv")
    else:
        (self_source, pair_source, out_source, query_source) = gather_flips(
            [self_in, cross_kv, self_out, cross_q], "xyxy"
        )
        self_parts = [columns_of((self_source, WIDTH * kind, WIDTH)) for kind in range(3)]
        pair_parts = [columns_of((pair_source, WIDTH * kind, WIDTH)) for kind in range(2)]
        self_qkv = as_rows(
            exchange(project_blocks(flat_tokens, self_parts, lanes, width, "self_in"))
        )
        pair_own = as_rows(
            exchange(project_blocks(flat_encoder, pair_parts, lanes, width, "cross_kv"))
        )
    self_out_part = columns_of((out_source, 0, WIDTH))
    query_part = columns_of((query_source, 0, WIDTH))

    self_mid, self_full, self_lse = attn_forward(
        tgt_ends, tgt_ends, self_qkv, self_qkv, width, True
    )
    self_sent = after(self_mid, out_source.stages[1], query_source.stages[1])
    if paired():
        self_sent = after(self_sent, encoder_stages[0])
    self_back = exchange(as_blocks(self_sent))
    if paired():
        self_back = after(self_back, encoder_stages[1])
    self_low, normed, scale, hidden_low, query_blocks = after_self(
        self_back,
        flat_tokens,
        norm_gain,
        norm_bias,
        self_out_part,
        query_part,
        lanes,
        width,
    )
    cross_own = as_rows(exchange(query_blocks))
    cross_mid, cross_full, cross_lse = attn_forward(
        tgt_ends, src_ends, cross_own, pair_own, width, False
    )
    cross_back = exchange(as_blocks(cross_mid))
    ready = after(packed, cross_mid) if paired() else None
    ff_parts, down_parts, ffo_parts, up_parts, (cross_out_part,) = packed_parts(frozen, ready)
    if paired():
        self_packed = gather_packed(after(self_packed, cross_back))
    (
        output,
        cross_low,
        mixed_low,
        adapter_low,
        grad_under,
        adapt_low,
        cross_branch_low,
        grad_resid_two,
        cross_grad_blocks,
        norms_high,
    ) = feed_forward(
        cross_back,
        normed,
        cotangent.reshape(rows, WIDTH),
        norm_gain,
        norm_bias,
        cross_out_part,
        ff_parts,
        down_parts[0],
        ffo_parts[0],
        up_parts[0],
        lanes,
        width,
    )
    high_groups = [
        [(cross_low, cross_branch_low)],
        [(mixed_low, grad_under), (adapter_low, adapt_low)],
    ]
    high_terms = [grad_terms(pairs) for pairs in high_groups]
    high_orders = [(2, 1, 4, 8), (1, 2, 4, 8)]
    high_terms, high_stages = scatter_chips(high_terms, high_orders, 0, 2)
    cross_dq, cross_dkv = attn_backward(
        tgt_ends,
        src_ends,
        cross_own,
        pair_own,
        as_rows(after(exchange(cross_grad_blocks), high_stages[0])),
        cross_full,
        cross_lse,
        False,
    )
    cross_dq_got = after(exchange(as_blocks(cross_dq)), high_stages[1])
    if paired():
        dkv_late = after(cross_dkv, high_stages[1])
        pair_terms = row_back(dkv_late, pair_heads, "encoder_grad")
        kv_sent = row_grad(encoder_row, dkv_late, "cross_kv_grad")
        cross_dq_got = after(cross_dq_got, pair_terms, kv_sent)
    cq_low, grad_resid_one, self_branch_low, self_grad_blocks, norms_low = before_self(
        cross_dq_got,
        grad_resid_two,
        normed,
        scale,
        norm_gain,
        query_part,
        self_out_part,
        lanes,
        width,
    )
    norms = jnp.concatenate([norms_low, norms_high], axis=0)
    mid_pairs = [(hidden_low, cq_low), (self_low, self_branch_low)]
    mid_orders = [(2, 1, 4, 8), (1, 2, 4, 8)]
    mid_terms = [grad_terms([pair]) for pair in mid_pairs]
    mid_terms, _ = scatter_chips(mid_terms, mid_orders, 0, 1)
    if paired():
        high_terms = [jnp.concatenate(after(high_terms, self_grad_blocks), axis=2)]
        high_terms, _ = scatter_chips(high_terms, [(2, 1, 4, 8)], 2, 3)
    self_upstream = after(exchange(self_grad_blocks), high_stages[2])
    (self_grads,) = attn_backward(
        tgt_ends,
        tgt_ends,
        self_qkv,
        self_qkv,
        as_rows(self_upstream),
        self_full,
        self_lse,
        True,
        joined=True,
    )
    if paired():
        (self_parts,) = packed_parts([self_in], after(self_packed, self_grads))
        self_got = exchange(as_blocks(self_grads))
        self_sent = row_grad(token_row, self_grads, "self_in_grad")
        encoder_grad, _ = reduce_row(pair_terms, {1: self_grads, 2: self_got})
        encoder_grad = encoder_grad.reshape(rows, WIDTH)
        mid_terms, _ = scatter_chips(after(mid_terms, self_grads), mid_orders, 1, 2)
        mid_terms = [jnp.concatenate(mid_terms, axis=2)]
        mid_terms, _ = scatter_chips(mid_terms, mid_orders[:1], 2, 4)
        high_terms, _ = scatter_chips(after(high_terms, self_grads), [(2, 1, 4, 8)], 3, 4)
        chunks = [
            array[:, :, first : first + width]
            for array in (self_sent, kv_sent)
            for first in range(0, array.shape[2], width)
        ]
        partials = norms.astype(jnp.bfloat16).reshape(1, 48, width)
        chunks.append(jnp.broadcast_to(partials, (16, 48, width)))
        sent = after(jnp.concatenate(chunks, axis=1), self_got)
        got = exchange(sent)
        (tokens_grad,) = input_grad(
            self_got, grad_resid_one, self_parts, lanes, span, width, "tokens_grad"
        )
        got = after(got, tokens_grad)
        chunks = [got[:, first : first + 32] for first in range(0, 160, 32)]
        grad_self_in = finish_row_grad(jnp.concatenate(chunks[:3], axis=2), 3)
        grad_cross_kv = finish_row_grad(jnp.concatenate(chunks[3:], axis=2), 2)
        norms = jnp.sum(got[:, 160:].astype(jnp.float32), axis=0).reshape(6, WIDTH)
        norms = norms + swap_core(norms)
    else:
        pair_got = exchange(as_blocks(cross_dkv))
        self_got = exchange(as_blocks(self_grads))
        (encoder_grad,) = input_grad(
            pair_got, None, pair_parts, lanes, span, width, "encoder_grad"
        )
        (tokens_grad,) = input_grad(
            self_got, grad_resid_one, self_parts, lanes, span, width, "tokens_grad"
        )
        pair_low = pair_got.reshape(lanes, -1, span, 2, width).transpose(0, 2, 3, 1, 4)
        self_low_grads = self_got.reshape(lanes, -1, span, 3, width).transpose(0, 2, 3, 1, 4)
        grad_cross_kv = weight_grad(flat_encoder, pair_low.reshape(rows, 2 * WIDTH))
        grad_self_in = weight_grad(flat_tokens, self_low_grads.reshape(rows, 3 * WIDTH))
        norms = lax.psum(norms, ("dp", "blk"))
    ((grad_cross_q, grad_self_out),) = finish_terms([mid_pairs], mid_terms)
    (grad_cross_out,), (grad_adapt_down, grad_adapt_up) = finish_terms(high_groups, high_terms)
    return (
        output.reshape(lanes, span, WIDTH),
        tokens_grad.reshape(lanes, span, WIDTH),
        encoder_grad.reshape(lanes, span, WIDTH),
        grad_self_in,
        grad_self_out,
        grad_cross_q,
        grad_cross_kv,
        grad_cross_out,
        grad_adapt_down,
        grad_adapt_up,
        jnp.stack([norms[0], norms[4], norms[2]]),
        jnp.stack([norms[1], norms[5], norms[3]]),
    )


def solution(mesh):
    placed = (
        P("dp", "blk", None),
        P("dp", "blk", None),
        P("dp", "blk", None),
        P("blk", None),
        P("blk", None),
        P("blk", None),
        P("blk", None),
        P("blk", None),
        P("blk", None),
        P("blk", None),
        P("blk", None),
        P("blk", None),
        P(),
        P(),
        P("dp", None),
        P("dp", None),
    )
    return jax.shard_map(
        shards,
        mesh=mesh,
        in_specs=placed,
        out_specs=(
            P("dp", "blk", None),
            P("dp", "blk", None),
            P("dp", "blk", None),
            P("blk", None),
            P("blk", None),
            P("blk", None),
            P("blk", None),
            P("blk", None),
            P("blk", None),
            P("blk", None),
            P(),
            P(),
        ),
        check_vma=False,
    )
```

```python
import functools
import math

import jax
import jax.numpy as jnp
from jax import lax
from jax.experimental import pallas as pl
from jax.experimental.pallas import tpu as pltpu
from jax.sharding import PartitionSpec as P

HEADS = 16
HEAD_DIM = 64
WIDTH = HEADS * HEAD_DIM


NEG = -1e30
VMEM_BYTES = 56 * 1024 * 1024


def cost(microseconds):
    return pl.CostEstimate(
        flops=int(microseconds * 0.4e9),
        bytes_accessed=int(microseconds * 1.2e6),
        transcendentals=0,
    )


def paired():
    return lax.axis_size("blk") == 16 and lax.axis_size("dp") == 2


def swap_core(block):
    cores = lax.axis_size("dp")
    return lax.ppermute(block, "dp", [(i ^ 1, i) for i in range(cores)])


def flip(block, bit):
    chips = lax.axis_size("blk")
    return lax.ppermute(block, "blk", [(i ^ bit, i) for i in range(chips)])


FLIPS = (8, 4, 2, 1)


def with_flip(block, bit):
    return jnp.stack([block, flip(block, bit)])


def own_half(values, which):
    half = values.shape[1] // 2
    return lax.dynamic_slice_in_dim(values, which * half, half, 1)


def scatter_chips(terms, orders, first, last, holds=None):
    if not paired():
        return terms, [terms] * 5
    own = lax.axis_index("blk")

    def fold(blocks, left, bit):
        axis, place = left.index(bit), (own // bit) % 2
        kept = lax.dynamic_index_in_dim(blocks, place, axis, keepdims=False)
        sent = lax.dynamic_index_in_dim(blocks, 1 - place, axis, keepdims=False)
        got = flip(sent, bit)
        return (kept.astype(jnp.float32) + got.astype(jnp.float32)).astype(jnp.bfloat16)

    if first == 0:
        terms = [blocks.reshape(2, 2, 2, 2, *blocks.shape[1:]) for blocks in terms]
    stages = [terms[0]]
    for stage in range(first, last):
        if holds and stage in holds:
            terms = after(terms, holds[stage])
        terms = [
            fold(blocks, [bit for bit in FLIPS if bit not in order[:stage]], order[stage])
            for blocks, order in zip(terms, orders)
        ]
        stages.append(terms[0])
    return terms, stages


CHUNK = 256


def grad_terms(pairs):
    if not paired():
        return pairs[0][1]
    core = lax.axis_index("dp")
    packed = []
    for inputs, upstream in pairs:
        both = jnp.concatenate([inputs, swap_core(inputs)], axis=0)
        half = jnp.concatenate(
            [own_half(upstream, core), swap_core(own_half(upstream, 1 - core))], axis=0
        )
        term = lax.dot_general(
            both, half, (((0,), (0,)), ((), ())), preferred_element_type=jnp.float32
        ).astype(jnp.bfloat16)
        rows = term.shape[0] // 16
        chunks = term.shape[1] // CHUNK
        packed += [
            term[:, c * CHUNK : (c + 1) * CHUNK].reshape(16, rows, CHUNK) for c in range(chunks)
        ]
    return jnp.concatenate(packed, axis=1)


def finish_terms(groups, terms):
    if not paired():
        return [[weight_grad(inputs, upstream) for inputs, upstream in pairs] for pairs in groups]
    core = lax.axis_index("dp")
    mine = jnp.concatenate(terms, axis=0)
    other = swap_core(mine)
    low = jnp.where(core == 0, mine, other).astype(jnp.float32)
    high = jnp.where(core == 0, other, mine).astype(jnp.float32)
    found, place = [], 0
    for pairs in groups:
        found.append([])
        for inputs, upstream in pairs:
            rows = inputs.shape[1] // 16
            chunks = upstream.shape[1] // 2 // CHUNK
            spots = [slice(place + c * rows, place + (c + 1) * rows) for c in range(chunks)]
            found[-1].append(
                jnp.concatenate(
                    [low[spot] for spot in spots] + [high[spot] for spot in spots], axis=1
                )
            )
            place += rows * chunks
    return found


def weight_grad(inputs, upstream):
    scattered = lax.psum_scatter(
        lax.dot_general(
            inputs, upstream, (((0,), (0,)), ((), ())), preferred_element_type=jnp.float32
        ).astype(jnp.bfloat16),
        "blk",
        scatter_dimension=0,
        tiled=True,
    )
    return lax.psum(scattered, "dp").astype(jnp.float32)


class Source:
    def __init__(self, kind, arrays, first_flip="x", column=None):
        self.kind, self.arrays, self.first_flip = kind, arrays, first_flip
        self.stages = arrays[:1] * 3 if column is None else [column] + arrays[:2]


class Part:
    def __init__(self, rows, width, spots):
        self.rows, self.width, self.spots = rows, width, spots

    def scratch(self):
        return pltpu.VMEM((2, 2, 2, 2, 2, self.rows // 32, self.width), jnp.bfloat16)

    def start(self, refs_of, place, dst, sem):
        z1, z0, y, x, core = [place[axis] for axis in range(5)]
        high = self.rows // 32
        for source, first_row, first_col, at_col, width in self.spots:
            refs = refs_of(source)
            cols = slice(first_col, first_col + width)
            into = slice(at_col, at_col + width)
            if source.kind == "whole":
                pltpu.make_async_copy(
                    refs[0].at[:, :, :, :, :, :, cols], dst.at[:, :, :, :, :, :, into], sem
                ).start()
            elif source.kind == "cores":
                for which in range(2):
                    owner = core if which == 0 else 1 - core
                    pltpu.make_async_copy(
                        refs[which].at[:, :, :, :, first_row : first_row + high, cols],
                        dst.at[:, :, :, :, owner, :, into],
                        sem,
                    ).start()
            else:
                for which in range(4):
                    owner = core if which < 2 else 1 - core
                    for near, at_y, at_x in flipped(source.first_flip, which % 2, y, x):
                        for up, at_z1, at_z0 in four(z1, z0):
                            pltpu.make_async_copy(
                                refs[which].at[near, up[0], up[1], :, cols],
                                dst.at[at_z1, at_z0, at_y, at_x, owner, :, into],
                                sem,
                            ).start()


def four(z1, z0):
    return [
        ((low, high), z1 if high == 0 else 1 - z1, z0 if low == 0 else 1 - z0)
        for low in range(2)
        for high in range(2)
    ]


def flipped(first_flip, beyond, y, x):
    found = []
    for near in range(2):
        a, b = (near, beyond) if first_flip == "x" else (beyond, near)
        found.append((near, y if b == 0 else 1 - y, x if a == 0 else 1 - x))
    return found


def after(value, *others):
    return lax.optimization_barrier((value, *others))[0]


def gather_flips(shards, first_flips, hold=None):
    if not paired():
        full = [lax.all_gather(shard, "blk", axis=0, tiled=True) for shard in shards]
        return [
            Source("whole", [array.reshape(2, 2, 2, 2, 2, array.shape[0] // 32, array.shape[1])])
            for array in full
        ]
    core = lax.axis_index("dp")
    columns = []
    for shard in shards:
        rows = shard.shape[0]
        own = lax.dynamic_slice_in_dim(shard, core * (rows // 2), rows // 2, 0)
        columns.append(with_flip(with_flip(own, 8), 4))
    sources, bits = [], {"x": (1, 2), "y": (2, 1)}
    if hold is not None:
        columns = after(columns, hold)
    planes = [
        with_flip(column, bits[first][0]) for column, first in zip(columns, first_flips)
    ]
    for column, plane, first in zip(columns, planes, first_flips):
        beyond = flip(plane, bits[first][1])
        sources.append(
            Source("flips", [plane, beyond, swap_core(plane), swap_core(beyond)], first, column)
        )
    return sources


class RowPart:
    def __init__(self, sources, span):
        self.span = span
        self.rows, self.width = 16 * span, WIDTH
        self.spots = [(source,) for source in sources]

    def scratch(self):
        return pltpu.VMEM((2, 2, 2, 2, self.span, WIDTH), jnp.bfloat16)

    def start(self, refs_of, place, dst, sem):
        z1, z0, y, x = [place[axis] for axis in range(4)]
        half = WIDTH // 2
        for side, (source,) in enumerate(self.spots):
            refs = refs_of(source)
            for beyond in range(2):
                for near, at_y, at_x in flipped(source.first_flip, beyond, y, x):
                    for up, at_z1, at_z0 in four(z1, z0):
                        pltpu.make_async_copy(
                            refs[beyond].at[near, up[0], up[1]],
                            dst.at[at_z1, at_z0, at_y, at_x, :, side * half : (side + 1) * half],
                            sem,
                        ).start()


def gather_row(block, hold_near=None, hold=None):
    row = lax.axis_index("blk") // 8
    own = lax.dynamic_index_in_dim(block, row, 0, keepdims=False)
    other = lax.dynamic_index_in_dim(block, 1 - row, 0, keepdims=False)
    pair = jnp.stack([own, flip(other, 8)])
    if hold_near is not None:
        pair = after(pair, hold_near)
    column = with_flip(pair, 4)
    stages, sources = [pair, column], []
    if hold is not None:
        column = after(column, hold)
    half = WIDTH // 2
    planes = [with_flip(column[..., :half], 1), with_flip(column[..., half:], 2)]
    for plane, first, bit in zip(planes, "xy", (2, 1)):
        sources.append(Source("row", [plane, flip(plane, bit)], first))
    stages += [planes, [source.arrays[1] for source in sources]]
    return RowPart(sources, block.shape[1]), stages


def head_columns(shards, kinds):
    core = lax.axis_index("dp")
    blocks, widths = [], [128 * kind for kind in kinds]
    for shard, kind in zip(shards, kinds):
        own = lax.dynamic_slice_in_dim(shard, core * 32, 32, 0)
        own = own.reshape(32, kind, 8, 128).transpose(2, 0, 1, 3)
        blocks.append(own.reshape(8, 32, kind * 128))
    blocks = jnp.concatenate(blocks, axis=2)
    mine = exchange(jnp.concatenate([blocks, blocks], axis=0))
    mine = mine.reshape(2, 2, 2, 2, 32, sum(widths))
    source = Source("cores", [mine, swap_core(mine)])
    parts, place = [], 0
    for width in widths:
        parts.append(Part(1024, width, [(source, 0, place, 0, width)]))
        place += width
    return parts


def project_row(row_part, head_part, name):
    def body(ins, loaded, outs, _):
        weight = loaded[1].value()
        inputs = loaded[0].value()
        for first in range(0, row_part.rows, 256):
            rows = slice(first, first + 256)
            outs[0][rows, :] = dot(inputs[rows], weight).astype(jnp.bfloat16)

    (found,) = call_with_parts(
        body,
        [],
        [row_part, head_part],
        [shape(row_part.rows, head_part.width, of=jnp.bfloat16)],
        name,
    )
    return found


def row_grad(row_part, upstream, name):
    columns = upstream.shape[1]

    def body(ins, loaded, outs, _):
        core = ins[1][0]
        inputs = loaded[0].value()
        grads = []
        for first in range(0, columns, 128):
            grads.append(pair_dot(ins[0][:, first : first + 128], inputs, 0, 0).T)
        grad = jnp.concatenate(grads, axis=1).astype(jnp.bfloat16).reshape(16, 2, 32, columns)
        outs[0][core] = grad[:, 0]
        outs[0][1 - core] = grad[:, 1]

    (terms,) = call_with_parts(
        body,
        [upstream],
        [row_part],
        [shape(2, 16, 32, columns, of=jnp.bfloat16)],
        name,
        scalars=[lax.axis_index("dp").reshape(1).astype(jnp.int32)],
    )
    got = swap_core(terms[1])
    return (terms[0].astype(jnp.float32) + got.astype(jnp.float32)).astype(jnp.bfloat16)


def row_back(upstream, head_part, name):
    def body(ins, loaded, outs, _):
        weight = loaded[0].value()
        for first in range(0, ins[0].shape[0], 256):
            rows = slice(first, first + 256)
            outs[0][rows, :] = dot_back(ins[0][rows, :], weight).astype(jnp.bfloat16)

    (terms,) = call_with_parts(
        body, [upstream], [head_part], [shape(upstream.shape[0], WIDTH, of=jnp.bfloat16)], name
    )
    return terms


def reduce_row(terms, holds=None):
    blocks = terms.reshape(16, terms.shape[0] // 16, WIDTH)
    (both,), stages = scatter_chips([blocks], [(1, 2, 4, 8)], 0, 3, holds)
    row = lax.axis_index("blk") // 8
    kept = lax.dynamic_index_in_dim(both, row, 0, keepdims=False)
    got = flip(lax.dynamic_index_in_dim(both, 1 - row, 0, keepdims=False), 8)
    found = jnp.stack([jnp.where(row == 0, kept, got), jnp.where(row == 0, got, kept)])
    return found.astype(jnp.float32), stages


def finish_row_grad(got, kinds):
    total = jnp.sum(got.reshape(2, 8, 32, kinds, 128).astype(jnp.float32), axis=0)
    mine = total.astype(jnp.bfloat16).transpose(1, 2, 0, 3).reshape(32, kinds * WIDTH)
    other = swap_core(mine)
    core = lax.axis_index("dp")
    low = jnp.where(core == 0, mine, other)
    high = jnp.where(core == 0, other, mine)
    return jnp.concatenate([low, high], axis=0).astype(jnp.float32)


def columns_of(*pieces):
    spots, place = [], 0
    for source, first, width in pieces:
        spots.append((source, 0, first, place, width))
        place += width
    return Part(1024, place, spots)


PACK = 512


def pack_halves(shards):
    places = [
        (index, shard.shape[0] // 2, first)
        for index, shard in enumerate(shards)
        for first in range(0, shard.shape[1], PACK)
    ]

    def body(core, *refs):
        out_ref, place = refs[-1], 0
        for index, high, first in places:
            start = pl.multiple_of(core[0] * high, 16)
            out_ref[place : place + high, :] = refs[index][pl.ds(start, high), first : first + PACK]
            place += high

    return pl.pallas_call(
        body,
        out_shape=shape(sum(high for _, high, _ in places), PACK, of=jnp.bfloat16),
        in_specs=[smem_spec()] + [vmem_spec()] * len(shards),
        out_specs=vmem_spec(),
        compiler_params=pltpu.CompilerParams(vmem_limit_bytes=VMEM_BYTES),
        cost_estimate=cost(2),
        name="pack_halves",
    )(lax.axis_index("dp").reshape(1).astype(jnp.int32), *shards)


def gather_packed(packed):
    return lax.all_gather(packed, "blk", axis=0)


def packed_parts(shards, mine):
    if not paired():
        found = []
        for source, shard in zip(gather_flips(shards, "x" * len(shards)), shards):
            rows, columns = 32 * source.arrays[0].shape[5], shard.shape[1]
            step = min(columns, 1024)
            found.append(
                [
                    Part(rows, step, [(source, 0, first, 0, step)])
                    for first in range(0, columns, step)
                ]
            )
        return found
    spots, place = [], 0
    for shard in shards:
        high = shard.shape[0] // 2
        places = []
        for first in range(0, shard.shape[1], PACK):
            places.append(place)
            place += high
        spots.append((shard.shape[0] * 16, places))
    mine = mine.reshape(2, 2, 2, 2, place, PACK)
    source = Source("cores", [mine, swap_core(mine)])
    found = []
    for rows, places in spots:
        parts = []
        for first in range(0, len(places), 2):
            two = places[first : first + 2]
            parts.append(
                Part(
                    rows,
                    PACK * len(two),
                    [(source, row, 0, PACK * side, PACK) for side, row in enumerate(two)],
                )
            )
        found.append(parts)
    return found


def place_now():
    own, core = lax.axis_index("blk"), lax.axis_index("dp")
    bits = [(own // bit) % 2 for bit in FLIPS]
    return jnp.stack(bits + [core]).astype(jnp.int32)


class Loaded:
    def __init__(self, part, dst, sem):
        self.part, self.dst, self.sem, self.here = part, dst, sem, False

    def value(self):
        if not self.here:
            pltpu.make_async_copy(self.dst, self.dst, self.sem).wait()
            self.here = True
        return self.dst[...].reshape(self.part.rows, self.part.width)


def call_with_parts(body, inputs, parts, outputs, name, scratch=(), takes=5, scalars=()):
    sources = []
    for part in parts:
        sources += [spot[0] for spot in part.spots if spot[0] not in sources]
    arrays = [array for source in sources for array in source.arrays]

    def kernel(place, *refs):
        refs = list(refs)
        ins = [refs.pop(0) for _ in (*inputs, *scalars)]
        pieces = [[refs.pop(0) for _ in source.arrays] for source in sources]
        outs = [refs.pop(0) for _ in outputs]
        dsts = [refs.pop(0) for _ in parts]
        sems = refs.pop(0)
        loaded = []
        for index, part in enumerate(parts):
            part.start(
                lambda source: pieces[sources.index(source)], place, dsts[index], sems.at[index]
            )
            loaded.append(Loaded(part, dsts[index], sems.at[index]))
        body(ins, loaded, outs, refs)

    return pl.pallas_call(
        kernel,
        out_shape=tuple(outputs),
        in_specs=[smem_spec()]
        + [vmem_spec()] * len(inputs)
        + [smem_spec()] * len(scalars)
        + [pl.BlockSpec(memory_space=pl.ANY)] * len(arrays),
        out_specs=(vmem_spec(),) * len(outputs),
        scratch_shapes=[part.scratch() for part in parts]
        + [pltpu.SemaphoreType.DMA((len(parts),))]
        + list(scratch),
        compiler_params=pltpu.CompilerParams(vmem_limit_bytes=VMEM_BYTES),
        cost_estimate=cost(takes),
        name=name,
    )(place_now(), *inputs, *scalars, *arrays)


def vmem_spec():
    return pl.BlockSpec(memory_space=pltpu.VMEM)


def smem_spec():
    return pl.BlockSpec(memory_space=pltpu.SMEM)


def seg_of_pos(ends_ref, pos):
    seg = jnp.zeros(pos.shape, jnp.int32)
    for slot in range(ends_ref.shape[0]):
        seg = seg + (ends_ref[slot] <= pos).astype(jnp.int32)
    return seg


def pair_dot(left, right, left_dim, right_dim):
    return lax.dot_general(
        left, right, (((left_dim,), (right_dim,)), ((), ())), preferred_element_type=jnp.float32
    )


def seg_tables(q_ends, k_ends, span):
    seg_q = seg_of_pos(q_ends, lax.broadcasted_iota(jnp.int32, (1, span), 1))
    seg_k = seg_of_pos(k_ends, lax.broadcasted_iota(jnp.int32, (span, 1), 0))
    return seg_q, seg_k


def masked_scores(keys, queries, seg_q, seg_k, first, causal):
    scores = pair_dot(keys, queries, 1, 1)
    allowed = seg_k == seg_q
    if causal:
        key_pos = lax.broadcasted_iota(jnp.int32, scores.shape, 0)
        query_pos = first + lax.broadcasted_iota(jnp.int32, scores.shape, 1)
        allowed = allowed & (key_pos <= query_pos)
    return jnp.where(allowed, scores, NEG)


def attn_forward_body(causal, width, q_ends, k_ends, q_ref, kv_ref, low_ref, full_ref, lse_ref):
    span = q_ref.shape[0]
    step = math.gcd(span, 256)
    heads = width // HEAD_DIM
    seg_q, seg_k = seg_tables(q_ends, k_ends, span)
    key_at = kv_ref.shape[1] - 2 * width
    scaled = q_ref[:, :width] * jnp.bfloat16(HEAD_DIM ** (-0.5))
    keys = kv_ref[:, key_at : key_at + width]
    values = kv_ref[:, key_at + width : key_at + 2 * width]
    for first in range(0, span, step):
        reach = first + step if causal else span
        parts = []
        for head in range(heads):
            cols = slice(head * HEAD_DIM, (head + 1) * HEAD_DIM)
            scores = masked_scores(
                keys[:reach, cols],
                scaled[first : first + step, cols],
                seg_q[:, first : first + step],
                seg_k[:reach],
                first,
                causal,
            )
            top = jnp.max(scores, axis=0, keepdims=True)
            probs = jnp.exp(scores - top)
            total = jnp.sum(probs, axis=0, keepdims=True)
            mixed = pair_dot(values[:reach, cols], probs.astype(jnp.bfloat16), 0, 0)
            parts.append(mixed / total)
            lse_ref[head : head + 1, first : first + step] = top + jnp.log(total)
        joined = jnp.concatenate(parts, axis=0).T
        full_ref[first : first + step, :] = joined
        low_ref[first : first + step, :] = joined.astype(jnp.bfloat16)


def attn_forward(q_ends, k_ends, queries, keys_values, width, causal):
    span = queries.shape[0]
    return pl.pallas_call(
        functools.partial(attn_forward_body, causal, width),
        out_shape=(
            jax.ShapeDtypeStruct((span, width), jnp.bfloat16),
            jax.ShapeDtypeStruct((span, width), jnp.float32),
            jax.ShapeDtypeStruct((width // HEAD_DIM, span), jnp.float32),
        ),
        in_specs=[smem_spec(), smem_spec()] + [vmem_spec()] * 2,
        out_specs=(vmem_spec(),) * 3,
        compiler_params=pltpu.CompilerParams(vmem_limit_bytes=VMEM_BYTES),
        cost_estimate=cost(8),
        name="attn_forward",
    )(q_ends, k_ends, queries, keys_values)


def attn_backward_body(
    causal,
    width,
    q_ends,
    k_ends,
    q_ref,
    kv_ref,
    up_ref,
    full_ref,
    lse_ref,
    *outs,
):
    dq_ref, dkv_ref = outs[0], outs[-3]
    dk_sum, dv_sum = outs[-2:]
    span = q_ref.shape[0]
    step = math.gcd(span, 256)
    heads = width // HEAD_DIM
    seg_q, seg_k = seg_tables(q_ends, k_ends, span)
    key_at = kv_ref.shape[1] - 2 * width
    scaled = q_ref[:, :width] * jnp.bfloat16(HEAD_DIM ** (-0.5))
    keys = kv_ref[:, key_at : key_at + width]
    values = kv_ref[:, key_at + width : key_at + 2 * width]
    upstream = up_ref[...]
    dk_sum[...] = jnp.zeros_like(dk_sum)
    dv_sum[...] = jnp.zeros_like(dv_sum)
    for first in range(0, span, step):
        reach = first + step if causal else span
        rows = slice(first, first + step)
        product = (upstream[rows].astype(jnp.float32) * full_ref[rows, :]).T
        parts = []
        for head in range(heads):
            cols = slice(head * HEAD_DIM, (head + 1) * HEAD_DIM)
            delta = jnp.sum(product[cols], axis=0, keepdims=True)
            scores = masked_scores(
                keys[:reach, cols], scaled[rows, cols], seg_q[:, rows], seg_k[:reach], first, causal
            )
            probs = jnp.exp(scores - lse_ref[head : head + 1, rows])
            dv_sum[head, :reach] += pair_dot(
                probs.astype(jnp.bfloat16), upstream[rows, cols], 1, 0
            )
            grad_probs = pair_dot(values[:reach, cols], upstream[rows, cols], 1, 1)
            grad_scores = (probs * (grad_probs - delta)).astype(jnp.bfloat16)
            dk_sum[head, :reach] += pair_dot(grad_scores, scaled[rows, cols], 1, 0)
            parts.append(pair_dot(keys[:reach, cols], grad_scores, 0, 0))
        joined = jnp.concatenate(parts, axis=0).T * HEAD_DIM ** (-0.5)
        dq_ref[rows, :width] = joined.astype(jnp.bfloat16)
    sums = [dk_sum[head] for head in range(heads)] + [dv_sum[head] for head in range(heads)]
    kv_at = dkv_ref.shape[1] - 2 * width
    dkv_ref[:, kv_at:] = jnp.concatenate(sums, axis=1).astype(jnp.bfloat16)


def attn_backward(
    q_ends, k_ends, queries, keys_values, upstream, full, lse, causal, joined=False
):
    span, width = upstream.shape
    kinds = [3] if joined else [1, 2]
    heads = width // HEAD_DIM
    return pl.pallas_call(
        functools.partial(attn_backward_body, causal, width),
        out_shape=[jax.ShapeDtypeStruct((span, kind * width), jnp.bfloat16) for kind in kinds],
        in_specs=[smem_spec(), smem_spec()] + [vmem_spec()] * 5,
        out_specs=[vmem_spec()] * len(kinds),
        scratch_shapes=[pltpu.VMEM((heads, span, HEAD_DIM), jnp.float32)] * 2,
        compiler_params=pltpu.CompilerParams(vmem_limit_bytes=VMEM_BYTES),
        cost_estimate=cost(8),
        name="attn_backward",
    )(q_ends, k_ends, queries, keys_values, upstream, full, lse)


def exchange(blocks):
    return lax.all_to_all(blocks, "blk", 0, 0, tiled=True)


def as_rows(blocks):
    return blocks.reshape(blocks.shape[0] * blocks.shape[1], blocks.shape[2])


def as_blocks(rows):
    devices = lax.axis_size("blk")
    return rows.reshape(devices, rows.shape[0] // devices, rows.shape[1])


def write_blocks(out_ref, values, lanes, kind, width):
    span = values.shape[0] // lanes
    for group in range(WIDTH // width):
        for lane in range(lanes):
            out_ref[lane * (WIDTH // width) + group, :, kind * width : (kind + 1) * width] = values[
                lane * span : (lane + 1) * span, group * width : (group + 1) * width
            ]


def read_blocks(got_ref, lanes, kind, width):
    groups = got_ref.shape[0] // lanes
    cols = slice(kind * width, (kind + 1) * width)
    rows = [
        jnp.concatenate([got_ref[lane * groups + group, :, cols] for group in range(groups)], axis=1)
        for lane in range(lanes)
    ]
    return jnp.concatenate(rows, axis=0)


def dot(left, right):
    return pair_dot(left, right, 1, 0)


def dot_back(left, right):
    return pair_dot(left, right, 1, 1)


def shape(*sizes, of=jnp.float32):
    return jax.ShapeDtypeStruct(sizes, of)


def normalize(values):
    center = values - jnp.mean(values, -1, keepdims=True)
    scale = lax.rsqrt(jnp.mean(center * center, -1, keepdims=True) + 1e-05)
    return center * scale, scale


def norm_back(upstream, normed, scale, gains_row):
    grad = upstream * gains_row
    return scale * (
        grad
        - jnp.mean(grad, -1, keepdims=True)
        - normed * jnp.mean(grad * normed, -1, keepdims=True)
    )


def project_blocks(inputs, parts, lanes, width, name):
    def body(ins, loaded, outs, _):
        for kind, weight in enumerate(loaded):
            write_blocks(
                outs[0], dot(ins[0][...], weight.value()).astype(jnp.bfloat16), lanes, kind, width
            )

    devices, span = lax.axis_size("blk"), inputs.shape[0] // lanes
    (blocks,) = call_with_parts(
        body,
        [inputs],
        parts,
        [shape(devices, span, width * len(parts), of=jnp.bfloat16)],
        name,
    )
    return blocks


def after_self(got, tokens, gains, biases, out_part, query_part, lanes, width):
    def body(ins, loaded, outs, _):
        got_ref, tokens_ref, gains_ref, biases_ref = ins
        low_ref, normed_ref, scale_ref, hidden_ref, blocks_ref = outs
        attended = read_blocks(got_ref, lanes, 0, width)
        low_ref[...] = attended
        resid = tokens_ref[...].astype(jnp.float32) + dot(attended, loaded[0].value())
        normed, scale = normalize(resid)
        normed_ref[...] = normed
        scale_ref[...] = scale
        hidden = (normed * gains_ref[0:1] + biases_ref[0:1]).astype(jnp.bfloat16)
        hidden_ref[...] = hidden
        query = dot(hidden, loaded[1].value()).astype(jnp.bfloat16)
        write_blocks(blocks_ref, query, lanes, 0, width)

    rows = tokens.shape[0]
    return call_with_parts(
        body,
        [got, tokens, gains, biases],
        [out_part, query_part],
        [
            shape(rows, WIDTH, of=jnp.bfloat16),
            shape(rows, WIDTH),
            shape(rows, 1),
            shape(rows, WIDTH, of=jnp.bfloat16),
            shape(*got.shape, of=jnp.bfloat16),
        ],
        "after_self",
    )


def feed_forward(got, normed_in, cotangent, gains, biases, out_part, in_parts, down, outs, up, lanes, width):
    pieces = len(in_parts)
    step = in_parts[0].width

    def body(ins, loaded, refs, scratch):
        got_ref, normed_in_ref, cot_ref, gains_ref, biases_ref = ins
        (
            output_ref,
            low_ref,
            mixed_ref,
            adapted_ref,
            dunder_ref,
            dab_ref,
            dcb_ref,
            dresid_ref,
            blocks_ref,
            norms_ref,
        ) = refs
        slopes, acts = scratch
        w_out, w_down, w_in = loaded[0], loaded[1], loaded[2 : 2 + pieces]
        w_ff, w_up = loaded[2 + pieces :]
        attended = read_blocks(got_ref, lanes, 0, width)
        low_ref[...] = attended
        hidden = normed_in_ref[...] * gains_ref[0:1] + biases_ref[0:1]
        normed_one, scale_one = normalize(hidden + dot(attended, w_out.value()))
        mixed = normed_one * gains_ref[1:2] + biases_ref[1:2]
        mixed_low = mixed.astype(jnp.bfloat16)
        mixed_ref[...] = mixed_low
        summed = mixed
        under = dot(mixed_low, w_down.value())
        gate = 1.0 / (1.0 + jnp.exp(-under))
        adapted = (under * gate).astype(jnp.bfloat16)
        adapted_ref[...] = adapted
        under_slope = gate * (1.0 + under * (1.0 - gate))
        for piece in range(pieces):
            before = dot(mixed_low, w_in[piece].value())
            below = 0.5 + 0.5 * lax.erf(before * (0.5**0.5))
            slopes[piece] = below + before * jnp.exp(-0.5 * before * before) * (
                (2.0 * math.pi) ** -0.5
            )
            acts[piece] = (before * below).astype(jnp.bfloat16)
        for piece in range(pieces):
            summed = summed + dot(acts[piece], w_ff[piece].value())
        summed = summed + 4.0 * dot(adapted, w_up.value())
        normed_two, scale_two = normalize(summed)
        output_ref[...] = (normed_two * gains_ref[2:3] + biases_ref[2:3]).astype(jnp.bfloat16)
        upstream = cot_ref[...].astype(jnp.float32)
        norms_ref[0:1] = jnp.sum(upstream * normed_two, axis=0, keepdims=True)
        norms_ref[1:2] = jnp.sum(upstream, axis=0, keepdims=True)
        dz = norm_back(upstream, normed_two, scale_two, gains_ref[2:3])
        dzb = dz.astype(jnp.bfloat16)
        dab = (4.0 * dz).astype(jnp.bfloat16)
        dab_ref[...] = dab
        dunder = (under_slope * dot_back(dab, w_up.value())).astype(jnp.bfloat16)
        dunder_ref[...] = dunder
        dmixed = dz + dot_back(dunder, w_down.value())
        for piece in range(pieces):
            dpre = (slopes[piece] * dot_back(dzb, w_ff[piece].value())).astype(jnp.bfloat16)
            dmixed = dmixed + dot_back(dpre, w_in[piece].value())
        norms_ref[2:3] = jnp.sum(dmixed * normed_one, axis=0, keepdims=True)
        norms_ref[3:4] = jnp.sum(dmixed, axis=0, keepdims=True)
        dresid = norm_back(dmixed, normed_one, scale_one, gains_ref[1:2])
        dresid_ref[...] = dresid
        dcb = dresid.astype(jnp.bfloat16)
        dcb_ref[...] = dcb
        write_blocks(
            blocks_ref, dot_back(dcb, w_out.value()).astype(jnp.bfloat16), lanes, 0, width
        )

    rows = normed_in.shape[0]
    low = jnp.bfloat16

    def body_rows(ins, loaded, refs, scratch):
        whole_ff = loaded[2 + pieces]

        class Rows:
            def __init__(self, piece):
                self.piece = piece

            def value(self):
                return whole_ff.value()[self.piece * step : (self.piece + 1) * step]

        loaded = loaded[: 2 + pieces] + [[Rows(piece) for piece in range(pieces)], loaded[-1]]
        body(ins, loaded, refs, scratch)

    return call_with_parts(
        body_rows,
        [got, normed_in, cotangent, gains, biases],
        [out_part, down] + in_parts + [outs, up],
        [
            shape(rows, WIDTH, of=low),
            shape(rows, WIDTH, of=low),
            shape(rows, WIDTH, of=low),
            shape(rows, down.width, of=low),
            shape(rows, down.width, of=low),
            shape(rows, WIDTH, of=low),
            shape(rows, WIDTH, of=low),
            shape(rows, WIDTH),
            shape(*got.shape, of=low),
            shape(4, WIDTH),
        ],
        "feed_forward",
        [
            pltpu.VMEM((pieces, rows, step), jnp.float32),
            pltpu.VMEM((pieces, rows, step), jnp.bfloat16),
        ],
        20,
    )


def before_self(got, dresid, normed, scale, gains, query_part, out_part, lanes, width):
    def body(ins, loaded, outs, _):
        got_ref, dresid_ref, normed_ref, scale_ref, gains_ref = ins
        dcq_ref, dr_ref, dsb_ref, blocks_ref, norms_ref = outs
        dcq = read_blocks(got_ref, lanes, 0, width)
        dcq_ref[...] = dcq
        dhidden = dresid_ref[...] + dot_back(dcq, loaded[0].value())
        normed = normed_ref[...]
        norms_ref[0:1] = jnp.sum(dhidden * normed, axis=0, keepdims=True)
        norms_ref[1:2] = jnp.sum(dhidden, axis=0, keepdims=True)
        dr = norm_back(dhidden, normed, scale_ref[...], gains_ref[0:1])
        dr_ref[...] = dr
        dsb = dr.astype(jnp.bfloat16)
        dsb_ref[...] = dsb
        grad = dot_back(dsb, loaded[1].value()).astype(jnp.bfloat16)
        write_blocks(blocks_ref, grad, lanes, 0, width)

    rows = dresid.shape[0]
    return call_with_parts(
        body,
        [got, dresid, normed, scale, gains],
        [query_part, out_part],
        [
            shape(rows, WIDTH, of=jnp.bfloat16),
            shape(rows, WIDTH),
            shape(rows, WIDTH, of=jnp.bfloat16),
            shape(*got.shape, of=jnp.bfloat16),
            shape(2, WIDTH),
        ],
        "before_self",
    )


def input_grad(got, start, parts, lanes, span, width, name):
    def body(ins, loaded, outs, _):
        total = None
        for kind, weight in enumerate(loaded):
            values = read_blocks(ins[0], lanes, kind, width)
            term = dot_back(values, weight.value())
            total = term if total is None else total + term
        outs[0][...] = total if len(ins) == 1 else total + ins[1][...]

    rows = span * lanes
    return call_with_parts(
        body,
        [got] if start is None else [got, start],
        parts,
        [shape(rows, WIDTH)],
        name,
    )


def shards(
    tokens,
    encoder,
    cotangent,
    self_in,
    self_out,
    cross_q,
    cross_kv,
    cross_out,
    ffn_in,
    ffn_out,
    adapt_down,
    adapt_up,
    norm_gain,
    norm_bias,
    tgt_lengths,
    src_lengths,
):
    lanes, span, _ = tokens.shape
    rows = lanes * span
    width = WIDTH * lanes // lax.axis_size("blk")
    own_row = lax.axis_index("blk") // (lax.axis_size("blk") // lanes)
    tgt_ends = jnp.cumsum(lax.dynamic_index_in_dim(tgt_lengths, own_row, 0, keepdims=False))
    src_ends = jnp.cumsum(lax.dynamic_index_in_dim(src_lengths, own_row, 0, keepdims=False))
    flat_tokens = tokens.reshape(rows, WIDTH)
    flat_encoder = encoder.reshape(rows, WIDTH)
    frozen = [ffn_in, adapt_down, ffn_out, adapt_up, cross_out]

    if paired():
        packed = gather_packed(pack_halves(frozen))
        self_packed = pack_halves([self_in])
        token_row, stages = gather_row(tokens)
        self_heads, pair_heads = head_columns([self_in, cross_kv], [3, 2])
        out_shard, query_shard = after((self_out, cross_q), stages[1])
        encoder_block = after(encoder, stages[1])
        self_qkv = project_row(token_row, self_heads, "self_in")
        out_source, query_source = gather_flips([out_shard, query_shard], "xy", self_qkv)
        encoder_row, encoder_stages = gather_row(
            encoder_block, self_qkv, (out_source.arrays[1], query_source.arrays[1])
        )
        self_qkv = after(self_qkv, out_source.stages[0], query_source.stages[0])
        pair_own = project_row(encoder_row, pair_heads, "cross_kv")
    else:
        (self_source, pair_source, out_source, query_source) = gather_flips(
            [self_in, cross_kv, self_out, cross_q], "xyxy"
        )
        self_parts = [columns_of((self_source, WIDTH * kind, WIDTH)) for kind in range(3)]
        pair_parts = [columns_of((pair_source, WIDTH * kind, WIDTH)) for kind in range(2)]
        self_qkv = as_rows(
            exchange(project_blocks(flat_tokens, self_parts, lanes, width, "self_in"))
        )
        pair_own = as_rows(
            exchange(project_blocks(flat_encoder, pair_parts, lanes, width, "cross_kv"))
        )
    self_out_part = columns_of((out_source, 0, WIDTH))
    query_part = columns_of((query_source, 0, WIDTH))

    self_mid, self_full, self_lse = attn_forward(
        tgt_ends, tgt_ends, self_qkv, self_qkv, width, True
    )
    self_sent = after(self_mid, out_source.stages[1], query_source.stages[1])
    if paired():
        self_sent = after(self_sent, encoder_stages[0])
    self_back = exchange(as_blocks(self_sent))
    if paired():
        self_back = after(self_back, encoder_stages[1])
    self_low, normed, scale, hidden_low, query_blocks = after_self(
        self_back,
        flat_tokens,
        norm_gain,
        norm_bias,
        self_out_part,
        query_part,
        lanes,
        width,
    )
    cross_own = as_rows(exchange(query_blocks))
    cross_mid, cross_full, cross_lse = attn_forward(
        tgt_ends, src_ends, cross_own, pair_own, width, False
    )
    cross_back = exchange(as_blocks(cross_mid))
    ready = after(packed, cross_mid) if paired() else None
    ff_parts, down_parts, ffo_parts, up_parts, (cross_out_part,) = packed_parts(frozen, ready)
    if paired():
        self_packed = gather_packed(after(self_packed, cross_back))
    (
        output,
        cross_low,
        mixed_low,
        adapter_low,
        grad_under,
        adapt_low,
        cross_branch_low,
        grad_resid_two,
        cross_grad_blocks,
        norms_high,
    ) = feed_forward(
        cross_back,
        normed,
        cotangent.reshape(rows, WIDTH),
        norm_gain,
        norm_bias,
        cross_out_part,
        ff_parts,
        down_parts[0],
        ffo_parts[0],
        up_parts[0],
        lanes,
        width,
    )
    high_groups = [
        [(cross_low, cross_branch_low)],
        [(mixed_low, grad_under), (adapter_low, adapt_low)],
    ]
    high_terms = [grad_terms(pairs) for pairs in high_groups]
    high_orders = [(2, 1, 4, 8), (1, 2, 4, 8)]
    high_terms, high_stages = scatter_chips(high_terms, high_orders, 0, 2)
    cross_dq, cross_dkv = attn_backward(
        tgt_ends,
        src_ends,
        cross_own,
        pair_own,
        as_rows(after(exchange(cross_grad_blocks), high_stages[0])),
        cross_full,
        cross_lse,
        False,
    )
    cross_dq_got = after(exchange(as_blocks(cross_dq)), high_stages[1])
    if paired():
        dkv_late = after(cross_dkv, high_stages[1])
        pair_terms = row_back(dkv_late, pair_heads, "encoder_grad")
        kv_sent = row_grad(encoder_row, dkv_late, "cross_kv_grad")
        cross_dq_got = after(cross_dq_got, pair_terms, kv_sent)
    cq_low, grad_resid_one, self_branch_low, self_grad_blocks, norms_low = before_self(
        cross_dq_got,
        grad_resid_two,
        normed,
        scale,
        norm_gain,
        query_part,
        self_out_part,
        lanes,
        width,
    )
    norms = jnp.concatenate([norms_low, norms_high], axis=0)
    mid_pairs = [(hidden_low, cq_low), (self_low, self_branch_low)]
    mid_orders = [(2, 1, 4, 8), (1, 2, 4, 8)]
    mid_terms = [grad_terms([pair]) for pair in mid_pairs]
    mid_terms, _ = scatter_chips(mid_terms, mid_orders, 0, 1)
    if paired():
        high_terms = [jnp.concatenate(after(high_terms, self_grad_blocks), axis=2)]
        high_terms, _ = scatter_chips(high_terms, [(2, 1, 4, 8)], 2, 3)
    self_upstream = after(exchange(self_grad_blocks), high_stages[2])
    (self_grads,) = attn_backward(
        tgt_ends,
        tgt_ends,
        self_qkv,
        self_qkv,
        as_rows(self_upstream),
        self_full,
        self_lse,
        True,
        joined=True,
    )
    if paired():
        (self_parts,) = packed_parts([self_in], after(self_packed, self_grads))
        self_got = exchange(as_blocks(self_grads))
        high_terms, _ = scatter_chips(after(high_terms, self_grads), [(2, 1, 4, 8)], 3, 4)
        self_sent = row_grad(token_row, after(self_grads, high_terms[0]), "self_in_grad")
        encoder_grad, _ = reduce_row(pair_terms, {2: self_grads})
        encoder_grad = encoder_grad.reshape(rows, WIDTH)
        mid_terms, _ = scatter_chips(after(mid_terms, self_grads), mid_orders, 1, 2)
        mid_terms = [jnp.concatenate(mid_terms, axis=2)]
        mid_terms, _ = scatter_chips(mid_terms, mid_orders[:1], 2, 4)
        chunks = [
            array[:, :, first : first + width]
            for array in (self_sent, kv_sent)
            for first in range(0, array.shape[2], width)
        ]
        partials = norms.astype(jnp.bfloat16).reshape(1, 48, width)
        chunks.append(jnp.broadcast_to(partials, (16, 48, width)))
        sent = after(jnp.concatenate(chunks, axis=1), self_got)
        got = exchange(sent)
        (tokens_grad,) = input_grad(
            self_got, grad_resid_one, self_parts, lanes, span, width, "tokens_grad"
        )
        got = after(got, tokens_grad)
        chunks = [got[:, first : first + 32] for first in range(0, 160, 32)]
        grad_self_in = finish_row_grad(jnp.concatenate(chunks[:3], axis=2), 3)
        grad_cross_kv = finish_row_grad(jnp.concatenate(chunks[3:], axis=2), 2)
        norms = jnp.sum(got[:, 160:].astype(jnp.float32), axis=0).reshape(6, WIDTH)
        norms = norms + swap_core(norms)
    else:
        pair_got = exchange(as_blocks(cross_dkv))
        self_got = exchange(as_blocks(self_grads))
        (encoder_grad,) = input_grad(
            pair_got, None, pair_parts, lanes, span, width, "encoder_grad"
        )
        (tokens_grad,) = input_grad(
            self_got, grad_resid_one, self_parts, lanes, span, width, "tokens_grad"
        )
        pair_low = pair_got.reshape(lanes, -1, span, 2, width).transpose(0, 2, 3, 1, 4)
        self_low_grads = self_got.reshape(lanes, -1, span, 3, width).transpose(0, 2, 3, 1, 4)
        grad_cross_kv = weight_grad(flat_encoder, pair_low.reshape(rows, 2 * WIDTH))
        grad_self_in = weight_grad(flat_tokens, self_low_grads.reshape(rows, 3 * WIDTH))
        norms = lax.psum(norms, ("dp", "blk"))
    ((grad_cross_q, grad_self_out),) = finish_terms([mid_pairs], mid_terms)
    (grad_cross_out,), (grad_adapt_down, grad_adapt_up) = finish_terms(high_groups, high_terms)
    return (
        output.reshape(lanes, span, WIDTH),
        tokens_grad.reshape(lanes, span, WIDTH),
        encoder_grad.reshape(lanes, span, WIDTH),
        grad_self_in,
        grad_self_out,
        grad_cross_q,
        grad_cross_kv,
        grad_cross_out,
        grad_adapt_down,
        grad_adapt_up,
        jnp.stack([norms[0], norms[4], norms[2]]),
        jnp.stack([norms[1], norms[5], norms[3]]),
    )


def solution(mesh):
    placed = (
        P("dp", "blk", None),
        P("dp", "blk", None),
        P("dp", "blk", None),
        P("blk", None),
        P("blk", None),
        P("blk", None),
        P("blk", None),
        P("blk", None),
        P("blk", None),
        P("blk", None),
        P("blk", None),
        P("blk", None),
        P(),
        P(),
        P("dp", None),
        P("dp", None),
    )
    return jax.shard_map(
        shards,
        mesh=mesh,
        in_specs=placed,
        out_specs=(
            P("dp", "blk", None),
            P("dp", "blk", None),
            P("dp", "blk", None),
            P("blk", None),
            P("blk", None),
            P("blk", None),
            P("blk", None),
            P("blk", None),
            P("blk", None),
            P("blk", None),
            P(),
            P(),
        ),
        check_vma=False,
    )
```

```python
import functools
import math

import jax
import jax.numpy as jnp
from jax import lax
from jax.experimental import pallas as pl
from jax.experimental.pallas import tpu as pltpu
from jax.sharding import PartitionSpec as P

HEADS = 16
HEAD_DIM = 64
WIDTH = HEADS * HEAD_DIM


NEG = -1e30
VMEM_BYTES = 56 * 1024 * 1024


def cost(microseconds):
    return pl.CostEstimate(
        flops=int(microseconds * 0.4e9),
        bytes_accessed=int(microseconds * 1.2e6),
        transcendentals=0,
    )


def paired():
    return lax.axis_size("blk") == 16 and lax.axis_size("dp") == 2


def swap_core(block):
    cores = lax.axis_size("dp")
    return lax.ppermute(block, "dp", [(i ^ 1, i) for i in range(cores)])


def flip(block, bit):
    chips = lax.axis_size("blk")
    return lax.ppermute(block, "blk", [(i ^ bit, i) for i in range(chips)])


FLIPS = (8, 4, 2, 1)


def with_flip(block, bit):
    return jnp.stack([block, flip(block, bit)])


def own_half(values, which):
    half = values.shape[1] // 2
    return lax.dynamic_slice_in_dim(values, which * half, half, 1)


def scatter_chips(terms, orders, first, last, holds=None):
    if not paired():
        return terms, [terms] * 5
    own = lax.axis_index("blk")

    def fold(blocks, left, bit):
        axis, place = left.index(bit), (own // bit) % 2
        kept = lax.dynamic_index_in_dim(blocks, place, axis, keepdims=False)
        sent = lax.dynamic_index_in_dim(blocks, 1 - place, axis, keepdims=False)
        got = flip(sent, bit)
        return (kept.astype(jnp.float32) + got.astype(jnp.float32)).astype(jnp.bfloat16)

    if first == 0:
        terms = [blocks.reshape(2, 2, 2, 2, *blocks.shape[1:]) for blocks in terms]
    stages = [terms[0]]
    for stage in range(first, last):
        if holds and stage in holds:
            terms = after(terms, holds[stage])
        terms = [
            fold(blocks, [bit for bit in FLIPS if bit not in order[:stage]], order[stage])
            for blocks, order in zip(terms, orders)
        ]
        stages.append(terms[0])
    return terms, stages


CHUNK = 256


def grad_terms(pairs):
    if not paired():
        return pairs[0][1]
    core = lax.axis_index("dp")
    packed = []
    for inputs, upstream in pairs:
        both = jnp.concatenate([inputs, swap_core(inputs)], axis=0)
        half = jnp.concatenate(
            [own_half(upstream, core), swap_core(own_half(upstream, 1 - core))], axis=0
        )
        term = lax.dot_general(
            both, half, (((0,), (0,)), ((), ())), preferred_element_type=jnp.float32
        ).astype(jnp.bfloat16)
        rows = term.shape[0] // 16
        chunks = term.shape[1] // CHUNK
        packed += [
            term[:, c * CHUNK : (c + 1) * CHUNK].reshape(16, rows, CHUNK) for c in range(chunks)
        ]
    return jnp.concatenate(packed, axis=1)


def finish_terms(groups, terms):
    if not paired():
        return [[weight_grad(inputs, upstream) for inputs, upstream in pairs] for pairs in groups]
    core = lax.axis_index("dp")
    mine = jnp.concatenate(terms, axis=0)
    other = swap_core(mine)
    low = jnp.where(core == 0, mine, other).astype(jnp.float32)
    high = jnp.where(core == 0, other, mine).astype(jnp.float32)
    found, place = [], 0
    for pairs in groups:
        found.append([])
        for inputs, upstream in pairs:
            rows = inputs.shape[1] // 16
            chunks = upstream.shape[1] // 2 // CHUNK
            spots = [slice(place + c * rows, place + (c + 1) * rows) for c in range(chunks)]
            found[-1].append(
                jnp.concatenate(
                    [low[spot] for spot in spots] + [high[spot] for spot in spots], axis=1
                )
            )
            place += rows * chunks
    return found


def weight_grad(inputs, upstream):
    scattered = lax.psum_scatter(
        lax.dot_general(
            inputs, upstream, (((0,), (0,)), ((), ())), preferred_element_type=jnp.float32
        ).astype(jnp.bfloat16),
        "blk",
        scatter_dimension=0,
        tiled=True,
    )
    return lax.psum(scattered, "dp").astype(jnp.float32)


class Source:
    def __init__(self, kind, arrays, first_flip="x", column=None):
        self.kind, self.arrays, self.first_flip = kind, arrays, first_flip
        self.stages = arrays[:1] * 3 if column is None else [column] + arrays[:2]


class Part:
    def __init__(self, rows, width, spots):
        self.rows, self.width, self.spots = rows, width, spots

    def scratch(self):
        return pltpu.VMEM((2, 2, 2, 2, 2, self.rows // 32, self.width), jnp.bfloat16)

    def start(self, refs_of, place, dst, sem):
        z1, z0, y, x, core = [place[axis] for axis in range(5)]
        high = self.rows // 32
        for source, first_row, first_col, at_col, width in self.spots:
            refs = refs_of(source)
            cols = slice(first_col, first_col + width)
            into = slice(at_col, at_col + width)
            if source.kind == "whole":
                pltpu.make_async_copy(
                    refs[0].at[:, :, :, :, :, :, cols], dst.at[:, :, :, :, :, :, into], sem
                ).start()
            elif source.kind == "cores":
                for which in range(2):
                    owner = core if which == 0 else 1 - core
                    pltpu.make_async_copy(
                        refs[which].at[:, :, :, :, first_row : first_row + high, cols],
                        dst.at[:, :, :, :, owner, :, into],
                        sem,
                    ).start()
            else:
                for which in range(4):
                    owner = core if which < 2 else 1 - core
                    for near, at_y, at_x in flipped(source.first_flip, which % 2, y, x):
                        for up, at_z1, at_z0 in four(z1, z0):
                            pltpu.make_async_copy(
                                refs[which].at[near, up[0], up[1], :, cols],
                                dst.at[at_z1, at_z0, at_y, at_x, owner, :, into],
                                sem,
                            ).start()


def four(z1, z0):
    return [
        ((low, high), z1 if high == 0 else 1 - z1, z0 if low == 0 else 1 - z0)
        for low in range(2)
        for high in range(2)
    ]


def flipped(first_flip, beyond, y, x):
    found = []
    for near in range(2):
        a, b = (near, beyond) if first_flip == "x" else (beyond, near)
        found.append((near, y if b == 0 else 1 - y, x if a == 0 else 1 - x))
    return found


def after(value, *others):
    return lax.optimization_barrier((value, *others))[0]


def gather_flips(shards, first_flips, hold=None):
    if not paired():
        full = [lax.all_gather(shard, "blk", axis=0, tiled=True) for shard in shards]
        return [
            Source("whole", [array.reshape(2, 2, 2, 2, 2, array.shape[0] // 32, array.shape[1])])
            for array in full
        ]
    core = lax.axis_index("dp")
    columns = []
    for shard in shards:
        rows = shard.shape[0]
        own = lax.dynamic_slice_in_dim(shard, core * (rows // 2), rows // 2, 0)
        columns.append(with_flip(with_flip(own, 8), 4))
    sources, bits = [], {"x": (1, 2), "y": (2, 1)}
    if hold is not None:
        columns = after(columns, hold)
    planes = [
        with_flip(column, bits[first][0]) for column, first in zip(columns, first_flips)
    ]
    for column, plane, first in zip(columns, planes, first_flips):
        beyond = flip(plane, bits[first][1])
        sources.append(
            Source("flips", [plane, beyond, swap_core(plane), swap_core(beyond)], first, column)
        )
    return sources


class RowPart:
    def __init__(self, sources, span):
        self.span = span
        self.rows, self.width = 16 * span, WIDTH
        self.spots = [(source,) for source in sources]

    def scratch(self):
        return pltpu.VMEM((2, 2, 2, 2, self.span, WIDTH), jnp.bfloat16)

    def start(self, refs_of, place, dst, sem):
        z1, z0, y, x = [place[axis] for axis in range(4)]
        half = WIDTH // 2
        for side, (source,) in enumerate(self.spots):
            refs = refs_of(source)
            for beyond in range(2):
                for near, at_y, at_x in flipped(source.first_flip, beyond, y, x):
                    for up, at_z1, at_z0 in four(z1, z0):
                        pltpu.make_async_copy(
                            refs[beyond].at[near, up[0], up[1]],
                            dst.at[at_z1, at_z0, at_y, at_x, :, side * half : (side + 1) * half],
                            sem,
                        ).start()


def gather_row(block, hold_near=None, hold=None):
    row = lax.axis_index("blk") // 8
    own = lax.dynamic_index_in_dim(block, row, 0, keepdims=False)
    other = lax.dynamic_index_in_dim(block, 1 - row, 0, keepdims=False)
    pair = jnp.stack([own, flip(other, 8)])
    if hold_near is not None:
        pair = after(pair, hold_near)
    column = with_flip(pair, 4)
    stages, sources = [pair, column], []
    if hold is not None:
        column = after(column, hold)
    half = WIDTH // 2
    planes = [with_flip(column[..., :half], 1), with_flip(column[..., half:], 2)]
    for plane, first, bit in zip(planes, "xy", (2, 1)):
        sources.append(Source("row", [plane, flip(plane, bit)], first))
    stages += [planes, [source.arrays[1] for source in sources]]
    return RowPart(sources, block.shape[1]), stages


def head_columns(shards, kinds):
    core = lax.axis_index("dp")
    blocks, widths = [], [128 * kind for kind in kinds]
    for shard, kind in zip(shards, kinds):
        own = lax.dynamic_slice_in_dim(shard, core * 32, 32, 0)
        own = own.reshape(32, kind, 8, 128).transpose(2, 0, 1, 3)
        blocks.append(own.reshape(8, 32, kind * 128))
    blocks = jnp.concatenate(blocks, axis=2)
    mine = exchange(jnp.concatenate([blocks, blocks], axis=0))
    mine = mine.reshape(2, 2, 2, 2, 32, sum(widths))
    source = Source("cores", [mine, swap_core(mine)])
    parts, place = [], 0
    for width in widths:
        parts.append(Part(1024, width, [(source, 0, place, 0, width)]))
        place += width
    return parts


def project_row(row_part, head_part, name):
    def body(ins, loaded, outs, _):
        weight = loaded[1].value()
        inputs = loaded[0].value()
        for first in range(0, row_part.rows, 256):
            rows = slice(first, first + 256)
            outs[0][rows, :] = dot(inputs[rows], weight).astype(jnp.bfloat16)

    (found,) = call_with_parts(
        body,
        [],
        [row_part, head_part],
        [shape(row_part.rows, head_part.width, of=jnp.bfloat16)],
        name,
    )
    return found


def row_grad(row_part, upstream, name):
    columns = upstream.shape[1]

    def body(ins, loaded, outs, _):
        core = ins[1][0]
        inputs = loaded[0].value()
        grads = []
        for first in range(0, columns, 128):
            grads.append(pair_dot(ins[0][:, first : first + 128], inputs, 0, 0).T)
        grad = jnp.concatenate(grads, axis=1).astype(jnp.bfloat16).reshape(16, 2, 32, columns)
        outs[0][core] = grad[:, 0]
        outs[0][1 - core] = grad[:, 1]

    (terms,) = call_with_parts(
        body,
        [upstream],
        [row_part],
        [shape(2, 16, 32, columns, of=jnp.bfloat16)],
        name,
        scalars=[lax.axis_index("dp").reshape(1).astype(jnp.int32)],
    )
    got = swap_core(terms[1])
    return (terms[0].astype(jnp.float32) + got.astype(jnp.float32)).astype(jnp.bfloat16)


def row_back(upstream, head_part, name):
    def body(ins, loaded, outs, _):
        weight = loaded[0].value()
        for first in range(0, ins[0].shape[0], 256):
            rows = slice(first, first + 256)
            outs[0][rows, :] = dot_back(ins[0][rows, :], weight).astype(jnp.bfloat16)

    (terms,) = call_with_parts(
        body, [upstream], [head_part], [shape(upstream.shape[0], WIDTH, of=jnp.bfloat16)], name
    )
    return terms


def reduce_row(terms, holds=None):
    blocks = terms.reshape(16, terms.shape[0] // 16, WIDTH)
    (both,), stages = scatter_chips([blocks], [(1, 2, 4, 8)], 0, 3, holds)
    row = lax.axis_index("blk") // 8
    kept = lax.dynamic_index_in_dim(both, row, 0, keepdims=False)
    other = lax.dynamic_index_in_dim(both, 1 - row, 0, keepdims=False)
    if holds and 3 in holds:
        other = after(other, holds[3])
    got = flip(other, 8)
    found = jnp.stack([jnp.where(row == 0, kept, got), jnp.where(row == 0, got, kept)])
    return found.astype(jnp.float32), stages


def finish_row_grad(got, kinds):
    total = jnp.sum(got.reshape(2, 8, 32, kinds, 128).astype(jnp.float32), axis=0)
    mine = total.astype(jnp.bfloat16).transpose(1, 2, 0, 3).reshape(32, kinds * WIDTH)
    other = swap_core(mine)
    core = lax.axis_index("dp")
    low = jnp.where(core == 0, mine, other)
    high = jnp.where(core == 0, other, mine)
    return jnp.concatenate([low, high], axis=0).astype(jnp.float32)


def columns_of(*pieces):
    spots, place = [], 0
    for source, first, width in pieces:
        spots.append((source, 0, first, place, width))
        place += width
    return Part(1024, place, spots)


PACK = 512


def pack_halves(shards):
    places = [
        (index, shard.shape[0] // 2, first)
        for index, shard in enumerate(shards)
        for first in range(0, shard.shape[1], PACK)
    ]

    def body(core, *refs):
        out_ref, place = refs[-1], 0
        for index, high, first in places:
            start = pl.multiple_of(core[0] * high, 16)
            out_ref[place : place + high, :] = refs[index][pl.ds(start, high), first : first + PACK]
            place += high

    return pl.pallas_call(
        body,
        out_shape=shape(sum(high for _, high, _ in places), PACK, of=jnp.bfloat16),
        in_specs=[smem_spec()] + [vmem_spec()] * len(shards),
        out_specs=vmem_spec(),
        compiler_params=pltpu.CompilerParams(vmem_limit_bytes=VMEM_BYTES),
        cost_estimate=cost(2),
        name="pack_halves",
    )(lax.axis_index("dp").reshape(1).astype(jnp.int32), *shards)


def gather_packed(packed):
    return lax.all_gather(packed, "blk", axis=0)


def packed_parts(shards, mine):
    if not paired():
        found = []
        for source, shard in zip(gather_flips(shards, "x" * len(shards)), shards):
            rows, columns = 32 * source.arrays[0].shape[5], shard.shape[1]
            step = min(columns, 1024)
            found.append(
                [
                    Part(rows, step, [(source, 0, first, 0, step)])
                    for first in range(0, columns, step)
                ]
            )
        return found
    spots, place = [], 0
    for shard in shards:
        high = shard.shape[0] // 2
        places = []
        for first in range(0, shard.shape[1], PACK):
            places.append(place)
            place += high
        spots.append((shard.shape[0] * 16, places))
    mine = mine.reshape(2, 2, 2, 2, place, PACK)
    source = Source("cores", [mine, swap_core(mine)])
    found = []
    for rows, places in spots:
        parts = []
        for first in range(0, len(places), 2):
            two = places[first : first + 2]
            parts.append(
                Part(
                    rows,
                    PACK * len(two),
                    [(source, row, 0, PACK * side, PACK) for side, row in enumerate(two)],
                )
            )
        found.append(parts)
    return found


def place_now():
    own, core = lax.axis_index("blk"), lax.axis_index("dp")
    bits = [(own // bit) % 2 for bit in FLIPS]
    return jnp.stack(bits + [core]).astype(jnp.int32)


class Loaded:
    def __init__(self, part, dst, sem):
        self.part, self.dst, self.sem, self.here = part, dst, sem, False

    def value(self):
        if not self.here:
            pltpu.make_async_copy(self.dst, self.dst, self.sem).wait()
            self.here = True
        return self.dst[...].reshape(self.part.rows, self.part.width)


def call_with_parts(body, inputs, parts, outputs, name, scratch=(), takes=5, scalars=()):
    sources = []
    for part in parts:
        sources += [spot[0] for spot in part.spots if spot[0] not in sources]
    arrays = [array for source in sources for array in source.arrays]

    def kernel(place, *refs):
        refs = list(refs)
        ins = [refs.pop(0) for _ in (*inputs, *scalars)]
        pieces = [[refs.pop(0) for _ in source.arrays] for source in sources]
        outs = [refs.pop(0) for _ in outputs]
        dsts = [refs.pop(0) for _ in parts]
        sems = refs.pop(0)
        loaded = []
        for index, part in enumerate(parts):
            part.start(
                lambda source: pieces[sources.index(source)], place, dsts[index], sems.at[index]
            )
            loaded.append(Loaded(part, dsts[index], sems.at[index]))
        body(ins, loaded, outs, refs)

    return pl.pallas_call(
        kernel,
        out_shape=tuple(outputs),
        in_specs=[smem_spec()]
        + [vmem_spec()] * len(inputs)
        + [smem_spec()] * len(scalars)
        + [pl.BlockSpec(memory_space=pl.ANY)] * len(arrays),
        out_specs=(vmem_spec(),) * len(outputs),
        scratch_shapes=[part.scratch() for part in parts]
        + [pltpu.SemaphoreType.DMA((len(parts),))]
        + list(scratch),
        compiler_params=pltpu.CompilerParams(vmem_limit_bytes=VMEM_BYTES),
        cost_estimate=cost(takes),
        name=name,
    )(place_now(), *inputs, *scalars, *arrays)


def vmem_spec():
    return pl.BlockSpec(memory_space=pltpu.VMEM)


def smem_spec():
    return pl.BlockSpec(memory_space=pltpu.SMEM)


def seg_of_pos(ends_ref, pos):
    seg = jnp.zeros(pos.shape, jnp.int32)
    for slot in range(ends_ref.shape[0]):
        seg = seg + (ends_ref[slot] <= pos).astype(jnp.int32)
    return seg


def pair_dot(left, right, left_dim, right_dim):
    return lax.dot_general(
        left, right, (((left_dim,), (right_dim,)), ((), ())), preferred_element_type=jnp.float32
    )


def seg_tables(q_ends, k_ends, span):
    seg_q = seg_of_pos(q_ends, lax.broadcasted_iota(jnp.int32, (1, span), 1))
    seg_k = seg_of_pos(k_ends, lax.broadcasted_iota(jnp.int32, (span, 1), 0))
    return seg_q, seg_k


def masked_scores(keys, queries, seg_q, seg_k, first, causal):
    scores = pair_dot(keys, queries, 1, 1)
    allowed = seg_k == seg_q
    if causal:
        key_pos = lax.broadcasted_iota(jnp.int32, scores.shape, 0)
        query_pos = first + lax.broadcasted_iota(jnp.int32, scores.shape, 1)
        allowed = allowed & (key_pos <= query_pos)
    return jnp.where(allowed, scores, NEG)


def attn_forward_body(causal, width, q_ends, k_ends, q_ref, kv_ref, low_ref, full_ref, lse_ref):
    span = q_ref.shape[0]
    step = math.gcd(span, 256)
    heads = width // HEAD_DIM
    seg_q, seg_k = seg_tables(q_ends, k_ends, span)
    key_at = kv_ref.shape[1] - 2 * width
    scaled = q_ref[:, :width] * jnp.bfloat16(HEAD_DIM ** (-0.5))
    keys = kv_ref[:, key_at : key_at + width]
    values = kv_ref[:, key_at + width : key_at + 2 * width]
    for first in range(0, span, step):
        reach = first + step if causal else span
        parts = []
        for head in range(heads):
            cols = slice(head * HEAD_DIM, (head + 1) * HEAD_DIM)
            scores = masked_scores(
                keys[:reach, cols],
                scaled[first : first + step, cols],
                seg_q[:, first : first + step],
                seg_k[:reach],
                first,
                causal,
            )
            top = jnp.max(scores, axis=0, keepdims=True)
            probs = jnp.exp(scores - top)
            total = jnp.sum(probs, axis=0, keepdims=True)
            mixed = pair_dot(values[:reach, cols], probs.astype(jnp.bfloat16), 0, 0)
            parts.append(mixed / total)
            lse_ref[head : head + 1, first : first + step] = top + jnp.log(total)
        joined = jnp.concatenate(parts, axis=0).T
        full_ref[first : first + step, :] = joined
        low_ref[first : first + step, :] = joined.astype(jnp.bfloat16)


def attn_forward(q_ends, k_ends, queries, keys_values, width, causal):
    span = queries.shape[0]
    return pl.pallas_call(
        functools.partial(attn_forward_body, causal, width),
        out_shape=(
            jax.ShapeDtypeStruct((span, width), jnp.bfloat16),
            jax.ShapeDtypeStruct((span, width), jnp.float32),
            jax.ShapeDtypeStruct((width // HEAD_DIM, span), jnp.float32),
        ),
        in_specs=[smem_spec(), smem_spec()] + [vmem_spec()] * 2,
        out_specs=(vmem_spec(),) * 3,
        compiler_params=pltpu.CompilerParams(vmem_limit_bytes=VMEM_BYTES),
        cost_estimate=cost(8),
        name="attn_forward",
    )(q_ends, k_ends, queries, keys_values)


def attn_backward_body(
    causal,
    width,
    q_ends,
    k_ends,
    q_ref,
    kv_ref,
    up_ref,
    full_ref,
    lse_ref,
    *outs,
):
    dq_ref, dkv_ref = outs[0], outs[-3]
    dk_sum, dv_sum = outs[-2:]
    span = q_ref.shape[0]
    step = math.gcd(span, 256)
    heads = width // HEAD_DIM
    seg_q, seg_k = seg_tables(q_ends, k_ends, span)
    key_at = kv_ref.shape[1] - 2 * width
    scaled = q_ref[:, :width] * jnp.bfloat16(HEAD_DIM ** (-0.5))
    keys = kv_ref[:, key_at : key_at + width]
    values = kv_ref[:, key_at + width : key_at + 2 * width]
    upstream = up_ref[...]
    dk_sum[...] = jnp.zeros_like(dk_sum)
    dv_sum[...] = jnp.zeros_like(dv_sum)
    for first in range(0, span, step):
        reach = first + step if causal else span
        rows = slice(first, first + step)
        product = (upstream[rows].astype(jnp.float32) * full_ref[rows, :]).T
        parts = []
        for head in range(heads):
            cols = slice(head * HEAD_DIM, (head + 1) * HEAD_DIM)
            delta = jnp.sum(product[cols], axis=0, keepdims=True)
            scores = masked_scores(
                keys[:reach, cols], scaled[rows, cols], seg_q[:, rows], seg_k[:reach], first, causal
            )
            probs = jnp.exp(scores - lse_ref[head : head + 1, rows])
            dv_sum[head, :reach] += pair_dot(
                probs.astype(jnp.bfloat16), upstream[rows, cols], 1, 0
            )
            grad_probs = pair_dot(values[:reach, cols], upstream[rows, cols], 1, 1)
            grad_scores = (probs * (grad_probs - delta)).astype(jnp.bfloat16)
            dk_sum[head, :reach] += pair_dot(grad_scores, scaled[rows, cols], 1, 0)
            parts.append(pair_dot(keys[:reach, cols], grad_scores, 0, 0))
        joined = jnp.concatenate(parts, axis=0).T * HEAD_DIM ** (-0.5)
        dq_ref[rows, :width] = joined.astype(jnp.bfloat16)
    sums = [dk_sum[head] for head in range(heads)] + [dv_sum[head] for head in range(heads)]
    kv_at = dkv_ref.shape[1] - 2 * width
    dkv_ref[:, kv_at:] = jnp.concatenate(sums, axis=1).astype(jnp.bfloat16)


def attn_backward(
    q_ends, k_ends, queries, keys_values, upstream, full, lse, causal, joined=False
):
    span, width = upstream.shape
    kinds = [3] if joined else [1, 2]
    heads = width // HEAD_DIM
    return pl.pallas_call(
        functools.partial(attn_backward_body, causal, width),
        out_shape=[jax.ShapeDtypeStruct((span, kind * width), jnp.bfloat16) for kind in kinds],
        in_specs=[smem_spec(), smem_spec()] + [vmem_spec()] * 5,
        out_specs=[vmem_spec()] * len(kinds),
        scratch_shapes=[pltpu.VMEM((heads, span, HEAD_DIM), jnp.float32)] * 2,
        compiler_params=pltpu.CompilerParams(vmem_limit_bytes=VMEM_BYTES),
        cost_estimate=cost(8),
        name="attn_backward",
    )(q_ends, k_ends, queries, keys_values, upstream, full, lse)


def exchange(blocks):
    return lax.all_to_all(blocks, "blk", 0, 0, tiled=True)


def as_rows(blocks):
    return blocks.reshape(blocks.shape[0] * blocks.shape[1], blocks.shape[2])


def as_blocks(rows):
    devices = lax.axis_size("blk")
    return rows.reshape(devices, rows.shape[0] // devices, rows.shape[1])


def write_blocks(out_ref, values, lanes, kind, width):
    span = values.shape[0] // lanes
    for group in range(WIDTH // width):
        for lane in range(lanes):
            out_ref[lane * (WIDTH // width) + group, :, kind * width : (kind + 1) * width] = values[
                lane * span : (lane + 1) * span, group * width : (group + 1) * width
            ]


def read_blocks(got_ref, lanes, kind, width):
    groups = got_ref.shape[0] // lanes
    cols = slice(kind * width, (kind + 1) * width)
    rows = [
        jnp.concatenate([got_ref[lane * groups + group, :, cols] for group in range(groups)], axis=1)
        for lane in range(lanes)
    ]
    return jnp.concatenate(rows, axis=0)


def dot(left, right):
    return pair_dot(left, right, 1, 0)


def dot_back(left, right):
    return pair_dot(left, right, 1, 1)


def shape(*sizes, of=jnp.float32):
    return jax.ShapeDtypeStruct(sizes, of)


def normalize(values):
    center = values - jnp.mean(values, -1, keepdims=True)
    scale = lax.rsqrt(jnp.mean(center * center, -1, keepdims=True) + 1e-05)
    return center * scale, scale


def norm_back(upstream, normed, scale, gains_row):
    grad = upstream * gains_row
    return scale * (
        grad
        - jnp.mean(grad, -1, keepdims=True)
        - normed * jnp.mean(grad * normed, -1, keepdims=True)
    )


def project_blocks(inputs, parts, lanes, width, name):
    def body(ins, loaded, outs, _):
        for kind, weight in enumerate(loaded):
            write_blocks(
                outs[0], dot(ins[0][...], weight.value()).astype(jnp.bfloat16), lanes, kind, width
            )

    devices, span = lax.axis_size("blk"), inputs.shape[0] // lanes
    (blocks,) = call_with_parts(
        body,
        [inputs],
        parts,
        [shape(devices, span, width * len(parts), of=jnp.bfloat16)],
        name,
    )
    return blocks


def after_self(got, tokens, gains, biases, out_part, query_part, lanes, width):
    def body(ins, loaded, outs, _):
        got_ref, tokens_ref, gains_ref, biases_ref = ins
        low_ref, normed_ref, scale_ref, hidden_ref, blocks_ref = outs
        attended = read_blocks(got_ref, lanes, 0, width)
        low_ref[...] = attended
        resid = tokens_ref[...].astype(jnp.float32) + dot(attended, loaded[0].value())
        normed, scale = normalize(resid)
        normed_ref[...] = normed
        scale_ref[...] = scale
        hidden = (normed * gains_ref[0:1] + biases_ref[0:1]).astype(jnp.bfloat16)
        hidden_ref[...] = hidden
        query = dot(hidden, loaded[1].value()).astype(jnp.bfloat16)
        write_blocks(blocks_ref, query, lanes, 0, width)

    rows = tokens.shape[0]
    return call_with_parts(
        body,
        [got, tokens, gains, biases],
        [out_part, query_part],
        [
            shape(rows, WIDTH, of=jnp.bfloat16),
            shape(rows, WIDTH),
            shape(rows, 1),
            shape(rows, WIDTH, of=jnp.bfloat16),
            shape(*got.shape, of=jnp.bfloat16),
        ],
        "after_self",
    )


def feed_forward(got, normed_in, cotangent, gains, biases, out_part, in_parts, down, outs, up, lanes, width):
    pieces = len(in_parts)
    step = in_parts[0].width

    def body(ins, loaded, refs, scratch):
        got_ref, normed_in_ref, cot_ref, gains_ref, biases_ref = ins
        (
            output_ref,
            low_ref,
            mixed_ref,
            adapted_ref,
            dunder_ref,
            dab_ref,
            dcb_ref,
            dresid_ref,
            blocks_ref,
            norms_ref,
        ) = refs
        slopes, acts = scratch
        w_out, w_down, w_in = loaded[0], loaded[1], loaded[2 : 2 + pieces]
        w_ff, w_up = loaded[2 + pieces :]
        attended = read_blocks(got_ref, lanes, 0, width)
        low_ref[...] = attended
        hidden = normed_in_ref[...] * gains_ref[0:1] + biases_ref[0:1]
        normed_one, scale_one = normalize(hidden + dot(attended, w_out.value()))
        mixed = normed_one * gains_ref[1:2] + biases_ref[1:2]
        mixed_low = mixed.astype(jnp.bfloat16)
        mixed_ref[...] = mixed_low
        summed = mixed
        under = dot(mixed_low, w_down.value())
        gate = 1.0 / (1.0 + jnp.exp(-under))
        adapted = (under * gate).astype(jnp.bfloat16)
        adapted_ref[...] = adapted
        under_slope = gate * (1.0 + under * (1.0 - gate))
        for piece in range(pieces):
            before = dot(mixed_low, w_in[piece].value())
            below = 0.5 + 0.5 * lax.erf(before * (0.5**0.5))
            slopes[piece] = below + before * jnp.exp(-0.5 * before * before) * (
                (2.0 * math.pi) ** -0.5
            )
            acts[piece] = (before * below).astype(jnp.bfloat16)
        for piece in range(pieces):
            summed = summed + dot(acts[piece], w_ff[piece].value())
        summed = summed + 4.0 * dot(adapted, w_up.value())
        normed_two, scale_two = normalize(summed)
        output_ref[...] = (normed_two * gains_ref[2:3] + biases_ref[2:3]).astype(jnp.bfloat16)
        upstream = cot_ref[...].astype(jnp.float32)
        norms_ref[0:1] = jnp.sum(upstream * normed_two, axis=0, keepdims=True)
        norms_ref[1:2] = jnp.sum(upstream, axis=0, keepdims=True)
        dz = norm_back(upstream, normed_two, scale_two, gains_ref[2:3])
        dzb = dz.astype(jnp.bfloat16)
        dab = (4.0 * dz).astype(jnp.bfloat16)
        dab_ref[...] = dab
        dunder = (under_slope * dot_back(dab, w_up.value())).astype(jnp.bfloat16)
        dunder_ref[...] = dunder
        dmixed = dz + dot_back(dunder, w_down.value())
        for piece in range(pieces):
            dpre = (slopes[piece] * dot_back(dzb, w_ff[piece].value())).astype(jnp.bfloat16)
            dmixed = dmixed + dot_back(dpre, w_in[piece].value())
        norms_ref[2:3] = jnp.sum(dmixed * normed_one, axis=0, keepdims=True)
        norms_ref[3:4] = jnp.sum(dmixed, axis=0, keepdims=True)
        dresid = norm_back(dmixed, normed_one, scale_one, gains_ref[1:2])
        dresid_ref[...] = dresid
        dcb = dresid.astype(jnp.bfloat16)
        dcb_ref[...] = dcb
        write_blocks(
            blocks_ref, dot_back(dcb, w_out.value()).astype(jnp.bfloat16), lanes, 0, width
        )

    rows = normed_in.shape[0]
    low = jnp.bfloat16

    def body_rows(ins, loaded, refs, scratch):
        whole_ff = loaded[2 + pieces]

        class Rows:
            def __init__(self, piece):
                self.piece = piece

            def value(self):
                return whole_ff.value()[self.piece * step : (self.piece + 1) * step]

        loaded = loaded[: 2 + pieces] + [[Rows(piece) for piece in range(pieces)], loaded[-1]]
        body(ins, loaded, refs, scratch)

    return call_with_parts(
        body_rows,
        [got, normed_in, cotangent, gains, biases],
        [out_part, down] + in_parts + [outs, up],
        [
            shape(rows, WIDTH, of=low),
            shape(rows, WIDTH, of=low),
            shape(rows, WIDTH, of=low),
            shape(rows, down.width, of=low),
            shape(rows, down.width, of=low),
            shape(rows, WIDTH, of=low),
            shape(rows, WIDTH, of=low),
            shape(rows, WIDTH),
            shape(*got.shape, of=low),
            shape(4, WIDTH),
        ],
        "feed_forward",
        [
            pltpu.VMEM((pieces, rows, step), jnp.float32),
            pltpu.VMEM((pieces, rows, step), jnp.bfloat16),
        ],
        20,
    )


def before_self(got, dresid, normed, scale, gains, query_part, out_part, lanes, width):
    def body(ins, loaded, outs, _):
        got_ref, dresid_ref, normed_ref, scale_ref, gains_ref = ins
        dcq_ref, dr_ref, dsb_ref, blocks_ref, norms_ref = outs
        dcq = read_blocks(got_ref, lanes, 0, width)
        dcq_ref[...] = dcq
        dhidden = dresid_ref[...] + dot_back(dcq, loaded[0].value())
        normed = normed_ref[...]
        norms_ref[0:1] = jnp.sum(dhidden * normed, axis=0, keepdims=True)
        norms_ref[1:2] = jnp.sum(dhidden, axis=0, keepdims=True)
        dr = norm_back(dhidden, normed, scale_ref[...], gains_ref[0:1])
        dr_ref[...] = dr
        dsb = dr.astype(jnp.bfloat16)
        dsb_ref[...] = dsb
        grad = dot_back(dsb, loaded[1].value()).astype(jnp.bfloat16)
        write_blocks(blocks_ref, grad, lanes, 0, width)

    rows = dresid.shape[0]
    return call_with_parts(
        body,
        [got, dresid, normed, scale, gains],
        [query_part, out_part],
        [
            shape(rows, WIDTH, of=jnp.bfloat16),
            shape(rows, WIDTH),
            shape(rows, WIDTH, of=jnp.bfloat16),
            shape(*got.shape, of=jnp.bfloat16),
            shape(2, WIDTH),
        ],
        "before_self",
    )


def input_grad(got, start, parts, lanes, span, width, name):
    def body(ins, loaded, outs, _):
        total = None
        for kind, weight in enumerate(loaded):
            values = read_blocks(ins[0], lanes, kind, width)
            term = dot_back(values, weight.value())
            total = term if total is None else total + term
        outs[0][...] = total if len(ins) == 1 else total + ins[1][...]

    rows = span * lanes
    return call_with_parts(
        body,
        [got] if start is None else [got, start],
        parts,
        [shape(rows, WIDTH)],
        name,
    )


def shards(
    tokens,
    encoder,
    cotangent,
    self_in,
    self_out,
    cross_q,
    cross_kv,
    cross_out,
    ffn_in,
    ffn_out,
    adapt_down,
    adapt_up,
    norm_gain,
    norm_bias,
    tgt_lengths,
    src_lengths,
):
    lanes, span, _ = tokens.shape
    rows = lanes * span
    width = WIDTH * lanes // lax.axis_size("blk")
    own_row = lax.axis_index("blk") // (lax.axis_size("blk") // lanes)
    tgt_ends = jnp.cumsum(lax.dynamic_index_in_dim(tgt_lengths, own_row, 0, keepdims=False))
    src_ends = jnp.cumsum(lax.dynamic_index_in_dim(src_lengths, own_row, 0, keepdims=False))
    flat_tokens = tokens.reshape(rows, WIDTH)
    flat_encoder = encoder.reshape(rows, WIDTH)
    frozen = [ffn_in, adapt_down, ffn_out, adapt_up, cross_out]

    if paired():
        packed = gather_packed(pack_halves(frozen))
        self_packed = pack_halves([self_in])
        token_row, stages = gather_row(tokens)
        self_heads, pair_heads = head_columns([self_in, cross_kv], [3, 2])
        out_shard, query_shard = after((self_out, cross_q), stages[1])
        encoder_block = after(encoder, stages[1])
        self_qkv = project_row(token_row, self_heads, "self_in")
        out_source, query_source = gather_flips([out_shard, query_shard], "xy", self_qkv)
        encoder_row, encoder_stages = gather_row(
            encoder_block, self_qkv, (out_source.arrays[1], query_source.arrays[1])
        )
        self_qkv = after(self_qkv, out_source.stages[0], query_source.stages[0])
        pair_own = project_row(encoder_row, pair_heads, "cross_kv")
    else:
        (self_source, pair_source, out_source, query_source) = gather_flips(
            [self_in, cross_kv, self_out, cross_q], "xyxy"
        )
        self_parts = [columns_of((self_source, WIDTH * kind, WIDTH)) for kind in range(3)]
        pair_parts = [columns_of((pair_source, WIDTH * kind, WIDTH)) for kind in range(2)]
        self_qkv = as_rows(
            exchange(project_blocks(flat_tokens, self_parts, lanes, width, "self_in"))
        )
        pair_own = as_rows(
            exchange(project_blocks(flat_encoder, pair_parts, lanes, width, "cross_kv"))
        )
    self_out_part = columns_of((out_source, 0, WIDTH))
    query_part = columns_of((query_source, 0, WIDTH))

    self_mid, self_full, self_lse = attn_forward(
        tgt_ends, tgt_ends, self_qkv, self_qkv, width, True
    )
    self_sent = after(self_mid, out_source.stages[1], query_source.stages[1])
    if paired():
        self_sent = after(self_sent, encoder_stages[0])
    self_back = exchange(as_blocks(self_sent))
    if paired():
        self_back = after(self_back, encoder_stages[1])
    self_low, normed, scale, hidden_low, query_blocks = after_self(
        self_back,
        flat_tokens,
        norm_gain,
        norm_bias,
        self_out_part,
        query_part,
        lanes,
        width,
    )
    cross_own = as_rows(exchange(query_blocks))
    cross_mid, cross_full, cross_lse = attn_forward(
        tgt_ends, src_ends, cross_own, pair_own, width, False
    )
    cross_back = exchange(as_blocks(cross_mid))
    ready = after(packed, cross_mid) if paired() else None
    ff_parts, down_parts, ffo_parts, up_parts, (cross_out_part,) = packed_parts(frozen, ready)
    if paired():
        self_packed = gather_packed(after(self_packed, cross_back))
    (
        output,
        cross_low,
        mixed_low,
        adapter_low,
        grad_under,
        adapt_low,
        cross_branch_low,
        grad_resid_two,
        cross_grad_blocks,
        norms_high,
    ) = feed_forward(
        cross_back,
        normed,
        cotangent.reshape(rows, WIDTH),
        norm_gain,
        norm_bias,
        cross_out_part,
        ff_parts,
        down_parts[0],
        ffo_parts[0],
        up_parts[0],
        lanes,
        width,
    )
    high_groups = [
        [(cross_low, cross_branch_low)],
        [(mixed_low, grad_under), (adapter_low, adapt_low)],
    ]
    high_terms = [grad_terms(pairs) for pairs in high_groups]
    high_orders = [(2, 1, 4, 8), (1, 2, 4, 8)]
    high_terms, high_stages = scatter_chips(high_terms, high_orders, 0, 2)
    cross_dq, cross_dkv = attn_backward(
        tgt_ends,
        src_ends,
        cross_own,
        pair_own,
        as_rows(after(exchange(cross_grad_blocks), high_stages[0])),
        cross_full,
        cross_lse,
        False,
    )
    cross_dq_got = after(exchange(as_blocks(cross_dq)), high_stages[1])
    if paired():
        dkv_late = after(cross_dkv, high_stages[1])
        pair_terms = row_back(dkv_late, pair_heads, "encoder_grad")
        kv_sent = row_grad(encoder_row, dkv_late, "cross_kv_grad")
        cross_dq_got = after(cross_dq_got, pair_terms, kv_sent)
    cq_low, grad_resid_one, self_branch_low, self_grad_blocks, norms_low = before_self(
        cross_dq_got,
        grad_resid_two,
        normed,
        scale,
        norm_gain,
        query_part,
        self_out_part,
        lanes,
        width,
    )
    norms = jnp.concatenate([norms_low, norms_high], axis=0)
    mid_pairs = [(hidden_low, cq_low), (self_low, self_branch_low)]
    mid_orders = [(2, 1, 4, 8), (1, 2, 4, 8)]
    mid_terms = [grad_terms([pair]) for pair in mid_pairs]
    mid_terms, _ = scatter_chips(mid_terms, mid_orders, 0, 1)
    if paired():
        high_terms = [jnp.concatenate(after(high_terms, self_grad_blocks), axis=2)]
        high_terms, _ = scatter_chips(high_terms, [(2, 1, 4, 8)], 2, 3)
    self_upstream = after(exchange(self_grad_blocks), high_stages[2])
    (self_grads,) = attn_backward(
        tgt_ends,
        tgt_ends,
        self_qkv,
        self_qkv,
        as_rows(self_upstream),
        self_full,
        self_lse,
        True,
        joined=True,
    )
    if paired():
        (self_parts,) = packed_parts([self_in], after(self_packed, self_grads))
        self_got = exchange(as_blocks(self_grads))
        high_terms, _ = scatter_chips(after(high_terms, self_grads), [(2, 1, 4, 8)], 3, 4)
        self_sent = row_grad(token_row, after(self_grads, high_terms[0]), "self_in_grad")
        mid_terms, _ = scatter_chips(after(mid_terms, self_grads), mid_orders, 1, 2)
        mid_terms = [jnp.concatenate(mid_terms, axis=2)]
        chunks = [
            array[:, :, first : first + width]
            for array in (self_sent, kv_sent)
            for first in range(0, array.shape[2], width)
        ]
        partials = norms.astype(jnp.bfloat16).reshape(1, 48, width)
        chunks.append(jnp.broadcast_to(partials, (16, 48, width)))
        sent = after(jnp.concatenate(chunks, axis=1), self_got)
        got = exchange(sent)
        (tokens_grad,) = input_grad(
            self_got, grad_resid_one, self_parts, lanes, span, width, "tokens_grad"
        )
        encoder_grad, _ = reduce_row(pair_terms, {2: self_grads, 3: tokens_grad})
        encoder_grad = encoder_grad.reshape(rows, WIDTH)
        mid_terms, _ = scatter_chips(
            mid_terms, mid_orders[:1], 2, 4, {2: self_got, 3: tokens_grad}
        )
        got = after(got, tokens_grad)
        chunks = [got[:, first : first + 32] for first in range(0, 160, 32)]
        grad_self_in = finish_row_grad(jnp.concatenate(chunks[:3], axis=2), 3)
        grad_cross_kv = finish_row_grad(jnp.concatenate(chunks[3:], axis=2), 2)
        norms = jnp.sum(got[:, 160:].astype(jnp.float32), axis=0).reshape(6, WIDTH)
        norms = norms + swap_core(norms)
    else:
        pair_got = exchange(as_blocks(cross_dkv))
        self_got = exchange(as_blocks(self_grads))
        (encoder_grad,) = input_grad(
            pair_got, None, pair_parts, lanes, span, width, "encoder_grad"
        )
        (tokens_grad,) = input_grad(
            self_got, grad_resid_one, self_parts, lanes, span, width, "tokens_grad"
        )
        pair_low = pair_got.reshape(lanes, -1, span, 2, width).transpose(0, 2, 3, 1, 4)
        self_low_grads = self_got.reshape(lanes, -1, span, 3, width).transpose(0, 2, 3, 1, 4)
        grad_cross_kv = weight_grad(flat_encoder, pair_low.reshape(rows, 2 * WIDTH))
        grad_self_in = weight_grad(flat_tokens, self_low_grads.reshape(rows, 3 * WIDTH))
        norms = lax.psum(norms, ("dp", "blk"))
    ((grad_cross_q, grad_self_out),) = finish_terms([mid_pairs], mid_terms)
    (grad_cross_out,), (grad_adapt_down, grad_adapt_up) = finish_terms(high_groups, high_terms)
    return (
        output.reshape(lanes, span, WIDTH),
        tokens_grad.reshape(lanes, span, WIDTH),
        encoder_grad.reshape(lanes, span, WIDTH),
        grad_self_in,
        grad_self_out,
        grad_cross_q,
        grad_cross_kv,
        grad_cross_out,
        grad_adapt_down,
        grad_adapt_up,
        jnp.stack([norms[0], norms[4], norms[2]]),
        jnp.stack([norms[1], norms[5], norms[3]]),
    )


def solution(mesh):
    placed = (
        P("dp", "blk", None),
        P("dp", "blk", None),
        P("dp", "blk", None),
        P("blk", None),
        P("blk", None),
        P("blk", None),
        P("blk", None),
        P("blk", None),
        P("blk", None),
        P("blk", None),
        P("blk", None),
        P("blk", None),
        P(),
        P(),
        P("dp", None),
        P("dp", None),
    )
    return jax.shard_map(
        shards,
        mesh=mesh,
        in_specs=placed,
        out_specs=(
            P("dp", "blk", None),
            P("dp", "blk", None),
            P("dp", "blk", None),
            P("blk", None),
            P("blk", None),
            P("blk", None),
            P("blk", None),
            P("blk", None),
            P("blk", None),
            P("blk", None),
            P(),
            P(),
        ),
        check_vma=False,
    )
```

```python
import functools
import math

import jax
import jax.numpy as jnp
from jax import lax
from jax.experimental import pallas as pl
from jax.experimental.pallas import tpu as pltpu
from jax.sharding import PartitionSpec as P

HEADS = 16
HEAD_DIM = 64
WIDTH = HEADS * HEAD_DIM


NEG = -1e30
VMEM_BYTES = 56 * 1024 * 1024


def cost(microseconds):
    return pl.CostEstimate(
        flops=int(microseconds * 0.4e9),
        bytes_accessed=int(microseconds * 1.2e6),
        transcendentals=0,
    )


def paired():
    return lax.axis_size("blk") == 16 and lax.axis_size("dp") == 2


def swap_core(block):
    cores = lax.axis_size("dp")
    return lax.ppermute(block, "dp", [(i ^ 1, i) for i in range(cores)])


def flip(block, bit):
    chips = lax.axis_size("blk")
    return lax.ppermute(block, "blk", [(i ^ bit, i) for i in range(chips)])


FLIPS = (8, 4, 2, 1)


def with_flip(block, bit):
    return jnp.stack([block, flip(block, bit)])


def own_half(values, which):
    half = values.shape[1] // 2
    return lax.dynamic_slice_in_dim(values, which * half, half, 1)


def scatter_chips(terms, orders, first, last, holds=None):
    if not paired():
        return terms, [terms] * 5
    own = lax.axis_index("blk")

    def fold(blocks, left, bit):
        axis, place = left.index(bit), (own // bit) % 2
        kept = lax.dynamic_index_in_dim(blocks, place, axis, keepdims=False)
        sent = lax.dynamic_index_in_dim(blocks, 1 - place, axis, keepdims=False)
        got = flip(sent, bit)
        return (kept.astype(jnp.float32) + got.astype(jnp.float32)).astype(jnp.bfloat16)

    if first == 0:
        terms = [blocks.reshape(2, 2, 2, 2, *blocks.shape[1:]) for blocks in terms]
    stages = [terms[0]]
    for stage in range(first, last):
        if holds and stage in holds:
            terms = after(terms, holds[stage])
        terms = [
            fold(blocks, [bit for bit in FLIPS if bit not in order[:stage]], order[stage])
            for blocks, order in zip(terms, orders)
        ]
        stages.append(terms[0])
    return terms, stages


CHUNK = 256


def grad_terms(pairs):
    if not paired():
        return pairs[0][1]
    core = lax.axis_index("dp")
    packed = []
    for inputs, upstream in pairs:
        both = jnp.concatenate([inputs, swap_core(inputs)], axis=0)
        half = jnp.concatenate(
            [own_half(upstream, core), swap_core(own_half(upstream, 1 - core))], axis=0
        )
        term = lax.dot_general(
            both, half, (((0,), (0,)), ((), ())), preferred_element_type=jnp.float32
        ).astype(jnp.bfloat16)
        rows = term.shape[0] // 16
        chunks = term.shape[1] // CHUNK
        packed += [
            term[:, c * CHUNK : (c + 1) * CHUNK].reshape(16, rows, CHUNK) for c in range(chunks)
        ]
    return jnp.concatenate(packed, axis=1)


def finish_terms(groups, terms):
    if not paired():
        return [[weight_grad(inputs, upstream) for inputs, upstream in pairs] for pairs in groups]
    core = lax.axis_index("dp")
    mine = jnp.concatenate(terms, axis=0)
    other = swap_core(mine)
    low = jnp.where(core == 0, mine, other).astype(jnp.float32)
    high = jnp.where(core == 0, other, mine).astype(jnp.float32)
    found, place = [], 0
    for pairs in groups:
        found.append([])
        for inputs, upstream in pairs:
            rows = inputs.shape[1] // 16
            chunks = upstream.shape[1] // 2 // CHUNK
            spots = [slice(place + c * rows, place + (c + 1) * rows) for c in range(chunks)]
            found[-1].append(
                jnp.concatenate(
                    [low[spot] for spot in spots] + [high[spot] for spot in spots], axis=1
                )
            )
            place += rows * chunks
    return found


def weight_grad(inputs, upstream):
    scattered = lax.psum_scatter(
        lax.dot_general(
            inputs, upstream, (((0,), (0,)), ((), ())), preferred_element_type=jnp.float32
        ).astype(jnp.bfloat16),
        "blk",
        scatter_dimension=0,
        tiled=True,
    )
    return lax.psum(scattered, "dp").astype(jnp.float32)


class Source:
    def __init__(self, kind, arrays, first_flip="x", column=None):
        self.kind, self.arrays, self.first_flip = kind, arrays, first_flip
        self.stages = arrays[:1] * 3 if column is None else [column] + arrays[:2]


class Part:
    def __init__(self, rows, width, spots):
        self.rows, self.width, self.spots = rows, width, spots

    def scratch(self):
        return pltpu.VMEM((2, 2, 2, 2, 2, self.rows // 32, self.width), jnp.bfloat16)

    def start(self, refs_of, place, dst, sem):
        z1, z0, y, x, core = [place[axis] for axis in range(5)]
        high = self.rows // 32
        for source, first_row, first_col, at_col, width in self.spots:
            refs = refs_of(source)
            cols = slice(first_col, first_col + width)
            into = slice(at_col, at_col + width)
            if source.kind == "whole":
                pltpu.make_async_copy(
                    refs[0].at[:, :, :, :, :, :, cols], dst.at[:, :, :, :, :, :, into], sem
                ).start()
            elif source.kind == "cores":
                for which in range(2):
                    owner = core if which == 0 else 1 - core
                    pltpu.make_async_copy(
                        refs[which].at[:, :, :, :, first_row : first_row + high, cols],
                        dst.at[:, :, :, :, owner, :, into],
                        sem,
                    ).start()
            else:
                for which in range(4):
                    owner = core if which < 2 else 1 - core
                    for near, at_y, at_x in flipped(source.first_flip, which % 2, y, x):
                        for up, at_z1, at_z0 in four(z1, z0):
                            pltpu.make_async_copy(
                                refs[which].at[near, up[0], up[1], :, cols],
                                dst.at[at_z1, at_z0, at_y, at_x, owner, :, into],
                                sem,
                            ).start()


def four(z1, z0):
    return [
        ((low, high), z1 if high == 0 else 1 - z1, z0 if low == 0 else 1 - z0)
        for low in range(2)
        for high in range(2)
    ]


def flipped(first_flip, beyond, y, x):
    found = []
    for near in range(2):
        a, b = (near, beyond) if first_flip == "x" else (beyond, near)
        found.append((near, y if b == 0 else 1 - y, x if a == 0 else 1 - x))
    return found


def after(value, *others):
    return lax.optimization_barrier((value, *others))[0]


def gather_flips(shards, first_flips, hold=None):
    if not paired():
        full = [lax.all_gather(shard, "blk", axis=0, tiled=True) for shard in shards]
        return [
            Source("whole", [array.reshape(2, 2, 2, 2, 2, array.shape[0] // 32, array.shape[1])])
            for array in full
        ]
    core = lax.axis_index("dp")
    columns = []
    for shard in shards:
        rows = shard.shape[0]
        own = lax.dynamic_slice_in_dim(shard, core * (rows // 2), rows // 2, 0)
        columns.append(with_flip(with_flip(own, 8), 4))
    sources, bits = [], {"x": (1, 2), "y": (2, 1)}
    if hold is not None:
        columns = after(columns, hold)
    planes = [
        with_flip(column, bits[first][0]) for column, first in zip(columns, first_flips)
    ]
    for column, plane, first in zip(columns, planes, first_flips):
        beyond = flip(plane, bits[first][1])
        sources.append(
            Source("flips", [plane, beyond, swap_core(plane), swap_core(beyond)], first, column)
        )
    return sources


class RowPart:
    def __init__(self, sources, span):
        self.span = span
        self.rows, self.width = 16 * span, WIDTH
        self.spots = [(source,) for source in sources]

    def scratch(self):
        return pltpu.VMEM((2, 2, 2, 2, self.span, WIDTH), jnp.bfloat16)

    def start(self, refs_of, place, dst, sem):
        z1, z0, y, x = [place[axis] for axis in range(4)]
        half = WIDTH // 2
        for side, (source,) in enumerate(self.spots):
            refs = refs_of(source)
            for beyond in range(2):
                for near, at_y, at_x in flipped(source.first_flip, beyond, y, x):
                    for up, at_z1, at_z0 in four(z1, z0):
                        pltpu.make_async_copy(
                            refs[beyond].at[near, up[0], up[1]],
                            dst.at[at_z1, at_z0, at_y, at_x, :, side * half : (side + 1) * half],
                            sem,
                        ).start()


def gather_row(block, hold_near=None, hold=None):
    row = lax.axis_index("blk") // 8
    own = lax.dynamic_index_in_dim(block, row, 0, keepdims=False)
    other = lax.dynamic_index_in_dim(block, 1 - row, 0, keepdims=False)
    pair = jnp.stack([own, flip(other, 8)])
    if hold_near is not None:
        pair = after(pair, hold_near)
    column = with_flip(pair, 4)
    stages, sources = [pair, column], []
    if hold is not None:
        column = after(column, hold)
    half = WIDTH // 2
    planes = [with_flip(column[..., :half], 1), with_flip(column[..., half:], 2)]
    for plane, first, bit in zip(planes, "xy", (2, 1)):
        sources.append(Source("row", [plane, flip(plane, bit)], first))
    stages += [planes, [source.arrays[1] for source in sources]]
    return RowPart(sources, block.shape[1]), stages


def head_columns(shards, kinds):
    core = lax.axis_index("dp")
    blocks, widths = [], [128 * kind for kind in kinds]
    for shard, kind in zip(shards, kinds):
        own = lax.dynamic_slice_in_dim(shard, core * 32, 32, 0)
        own = own.reshape(32, kind, 8, 128).transpose(2, 0, 1, 3)
        blocks.append(own.reshape(8, 32, kind * 128))
    blocks = jnp.concatenate(blocks, axis=2)
    mine = exchange(jnp.concatenate([blocks, blocks], axis=0))
    mine = mine.reshape(2, 2, 2, 2, 32, sum(widths))
    source = Source("cores", [mine, swap_core(mine)])
    parts, place = [], 0
    for width in widths:
        parts.append(Part(1024, width, [(source, 0, place, 0, width)]))
        place += width
    return parts


def project_row(row_part, head_part, name):
    def body(ins, loaded, outs, _):
        weight = loaded[1].value()
        inputs = loaded[0].value()
        for first in range(0, row_part.rows, 256):
            rows = slice(first, first + 256)
            outs[0][rows, :] = dot(inputs[rows], weight).astype(jnp.bfloat16)

    (found,) = call_with_parts(
        body,
        [],
        [row_part, head_part],
        [shape(row_part.rows, head_part.width, of=jnp.bfloat16)],
        name,
    )
    return found


def row_grad(row_part, upstream, name):
    columns = upstream.shape[1]

    def body(ins, loaded, outs, _):
        core = ins[1][0]
        inputs = loaded[0].value()
        grads = []
        for first in range(0, columns, 128):
            grads.append(pair_dot(ins[0][:, first : first + 128], inputs, 0, 0).T)
        grad = jnp.concatenate(grads, axis=1).astype(jnp.bfloat16).reshape(16, 2, 32, columns)
        outs[0][core] = grad[:, 0]
        outs[0][1 - core] = grad[:, 1]

    (terms,) = call_with_parts(
        body,
        [upstream],
        [row_part],
        [shape(2, 16, 32, columns, of=jnp.bfloat16)],
        name,
        scalars=[lax.axis_index("dp").reshape(1).astype(jnp.int32)],
    )
    got = swap_core(terms[1])
    return (terms[0].astype(jnp.float32) + got.astype(jnp.float32)).astype(jnp.bfloat16)


def row_back(upstream, head_part, name):
    def body(ins, loaded, outs, _):
        weight = loaded[0].value()
        for first in range(0, ins[0].shape[0], 256):
            rows = slice(first, first + 256)
            outs[0][rows, :] = dot_back(ins[0][rows, :], weight).astype(jnp.bfloat16)

    (terms,) = call_with_parts(
        body, [upstream], [head_part], [shape(upstream.shape[0], WIDTH, of=jnp.bfloat16)], name
    )
    return terms


def reduce_row(terms, holds=None):
    blocks = terms.reshape(16, terms.shape[0] // 16, WIDTH)
    (both,), stages = scatter_chips([blocks], [(1, 2, 4, 8)], 0, 3, holds)
    row = lax.axis_index("blk") // 8
    kept = lax.dynamic_index_in_dim(both, row, 0, keepdims=False)
    other = lax.dynamic_index_in_dim(both, 1 - row, 0, keepdims=False)
    got = flip(other, 8)
    found = jnp.stack([jnp.where(row == 0, kept, got), jnp.where(row == 0, got, kept)])
    return found.astype(jnp.float32), stages


def finish_row_grad(got, kinds):
    total = jnp.sum(got.reshape(2, 8, 32, kinds, 128).astype(jnp.float32), axis=0)
    mine = total.astype(jnp.bfloat16).transpose(1, 2, 0, 3).reshape(32, kinds * WIDTH)
    other = swap_core(mine)
    core = lax.axis_index("dp")
    low = jnp.where(core == 0, mine, other)
    high = jnp.where(core == 0, other, mine)
    return jnp.concatenate([low, high], axis=0).astype(jnp.float32)


def columns_of(*pieces):
    spots, place = [], 0
    for source, first, width in pieces:
        spots.append((source, 0, first, place, width))
        place += width
    return Part(1024, place, spots)


PACK = 512


def pack_halves(shards):
    places = [
        (index, shard.shape[0] // 2, first)
        for index, shard in enumerate(shards)
        for first in range(0, shard.shape[1], PACK)
    ]

    def body(core, *refs):
        out_ref, place = refs[-1], 0
        for index, high, first in places:
            start = pl.multiple_of(core[0] * high, 16)
            out_ref[place : place + high, :] = refs[index][pl.ds(start, high), first : first + PACK]
            place += high

    return pl.pallas_call(
        body,
        out_shape=shape(sum(high for _, high, _ in places), PACK, of=jnp.bfloat16),
        in_specs=[smem_spec()] + [vmem_spec()] * len(shards),
        out_specs=vmem_spec(),
        compiler_params=pltpu.CompilerParams(vmem_limit_bytes=VMEM_BYTES),
        cost_estimate=cost(2),
        name="pack_halves",
    )(lax.axis_index("dp").reshape(1).astype(jnp.int32), *shards)


def gather_packed(packed):
    return lax.all_gather(packed, "blk", axis=0)


def packed_parts(shards, mine):
    if not paired():
        found = []
        for source, shard in zip(gather_flips(shards, "x" * len(shards)), shards):
            rows, columns = 32 * source.arrays[0].shape[5], shard.shape[1]
            step = min(columns, 1024)
            found.append(
                [
                    Part(rows, step, [(source, 0, first, 0, step)])
                    for first in range(0, columns, step)
                ]
            )
        return found
    spots, place = [], 0
    for shard in shards:
        high = shard.shape[0] // 2
        places = []
        for first in range(0, shard.shape[1], PACK):
            places.append(place)
            place += high
        spots.append((shard.shape[0] * 16, places))
    mine = mine.reshape(2, 2, 2, 2, place, PACK)
    source = Source("cores", [mine, swap_core(mine)])
    found = []
    for rows, places in spots:
        parts = []
        for first in range(0, len(places), 2):
            two = places[first : first + 2]
            parts.append(
                Part(
                    rows,
                    PACK * len(two),
                    [(source, row, 0, PACK * side, PACK) for side, row in enumerate(two)],
                )
            )
        found.append(parts)
    return found


def place_now():
    own, core = lax.axis_index("blk"), lax.axis_index("dp")
    bits = [(own // bit) % 2 for bit in FLIPS]
    return jnp.stack(bits + [core]).astype(jnp.int32)


class Loaded:
    def __init__(self, part, dst, sem):
        self.part, self.dst, self.sem, self.here = part, dst, sem, False

    def value(self):
        if not self.here:
            pltpu.make_async_copy(self.dst, self.dst, self.sem).wait()
            self.here = True
        return self.dst[...].reshape(self.part.rows, self.part.width)


def call_with_parts(body, inputs, parts, outputs, name, scratch=(), takes=5, scalars=()):
    sources = []
    for part in parts:
        sources += [spot[0] for spot in part.spots if spot[0] not in sources]
    arrays = [array for source in sources for array in source.arrays]

    def kernel(place, *refs):
        refs = list(refs)
        ins = [refs.pop(0) for _ in (*inputs, *scalars)]
        pieces = [[refs.pop(0) for _ in source.arrays] for source in sources]
        outs = [refs.pop(0) for _ in outputs]
        dsts = [refs.pop(0) for _ in parts]
        sems = refs.pop(0)
        loaded = []
        for index, part in enumerate(parts):
            part.start(
                lambda source: pieces[sources.index(source)], place, dsts[index], sems.at[index]
            )
            loaded.append(Loaded(part, dsts[index], sems.at[index]))
        body(ins, loaded, outs, refs)

    return pl.pallas_call(
        kernel,
        out_shape=tuple(outputs),
        in_specs=[smem_spec()]
        + [vmem_spec()] * len(inputs)
        + [smem_spec()] * len(scalars)
        + [pl.BlockSpec(memory_space=pl.ANY)] * len(arrays),
        out_specs=(vmem_spec(),) * len(outputs),
        scratch_shapes=[part.scratch() for part in parts]
        + [pltpu.SemaphoreType.DMA((len(parts),))]
        + list(scratch),
        compiler_params=pltpu.CompilerParams(vmem_limit_bytes=VMEM_BYTES),
        cost_estimate=cost(takes),
        name=name,
    )(place_now(), *inputs, *scalars, *arrays)


def vmem_spec():
    return pl.BlockSpec(memory_space=pltpu.VMEM)


def smem_spec():
    return pl.BlockSpec(memory_space=pltpu.SMEM)


def seg_of_pos(ends_ref, pos):
    seg = jnp.zeros(pos.shape, jnp.int32)
    for slot in range(ends_ref.shape[0]):
        seg = seg + (ends_ref[slot] <= pos).astype(jnp.int32)
    return seg


def pair_dot(left, right, left_dim, right_dim):
    return lax.dot_general(
        left, right, (((left_dim,), (right_dim,)), ((), ())), preferred_element_type=jnp.float32
    )


def seg_tables(q_ends, k_ends, span):
    seg_q = seg_of_pos(q_ends, lax.broadcasted_iota(jnp.int32, (1, span), 1))
    seg_k = seg_of_pos(k_ends, lax.broadcasted_iota(jnp.int32, (span, 1), 0))
    return seg_q, seg_k


def masked_scores(keys, queries, seg_q, seg_k, first, causal):
    scores = pair_dot(keys, queries, 1, 1)
    allowed = seg_k == seg_q
    if causal:
        key_pos = lax.broadcasted_iota(jnp.int32, scores.shape, 0)
        query_pos = first + lax.broadcasted_iota(jnp.int32, scores.shape, 1)
        allowed = allowed & (key_pos <= query_pos)
    return jnp.where(allowed, scores, NEG)


def attn_forward_body(causal, width, q_ends, k_ends, q_ref, kv_ref, low_ref, full_ref, lse_ref):
    span = q_ref.shape[0]
    step = math.gcd(span, 256)
    heads = width // HEAD_DIM
    seg_q, seg_k = seg_tables(q_ends, k_ends, span)
    key_at = kv_ref.shape[1] - 2 * width
    scaled = q_ref[:, :width] * jnp.bfloat16(HEAD_DIM ** (-0.5))
    keys = kv_ref[:, key_at : key_at + width]
    values = kv_ref[:, key_at + width : key_at + 2 * width]
    for first in range(0, span, step):
        reach = first + step if causal else span
        parts = []
        for head in range(heads):
            cols = slice(head * HEAD_DIM, (head + 1) * HEAD_DIM)
            scores = masked_scores(
                keys[:reach, cols],
                scaled[first : first + step, cols],
                seg_q[:, first : first + step],
                seg_k[:reach],
                first,
                causal,
            )
            top = jnp.max(scores, axis=0, keepdims=True)
            probs = jnp.exp(scores - top)
            total = jnp.sum(probs, axis=0, keepdims=True)
            mixed = pair_dot(values[:reach, cols], probs.astype(jnp.bfloat16), 0, 0)
            parts.append(mixed / total)
            lse_ref[head : head + 1, first : first + step] = top + jnp.log(total)
        joined = jnp.concatenate(parts, axis=0).T
        full_ref[first : first + step, :] = joined
        low_ref[first : first + step, :] = joined.astype(jnp.bfloat16)


def attn_forward(q_ends, k_ends, queries, keys_values, width, causal):
    span = queries.shape[0]
    return pl.pallas_call(
        functools.partial(attn_forward_body, causal, width),
        out_shape=(
            jax.ShapeDtypeStruct((span, width), jnp.bfloat16),
            jax.ShapeDtypeStruct((span, width), jnp.float32),
            jax.ShapeDtypeStruct((width // HEAD_DIM, span), jnp.float32),
        ),
        in_specs=[smem_spec(), smem_spec()] + [vmem_spec()] * 2,
        out_specs=(vmem_spec(),) * 3,
        compiler_params=pltpu.CompilerParams(vmem_limit_bytes=VMEM_BYTES),
        cost_estimate=cost(8),
        name="attn_forward",
    )(q_ends, k_ends, queries, keys_values)


def attn_backward_body(
    causal,
    width,
    q_ends,
    k_ends,
    q_ref,
    kv_ref,
    up_ref,
    full_ref,
    lse_ref,
    *outs,
):
    dq_ref, dkv_ref = outs[0], outs[-3]
    dk_sum, dv_sum = outs[-2:]
    span = q_ref.shape[0]
    step = math.gcd(span, 256)
    heads = width // HEAD_DIM
    seg_q, seg_k = seg_tables(q_ends, k_ends, span)
    key_at = kv_ref.shape[1] - 2 * width
    scaled = q_ref[:, :width] * jnp.bfloat16(HEAD_DIM ** (-0.5))
    keys = kv_ref[:, key_at : key_at + width]
    values = kv_ref[:, key_at + width : key_at + 2 * width]
    upstream = up_ref[...]
    dk_sum[...] = jnp.zeros_like(dk_sum)
    dv_sum[...] = jnp.zeros_like(dv_sum)
    for first in range(0, span, step):
        reach = first + step if causal else span
        rows = slice(first, first + step)
        product = (upstream[rows].astype(jnp.float32) * full_ref[rows, :]).T
        parts = []
        for head in range(heads):
            cols = slice(head * HEAD_DIM, (head + 1) * HEAD_DIM)
            delta = jnp.sum(product[cols], axis=0, keepdims=True)
            scores = masked_scores(
                keys[:reach, cols], scaled[rows, cols], seg_q[:, rows], seg_k[:reach], first, causal
            )
            probs = jnp.exp(scores - lse_ref[head : head + 1, rows])
            dv_sum[head, :reach] += pair_dot(
                probs.astype(jnp.bfloat16), upstream[rows, cols], 1, 0
            )
            grad_probs = pair_dot(values[:reach, cols], upstream[rows, cols], 1, 1)
            grad_scores = (probs * (grad_probs - delta)).astype(jnp.bfloat16)
            dk_sum[head, :reach] += pair_dot(grad_scores, scaled[rows, cols], 1, 0)
            parts.append(pair_dot(keys[:reach, cols], grad_scores, 0, 0))
        joined = jnp.concatenate(parts, axis=0).T * HEAD_DIM ** (-0.5)
        dq_ref[rows, :width] = joined.astype(jnp.bfloat16)
    sums = [dk_sum[head] for head in range(heads)] + [dv_sum[head] for head in range(heads)]
    kv_at = dkv_ref.shape[1] - 2 * width
    dkv_ref[:, kv_at:] = jnp.concatenate(sums, axis=1).astype(jnp.bfloat16)


def attn_backward(
    q_ends, k_ends, queries, keys_values, upstream, full, lse, causal, joined=False
):
    span, width = upstream.shape
    kinds = [3] if joined else [1, 2]
    heads = width // HEAD_DIM
    return pl.pallas_call(
        functools.partial(attn_backward_body, causal, width),
        out_shape=[jax.ShapeDtypeStruct((span, kind * width), jnp.bfloat16) for kind in kinds],
        in_specs=[smem_spec(), smem_spec()] + [vmem_spec()] * 5,
        out_specs=[vmem_spec()] * len(kinds),
        scratch_shapes=[pltpu.VMEM((heads, span, HEAD_DIM), jnp.float32)] * 2,
        compiler_params=pltpu.CompilerParams(vmem_limit_bytes=VMEM_BYTES),
        cost_estimate=cost(8),
        name="attn_backward",
    )(q_ends, k_ends, queries, keys_values, upstream, full, lse)


def exchange(blocks):
    return lax.all_to_all(blocks, "blk", 0, 0, tiled=True)


def as_rows(blocks):
    return blocks.reshape(blocks.shape[0] * blocks.shape[1], blocks.shape[2])


def as_blocks(rows):
    devices = lax.axis_size("blk")
    return rows.reshape(devices, rows.shape[0] // devices, rows.shape[1])


def write_blocks(out_ref, values, lanes, kind, width):
    span = values.shape[0] // lanes
    for group in range(WIDTH // width):
        for lane in range(lanes):
            out_ref[lane * (WIDTH // width) + group, :, kind * width : (kind + 1) * width] = values[
                lane * span : (lane + 1) * span, group * width : (group + 1) * width
            ]


def read_blocks(got_ref, lanes, kind, width):
    groups = got_ref.shape[0] // lanes
    cols = slice(kind * width, (kind + 1) * width)
    rows = [
        jnp.concatenate([got_ref[lane * groups + group, :, cols] for group in range(groups)], axis=1)
        for lane in range(lanes)
    ]
    return jnp.concatenate(rows, axis=0)


def dot(left, right):
    return pair_dot(left, right, 1, 0)


def dot_back(left, right):
    return pair_dot(left, right, 1, 1)


def shape(*sizes, of=jnp.float32):
    return jax.ShapeDtypeStruct(sizes, of)


def normalize(values):
    center = values - jnp.mean(values, -1, keepdims=True)
    scale = lax.rsqrt(jnp.mean(center * center, -1, keepdims=True) + 1e-05)
    return center * scale, scale


def norm_back(upstream, normed, scale, gains_row):
    grad = upstream * gains_row
    return scale * (
        grad
        - jnp.mean(grad, -1, keepdims=True)
        - normed * jnp.mean(grad * normed, -1, keepdims=True)
    )


def project_blocks(inputs, parts, lanes, width, name):
    def body(ins, loaded, outs, _):
        for kind, weight in enumerate(loaded):
            write_blocks(
                outs[0], dot(ins[0][...], weight.value()).astype(jnp.bfloat16), lanes, kind, width
            )

    devices, span = lax.axis_size("blk"), inputs.shape[0] // lanes
    (blocks,) = call_with_parts(
        body,
        [inputs],
        parts,
        [shape(devices, span, width * len(parts), of=jnp.bfloat16)],
        name,
    )
    return blocks


def after_self(got, tokens, gains, biases, out_part, query_part, lanes, width):
    def body(ins, loaded, outs, _):
        got_ref, tokens_ref, gains_ref, biases_ref = ins
        low_ref, normed_ref, scale_ref, hidden_ref, blocks_ref = outs
        attended = read_blocks(got_ref, lanes, 0, width)
        low_ref[...] = attended
        resid = tokens_ref[...].astype(jnp.float32) + dot(attended, loaded[0].value())
        normed, scale = normalize(resid)
        normed_ref[...] = normed
        scale_ref[...] = scale
        hidden = (normed * gains_ref[0:1] + biases_ref[0:1]).astype(jnp.bfloat16)
        hidden_ref[...] = hidden
        query = dot(hidden, loaded[1].value()).astype(jnp.bfloat16)
        write_blocks(blocks_ref, query, lanes, 0, width)

    rows = tokens.shape[0]
    return call_with_parts(
        body,
        [got, tokens, gains, biases],
        [out_part, query_part],
        [
            shape(rows, WIDTH, of=jnp.bfloat16),
            shape(rows, WIDTH),
            shape(rows, 1),
            shape(rows, WIDTH, of=jnp.bfloat16),
            shape(*got.shape, of=jnp.bfloat16),
        ],
        "after_self",
    )


def feed_forward(got, normed_in, cotangent, gains, biases, out_part, in_parts, down, outs, up, lanes, width):
    pieces = len(in_parts)
    step = in_parts[0].width

    def body(ins, loaded, refs, scratch):
        got_ref, normed_in_ref, cot_ref, gains_ref, biases_ref = ins
        (
            output_ref,
            low_ref,
            mixed_ref,
            adapted_ref,
            dunder_ref,
            dab_ref,
            dcb_ref,
            dresid_ref,
            blocks_ref,
            norms_ref,
        ) = refs
        slopes, acts = scratch
        w_out, w_down, w_in = loaded[0], loaded[1], loaded[2 : 2 + pieces]
        w_ff, w_up = loaded[2 + pieces :]
        attended = read_blocks(got_ref, lanes, 0, width)
        low_ref[...] = attended
        hidden = normed_in_ref[...] * gains_ref[0:1] + biases_ref[0:1]
        normed_one, scale_one = normalize(hidden + dot(attended, w_out.value()))
        mixed = normed_one * gains_ref[1:2] + biases_ref[1:2]
        mixed_low = mixed.astype(jnp.bfloat16)
        mixed_ref[...] = mixed_low
        summed = mixed
        under = dot(mixed_low, w_down.value())
        gate = 1.0 / (1.0 + jnp.exp(-under))
        adapted = (under * gate).astype(jnp.bfloat16)
        adapted_ref[...] = adapted
        under_slope = gate * (1.0 + under * (1.0 - gate))
        for piece in range(pieces):
            before = dot(mixed_low, w_in[piece].value())
            below = 0.5 + 0.5 * lax.erf(before * (0.5**0.5))
            slopes[piece] = below + before * jnp.exp(-0.5 * before * before) * (
                (2.0 * math.pi) ** -0.5
            )
            acts[piece] = (before * below).astype(jnp.bfloat16)
        for piece in range(pieces):
            summed = summed + dot(acts[piece], w_ff[piece].value())
        summed = summed + 4.0 * dot(adapted, w_up.value())
        normed_two, scale_two = normalize(summed)
        output_ref[...] = (normed_two * gains_ref[2:3] + biases_ref[2:3]).astype(jnp.bfloat16)
        upstream = cot_ref[...].astype(jnp.float32)
        norms_ref[0:1] = jnp.sum(upstream * normed_two, axis=0, keepdims=True)
        norms_ref[1:2] = jnp.sum(upstream, axis=0, keepdims=True)
        dz = norm_back(upstream, normed_two, scale_two, gains_ref[2:3])
        dzb = dz.astype(jnp.bfloat16)
        dab = (4.0 * dz).astype(jnp.bfloat16)
        dab_ref[...] = dab
        dunder = (under_slope * dot_back(dab, w_up.value())).astype(jnp.bfloat16)
        dunder_ref[...] = dunder
        dmixed = dz + dot_back(dunder, w_down.value())
        for piece in range(pieces):
            dpre = (slopes[piece] * dot_back(dzb, w_ff[piece].value())).astype(jnp.bfloat16)
            dmixed = dmixed + dot_back(dpre, w_in[piece].value())
        norms_ref[2:3] = jnp.sum(dmixed * normed_one, axis=0, keepdims=True)
        norms_ref[3:4] = jnp.sum(dmixed, axis=0, keepdims=True)
        dresid = norm_back(dmixed, normed_one, scale_one, gains_ref[1:2])
        dresid_ref[...] = dresid
        dcb = dresid.astype(jnp.bfloat16)
        dcb_ref[...] = dcb
        write_blocks(
            blocks_ref, dot_back(dcb, w_out.value()).astype(jnp.bfloat16), lanes, 0, width
        )

    rows = normed_in.shape[0]
    low = jnp.bfloat16

    def body_rows(ins, loaded, refs, scratch):
        whole_ff = loaded[2 + pieces]

        class Rows:
            def __init__(self, piece):
                self.piece = piece

            def value(self):
                return whole_ff.value()[self.piece * step : (self.piece + 1) * step]

        loaded = loaded[: 2 + pieces] + [[Rows(piece) for piece in range(pieces)], loaded[-1]]
        body(ins, loaded, refs, scratch)

    return call_with_parts(
        body_rows,
        [got, normed_in, cotangent, gains, biases],
        [out_part, down] + in_parts + [outs, up],
        [
            shape(rows, WIDTH, of=low),
            shape(rows, WIDTH, of=low),
            shape(rows, WIDTH, of=low),
            shape(rows, down.width, of=low),
            shape(rows, down.width, of=low),
            shape(rows, WIDTH, of=low),
            shape(rows, WIDTH, of=low),
            shape(rows, WIDTH),
            shape(*got.shape, of=low),
            shape(4, WIDTH),
        ],
        "feed_forward",
        [
            pltpu.VMEM((pieces, rows, step), jnp.float32),
            pltpu.VMEM((pieces, rows, step), jnp.bfloat16),
        ],
        20,
    )


def before_self(got, dresid, normed, scale, gains, query_part, out_part, lanes, width):
    def body(ins, loaded, outs, _):
        got_ref, dresid_ref, normed_ref, scale_ref, gains_ref = ins
        dcq_ref, dr_ref, dsb_ref, blocks_ref, norms_ref = outs
        dcq = read_blocks(got_ref, lanes, 0, width)
        dcq_ref[...] = dcq
        dhidden = dresid_ref[...] + dot_back(dcq, loaded[0].value())
        normed = normed_ref[...]
        norms_ref[0:1] = jnp.sum(dhidden * normed, axis=0, keepdims=True)
        norms_ref[1:2] = jnp.sum(dhidden, axis=0, keepdims=True)
        dr = norm_back(dhidden, normed, scale_ref[...], gains_ref[0:1])
        dr_ref[...] = dr
        dsb = dr.astype(jnp.bfloat16)
        dsb_ref[...] = dsb
        grad = dot_back(dsb, loaded[1].value()).astype(jnp.bfloat16)
        write_blocks(blocks_ref, grad, lanes, 0, width)

    rows = dresid.shape[0]
    return call_with_parts(
        body,
        [got, dresid, normed, scale, gains],
        [query_part, out_part],
        [
            shape(rows, WIDTH, of=jnp.bfloat16),
            shape(rows, WIDTH),
            shape(rows, WIDTH, of=jnp.bfloat16),
            shape(*got.shape, of=jnp.bfloat16),
            shape(2, WIDTH),
        ],
        "before_self",
    )


def input_grad(got, start, parts, lanes, span, width, name):
    def body(ins, loaded, outs, _):
        total = None
        for kind, weight in enumerate(loaded):
            values = read_blocks(ins[0], lanes, kind, width)
            term = dot_back(values, weight.value())
            total = term if total is None else total + term
        outs[0][...] = total if len(ins) == 1 else total + ins[1][...]

    rows = span * lanes
    return call_with_parts(
        body,
        [got] if start is None else [got, start],
        parts,
        [shape(rows, WIDTH)],
        name,
    )


def shards(
    tokens,
    encoder,
    cotangent,
    self_in,
    self_out,
    cross_q,
    cross_kv,
    cross_out,
    ffn_in,
    ffn_out,
    adapt_down,
    adapt_up,
    norm_gain,
    norm_bias,
    tgt_lengths,
    src_lengths,
):
    lanes, span, _ = tokens.shape
    rows = lanes * span
    width = WIDTH * lanes // lax.axis_size("blk")
    own_row = lax.axis_index("blk") // (lax.axis_size("blk") // lanes)
    tgt_ends = jnp.cumsum(lax.dynamic_index_in_dim(tgt_lengths, own_row, 0, keepdims=False))
    src_ends = jnp.cumsum(lax.dynamic_index_in_dim(src_lengths, own_row, 0, keepdims=False))
    flat_tokens = tokens.reshape(rows, WIDTH)
    flat_encoder = encoder.reshape(rows, WIDTH)
    frozen = [ffn_in, adapt_down, ffn_out, adapt_up, cross_out]

    if paired():
        packed = gather_packed(pack_halves(frozen))
        self_packed = pack_halves([self_in])
        token_row, stages = gather_row(tokens)
        self_heads, pair_heads = head_columns([self_in, cross_kv], [3, 2])
        out_shard, query_shard = after((self_out, cross_q), stages[1])
        encoder_block = after(encoder, stages[1])
        self_qkv = project_row(token_row, self_heads, "self_in")
        out_source, query_source = gather_flips([out_shard, query_shard], "xy", self_qkv)
        encoder_row, encoder_stages = gather_row(
            encoder_block, self_qkv, (out_source.arrays[1], query_source.arrays[1])
        )
        self_qkv = after(self_qkv, out_source.stages[0], query_source.stages[0])
        pair_own = project_row(encoder_row, pair_heads, "cross_kv")
    else:
        (self_source, pair_source, out_source, query_source) = gather_flips(
            [self_in, cross_kv, self_out, cross_q], "xyxy"
        )
        self_parts = [columns_of((self_source, WIDTH * kind, WIDTH)) for kind in range(3)]
        pair_parts = [columns_of((pair_source, WIDTH * kind, WIDTH)) for kind in range(2)]
        self_qkv = as_rows(
            exchange(project_blocks(flat_tokens, self_parts, lanes, width, "self_in"))
        )
        pair_own = as_rows(
            exchange(project_blocks(flat_encoder, pair_parts, lanes, width, "cross_kv"))
        )
    self_out_part = columns_of((out_source, 0, WIDTH))
    query_part = columns_of((query_source, 0, WIDTH))

    self_mid, self_full, self_lse = attn_forward(
        tgt_ends, tgt_ends, self_qkv, self_qkv, width, True
    )
    self_sent = after(self_mid, out_source.stages[1], query_source.stages[1])
    if paired():
        self_sent = after(self_sent, encoder_stages[0])
    self_back = exchange(as_blocks(self_sent))
    if paired():
        self_back = after(self_back, encoder_stages[1])
    self_low, normed, scale, hidden_low, query_blocks = after_self(
        self_back,
        flat_tokens,
        norm_gain,
        norm_bias,
        self_out_part,
        query_part,
        lanes,
        width,
    )
    cross_own = as_rows(exchange(query_blocks))
    cross_mid, cross_full, cross_lse = attn_forward(
        tgt_ends, src_ends, cross_own, pair_own, width, False
    )
    cross_back = exchange(as_blocks(cross_mid))
    ready = after(packed, cross_mid) if paired() else None
    ff_parts, down_parts, ffo_parts, up_parts, (cross_out_part,) = packed_parts(frozen, ready)
    if paired():
        self_packed = gather_packed(after(self_packed, cross_back))
    (
        output,
        cross_low,
        mixed_low,
        adapter_low,
        grad_under,
        adapt_low,
        cross_branch_low,
        grad_resid_two,
        cross_grad_blocks,
        norms_high,
    ) = feed_forward(
        cross_back,
        normed,
        cotangent.reshape(rows, WIDTH),
        norm_gain,
        norm_bias,
        cross_out_part,
        ff_parts,
        down_parts[0],
        ffo_parts[0],
        up_parts[0],
        lanes,
        width,
    )
    high_groups = [
        [(cross_low, cross_branch_low)],
        [(mixed_low, grad_under), (adapter_low, adapt_low)],
    ]
    high_terms = [grad_terms(pairs) for pairs in high_groups]
    high_orders = [(2, 1, 4, 8), (1, 2, 4, 8)]
    high_terms, high_stages = scatter_chips(high_terms, high_orders, 0, 2)
    cross_dq, cross_dkv = attn_backward(
        tgt_ends,
        src_ends,
        cross_own,
        pair_own,
        as_rows(after(exchange(cross_grad_blocks), high_stages[0])),
        cross_full,
        cross_lse,
        False,
    )
    cross_dq_got = after(exchange(as_blocks(cross_dq)), high_stages[1])
    if paired():
        dkv_late = after(cross_dkv, high_stages[1])
        pair_terms = row_back(dkv_late, pair_heads, "encoder_grad")
        kv_sent = row_grad(encoder_row, dkv_late, "cross_kv_grad")
        cross_dq_got = after(cross_dq_got, pair_terms, kv_sent)
    cq_low, grad_resid_one, self_branch_low, self_grad_blocks, norms_low = before_self(
        cross_dq_got,
        grad_resid_two,
        normed,
        scale,
        norm_gain,
        query_part,
        self_out_part,
        lanes,
        width,
    )
    norms = jnp.concatenate([norms_low, norms_high], axis=0)
    mid_pairs = [(hidden_low, cq_low), (self_low, self_branch_low)]
    mid_orders = [(2, 1, 4, 8), (1, 2, 4, 8)]
    mid_terms = [grad_terms([pair]) for pair in mid_pairs]
    mid_terms, _ = scatter_chips(mid_terms, mid_orders, 0, 1)
    if paired():
        high_terms = [jnp.concatenate(after(high_terms, self_grad_blocks), axis=2)]
        high_terms, _ = scatter_chips(high_terms, [(2, 1, 4, 8)], 2, 3)
    self_upstream = after(exchange(self_grad_blocks), high_stages[2])
    (self_grads,) = attn_backward(
        tgt_ends,
        tgt_ends,
        self_qkv,
        self_qkv,
        as_rows(self_upstream),
        self_full,
        self_lse,
        True,
        joined=True,
    )
    if paired():
        (self_parts,) = packed_parts([self_in], after(self_packed, self_grads))
        self_got = exchange(as_blocks(self_grads))
        high_terms, _ = scatter_chips(after(high_terms, self_grads), [(2, 1, 4, 8)], 3, 4)
        self_sent = row_grad(token_row, after(self_grads, high_terms[0]), "self_in_grad")
        mid_terms, _ = scatter_chips(after(mid_terms, self_grads), mid_orders, 1, 2)
        mid_terms = [jnp.concatenate(mid_terms, axis=2)]
        chunks = [
            array[:, :, first : first + width]
            for array in (self_sent, kv_sent)
            for first in range(0, array.shape[2], width)
        ]
        partials = norms.astype(jnp.bfloat16).reshape(1, 48, width)
        chunks.append(jnp.broadcast_to(partials, (16, 48, width)))
        sent = after(jnp.concatenate(chunks, axis=1), self_got)
        got = exchange(sent)
        (tokens_grad,) = input_grad(
            self_got, grad_resid_one, self_parts, lanes, span, width, "tokens_grad"
        )
        encoder_grad, _ = reduce_row(pair_terms, {2: tokens_grad})
        encoder_grad = encoder_grad.reshape(rows, WIDTH)
        mid_terms, _ = scatter_chips(
            mid_terms, mid_orders[:1], 2, 4, {2: tokens_grad}
        )
        chunks = [got[:, first : first + 32] for first in range(0, 160, 32)]
        grad_self_in = finish_row_grad(jnp.concatenate(chunks[:3], axis=2), 3)
        grad_cross_kv = finish_row_grad(jnp.concatenate(chunks[3:], axis=2), 2)
        norms = jnp.sum(got[:, 160:].astype(jnp.float32), axis=0).reshape(6, WIDTH)
        norms = norms + swap_core(norms)
    else:
        pair_got = exchange(as_blocks(cross_dkv))
        self_got = exchange(as_blocks(self_grads))
        (encoder_grad,) = input_grad(
            pair_got, None, pair_parts, lanes, span, width, "encoder_grad"
        )
        (tokens_grad,) = input_grad(
            self_got, grad_resid_one, self_parts, lanes, span, width, "tokens_grad"
        )
        pair_low = pair_got.reshape(lanes, -1, span, 2, width).transpose(0, 2, 3, 1, 4)
        self_low_grads = self_got.reshape(lanes, -1, span, 3, width).transpose(0, 2, 3, 1, 4)
        grad_cross_kv = weight_grad(flat_encoder, pair_low.reshape(rows, 2 * WIDTH))
        grad_self_in = weight_grad(flat_tokens, self_low_grads.reshape(rows, 3 * WIDTH))
        norms = lax.psum(norms, ("dp", "blk"))
    ((grad_cross_q, grad_self_out),) = finish_terms([mid_pairs], mid_terms)
    (grad_cross_out,), (grad_adapt_down, grad_adapt_up) = finish_terms(high_groups, high_terms)
    return (
        output.reshape(lanes, span, WIDTH),
        tokens_grad.reshape(lanes, span, WIDTH),
        encoder_grad.reshape(lanes, span, WIDTH),
        grad_self_in,
        grad_self_out,
        grad_cross_q,
        grad_cross_kv,
        grad_cross_out,
        grad_adapt_down,
        grad_adapt_up,
        jnp.stack([norms[0], norms[4], norms[2]]),
        jnp.stack([norms[1], norms[5], norms[3]]),
    )


def solution(mesh):
    placed = (
        P("dp", "blk", None),
        P("dp", "blk", None),
        P("dp", "blk", None),
        P("blk", None),
        P("blk", None),
        P("blk", None),
        P("blk", None),
        P("blk", None),
        P("blk", None),
        P("blk", None),
        P("blk", None),
        P("blk", None),
        P(),
        P(),
        P("dp", None),
        P("dp", None),
    )
    return jax.shard_map(
        shards,
        mesh=mesh,
        in_specs=placed,
        out_specs=(
            P("dp", "blk", None),
            P("dp", "blk", None),
            P("dp", "blk", None),
            P("blk", None),
            P("blk", None),
            P("blk", None),
            P("blk", None),
            P("blk", None),
            P("blk", None),
            P("blk", None),
            P(),
            P(),
        ),
        check_vma=False,
    )
```

```python
import functools
import math

import jax
import jax.numpy as jnp
from jax import lax
from jax.experimental import pallas as pl
from jax.experimental.pallas import tpu as pltpu
from jax.sharding import PartitionSpec as P

HEADS = 16
HEAD_DIM = 64
WIDTH = HEADS * HEAD_DIM


NEG = -1e30
VMEM_BYTES = 56 * 1024 * 1024


def cost(microseconds):
    return pl.CostEstimate(
        flops=int(microseconds * 0.4e9),
        bytes_accessed=int(microseconds * 1.2e6),
        transcendentals=0,
    )


def paired():
    return lax.axis_size("blk") == 16 and lax.axis_size("dp") == 2


def swap_core(block):
    cores = lax.axis_size("dp")
    return lax.ppermute(block, "dp", [(i ^ 1, i) for i in range(cores)])


def flip(block, bit):
    chips = lax.axis_size("blk")
    return lax.ppermute(block, "blk", [(i ^ bit, i) for i in range(chips)])


FLIPS = (8, 4, 2, 1)


def with_flip(block, bit):
    return jnp.stack([block, flip(block, bit)])


def own_half(values, which):
    half = values.shape[1] // 2
    return lax.dynamic_slice_in_dim(values, which * half, half, 1)


def scatter_chips(terms, orders, first, last, holds=None):
    if not paired():
        return terms, [terms] * 5
    own = lax.axis_index("blk")

    def fold(blocks, left, bit):
        axis, place = left.index(bit), (own // bit) % 2
        kept = lax.dynamic_index_in_dim(blocks, place, axis, keepdims=False)
        sent = lax.dynamic_index_in_dim(blocks, 1 - place, axis, keepdims=False)
        got = flip(sent, bit)
        return (kept.astype(jnp.float32) + got.astype(jnp.float32)).astype(jnp.bfloat16)

    if first == 0:
        terms = [blocks.reshape(2, 2, 2, 2, *blocks.shape[1:]) for blocks in terms]
    stages = [terms[0]]
    for stage in range(first, last):
        if holds and stage in holds:
            terms = after(terms, holds[stage])
        terms = [
            fold(blocks, [bit for bit in FLIPS if bit not in order[:stage]], order[stage])
            for blocks, order in zip(terms, orders)
        ]
        stages.append(terms[0])
    return terms, stages


CHUNK = 256


def grad_terms(pairs):
    if not paired():
        return pairs[0][1]
    core = lax.axis_index("dp")
    packed = []
    for inputs, upstream in pairs:
        both = jnp.concatenate([inputs, swap_core(inputs)], axis=0)
        half = jnp.concatenate(
            [own_half(upstream, core), swap_core(own_half(upstream, 1 - core))], axis=0
        )
        term = lax.dot_general(
            both, half, (((0,), (0,)), ((), ())), preferred_element_type=jnp.float32
        ).astype(jnp.bfloat16)
        rows = term.shape[0] // 16
        chunks = term.shape[1] // CHUNK
        packed += [
            term[:, c * CHUNK : (c + 1) * CHUNK].reshape(16, rows, CHUNK) for c in range(chunks)
        ]
    return jnp.concatenate(packed, axis=1)


def finish_terms(groups, terms):
    if not paired():
        return [[weight_grad(inputs, upstream) for inputs, upstream in pairs] for pairs in groups]
    core = lax.axis_index("dp")
    mine = jnp.concatenate(terms, axis=0)
    other = swap_core(mine)
    low = jnp.where(core == 0, mine, other).astype(jnp.float32)
    high = jnp.where(core == 0, other, mine).astype(jnp.float32)
    found, place = [], 0
    for pairs in groups:
        found.append([])
        for inputs, upstream in pairs:
            rows = inputs.shape[1] // 16
            chunks = upstream.shape[1] // 2 // CHUNK
            spots = [slice(place + c * rows, place + (c + 1) * rows) for c in range(chunks)]
            found[-1].append(
                jnp.concatenate(
                    [low[spot] for spot in spots] + [high[spot] for spot in spots], axis=1
                )
            )
            place += rows * chunks
    return found


def weight_grad(inputs, upstream):
    scattered = lax.psum_scatter(
        lax.dot_general(
            inputs, upstream, (((0,), (0,)), ((), ())), preferred_element_type=jnp.float32
        ).astype(jnp.bfloat16),
        "blk",
        scatter_dimension=0,
        tiled=True,
    )
    return lax.psum(scattered, "dp").astype(jnp.float32)


class Source:
    def __init__(self, kind, arrays, first_flip="x", column=None):
        self.kind, self.arrays, self.first_flip = kind, arrays, first_flip
        self.stages = arrays[:1] * 3 if column is None else [column] + arrays[:2]


class Part:
    def __init__(self, rows, width, spots):
        self.rows, self.width, self.spots = rows, width, spots

    def scratch(self):
        return pltpu.VMEM((2, 2, 2, 2, 2, self.rows // 32, self.width), jnp.bfloat16)

    def start(self, refs_of, place, dst, sem):
        z1, z0, y, x, core = [place[axis] for axis in range(5)]
        high = self.rows // 32
        for source, first_row, first_col, at_col, width in self.spots:
            refs = refs_of(source)
            cols = slice(first_col, first_col + width)
            into = slice(at_col, at_col + width)
            if source.kind == "whole":
                pltpu.make_async_copy(
                    refs[0].at[:, :, :, :, :, :, cols], dst.at[:, :, :, :, :, :, into], sem
                ).start()
            elif source.kind == "cores":
                for which in range(2):
                    owner = core if which == 0 else 1 - core
                    pltpu.make_async_copy(
                        refs[which].at[:, :, :, :, first_row : first_row + high, cols],
                        dst.at[:, :, :, :, owner, :, into],
                        sem,
                    ).start()
            else:
                for which in range(4):
                    owner = core if which < 2 else 1 - core
                    for near, at_y, at_x in flipped(source.first_flip, which % 2, y, x):
                        for up, at_z1, at_z0 in four(z1, z0):
                            pltpu.make_async_copy(
                                refs[which].at[near, up[0], up[1], :, cols],
                                dst.at[at_z1, at_z0, at_y, at_x, owner, :, into],
                                sem,
                            ).start()


def four(z1, z0):
    return [
        ((low, high), z1 if high == 0 else 1 - z1, z0 if low == 0 else 1 - z0)
        for low in range(2)
        for high in range(2)
    ]


def flipped(first_flip, beyond, y, x):
    found = []
    for near in range(2):
        a, b = (near, beyond) if first_flip == "x" else (beyond, near)
        found.append((near, y if b == 0 else 1 - y, x if a == 0 else 1 - x))
    return found


def after(value, *others):
    return lax.optimization_barrier((value, *others))[0]


def gather_flips(shards, first_flips, hold=None):
    if not paired():
        full = [lax.all_gather(shard, "blk", axis=0, tiled=True) for shard in shards]
        return [
            Source("whole", [array.reshape(2, 2, 2, 2, 2, array.shape[0] // 32, array.shape[1])])
            for array in full
        ]
    core = lax.axis_index("dp")
    columns = []
    for shard in shards:
        rows = shard.shape[0]
        own = lax.dynamic_slice_in_dim(shard, core * (rows // 2), rows // 2, 0)
        columns.append(with_flip(with_flip(own, 8), 4))
    sources, bits = [], {"x": (1, 2), "y": (2, 1)}
    if hold is not None:
        columns = after(columns, hold)
    planes = [
        with_flip(column, bits[first][0]) for column, first in zip(columns, first_flips)
    ]
    for column, plane, first in zip(columns, planes, first_flips):
        beyond = flip(plane, bits[first][1])
        sources.append(
            Source("flips", [plane, beyond, swap_core(plane), swap_core(beyond)], first, column)
        )
    return sources


class RowPart:
    def __init__(self, sources, span):
        self.span = span
        self.rows, self.width = 16 * span, WIDTH
        self.spots = [(source,) for source in sources]

    def scratch(self):
        return pltpu.VMEM((2, 2, 2, 2, self.span, WIDTH), jnp.bfloat16)

    def start(self, refs_of, place, dst, sem):
        z1, z0, y, x = [place[axis] for axis in range(4)]
        half = WIDTH // 2
        for side, (source,) in enumerate(self.spots):
            refs = refs_of(source)
            for beyond in range(2):
                for near, at_y, at_x in flipped(source.first_flip, beyond, y, x):
                    for up, at_z1, at_z0 in four(z1, z0):
                        pltpu.make_async_copy(
                            refs[beyond].at[near, up[0], up[1]],
                            dst.at[at_z1, at_z0, at_y, at_x, :, side * half : (side + 1) * half],
                            sem,
                        ).start()


def gather_row(block, hold_near=None, hold=None):
    row = lax.axis_index("blk") // 8
    own = lax.dynamic_index_in_dim(block, row, 0, keepdims=False)
    other = lax.dynamic_index_in_dim(block, 1 - row, 0, keepdims=False)
    pair = jnp.stack([own, flip(other, 8)])
    if hold_near is not None:
        pair = after(pair, hold_near)
    column = with_flip(pair, 4)
    stages, sources = [pair, column], []
    if hold is not None:
        column = after(column, hold)
    half = WIDTH // 2
    planes = [with_flip(column[..., :half], 1), with_flip(column[..., half:], 2)]
    for plane, first, bit in zip(planes, "xy", (2, 1)):
        sources.append(Source("row", [plane, flip(plane, bit)], first))
    stages += [planes, [source.arrays[1] for source in sources]]
    return RowPart(sources, block.shape[1]), stages


def head_columns(shards, kinds):
    core = lax.axis_index("dp")
    blocks, widths = [], [128 * kind for kind in kinds]
    for shard, kind in zip(shards, kinds):
        own = lax.dynamic_slice_in_dim(shard, core * 32, 32, 0)
        own = own.reshape(32, kind, 8, 128).transpose(2, 0, 1, 3)
        blocks.append(own.reshape(8, 32, kind * 128))
    blocks = jnp.concatenate(blocks, axis=2)
    mine = exchange(jnp.concatenate([blocks, blocks], axis=0))
    mine = mine.reshape(2, 2, 2, 2, 32, sum(widths))
    source = Source("cores", [mine, swap_core(mine)])
    parts, place = [], 0
    for width in widths:
        parts.append(Part(1024, width, [(source, 0, place, 0, width)]))
        place += width
    return parts


def project_row(row_part, head_part, name):
    def body(ins, loaded, outs, _):
        weight = loaded[1].value()
        inputs = loaded[0].value()
        for first in range(0, row_part.rows, 256):
            rows = slice(first, first + 256)
            outs[0][rows, :] = dot(inputs[rows], weight).astype(jnp.bfloat16)

    (found,) = call_with_parts(
        body,
        [],
        [row_part, head_part],
        [shape(row_part.rows, head_part.width, of=jnp.bfloat16)],
        name,
    )
    return found


def row_grad(row_part, upstream, name):
    columns = upstream.shape[1]

    def body(ins, loaded, outs, _):
        core = ins[1][0]
        inputs = loaded[0].value()
        grads = []
        for first in range(0, columns, 128):
            grads.append(pair_dot(ins[0][:, first : first + 128], inputs, 0, 0).T)
        grad = jnp.concatenate(grads, axis=1).astype(jnp.bfloat16).reshape(16, 2, 32, columns)
        outs[0][core] = grad[:, 0]
        outs[0][1 - core] = grad[:, 1]

    (terms,) = call_with_parts(
        body,
        [upstream],
        [row_part],
        [shape(2, 16, 32, columns, of=jnp.bfloat16)],
        name,
        scalars=[lax.axis_index("dp").reshape(1).astype(jnp.int32)],
    )
    got = swap_core(terms[1])
    return (terms[0].astype(jnp.float32) + got.astype(jnp.float32)).astype(jnp.bfloat16)


def row_back(upstream, head_part, name):
    def body(ins, loaded, outs, _):
        weight = loaded[0].value()
        for first in range(0, ins[0].shape[0], 256):
            rows = slice(first, first + 256)
            outs[0][rows, :] = dot_back(ins[0][rows, :], weight).astype(jnp.bfloat16)

    (terms,) = call_with_parts(
        body, [upstream], [head_part], [shape(upstream.shape[0], WIDTH, of=jnp.bfloat16)], name
    )
    return terms


def reduce_row(terms, holds=None):
    blocks = terms.reshape(16, terms.shape[0] // 16, WIDTH)
    (both,), stages = scatter_chips([blocks], [(1, 2, 4, 8)], 0, 3, holds)
    row = lax.axis_index("blk") // 8
    kept = lax.dynamic_index_in_dim(both, row, 0, keepdims=False)
    other = lax.dynamic_index_in_dim(both, 1 - row, 0, keepdims=False)
    got = flip(other, 8)
    found = jnp.stack([jnp.where(row == 0, kept, got), jnp.where(row == 0, got, kept)])
    return found.astype(jnp.float32), stages


def finish_row_grad(got, kinds):
    total = jnp.sum(got.reshape(2, 8, 32, kinds, 128).astype(jnp.float32), axis=0)
    mine = total.astype(jnp.bfloat16).transpose(1, 2, 0, 3).reshape(32, kinds * WIDTH)
    other = swap_core(mine)
    core = lax.axis_index("dp")
    low = jnp.where(core == 0, mine, other)
    high = jnp.where(core == 0, other, mine)
    return jnp.concatenate([low, high], axis=0).astype(jnp.float32)


def columns_of(*pieces):
    spots, place = [], 0
    for source, first, width in pieces:
        spots.append((source, 0, first, place, width))
        place += width
    return Part(1024, place, spots)


PACK = 512


def pack_halves(shards):
    places = [
        (index, shard.shape[0] // 2, first)
        for index, shard in enumerate(shards)
        for first in range(0, shard.shape[1], PACK)
    ]

    def body(core, *refs):
        out_ref, place = refs[-1], 0
        for index, high, first in places:
            start = pl.multiple_of(core[0] * high, 16)
            out_ref[place : place + high, :] = refs[index][pl.ds(start, high), first : first + PACK]
            place += high

    return pl.pallas_call(
        body,
        out_shape=shape(sum(high for _, high, _ in places), PACK, of=jnp.bfloat16),
        in_specs=[smem_spec()] + [vmem_spec()] * len(shards),
        out_specs=vmem_spec(),
        compiler_params=pltpu.CompilerParams(vmem_limit_bytes=VMEM_BYTES),
        cost_estimate=cost(2),
        name="pack_halves",
    )(lax.axis_index("dp").reshape(1).astype(jnp.int32), *shards)


def gather_packed(packed):
    return lax.all_gather(packed, "blk", axis=0)


def packed_parts(shards, mine):
    if not paired():
        found = []
        for source, shard in zip(gather_flips(shards, "x" * len(shards)), shards):
            rows, columns = 32 * source.arrays[0].shape[5], shard.shape[1]
            step = min(columns, 1024)
            found.append(
                [
                    Part(rows, step, [(source, 0, first, 0, step)])
                    for first in range(0, columns, step)
                ]
            )
        return found
    spots, place = [], 0
    for shard in shards:
        high = shard.shape[0] // 2
        places = []
        for first in range(0, shard.shape[1], PACK):
            places.append(place)
            place += high
        spots.append((shard.shape[0] * 16, places))
    mine = mine.reshape(2, 2, 2, 2, place, PACK)
    source = Source("cores", [mine, swap_core(mine)])
    found = []
    for rows, places in spots:
        parts = []
        for first in range(0, len(places), 2):
            two = places[first : first + 2]
            parts.append(
                Part(
                    rows,
                    PACK * len(two),
                    [(source, row, 0, PACK * side, PACK) for side, row in enumerate(two)],
                )
            )
        found.append(parts)
    return found


def place_now():
    own, core = lax.axis_index("blk"), lax.axis_index("dp")
    bits = [(own // bit) % 2 for bit in FLIPS]
    return jnp.stack(bits + [core]).astype(jnp.int32)


class Loaded:
    def __init__(self, part, dst, sem):
        self.part, self.dst, self.sem, self.here = part, dst, sem, False

    def value(self):
        if not self.here:
            pltpu.make_async_copy(self.dst, self.dst, self.sem).wait()
            self.here = True
        return self.dst[...].reshape(self.part.rows, self.part.width)


def call_with_parts(body, inputs, parts, outputs, name, scratch=(), takes=5, scalars=()):
    sources = []
    for part in parts:
        sources += [spot[0] for spot in part.spots if spot[0] not in sources]
    arrays = [array for source in sources for array in source.arrays]

    def kernel(place, *refs):
        refs = list(refs)
        ins = [refs.pop(0) for _ in (*inputs, *scalars)]
        pieces = [[refs.pop(0) for _ in source.arrays] for source in sources]
        outs = [refs.pop(0) for _ in outputs]
        dsts = [refs.pop(0) for _ in parts]
        sems = refs.pop(0)
        loaded = []
        for index, part in enumerate(parts):
            part.start(
                lambda source: pieces[sources.index(source)], place, dsts[index], sems.at[index]
            )
            loaded.append(Loaded(part, dsts[index], sems.at[index]))
        body(ins, loaded, outs, refs)

    return pl.pallas_call(
        kernel,
        out_shape=tuple(outputs),
        in_specs=[smem_spec()]
        + [vmem_spec()] * len(inputs)
        + [smem_spec()] * len(scalars)
        + [pl.BlockSpec(memory_space=pl.ANY)] * len(arrays),
        out_specs=(vmem_spec(),) * len(outputs),
        scratch_shapes=[part.scratch() for part in parts]
        + [pltpu.SemaphoreType.DMA((len(parts),))]
        + list(scratch),
        compiler_params=pltpu.CompilerParams(vmem_limit_bytes=VMEM_BYTES),
        cost_estimate=cost(takes),
        name=name,
    )(place_now(), *inputs, *scalars, *arrays)


def vmem_spec():
    return pl.BlockSpec(memory_space=pltpu.VMEM)


def smem_spec():
    return pl.BlockSpec(memory_space=pltpu.SMEM)


def seg_of_pos(ends_ref, pos):
    seg = jnp.zeros(pos.shape, jnp.int32)
    for slot in range(ends_ref.shape[0]):
        seg = seg + (ends_ref[slot] <= pos).astype(jnp.int32)
    return seg


def pair_dot(left, right, left_dim, right_dim):
    return lax.dot_general(
        left, right, (((left_dim,), (right_dim,)), ((), ())), preferred_element_type=jnp.float32
    )


def seg_tables(q_ends, k_ends, span):
    seg_q = seg_of_pos(q_ends, lax.broadcasted_iota(jnp.int32, (1, span), 1))
    seg_k = seg_of_pos(k_ends, lax.broadcasted_iota(jnp.int32, (span, 1), 0))
    return seg_q, seg_k


def masked_scores(keys, queries, seg_q, seg_k, first, causal):
    scores = pair_dot(keys, queries, 1, 1)
    allowed = seg_k == seg_q
    if causal:
        key_pos = lax.broadcasted_iota(jnp.int32, scores.shape, 0)
        query_pos = first + lax.broadcasted_iota(jnp.int32, scores.shape, 1)
        allowed = allowed & (key_pos <= query_pos)
    return jnp.where(allowed, scores, NEG)


def attn_forward_body(causal, width, q_ends, k_ends, q_ref, kv_ref, low_ref, full_ref, lse_ref):
    span = q_ref.shape[0]
    step = math.gcd(span, 256)
    heads = width // HEAD_DIM
    seg_q, seg_k = seg_tables(q_ends, k_ends, span)
    key_at = kv_ref.shape[1] - 2 * width
    scaled = q_ref[:, :width] * jnp.bfloat16(HEAD_DIM ** (-0.5))
    keys = kv_ref[:, key_at : key_at + width]
    values = kv_ref[:, key_at + width : key_at + 2 * width]
    for first in range(0, span, step):
        reach = first + step if causal else span
        parts = []
        for head in range(heads):
            cols = slice(head * HEAD_DIM, (head + 1) * HEAD_DIM)
            scores = masked_scores(
                keys[:reach, cols],
                scaled[first : first + step, cols],
                seg_q[:, first : first + step],
                seg_k[:reach],
                first,
                causal,
            )
            top = jnp.max(scores, axis=0, keepdims=True)
            probs = jnp.exp(scores - top)
            total = jnp.sum(probs, axis=0, keepdims=True)
            mixed = pair_dot(values[:reach, cols], probs.astype(jnp.bfloat16), 0, 0)
            parts.append(mixed / total)
            lse_ref[head : head + 1, first : first + step] = top + jnp.log(total)
        joined = jnp.concatenate(parts, axis=0).T
        full_ref[first : first + step, :] = joined
        low_ref[first : first + step, :] = joined.astype(jnp.bfloat16)


def attn_forward(q_ends, k_ends, queries, keys_values, width, causal):
    span = queries.shape[0]
    return pl.pallas_call(
        functools.partial(attn_forward_body, causal, width),
        out_shape=(
            jax.ShapeDtypeStruct((span, width), jnp.bfloat16),
            jax.ShapeDtypeStruct((span, width), jnp.float32),
            jax.ShapeDtypeStruct((width // HEAD_DIM, span), jnp.float32),
        ),
        in_specs=[smem_spec(), smem_spec()] + [vmem_spec()] * 2,
        out_specs=(vmem_spec(),) * 3,
        compiler_params=pltpu.CompilerParams(vmem_limit_bytes=VMEM_BYTES),
        cost_estimate=cost(8),
        name="attn_forward",
    )(q_ends, k_ends, queries, keys_values)


def attn_backward_body(
    causal,
    width,
    q_ends,
    k_ends,
    q_ref,
    kv_ref,
    up_ref,
    full_ref,
    lse_ref,
    *outs,
):
    dq_ref, dkv_ref = outs[0], outs[-3]
    dk_sum, dv_sum = outs[-2:]
    span = q_ref.shape[0]
    step = math.gcd(span, 256)
    heads = width // HEAD_DIM
    seg_q, seg_k = seg_tables(q_ends, k_ends, span)
    key_at = kv_ref.shape[1] - 2 * width
    scaled = q_ref[:, :width] * jnp.bfloat16(HEAD_DIM ** (-0.5))
    keys = kv_ref[:, key_at : key_at + width]
    values = kv_ref[:, key_at + width : key_at + 2 * width]
    upstream = up_ref[...]
    dk_sum[...] = jnp.zeros_like(dk_sum)
    dv_sum[...] = jnp.zeros_like(dv_sum)
    for first in range(0, span, step):
        reach = first + step if causal else span
        rows = slice(first, first + step)
        product = (upstream[rows].astype(jnp.float32) * full_ref[rows, :]).T
        parts = []
        for head in range(heads):
            cols = slice(head * HEAD_DIM, (head + 1) * HEAD_DIM)
            delta = jnp.sum(product[cols], axis=0, keepdims=True)
            scores = masked_scores(
                keys[:reach, cols], scaled[rows, cols], seg_q[:, rows], seg_k[:reach], first, causal
            )
            probs = jnp.exp(scores - lse_ref[head : head + 1, rows])
            dv_sum[head, :reach] += pair_dot(
                probs.astype(jnp.bfloat16), upstream[rows, cols], 1, 0
            )
            grad_probs = pair_dot(values[:reach, cols], upstream[rows, cols], 1, 1)
            grad_scores = (probs * (grad_probs - delta)).astype(jnp.bfloat16)
            dk_sum[head, :reach] += pair_dot(grad_scores, scaled[rows, cols], 1, 0)
            parts.append(pair_dot(keys[:reach, cols], grad_scores, 0, 0))
        joined = jnp.concatenate(parts, axis=0).T * HEAD_DIM ** (-0.5)
        dq_ref[rows, :width] = joined.astype(jnp.bfloat16)
    sums = [dk_sum[head] for head in range(heads)] + [dv_sum[head] for head in range(heads)]
    kv_at = dkv_ref.shape[1] - 2 * width
    dkv_ref[:, kv_at:] = jnp.concatenate(sums, axis=1).astype(jnp.bfloat16)


def attn_backward(
    q_ends, k_ends, queries, keys_values, upstream, full, lse, causal, joined=False
):
    span, width = upstream.shape
    kinds = [3] if joined else [1, 2]
    heads = width // HEAD_DIM
    return pl.pallas_call(
        functools.partial(attn_backward_body, causal, width),
        out_shape=[jax.ShapeDtypeStruct((span, kind * width), jnp.bfloat16) for kind in kinds],
        in_specs=[smem_spec(), smem_spec()] + [vmem_spec()] * 5,
        out_specs=[vmem_spec()] * len(kinds),
        scratch_shapes=[pltpu.VMEM((heads, span, HEAD_DIM), jnp.float32)] * 2,
        compiler_params=pltpu.CompilerParams(vmem_limit_bytes=VMEM_BYTES),
        cost_estimate=cost(8),
        name="attn_backward",
    )(q_ends, k_ends, queries, keys_values, upstream, full, lse)


def exchange(blocks):
    return lax.all_to_all(blocks, "blk", 0, 0, tiled=True)


def as_rows(blocks):
    return blocks.reshape(blocks.shape[0] * blocks.shape[1], blocks.shape[2])


def as_blocks(rows):
    devices = lax.axis_size("blk")
    return rows.reshape(devices, rows.shape[0] // devices, rows.shape[1])


def write_blocks(out_ref, values, lanes, kind, width):
    span = values.shape[0] // lanes
    for group in range(WIDTH // width):
        for lane in range(lanes):
            out_ref[lane * (WIDTH // width) + group, :, kind * width : (kind + 1) * width] = values[
                lane * span : (lane + 1) * span, group * width : (group + 1) * width
            ]


def read_blocks(got_ref, lanes, kind, width):
    groups = got_ref.shape[0] // lanes
    cols = slice(kind * width, (kind + 1) * width)
    rows = [
        jnp.concatenate([got_ref[lane * groups + group, :, cols] for group in range(groups)], axis=1)
        for lane in range(lanes)
    ]
    return jnp.concatenate(rows, axis=0)


def dot(left, right):
    return pair_dot(left, right, 1, 0)


def dot_back(left, right):
    return pair_dot(left, right, 1, 1)


def shape(*sizes, of=jnp.float32):
    return jax.ShapeDtypeStruct(sizes, of)


def normalize(values):
    center = values - jnp.mean(values, -1, keepdims=True)
    scale = lax.rsqrt(jnp.mean(center * center, -1, keepdims=True) + 1e-05)
    return center * scale, scale


def norm_back(upstream, normed, scale, gains_row):
    grad = upstream * gains_row
    return scale * (
        grad
        - jnp.mean(grad, -1, keepdims=True)
        - normed * jnp.mean(grad * normed, -1, keepdims=True)
    )


def project_blocks(inputs, parts, lanes, width, name):
    def body(ins, loaded, outs, _):
        for kind, weight in enumerate(loaded):
            write_blocks(
                outs[0], dot(ins[0][...], weight.value()).astype(jnp.bfloat16), lanes, kind, width
            )

    devices, span = lax.axis_size("blk"), inputs.shape[0] // lanes
    (blocks,) = call_with_parts(
        body,
        [inputs],
        parts,
        [shape(devices, span, width * len(parts), of=jnp.bfloat16)],
        name,
    )
    return blocks


def after_self(got, tokens, gains, biases, out_part, query_part, lanes, width):
    def body(ins, loaded, outs, _):
        got_ref, tokens_ref, gains_ref, biases_ref = ins
        low_ref, normed_ref, scale_ref, hidden_ref, blocks_ref = outs
        attended = read_blocks(got_ref, lanes, 0, width)
        low_ref[...] = attended
        resid = tokens_ref[...].astype(jnp.float32) + dot(attended, loaded[0].value())
        normed, scale = normalize(resid)
        normed_ref[...] = normed
        scale_ref[...] = scale
        hidden = (normed * gains_ref[0:1] + biases_ref[0:1]).astype(jnp.bfloat16)
        hidden_ref[...] = hidden
        query = dot(hidden, loaded[1].value()).astype(jnp.bfloat16)
        write_blocks(blocks_ref, query, lanes, 0, width)

    rows = tokens.shape[0]
    return call_with_parts(
        body,
        [got, tokens, gains, biases],
        [out_part, query_part],
        [
            shape(rows, WIDTH, of=jnp.bfloat16),
            shape(rows, WIDTH),
            shape(rows, 1),
            shape(rows, WIDTH, of=jnp.bfloat16),
            shape(*got.shape, of=jnp.bfloat16),
        ],
        "after_self",
    )


def feed_forward(got, normed_in, cotangent, gains, biases, out_part, in_parts, down, outs, up, lanes, width):
    pieces = len(in_parts)
    step = in_parts[0].width

    def body(ins, loaded, refs, scratch):
        got_ref, normed_in_ref, cot_ref, gains_ref, biases_ref = ins
        (
            output_ref,
            low_ref,
            mixed_ref,
            adapted_ref,
            dunder_ref,
            dab_ref,
            dcb_ref,
            dresid_ref,
            blocks_ref,
            norms_ref,
        ) = refs
        slopes, acts = scratch
        w_out, w_down, w_in = loaded[0], loaded[1], loaded[2 : 2 + pieces]
        w_ff, w_up = loaded[2 + pieces :]
        attended = read_blocks(got_ref, lanes, 0, width)
        low_ref[...] = attended
        hidden = normed_in_ref[...] * gains_ref[0:1] + biases_ref[0:1]
        normed_one, scale_one = normalize(hidden + dot(attended, w_out.value()))
        mixed = normed_one * gains_ref[1:2] + biases_ref[1:2]
        mixed_low = mixed.astype(jnp.bfloat16)
        mixed_ref[...] = mixed_low
        summed = mixed
        under = dot(mixed_low, w_down.value())
        gate = 1.0 / (1.0 + jnp.exp(-under))
        adapted = (under * gate).astype(jnp.bfloat16)
        adapted_ref[...] = adapted
        under_slope = gate * (1.0 + under * (1.0 - gate))
        for piece in range(pieces):
            before = dot(mixed_low, w_in[piece].value())
            below = 0.5 + 0.5 * lax.erf(before * (0.5**0.5))
            slopes[piece] = below + before * jnp.exp(-0.5 * before * before) * (
                (2.0 * math.pi) ** -0.5
            )
            acts[piece] = (before * below).astype(jnp.bfloat16)
        for piece in range(pieces):
            summed = summed + dot(acts[piece], w_ff[piece].value())
        summed = summed + 4.0 * dot(adapted, w_up.value())
        normed_two, scale_two = normalize(summed)
        output_ref[...] = (normed_two * gains_ref[2:3] + biases_ref[2:3]).astype(jnp.bfloat16)
        upstream = cot_ref[...].astype(jnp.float32)
        norms_ref[0:1] = jnp.sum(upstream * normed_two, axis=0, keepdims=True)
        norms_ref[1:2] = jnp.sum(upstream, axis=0, keepdims=True)
        dz = norm_back(upstream, normed_two, scale_two, gains_ref[2:3])
        dzb = dz.astype(jnp.bfloat16)
        dab = (4.0 * dz).astype(jnp.bfloat16)
        dab_ref[...] = dab
        dunder = (under_slope * dot_back(dab, w_up.value())).astype(jnp.bfloat16)
        dunder_ref[...] = dunder
        dmixed = dz + dot_back(dunder, w_down.value())
        for piece in range(pieces):
            dpre = (slopes[piece] * dot_back(dzb, w_ff[piece].value())).astype(jnp.bfloat16)
            dmixed = dmixed + dot_back(dpre, w_in[piece].value())
        norms_ref[2:3] = jnp.sum(dmixed * normed_one, axis=0, keepdims=True)
        norms_ref[3:4] = jnp.sum(dmixed, axis=0, keepdims=True)
        dresid = norm_back(dmixed, normed_one, scale_one, gains_ref[1:2])
        dresid_ref[...] = dresid
        dcb = dresid.astype(jnp.bfloat16)
        dcb_ref[...] = dcb
        write_blocks(
            blocks_ref, dot_back(dcb, w_out.value()).astype(jnp.bfloat16), lanes, 0, width
        )

    rows = normed_in.shape[0]
    low = jnp.bfloat16

    def body_rows(ins, loaded, refs, scratch):
        whole_ff = loaded[2 + pieces]

        class Rows:
            def __init__(self, piece):
                self.piece = piece

            def value(self):
                return whole_ff.value()[self.piece * step : (self.piece + 1) * step]

        loaded = loaded[: 2 + pieces] + [[Rows(piece) for piece in range(pieces)], loaded[-1]]
        body(ins, loaded, refs, scratch)

    return call_with_parts(
        body_rows,
        [got, normed_in, cotangent, gains, biases],
        [out_part, down] + in_parts + [outs, up],
        [
            shape(rows, WIDTH, of=low),
            shape(rows, WIDTH, of=low),
            shape(rows, WIDTH, of=low),
            shape(rows, down.width, of=low),
            shape(rows, down.width, of=low),
            shape(rows, WIDTH, of=low),
            shape(rows, WIDTH, of=low),
            shape(rows, WIDTH),
            shape(*got.shape, of=low),
            shape(4, WIDTH),
        ],
        "feed_forward",
        [
            pltpu.VMEM((pieces, rows, step), jnp.float32),
            pltpu.VMEM((pieces, rows, step), jnp.bfloat16),
        ],
        20,
    )


def before_self(got, dresid, normed, scale, gains, query_part, out_part, lanes, width):
    def body(ins, loaded, outs, _):
        got_ref, dresid_ref, normed_ref, scale_ref, gains_ref = ins
        dcq_ref, dr_ref, dsb_ref, blocks_ref, norms_ref = outs
        dcq = read_blocks(got_ref, lanes, 0, width)
        dcq_ref[...] = dcq
        dhidden = dresid_ref[...] + dot_back(dcq, loaded[0].value())
        normed = normed_ref[...]
        norms_ref[0:1] = jnp.sum(dhidden * normed, axis=0, keepdims=True)
        norms_ref[1:2] = jnp.sum(dhidden, axis=0, keepdims=True)
        dr = norm_back(dhidden, normed, scale_ref[...], gains_ref[0:1])
        dr_ref[...] = dr
        dsb = dr.astype(jnp.bfloat16)
        dsb_ref[...] = dsb
        grad = dot_back(dsb, loaded[1].value()).astype(jnp.bfloat16)
        write_blocks(blocks_ref, grad, lanes, 0, width)

    rows = dresid.shape[0]
    return call_with_parts(
        body,
        [got, dresid, normed, scale, gains],
        [query_part, out_part],
        [
            shape(rows, WIDTH, of=jnp.bfloat16),
            shape(rows, WIDTH),
            shape(rows, WIDTH, of=jnp.bfloat16),
            shape(*got.shape, of=jnp.bfloat16),
            shape(2, WIDTH),
        ],
        "before_self",
    )


def input_grad(got, start, parts, lanes, span, width, name):
    def body(ins, loaded, outs, _):
        total = None
        for kind, weight in enumerate(loaded):
            values = read_blocks(ins[0], lanes, kind, width)
            term = dot_back(values, weight.value())
            total = term if total is None else total + term
        outs[0][...] = total if len(ins) == 1 else total + ins[1][...]

    rows = span * lanes
    return call_with_parts(
        body,
        [got] if start is None else [got, start],
        parts,
        [shape(rows, WIDTH)],
        name,
    )


def shards(
    tokens,
    encoder,
    cotangent,
    self_in,
    self_out,
    cross_q,
    cross_kv,
    cross_out,
    ffn_in,
    ffn_out,
    adapt_down,
    adapt_up,
    norm_gain,
    norm_bias,
    tgt_lengths,
    src_lengths,
):
    lanes, span, _ = tokens.shape
    rows = lanes * span
    width = WIDTH * lanes // lax.axis_size("blk")
    own_row = lax.axis_index("blk") // (lax.axis_size("blk") // lanes)
    tgt_ends = jnp.cumsum(lax.dynamic_index_in_dim(tgt_lengths, own_row, 0, keepdims=False))
    src_ends = jnp.cumsum(lax.dynamic_index_in_dim(src_lengths, own_row, 0, keepdims=False))
    flat_tokens = tokens.reshape(rows, WIDTH)
    flat_encoder = encoder.reshape(rows, WIDTH)
    frozen = [ffn_in, adapt_down, ffn_out, adapt_up, cross_out]

    if paired():
        packed = gather_packed(pack_halves(frozen))
        self_packed = pack_halves([self_in])
        token_row, stages = gather_row(tokens)
        self_heads, pair_heads = head_columns([self_in, cross_kv], [3, 2])
        out_shard, query_shard = after((self_out, cross_q), stages[1])
        encoder_block = after(encoder, stages[1])
        self_qkv = project_row(token_row, self_heads, "self_in")
        out_source, query_source = gather_flips([out_shard, query_shard], "xy", self_qkv)
        encoder_row, encoder_stages = gather_row(
            encoder_block, self_qkv, (out_source.arrays[1], query_source.arrays[1])
        )
        self_qkv = after(self_qkv, out_source.stages[0], query_source.stages[0])
        pair_own = project_row(encoder_row, pair_heads, "cross_kv")
    else:
        (self_source, pair_source, out_source, query_source) = gather_flips(
            [self_in, cross_kv, self_out, cross_q], "xyxy"
        )
        self_parts = [columns_of((self_source, WIDTH * kind, WIDTH)) for kind in range(3)]
        pair_parts = [columns_of((pair_source, WIDTH * kind, WIDTH)) for kind in range(2)]
        self_qkv = as_rows(
            exchange(project_blocks(flat_tokens, self_parts, lanes, width, "self_in"))
        )
        pair_own = as_rows(
            exchange(project_blocks(flat_encoder, pair_parts, lanes, width, "cross_kv"))
        )
    self_out_part = columns_of((out_source, 0, WIDTH))
    query_part = columns_of((query_source, 0, WIDTH))

    self_mid, self_full, self_lse = attn_forward(
        tgt_ends, tgt_ends, self_qkv, self_qkv, width, True
    )
    self_sent = after(self_mid, out_source.stages[1], query_source.stages[1])
    if paired():
        self_sent = after(self_sent, encoder_stages[0])
    self_back = exchange(as_blocks(self_sent))
    if paired():
        self_back = after(self_back, encoder_stages[1])
    self_low, normed, scale, hidden_low, query_blocks = after_self(
        self_back,
        flat_tokens,
        norm_gain,
        norm_bias,
        self_out_part,
        query_part,
        lanes,
        width,
    )
    cross_own = as_rows(exchange(query_blocks))
    cross_mid, cross_full, cross_lse = attn_forward(
        tgt_ends, src_ends, cross_own, pair_own, width, False
    )
    cross_back = exchange(as_blocks(cross_mid))
    ready = after(packed, cross_mid) if paired() else None
    ff_parts, down_parts, ffo_parts, up_parts, (cross_out_part,) = packed_parts(frozen, ready)
    if paired():
        self_packed = gather_packed(after(self_packed, cross_back))
    (
        output,
        cross_low,
        mixed_low,
        adapter_low,
        grad_under,
        adapt_low,
        cross_branch_low,
        grad_resid_two,
        cross_grad_blocks,
        norms_high,
    ) = feed_forward(
        cross_back,
        normed,
        cotangent.reshape(rows, WIDTH),
        norm_gain,
        norm_bias,
        cross_out_part,
        ff_parts,
        down_parts[0],
        ffo_parts[0],
        up_parts[0],
        lanes,
        width,
    )
    high_groups = [
        [(cross_low, cross_branch_low)],
        [(mixed_low, grad_under), (adapter_low, adapt_low)],
    ]
    high_terms = [grad_terms(pairs) for pairs in high_groups]
    high_orders = [(2, 1, 4, 8), (1, 2, 4, 8)]
    high_terms, high_stages = scatter_chips(high_terms, high_orders, 0, 2)
    cross_dq, cross_dkv = attn_backward(
        tgt_ends,
        src_ends,
        cross_own,
        pair_own,
        as_rows(after(exchange(cross_grad_blocks), high_stages[0])),
        cross_full,
        cross_lse,
        False,
    )
    cross_dq_got = after(exchange(as_blocks(cross_dq)), high_stages[1])
    if paired():
        dkv_late = after(cross_dkv, high_stages[1])
        pair_terms = row_back(dkv_late, pair_heads, "encoder_grad")
        kv_sent = row_grad(encoder_row, dkv_late, "cross_kv_grad")
        cross_dq_got = after(cross_dq_got, pair_terms, kv_sent)
    cq_low, grad_resid_one, self_branch_low, self_grad_blocks, norms_low = before_self(
        cross_dq_got,
        grad_resid_two,
        normed,
        scale,
        norm_gain,
        query_part,
        self_out_part,
        lanes,
        width,
    )
    norms = jnp.concatenate([norms_low, norms_high], axis=0)
    mid_pairs = [(hidden_low, cq_low), (self_low, self_branch_low)]
    mid_orders = [(2, 1, 4, 8), (1, 2, 4, 8)]
    mid_terms = [grad_terms([pair]) for pair in mid_pairs]
    mid_terms, _ = scatter_chips(mid_terms, mid_orders, 0, 1)
    if paired():
        high_terms = [jnp.concatenate(after(high_terms, self_grad_blocks), axis=2)]
        high_terms, _ = scatter_chips(high_terms, [(2, 1, 4, 8)], 2, 3)
    self_upstream = after(exchange(self_grad_blocks), high_stages[2])
    (self_grads,) = attn_backward(
        tgt_ends,
        tgt_ends,
        self_qkv,
        self_qkv,
        as_rows(self_upstream),
        self_full,
        self_lse,
        True,
        joined=True,
    )
    if paired():
        (self_parts,) = packed_parts([self_in], after(self_packed, self_grads))
        self_got = exchange(as_blocks(self_grads))
        high_terms, _ = scatter_chips(after(high_terms, self_grads), [(2, 1, 4, 8)], 3, 4)
        self_sent = row_grad(token_row, after(self_grads, high_terms[0]), "self_in_grad")
        mid_terms, _ = scatter_chips(after(mid_terms, self_grads), mid_orders, 1, 2)
        mid_terms = [jnp.concatenate(mid_terms, axis=2)]
        chunks = [
            array[:, :, first : first + width]
            for array in (self_sent, kv_sent)
            for first in range(0, array.shape[2], width)
        ]
        partials = norms.astype(jnp.bfloat16).reshape(1, 48, width)
        chunks.append(jnp.broadcast_to(partials, (16, 48, width)))
        sent = after(jnp.concatenate(chunks, axis=1), self_got)
        got = exchange(sent)
        (tokens_grad,) = input_grad(
            self_got, grad_resid_one, self_parts, lanes, span, width, "tokens_grad"
        )
        encoder_grad, _ = reduce_row(pair_terms, {2: tokens_grad})
        encoder_grad = encoder_grad.reshape(rows, WIDTH)
        mid_terms, _ = scatter_chips(
            mid_terms, mid_orders[:1], 2, 4, {2: tokens_grad}
        )
        got = after(got, tokens_grad)
        chunks = [got[:, first : first + 32] for first in range(0, 160, 32)]
        grad_self_in = finish_row_grad(jnp.concatenate(chunks[:3], axis=2), 3)
        grad_cross_kv = finish_row_grad(jnp.concatenate(chunks[3:], axis=2), 2)
        norms = jnp.sum(got[:, 160:].astype(jnp.float32), axis=0).reshape(6, WIDTH)
        norms = norms + swap_core(norms)
    else:
        pair_got = exchange(as_blocks(cross_dkv))
        self_got = exchange(as_blocks(self_grads))
        (encoder_grad,) = input_grad(
            pair_got, None, pair_parts, lanes, span, width, "encoder_grad"
        )
        (tokens_grad,) = input_grad(
            self_got, grad_resid_one, self_parts, lanes, span, width, "tokens_grad"
        )
        pair_low = pair_got.reshape(lanes, -1, span, 2, width).transpose(0, 2, 3, 1, 4)
        self_low_grads = self_got.reshape(lanes, -1, span, 3, width).transpose(0, 2, 3, 1, 4)
        grad_cross_kv = weight_grad(flat_encoder, pair_low.reshape(rows, 2 * WIDTH))
        grad_self_in = weight_grad(flat_tokens, self_low_grads.reshape(rows, 3 * WIDTH))
        norms = lax.psum(norms, ("dp", "blk"))
    ((grad_cross_q, grad_self_out),) = finish_terms([mid_pairs], mid_terms)
    (grad_cross_out,), (grad_adapt_down, grad_adapt_up) = finish_terms(high_groups, high_terms)
    return (
        output.reshape(lanes, span, WIDTH),
        tokens_grad.reshape(lanes, span, WIDTH),
        encoder_grad.reshape(lanes, span, WIDTH),
        grad_self_in,
        grad_self_out,
        grad_cross_q,
        grad_cross_kv,
        grad_cross_out,
        grad_adapt_down,
        grad_adapt_up,
        jnp.stack([norms[0], norms[4], norms[2]]),
        jnp.stack([norms[1], norms[5], norms[3]]),
    )


def solution(mesh):
    placed = (
        P("dp", "blk", None),
        P("dp", "blk", None),
        P("dp", "blk", None),
        P("blk", None),
        P("blk", None),
        P("blk", None),
        P("blk", None),
        P("blk", None),
        P("blk", None),
        P("blk", None),
        P("blk", None),
        P("blk", None),
        P(),
        P(),
        P("dp", None),
        P("dp", None),
    )
    return jax.shard_map(
        shards,
        mesh=mesh,
        in_specs=placed,
        out_specs=(
            P("dp", "blk", None),
            P("dp", "blk", None),
            P("dp", "blk", None),
            P("blk", None),
            P("blk", None),
            P("blk", None),
            P("blk", None),
            P("blk", None),
            P("blk", None),
            P("blk", None),
            P(),
            P(),
        ),
        check_vma=False,
    )
```

```python
import functools
import math

import jax
import jax.numpy as jnp
from jax import lax
from jax.experimental import pallas as pl
from jax.experimental.pallas import tpu as pltpu
from jax.sharding import PartitionSpec as P

HEADS = 16
HEAD_DIM = 64
WIDTH = HEADS * HEAD_DIM


NEG = -1e30
VMEM_BYTES = 56 * 1024 * 1024


def cost(microseconds):
    return pl.CostEstimate(
        flops=int(microseconds * 0.4e9),
        bytes_accessed=int(microseconds * 1.2e6),
        transcendentals=0,
    )


def paired():
    return lax.axis_size("blk") == 16 and lax.axis_size("dp") == 2


def swap_core(block):
    cores = lax.axis_size("dp")
    return lax.ppermute(block, "dp", [(i ^ 1, i) for i in range(cores)])


def flip(block, bit):
    chips = lax.axis_size("blk")
    return lax.ppermute(block, "blk", [(i ^ bit, i) for i in range(chips)])


FLIPS = (8, 4, 2, 1)


def with_flip(block, bit):
    return jnp.stack([block, flip(block, bit)])


def own_half(values, which):
    half = values.shape[1] // 2
    return lax.dynamic_slice_in_dim(values, which * half, half, 1)


def scatter_chips(terms, orders, first, last, holds=None):
    if not paired():
        return terms, [terms] * 5
    own = lax.axis_index("blk")

    def fold(blocks, left, bit):
        axis, place = left.index(bit), (own // bit) % 2
        kept = lax.dynamic_index_in_dim(blocks, place, axis, keepdims=False)
        sent = lax.dynamic_index_in_dim(blocks, 1 - place, axis, keepdims=False)
        got = flip(sent, bit)
        return (kept.astype(jnp.float32) + got.astype(jnp.float32)).astype(jnp.bfloat16)

    if first == 0:
        terms = [blocks.reshape(2, 2, 2, 2, *blocks.shape[1:]) for blocks in terms]
    stages = [terms[0]]
    for stage in range(first, last):
        if holds and stage in holds:
            terms = after(terms, holds[stage])
        terms = [
            fold(blocks, [bit for bit in FLIPS if bit not in order[:stage]], order[stage])
            for blocks, order in zip(terms, orders)
        ]
        stages.append(terms[0])
    return terms, stages


CHUNK = 256


def grad_terms(pairs):
    if not paired():
        return pairs[0][1]
    core = lax.axis_index("dp")
    packed = []
    for inputs, upstream in pairs:
        both = jnp.concatenate([inputs, swap_core(inputs)], axis=0)
        half = jnp.concatenate(
            [own_half(upstream, core), swap_core(own_half(upstream, 1 - core))], axis=0
        )
        term = lax.dot_general(
            both, half, (((0,), (0,)), ((), ())), preferred_element_type=jnp.float32
        ).astype(jnp.bfloat16)
        rows = term.shape[0] // 16
        chunks = term.shape[1] // CHUNK
        packed += [
            term[:, c * CHUNK : (c + 1) * CHUNK].reshape(16, rows, CHUNK) for c in range(chunks)
        ]
    return jnp.concatenate(packed, axis=1)


def finish_terms(groups, terms):
    if not paired():
        return [[weight_grad(inputs, upstream) for inputs, upstream in pairs] for pairs in groups]
    core = lax.axis_index("dp")
    mine = jnp.concatenate(terms, axis=0)
    other = swap_core(mine)
    low = jnp.where(core == 0, mine, other).astype(jnp.float32)
    high = jnp.where(core == 0, other, mine).astype(jnp.float32)
    found, place = [], 0
    for pairs in groups:
        found.append([])
        for inputs, upstream in pairs:
            rows = inputs.shape[1] // 16
            chunks = upstream.shape[1] // 2 // CHUNK
            spots = [slice(place + c * rows, place + (c + 1) * rows) for c in range(chunks)]
            found[-1].append(
                jnp.concatenate(
                    [low[spot] for spot in spots] + [high[spot] for spot in spots], axis=1
                )
            )
            place += rows * chunks
    return found


def weight_grad(inputs, upstream):
    scattered = lax.psum_scatter(
        lax.dot_general(
            inputs, upstream, (((0,), (0,)), ((), ())), preferred_element_type=jnp.float32
        ).astype(jnp.bfloat16),
        "blk",
        scatter_dimension=0,
        tiled=True,
    )
    return lax.psum(scattered, "dp").astype(jnp.float32)


class Source:
    def __init__(self, kind, arrays, first_flip="x", column=None):
        self.kind, self.arrays, self.first_flip = kind, arrays, first_flip
        self.stages = arrays[:1] * 3 if column is None else [column] + arrays[:2]


class Part:
    def __init__(self, rows, width, spots):
        self.rows, self.width, self.spots = rows, width, spots

    def scratch(self):
        return pltpu.VMEM((2, 2, 2, 2, 2, self.rows // 32, self.width), jnp.bfloat16)

    def start(self, refs_of, place, dst, sem):
        z1, z0, y, x, core = [place[axis] for axis in range(5)]
        high = self.rows // 32
        for source, first_row, first_col, at_col, width in self.spots:
            refs = refs_of(source)
            cols = slice(first_col, first_col + width)
            into = slice(at_col, at_col + width)
            if source.kind == "whole":
                pltpu.make_async_copy(
                    refs[0].at[:, :, :, :, :, :, cols], dst.at[:, :, :, :, :, :, into], sem
                ).start()
            elif source.kind == "cores":
                for which in range(2):
                    owner = core if which == 0 else 1 - core
                    pltpu.make_async_copy(
                        refs[which].at[:, :, :, :, first_row : first_row + high, cols],
                        dst.at[:, :, :, :, owner, :, into],
                        sem,
                    ).start()
            else:
                for which in range(4):
                    owner = core if which < 2 else 1 - core
                    for near, at_y, at_x in flipped(source.first_flip, which % 2, y, x):
                        for up, at_z1, at_z0 in four(z1, z0):
                            pltpu.make_async_copy(
                                refs[which].at[near, up[0], up[1], :, cols],
                                dst.at[at_z1, at_z0, at_y, at_x, owner, :, into],
                                sem,
                            ).start()


def four(z1, z0):
    return [
        ((low, high), z1 if high == 0 else 1 - z1, z0 if low == 0 else 1 - z0)
        for low in range(2)
        for high in range(2)
    ]


def flipped(first_flip, beyond, y, x):
    found = []
    for near in range(2):
        a, b = (near, beyond) if first_flip == "x" else (beyond, near)
        found.append((near, y if b == 0 else 1 - y, x if a == 0 else 1 - x))
    return found


def after(value, *others):
    return lax.optimization_barrier((value, *others))[0]


def gather_flips(shards, first_flips, hold=None):
    if not paired():
        full = [lax.all_gather(shard, "blk", axis=0, tiled=True) for shard in shards]
        return [
            Source("whole", [array.reshape(2, 2, 2, 2, 2, array.shape[0] // 32, array.shape[1])])
            for array in full
        ]
    core = lax.axis_index("dp")
    columns = []
    for shard in shards:
        rows = shard.shape[0]
        own = lax.dynamic_slice_in_dim(shard, core * (rows // 2), rows // 2, 0)
        columns.append(with_flip(with_flip(own, 8), 4))
    sources, bits = [], {"x": (1, 2), "y": (2, 1)}
    if hold is not None:
        columns = after(columns, hold)
    planes = [
        with_flip(column, bits[first][0]) for column, first in zip(columns, first_flips)
    ]
    for column, plane, first in zip(columns, planes, first_flips):
        beyond = flip(plane, bits[first][1])
        sources.append(
            Source("flips", [plane, beyond, swap_core(plane), swap_core(beyond)], first, column)
        )
    return sources


class RowPart:
    def __init__(self, sources, span):
        self.span = span
        self.rows, self.width = 16 * span, WIDTH
        self.spots = [(source,) for source in sources]

    def scratch(self):
        return pltpu.VMEM((2, 2, 2, 2, self.span, WIDTH), jnp.bfloat16)

    def start(self, refs_of, place, dst, sem):
        z1, z0, y, x = [place[axis] for axis in range(4)]
        half = WIDTH // 2
        for side, (source,) in enumerate(self.spots):
            refs = refs_of(source)
            for beyond in range(2):
                for near, at_y, at_x in flipped(source.first_flip, beyond, y, x):
                    for up, at_z1, at_z0 in four(z1, z0):
                        pltpu.make_async_copy(
                            refs[beyond].at[near, up[0], up[1]],
                            dst.at[at_z1, at_z0, at_y, at_x, :, side * half : (side + 1) * half],
                            sem,
                        ).start()


def gather_row(block, hold_near=None, hold=None):
    row = lax.axis_index("blk") // 8
    own = lax.dynamic_index_in_dim(block, row, 0, keepdims=False)
    other = lax.dynamic_index_in_dim(block, 1 - row, 0, keepdims=False)
    pair = jnp.stack([own, flip(other, 8)])
    if hold_near is not None:
        pair = after(pair, hold_near)
    column = with_flip(pair, 4)
    stages, sources = [pair, column], []
    if hold is not None:
        column = after(column, hold)
    half = WIDTH // 2
    planes = [with_flip(column[..., :half], 1), with_flip(column[..., half:], 2)]
    for plane, first, bit in zip(planes, "xy", (2, 1)):
        sources.append(Source("row", [plane, flip(plane, bit)], first))
    stages += [planes, [source.arrays[1] for source in sources]]
    return RowPart(sources, block.shape[1]), stages


def head_columns(shards, kinds):
    core = lax.axis_index("dp")
    blocks, widths = [], [128 * kind for kind in kinds]
    for shard, kind in zip(shards, kinds):
        own = lax.dynamic_slice_in_dim(shard, core * 32, 32, 0)
        own = own.reshape(32, kind, 8, 128).transpose(2, 0, 1, 3)
        blocks.append(own.reshape(8, 32, kind * 128))
    blocks = jnp.concatenate(blocks, axis=2)
    mine = exchange(jnp.concatenate([blocks, blocks], axis=0))
    mine = mine.reshape(2, 2, 2, 2, 32, sum(widths))
    source = Source("cores", [mine, swap_core(mine)])
    parts, place = [], 0
    for width in widths:
        parts.append(Part(1024, width, [(source, 0, place, 0, width)]))
        place += width
    return parts


def project_row(row_part, head_part, name):
    def body(ins, loaded, outs, _):
        weight = loaded[1].value()
        inputs = loaded[0].value()
        for first in range(0, row_part.rows, 256):
            rows = slice(first, first + 256)
            outs[0][rows, :] = dot(inputs[rows], weight).astype(jnp.bfloat16)

    (found,) = call_with_parts(
        body,
        [],
        [row_part, head_part],
        [shape(row_part.rows, head_part.width, of=jnp.bfloat16)],
        name,
    )
    return found


def row_grad(row_part, upstream, name):
    columns = upstream.shape[1]

    def body(ins, loaded, outs, _):
        core = ins[1][0]
        inputs = loaded[0].value()
        grads = []
        for first in range(0, columns, 128):
            grads.append(pair_dot(ins[0][:, first : first + 128], inputs, 0, 0).T)
        grad = jnp.concatenate(grads, axis=1).astype(jnp.bfloat16).reshape(16, 2, 32, columns)
        outs[0][core] = grad[:, 0]
        outs[0][1 - core] = grad[:, 1]

    (terms,) = call_with_parts(
        body,
        [upstream],
        [row_part],
        [shape(2, 16, 32, columns, of=jnp.bfloat16)],
        name,
        scalars=[lax.axis_index("dp").reshape(1).astype(jnp.int32)],
    )
    got = swap_core(terms[1])
    return (terms[0].astype(jnp.float32) + got.astype(jnp.float32)).astype(jnp.bfloat16)


def row_back(upstream, head_part, name):
    def body(ins, loaded, outs, _):
        weight = loaded[0].value()
        for first in range(0, ins[0].shape[0], 256):
            rows = slice(first, first + 256)
            outs[0][rows, :] = dot_back(ins[0][rows, :], weight).astype(jnp.bfloat16)

    (terms,) = call_with_parts(
        body, [upstream], [head_part], [shape(upstream.shape[0], WIDTH, of=jnp.bfloat16)], name
    )
    return terms


def reduce_row(terms, holds=None):
    blocks = terms.reshape(16, terms.shape[0] // 16, WIDTH)
    (both,), stages = scatter_chips([blocks], [(1, 2, 4, 8)], 0, 3, holds)
    row = lax.axis_index("blk") // 8
    kept = lax.dynamic_index_in_dim(both, row, 0, keepdims=False)
    other = lax.dynamic_index_in_dim(both, 1 - row, 0, keepdims=False)
    got = flip(other, 8)
    found = jnp.stack([jnp.where(row == 0, kept, got), jnp.where(row == 0, got, kept)])
    return found.astype(jnp.float32), stages


def finish_row_grad(got, kinds):
    total = jnp.sum(got.reshape(2, 8, 32, kinds, 128).astype(jnp.float32), axis=0)
    mine = total.astype(jnp.bfloat16).transpose(1, 2, 0, 3).reshape(32, kinds * WIDTH)
    other = swap_core(mine)
    core = lax.axis_index("dp")
    low = jnp.where(core == 0, mine, other)
    high = jnp.where(core == 0, other, mine)
    return jnp.concatenate([low, high], axis=0).astype(jnp.float32)


def columns_of(*pieces):
    spots, place = [], 0
    for source, first, width in pieces:
        spots.append((source, 0, first, place, width))
        place += width
    return Part(1024, place, spots)


PACK = 512


def pack_halves(shards):
    places = [
        (index, shard.shape[0] // 2, first)
        for index, shard in enumerate(shards)
        for first in range(0, shard.shape[1], PACK)
    ]

    def body(core, *refs):
        out_ref, place = refs[-1], 0
        for index, high, first in places:
            start = pl.multiple_of(core[0] * high, 16)
            out_ref[place : place + high, :] = refs[index][pl.ds(start, high), first : first + PACK]
            place += high

    return pl.pallas_call(
        body,
        out_shape=shape(sum(high for _, high, _ in places), PACK, of=jnp.bfloat16),
        in_specs=[smem_spec()] + [vmem_spec()] * len(shards),
        out_specs=vmem_spec(),
        compiler_params=pltpu.CompilerParams(vmem_limit_bytes=VMEM_BYTES),
        cost_estimate=cost(2),
        name="pack_halves",
    )(lax.axis_index("dp").reshape(1).astype(jnp.int32), *shards)


def gather_packed(packed):
    return lax.all_gather(packed, "blk", axis=0)


def packed_parts(shards, mine):
    if not paired():
        found = []
        for source, shard in zip(gather_flips(shards, "x" * len(shards)), shards):
            rows, columns = 32 * source.arrays[0].shape[5], shard.shape[1]
            step = min(columns, 1024)
            found.append(
                [
                    Part(rows, step, [(source, 0, first, 0, step)])
                    for first in range(0, columns, step)
                ]
            )
        return found
    spots, place = [], 0
    for shard in shards:
        high = shard.shape[0] // 2
        places = []
        for first in range(0, shard.shape[1], PACK):
            places.append(place)
            place += high
        spots.append((shard.shape[0] * 16, places))
    mine = mine.reshape(2, 2, 2, 2, place, PACK)
    source = Source("cores", [mine, swap_core(mine)])
    found = []
    for rows, places in spots:
        parts = []
        for first in range(0, len(places), 2):
            two = places[first : first + 2]
            parts.append(
                Part(
                    rows,
                    PACK * len(two),
                    [(source, row, 0, PACK * side, PACK) for side, row in enumerate(two)],
                )
            )
        found.append(parts)
    return found


def place_now():
    own, core = lax.axis_index("blk"), lax.axis_index("dp")
    bits = [(own // bit) % 2 for bit in FLIPS]
    return jnp.stack(bits + [core]).astype(jnp.int32)


class Loaded:
    def __init__(self, part, dst, sem):
        self.part, self.dst, self.sem, self.here = part, dst, sem, False

    def value(self):
        if not self.here:
            pltpu.make_async_copy(self.dst, self.dst, self.sem).wait()
            self.here = True
        return self.dst[...].reshape(self.part.rows, self.part.width)


def call_with_parts(body, inputs, parts, outputs, name, scratch=(), takes=5, scalars=()):
    sources = []
    for part in parts:
        sources += [spot[0] for spot in part.spots if spot[0] not in sources]
    arrays = [array for source in sources for array in source.arrays]

    def kernel(place, *refs):
        refs = list(refs)
        ins = [refs.pop(0) for _ in (*inputs, *scalars)]
        pieces = [[refs.pop(0) for _ in source.arrays] for source in sources]
        outs = [refs.pop(0) for _ in outputs]
        dsts = [refs.pop(0) for _ in parts]
        sems = refs.pop(0)
        loaded = []
        for index, part in enumerate(parts):
            part.start(
                lambda source: pieces[sources.index(source)], place, dsts[index], sems.at[index]
            )
            loaded.append(Loaded(part, dsts[index], sems.at[index]))
        body(ins, loaded, outs, refs)

    return pl.pallas_call(
        kernel,
        out_shape=tuple(outputs),
        in_specs=[smem_spec()]
        + [vmem_spec()] * len(inputs)
        + [smem_spec()] * len(scalars)
        + [pl.BlockSpec(memory_space=pl.ANY)] * len(arrays),
        out_specs=(vmem_spec(),) * len(outputs),
        scratch_shapes=[part.scratch() for part in parts]
        + [pltpu.SemaphoreType.DMA((len(parts),))]
        + list(scratch),
        compiler_params=pltpu.CompilerParams(vmem_limit_bytes=VMEM_BYTES),
        cost_estimate=cost(takes),
        name=name,
    )(place_now(), *inputs, *scalars, *arrays)


def vmem_spec():
    return pl.BlockSpec(memory_space=pltpu.VMEM)


def smem_spec():
    return pl.BlockSpec(memory_space=pltpu.SMEM)


def seg_of_pos(ends_ref, pos):
    seg = jnp.zeros(pos.shape, jnp.int32)
    for slot in range(ends_ref.shape[0]):
        seg = seg + (ends_ref[slot] <= pos).astype(jnp.int32)
    return seg


def pair_dot(left, right, left_dim, right_dim):
    return lax.dot_general(
        left, right, (((left_dim,), (right_dim,)), ((), ())), preferred_element_type=jnp.float32
    )


def seg_tables(q_ends, k_ends, span):
    seg_q = seg_of_pos(q_ends, lax.broadcasted_iota(jnp.int32, (1, span), 1))
    seg_k = seg_of_pos(k_ends, lax.broadcasted_iota(jnp.int32, (span, 1), 0))
    return seg_q, seg_k


def masked_scores(keys, queries, seg_q, seg_k, first, causal):
    scores = pair_dot(keys, queries, 1, 1)
    allowed = seg_k == seg_q
    if causal:
        key_pos = lax.broadcasted_iota(jnp.int32, scores.shape, 0)
        query_pos = first + lax.broadcasted_iota(jnp.int32, scores.shape, 1)
        allowed = allowed & (key_pos <= query_pos)
    return jnp.where(allowed, scores, NEG)


def attn_forward_body(causal, width, q_ends, k_ends, q_ref, kv_ref, low_ref, full_ref, lse_ref):
    span = q_ref.shape[0]
    step = math.gcd(span, 256)
    heads = width // HEAD_DIM
    seg_q, seg_k = seg_tables(q_ends, k_ends, span)
    key_at = kv_ref.shape[1] - 2 * width
    scaled = q_ref[:, :width] * jnp.bfloat16(HEAD_DIM ** (-0.5))
    keys = kv_ref[:, key_at : key_at + width]
    values = kv_ref[:, key_at + width : key_at + 2 * width]
    for first in range(0, span, step):
        reach = first + step if causal else span
        parts = []
        for head in range(heads):
            cols = slice(head * HEAD_DIM, (head + 1) * HEAD_DIM)
            scores = masked_scores(
                keys[:reach, cols],
                scaled[first : first + step, cols],
                seg_q[:, first : first + step],
                seg_k[:reach],
                first,
                causal,
            )
            top = jnp.max(scores, axis=0, keepdims=True)
            probs = jnp.exp(scores - top)
            total = jnp.sum(probs, axis=0, keepdims=True)
            mixed = pair_dot(values[:reach, cols], probs.astype(jnp.bfloat16), 0, 0)
            parts.append(mixed / total)
            lse_ref[head : head + 1, first : first + step] = top + jnp.log(total)
        joined = jnp.concatenate(parts, axis=0).T
        full_ref[first : first + step, :] = joined
        low_ref[first : first + step, :] = joined.astype(jnp.bfloat16)


def attn_forward(q_ends, k_ends, queries, keys_values, width, causal):
    span = queries.shape[0]
    return pl.pallas_call(
        functools.partial(attn_forward_body, causal, width),
        out_shape=(
            jax.ShapeDtypeStruct((span, width), jnp.bfloat16),
            jax.ShapeDtypeStruct((span, width), jnp.float32),
            jax.ShapeDtypeStruct((width // HEAD_DIM, span), jnp.float32),
        ),
        in_specs=[smem_spec(), smem_spec()] + [vmem_spec()] * 2,
        out_specs=(vmem_spec(),) * 3,
        compiler_params=pltpu.CompilerParams(vmem_limit_bytes=VMEM_BYTES),
        cost_estimate=cost(8),
        name="attn_forward",
    )(q_ends, k_ends, queries, keys_values)


def attn_backward_body(
    causal,
    width,
    q_ends,
    k_ends,
    q_ref,
    kv_ref,
    up_ref,
    full_ref,
    lse_ref,
    *outs,
):
    dq_ref, dkv_ref = outs[0], outs[-3]
    dk_sum, dv_sum = outs[-2:]
    span = q_ref.shape[0]
    step = math.gcd(span, 256)
    heads = width // HEAD_DIM
    seg_q, seg_k = seg_tables(q_ends, k_ends, span)
    key_at = kv_ref.shape[1] - 2 * width
    scaled = q_ref[:, :width] * jnp.bfloat16(HEAD_DIM ** (-0.5))
    keys = kv_ref[:, key_at : key_at + width]
    values = kv_ref[:, key_at + width : key_at + 2 * width]
    upstream = up_ref[...]
    dk_sum[...] = jnp.zeros_like(dk_sum)
    dv_sum[...] = jnp.zeros_like(dv_sum)
    for first in range(0, span, step):
        reach = first + step if causal else span
        rows = slice(first, first + step)
        product = (upstream[rows].astype(jnp.float32) * full_ref[rows, :]).T
        parts = []
        for head in range(heads):
            cols = slice(head * HEAD_DIM, (head + 1) * HEAD_DIM)
            delta = jnp.sum(product[cols], axis=0, keepdims=True)
            scores = masked_scores(
                keys[:reach, cols], scaled[rows, cols], seg_q[:, rows], seg_k[:reach], first, causal
            )
            probs = jnp.exp(scores - lse_ref[head : head + 1, rows])
            dv_sum[head, :reach] += pair_dot(
                probs.astype(jnp.bfloat16), upstream[rows, cols], 1, 0
            )
            grad_probs = pair_dot(values[:reach, cols], upstream[rows, cols], 1, 1)
            grad_scores = (probs * (grad_probs - delta)).astype(jnp.bfloat16)
            dk_sum[head, :reach] += pair_dot(grad_scores, scaled[rows, cols], 1, 0)
            parts.append(pair_dot(keys[:reach, cols], grad_scores, 0, 0))
        joined = jnp.concatenate(parts, axis=0).T * HEAD_DIM ** (-0.5)
        dq_ref[rows, :width] = joined.astype(jnp.bfloat16)
    sums = [dk_sum[head] for head in range(heads)] + [dv_sum[head] for head in range(heads)]
    kv_at = dkv_ref.shape[1] - 2 * width
    dkv_ref[:, kv_at:] = jnp.concatenate(sums, axis=1).astype(jnp.bfloat16)


def attn_backward(
    q_ends, k_ends, queries, keys_values, upstream, full, lse, causal, joined=False
):
    span, width = upstream.shape
    kinds = [3] if joined else [1, 2]
    heads = width // HEAD_DIM
    return pl.pallas_call(
        functools.partial(attn_backward_body, causal, width),
        out_shape=[jax.ShapeDtypeStruct((span, kind * width), jnp.bfloat16) for kind in kinds],
        in_specs=[smem_spec(), smem_spec()] + [vmem_spec()] * 5,
        out_specs=[vmem_spec()] * len(kinds),
        scratch_shapes=[pltpu.VMEM((heads, span, HEAD_DIM), jnp.float32)] * 2,
        compiler_params=pltpu.CompilerParams(vmem_limit_bytes=VMEM_BYTES),
        cost_estimate=cost(8),
        name="attn_backward",
    )(q_ends, k_ends, queries, keys_values, upstream, full, lse)


def exchange(blocks):
    return lax.all_to_all(blocks, "blk", 0, 0, tiled=True)


def as_rows(blocks):
    return blocks.reshape(blocks.shape[0] * blocks.shape[1], blocks.shape[2])


def as_blocks(rows):
    devices = lax.axis_size("blk")
    return rows.reshape(devices, rows.shape[0] // devices, rows.shape[1])


def write_blocks(out_ref, values, lanes, kind, width):
    span = values.shape[0] // lanes
    for group in range(WIDTH // width):
        for lane in range(lanes):
            out_ref[lane * (WIDTH // width) + group, :, kind * width : (kind + 1) * width] = values[
                lane * span : (lane + 1) * span, group * width : (group + 1) * width
            ]


def read_blocks(got_ref, lanes, kind, width):
    groups = got_ref.shape[0] // lanes
    cols = slice(kind * width, (kind + 1) * width)
    rows = [
        jnp.concatenate([got_ref[lane * groups + group, :, cols] for group in range(groups)], axis=1)
        for lane in range(lanes)
    ]
    return jnp.concatenate(rows, axis=0)


def dot(left, right):
    return pair_dot(left, right, 1, 0)


def dot_back(left, right):
    return pair_dot(left, right, 1, 1)


def shape(*sizes, of=jnp.float32):
    return jax.ShapeDtypeStruct(sizes, of)


def normalize(values):
    center = values - jnp.mean(values, -1, keepdims=True)
    scale = lax.rsqrt(jnp.mean(center * center, -1, keepdims=True) + 1e-05)
    return center * scale, scale


def norm_back(upstream, normed, scale, gains_row):
    grad = upstream * gains_row
    return scale * (
        grad
        - jnp.mean(grad, -1, keepdims=True)
        - normed * jnp.mean(grad * normed, -1, keepdims=True)
    )


def project_blocks(inputs, parts, lanes, width, name):
    def body(ins, loaded, outs, _):
        for kind, weight in enumerate(loaded):
            write_blocks(
                outs[0], dot(ins[0][...], weight.value()).astype(jnp.bfloat16), lanes, kind, width
            )

    devices, span = lax.axis_size("blk"), inputs.shape[0] // lanes
    (blocks,) = call_with_parts(
        body,
        [inputs],
        parts,
        [shape(devices, span, width * len(parts), of=jnp.bfloat16)],
        name,
    )
    return blocks


def after_self(got, tokens, gains, biases, out_part, query_part, lanes, width):
    def body(ins, loaded, outs, _):
        got_ref, tokens_ref, gains_ref, biases_ref = ins
        low_ref, normed_ref, scale_ref, hidden_ref, blocks_ref = outs
        attended = read_blocks(got_ref, lanes, 0, width)
        low_ref[...] = attended
        resid = tokens_ref[...].astype(jnp.float32) + dot(attended, loaded[0].value())
        normed, scale = normalize(resid)
        normed_ref[...] = normed
        scale_ref[...] = scale
        hidden = (normed * gains_ref[0:1] + biases_ref[0:1]).astype(jnp.bfloat16)
        hidden_ref[...] = hidden
        query = dot(hidden, loaded[1].value()).astype(jnp.bfloat16)
        write_blocks(blocks_ref, query, lanes, 0, width)

    rows = tokens.shape[0]
    return call_with_parts(
        body,
        [got, tokens, gains, biases],
        [out_part, query_part],
        [
            shape(rows, WIDTH, of=jnp.bfloat16),
            shape(rows, WIDTH),
            shape(rows, 1),
            shape(rows, WIDTH, of=jnp.bfloat16),
            shape(*got.shape, of=jnp.bfloat16),
        ],
        "after_self",
    )


def feed_forward(got, normed_in, cotangent, gains, biases, out_part, in_parts, down, outs, up, lanes, width):
    pieces = len(in_parts)
    step = in_parts[0].width

    def body(ins, loaded, refs, scratch):
        got_ref, normed_in_ref, cot_ref, gains_ref, biases_ref = ins
        (
            output_ref,
            low_ref,
            mixed_ref,
            adapted_ref,
            dunder_ref,
            dab_ref,
            dcb_ref,
            dresid_ref,
            blocks_ref,
            norms_ref,
        ) = refs
        slopes, acts = scratch
        w_out, w_down, w_in = loaded[0], loaded[1], loaded[2 : 2 + pieces]
        w_ff, w_up = loaded[2 + pieces :]
        attended = read_blocks(got_ref, lanes, 0, width)
        low_ref[...] = attended
        hidden = normed_in_ref[...] * gains_ref[0:1] + biases_ref[0:1]
        normed_one, scale_one = normalize(hidden + dot(attended, w_out.value()))
        mixed = normed_one * gains_ref[1:2] + biases_ref[1:2]
        mixed_low = mixed.astype(jnp.bfloat16)
        mixed_ref[...] = mixed_low
        summed = mixed
        under = dot(mixed_low, w_down.value())
        gate = 1.0 / (1.0 + jnp.exp(-under))
        adapted = (under * gate).astype(jnp.bfloat16)
        adapted_ref[...] = adapted
        under_slope = gate * (1.0 + under * (1.0 - gate))
        for piece in range(pieces):
            before = dot(mixed_low, w_in[piece].value())
            below = 0.5 + 0.5 * lax.erf(before * (0.5**0.5))
            slopes[piece] = below + before * jnp.exp(-0.5 * before * before) * (
                (2.0 * math.pi) ** -0.5
            )
            acts[piece] = (before * below).astype(jnp.bfloat16)
        for piece in range(pieces):
            summed = summed + dot(acts[piece], w_ff[piece].value())
        summed = summed + 4.0 * dot(adapted, w_up.value())
        normed_two, scale_two = normalize(summed)
        output_ref[...] = (normed_two * gains_ref[2:3] + biases_ref[2:3]).astype(jnp.bfloat16)
        upstream = cot_ref[...].astype(jnp.float32)
        norms_ref[0:1] = jnp.sum(upstream * normed_two, axis=0, keepdims=True)
        norms_ref[1:2] = jnp.sum(upstream, axis=0, keepdims=True)
        dz = norm_back(upstream, normed_two, scale_two, gains_ref[2:3])
        dzb = dz.astype(jnp.bfloat16)
        dab = (4.0 * dz).astype(jnp.bfloat16)
        dab_ref[...] = dab
        dunder = (under_slope * dot_back(dab, w_up.value())).astype(jnp.bfloat16)
        dunder_ref[...] = dunder
        dmixed = dz + dot_back(dunder, w_down.value())
        for piece in range(pieces):
            dpre = (slopes[piece] * dot_back(dzb, w_ff[piece].value())).astype(jnp.bfloat16)
            dmixed = dmixed + dot_back(dpre, w_in[piece].value())
        norms_ref[2:3] = jnp.sum(dmixed * normed_one, axis=0, keepdims=True)
        norms_ref[3:4] = jnp.sum(dmixed, axis=0, keepdims=True)
        dresid = norm_back(dmixed, normed_one, scale_one, gains_ref[1:2])
        dresid_ref[...] = dresid
        dcb = dresid.astype(jnp.bfloat16)
        dcb_ref[...] = dcb
        write_blocks(
            blocks_ref, dot_back(dcb, w_out.value()).astype(jnp.bfloat16), lanes, 0, width
        )

    rows = normed_in.shape[0]
    low = jnp.bfloat16

    def body_rows(ins, loaded, refs, scratch):
        whole_ff = loaded[2 + pieces]

        class Rows:
            def __init__(self, piece):
                self.piece = piece

            def value(self):
                return whole_ff.value()[self.piece * step : (self.piece + 1) * step]

        loaded = loaded[: 2 + pieces] + [[Rows(piece) for piece in range(pieces)], loaded[-1]]
        body(ins, loaded, refs, scratch)

    return call_with_parts(
        body_rows,
        [got, normed_in, cotangent, gains, biases],
        [out_part, down] + in_parts + [outs, up],
        [
            shape(rows, WIDTH, of=low),
            shape(rows, WIDTH, of=low),
            shape(rows, WIDTH, of=low),
            shape(rows, down.width, of=low),
            shape(rows, down.width, of=low),
            shape(rows, WIDTH, of=low),
            shape(rows, WIDTH, of=low),
            shape(rows, WIDTH),
            shape(*got.shape, of=low),
            shape(4, WIDTH),
        ],
        "feed_forward",
        [
            pltpu.VMEM((pieces, rows, step), jnp.float32),
            pltpu.VMEM((pieces, rows, step), jnp.bfloat16),
        ],
        20,
    )


def before_self(got, dresid, normed, scale, gains, query_part, out_part, lanes, width):
    def body(ins, loaded, outs, _):
        got_ref, dresid_ref, normed_ref, scale_ref, gains_ref = ins
        dcq_ref, dr_ref, dsb_ref, blocks_ref, norms_ref = outs
        dcq = read_blocks(got_ref, lanes, 0, width)
        dcq_ref[...] = dcq
        dhidden = dresid_ref[...] + dot_back(dcq, loaded[0].value())
        normed = normed_ref[...]
        norms_ref[0:1] = jnp.sum(dhidden * normed, axis=0, keepdims=True)
        norms_ref[1:2] = jnp.sum(dhidden, axis=0, keepdims=True)
        dr = norm_back(dhidden, normed, scale_ref[...], gains_ref[0:1])
        dr_ref[...] = dr
        dsb = dr.astype(jnp.bfloat16)
        dsb_ref[...] = dsb
        grad = dot_back(dsb, loaded[1].value()).astype(jnp.bfloat16)
        write_blocks(blocks_ref, grad, lanes, 0, width)

    rows = dresid.shape[0]
    return call_with_parts(
        body,
        [got, dresid, normed, scale, gains],
        [query_part, out_part],
        [
            shape(rows, WIDTH, of=jnp.bfloat16),
            shape(rows, WIDTH),
            shape(rows, WIDTH, of=jnp.bfloat16),
            shape(*got.shape, of=jnp.bfloat16),
            shape(2, WIDTH),
        ],
        "before_self",
    )


def input_grad(got, start, parts, lanes, span, width, name):
    def body(ins, loaded, outs, _):
        total = None
        for kind, weight in enumerate(loaded):
            values = read_blocks(ins[0], lanes, kind, width)
            term = dot_back(values, weight.value())
            total = term if total is None else total + term
        outs[0][...] = total if len(ins) == 1 else total + ins[1][...]

    rows = span * lanes
    return call_with_parts(
        body,
        [got] if start is None else [got, start],
        parts,
        [shape(rows, WIDTH)],
        name,
    )


def shards(
    tokens,
    encoder,
    cotangent,
    self_in,
    self_out,
    cross_q,
    cross_kv,
    cross_out,
    ffn_in,
    ffn_out,
    adapt_down,
    adapt_up,
    norm_gain,
    norm_bias,
    tgt_lengths,
    src_lengths,
):
    lanes, span, _ = tokens.shape
    rows = lanes * span
    width = WIDTH * lanes // lax.axis_size("blk")
    own_row = lax.axis_index("blk") // (lax.axis_size("blk") // lanes)
    tgt_ends = jnp.cumsum(lax.dynamic_index_in_dim(tgt_lengths, own_row, 0, keepdims=False))
    src_ends = jnp.cumsum(lax.dynamic_index_in_dim(src_lengths, own_row, 0, keepdims=False))
    flat_tokens = tokens.reshape(rows, WIDTH)
    flat_encoder = encoder.reshape(rows, WIDTH)
    frozen = [ffn_in, adapt_down, ffn_out, adapt_up, cross_out]

    if paired():
        packed = gather_packed(pack_halves(frozen))
        self_packed = pack_halves([self_in])
        token_row, stages = gather_row(tokens)
        self_heads, pair_heads = head_columns([self_in, cross_kv], [3, 2])
        out_shard, query_shard = after((self_out, cross_q), stages[1])
        encoder_block = after(encoder, stages[1])
        self_qkv = project_row(token_row, self_heads, "self_in")
        out_source, query_source = gather_flips([out_shard, query_shard], "xy", self_qkv)
        encoder_row, encoder_stages = gather_row(
            encoder_block, self_qkv, (out_source.arrays[1], query_source.arrays[1])
        )
        self_qkv = after(self_qkv, out_source.stages[0], query_source.stages[0])
        pair_own = project_row(encoder_row, pair_heads, "cross_kv")
    else:
        (self_source, pair_source, out_source, query_source) = gather_flips(
            [self_in, cross_kv, self_out, cross_q], "xyxy"
        )
        self_parts = [columns_of((self_source, WIDTH * kind, WIDTH)) for kind in range(3)]
        pair_parts = [columns_of((pair_source, WIDTH * kind, WIDTH)) for kind in range(2)]
        self_qkv = as_rows(
            exchange(project_blocks(flat_tokens, self_parts, lanes, width, "self_in"))
        )
        pair_own = as_rows(
            exchange(project_blocks(flat_encoder, pair_parts, lanes, width, "cross_kv"))
        )
    self_out_part = columns_of((out_source, 0, WIDTH))
    query_part = columns_of((query_source, 0, WIDTH))

    self_mid, self_full, self_lse = attn_forward(
        tgt_ends, tgt_ends, self_qkv, self_qkv, width, True
    )
    self_sent = after(self_mid, out_source.stages[1], query_source.stages[1])
    if paired():
        self_sent = after(self_sent, encoder_stages[0])
    self_back = exchange(as_blocks(self_sent))
    if paired():
        self_back = after(self_back, encoder_stages[1])
    self_low, normed, scale, hidden_low, query_blocks = after_self(
        self_back,
        flat_tokens,
        norm_gain,
        norm_bias,
        self_out_part,
        query_part,
        lanes,
        width,
    )
    cross_own = as_rows(exchange(query_blocks))
    cross_mid, cross_full, cross_lse = attn_forward(
        tgt_ends, src_ends, cross_own, pair_own, width, False
    )
    cross_back = exchange(as_blocks(cross_mid))
    ready = after(packed, cross_mid) if paired() else None
    ff_parts, down_parts, ffo_parts, up_parts, (cross_out_part,) = packed_parts(frozen, ready)
    if paired():
        self_packed = gather_packed(after(self_packed, cross_back))
    (
        output,
        cross_low,
        mixed_low,
        adapter_low,
        grad_under,
        adapt_low,
        cross_branch_low,
        grad_resid_two,
        cross_grad_blocks,
        norms_high,
    ) = feed_forward(
        cross_back,
        normed,
        cotangent.reshape(rows, WIDTH),
        norm_gain,
        norm_bias,
        cross_out_part,
        ff_parts,
        down_parts[0],
        ffo_parts[0],
        up_parts[0],
        lanes,
        width,
    )
    high_groups = [
        [(cross_low, cross_branch_low)],
        [(mixed_low, grad_under), (adapter_low, adapt_low)],
    ]
    high_terms = [grad_terms(pairs) for pairs in high_groups]
    high_orders = [(2, 1, 4, 8), (1, 2, 4, 8)]
    high_terms, high_stages = scatter_chips(high_terms, high_orders, 0, 2)
    cross_dq, cross_dkv = attn_backward(
        tgt_ends,
        src_ends,
        cross_own,
        pair_own,
        as_rows(after(exchange(cross_grad_blocks), high_stages[0])),
        cross_full,
        cross_lse,
        False,
    )
    cross_dq_got = after(exchange(as_blocks(cross_dq)), high_stages[1])
    if paired():
        dkv_late = after(cross_dkv, high_stages[1])
        pair_terms = row_back(dkv_late, pair_heads, "encoder_grad")
        kv_sent = row_grad(encoder_row, dkv_late, "cross_kv_grad")
        cross_dq_got = after(cross_dq_got, pair_terms, kv_sent)
    cq_low, grad_resid_one, self_branch_low, self_grad_blocks, norms_low = before_self(
        cross_dq_got,
        grad_resid_two,
        normed,
        scale,
        norm_gain,
        query_part,
        self_out_part,
        lanes,
        width,
    )
    norms = jnp.concatenate([norms_low, norms_high], axis=0)
    mid_pairs = [(hidden_low, cq_low), (self_low, self_branch_low)]
    mid_orders = [(2, 1, 4, 8), (1, 2, 4, 8)]
    mid_terms = [grad_terms([pair]) for pair in mid_pairs]
    mid_terms, _ = scatter_chips(mid_terms, mid_orders, 0, 1)
    if paired():
        high_terms = [jnp.concatenate(after(high_terms, self_grad_blocks), axis=2)]
        high_terms, _ = scatter_chips(high_terms, [(2, 1, 4, 8)], 2, 3)
    self_upstream = after(exchange(self_grad_blocks), high_stages[2])
    (self_grads,) = attn_backward(
        tgt_ends,
        tgt_ends,
        self_qkv,
        self_qkv,
        as_rows(self_upstream),
        self_full,
        self_lse,
        True,
        joined=True,
    )
    if paired():
        (self_parts,) = packed_parts([self_in], after(self_packed, self_grads))
        self_got = exchange(as_blocks(self_grads))
        high_terms, _ = scatter_chips(after(high_terms, self_grads), [(2, 1, 4, 8)], 3, 4)
        self_sent = row_grad(token_row, after(self_grads, high_terms[0]), "self_in_grad")
        mid_terms, _ = scatter_chips(after(mid_terms, self_grads), mid_orders, 1, 2)
        mid_terms = [jnp.concatenate(mid_terms, axis=2)]
        chunks = [
            array[:, :, first : first + width]
            for array in (self_sent, kv_sent)
            for first in range(0, array.shape[2], width)
        ]
        partials = norms.astype(jnp.bfloat16).reshape(1, 48, width)
        chunks.append(jnp.broadcast_to(partials, (16, 48, width)))
        (tokens_grad,) = input_grad(
            self_got, grad_resid_one, self_parts, lanes, span, width, "tokens_grad"
        )
        encoder_grad, stages = reduce_row(pair_terms, {2: tokens_grad})
        encoder_grad = encoder_grad.reshape(rows, WIDTH)
        sent = jnp.concatenate(chunks, axis=1)
        got = exchange(after(sent, self_got, stages[2], mid_terms))
        mid_terms, _ = scatter_chips(
            mid_terms, mid_orders[:1], 2, 4, {2: tokens_grad}
        )
        got = after(got, tokens_grad)
        chunks = [got[:, first : first + 32] for first in range(0, 160, 32)]
        grad_self_in = finish_row_grad(jnp.concatenate(chunks[:3], axis=2), 3)
        grad_cross_kv = finish_row_grad(jnp.concatenate(chunks[3:], axis=2), 2)
        norms = jnp.sum(got[:, 160:].astype(jnp.float32), axis=0).reshape(6, WIDTH)
        norms = norms + swap_core(norms)
    else:
        pair_got = exchange(as_blocks(cross_dkv))
        self_got = exchange(as_blocks(self_grads))
        (encoder_grad,) = input_grad(
            pair_got, None, pair_parts, lanes, span, width, "encoder_grad"
        )
        (tokens_grad,) = input_grad(
            self_got, grad_resid_one, self_parts, lanes, span, width, "tokens_grad"
        )
        pair_low = pair_got.reshape(lanes, -1, span, 2, width).transpose(0, 2, 3, 1, 4)
        self_low_grads = self_got.reshape(lanes, -1, span, 3, width).transpose(0, 2, 3, 1, 4)
        grad_cross_kv = weight_grad(flat_encoder, pair_low.reshape(rows, 2 * WIDTH))
        grad_self_in = weight_grad(flat_tokens, self_low_grads.reshape(rows, 3 * WIDTH))
        norms = lax.psum(norms, ("dp", "blk"))
    ((grad_cross_q, grad_self_out),) = finish_terms([mid_pairs], mid_terms)
    (grad_cross_out,), (grad_adapt_down, grad_adapt_up) = finish_terms(high_groups, high_terms)
    return (
        output.reshape(lanes, span, WIDTH),
        tokens_grad.reshape(lanes, span, WIDTH),
        encoder_grad.reshape(lanes, span, WIDTH),
        grad_self_in,
        grad_self_out,
        grad_cross_q,
        grad_cross_kv,
        grad_cross_out,
        grad_adapt_down,
        grad_adapt_up,
        jnp.stack([norms[0], norms[4], norms[2]]),
        jnp.stack([norms[1], norms[5], norms[3]]),
    )


def solution(mesh):
    placed = (
        P("dp", "blk", None),
        P("dp", "blk", None),
        P("dp", "blk", None),
        P("blk", None),
        P("blk", None),
        P("blk", None),
        P("blk", None),
        P("blk", None),
        P("blk", None),
        P("blk", None),
        P("blk", None),
        P("blk", None),
        P(),
        P(),
        P("dp", None),
        P("dp", None),
    )
    return jax.shard_map(
        shards,
        mesh=mesh,
        in_specs=placed,
        out_specs=(
            P("dp", "blk", None),
            P("dp", "blk", None),
            P("dp", "blk", None),
            P("blk", None),
            P("blk", None),
            P("blk", None),
            P("blk", None),
            P("blk", None),
            P("blk", None),
            P("blk", None),
            P(),
            P(),
        ),
        check_vma=False,
    )
```

```python
import functools
import math

import jax
import jax.numpy as jnp
from jax import lax
from jax.experimental import pallas as pl
from jax.experimental.pallas import tpu as pltpu
from jax.sharding import PartitionSpec as P

HEADS = 16
HEAD_DIM = 64
WIDTH = HEADS * HEAD_DIM


NEG = -1e30
VMEM_BYTES = 56 * 1024 * 1024


def cost(microseconds):
    return pl.CostEstimate(
        flops=int(microseconds * 0.4e9),
        bytes_accessed=int(microseconds * 1.2e6),
        transcendentals=0,
    )


def paired():
    return lax.axis_size("blk") == 16 and lax.axis_size("dp") == 2


def swap_core(block):
    cores = lax.axis_size("dp")
    return lax.ppermute(block, "dp", [(i ^ 1, i) for i in range(cores)])


def flip(block, bit):
    chips = lax.axis_size("blk")
    return lax.ppermute(block, "blk", [(i ^ bit, i) for i in range(chips)])


FLIPS = (8, 4, 2, 1)


def with_flip(block, bit):
    return jnp.stack([block, flip(block, bit)])


def own_half(values, which):
    half = values.shape[1] // 2
    return lax.dynamic_slice_in_dim(values, which * half, half, 1)


def scatter_chips(terms, orders, first, last, holds=None):
    if not paired():
        return terms, [terms] * 5
    own = lax.axis_index("blk")

    def fold(blocks, left, bit):
        axis, place = left.index(bit), (own // bit) % 2
        kept = lax.dynamic_index_in_dim(blocks, place, axis, keepdims=False)
        sent = lax.dynamic_index_in_dim(blocks, 1 - place, axis, keepdims=False)
        got = flip(sent, bit)
        return (kept.astype(jnp.float32) + got.astype(jnp.float32)).astype(jnp.bfloat16)

    if first == 0:
        terms = [blocks.reshape(2, 2, 2, 2, *blocks.shape[1:]) for blocks in terms]
    stages = [terms[0]]
    for stage in range(first, last):
        if holds and stage in holds:
            terms = after(terms, holds[stage])
        terms = [
            fold(blocks, [bit for bit in FLIPS if bit not in order[:stage]], order[stage])
            for blocks, order in zip(terms, orders)
        ]
        stages.append(terms[0])
    return terms, stages


CHUNK = 256


def grad_terms(pairs):
    if not paired():
        return pairs[0][1]
    core = lax.axis_index("dp")
    packed = []
    for inputs, upstream in pairs:
        both = jnp.concatenate([inputs, swap_core(inputs)], axis=0)
        half = jnp.concatenate(
            [own_half(upstream, core), swap_core(own_half(upstream, 1 - core))], axis=0
        )
        term = lax.dot_general(
            both, half, (((0,), (0,)), ((), ())), preferred_element_type=jnp.float32
        ).astype(jnp.bfloat16)
        rows = term.shape[0] // 16
        chunks = term.shape[1] // CHUNK
        packed += [
            term[:, c * CHUNK : (c + 1) * CHUNK].reshape(16, rows, CHUNK) for c in range(chunks)
        ]
    return jnp.concatenate(packed, axis=1)


def finish_terms(groups, terms):
    if not paired():
        return [[weight_grad(inputs, upstream) for inputs, upstream in pairs] for pairs in groups]
    core = lax.axis_index("dp")
    mine = jnp.concatenate(terms, axis=0)
    other = swap_core(mine)
    low = jnp.where(core == 0, mine, other).astype(jnp.float32)
    high = jnp.where(core == 0, other, mine).astype(jnp.float32)
    found, place = [], 0
    for pairs in groups:
        found.append([])
        for inputs, upstream in pairs:
            rows = inputs.shape[1] // 16
            chunks = upstream.shape[1] // 2 // CHUNK
            spots = [slice(place + c * rows, place + (c + 1) * rows) for c in range(chunks)]
            found[-1].append(
                jnp.concatenate(
                    [low[spot] for spot in spots] + [high[spot] for spot in spots], axis=1
                )
            )
            place += rows * chunks
    return found


def weight_grad(inputs, upstream):
    scattered = lax.psum_scatter(
        lax.dot_general(
            inputs, upstream, (((0,), (0,)), ((), ())), preferred_element_type=jnp.float32
        ).astype(jnp.bfloat16),
        "blk",
        scatter_dimension=0,
        tiled=True,
    )
    return lax.psum(scattered, "dp").astype(jnp.float32)


class Source:
    def __init__(self, kind, arrays, first_flip="x", column=None):
        self.kind, self.arrays, self.first_flip = kind, arrays, first_flip
        self.stages = arrays[:1] * 3 if column is None else [column] + arrays[:2]


class Part:
    def __init__(self, rows, width, spots):
        self.rows, self.width, self.spots = rows, width, spots

    def scratch(self):
        return pltpu.VMEM((2, 2, 2, 2, 2, self.rows // 32, self.width), jnp.bfloat16)

    def start(self, refs_of, place, dst, sem):
        z1, z0, y, x, core = [place[axis] for axis in range(5)]
        high = self.rows // 32
        for source, first_row, first_col, at_col, width in self.spots:
            refs = refs_of(source)
            cols = slice(first_col, first_col + width)
            into = slice(at_col, at_col + width)
            if source.kind == "whole":
                pltpu.make_async_copy(
                    refs[0].at[:, :, :, :, :, :, cols], dst.at[:, :, :, :, :, :, into], sem
                ).start()
            elif source.kind == "cores":
                for which in range(2):
                    owner = core if which == 0 else 1 - core
                    pltpu.make_async_copy(
                        refs[which].at[:, :, :, :, first_row : first_row + high, cols],
                        dst.at[:, :, :, :, owner, :, into],
                        sem,
                    ).start()
            else:
                for which in range(4):
                    owner = core if which < 2 else 1 - core
                    for near, at_y, at_x in flipped(source.first_flip, which % 2, y, x):
                        for up, at_z1, at_z0 in four(z1, z0):
                            pltpu.make_async_copy(
                                refs[which].at[near, up[0], up[1], :, cols],
                                dst.at[at_z1, at_z0, at_y, at_x, owner, :, into],
                                sem,
                            ).start()


def four(z1, z0):
    return [
        ((low, high), z1 if high == 0 else 1 - z1, z0 if low == 0 else 1 - z0)
        for low in range(2)
        for high in range(2)
    ]


def flipped(first_flip, beyond, y, x):
    found = []
    for near in range(2):
        a, b = (near, beyond) if first_flip == "x" else (beyond, near)
        found.append((near, y if b == 0 else 1 - y, x if a == 0 else 1 - x))
    return found


def after(value, *others):
    return lax.optimization_barrier((value, *others))[0]


def gather_flips(shards, first_flips, hold=None):
    if not paired():
        full = [lax.all_gather(shard, "blk", axis=0, tiled=True) for shard in shards]
        return [
            Source("whole", [array.reshape(2, 2, 2, 2, 2, array.shape[0] // 32, array.shape[1])])
            for array in full
        ]
    core = lax.axis_index("dp")
    columns = []
    for shard in shards:
        rows = shard.shape[0]
        own = lax.dynamic_slice_in_dim(shard, core * (rows // 2), rows // 2, 0)
        columns.append(with_flip(with_flip(own, 8), 4))
    sources, bits = [], {"x": (1, 2), "y": (2, 1)}
    if hold is not None:
        columns = after(columns, hold)
    planes = [
        with_flip(column, bits[first][0]) for column, first in zip(columns, first_flips)
    ]
    for column, plane, first in zip(columns, planes, first_flips):
        beyond = flip(plane, bits[first][1])
        sources.append(
            Source("flips", [plane, beyond, swap_core(plane), swap_core(beyond)], first, column)
        )
    return sources


class RowPart:
    def __init__(self, sources, span):
        self.span = span
        self.rows, self.width = 16 * span, WIDTH
        self.spots = [(source,) for source in sources]

    def scratch(self):
        return pltpu.VMEM((2, 2, 2, 2, self.span, WIDTH), jnp.bfloat16)

    def start(self, refs_of, place, dst, sem):
        z1, z0, y, x = [place[axis] for axis in range(4)]
        half = WIDTH // 2
        for side, (source,) in enumerate(self.spots):
            refs = refs_of(source)
            for beyond in range(2):
                for near, at_y, at_x in flipped(source.first_flip, beyond, y, x):
                    for up, at_z1, at_z0 in four(z1, z0):
                        pltpu.make_async_copy(
                            refs[beyond].at[near, up[0], up[1]],
                            dst.at[at_z1, at_z0, at_y, at_x, :, side * half : (side + 1) * half],
                            sem,
                        ).start()


def gather_row(block, hold_near=None, hold=None):
    row = lax.axis_index("blk") // 8
    own = lax.dynamic_index_in_dim(block, row, 0, keepdims=False)
    other = lax.dynamic_index_in_dim(block, 1 - row, 0, keepdims=False)
    pair = jnp.stack([own, flip(other, 8)])
    if hold_near is not None:
        pair = after(pair, hold_near)
    column = with_flip(pair, 4)
    stages, sources = [pair, column], []
    if hold is not None:
        column = after(column, hold)
    half = WIDTH // 2
    planes = [with_flip(column[..., :half], 1), with_flip(column[..., half:], 2)]
    for plane, first, bit in zip(planes, "xy", (2, 1)):
        sources.append(Source("row", [plane, flip(plane, bit)], first))
    stages += [planes, [source.arrays[1] for source in sources]]
    return RowPart(sources, block.shape[1]), stages


def head_columns(shards, kinds):
    core = lax.axis_index("dp")
    blocks, widths = [], [128 * kind for kind in kinds]
    for shard, kind in zip(shards, kinds):
        own = lax.dynamic_slice_in_dim(shard, core * 32, 32, 0)
        own = own.reshape(32, kind, 8, 128).transpose(2, 0, 1, 3)
        blocks.append(own.reshape(8, 32, kind * 128))
    blocks = jnp.concatenate(blocks, axis=2)
    mine = exchange(jnp.concatenate([blocks, blocks], axis=0))
    mine = mine.reshape(2, 2, 2, 2, 32, sum(widths))
    source = Source("cores", [mine, swap_core(mine)])
    parts, place = [], 0
    for width in widths:
        parts.append(Part(1024, width, [(source, 0, place, 0, width)]))
        place += width
    return parts


def project_row(row_part, head_part, name):
    def body(ins, loaded, outs, _):
        weight = loaded[1].value()
        inputs = loaded[0].value()
        for first in range(0, row_part.rows, 256):
            rows = slice(first, first + 256)
            outs[0][rows, :] = dot(inputs[rows], weight).astype(jnp.bfloat16)

    (found,) = call_with_parts(
        body,
        [],
        [row_part, head_part],
        [shape(row_part.rows, head_part.width, of=jnp.bfloat16)],
        name,
    )
    return found


def row_grad(row_part, upstream, name):
    columns = upstream.shape[1]

    def body(ins, loaded, outs, _):
        core = ins[1][0]
        inputs = loaded[0].value()
        grads = []
        for first in range(0, columns, 128):
            grads.append(pair_dot(ins[0][:, first : first + 128], inputs, 0, 0).T)
        grad = jnp.concatenate(grads, axis=1).astype(jnp.bfloat16).reshape(16, 2, 32, columns)
        outs[0][core] = grad[:, 0]
        outs[0][1 - core] = grad[:, 1]

    (terms,) = call_with_parts(
        body,
        [upstream],
        [row_part],
        [shape(2, 16, 32, columns, of=jnp.bfloat16)],
        name,
        scalars=[lax.axis_index("dp").reshape(1).astype(jnp.int32)],
    )
    got = swap_core(terms[1])
    return (terms[0].astype(jnp.float32) + got.astype(jnp.float32)).astype(jnp.bfloat16)


def row_back(upstream, head_part, name):
    def body(ins, loaded, outs, _):
        weight = loaded[0].value()
        for first in range(0, ins[0].shape[0], 256):
            rows = slice(first, first + 256)
            outs[0][rows, :] = dot_back(ins[0][rows, :], weight).astype(jnp.bfloat16)

    (terms,) = call_with_parts(
        body, [upstream], [head_part], [shape(upstream.shape[0], WIDTH, of=jnp.bfloat16)], name
    )
    return terms


def reduce_row(terms, holds=None):
    blocks = terms.reshape(16, terms.shape[0] // 16, WIDTH)
    (both,), stages = scatter_chips([blocks], [(1, 2, 4, 8)], 0, 3, holds)
    row = lax.axis_index("blk") // 8
    kept = lax.dynamic_index_in_dim(both, row, 0, keepdims=False)
    other = lax.dynamic_index_in_dim(both, 1 - row, 0, keepdims=False)
    got = flip(other, 8)
    found = jnp.stack([jnp.where(row == 0, kept, got), jnp.where(row == 0, got, kept)])
    return found.astype(jnp.float32), stages


def finish_row_grad(got, kinds):
    total = jnp.sum(got.reshape(2, 8, 32, kinds, 128).astype(jnp.float32), axis=0)
    mine = total.astype(jnp.bfloat16).transpose(1, 2, 0, 3).reshape(32, kinds * WIDTH)
    other = swap_core(mine)
    core = lax.axis_index("dp")
    low = jnp.where(core == 0, mine, other)
    high = jnp.where(core == 0, other, mine)
    return jnp.concatenate([low, high], axis=0).astype(jnp.float32)


def columns_of(*pieces):
    spots, place = [], 0
    for source, first, width in pieces:
        spots.append((source, 0, first, place, width))
        place += width
    return Part(1024, place, spots)


PACK = 512


def pack_halves(shards):
    places = [
        (index, shard.shape[0] // 2, first)
        for index, shard in enumerate(shards)
        for first in range(0, shard.shape[1], PACK)
    ]

    def body(core, *refs):
        out_ref, place = refs[-1], 0
        for index, high, first in places:
            start = pl.multiple_of(core[0] * high, 16)
            out_ref[place : place + high, :] = refs[index][pl.ds(start, high), first : first + PACK]
            place += high

    return pl.pallas_call(
        body,
        out_shape=shape(sum(high for _, high, _ in places), PACK, of=jnp.bfloat16),
        in_specs=[smem_spec()] + [vmem_spec()] * len(shards),
        out_specs=vmem_spec(),
        compiler_params=pltpu.CompilerParams(vmem_limit_bytes=VMEM_BYTES),
        cost_estimate=cost(2),
        name="pack_halves",
    )(lax.axis_index("dp").reshape(1).astype(jnp.int32), *shards)


def gather_packed(packed):
    return lax.all_gather(packed, "blk", axis=0)


def packed_parts(shards, mine):
    if not paired():
        found = []
        for source, shard in zip(gather_flips(shards, "x" * len(shards)), shards):
            rows, columns = 32 * source.arrays[0].shape[5], shard.shape[1]
            step = min(columns, 1024)
            found.append(
                [
                    Part(rows, step, [(source, 0, first, 0, step)])
                    for first in range(0, columns, step)
                ]
            )
        return found
    spots, place = [], 0
    for shard in shards:
        high = shard.shape[0] // 2
        places = []
        for first in range(0, shard.shape[1], PACK):
            places.append(place)
            place += high
        spots.append((shard.shape[0] * 16, places))
    mine = mine.reshape(2, 2, 2, 2, place, PACK)
    source = Source("cores", [mine, swap_core(mine)])
    found = []
    for rows, places in spots:
        parts = []
        for first in range(0, len(places), 2):
            two = places[first : first + 2]
            parts.append(
                Part(
                    rows,
                    PACK * len(two),
                    [(source, row, 0, PACK * side, PACK) for side, row in enumerate(two)],
                )
            )
        found.append(parts)
    return found


def place_now():
    own, core = lax.axis_index("blk"), lax.axis_index("dp")
    bits = [(own // bit) % 2 for bit in FLIPS]
    return jnp.stack(bits + [core]).astype(jnp.int32)


class Loaded:
    def __init__(self, part, dst, sem):
        self.part, self.dst, self.sem, self.here = part, dst, sem, False

    def value(self):
        if not self.here:
            pltpu.make_async_copy(self.dst, self.dst, self.sem).wait()
            self.here = True
        return self.dst[...].reshape(self.part.rows, self.part.width)


def call_with_parts(body, inputs, parts, outputs, name, scratch=(), takes=5, scalars=()):
    sources = []
    for part in parts:
        sources += [spot[0] for spot in part.spots if spot[0] not in sources]
    arrays = [array for source in sources for array in source.arrays]

    def kernel(place, *refs):
        refs = list(refs)
        ins = [refs.pop(0) for _ in (*inputs, *scalars)]
        pieces = [[refs.pop(0) for _ in source.arrays] for source in sources]
        outs = [refs.pop(0) for _ in outputs]
        dsts = [refs.pop(0) for _ in parts]
        sems = refs.pop(0)
        loaded = []
        for index, part in enumerate(parts):
            part.start(
                lambda source: pieces[sources.index(source)], place, dsts[index], sems.at[index]
            )
            loaded.append(Loaded(part, dsts[index], sems.at[index]))
        body(ins, loaded, outs, refs)

    return pl.pallas_call(
        kernel,
        out_shape=tuple(outputs),
        in_specs=[smem_spec()]
        + [vmem_spec()] * len(inputs)
        + [smem_spec()] * len(scalars)
        + [pl.BlockSpec(memory_space=pl.ANY)] * len(arrays),
        out_specs=(vmem_spec(),) * len(outputs),
        scratch_shapes=[part.scratch() for part in parts]
        + [pltpu.SemaphoreType.DMA((len(parts),))]
        + list(scratch),
        compiler_params=pltpu.CompilerParams(vmem_limit_bytes=VMEM_BYTES),
        cost_estimate=cost(takes),
        name=name,
    )(place_now(), *inputs, *scalars, *arrays)


def vmem_spec():
    return pl.BlockSpec(memory_space=pltpu.VMEM)


def smem_spec():
    return pl.BlockSpec(memory_space=pltpu.SMEM)


def seg_of_pos(ends_ref, pos):
    seg = jnp.zeros(pos.shape, jnp.int32)
    for slot in range(ends_ref.shape[0]):
        seg = seg + (ends_ref[slot] <= pos).astype(jnp.int32)
    return seg


def pair_dot(left, right, left_dim, right_dim):
    return lax.dot_general(
        left, right, (((left_dim,), (right_dim,)), ((), ())), preferred_element_type=jnp.float32
    )


def seg_tables(q_ends, k_ends, span):
    seg_q = seg_of_pos(q_ends, lax.broadcasted_iota(jnp.int32, (1, span), 1))
    seg_k = seg_of_pos(k_ends, lax.broadcasted_iota(jnp.int32, (span, 1), 0))
    return seg_q, seg_k


def masked_scores(keys, queries, seg_q, seg_k, first, causal):
    scores = pair_dot(keys, queries, 1, 1)
    allowed = seg_k == seg_q
    if causal:
        key_pos = lax.broadcasted_iota(jnp.int32, scores.shape, 0)
        query_pos = first + lax.broadcasted_iota(jnp.int32, scores.shape, 1)
        allowed = allowed & (key_pos <= query_pos)
    return jnp.where(allowed, scores, NEG)


def attn_forward_body(causal, width, q_ends, k_ends, q_ref, kv_ref, low_ref, full_ref, lse_ref):
    span = q_ref.shape[0]
    step = math.gcd(span, 256)
    heads = width // HEAD_DIM
    seg_q, seg_k = seg_tables(q_ends, k_ends, span)
    key_at = kv_ref.shape[1] - 2 * width
    scaled = q_ref[:, :width] * jnp.bfloat16(HEAD_DIM ** (-0.5))
    keys = kv_ref[:, key_at : key_at + width]
    values = kv_ref[:, key_at + width : key_at + 2 * width]
    for first in range(0, span, step):
        reach = first + step if causal else span
        parts = []
        for head in range(heads):
            cols = slice(head * HEAD_DIM, (head + 1) * HEAD_DIM)
            scores = masked_scores(
                keys[:reach, cols],
                scaled[first : first + step, cols],
                seg_q[:, first : first + step],
                seg_k[:reach],
                first,
                causal,
            )
            top = jnp.max(scores, axis=0, keepdims=True)
            probs = jnp.exp(scores - top)
            total = jnp.sum(probs, axis=0, keepdims=True)
            mixed = pair_dot(values[:reach, cols], probs.astype(jnp.bfloat16), 0, 0)
            parts.append(mixed / total)
            lse_ref[head : head + 1, first : first + step] = top + jnp.log(total)
        joined = jnp.concatenate(parts, axis=0).T
        full_ref[first : first + step, :] = joined
        low_ref[first : first + step, :] = joined.astype(jnp.bfloat16)


def attn_forward(q_ends, k_ends, queries, keys_values, width, causal):
    span = queries.shape[0]
    return pl.pallas_call(
        functools.partial(attn_forward_body, causal, width),
        out_shape=(
            jax.ShapeDtypeStruct((span, width), jnp.bfloat16),
            jax.ShapeDtypeStruct((span, width), jnp.float32),
            jax.ShapeDtypeStruct((width // HEAD_DIM, span), jnp.float32),
        ),
        in_specs=[smem_spec(), smem_spec()] + [vmem_spec()] * 2,
        out_specs=(vmem_spec(),) * 3,
        compiler_params=pltpu.CompilerParams(vmem_limit_bytes=VMEM_BYTES),
        cost_estimate=cost(8),
        name="attn_forward",
    )(q_ends, k_ends, queries, keys_values)


def attn_backward_body(
    causal,
    width,
    q_ends,
    k_ends,
    q_ref,
    kv_ref,
    up_ref,
    full_ref,
    lse_ref,
    *outs,
):
    dq_ref, dkv_ref = outs[0], outs[-3]
    dk_sum, dv_sum = outs[-2:]
    span = q_ref.shape[0]
    step = math.gcd(span, 256)
    heads = width // HEAD_DIM
    seg_q, seg_k = seg_tables(q_ends, k_ends, span)
    key_at = kv_ref.shape[1] - 2 * width
    scaled = q_ref[:, :width] * jnp.bfloat16(HEAD_DIM ** (-0.5))
    keys = kv_ref[:, key_at : key_at + width]
    values = kv_ref[:, key_at + width : key_at + 2 * width]
    upstream = up_ref[...]
    dk_sum[...] = jnp.zeros_like(dk_sum)
    dv_sum[...] = jnp.zeros_like(dv_sum)
    for first in range(0, span, step):
        reach = first + step if causal else span
        rows = slice(first, first + step)
        product = (upstream[rows].astype(jnp.float32) * full_ref[rows, :]).T
        parts = []
        for head in range(heads):
            cols = slice(head * HEAD_DIM, (head + 1) * HEAD_DIM)
            delta = jnp.sum(product[cols], axis=0, keepdims=True)
            scores = masked_scores(
                keys[:reach, cols], scaled[rows, cols], seg_q[:, rows], seg_k[:reach], first, causal
            )
            probs = jnp.exp(scores - lse_ref[head : head + 1, rows])
            dv_sum[head, :reach] += pair_dot(
                probs.astype(jnp.bfloat16), upstream[rows, cols], 1, 0
            )
            grad_probs = pair_dot(values[:reach, cols], upstream[rows, cols], 1, 1)
            grad_scores = (probs * (grad_probs - delta)).astype(jnp.bfloat16)
            dk_sum[head, :reach] += pair_dot(grad_scores, scaled[rows, cols], 1, 0)
            parts.append(pair_dot(keys[:reach, cols], grad_scores, 0, 0))
        joined = jnp.concatenate(parts, axis=0).T * HEAD_DIM ** (-0.5)
        dq_ref[rows, :width] = joined.astype(jnp.bfloat16)
    sums = [dk_sum[head] for head in range(heads)] + [dv_sum[head] for head in range(heads)]
    kv_at = dkv_ref.shape[1] - 2 * width
    dkv_ref[:, kv_at:] = jnp.concatenate(sums, axis=1).astype(jnp.bfloat16)


def attn_backward(
    q_ends, k_ends, queries, keys_values, upstream, full, lse, causal, joined=False
):
    span, width = upstream.shape
    kinds = [3] if joined else [1, 2]
    heads = width // HEAD_DIM
    return pl.pallas_call(
        functools.partial(attn_backward_body, causal, width),
        out_shape=[jax.ShapeDtypeStruct((span, kind * width), jnp.bfloat16) for kind in kinds],
        in_specs=[smem_spec(), smem_spec()] + [vmem_spec()] * 5,
        out_specs=[vmem_spec()] * len(kinds),
        scratch_shapes=[pltpu.VMEM((heads, span, HEAD_DIM), jnp.float32)] * 2,
        compiler_params=pltpu.CompilerParams(vmem_limit_bytes=VMEM_BYTES),
        cost_estimate=cost(8),
        name="attn_backward",
    )(q_ends, k_ends, queries, keys_values, upstream, full, lse)


def exchange(blocks):
    return lax.all_to_all(blocks, "blk", 0, 0, tiled=True)


def as_rows(blocks):
    return blocks.reshape(blocks.shape[0] * blocks.shape[1], blocks.shape[2])


def as_blocks(rows):
    devices = lax.axis_size("blk")
    return rows.reshape(devices, rows.shape[0] // devices, rows.shape[1])


def write_blocks(out_ref, values, lanes, kind, width):
    span = values.shape[0] // lanes
    for group in range(WIDTH // width):
        for lane in range(lanes):
            out_ref[lane * (WIDTH // width) + group, :, kind * width : (kind + 1) * width] = values[
                lane * span : (lane + 1) * span, group * width : (group + 1) * width
            ]


def read_blocks(got_ref, lanes, kind, width):
    groups = got_ref.shape[0] // lanes
    cols = slice(kind * width, (kind + 1) * width)
    rows = [
        jnp.concatenate([got_ref[lane * groups + group, :, cols] for group in range(groups)], axis=1)
        for lane in range(lanes)
    ]
    return jnp.concatenate(rows, axis=0)


def dot(left, right):
    return pair_dot(left, right, 1, 0)


def dot_back(left, right):
    return pair_dot(left, right, 1, 1)


def shape(*sizes, of=jnp.float32):
    return jax.ShapeDtypeStruct(sizes, of)


def normalize(values):
    center = values - jnp.mean(values, -1, keepdims=True)
    scale = lax.rsqrt(jnp.mean(center * center, -1, keepdims=True) + 1e-05)
    return center * scale, scale


def norm_back(upstream, normed, scale, gains_row):
    grad = upstream * gains_row
    return scale * (
        grad
        - jnp.mean(grad, -1, keepdims=True)
        - normed * jnp.mean(grad * normed, -1, keepdims=True)
    )


def project_blocks(inputs, parts, lanes, width, name):
    def body(ins, loaded, outs, _):
        for kind, weight in enumerate(loaded):
            write_blocks(
                outs[0], dot(ins[0][...], weight.value()).astype(jnp.bfloat16), lanes, kind, width
            )

    devices, span = lax.axis_size("blk"), inputs.shape[0] // lanes
    (blocks,) = call_with_parts(
        body,
        [inputs],
        parts,
        [shape(devices, span, width * len(parts), of=jnp.bfloat16)],
        name,
    )
    return blocks


def after_self(got, tokens, gains, biases, out_part, query_part, lanes, width):
    def body(ins, loaded, outs, _):
        got_ref, tokens_ref, gains_ref, biases_ref = ins
        low_ref, normed_ref, scale_ref, hidden_ref, blocks_ref = outs
        attended = read_blocks(got_ref, lanes, 0, width)
        low_ref[...] = attended
        resid = tokens_ref[...].astype(jnp.float32) + dot(attended, loaded[0].value())
        normed, scale = normalize(resid)
        normed_ref[...] = normed
        scale_ref[...] = scale
        hidden = (normed * gains_ref[0:1] + biases_ref[0:1]).astype(jnp.bfloat16)
        hidden_ref[...] = hidden
        query = dot(hidden, loaded[1].value()).astype(jnp.bfloat16)
        write_blocks(blocks_ref, query, lanes, 0, width)

    rows = tokens.shape[0]
    return call_with_parts(
        body,
        [got, tokens, gains, biases],
        [out_part, query_part],
        [
            shape(rows, WIDTH, of=jnp.bfloat16),
            shape(rows, WIDTH),
            shape(rows, 1),
            shape(rows, WIDTH, of=jnp.bfloat16),
            shape(*got.shape, of=jnp.bfloat16),
        ],
        "after_self",
    )


def feed_forward(got, normed_in, cotangent, gains, biases, out_part, in_parts, down, outs, up, lanes, width):
    pieces = len(in_parts)
    step = in_parts[0].width

    def body(ins, loaded, refs, scratch):
        got_ref, normed_in_ref, cot_ref, gains_ref, biases_ref = ins
        (
            output_ref,
            low_ref,
            mixed_ref,
            adapted_ref,
            dunder_ref,
            dab_ref,
            dcb_ref,
            dresid_ref,
            blocks_ref,
            norms_ref,
        ) = refs
        slopes, acts = scratch
        w_out, w_down, w_in = loaded[0], loaded[1], loaded[2 : 2 + pieces]
        w_ff, w_up = loaded[2 + pieces :]
        attended = read_blocks(got_ref, lanes, 0, width)
        low_ref[...] = attended
        hidden = normed_in_ref[...] * gains_ref[0:1] + biases_ref[0:1]
        normed_one, scale_one = normalize(hidden + dot(attended, w_out.value()))
        mixed = normed_one * gains_ref[1:2] + biases_ref[1:2]
        mixed_low = mixed.astype(jnp.bfloat16)
        mixed_ref[...] = mixed_low
        summed = mixed
        under = dot(mixed_low, w_down.value())
        gate = 1.0 / (1.0 + jnp.exp(-under))
        adapted = (under * gate).astype(jnp.bfloat16)
        adapted_ref[...] = adapted
        under_slope = gate * (1.0 + under * (1.0 - gate))
        for piece in range(pieces):
            before = dot(mixed_low, w_in[piece].value())
            below = 0.5 + 0.5 * lax.erf(before * (0.5**0.5))
            slopes[piece] = below + before * jnp.exp(-0.5 * before * before) * (
                (2.0 * math.pi) ** -0.5
            )
            acts[piece] = (before * below).astype(jnp.bfloat16)
        for piece in range(pieces):
            summed = summed + dot(acts[piece], w_ff[piece].value())
        summed = summed + 4.0 * dot(adapted, w_up.value())
        normed_two, scale_two = normalize(summed)
        output_ref[...] = (normed_two * gains_ref[2:3] + biases_ref[2:3]).astype(jnp.bfloat16)
        upstream = cot_ref[...].astype(jnp.float32)
        norms_ref[0:1] = jnp.sum(upstream * normed_two, axis=0, keepdims=True)
        norms_ref[1:2] = jnp.sum(upstream, axis=0, keepdims=True)
        dz = norm_back(upstream, normed_two, scale_two, gains_ref[2:3])
        dzb = dz.astype(jnp.bfloat16)
        dab = (4.0 * dz).astype(jnp.bfloat16)
        dab_ref[...] = dab
        dunder = (under_slope * dot_back(dab, w_up.value())).astype(jnp.bfloat16)
        dunder_ref[...] = dunder
        dmixed = dz + dot_back(dunder, w_down.value())
        for piece in range(pieces):
            dpre = (slopes[piece] * dot_back(dzb, w_ff[piece].value())).astype(jnp.bfloat16)
            dmixed = dmixed + dot_back(dpre, w_in[piece].value())
        norms_ref[2:3] = jnp.sum(dmixed * normed_one, axis=0, keepdims=True)
        norms_ref[3:4] = jnp.sum(dmixed, axis=0, keepdims=True)
        dresid = norm_back(dmixed, normed_one, scale_one, gains_ref[1:2])
        dresid_ref[...] = dresid
        dcb = dresid.astype(jnp.bfloat16)
        dcb_ref[...] = dcb
        write_blocks(
            blocks_ref, dot_back(dcb, w_out.value()).astype(jnp.bfloat16), lanes, 0, width
        )

    rows = normed_in.shape[0]
    low = jnp.bfloat16

    def body_rows(ins, loaded, refs, scratch):
        whole_ff = loaded[2 + pieces]

        class Rows:
            def __init__(self, piece):
                self.piece = piece

            def value(self):
                return whole_ff.value()[self.piece * step : (self.piece + 1) * step]

        loaded = loaded[: 2 + pieces] + [[Rows(piece) for piece in range(pieces)], loaded[-1]]
        body(ins, loaded, refs, scratch)

    return call_with_parts(
        body_rows,
        [got, normed_in, cotangent, gains, biases],
        [out_part, down] + in_parts + [outs, up],
        [
            shape(rows, WIDTH, of=low),
            shape(rows, WIDTH, of=low),
            shape(rows, WIDTH, of=low),
            shape(rows, down.width, of=low),
            shape(rows, down.width, of=low),
            shape(rows, WIDTH, of=low),
            shape(rows, WIDTH, of=low),
            shape(rows, WIDTH),
            shape(*got.shape, of=low),
            shape(4, WIDTH),
        ],
        "feed_forward",
        [
            pltpu.VMEM((pieces, rows, step), jnp.float32),
            pltpu.VMEM((pieces, rows, step), jnp.bfloat16),
        ],
        20,
    )


def before_self(got, dresid, normed, scale, gains, query_part, out_part, lanes, width):
    def body(ins, loaded, outs, _):
        got_ref, dresid_ref, normed_ref, scale_ref, gains_ref = ins
        dcq_ref, dr_ref, dsb_ref, blocks_ref, norms_ref = outs
        dcq = read_blocks(got_ref, lanes, 0, width)
        dcq_ref[...] = dcq
        dhidden = dresid_ref[...] + dot_back(dcq, loaded[0].value())
        normed = normed_ref[...]
        norms_ref[0:1] = jnp.sum(dhidden * normed, axis=0, keepdims=True)
        norms_ref[1:2] = jnp.sum(dhidden, axis=0, keepdims=True)
        dr = norm_back(dhidden, normed, scale_ref[...], gains_ref[0:1])
        dr_ref[...] = dr
        dsb = dr.astype(jnp.bfloat16)
        dsb_ref[...] = dsb
        grad = dot_back(dsb, loaded[1].value()).astype(jnp.bfloat16)
        write_blocks(blocks_ref, grad, lanes, 0, width)

    rows = dresid.shape[0]
    return call_with_parts(
        body,
        [got, dresid, normed, scale, gains],
        [query_part, out_part],
        [
            shape(rows, WIDTH, of=jnp.bfloat16),
            shape(rows, WIDTH),
            shape(rows, WIDTH, of=jnp.bfloat16),
            shape(*got.shape, of=jnp.bfloat16),
            shape(2, WIDTH),
        ],
        "before_self",
    )


def input_grad(got, start, parts, lanes, span, width, name):
    def body(ins, loaded, outs, _):
        total = None
        for kind, weight in enumerate(loaded):
            values = read_blocks(ins[0], lanes, kind, width)
            term = dot_back(values, weight.value())
            total = term if total is None else total + term
        outs[0][...] = total if len(ins) == 1 else total + ins[1][...]

    rows = span * lanes
    return call_with_parts(
        body,
        [got] if start is None else [got, start],
        parts,
        [shape(rows, WIDTH)],
        name,
    )


def shards(
    tokens,
    encoder,
    cotangent,
    self_in,
    self_out,
    cross_q,
    cross_kv,
    cross_out,
    ffn_in,
    ffn_out,
    adapt_down,
    adapt_up,
    norm_gain,
    norm_bias,
    tgt_lengths,
    src_lengths,
):
    lanes, span, _ = tokens.shape
    rows = lanes * span
    width = WIDTH * lanes // lax.axis_size("blk")
    own_row = lax.axis_index("blk") // (lax.axis_size("blk") // lanes)
    tgt_ends = jnp.cumsum(lax.dynamic_index_in_dim(tgt_lengths, own_row, 0, keepdims=False))
    src_ends = jnp.cumsum(lax.dynamic_index_in_dim(src_lengths, own_row, 0, keepdims=False))
    flat_tokens = tokens.reshape(rows, WIDTH)
    flat_encoder = encoder.reshape(rows, WIDTH)
    frozen = [ffn_in, adapt_down, ffn_out, adapt_up, cross_out]

    if paired():
        packed = gather_packed(pack_halves(frozen))
        self_packed = pack_halves([self_in])
        token_row, stages = gather_row(tokens)
        self_heads, pair_heads = head_columns([self_in, cross_kv], [3, 2])
        out_shard, query_shard = after((self_out, cross_q), stages[1])
        encoder_block = after(encoder, stages[1])
        self_qkv = project_row(token_row, self_heads, "self_in")
        out_source, query_source = gather_flips([out_shard, query_shard], "xy", self_qkv)
        encoder_row, encoder_stages = gather_row(
            encoder_block, self_qkv, (out_source.arrays[1], query_source.arrays[1])
        )
        self_qkv = after(self_qkv, out_source.stages[0], query_source.stages[0])
        pair_own = project_row(encoder_row, pair_heads, "cross_kv")
    else:
        (self_source, pair_source, out_source, query_source) = gather_flips(
            [self_in, cross_kv, self_out, cross_q], "xyxy"
        )
        self_parts = [columns_of((self_source, WIDTH * kind, WIDTH)) for kind in range(3)]
        pair_parts = [columns_of((pair_source, WIDTH * kind, WIDTH)) for kind in range(2)]
        self_qkv = as_rows(
            exchange(project_blocks(flat_tokens, self_parts, lanes, width, "self_in"))
        )
        pair_own = as_rows(
            exchange(project_blocks(flat_encoder, pair_parts, lanes, width, "cross_kv"))
        )
    self_out_part = columns_of((out_source, 0, WIDTH))
    query_part = columns_of((query_source, 0, WIDTH))

    self_mid, self_full, self_lse = attn_forward(
        tgt_ends, tgt_ends, self_qkv, self_qkv, width, True
    )
    self_sent = after(self_mid, out_source.stages[1], query_source.stages[1])
    if paired():
        self_sent = after(self_sent, encoder_stages[0])
    self_back = exchange(as_blocks(self_sent))
    if paired():
        self_back = after(self_back, encoder_stages[1])
    self_low, normed, scale, hidden_low, query_blocks = after_self(
        self_back,
        flat_tokens,
        norm_gain,
        norm_bias,
        self_out_part,
        query_part,
        lanes,
        width,
    )
    cross_own = as_rows(exchange(query_blocks))
    cross_mid, cross_full, cross_lse = attn_forward(
        tgt_ends, src_ends, cross_own, pair_own, width, False
    )
    cross_back = exchange(as_blocks(cross_mid))
    ready = after(packed, cross_mid) if paired() else None
    ff_parts, down_parts, ffo_parts, up_parts, (cross_out_part,) = packed_parts(frozen, ready)
    if paired():
        self_packed = gather_packed(after(self_packed, cross_back))
    (
        output,
        cross_low,
        mixed_low,
        adapter_low,
        grad_under,
        adapt_low,
        cross_branch_low,
        grad_resid_two,
        cross_grad_blocks,
        norms_high,
    ) = feed_forward(
        cross_back,
        normed,
        cotangent.reshape(rows, WIDTH),
        norm_gain,
        norm_bias,
        cross_out_part,
        ff_parts,
        down_parts[0],
        ffo_parts[0],
        up_parts[0],
        lanes,
        width,
    )
    high_groups = [
        [(cross_low, cross_branch_low)],
        [(mixed_low, grad_under), (adapter_low, adapt_low)],
    ]
    high_terms = [grad_terms(pairs) for pairs in high_groups]
    high_orders = [(2, 1, 4, 8), (1, 2, 4, 8)]
    high_terms, high_stages = scatter_chips(high_terms, high_orders, 0, 2)
    cross_dq, cross_dkv = attn_backward(
        tgt_ends,
        src_ends,
        cross_own,
        pair_own,
        as_rows(after(exchange(cross_grad_blocks), high_stages[0])),
        cross_full,
        cross_lse,
        False,
    )
    cross_dq_got = after(exchange(as_blocks(cross_dq)), high_stages[1])
    if paired():
        dkv_late = after(cross_dkv, high_stages[1])
        pair_terms = row_back(dkv_late, pair_heads, "encoder_grad")
        kv_sent = row_grad(encoder_row, dkv_late, "cross_kv_grad")
        cross_dq_got = after(cross_dq_got, pair_terms, kv_sent)
    cq_low, grad_resid_one, self_branch_low, self_grad_blocks, norms_low = before_self(
        cross_dq_got,
        grad_resid_two,
        normed,
        scale,
        norm_gain,
        query_part,
        self_out_part,
        lanes,
        width,
    )
    norms = jnp.concatenate([norms_low, norms_high], axis=0)
    mid_pairs = [(hidden_low, cq_low), (self_low, self_branch_low)]
    mid_orders = [(2, 1, 4, 8), (1, 2, 4, 8)]
    mid_terms = [grad_terms([pair]) for pair in mid_pairs]
    mid_terms, _ = scatter_chips(mid_terms, mid_orders, 0, 1)
    if paired():
        high_terms = [jnp.concatenate(after(high_terms, self_grad_blocks), axis=2)]
        high_terms, _ = scatter_chips(high_terms, [(2, 1, 4, 8)], 2, 3)
    self_upstream = after(exchange(self_grad_blocks), high_stages[2])
    (self_grads,) = attn_backward(
        tgt_ends,
        tgt_ends,
        self_qkv,
        self_qkv,
        as_rows(self_upstream),
        self_full,
        self_lse,
        True,
        joined=True,
    )
    if paired():
        (self_parts,) = packed_parts([self_in], after(self_packed, self_grads))
        self_got = exchange(as_blocks(self_grads))
        high_terms, _ = scatter_chips(after(high_terms, self_grads), [(2, 1, 4, 8)], 3, 4)
        self_sent = row_grad(token_row, after(self_grads, high_terms[0]), "self_in_grad")
        mid_terms, _ = scatter_chips(after(mid_terms, self_grads), mid_orders, 1, 2)
        mid_terms = [jnp.concatenate(mid_terms, axis=2)]
        chunks = [
            array[:, :, first : first + width]
            for array in (self_sent, kv_sent)
            for first in range(0, array.shape[2], width)
        ]
        partials = norms.astype(jnp.bfloat16).reshape(1, 48, width)
        chunks.append(jnp.broadcast_to(partials, (16, 48, width)))
        (tokens_grad,) = input_grad(
            self_got, grad_resid_one, self_parts, lanes, span, width, "tokens_grad"
        )
        encoder_grad, stages = reduce_row(pair_terms, {2: tokens_grad})
        encoder_grad = encoder_grad.reshape(rows, WIDTH)
        sent = jnp.concatenate(chunks, axis=1)
        got = exchange(after(sent, self_got, stages[2], mid_terms))
        mid_terms, mid_stages = scatter_chips(
            mid_terms, mid_orders[:1], 2, 4, {2: tokens_grad}
        )
        got = after(got, tokens_grad, stages[3], mid_stages[1])
        chunks = [got[:, first : first + 32] for first in range(0, 160, 32)]
        grad_self_in = finish_row_grad(jnp.concatenate(chunks[:3], axis=2), 3)
        grad_cross_kv = finish_row_grad(jnp.concatenate(chunks[3:], axis=2), 2)
        norms = jnp.sum(got[:, 160:].astype(jnp.float32), axis=0).reshape(6, WIDTH)
        norms = norms + swap_core(norms)
    else:
        pair_got = exchange(as_blocks(cross_dkv))
        self_got = exchange(as_blocks(self_grads))
        (encoder_grad,) = input_grad(
            pair_got, None, pair_parts, lanes, span, width, "encoder_grad"
        )
        (tokens_grad,) = input_grad(
            self_got, grad_resid_one, self_parts, lanes, span, width, "tokens_grad"
        )
        pair_low = pair_got.reshape(lanes, -1, span, 2, width).transpose(0, 2, 3, 1, 4)
        self_low_grads = self_got.reshape(lanes, -1, span, 3, width).transpose(0, 2, 3, 1, 4)
        grad_cross_kv = weight_grad(flat_encoder, pair_low.reshape(rows, 2 * WIDTH))
        grad_self_in = weight_grad(flat_tokens, self_low_grads.reshape(rows, 3 * WIDTH))
        norms = lax.psum(norms, ("dp", "blk"))
    ((grad_cross_q, grad_self_out),) = finish_terms([mid_pairs], mid_terms)
    (grad_cross_out,), (grad_adapt_down, grad_adapt_up) = finish_terms(high_groups, high_terms)
    return (
        output.reshape(lanes, span, WIDTH),
        tokens_grad.reshape(lanes, span, WIDTH),
        encoder_grad.reshape(lanes, span, WIDTH),
        grad_self_in,
        grad_self_out,
        grad_cross_q,
        grad_cross_kv,
        grad_cross_out,
        grad_adapt_down,
        grad_adapt_up,
        jnp.stack([norms[0], norms[4], norms[2]]),
        jnp.stack([norms[1], norms[5], norms[3]]),
    )


def solution(mesh):
    placed = (
        P("dp", "blk", None),
        P("dp", "blk", None),
        P("dp", "blk", None),
        P("blk", None),
        P("blk", None),
        P("blk", None),
        P("blk", None),
        P("blk", None),
        P("blk", None),
        P("blk", None),
        P("blk", None),
        P("blk", None),
        P(),
        P(),
        P("dp", None),
        P("dp", None),
    )
    return jax.shard_map(
        shards,
        mesh=mesh,
        in_specs=placed,
        out_specs=(
            P("dp", "blk", None),
            P("dp", "blk", None),
            P("dp", "blk", None),
            P("blk", None),
            P("blk", None),
            P("blk", None),
            P("blk", None),
            P("blk", None),
            P("blk", None),
            P("blk", None),
            P(),
            P(),
        ),
        check_vma=False,
    )
```
